32 devices in a mesh: row: 4 (over x, core), col: 8 (over z, y).
Axes of the slice: x: 2, y: 2, z: 4, core: 2. Of those that a mesh axis runs over, the one named last changes fastest.
Arguments:
- field_rhs: float32 [4, 8, 2, 3, 512], P('row', 'col'), may hold values from -6 to 6
- positions: float32 [4, 8, 3, 512], P('row', 'col'), may hold values from 0.25 to 255.75, as said below
- polar: float32 [4, 8, 512], P('row', 'col'), may hold values from 0.5 to 4
- grid_base: int32 [4, 8, 3, 512], P('row', 'col'), may hold values from 0 to 255, as said below
- tile_lists: int32 [4, 8, 4, 12], P('row', 'col'), may hold values from 0 to 35, as said below
Outputs:
- dipoles: float32 [4, 8, 2, 3, 512], P('row', 'col')
- residual: float32 [4, 8, 2, 3, 512], P('row', 'col')
The draws below stay inside these ranges and needn't reach their ends.
Inputs may be any that keep to these rules, and one draw needn't show every extreme that they name: grid_base + 2, modulo the grid's length in that dimension, is the grid cell holding the atom; the atoms of brick (r, c) lie in its cells r * 8 to r * 8 + 7 along x and c * 4 to c * 4 + 3 along y, no two atoms share a cell, and atom t * 128 + i of a brick lies in z cells t * 64 to (t + 1) * 64 - 1. positions minus the atom's cell lies in 0.25 to 0.75 in every dimension. `tile_lists`: entry k of tile t names a tile of the 3 x 3 bricks around the tile's own brick as value = b * 4 + tile with brick offset (b // 3 - 1, b mod 3 - 1); entry 0 is tile t itself (b = 4); the entries of one list are distinct, and each other entry is tile t - 1, t or t + 1 (modulo 4) of its brick.
All inputs are finite; a program needn't handle non-finite values.
Results may differ from the reference program's by a relative error of at most 0.0003.
Values sent between devices are 32-bit elements; how exact they have to be, the bound alone decides.
No kernel may reach another device: no remote copies, remote signals or barrier semaphores. Data moves between devices by JAX's collectives and lax.ppermute only.
A program may use at most 64 MiB of HBM per device.

```python
import math
import jax
import jax.numpy as jnp
from jax import lax

CX = 8
CY = 4
KZ = 256
ATOM_DEV = 512
TILE = 128
NBR = 12
RHS = 2
ITERS = 2
TILES = 4
KX = 32
KY = 32
N_ROW = 4
N_COL = 8


def atom_cells(key):
    brick_rows = KX // CX
    brick_cols = KY // CY
    slab_depth = KZ // TILES
    region = CX * CY * slab_depth
    scores = jax.random.randint(key, (brick_rows, brick_cols, TILES, region), 0, 2 ** 30 // region)
    scores = scores * region + jnp.arange(region, dtype=jnp.int32)
    chosen = jnp.argsort(scores, axis=-1)[..., :TILE].astype(jnp.int32)
    along_x = chosen // (CY * slab_depth) + (jnp.arange(brick_rows, dtype=jnp.int32) * CX)[:, None, None, None]
    along_y = chosen // slab_depth % CY + (jnp.arange(brick_cols, dtype=jnp.int32) * CY)[None, :, None, None]
    along_z = chosen % slab_depth + (jnp.arange(TILES, dtype=jnp.int32) * slab_depth)[None, None, :, None]
    cell_index = jnp.stack([along_x, along_y, along_z], axis=2)
    return cell_index.reshape(brick_rows, brick_cols, 3, TILES * TILE)


def draw_grid_base(key, part):
    cell_index = atom_cells(key)
    lengths = jnp.array([KX, KY, KZ], dtype=jnp.int32)[None, None, :, None]
    return ((cell_index - 2) % lengths).astype(jnp.int32)


def draw_positions(key, part):
    cell_index = atom_cells(key)
    key = jax.random.fold_in(key, 5)
    uniform_draw = jax.random.uniform(key, cell_index.shape, jnp.float32)
    fraction = 0.25 + 0.5 * uniform_draw
    return cell_index.astype(jnp.float32) + fraction


def draw_tile_lists(key, part):
    key = jax.random.fold_in(key, 9)
    brick_rows = KX // CX
    brick_cols = KY // CY
    scores = jax.random.randint(key, (brick_rows, brick_cols, TILES, 26), 0, 2 ** 20)
    scores = scores * 26 + jnp.arange(26, dtype=jnp.int32)
    picked = jnp.argsort(scores, axis=-1)[..., :NBR - 1].astype(jnp.int32)
    candidate = picked + (picked >= 13).astype(jnp.int32)
    brick_index = candidate // 3
    tile_step = candidate % 3 - 1
    own_tile = jnp.arange(TILES, dtype=jnp.int32)[None, None, :, None]
    listed = brick_index * TILES + (own_tile + tile_step) % TILES
    itself_entry = jnp.broadcast_to(4 * TILES + own_tile, (brick_rows, brick_cols, TILES, 1))
    return jnp.concatenate([itself_entry, listed], axis=-1).astype(jnp.int32)


def levels(key, shape, split, least, largest):
    def one(position, parts):
        heights = jax.random.uniform(jax.random.fold_in(jax.random.fold_in(key, 6), position), (parts,), jnp.float32, least / len(split), largest / len(split))
        return jnp.repeat(jnp.exp(heights), shape[position] // parts).reshape((-1,) + (1,) * (len(shape) - position - 1))

    factor_of = one(*split[0])
    for cut in split[1:]:
        factor_of = factor_of * one(*cut)
    return factor_of


def noise(key, shape, deviation, bound, split=(), held_as=jnp.bfloat16):
    values = deviation * jax.random.normal(key, shape, jnp.float32)
    if split:
        values = values * levels(key, shape, split, -0.22, 0.18)
    return jnp.clip(values, -bound, bound).astype(held_as)


def setup_inputs(seed: int = 0) -> dict:
    arg_keys = jax.random.split(jax.random.key(seed), 6)
    field_rhs = noise(arg_keys[0], (N_ROW, N_COL, RHS, 3, ATOM_DEV), 1.0, 6.0, ((0, 4), (1, 8)), jnp.float32)
    positions = draw_positions(jax.random.fold_in(arg_keys[5], 71), 0)
    polar = jnp.clip(jnp.exp(math.log(4.0) - 2.0794415 * jax.random.uniform(arg_keys[2], (N_ROW, N_COL, ATOM_DEV), jnp.float32) ** levels(arg_keys[2], (N_ROW, N_COL, ATOM_DEV), ((0, 4), (1, 8)), -0.2, 0.2)), 0.5, 4.0)
    grid_base = draw_grid_base(jax.random.fold_in(arg_keys[5], 71), 0)
    tile_lists = draw_tile_lists(jax.random.fold_in(arg_keys[5], 71), 0)
    return dict(field_rhs=field_rhs, positions=positions, polar=polar, grid_base=grid_base, tile_lists=tile_lists)


ewald_beta = 0.4
thole_a = 0.39
self_coef = 4.0 * ewald_beta ** 3 / (3.0 * math.sqrt(math.pi))

def spline_table(fraction):
    previous = {0: jnp.ones_like(fraction)}
    fourth = previous
    for degree in range(2, 6):
        current = {}
        for offset in range(degree):
            abscissa = fraction + offset
            summed = abscissa * previous.get(offset, 0.0) + (degree - abscissa) * previous.get(offset - 1, 0.0)
            current[offset] = summed / (degree - 1)
        if degree == 4:
            fourth = current
        previous = current
    values = jnp.stack([previous[4 - stencil] for stencil in range(5)])
    slopes = jnp.stack([fourth.get(4 - stencil, 0.0) - fourth.get(3 - stencil, 0.0) for stencil in range(5)])
    return (values, slopes)

def spline_modulus(wave_index, length):
    spline_coef = (1.0 / 24.0, 11.0 / 24.0, 11.0 / 24.0, 1.0 / 24.0)
    cosine_sum = jnp.zeros(wave_index.shape, jnp.float32)
    sine_sum = jnp.zeros(wave_index.shape, jnp.float32)
    for offset in range(4):
        angles = 2.0 * math.pi / length * (wave_index * offset % length).astype(jnp.float32)
        cosine_sum = cosine_sum + spline_coef[offset] * jnp.cos(angles)
        sine_sum = sine_sum + spline_coef[offset] * jnp.sin(angles)
    return cosine_sum * cosine_sum + sine_sum * sine_sum

def folded_square(wave_index, length):
    nearest = jnp.minimum(wave_index, length - wave_index).astype(jnp.float32) / length
    return nearest * nearest

def influence(wave_x, wave_y, wave_z, length_x, length_y, length_z):
    wave_norm = folded_square(wave_x, length_x) + folded_square(wave_y, length_y) + folded_square(wave_z, length_z)
    modulus = spline_modulus(wave_x, length_x) * spline_modulus(wave_y, length_y) * spline_modulus(wave_z, length_z)
    excluded = (wave_x * 2 == length_x) | (wave_y * 2 == length_y) | (wave_z * 2 == length_z)
    excluded = excluded | (wave_x == 0) & (wave_y == 0) & (wave_z == 0)
    safe_norm = jnp.where(excluded, 1.0, wave_norm)
    safe_modulus = jnp.where(excluded, 1.0, modulus)
    result = jnp.exp(-(math.pi ** 2 / ewald_beta ** 2) * safe_norm) / (math.pi * safe_norm * safe_modulus)
    return jnp.where(excluded, 0.0, result)

def tile_field(own_static, near_static, near_dipole, box_spans):
    listed_count = near_static.shape[0]
    tile_width = own_static.shape[1]
    box_span = jnp.array(box_spans, dtype=jnp.float32)[None, :, None, None]
    separation = near_static[:, 0:3, None, :] - own_static[None, 0:3, :, None]
    separation = separation - box_span * jnp.floor(separation / box_span + 0.5)
    dist_sq = lax.optimization_barrier(jnp.sum(separation * separation, axis=1))
    itself = (jnp.arange(listed_count)[:, None, None] == 0) & (jnp.arange(tile_width)[:, None] == jnp.arange(tile_width)[None, :])[None]
    safe_sq = jnp.where(itself, 1.0, dist_sq)
    distance = jnp.sqrt(safe_sq)
    scaled = distance / (own_static[3][None, :, None] * near_static[:, 3][:, None, :])
    cubed = thole_a * scaled * scaled * scaled
    damping = jnp.exp(-cubed)
    screen = lax.erfc(ewald_beta * distance)
    gaussian = 2.0 * ewald_beta / math.sqrt(math.pi) * jnp.exp(-(ewald_beta * ewald_beta) * safe_sq)
    inverse_sq = 1.0 / safe_sq
    inverse_cube = inverse_sq / distance
    first_term = (screen - damping) * inverse_cube + gaussian * inverse_sq
    second = 3.0 * (screen - (1.0 + cubed) * damping) * inverse_cube * inverse_sq + gaussian * (2.0 * ewald_beta * ewald_beta + 3.0 * inverse_sq) * inverse_sq
    first_term = jnp.where(itself, 0.0, first_term)
    second = jnp.where(itself, 0.0, second)
    projected = lax.optimization_barrier(jnp.sum(near_dipole[:, :, :, None, :] * separation[:, None, :, :, :], axis=2))
    weighted = second[:, None] * projected
    outward = lax.optimization_barrier(jnp.sum(weighted[:, :, None] * separation[:, None], axis=(0, 4)))
    inward = lax.optimization_barrier(jnp.sum(first_term[:, None, None] * near_dipole[:, :, :, None, :], axis=(0, 4)))
    return outward - inward

def neighbour_stack(source):
    pieces = []
    for row_step in range(3):
        for col_step in range(3):
            pieces.append(jnp.roll(jnp.roll(source, 1 - row_step, axis=0), 1 - col_step, axis=1))
    return jnp.stack(pieces, axis=2)

def direct_field(dipoles_all, statics_all, tile_lists, box_spans):
    brick_rows, brick_cols = (statics_all.shape[0], statics_all.shape[1])
    tile_count = statics_all.shape[-1] // TILE
    near_dip = neighbour_stack(dipoles_all).reshape(brick_rows, brick_cols, 9, RHS, 3, tile_count, TILE)
    near_dip = jnp.moveaxis(near_dip, 5, 3).reshape(brick_rows, brick_cols, 9 * tile_count, RHS, 3, TILE)
    near_stat = neighbour_stack(statics_all).reshape(brick_rows, brick_cols, 9, 4, tile_count, TILE)
    near_stat = jnp.moveaxis(near_stat, 4, 3).reshape(brick_rows, brick_cols, 9 * tile_count, 4, TILE)
    own_stat = jnp.moveaxis(statics_all.reshape(brick_rows, brick_cols, 4, tile_count, TILE), 3, 2)

    def per_tile(flat_index):
        brick_index = flat_index // tile_count
        tile_pos = flat_index % tile_count
        row_pos = brick_index // brick_cols
        col_pos = brick_index % brick_cols
        picked = tile_lists[row_pos, col_pos, tile_pos]
        return tile_field(own_stat[row_pos, col_pos, tile_pos], near_stat[row_pos, col_pos][picked], near_dip[row_pos, col_pos][picked], box_spans)
    fields = lax.map(per_tile, jnp.arange(brick_rows * brick_cols * tile_count, dtype=jnp.int32))
    fields = fields.reshape(brick_rows, brick_cols, tile_count, RHS, 3, TILE)
    return jnp.moveaxis(fields, 2, 4).reshape(brick_rows, brick_cols, RHS, 3, tile_count * TILE)

def stencil_tables(positions, grid_base):
    lengths = jnp.array([KX, KY, KZ], dtype=jnp.int32)[:, None]
    base_flat = jnp.moveaxis(grid_base, 2, 0).reshape(3, -1)
    place_flat = jnp.moveaxis(positions, 2, 0).reshape(3, -1)
    cell_index = (base_flat + 2) % lengths
    fraction = place_flat - cell_index.astype(jnp.float32)
    values, slopes = spline_table(fraction)
    grid_index = jnp.stack([(base_flat + stencil) % lengths for stencil in range(5)])
    return (values, slopes, grid_index)

def stencil_weights(values, slopes, step_x, step_y, step_z):
    weight_x = slopes[step_x, 0] * values[step_y, 1] * values[step_z, 2]
    weight_y = values[step_x, 0] * slopes[step_y, 1] * values[step_z, 2]
    weight_z = values[step_x, 0] * values[step_y, 1] * slopes[step_z, 2]
    return (weight_x, weight_y, weight_z)

def spread_charges(dipole_flat, tables):
    values, slopes, grid_index = tables
    charge_grid = jnp.zeros((RHS, KX, KY, KZ), jnp.float32)
    for step_x in range(5):
        for step_y in range(5):
            for step_z in range(5):
                weight_x, weight_y, weight_z = stencil_weights(values, slopes, step_x, step_y, step_z)
                charge = dipole_flat[:, 0] * weight_x + dipole_flat[:, 1] * weight_y + dipole_flat[:, 2] * weight_z
                charge_grid = charge_grid.at[:, grid_index[step_x, 0], grid_index[step_y, 1], grid_index[step_z, 2]].add(charge)
    return charge_grid

def sample_field(potential, tables):
    values, slopes, grid_index = tables
    field_x = jnp.zeros((RHS, values.shape[-1]), jnp.float32)
    field_y = jnp.zeros((RHS, values.shape[-1]), jnp.float32)
    field_z = jnp.zeros((RHS, values.shape[-1]), jnp.float32)
    for step_x in range(5):
        for step_y in range(5):
            for step_z in range(5):
                weight_x, weight_y, weight_z = stencil_weights(values, slopes, step_x, step_y, step_z)
                sample = potential[:, grid_index[step_x, 0], grid_index[step_y, 1], grid_index[step_z, 2]]
                field_x = field_x + sample * weight_x
                field_y = field_y + sample * weight_y
                field_z = field_z + sample * weight_z
    return jnp.stack([field_x, field_y, field_z], axis=1)

def reciprocal(charge_grid):
    wave_x = jnp.arange(KX, dtype=jnp.int32)[:, None, None]
    wave_y = jnp.arange(KY, dtype=jnp.int32)[None, :, None]
    wave_z = jnp.arange(KZ, dtype=jnp.int32)[None, None, :]
    kernel = influence(wave_x, wave_y, wave_z, KX, KY, KZ)
    spectrum = jnp.fft.fftn(charge_grid, axes=(1, 2, 3))
    return jnp.real(jnp.fft.ifftn(spectrum * kernel[None], axes=(1, 2, 3))).astype(jnp.float32)

def reference(field_rhs, positions, polar, grid_base, tile_lists):
    brick_rows, brick_cols = (polar.shape[0], polar.shape[1])
    atom_count = polar.shape[2]
    box_spans = (float(KX), float(KY), float(KZ))
    tables = stencil_tables(positions, grid_base)
    root_scale = jnp.power(polar, 1.0 / 6.0)
    statics_all = jnp.concatenate([positions, root_scale[:, :, None, :]], axis=2)
    polar_wide = polar[:, :, None, None, :]

    def flatten(field):
        return jnp.moveaxis(field, (2, 3), (0, 1)).reshape(RHS, 3, -1)

    def unflatten(flat):
        return jnp.moveaxis(flat.reshape(RHS, 3, brick_rows, brick_cols, atom_count), (0, 1), (2, 3))

    def operate(direction):
        potential = reciprocal(spread_charges(flatten(direction), tables))
        recip_part = unflatten(sample_field(potential, tables))
        direct = direct_field(direction, statics_all, tile_lists, box_spans)
        return direction / polar_wide - direct + recip_part - self_coef * direction

    def inner_sum(left_arr, right_arr):
        return lax.optimization_barrier(jnp.sum(left_arr * right_arr, axis=(0, 1, 3, 4)))
    solution = jnp.zeros_like(field_rhs)
    residual = field_rhs
    scaled_res = polar_wide * residual
    direction = scaled_res
    progress = inner_sum(residual, scaled_res)
    for iteration in range(ITERS):
        image_field = operate(direction)
        step_size = (progress / inner_sum(direction, image_field))[None, None, :, None, None]
        solution = solution + step_size * direction
        residual = residual - step_size * image_field
        scaled_res = polar_wide * residual
        progress_next = inner_sum(residual, scaled_res)
        direction = scaled_res + (progress_next / progress)[None, None, :, None, None] * direction
        progress = progress_next
    return (solution, residual)
```

```python
import math

import jax
import jax.numpy as jnp
import ml_dtypes
import numpy as np
from jax import lax
from jax.experimental import pallas as pl
from jax.experimental.pallas import tpu as pltpu
from jax.sharding import PartitionSpec as P

CX = 8
CY = 4
KZ = 256
TILE = 128
RHS = 2
ITERS = 2


ewald_beta = 0.4
thole_a = 0.39
self_coef = 4.0 * ewald_beta**3 / (3.0 * math.sqrt(math.pi))
highest = lax.Precision.HIGHEST


def with_halo(cells, sides, width):
    for axis, dim in sides:
        count = lax.axis_size(axis)
        head = lax.slice_in_dim(cells, 0, width, axis=dim)
        tail = lax.slice_in_dim(cells, cells.shape[dim] - width, cells.shape[dim], axis=dim)
        cells = jnp.concatenate(
            [
                lax.ppermute(tail, axis, [(i, (i + 1) % count) for i in range(count)]),
                cells,
                lax.ppermute(head, axis, [((i + 1) % count, i) for i in range(count)]),
            ],
            axis=dim,
        )
    return cells


def spline_table(fraction):
    previous = {0: jnp.ones_like(fraction)}
    fourth = previous
    for degree in range(2, 6):
        current = {}
        for offset in range(degree):
            abscissa = fraction + offset
            summed = abscissa * previous.get(offset, 0.0) + (degree - abscissa) * previous.get(
                offset - 1, 0.0
            )
            current[offset] = summed / (degree - 1)
        if degree == 4:
            fourth = current
        previous = current
    values = jnp.stack([previous[4 - stencil] for stencil in range(5)])
    slopes = jnp.stack(
        [fourth.get(4 - stencil, 0.0) - fourth.get(3 - stencil, 0.0) for stencil in range(5)]
    )
    return (values, slopes)


def spline_modulus(wave_index, length):
    spline_coef = (1.0 / 24.0, 11.0 / 24.0, 11.0 / 24.0, 1.0 / 24.0)
    cosine_sum = jnp.zeros(wave_index.shape, jnp.float32)
    sine_sum = jnp.zeros(wave_index.shape, jnp.float32)
    for offset in range(4):
        angles = 2.0 * math.pi / length * (wave_index * offset % length).astype(jnp.float32)
        cosine_sum = cosine_sum + spline_coef[offset] * jnp.cos(angles)
        sine_sum = sine_sum + spline_coef[offset] * jnp.sin(angles)
    return cosine_sum * cosine_sum + sine_sum * sine_sum


def folded_square(wave_index, length):
    nearest = jnp.minimum(wave_index, length - wave_index).astype(jnp.float32) / length
    return nearest * nearest


def influence(wave_x, wave_y, wave_z, length_x, length_y, length_z):
    wave_norm = (
        folded_square(wave_x, length_x)
        + folded_square(wave_y, length_y)
        + folded_square(wave_z, length_z)
    )
    modulus = (
        spline_modulus(wave_x, length_x)
        * spline_modulus(wave_y, length_y)
        * spline_modulus(wave_z, length_z)
    )
    excluded = (wave_x * 2 == length_x) | (wave_y * 2 == length_y) | (wave_z * 2 == length_z)
    excluded = excluded | (wave_x == 0) & (wave_y == 0) & (wave_z == 0)
    safe_norm = jnp.where(excluded, 1.0, wave_norm)
    safe_modulus = jnp.where(excluded, 1.0, modulus)
    result = jnp.exp(-(math.pi**2 / ewald_beta**2) * safe_norm) / (
        math.pi * safe_norm * safe_modulus
    )
    return jnp.where(excluded, 0.0, result)


def tile_field(own_static, near_static, near_dipole, box_spans):
    listed_count = near_static.shape[0]
    tile_width = own_static.shape[1]
    box_span = jnp.array(box_spans, dtype=jnp.float32)[None, :, None, None]
    separation = near_static[:, 0:3, None, :] - own_static[None, 0:3, :, None]
    separation = separation - box_span * jnp.floor(separation / box_span + 0.5)
    dist_sq = jnp.sum(separation * separation, axis=1)
    itself = (jnp.arange(listed_count)[:, None, None] == 0) & (
        jnp.arange(tile_width)[:, None] == jnp.arange(tile_width)[None, :]
    )[None]
    safe_sq = jnp.where(itself, 1.0, dist_sq)
    distance = jnp.sqrt(safe_sq)
    scaled = distance / (own_static[3][None, :, None] * near_static[:, 3][:, None, :])
    cubed = thole_a * scaled * scaled * scaled
    damping = jnp.exp(-cubed)
    screen = lax.erfc(ewald_beta * distance)
    gaussian = 2.0 * ewald_beta / math.sqrt(math.pi) * jnp.exp(-(ewald_beta * ewald_beta) * safe_sq)
    inverse_sq = 1.0 / safe_sq
    inverse_cube = inverse_sq / distance
    first_term = (screen - damping) * inverse_cube + gaussian * inverse_sq
    second = (
        3.0 * (screen - (1.0 + cubed) * damping) * inverse_cube * inverse_sq
        + gaussian * (2.0 * ewald_beta * ewald_beta + 3.0 * inverse_sq) * inverse_sq
    )
    first_term = jnp.where(itself, 0.0, first_term)
    second = jnp.where(itself, 0.0, second)
    projected = jnp.sum(near_dipole[:, :, :, None, :] * separation[:, None, :, :, :], axis=2)
    weighted = second[:, None] * projected
    outward = jnp.sum(weighted[:, :, None] * separation[:, None], axis=(0, 4))
    inward = jnp.sum(first_term[:, None, None] * near_dipole[:, :, :, None, :], axis=(0, 4))
    return outward - inward


def hartley(length):
    counter = jnp.arange(length, dtype=jnp.int32)
    angles = (
        2.0 * math.pi / length * (counter[:, None] * counter[None, :] % length).astype(jnp.float32)
    )
    return jnp.cos(angles) + jnp.sin(angles)


def placed_table(first_cell, weights, extent):
    slot_index = jnp.arange(extent, dtype=jnp.int32)[:, None]
    placed = jnp.zeros((extent, first_cell.shape[0]), jnp.float32)
    for stencil in range(5):
        placed = placed + jnp.where(
            slot_index == (first_cell[None, :] + stencil) % extent, weights[stencil][None, :], 0.0
        )
    return placed


def pad_axis(source, axis_pos, leading, trailing):
    widths = [(0, 0)] * source.ndim
    widths[axis_pos] = (leading, trailing)
    return jnp.pad(source, widths)


def fold_cycle(cycle_only, axis_pos, inner_len):
    middle = lax.slice_in_dim(cycle_only, 4, inner_len + 4, axis=axis_pos)
    lower_cycle = lax.slice_in_dim(cycle_only, 0, 2, axis=axis_pos)
    upper_cycle = lax.slice_in_dim(cycle_only, inner_len + 6, inner_len + 8, axis=axis_pos)
    return (
        middle
        + pad_axis(lower_cycle, axis_pos, 0, inner_len - 2)
        + pad_axis(upper_cycle, axis_pos, inner_len - 2, 0)
    )


def clear_inside(extended, extents):
    inside = None
    for axis_pos, inner_len in extents:
        slot_index = lax.broadcasted_iota(jnp.int32, extended.shape, axis_pos)
        within = (slot_index >= 2) & (slot_index < inner_len + 6)
        inside = within if inside is None else inside & within
    return jnp.where(inside, 0.0, extended)


def inner_sum(left_arr, right_arr):
    return lax.psum(jnp.sum(left_arr * right_arr, axis=(1, 2)), ("row", "col"))


def pencil_local(field_rhs, positions, polar, grid_base, tile_lists):
    rows_count = lax.axis_size("row")
    cols_count = lax.axis_size("col")
    grid_x = CX * rows_count
    grid_y = CY * cols_count
    atom_count = polar.shape[-1]
    tile_count = atom_count // TILE
    slab_depth = KZ // tile_count
    window_len = slab_depth + 4
    box_spans = (float(grid_x), float(grid_y), float(KZ))
    own_place = positions[0, 0]
    own_base = grid_base[0, 0]
    own_polar = polar[0, 0]
    lengths = jnp.array([grid_x, grid_y, KZ], dtype=jnp.int32)[:, None]
    cell_index = (own_base + 2) % lengths
    fraction = own_place - cell_index.astype(jnp.float32)
    values, slopes = spline_table(fraction)
    first_x = (own_base[0] - lax.axis_index("row") * CX + 2) % grid_x
    first_y = (own_base[1] - lax.axis_index("col") * CY + 2) % grid_y
    rows_x = placed_table(first_x, values[:, 0], CX + 4)
    slope_x = placed_table(first_x, slopes[:, 0], CX + 4)
    rows_y = placed_table(first_y, values[:, 1], CY + 4)
    slope_y = placed_table(first_y, slopes[:, 1], CY + 4)
    tile_start = jnp.arange(atom_count, dtype=jnp.int32) // TILE * slab_depth
    first_z = (own_base[2] + 2 - tile_start) % KZ
    rows_z = placed_table(first_z, values[:, 2], window_len)
    slope_z = placed_table(first_z, slopes[:, 2], window_len)
    plane_count = (CX + 4) * (CY + 4)
    plane_dx = (slope_x[:, None, :] * rows_y[None, :, :]).reshape(plane_count, atom_count)
    plane_dy = (rows_x[:, None, :] * slope_y[None, :, :]).reshape(plane_count, atom_count)
    plane_flat = (rows_x[:, None, :] * rows_y[None, :, :]).reshape(plane_count, atom_count)
    window_rows = jnp.moveaxis(rows_z.reshape(window_len, tile_count, TILE), 1, 0)
    window_slope = jnp.moveaxis(slope_z.reshape(window_len, tile_count, TILE), 1, 0)
    depth_table = jnp.concatenate([window_rows, window_slope], axis=2)
    grid_scale = 1.0 / (grid_x * grid_y * KZ)
    hartley_x = hartley(grid_x)
    hartley_y = hartley(grid_y)
    hartley_z = hartley(KZ)
    block_y = grid_y // rows_count
    block_z = KZ // cols_count
    wave_x = jnp.arange(grid_x, dtype=jnp.int32)[:, None, None]
    wave_y = (lax.axis_index("row") * block_y + jnp.arange(block_y, dtype=jnp.int32))[None, :, None]
    wave_z = (lax.axis_index("col") * block_z + jnp.arange(block_z, dtype=jnp.int32))[None, None, :]
    kernel = influence(wave_x, wave_y, wave_z, grid_x, grid_y, KZ) * grid_scale
    root_scale = jnp.power(own_polar, 1.0 / 6.0)
    own_static = jnp.concatenate([own_place, root_scale[None]], axis=0)
    near_static = with_halo(own_static[None, None], (("row", 0), ("col", 1)), 1)
    near_static = jnp.moveaxis(near_static.reshape(9, 4, tile_count, TILE), 2, 1).reshape(
        9 * tile_count, 4, TILE
    )
    own_tiles = jnp.moveaxis(own_static.reshape(4, tile_count, TILE), 1, 0)
    own_lists = tile_lists[0, 0]
    polar_wide = own_polar[None, None, :]
    solution = jnp.zeros_like(field_rhs[0, 0])
    residual = field_rhs[0, 0]
    scaled_res = polar_wide * residual
    direction = scaled_res
    progress = inner_sum(residual, scaled_res)
    for iteration in range(ITERS):
        near_dip = with_halo(direction[None, None], (("row", 0), ("col", 1)), 1)
        near_dip = jnp.moveaxis(near_dip.reshape(9, RHS, 3, tile_count, TILE), 3, 1).reshape(
            9 * tile_count, RHS, 3, TILE
        )

        def one_tile(tile_pos):
            picked = own_lists[tile_pos]
            return tile_field(own_tiles[tile_pos], near_static[picked], near_dip[picked], box_spans)

        fields = lax.map(one_tile, jnp.arange(tile_count, dtype=jnp.int32))
        direct = jnp.moveaxis(fields, 0, 2).reshape(RHS, 3, atom_count)
        slope_terms = (
            direction[:, 0, None, :] * plane_dx[None] + direction[:, 1, None, :] * plane_dy[None]
        )
        flat_terms = direction[:, 2, None, :] * plane_flat[None]
        spread_left = jnp.concatenate(
            [
                slope_terms.reshape(RHS, plane_count, tile_count, TILE),
                flat_terms.reshape(RHS, plane_count, tile_count, TILE),
            ],
            axis=3,
        )
        spread_windows = jnp.einsum("sptb,twb->sptw", spread_left, depth_table, precision=highest)
        main_part = spread_windows[..., :slab_depth].reshape(spread_windows.shape[:-2] + (KZ,))
        tail_part = pad_axis(
            spread_windows[..., slab_depth:], spread_windows.ndim - 1, 0, slab_depth - 4
        )
        tail_part = tail_part.reshape(spread_windows.shape[:-2] + (KZ,))[..., : KZ + 4 - slab_depth]
        last_axis = main_part.ndim - 1
        padded_line = pad_axis(main_part, last_axis, 0, 4) + pad_axis(
            tail_part, last_axis, slab_depth, 0
        )
        inner = padded_line[..., 2 : KZ + 2]
        spread_tile = (
            inner
            + pad_axis(padded_line[..., 0:2], last_axis, KZ - 2, 0)
            + pad_axis(padded_line[..., KZ + 2 : KZ + 4], last_axis, 0, KZ - 2)
        ).reshape(RHS, CX + 4, CY + 4, KZ)
        extended = with_halo(spread_tile, (("row", 1), ("col", 2)), 2)
        cycle_only = clear_inside(extended, ((1, CX), (2, CY)))
        folded = fold_cycle(fold_cycle(cycle_only, 1, CX), 2, CY)
        spectrum = jnp.einsum(
            "sxyz,zk->sxyk",
            spread_tile[:, 2 : CX + 2, 2 : CY + 2] + folded,
            hartley_z,
            precision=highest,
        )
        along_y = jnp.einsum(
            "sxyz,yk->sxkz",
            lax.all_to_all(spectrum, "col", split_axis=3, concat_axis=2, tiled=True),
            hartley_y,
            precision=highest,
        )
        along_x = (
            jnp.einsum(
                "sxyz,xk->skyz",
                lax.all_to_all(along_y, "row", split_axis=2, concat_axis=1, tiled=True),
                hartley_x,
                precision=highest,
            )
            * kernel[None]
        )
        mixed_part = jnp.einsum("sxyz,xk->skyz", along_x, hartley_x, precision=highest)
        returned = lax.all_to_all(mixed_part, "row", split_axis=1, concat_axis=2, tiled=True)
        swapped = jnp.einsum("sxyz,yk->sxkz", returned, hartley_y, precision=highest)
        restored = lax.all_to_all(swapped, "col", split_axis=2, concat_axis=3, tiled=True)
        padded = with_halo(
            jnp.einsum("sxyz,zk->sxyk", restored, hartley_z, precision=highest),
            (("row", 1), ("col", 2)),
            2,
        )
        line = padded.reshape(RHS, plane_count, KZ)
        extended_line = jnp.concatenate([line[..., KZ - 2 :], line, line[..., :2]], axis=-1)
        windows = jnp.stack(
            [
                extended_line[..., tile * slab_depth : tile * slab_depth + window_len]
                for tile in range(tile_count)
            ],
            axis=-2,
        )
        sampled = jnp.einsum("sptw,twb->sptb", windows, depth_table, precision=highest)
        with_flat = sampled[..., :TILE].reshape(RHS, plane_count, atom_count)
        with_slope = sampled[..., TILE:].reshape(RHS, plane_count, atom_count)
        recip_part = jnp.stack(
            [
                jnp.sum(with_flat * plane_dx[None], axis=1),
                jnp.sum(with_flat * plane_dy[None], axis=1),
                jnp.sum(with_slope * plane_flat[None], axis=1),
            ],
            axis=1,
        )
        image_field = direction / polar_wide - direct + recip_part - self_coef * direction
        step_size = (progress / inner_sum(direction, image_field))[:, None, None]
        solution = solution + step_size * direction
        residual = residual - step_size * image_field
        scaled_res = polar_wide * residual
        progress_next = inner_sum(residual, scaled_res)
        direction = scaled_res + (progress_next / progress)[:, None, None] * direction
        progress = progress_next
    return (solution[None, None], residual[None, None])


X_PAD = CX + 4
Y_PAD = CY + 4
SLOT_ROWS = 16
PAIR_ROWS = 16
SCREEN_SCALE = 0.4
SCREEN_COEF = (
    0.22567588090896606,
    0.2256690263748169,
    0.20785020291805267,
    0.16849851608276367,
    0.14156343042850494,
    -0.005832736846059561,
    0.16930203139781952,
    -0.1830107867717743,
    0.05028456076979637,
)


def halves(value):
    high = value.astype(jnp.bfloat16)
    return high, (value - high.astype(jnp.float32)).astype(jnp.bfloat16)


def halves_np(value):
    value = value.astype(np.float32)
    high = value.astype(ml_dtypes.bfloat16)
    return high, (value - high.astype(np.float32)).astype(ml_dtypes.bfloat16)


def product(left, right, left_dim=1, right_dim=0):
    def one(first, second):
        return lax.dot_general(
            first,
            second,
            (((left_dim,), (right_dim,)), ((), ())),
            preferred_element_type=jnp.float32,
        )

    return one(left[0], right[0]) + (one(left[1], right[0]) + one(left[0], right[1]))


def cas_np(wave, place, length):
    angles = 2.0 * np.pi / length * (wave[:, None] * place[None, :] % length)
    return np.cos(angles) + np.sin(angles)


def modulus_np(wave, length):
    coef = np.array([1.0, 11.0, 11.0, 1.0]) / 24.0
    angles = 2.0 * np.pi / length * (wave[:, None] * np.arange(4)[None, :])
    return (coef * np.cos(angles)).sum(1) ** 2 + (coef * np.sin(angles)).sum(1) ** 2


def influence_np(length_x, length_y, length_z):
    total = np.zeros((length_x, length_y, length_z))
    modulus = np.ones((length_x, length_y, length_z))
    excluded = np.zeros((length_x, length_y, length_z), bool)
    for axis, length in enumerate((length_x, length_y, length_z)):
        wave = np.arange(length)
        shape = [1, 1, 1]
        shape[axis] = length
        total = total + ((np.minimum(wave, length - wave) / length) ** 2).reshape(shape)
        modulus = modulus * modulus_np(wave, length).reshape(shape)
        excluded = excluded | (wave * 2 == length).reshape(shape)
    excluded[0, 0, 0] = True
    safe = np.where(excluded, 1.0, total)
    result = np.exp(-(np.pi**2) / ewald_beta**2 * safe) / (
        np.pi * safe * np.where(excluded, 1.0, modulus)
    )
    return np.where(excluded, 0.0, result) / (length_x * length_y * length_z)


def slab_tables(rows_count, cols_count):
    grid_x = CX * rows_count
    grid_y = CY * cols_count
    devices = rows_count * cols_count
    chunk = KZ // devices
    wave_z = (np.arange(devices)[None, :] * chunk + np.arange(chunk)[:, None]).reshape(-1)
    along_z = cas_np(wave_z, np.arange(KZ), KZ)
    place_x = np.arange(rows_count)[:, None] * CX + np.arange(X_PAD)[None, :] - 2
    along_x = cas_np(np.arange(grid_x), place_x.reshape(-1) % grid_x, grid_x)
    padded_x = np.zeros((grid_x, rows_count, SLOT_ROWS))
    padded_x[:, :, :X_PAD] = along_x.reshape(grid_x, rows_count, X_PAD)
    padded_x = padded_x.reshape(grid_x, rows_count * SLOT_ROWS)
    x_high, x_low = halves_np(padded_x)
    forward_x = np.concatenate([x_high, x_low, x_high], axis=1)
    backward_x = np.concatenate([x_high.T, x_low.T, x_high.T], axis=1)
    place_y = (np.arange(cols_count)[:, None] * CY + np.arange(Y_PAD)[None, :] - 2) % grid_y
    along_y = cas_np(np.arange(grid_y), place_y.reshape(-1), grid_y)
    along_y = along_y.reshape(grid_y, cols_count, Y_PAD)
    units = chunk * RHS
    block = np.einsum("uv,kcy->cuyvk", np.eye(units), along_y)
    block = block.reshape(cols_count * units * Y_PAD, units * grid_y)
    kernel = influence_np(grid_x, grid_y, KZ).reshape(grid_x, grid_y, devices, chunk)
    kernel = np.transpose(kernel, (2, 0, 3, 1))[:, :, :, None, :]
    kernel = np.broadcast_to(kernel, (devices, grid_x, chunk, RHS, grid_y))
    kernel = kernel.reshape(devices, grid_x, units * grid_y).astype(np.float32)
    return dict(
        along_z=halves_np(along_z),
        forward_x=forward_x,
        backward_x=backward_x,
        block=halves_np(block),
        block_back=halves_np(np.ascontiguousarray(block.T)),
        kernel=kernel,
    )


def pack_body(rhs_ref, place_ref, polar_ref, start_ref, payload_ref):
    polar = polar_ref[...]
    start = rhs_ref[...] * polar
    start_ref[...] = start
    everything = jnp.concatenate([place_ref[...], 1.0 / jnp.sqrt(polar), start], axis=0)
    store_payload(payload_ref, everything)


def store_payload(payload_ref, everything):
    tile_count = everything.shape[1] // TILE
    for quantity in range(everything.shape[0]):
        for tile in range(tile_count):
            row = quantity * tile_count + tile
            payload_ref[row : row + 1, :] = everything[
                quantity : quantity + 1, tile * TILE : (tile + 1) * TILE
            ]


def placed_rows(slot, weights, extent):
    slot_index = lax.broadcasted_iota(jnp.int32, (extent, slot.shape[1]), 0)
    placed = jnp.zeros((extent, slot.shape[1]), jnp.float32)
    for stencil in range(5):
        target = slot + stencil
        if extent == KZ:
            target = jnp.where(target >= KZ, target - KZ, target)
        placed = placed + jnp.where(slot_index == target, weights[stencil], 0.0)
    return placed


def spread_into(message_ref, moment, rows_x, slope_x, rows_y, slope_y, depth, devices):
    blocks = []
    for step in range(X_PAD):
        flat_x = rows_x[step : step + 1]
        tilt_x = slope_x[step : step + 1]
        for rhs in range(RHS):
            part_x = tilt_x * moment[3 * rhs : 3 * rhs + 1]
            part_y = flat_x * moment[3 * rhs + 1 : 3 * rhs + 2]
            part_z = flat_x * moment[3 * rhs + 2 : 3 * rhs + 3]
            blocks.append(
                jnp.concatenate([part_x * rows_y + part_y * slope_y, part_z * rows_y], axis=1)
            )
    charges = jnp.concatenate(blocks, axis=0)
    spectrum = product(depth, halves(charges), 1, 1)
    chunk = KZ // devices
    width = RHS * Y_PAD
    for step in range(X_PAD):
        message_ref[pl.ds(step, devices, stride=SLOT_ROWS), :] = jnp.concatenate(
            [
                spectrum[unit * devices : (unit + 1) * devices, step * width : (step + 1) * width]
                for unit in range(chunk)
            ],
            axis=1,
        )


def sample_from(message_ref, rows_x, slope_x, rows_y, slope_y, depth, devices):
    chunk = KZ // devices
    width = RHS * Y_PAD
    pieces = [
        message_ref[pl.ds(step, devices, stride=SLOT_ROWS), :] for step in range(X_PAD)
    ]
    spare = jnp.zeros((devices, KZ - X_PAD * width), jnp.float32)
    spectrum = jnp.concatenate(
        [
            jnp.concatenate(
                [piece[:, unit * width : (unit + 1) * width] for piece in pieces] + [spare], axis=1
            )
            for unit in range(chunk)
        ],
        axis=0,
    )
    spectrum = jnp.transpose(spectrum)[: X_PAD * width]
    sampled = product(halves(spectrum), depth, 1, 0)
    atoms = rows_x.shape[1]
    fields = []
    for rhs in range(RHS):
        sum_x = sum_y = sum_z = None
        for step in range(X_PAD):
            first = step * width + rhs * Y_PAD
            flat = sampled[first : first + Y_PAD, :atoms]
            tilt = sampled[first : first + Y_PAD, atoms:]
            part_x = slope_x[step : step + 1] * flat
            part_y = rows_x[step : step + 1] * flat
            part_z = rows_x[step : step + 1] * tilt
            sum_x = part_x if sum_x is None else sum_x + part_x
            sum_y = part_y if sum_y is None else sum_y + part_y
            sum_z = part_z if sum_z is None else sum_z + part_z
        fields.append(jnp.sum(sum_x * rows_y, axis=0, keepdims=True))
        fields.append(jnp.sum(sum_y * slope_y, axis=0, keepdims=True))
        fields.append(jnp.sum(sum_z * rows_y, axis=0, keepdims=True))
    return jnp.concatenate(fields, axis=0)


def read_tables(tables_ref):
    return (
        tables_ref[0:X_PAD],
        tables_ref[SLOT_ROWS : SLOT_ROWS + X_PAD],
        tables_ref[2 * SLOT_ROWS : 2 * SLOT_ROWS + Y_PAD],
        tables_ref[2 * SLOT_ROWS + Y_PAD : 2 * SLOT_ROWS + 2 * Y_PAD],
    )


def clear_spare(message_ref, devices):
    spare = jnp.zeros((devices, message_ref.shape[1]), jnp.float32)
    for step in range(X_PAD, SLOT_ROWS):
        message_ref[pl.ds(step, devices, stride=SLOT_ROWS), :] = spare


def setup_body(
    lengths,
    devices,
    place_ref,
    base_ref,
    start_ref,
    z_high_ref,
    z_low_ref,
    message_ref,
    tables_ref,
    depth_high_ref,
    depth_low_ref,
):
    base = base_ref[...]
    fractions = []
    cells = []
    for dim in range(3):
        cell = base[dim : dim + 1] + 2
        cell = jnp.where(cell >= lengths[dim], cell - lengths[dim], cell)
        cells.append(cell)
        fractions.append(place_ref[dim : dim + 1, :] - cell.astype(jnp.float32))
    values, slopes = spline_table(jnp.concatenate(fractions, axis=0))
    values = [[values[stencil][dim : dim + 1] for stencil in range(5)] for dim in range(3)]
    slopes = [[slopes[stencil][dim : dim + 1] for stencil in range(5)] for dim in range(3)]
    slot_x = lax.rem(cells[0], CX)
    slot_y = lax.rem(cells[1], CY)
    tables_ref[0:SLOT_ROWS] = placed_rows(slot_x, values[0], SLOT_ROWS)
    tables_ref[SLOT_ROWS : 2 * SLOT_ROWS] = placed_rows(slot_x, slopes[0], SLOT_ROWS)
    tables_ref[2 * SLOT_ROWS : 2 * SLOT_ROWS + Y_PAD] = placed_rows(slot_y, values[1], Y_PAD)
    tables_ref[2 * SLOT_ROWS + Y_PAD : 2 * SLOT_ROWS + 2 * Y_PAD] = placed_rows(
        slot_y, slopes[1], Y_PAD
    )
    window = jnp.concatenate(
        [
            placed_rows(base[2:3], values[2], KZ),
            placed_rows(base[2:3], slopes[2], KZ),
        ],
        axis=1,
    )
    depth = product((z_high_ref[...], z_low_ref[...]), halves(window), 1, 0)
    depth = halves(depth)
    depth_high_ref[...] = depth[0]
    depth_low_ref[...] = depth[1]
    spread_into(message_ref, start_ref[...], *read_tables(tables_ref), depth, devices)
    clear_spare(message_ref, devices)


def transform_in(message_ref, forward_ref, block_high_ref, block_low_ref, rows_count, cols_count):
    gathered = jnp.concatenate(
        [
            jnp.concatenate(
                [
                    message_ref[(r * cols_count + c) * SLOT_ROWS :][:SLOT_ROWS]
                    for r in range(rows_count)
                ],
                axis=0,
            )
            for c in range(cols_count)
        ],
        axis=1,
    )
    high, low = halves(gathered)
    along = jnp.dot(
        forward_ref[...],
        jnp.concatenate([high, high, low], axis=0),
        preferred_element_type=jnp.float32,
    )
    return product(halves(along), (block_high_ref[...], block_low_ref[...]))


def transform_out(result_ref, values, backward_ref, block_high_ref, block_low_ref, counts):
    rows_count, cols_count = counts
    spread = product(halves(values), (block_high_ref[...], block_low_ref[...]))
    high, low = halves(spread)
    along = jnp.dot(
        backward_ref[...],
        jnp.concatenate([high, high, low], axis=0),
        preferred_element_type=jnp.float32,
    )
    width = along.shape[1] // cols_count
    for r in range(rows_count):
        for c in range(cols_count):
            first = (r * cols_count + c) * SLOT_ROWS
            result_ref[first : first + SLOT_ROWS, :] = along[
                r * SLOT_ROWS : (r + 1) * SLOT_ROWS, c * width : (c + 1) * width
            ]


def middle_first_body(
    counts,
    message_ref,
    kernel_ref,
    forward_ref,
    backward_ref,
    block_high_ref,
    block_low_ref,
    back_high_ref,
    back_low_ref,
    result_ref,
    wave_ref,
):
    wave = transform_in(message_ref, forward_ref, block_high_ref, block_low_ref, *counts)
    wave_ref[...] = wave
    transform_out(
        result_ref, wave * kernel_ref[...], backward_ref, back_high_ref, back_low_ref, counts
    )


def total(value):
    return jnp.sum(jnp.sum(value, axis=0, keepdims=True), axis=1, keepdims=True)


def middle_second_body(
    counts,
    message_ref,
    kernel_ref,
    forward_ref,
    backward_ref,
    block_high_ref,
    block_low_ref,
    back_high_ref,
    back_low_ref,
    wave_ref,
    rhs_ref,
    start_ref,
    image_ref,
    second_ref,
    near_ref,
    polar_ref,
    result_ref,
):
    wave = transform_in(message_ref, forward_ref, block_high_ref, block_low_ref, *counts)
    filtered = wave * kernel_ref[...]
    transform_out(result_ref, filtered, backward_ref, back_high_ref, back_low_ref, counts)
    before = wave_ref[...]
    grid_y = CY * counts[1]
    lane = lax.broadcasted_iota(jnp.int32, wave.shape, 1)
    own_rhs = lax.rem(lax.div(lane, grid_y), RHS)
    second = second_ref[...]
    local_part = second / polar_ref[...] - near_ref[0:6, :] - self_coef * second
    slot = lax.broadcasted_iota(jnp.int32, (1, result_ref.shape[1]), 1)
    sums = jnp.zeros((1, result_ref.shape[1]), jnp.float32)
    for rhs in range(RHS):
        rows = slice(3 * rhs, 3 * rhs + 3)
        start = start_ref[rows, :]
        image = image_ref[rows, :]
        mine = own_rhs == rhs
        parts = (
            total(rhs_ref[rows, :] * start),
            total(start * image),
            total(second[rows] * image),
            total(start * local_part[rows]) + total(jnp.where(mine, before * filtered, 0.0)),
            total(second[rows] * local_part[rows]) + total(jnp.where(mine, wave * filtered, 0.0)),
        )
        for index, part in enumerate(parts):
            sums = jnp.where(slot == rhs * len(parts) + index, part, sums)
    devices = counts[0] * counts[1]
    result_ref[pl.ds(X_PAD, devices, stride=SLOT_ROWS), :] = jnp.broadcast_to(
        sums, (devices, sums.shape[1])
    )


def again_body(
    devices,
    message_ref,
    tables_ref,
    depth_high_ref,
    depth_low_ref,
    start_ref,
    near_ref,
    polar_ref,
    image_ref,
    second_ref,
    payload_ref,
    result_ref,
):
    tables = read_tables(tables_ref)
    depth = (depth_high_ref[...], depth_low_ref[...])
    field = sample_from(message_ref, *tables, depth, devices)
    start = start_ref[...]
    polar = polar_ref[...]
    image = start / polar - near_ref[0:6, :] + field - self_coef * start
    second = polar * image
    image_ref[...] = image
    second_ref[...] = second
    store_payload(payload_ref, second)
    spread_into(result_ref, second, *tables, depth, devices)
    clear_spare(result_ref, devices)


def final_body(
    devices,
    message_ref,
    tables_ref,
    depth_high_ref,
    depth_low_ref,
    rhs_ref,
    start_ref,
    image_ref,
    second_ref,
    near_ref,
    polar_ref,
    dipole_ref,
    residual_ref,
):
    tables = read_tables(tables_ref)
    depth = (depth_high_ref[...], depth_low_ref[...])
    field = sample_from(message_ref, *tables, depth, devices)
    second = second_ref[...]
    image_second = second / polar_ref[...] - near_ref[0:6, :] + field - self_coef * second
    sums = jnp.sum(
        message_ref[pl.ds(X_PAD, devices, stride=SLOT_ROWS), :], axis=0, keepdims=True
    )
    for rhs in range(RHS):
        rows = slice(3 * rhs, 3 * rhs + 3)
        progress, start_image, second_image, start_next, second_next = [
            sums[:, rhs * 5 + index : rhs * 5 + index + 1] for index in range(5)
        ]
        step = progress / start_image
        progress_next = progress - 2.0 * step * start_image + step * step * second_image
        ratio = progress_next / progress
        grown = 1.0 + ratio
        curvature = (
            grown * grown * start_image
            - step * grown * (start_next + second_image)
            + step * step * second_next
        )
        step_next = progress_next / curvature
        start = start_ref[rows, :]
        image = image_ref[rows, :]
        direction = grown * start - step * second[rows]
        image_direction = grown * image - step * image_second[rows]
        dipole_ref[rows, :] = step * start + step_next * direction
        residual_ref[rows, :] = rhs_ref[rows, :] - step * image - step_next * image_direction


def near_base(entry, brick_rows):
    brick = lax.div(entry, 4)
    row_step = lax.div(brick, 3)
    col_step = lax.rem(brick, 3)
    return (col_step * 3 + row_step) * brick_rows + lax.rem(entry, 4)


def fill_near(scratch, left_ref, stack_ref, right_ref):
    rows = stack_ref.shape[0]
    scratch[0:rows, :] = left_ref[...]
    scratch[rows : 2 * rows, :] = stack_ref[...]
    scratch[2 * rows : 3 * rows, :] = right_ref[...]


def separations(near, base, tile_count, own, spans):
    result = []
    for dim in range(3):
        apart = near[pl.ds(base + dim * tile_count, 1), :] - own[dim]
        apart = apart - spans[dim] * jnp.floor(apart * (1.0 / spans[dim]) + 0.5)
        result.append(apart)
    return result


def add_field(sums, first_term, second_term, apart, near, base, tile_count, quantity):
    for rhs in range(RHS):
        moment = [
            near[pl.ds(base + (quantity + 3 * rhs + dim) * tile_count, 1), :] for dim in range(3)
        ]
        projected = moment[0] * apart[0] + moment[1] * apart[1] + moment[2] * apart[2]
        weighted = second_term * projected
        for dim in range(3):
            index = 3 * rhs + dim
            sums[index] = sums[index] + (weighted * apart[dim] - first_term * moment[dim])


def store_sums(sums, columns, rows):
    lane = lax.broadcasted_iota(jnp.int32, (PAIR_ROWS, TILE), 1)
    merged = jnp.zeros((PAIR_ROWS, TILE), jnp.float32)
    for index in range(6):
        merged = jnp.where(lane == index, jnp.sum(sums[index], axis=1, keepdims=True), merged)
    columns[rows, :] = merged


def own_columns(stack_ref, quantities, tile_count, tile, square, columns):
    offset = stack_ref.shape[0] // 3
    for quantity in range(quantities):
        square[quantity : quantity + 1, :] = stack_ref[
            pl.ds(offset + quantity * tile_count + tile, 1), :
        ]
    columns[...] = jnp.transpose(square[...])


def pair_first_body(
    first_tile,
    listed,
    tile_count,
    spans,
    lists_ref,
    left_ref,
    stack_ref,
    right_ref,
    first_ref,
    second_ref,
    field_ref,
    near,
    square,
    columns,
    out_columns,
):
    @pl.when(pl.program_id(0) == 0)
    def _():
        fill_near(near, left_ref, stack_ref, right_ref)
        square[...] = jnp.zeros_like(square)

    tile = first_tile + pl.program_id(0)
    brick_rows = stack_ref.shape[0] // 3
    own_columns(stack_ref, 4, tile_count, tile, square, columns)

    @pl.loop(0, TILE // PAIR_ROWS)
    def _(part):
        start = pl.multiple_of(part * PAIR_ROWS, PAIR_ROWS)
        rows = pl.ds(start, PAIR_ROWS)
        mine = columns[rows, :]
        own = [
            jnp.broadcast_to(mine[:, dim : dim + 1], (PAIR_ROWS, TILE)) for dim in range(4)
        ]
        own_damp = thole_a * own[3]
        sums = [jnp.zeros((PAIR_ROWS, TILE), jnp.float32) for _ in range(6)]
        itself = (
            lax.broadcasted_iota(jnp.int32, (PAIR_ROWS, TILE), 0) + start
        ) == lax.broadcasted_iota(jnp.int32, (PAIR_ROWS, TILE), 1)
        for entry in range(listed):
            base = near_base(lists_ref[tile * listed + entry], brick_rows)
            apart = separations(near, base, tile_count, own, spans)
            square_dist = apart[0] * apart[0] + apart[1] * apart[1] + apart[2] * apart[2]
            if entry == 0:
                square_dist = jnp.where(itself, 1.0, square_dist)
            inverse = lax.rsqrt(square_dist)
            distance = square_dist * inverse
            inverse_sq = inverse * inverse
            inverse_cube = inverse_sq * inverse
            damp = own_damp * near[pl.ds(base + 3 * tile_count, 1), :]
            cubed = damp * (distance * square_dist)
            damping = jnp.exp(-cubed)
            bell = jnp.exp(-(ewald_beta * ewald_beta) * square_dist)
            turned = 1.0 / (1.0 + (SCREEN_SCALE * ewald_beta) * distance)
            series = jnp.full_like(turned, SCREEN_COEF[-1])
            for coef in SCREEN_COEF[-2::-1]:
                series = series * turned + coef
            screen = bell * turned * series
            gaussian = (2.0 * ewald_beta / math.sqrt(math.pi)) * bell
            first_term = (screen - damping) * inverse_cube + gaussian * inverse_sq
            second_term = (
                3.0 * (screen - (1.0 + cubed) * damping) * inverse_cube
                + gaussian * (2.0 * ewald_beta * ewald_beta + 3.0 * inverse_sq)
            ) * inverse_sq
            if entry == 0:
                first_term = jnp.where(itself, 0.0, first_term)
                second_term = jnp.where(itself, 0.0, second_term)
            place = pl.ds(pl.multiple_of(entry * TILE + start, PAIR_ROWS), PAIR_ROWS)
            first_ref[place, :] = first_term
            second_ref[place, :] = second_term
            add_field(sums, first_term, second_term, apart, near, base, tile_count, 4)
        store_sums(sums, out_columns, rows)

    field_ref[...] = jnp.transpose(out_columns[...])[0:8]


def pair_second_body(
    first_tile,
    listed,
    tile_count,
    spans,
    lists_ref,
    left_ref,
    stack_ref,
    right_ref,
    left_moment_ref,
    stack_moment_ref,
    right_moment_ref,
    first_ref,
    second_ref,
    field_ref,
    near,
    near_moment,
    square,
    columns,
    out_columns,
):
    @pl.when(pl.program_id(0) == 0)
    def _():
        fill_near(near, left_ref, stack_ref, right_ref)
        fill_near(near_moment, left_moment_ref, stack_moment_ref, right_moment_ref)
        square[...] = jnp.zeros_like(square)

    tile = first_tile + pl.program_id(0)
    brick_rows = stack_ref.shape[0] // 3
    moment_rows = stack_moment_ref.shape[0] // 3
    own_columns(stack_ref, 3, tile_count, tile, square, columns)

    @pl.loop(0, TILE // PAIR_ROWS)
    def _(part):
        start = pl.multiple_of(part * PAIR_ROWS, PAIR_ROWS)
        rows = pl.ds(start, PAIR_ROWS)
        mine = columns[rows, :]
        own = [
            jnp.broadcast_to(mine[:, dim : dim + 1], (PAIR_ROWS, TILE)) for dim in range(3)
        ]
        sums = [jnp.zeros((PAIR_ROWS, TILE), jnp.float32) for _ in range(6)]
        for entry in range(listed):
            listing = lists_ref[tile * listed + entry]
            base = near_base(listing, brick_rows)
            apart = separations(near, base, tile_count, own, spans)
            place = pl.ds(pl.multiple_of(entry * TILE + start, PAIR_ROWS), PAIR_ROWS)
            add_field(
                sums,
                first_ref[place, :],
                second_ref[place, :],
                apart,
                near_moment,
                near_base(listing, moment_rows),
                tile_count,
                0,
            )
        store_sums(sums, out_columns, rows)

    field_ref[...] = jnp.transpose(out_columns[...])[0:8]


def shift(source, axis, step):
    count = lax.axis_size(axis)
    return lax.ppermute(source, axis, [(i, (i + step) % count) for i in range(count)])


def near_stack(payload):
    stack = jnp.concatenate([shift(payload, "row", 1), payload, shift(payload, "row", -1)], axis=0)
    return shift(stack, "col", 1), stack, shift(stack, "col", -1)


def call(body, outs, *operands, flops=0):
    return pl.pallas_call(
        body,
        out_shape=[jax.ShapeDtypeStruct(shape, dtype) for shape, dtype in outs],
        compiler_params=pltpu.CompilerParams(vmem_limit_bytes=48 * 1024 * 1024),
        cost_estimate=pl.CostEstimate(flops=flops, bytes_accessed=1 << 20, transcendentals=0),
    )(*operands)


def pair_call(body, outs, tiles, blocked, scratch, lists, *operands):
    def whole(operand):
        return pl.BlockSpec(operand.shape, lambda i, s: (0,) * operand.ndim)

    def block(operand):
        rows = operand.shape[0] // tiles
        return pl.BlockSpec((rows, operand.shape[1]), lambda i, s: (i, 0))

    out_shape = [jax.ShapeDtypeStruct(shape, jnp.float32) for shape in outs]
    plain = len(operands) - blocked
    return pl.pallas_call(
        body,
        out_shape=out_shape,
        grid_spec=pltpu.PrefetchScalarGridSpec(
            num_scalar_prefetch=1,
            grid=(tiles,),
            in_specs=[whole(operand) for operand in operands[:plain]]
            + [block(operand) for operand in operands[plain:]],
            out_specs=[block(shape) for shape in out_shape],
            scratch_shapes=[pltpu.VMEM(shape, jnp.float32) for shape in scratch],
        ),
        compiler_params=pltpu.CompilerParams(vmem_limit_bytes=48 * 1024 * 1024),
        cost_estimate=pl.CostEstimate(
            flops=20_000_000, bytes_accessed=1 << 20, transcendentals=1 << 20
        ),
    )(lists, *operands)


def exchange(message, devices):
    shape = message.shape
    sent = message.reshape(devices, 1, -1)
    return lax.all_to_all(sent, ("row", "col"), split_axis=0, concat_axis=0, tiled=True).reshape(
        shape
    )


def slab_local(field_rhs, positions, polar, grid_base, tile_lists):
    rows_count = lax.axis_size("row")
    cols_count = lax.axis_size("col")
    counts = (rows_count, cols_count)
    devices = rows_count * cols_count
    lengths = (CX * rows_count, CY * cols_count, KZ)
    spans = tuple(float(length) for length in lengths)
    atoms = polar.shape[-1]
    tile_count = atoms // TILE
    listed = tile_lists.shape[-1]
    tables = slab_tables(rows_count, cols_count)
    f32 = jnp.float32
    rhs = field_rhs.reshape(RHS * 3, atoms)
    place = positions.reshape(3, atoms)
    base = grid_base.reshape(3, atoms)
    polar = polar.reshape(1, atoms)
    lists = tile_lists.reshape(-1)
    brick_rows = 10 * tile_count
    moment_rows = 6 * tile_count
    message_shape = (devices * SLOT_ROWS, KZ // devices * RHS * Y_PAD)
    row_shape = (RHS * 3, atoms)

    start, payload = call(pack_body, [(row_shape, f32), ((brick_rows, TILE), f32)], rhs, place, polar)
    near = near_stack(payload)

    def setup(*refs):
        setup_body(lengths, devices, *refs)

    message, splines, depth_high, depth_low = call(
        setup,
        [
            (message_shape, f32),
            ((2 * SLOT_ROWS + 2 * Y_PAD, atoms), f32),
            ((KZ, 2 * atoms), jnp.bfloat16),
            ((KZ, 2 * atoms), jnp.bfloat16),
        ],
        place,
        base,
        start,
        *[jnp.asarray(table) for table in tables["along_z"]],
    )
    position = lax.axis_index("row") * cols_count + lax.axis_index("col")
    kernel = lax.dynamic_index_in_dim(jnp.asarray(tables["kernel"]), position, 0, keepdims=False)
    constants = (
        kernel,
        jnp.asarray(tables["forward_x"]),
        jnp.asarray(tables["backward_x"]),
        *[jnp.asarray(table) for table in tables["block"]],
        *[jnp.asarray(table) for table in tables["block_back"]],
    )
    arrived = exchange(message, devices)

    half = tile_count // 2
    scratch = [(3 * 3 * brick_rows, TILE)]
    squares = [(TILE, TILE)] * 3
    kept = []
    for first_tile in (0, half):

        def pair_first(*refs, first_tile=first_tile):
            pair_first_body(first_tile, listed, tile_count, spans, *refs)

        kept.append(
            pair_call(
                pair_first,
                [(half * listed * TILE, TILE)] * 2 + [(half * 8, TILE)],
                half,
                0,
                scratch + squares,
                lists,
                *near,
            )
        )

    def gather_rows(parts):
        whole = jnp.concatenate(parts, axis=0).reshape(tile_count, 8, TILE)
        return jnp.moveaxis(whole, 0, 1).reshape(8, atoms)

    direct = gather_rows([part[2] for part in kept])

    def middle_first(*refs):
        middle_first_body(counts, *refs)

    mixed, wave = call(
        middle_first, [(message_shape, f32), (kernel.shape, f32)], arrived, *constants
    )
    returned = exchange(mixed, devices)

    def again(*refs):
        again_body(devices, *refs)

    image, second, moments, message = call(
        again,
        [(row_shape, f32), (row_shape, f32), ((moment_rows, TILE), f32), (message_shape, f32)],
        returned,
        splines,
        depth_high,
        depth_low,
        start,
        direct,
        polar,
    )
    near_moments = near_stack(moments)
    arrived = exchange(message, devices)
    second_parts = []
    for first_tile, part in zip((0, half), kept):

        def pair_second(*refs, first_tile=first_tile):
            pair_second_body(first_tile, listed, tile_count, spans, *refs)

        second_parts.append(
            pair_call(
                pair_second,
                [(half * 8, TILE)],
                half,
                2,
                scratch + [(3 * 3 * moment_rows, TILE)] + squares,
                lists,
                *near,
                *near_moments,
                part[0],
                part[1],
            )[0]
        )
    direct = gather_rows(second_parts)

    def middle_second(*refs):
        middle_second_body(counts, *refs)

    (mixed,) = call(
        middle_second,
        [(message_shape, f32)],
        arrived,
        *constants,
        wave,
        rhs,
        start,
        image,
        second,
        direct,
        polar,
    )
    returned = exchange(mixed, devices)

    def final(*refs):
        final_body(devices, *refs)

    dipoles, residual = call(
        final,
        [(row_shape, f32), (row_shape, f32)],
        returned,
        splines,
        depth_high,
        depth_low,
        rhs,
        start,
        image,
        second,
        direct,
        polar,
    )
    return dipoles.reshape(field_rhs.shape), residual.reshape(field_rhs.shape)


def solution(mesh):
    placed = (
        P("row", "col", None, None, None),
        P("row", "col", None, None),
        P("row", "col", None),
        P("row", "col", None, None),
        P("row", "col", None, None),
    )
    devices = mesh.shape["row"] * mesh.shape["col"]
    return jax.shard_map(
        slab_local if KZ % devices == 0 else pencil_local,
        mesh=mesh,
        in_specs=placed,
        out_specs=(P("row", "col", None, None, None), P("row", "col", None, None, None)),
        check_vma=False,
    )
```

```python
import math

import jax
import jax.numpy as jnp
import ml_dtypes
import numpy as np
from jax import lax
from jax.experimental import pallas as pl
from jax.experimental.pallas import tpu as pltpu
from jax.sharding import PartitionSpec as P

CX = 8
CY = 4
KZ = 256
TILE = 128
RHS = 2
ITERS = 2


ewald_beta = 0.4
thole_a = 0.39
self_coef = 4.0 * ewald_beta**3 / (3.0 * math.sqrt(math.pi))
highest = lax.Precision.HIGHEST


def with_halo(cells, sides, width):
    for axis, dim in sides:
        count = lax.axis_size(axis)
        head = lax.slice_in_dim(cells, 0, width, axis=dim)
        tail = lax.slice_in_dim(cells, cells.shape[dim] - width, cells.shape[dim], axis=dim)
        cells = jnp.concatenate(
            [
                lax.ppermute(tail, axis, [(i, (i + 1) % count) for i in range(count)]),
                cells,
                lax.ppermute(head, axis, [((i + 1) % count, i) for i in range(count)]),
            ],
            axis=dim,
        )
    return cells


def spline_table(fraction):
    previous = {0: jnp.ones_like(fraction)}
    fourth = previous
    for degree in range(2, 6):
        current = {}
        for offset in range(degree):
            abscissa = fraction + offset
            summed = abscissa * previous.get(offset, 0.0) + (degree - abscissa) * previous.get(
                offset - 1, 0.0
            )
            current[offset] = summed / (degree - 1)
        if degree == 4:
            fourth = current
        previous = current
    values = jnp.stack([previous[4 - stencil] for stencil in range(5)])
    slopes = jnp.stack(
        [fourth.get(4 - stencil, 0.0) - fourth.get(3 - stencil, 0.0) for stencil in range(5)]
    )
    return (values, slopes)


def spline_modulus(wave_index, length):
    spline_coef = (1.0 / 24.0, 11.0 / 24.0, 11.0 / 24.0, 1.0 / 24.0)
    cosine_sum = jnp.zeros(wave_index.shape, jnp.float32)
    sine_sum = jnp.zeros(wave_index.shape, jnp.float32)
    for offset in range(4):
        angles = 2.0 * math.pi / length * (wave_index * offset % length).astype(jnp.float32)
        cosine_sum = cosine_sum + spline_coef[offset] * jnp.cos(angles)
        sine_sum = sine_sum + spline_coef[offset] * jnp.sin(angles)
    return cosine_sum * cosine_sum + sine_sum * sine_sum


def folded_square(wave_index, length):
    nearest = jnp.minimum(wave_index, length - wave_index).astype(jnp.float32) / length
    return nearest * nearest


def influence(wave_x, wave_y, wave_z, length_x, length_y, length_z):
    wave_norm = (
        folded_square(wave_x, length_x)
        + folded_square(wave_y, length_y)
        + folded_square(wave_z, length_z)
    )
    modulus = (
        spline_modulus(wave_x, length_x)
        * spline_modulus(wave_y, length_y)
        * spline_modulus(wave_z, length_z)
    )
    excluded = (wave_x * 2 == length_x) | (wave_y * 2 == length_y) | (wave_z * 2 == length_z)
    excluded = excluded | (wave_x == 0) & (wave_y == 0) & (wave_z == 0)
    safe_norm = jnp.where(excluded, 1.0, wave_norm)
    safe_modulus = jnp.where(excluded, 1.0, modulus)
    result = jnp.exp(-(math.pi**2 / ewald_beta**2) * safe_norm) / (
        math.pi * safe_norm * safe_modulus
    )
    return jnp.where(excluded, 0.0, result)


def tile_field(own_static, near_static, near_dipole, box_spans):
    listed_count = near_static.shape[0]
    tile_width = own_static.shape[1]
    box_span = jnp.array(box_spans, dtype=jnp.float32)[None, :, None, None]
    separation = near_static[:, 0:3, None, :] - own_static[None, 0:3, :, None]
    separation = separation - box_span * jnp.floor(separation / box_span + 0.5)
    dist_sq = jnp.sum(separation * separation, axis=1)
    itself = (jnp.arange(listed_count)[:, None, None] == 0) & (
        jnp.arange(tile_width)[:, None] == jnp.arange(tile_width)[None, :]
    )[None]
    safe_sq = jnp.where(itself, 1.0, dist_sq)
    distance = jnp.sqrt(safe_sq)
    scaled = distance / (own_static[3][None, :, None] * near_static[:, 3][:, None, :])
    cubed = thole_a * scaled * scaled * scaled
    damping = jnp.exp(-cubed)
    screen = lax.erfc(ewald_beta * distance)
    gaussian = 2.0 * ewald_beta / math.sqrt(math.pi) * jnp.exp(-(ewald_beta * ewald_beta) * safe_sq)
    inverse_sq = 1.0 / safe_sq
    inverse_cube = inverse_sq / distance
    first_term = (screen - damping) * inverse_cube + gaussian * inverse_sq
    second = (
        3.0 * (screen - (1.0 + cubed) * damping) * inverse_cube * inverse_sq
        + gaussian * (2.0 * ewald_beta * ewald_beta + 3.0 * inverse_sq) * inverse_sq
    )
    first_term = jnp.where(itself, 0.0, first_term)
    second = jnp.where(itself, 0.0, second)
    projected = jnp.sum(near_dipole[:, :, :, None, :] * separation[:, None, :, :, :], axis=2)
    weighted = second[:, None] * projected
    outward = jnp.sum(weighted[:, :, None] * separation[:, None], axis=(0, 4))
    inward = jnp.sum(first_term[:, None, None] * near_dipole[:, :, :, None, :], axis=(0, 4))
    return outward - inward


def hartley(length):
    counter = jnp.arange(length, dtype=jnp.int32)
    angles = (
        2.0 * math.pi / length * (counter[:, None] * counter[None, :] % length).astype(jnp.float32)
    )
    return jnp.cos(angles) + jnp.sin(angles)


def placed_table(first_cell, weights, extent):
    slot_index = jnp.arange(extent, dtype=jnp.int32)[:, None]
    placed = jnp.zeros((extent, first_cell.shape[0]), jnp.float32)
    for stencil in range(5):
        placed = placed + jnp.where(
            slot_index == (first_cell[None, :] + stencil) % extent, weights[stencil][None, :], 0.0
        )
    return placed


def pad_axis(source, axis_pos, leading, trailing):
    widths = [(0, 0)] * source.ndim
    widths[axis_pos] = (leading, trailing)
    return jnp.pad(source, widths)


def fold_cycle(cycle_only, axis_pos, inner_len):
    middle = lax.slice_in_dim(cycle_only, 4, inner_len + 4, axis=axis_pos)
    lower_cycle = lax.slice_in_dim(cycle_only, 0, 2, axis=axis_pos)
    upper_cycle = lax.slice_in_dim(cycle_only, inner_len + 6, inner_len + 8, axis=axis_pos)
    return (
        middle
        + pad_axis(lower_cycle, axis_pos, 0, inner_len - 2)
        + pad_axis(upper_cycle, axis_pos, inner_len - 2, 0)
    )


def clear_inside(extended, extents):
    inside = None
    for axis_pos, inner_len in extents:
        slot_index = lax.broadcasted_iota(jnp.int32, extended.shape, axis_pos)
        within = (slot_index >= 2) & (slot_index < inner_len + 6)
        inside = within if inside is None else inside & within
    return jnp.where(inside, 0.0, extended)


def inner_sum(left_arr, right_arr):
    return lax.psum(jnp.sum(left_arr * right_arr, axis=(1, 2)), ("row", "col"))


def pencil_local(field_rhs, positions, polar, grid_base, tile_lists):
    rows_count = lax.axis_size("row")
    cols_count = lax.axis_size("col")
    grid_x = CX * rows_count
    grid_y = CY * cols_count
    atom_count = polar.shape[-1]
    tile_count = atom_count // TILE
    slab_depth = KZ // tile_count
    window_len = slab_depth + 4
    box_spans = (float(grid_x), float(grid_y), float(KZ))
    own_place = positions[0, 0]
    own_base = grid_base[0, 0]
    own_polar = polar[0, 0]
    lengths = jnp.array([grid_x, grid_y, KZ], dtype=jnp.int32)[:, None]
    cell_index = (own_base + 2) % lengths
    fraction = own_place - cell_index.astype(jnp.float32)
    values, slopes = spline_table(fraction)
    first_x = (own_base[0] - lax.axis_index("row") * CX + 2) % grid_x
    first_y = (own_base[1] - lax.axis_index("col") * CY + 2) % grid_y
    rows_x = placed_table(first_x, values[:, 0], CX + 4)
    slope_x = placed_table(first_x, slopes[:, 0], CX + 4)
    rows_y = placed_table(first_y, values[:, 1], CY + 4)
    slope_y = placed_table(first_y, slopes[:, 1], CY + 4)
    tile_start = jnp.arange(atom_count, dtype=jnp.int32) // TILE * slab_depth
    first_z = (own_base[2] + 2 - tile_start) % KZ
    rows_z = placed_table(first_z, values[:, 2], window_len)
    slope_z = placed_table(first_z, slopes[:, 2], window_len)
    plane_count = (CX + 4) * (CY + 4)
    plane_dx = (slope_x[:, None, :] * rows_y[None, :, :]).reshape(plane_count, atom_count)
    plane_dy = (rows_x[:, None, :] * slope_y[None, :, :]).reshape(plane_count, atom_count)
    plane_flat = (rows_x[:, None, :] * rows_y[None, :, :]).reshape(plane_count, atom_count)
    window_rows = jnp.moveaxis(rows_z.reshape(window_len, tile_count, TILE), 1, 0)
    window_slope = jnp.moveaxis(slope_z.reshape(window_len, tile_count, TILE), 1, 0)
    depth_table = jnp.concatenate([window_rows, window_slope], axis=2)
    grid_scale = 1.0 / (grid_x * grid_y * KZ)
    hartley_x = hartley(grid_x)
    hartley_y = hartley(grid_y)
    hartley_z = hartley(KZ)
    block_y = grid_y // rows_count
    block_z = KZ // cols_count
    wave_x = jnp.arange(grid_x, dtype=jnp.int32)[:, None, None]
    wave_y = (lax.axis_index("row") * block_y + jnp.arange(block_y, dtype=jnp.int32))[None, :, None]
    wave_z = (lax.axis_index("col") * block_z + jnp.arange(block_z, dtype=jnp.int32))[None, None, :]
    kernel = influence(wave_x, wave_y, wave_z, grid_x, grid_y, KZ) * grid_scale
    root_scale = jnp.power(own_polar, 1.0 / 6.0)
    own_static = jnp.concatenate([own_place, root_scale[None]], axis=0)
    near_static = with_halo(own_static[None, None], (("row", 0), ("col", 1)), 1)
    near_static = jnp.moveaxis(near_static.reshape(9, 4, tile_count, TILE), 2, 1).reshape(
        9 * tile_count, 4, TILE
    )
    own_tiles = jnp.moveaxis(own_static.reshape(4, tile_count, TILE), 1, 0)
    own_lists = tile_lists[0, 0]
    polar_wide = own_polar[None, None, :]
    solution = jnp.zeros_like(field_rhs[0, 0])
    residual = field_rhs[0, 0]
    scaled_res = polar_wide * residual
    direction = scaled_res
    progress = inner_sum(residual, scaled_res)
    for iteration in range(ITERS):
        near_dip = with_halo(direction[None, None], (("row", 0), ("col", 1)), 1)
        near_dip = jnp.moveaxis(near_dip.reshape(9, RHS, 3, tile_count, TILE), 3, 1).reshape(
            9 * tile_count, RHS, 3, TILE
        )

        def one_tile(tile_pos):
            picked = own_lists[tile_pos]
            return tile_field(own_tiles[tile_pos], near_static[picked], near_dip[picked], box_spans)

        fields = lax.map(one_tile, jnp.arange(tile_count, dtype=jnp.int32))
        direct = jnp.moveaxis(fields, 0, 2).reshape(RHS, 3, atom_count)
        slope_terms = (
            direction[:, 0, None, :] * plane_dx[None] + direction[:, 1, None, :] * plane_dy[None]
        )
        flat_terms = direction[:, 2, None, :] * plane_flat[None]
        spread_left = jnp.concatenate(
            [
                slope_terms.reshape(RHS, plane_count, tile_count, TILE),
                flat_terms.reshape(RHS, plane_count, tile_count, TILE),
            ],
            axis=3,
        )
        spread_windows = jnp.einsum("sptb,twb->sptw", spread_left, depth_table, precision=highest)
        main_part = spread_windows[..., :slab_depth].reshape(spread_windows.shape[:-2] + (KZ,))
        tail_part = pad_axis(
            spread_windows[..., slab_depth:], spread_windows.ndim - 1, 0, slab_depth - 4
        )
        tail_part = tail_part.reshape(spread_windows.shape[:-2] + (KZ,))[..., : KZ + 4 - slab_depth]
        last_axis = main_part.ndim - 1
        padded_line = pad_axis(main_part, last_axis, 0, 4) + pad_axis(
            tail_part, last_axis, slab_depth, 0
        )
        inner = padded_line[..., 2 : KZ + 2]
        spread_tile = (
            inner
            + pad_axis(padded_line[..., 0:2], last_axis, KZ - 2, 0)
            + pad_axis(padded_line[..., KZ + 2 : KZ + 4], last_axis, 0, KZ - 2)
        ).reshape(RHS, CX + 4, CY + 4, KZ)
        extended = with_halo(spread_tile, (("row", 1), ("col", 2)), 2)
        cycle_only = clear_inside(extended, ((1, CX), (2, CY)))
        folded = fold_cycle(fold_cycle(cycle_only, 1, CX), 2, CY)
        spectrum = jnp.einsum(
            "sxyz,zk->sxyk",
            spread_tile[:, 2 : CX + 2, 2 : CY + 2] + folded,
            hartley_z,
            precision=highest,
        )
        along_y = jnp.einsum(
            "sxyz,yk->sxkz",
            lax.all_to_all(spectrum, "col", split_axis=3, concat_axis=2, tiled=True),
            hartley_y,
            precision=highest,
        )
        along_x = (
            jnp.einsum(
                "sxyz,xk->skyz",
                lax.all_to_all(along_y, "row", split_axis=2, concat_axis=1, tiled=True),
                hartley_x,
                precision=highest,
            )
            * kernel[None]
        )
        mixed_part = jnp.einsum("sxyz,xk->skyz", along_x, hartley_x, precision=highest)
        returned = lax.all_to_all(mixed_part, "row", split_axis=1, concat_axis=2, tiled=True)
        swapped = jnp.einsum("sxyz,yk->sxkz", returned, hartley_y, precision=highest)
        restored = lax.all_to_all(swapped, "col", split_axis=2, concat_axis=3, tiled=True)
        padded = with_halo(
            jnp.einsum("sxyz,zk->sxyk", restored, hartley_z, precision=highest),
            (("row", 1), ("col", 2)),
            2,
        )
        line = padded.reshape(RHS, plane_count, KZ)
        extended_line = jnp.concatenate([line[..., KZ - 2 :], line, line[..., :2]], axis=-1)
        windows = jnp.stack(
            [
                extended_line[..., tile * slab_depth : tile * slab_depth + window_len]
                for tile in range(tile_count)
            ],
            axis=-2,
        )
        sampled = jnp.einsum("sptw,twb->sptb", windows, depth_table, precision=highest)
        with_flat = sampled[..., :TILE].reshape(RHS, plane_count, atom_count)
        with_slope = sampled[..., TILE:].reshape(RHS, plane_count, atom_count)
        recip_part = jnp.stack(
            [
                jnp.sum(with_flat * plane_dx[None], axis=1),
                jnp.sum(with_flat * plane_dy[None], axis=1),
                jnp.sum(with_slope * plane_flat[None], axis=1),
            ],
            axis=1,
        )
        image_field = direction / polar_wide - direct + recip_part - self_coef * direction
        step_size = (progress / inner_sum(direction, image_field))[:, None, None]
        solution = solution + step_size * direction
        residual = residual - step_size * image_field
        scaled_res = polar_wide * residual
        progress_next = inner_sum(residual, scaled_res)
        direction = scaled_res + (progress_next / progress)[:, None, None] * direction
        progress = progress_next
    return (solution[None, None], residual[None, None])


X_PAD = CX + 4
Y_PAD = CY + 4
SLOT_ROWS = 16
SPLIT = 2
VMEM_LIMIT = 60_000_000
PAIR_ROWS = 16
SCREEN_SCALE = 0.4
SCREEN_COEF = (
    0.22567588090896606,
    0.2256690263748169,
    0.20785020291805267,
    0.16849851608276367,
    0.14156343042850494,
    -0.005832736846059561,
    0.16930203139781952,
    -0.1830107867717743,
    0.05028456076979637,
)


def halves(value):
    high = value.astype(jnp.bfloat16)
    return high, (value - high.astype(jnp.float32)).astype(jnp.bfloat16)


def halves_np(value):
    value = value.astype(np.float32)
    high = value.astype(ml_dtypes.bfloat16)
    return high, (value - high.astype(np.float32)).astype(ml_dtypes.bfloat16)


def product(left, right, left_dim=1, right_dim=0):
    def one(first, second):
        return lax.dot_general(
            first,
            second,
            (((left_dim,), (right_dim,)), ((), ())),
            preferred_element_type=jnp.float32,
        )

    return one(left[0], right[0]) + (one(left[1], right[0]) + one(left[0], right[1]))


def cas_np(wave, place, length):
    angles = 2.0 * np.pi / length * (wave[:, None] * place[None, :] % length)
    return np.cos(angles) + np.sin(angles)


def modulus_np(wave, length):
    coef = np.array([1.0, 11.0, 11.0, 1.0]) / 24.0
    angles = 2.0 * np.pi / length * (wave[:, None] * np.arange(4)[None, :])
    return (coef * np.cos(angles)).sum(1) ** 2 + (coef * np.sin(angles)).sum(1) ** 2


def influence_np(length_x, length_y, length_z):
    total = np.zeros((length_x, length_y, length_z))
    modulus = np.ones((length_x, length_y, length_z))
    excluded = np.zeros((length_x, length_y, length_z), bool)
    for axis, length in enumerate((length_x, length_y, length_z)):
        wave = np.arange(length)
        shape = [1, 1, 1]
        shape[axis] = length
        total = total + ((np.minimum(wave, length - wave) / length) ** 2).reshape(shape)
        modulus = modulus * modulus_np(wave, length).reshape(shape)
        excluded = excluded | (wave * 2 == length).reshape(shape)
    excluded[0, 0, 0] = True
    safe = np.where(excluded, 1.0, total)
    result = np.exp(-(np.pi**2) / ewald_beta**2 * safe) / (
        np.pi * safe * np.where(excluded, 1.0, modulus)
    )
    return np.where(excluded, 0.0, result) / (length_x * length_y * length_z)


def slab_tables(rows_count, cols_count):
    grid_x = CX * rows_count
    grid_y = CY * cols_count
    devices = rows_count * cols_count
    chunk = KZ // devices
    wave_z = (np.arange(devices)[None, :] * chunk + np.arange(chunk)[:, None]).reshape(-1)
    along_z = cas_np(wave_z, np.arange(KZ), KZ)
    place_x = np.arange(rows_count)[:, None] * CX + np.arange(X_PAD)[None, :] - 2
    along_x = cas_np(np.arange(grid_x), place_x.reshape(-1) % grid_x, grid_x)
    padded_x = np.zeros((grid_x, rows_count, SLOT_ROWS))
    padded_x[:, :, :X_PAD] = along_x.reshape(grid_x, rows_count, X_PAD)
    padded_x = padded_x.reshape(grid_x, rows_count * SLOT_ROWS)
    x_high, x_low = halves_np(padded_x)
    forward_x = np.concatenate([x_high, x_low, x_high], axis=1)
    backward_x = np.concatenate([x_high.T, x_low.T, x_high.T], axis=1)
    place_y = (np.arange(cols_count)[:, None] * CY + np.arange(Y_PAD)[None, :] - 2) % grid_y
    along_y = cas_np(np.arange(grid_y), place_y.reshape(-1), grid_y)
    along_y = along_y.reshape(grid_y, cols_count, Y_PAD)
    units = chunk * RHS // SPLIT
    block = np.einsum("uv,kcy->cuyvk", np.eye(units), along_y)
    block = block.reshape(cols_count * units * Y_PAD, units * grid_y)
    kernel = influence_np(grid_x, grid_y, KZ).reshape(grid_x, grid_y, devices, chunk)
    kernel = np.transpose(kernel, (2, 0, 3, 1))[:, :, :, None, :]
    kernel = np.broadcast_to(kernel, (devices, grid_x, chunk, RHS, grid_y))
    kernel = kernel.reshape(devices, grid_x, SPLIT, units * grid_y)
    kernel = np.moveaxis(kernel, 2, 1).reshape(devices, SPLIT * grid_x, units * grid_y)
    kernel = kernel.astype(np.float32)
    return dict(
        along_z=halves_np(along_z),
        forward_x=forward_x,
        backward_x=backward_x,
        block=halves_np(block),
        block_back=halves_np(np.ascontiguousarray(block.T)),
        kernel=kernel,
    )


def pack_body(rhs_ref, place_ref, polar_ref, start_ref, payload_ref):
    polar = polar_ref[...]
    start = read_rows(rhs_ref) * polar
    start_ref[...] = start
    everything = jnp.concatenate([place_ref[...], 1.0 / jnp.sqrt(polar), start], axis=0)
    store_payload(payload_ref, everything)


def read_rows(rows_ref):
    return jnp.concatenate([rows_ref[dim] for dim in range(3)], axis=0)


def store_payload(payload_ref, everything):
    tile_count = everything.shape[1] // TILE
    for quantity in range(everything.shape[0]):
        for tile in range(tile_count):
            row = quantity * tile_count + tile
            payload_ref[row : row + 1, :] = everything[
                quantity : quantity + 1, tile * TILE : (tile + 1) * TILE
            ]


def placed_rows(slot, weights, extent):
    slot_index = lax.broadcasted_iota(jnp.int32, (extent, slot.shape[1]), 0)
    placed = jnp.zeros((extent, slot.shape[1]), jnp.float32)
    for stencil in range(5):
        target = slot + stencil
        if extent == KZ:
            target = jnp.where(target >= KZ, target - KZ, target)
        placed = placed + jnp.where(slot_index == target, weights[stencil], 0.0)
    return placed


def spread_into(message_ref, moment, rows_x, slope_x, rows_y, slope_y, depth, devices):
    blocks = []
    for step in range(X_PAD):
        flat_x = rows_x[step : step + 1]
        tilt_x = slope_x[step : step + 1]
        for rhs in range(RHS):
            part_x = tilt_x * moment[rhs : rhs + 1]
            part_y = flat_x * moment[RHS + rhs : RHS + rhs + 1]
            part_z = flat_x * moment[2 * RHS + rhs : 2 * RHS + rhs + 1]
            blocks.append(
                jnp.concatenate([part_x * rows_y + part_y * slope_y, part_z * rows_y], axis=1)
            )
    charges = jnp.concatenate(blocks, axis=0)
    spectrum = product(depth, halves(charges), 1, 1)
    chunk = KZ // devices
    width = RHS * Y_PAD
    for step in range(X_PAD):
        message_ref[pl.ds(step, devices, stride=SLOT_ROWS), :] = jnp.concatenate(
            [
                spectrum[unit * devices : (unit + 1) * devices, step * width : (step + 1) * width]
                for unit in range(chunk)
            ],
            axis=1,
        )


def sample_from(message_ref, rows_x, slope_x, rows_y, slope_y, depth, devices):
    chunk = KZ // devices
    width = RHS * Y_PAD
    pieces = [
        message_ref[pl.ds(step, devices, stride=SLOT_ROWS), :] for step in range(X_PAD)
    ]
    spare = jnp.zeros((devices, KZ - X_PAD * width), jnp.float32)
    spectrum = jnp.concatenate(
        [
            jnp.concatenate(
                [piece[:, unit * width : (unit + 1) * width] for piece in pieces] + [spare], axis=1
            )
            for unit in range(chunk)
        ],
        axis=0,
    )
    spectrum = jnp.transpose(spectrum)[: X_PAD * width]
    sampled = product(halves(spectrum), depth, 1, 0)
    atoms = rows_x.shape[1]
    fields = [None] * (3 * RHS)
    for rhs in range(RHS):
        sum_x = sum_y = sum_z = None
        for step in range(X_PAD):
            first = step * width + rhs * Y_PAD
            flat = sampled[first : first + Y_PAD, :atoms]
            tilt = sampled[first : first + Y_PAD, atoms:]
            part_x = slope_x[step : step + 1] * flat
            part_y = rows_x[step : step + 1] * flat
            part_z = rows_x[step : step + 1] * tilt
            sum_x = part_x if sum_x is None else sum_x + part_x
            sum_y = part_y if sum_y is None else sum_y + part_y
            sum_z = part_z if sum_z is None else sum_z + part_z
        fields[rhs] = jnp.sum(sum_x * rows_y, axis=0, keepdims=True)
        fields[RHS + rhs] = jnp.sum(sum_y * slope_y, axis=0, keepdims=True)
        fields[2 * RHS + rhs] = jnp.sum(sum_z * rows_y, axis=0, keepdims=True)
    return jnp.concatenate(fields, axis=0)


def read_tables(tables_ref):
    return (
        tables_ref[0:X_PAD],
        tables_ref[SLOT_ROWS : SLOT_ROWS + X_PAD],
        tables_ref[2 * SLOT_ROWS : 2 * SLOT_ROWS + Y_PAD],
        tables_ref[2 * SLOT_ROWS + Y_PAD : 2 * SLOT_ROWS + 2 * Y_PAD],
    )


def clear_spare(message_ref, devices):
    spare = jnp.zeros((devices, message_ref.shape[1]), jnp.float32)
    for step in range(X_PAD, SLOT_ROWS):
        message_ref[pl.ds(step, devices, stride=SLOT_ROWS), :] = spare


def setup_body(
    lengths,
    devices,
    place_ref,
    base_ref,
    start_ref,
    z_high_ref,
    z_low_ref,
    message_ref,
    tables_ref,
    depth_high_ref,
    depth_low_ref,
):
    base = base_ref[...]
    fractions = []
    cells = []
    for dim in range(3):
        cell = base[dim : dim + 1] + 2
        cell = jnp.where(cell >= lengths[dim], cell - lengths[dim], cell)
        cells.append(cell)
        fractions.append(place_ref[dim : dim + 1, :] - cell.astype(jnp.float32))
    values, slopes = spline_table(jnp.concatenate(fractions, axis=0))
    values = [[values[stencil][dim : dim + 1] for stencil in range(5)] for dim in range(3)]
    slopes = [[slopes[stencil][dim : dim + 1] for stencil in range(5)] for dim in range(3)]
    slot_x = lax.rem(cells[0], CX)
    slot_y = lax.rem(cells[1], CY)
    tables_ref[0:SLOT_ROWS] = placed_rows(slot_x, values[0], SLOT_ROWS)
    tables_ref[SLOT_ROWS : 2 * SLOT_ROWS] = placed_rows(slot_x, slopes[0], SLOT_ROWS)
    tables_ref[2 * SLOT_ROWS : 2 * SLOT_ROWS + Y_PAD] = placed_rows(slot_y, values[1], Y_PAD)
    tables_ref[2 * SLOT_ROWS + Y_PAD : 2 * SLOT_ROWS + 2 * Y_PAD] = placed_rows(
        slot_y, slopes[1], Y_PAD
    )
    window = jnp.concatenate(
        [
            placed_rows(base[2:3], values[2], KZ),
            placed_rows(base[2:3], slopes[2], KZ),
        ],
        axis=1,
    )
    depth = product((z_high_ref[...], z_low_ref[...]), halves(window), 1, 0)
    depth = halves(depth)
    depth_high_ref[...] = depth[0]
    depth_low_ref[...] = depth[1]
    spread_into(message_ref, start_ref[...], *read_tables(tables_ref), depth, devices)
    clear_spare(message_ref, devices)


def transform_in(message_ref, forward_ref, block_high_ref, block_low_ref, rows_count, cols_count):
    gathered = jnp.concatenate(
        [
            jnp.concatenate(
                [
                    message_ref[(r * cols_count + c) * SLOT_ROWS :][:SLOT_ROWS]
                    for r in range(rows_count)
                ],
                axis=0,
            )
            for c in range(cols_count)
        ],
        axis=1,
    )
    high, low = halves(gathered)
    along = jnp.dot(
        forward_ref[...],
        jnp.concatenate([high, high, low], axis=0),
        preferred_element_type=jnp.float32,
    )
    part = along.shape[1] // cols_count // SPLIT
    along = jnp.concatenate(
        [
            jnp.concatenate(
                [
                    along[:, (c * SPLIT + half) * part : (c * SPLIT + half + 1) * part]
                    for c in range(cols_count)
                ],
                axis=1,
            )
            for half in range(SPLIT)
        ],
        axis=0,
    )
    return product(halves(along), (block_high_ref[...], block_low_ref[...]))


def transform_out(result_ref, values, backward_ref, block_high_ref, block_low_ref, counts):
    rows_count, cols_count = counts
    spread = product(halves(values), (block_high_ref[...], block_low_ref[...]))
    grid_x = spread.shape[0] // SPLIT
    part = spread.shape[1] // cols_count
    spread = jnp.concatenate(
        [
            spread[half * grid_x : (half + 1) * grid_x, c * part : (c + 1) * part]
            for c in range(cols_count)
            for half in range(SPLIT)
        ],
        axis=1,
    )
    high, low = halves(spread)
    along = jnp.dot(
        backward_ref[...],
        jnp.concatenate([high, high, low], axis=0),
        preferred_element_type=jnp.float32,
    )
    width = along.shape[1] // cols_count
    for r in range(rows_count):
        for c in range(cols_count):
            first = (r * cols_count + c) * SLOT_ROWS
            result_ref[first : first + SLOT_ROWS, :] = along[
                r * SLOT_ROWS : (r + 1) * SLOT_ROWS, c * width : (c + 1) * width
            ]


def middle_first_body(
    counts,
    message_ref,
    kernel_ref,
    forward_ref,
    backward_ref,
    block_high_ref,
    block_low_ref,
    back_high_ref,
    back_low_ref,
    result_ref,
    wave_ref,
):
    wave = transform_in(message_ref, forward_ref, block_high_ref, block_low_ref, *counts)
    wave_ref[...] = wave
    transform_out(
        result_ref, wave * kernel_ref[...], backward_ref, back_high_ref, back_low_ref, counts
    )


def gather_rows(parts_ref):
    tiles = [parts_ref[8 * tile : 8 * tile + 8, :] for tile in range(parts_ref.shape[0] // 8)]
    return jnp.concatenate(tiles, axis=1)[0 : 3 * RHS]


def row_total(value, rhs):
    row = lax.broadcasted_iota(jnp.int32, value.shape, 0)
    return total(jnp.where(lax.rem(row, RHS) == rhs, value, 0.0))


def total(value):
    return jnp.sum(jnp.sum(value, axis=0, keepdims=True), axis=1, keepdims=True)


def middle_second_body(
    counts,
    message_ref,
    kernel_ref,
    forward_ref,
    backward_ref,
    block_high_ref,
    block_low_ref,
    back_high_ref,
    back_low_ref,
    wave_ref,
    rhs_ref,
    start_ref,
    image_ref,
    second_ref,
    near_ref,
    polar_ref,
    result_ref,
):
    rhs_rows = read_rows(rhs_ref)
    near_rows = gather_rows(near_ref)
    wave = transform_in(message_ref, forward_ref, block_high_ref, block_low_ref, *counts)
    filtered = wave * kernel_ref[...]
    transform_out(result_ref, filtered, backward_ref, back_high_ref, back_low_ref, counts)
    before = wave_ref[...]
    grid_y = CY * counts[1]
    lane = lax.broadcasted_iota(jnp.int32, wave.shape, 1)
    own_rhs = lax.rem(lax.div(lane, grid_y), RHS)
    second = second_ref[...]
    start = start_ref[...]
    image = image_ref[...]
    local_part = second / polar_ref[...] - near_rows - self_coef * second
    slot = lax.broadcasted_iota(jnp.int32, (1, result_ref.shape[1]), 1)
    sums = jnp.zeros((1, result_ref.shape[1]), jnp.float32)
    for rhs in range(RHS):
        mine = own_rhs == rhs
        parts = (
            row_total(rhs_rows * start, rhs),
            row_total(start * image, rhs),
            row_total(second * image, rhs),
            row_total(start * local_part, rhs) + total(jnp.where(mine, before * filtered, 0.0)),
            row_total(second * local_part, rhs) + total(jnp.where(mine, wave * filtered, 0.0)),
        )
        for index, part in enumerate(parts):
            sums = jnp.where(slot == rhs * len(parts) + index, part, sums)
    devices = counts[0] * counts[1]
    result_ref[pl.ds(X_PAD, devices, stride=SLOT_ROWS), :] = jnp.broadcast_to(
        sums, (devices, sums.shape[1])
    )


def again_body(
    devices,
    message_ref,
    tables_ref,
    depth_high_ref,
    depth_low_ref,
    start_ref,
    near_ref,
    polar_ref,
    image_ref,
    second_ref,
    payload_ref,
    result_ref,
):
    tables = read_tables(tables_ref)
    depth = (depth_high_ref[...], depth_low_ref[...])
    field = sample_from(message_ref, *tables, depth, devices)
    start = start_ref[...]
    polar = polar_ref[...]
    image = start / polar - gather_rows(near_ref) + field - self_coef * start
    second = polar * image
    image_ref[...] = image
    second_ref[...] = second
    store_payload(payload_ref, second)
    spread_into(result_ref, second, *tables, depth, devices)
    clear_spare(result_ref, devices)


def final_body(
    devices,
    message_ref,
    tables_ref,
    depth_high_ref,
    depth_low_ref,
    rhs_ref,
    start_ref,
    image_ref,
    second_ref,
    near_ref,
    polar_ref,
    dipole_ref,
    residual_ref,
):
    tables = read_tables(tables_ref)
    depth = (depth_high_ref[...], depth_low_ref[...])
    field = sample_from(message_ref, *tables, depth, devices)
    second = second_ref[...]
    start = start_ref[...]
    image = image_ref[...]
    image_second = second / polar_ref[...] - gather_rows(near_ref) + field - self_coef * second
    sums = jnp.sum(
        message_ref[pl.ds(X_PAD, devices, stride=SLOT_ROWS), :], axis=0, keepdims=True
    )
    steps = []
    for rhs in range(RHS):
        progress, start_image, second_image, start_next, second_next = [
            sums[:, rhs * 5 + index : rhs * 5 + index + 1] for index in range(5)
        ]
        step = progress / start_image
        progress_next = progress - 2.0 * step * start_image + step * step * second_image
        grown = 1.0 + progress_next / progress
        curvature = (
            grown * grown * start_image
            - step * grown * (start_next + second_image)
            + step * step * second_next
        )
        steps.append((step, grown, progress_next / curvature))
    row = lax.broadcasted_iota(jnp.int32, (RHS, 1), 0)
    step, grown, step_next = [
        sum(jnp.where(row == rhs, steps[rhs][index], 0.0) for rhs in range(RHS))
        for index in range(3)
    ]
    for dim in range(3):
        rows = slice(dim * RHS, (dim + 1) * RHS)
        direction = grown * start[rows] - step * second[rows]
        image_direction = grown * image[rows] - step * image_second[rows]
        dipole_ref[dim] = step * start[rows] + step_next * direction
        residual_ref[dim] = rhs_ref[dim] - step * image[rows] - step_next * image_direction


def near_base(entry, brick_rows):
    return lax.shift_right_logical(entry, 2) * brick_rows + lax.bitwise_and(entry, 3)


def fill_near(scratch, left_ref, stack_ref, right_ref):
    rows = stack_ref.shape[0] // 3
    for row_step in range(3):
        for col_step, source in enumerate((left_ref, stack_ref, right_ref)):
            first = (row_step * 3 + col_step) * rows
            scratch[first : first + rows, :] = source[row_step * rows : (row_step + 1) * rows, :]


def nearest(places, origin, span):
    return places - span * jnp.floor((places - origin) * (1.0 / span) + 0.5)


def unwrap_near(near, stack_ref, tile_count, spans):
    rows = stack_ref.shape[0] // 3
    for dim in range(2):
        origin = stack_ref[rows + dim * tile_count : rows + dim * tile_count + 1, 0:1]
        for brick in range(9):
            first = brick * rows + dim * tile_count
            near[first : first + tile_count, :] = nearest(
                near[first : first + tile_count, :], origin, spans[dim]
            )


def separations(near, base, tile_count, own, origin, spans):
    along_z = nearest(near[pl.ds(base + 2 * tile_count, 1), :], origin, spans[2])
    return [
        near[pl.ds(base, 1), :] - own[0],
        near[pl.ds(base + tile_count, 1), :] - own[1],
        along_z - own[2],
    ]


def add_field(sums, first_term, second_term, apart, near, base, tile_count, quantity):
    for rhs in range(RHS):
        moment = [
            near[pl.ds(base + (quantity + RHS * dim + rhs) * tile_count, 1), :]
            for dim in range(3)
        ]
        projected = moment[0] * apart[0] + moment[1] * apart[1] + moment[2] * apart[2]
        weighted = second_term * projected
        for dim in range(3):
            index = RHS * dim + rhs
            sums[index] = sums[index] + (weighted * apart[dim] - first_term * moment[dim])


def store_sums(sums, columns, rows):
    lane = lax.broadcasted_iota(jnp.int32, (PAIR_ROWS, TILE), 1)
    merged = jnp.zeros((PAIR_ROWS, TILE), jnp.float32)
    for index in range(6):
        merged = jnp.where(lane == index, jnp.sum(sums[index], axis=1, keepdims=True), merged)
    columns[rows, :] = merged


def own_columns(stack_ref, quantities, tile_count, tile, square, columns):
    offset = stack_ref.shape[0] // 3
    for quantity in range(quantities):
        square[quantity : quantity + 1, :] = stack_ref[
            pl.ds(offset + quantity * tile_count + tile, 1), :
        ]
    columns[...] = jnp.transpose(square[...])


def pair_first_body(
    listed,
    tile_count,
    spans,
    lists_ref,
    left_ref,
    stack_ref,
    right_ref,
    after_ref,
    first_ref,
    second_ref,
    field_ref,
    near,
    square,
    columns,
    out_columns,
):
    @pl.when(pl.program_id(0) == 0)
    def _():
        fill_near(near, left_ref, stack_ref, right_ref)
        unwrap_near(near, stack_ref, tile_count, spans)
        square[...] = jnp.zeros_like(square)

    tile = pl.program_id(0)
    brick_rows = stack_ref.shape[0] // 3
    own_columns(stack_ref, 4, tile_count, tile, square, columns)

    @pl.loop(0, TILE // PAIR_ROWS)
    def _(part):
        start = pl.multiple_of(part * PAIR_ROWS, PAIR_ROWS)
        rows = pl.ds(start, PAIR_ROWS)
        mine = columns[rows, :]
        own = [
            jnp.broadcast_to(mine[:, dim : dim + 1], (PAIR_ROWS, TILE)) for dim in range(4)
        ]
        own_damp = thole_a * own[3]
        origin = columns[0:1, 2:3]
        sums = [jnp.zeros((PAIR_ROWS, TILE), jnp.float32) for _ in range(6)]
        itself = (
            lax.broadcasted_iota(jnp.int32, (PAIR_ROWS, TILE), 0) + start
        ) == lax.broadcasted_iota(jnp.int32, (PAIR_ROWS, TILE), 1)
        for entry in range(listed):
            base = near_base(lists_ref[tile * listed + entry], brick_rows)
            apart = separations(near, base, tile_count, own, origin, spans)
            square_dist = apart[0] * apart[0] + apart[1] * apart[1] + apart[2] * apart[2]
            if entry == 0:
                square_dist = jnp.where(itself, 1.0, square_dist)
            inverse = lax.rsqrt(square_dist)
            distance = square_dist * inverse
            inverse_sq = inverse * inverse
            inverse_cube = inverse_sq * inverse
            damp = own_damp * near[pl.ds(base + 3 * tile_count, 1), :]
            cubed = damp * (distance * square_dist)
            damping = jnp.exp(-cubed)
            bell = jnp.exp(-(ewald_beta * ewald_beta) * square_dist)
            turned = 1.0 / (1.0 + (SCREEN_SCALE * ewald_beta) * distance)
            series = jnp.full_like(turned, SCREEN_COEF[-1])
            for coef in SCREEN_COEF[-2::-1]:
                series = series * turned + coef
            screen = bell * turned * series
            gaussian = (2.0 * ewald_beta / math.sqrt(math.pi)) * bell
            first_term = (screen - damping) * inverse_cube + gaussian * inverse_sq
            second_term = (
                3.0 * (screen - (1.0 + cubed) * damping) * inverse_cube
                + gaussian * (2.0 * ewald_beta * ewald_beta + 3.0 * inverse_sq)
            ) * inverse_sq
            if entry == 0:
                first_term = jnp.where(itself, 0.0, first_term)
                second_term = jnp.where(itself, 0.0, second_term)
            place = pl.ds(pl.multiple_of(entry * TILE + start, PAIR_ROWS), PAIR_ROWS)
            first_ref[place, :] = first_term
            second_ref[place, :] = second_term
            add_field(sums, first_term, second_term, apart, near, base, tile_count, 4)
        store_sums(sums, out_columns, rows)

    field_ref[...] = jnp.transpose(out_columns[...])[0:8]


def pair_second_body(
    listed,
    tile_count,
    spans,
    lists_ref,
    left_ref,
    stack_ref,
    right_ref,
    left_moment_ref,
    stack_moment_ref,
    right_moment_ref,
    first_ref,
    second_ref,
    field_ref,
    near,
    near_moment,
    square,
    columns,
    out_columns,
):
    @pl.when(pl.program_id(0) == 0)
    def _():
        fill_near(near, left_ref, stack_ref, right_ref)
        unwrap_near(near, stack_ref, tile_count, spans)
        fill_near(near_moment, left_moment_ref, stack_moment_ref, right_moment_ref)
        square[...] = jnp.zeros_like(square)

    tile = pl.program_id(0)
    brick_rows = stack_ref.shape[0] // 3
    moment_rows = stack_moment_ref.shape[0] // 3
    own_columns(stack_ref, 3, tile_count, tile, square, columns)

    @pl.loop(0, TILE // PAIR_ROWS)
    def _(part):
        start = pl.multiple_of(part * PAIR_ROWS, PAIR_ROWS)
        rows = pl.ds(start, PAIR_ROWS)
        mine = columns[rows, :]
        own = [
            jnp.broadcast_to(mine[:, dim : dim + 1], (PAIR_ROWS, TILE)) for dim in range(3)
        ]
        origin = columns[0:1, 2:3]
        sums = [jnp.zeros((PAIR_ROWS, TILE), jnp.float32) for _ in range(6)]
        for entry in range(listed):
            listing = lists_ref[tile * listed + entry]
            base = near_base(listing, brick_rows)
            apart = separations(near, base, tile_count, own, origin, spans)
            place = pl.ds(pl.multiple_of(entry * TILE + start, PAIR_ROWS), PAIR_ROWS)
            add_field(
                sums,
                first_ref[place, :],
                second_ref[place, :],
                apart,
                near_moment,
                near_base(listing, moment_rows),
                tile_count,
                0,
            )
        store_sums(sums, out_columns, rows)

    field_ref[...] = jnp.transpose(out_columns[...])[0:8]


def shift(source, axis, step):
    count = lax.axis_size(axis)
    return lax.ppermute(source, axis, [(i, (i + step) % count) for i in range(count)])


def near_stack(payload):
    stack = jnp.concatenate([shift(payload, "row", 1), payload, shift(payload, "row", -1)], axis=0)
    return shift(stack, "col", 1), stack, shift(stack, "col", -1)


def whole(shape):
    return pl.BlockSpec(shape, lambda *_: (0,) * len(shape))


def anywhere():
    return pl.BlockSpec(memory_space=pl.ANY)


def call(body, outs, *operands, after=()):
    def run(*refs):
        body(*refs[len(after) :])

    return pl.pallas_call(
        run,
        grid=(1,),
        in_specs=[anywhere()] * len(after) + [whole(operand.shape) for operand in operands],
        out_specs=[whole(shape) for shape, _ in outs],
        out_shape=[jax.ShapeDtypeStruct(shape, dtype) for shape, dtype in outs],
        compiler_params=pltpu.CompilerParams(vmem_limit_bytes=VMEM_LIMIT),
        cost_estimate=pl.CostEstimate(
            flops=200_000_000, bytes_accessed=4 << 20, transcendentals=0
        ),
    )(*after, *operands)


def pair_call(body, outs, tiles, blocked, scratch, lists, *operands, after=()):
    def block(operand):
        rows = operand.shape[0] // tiles
        return pl.BlockSpec((rows, operand.shape[1]), lambda i, s: (i, 0))

    out_shape = [jax.ShapeDtypeStruct(shape, jnp.float32) for shape in outs]
    plain = len(operands) - blocked
    return pl.pallas_call(
        body,
        out_shape=out_shape,
        grid_spec=pltpu.PrefetchScalarGridSpec(
            num_scalar_prefetch=1,
            grid=(tiles,),
            in_specs=[whole(operand.shape) for operand in operands[:plain]]
            + [block(operand) for operand in operands[plain:]]
            + [anywhere()] * len(after),
            out_specs=[block(shape) for shape in out_shape],
            scratch_shapes=[pltpu.VMEM(shape, jnp.float32) for shape in scratch],
        ),
        compiler_params=pltpu.CompilerParams(vmem_limit_bytes=VMEM_LIMIT),
        cost_estimate=pl.CostEstimate(
            flops=80_000_000, bytes_accessed=8 << 20, transcendentals=1 << 21
        ),
    )(lists, *operands, *after)


def exchange(message, devices):
    shape = message.shape
    sent = message.reshape(devices, 1, -1)
    return lax.all_to_all(sent, ("row", "col"), split_axis=0, concat_axis=0, tiled=True).reshape(
        shape
    )


def slab_local(field_rhs, positions, polar, grid_base, tile_lists):
    rows_count = lax.axis_size("row")
    cols_count = lax.axis_size("col")
    counts = (rows_count, cols_count)
    devices = rows_count * cols_count
    lengths = (CX * rows_count, CY * cols_count, KZ)
    spans = tuple(float(length) for length in lengths)
    atoms = polar.shape[-1]
    tile_count = atoms // TILE
    listed = tile_lists.shape[-1]
    tables = slab_tables(rows_count, cols_count)
    f32 = jnp.float32
    rhs = jnp.swapaxes(field_rhs[0, 0], 0, 1)
    place = positions.reshape(3, atoms)
    base = grid_base.reshape(3, atoms)
    polar = polar.reshape(1, atoms)
    lists = tile_lists.reshape(-1)
    brick_rows = (4 + 3 * RHS) * tile_count
    moment_rows = 3 * RHS * tile_count
    message_shape = (devices * SLOT_ROWS, KZ // devices * RHS * Y_PAD)
    row_shape = (3 * RHS, atoms)
    square = (TILE, TILE)

    start, payload = call(pack_body, [(row_shape, f32), ((brick_rows, TILE), f32)], rhs, place, polar)
    near = near_stack(payload)

    def setup(*refs):
        setup_body(lengths, devices, *refs)

    message, splines, depth_high, depth_low = call(
        setup,
        [
            (message_shape, f32),
            ((2 * SLOT_ROWS + 2 * Y_PAD, atoms), f32),
            ((KZ, 2 * atoms), jnp.bfloat16),
            ((KZ, 2 * atoms), jnp.bfloat16),
        ],
        place,
        base,
        start,
        *[jnp.asarray(table) for table in tables["along_z"]],
    )
    position = lax.axis_index("row") * cols_count + lax.axis_index("col")
    kernel = lax.dynamic_index_in_dim(jnp.asarray(tables["kernel"]), position, 0, keepdims=False)
    constants = (
        kernel,
        jnp.asarray(tables["forward_x"]),
        jnp.asarray(tables["backward_x"]),
        *[jnp.asarray(table) for table in tables["block"]],
        *[jnp.asarray(table) for table in tables["block_back"]],
    )
    arrived = exchange(message, devices)

    def middle_first(*refs):
        middle_first_body(counts, *refs)

    mixed, wave = call(
        middle_first,
        [(message_shape, f32), (kernel.shape, f32)],
        arrived,
        *constants,
        after=(near[0], near[2]),
    )
    returned = exchange(mixed, devices)

    def pair_first(*refs):
        pair_first_body(listed, tile_count, spans, *refs)

    first_term, second_term, direct = pair_call(
        pair_first,
        [(tile_count * listed * TILE, TILE)] * 2 + [(tile_count * 8, TILE)],
        tile_count,
        0,
        [(9 * brick_rows, TILE)] + [square] * 3,
        lists,
        *near,
        after=(wave,),
    )

    def again(*refs):
        again_body(devices, *refs)

    image, second, moments, message = call(
        again,
        [(row_shape, f32), (row_shape, f32), ((moment_rows, TILE), f32), (message_shape, f32)],
        returned,
        splines,
        depth_high,
        depth_low,
        start,
        direct,
        polar,
    )
    near_moments = near_stack(moments)
    arrived = exchange(message, devices)

    def pair_second(*refs):
        pair_second_body(listed, tile_count, spans, *refs)

    (direct,) = pair_call(
        pair_second,
        [(tile_count * 8, TILE)],
        tile_count,
        2,
        [(9 * brick_rows, TILE), (9 * moment_rows, TILE)] + [square] * 3,
        lists,
        *near,
        *near_moments,
        first_term,
        second_term,
    )

    def middle_second(*refs):
        middle_second_body(counts, *refs)

    (mixed,) = call(
        middle_second,
        [(message_shape, f32)],
        arrived,
        *constants,
        wave,
        rhs,
        start,
        image,
        second,
        direct,
        polar,
    )
    returned = exchange(mixed, devices)

    def final(*refs):
        final_body(devices, *refs)

    outs = call(
        final,
        [(rhs.shape, f32), (rhs.shape, f32)],
        returned,
        splines,
        depth_high,
        depth_low,
        rhs,
        start,
        image,
        second,
        direct,
        polar,
    )
    return tuple(jnp.swapaxes(out, 0, 1)[None, None] for out in outs)


def solution(mesh):
    placed = (
        P("row", "col", None, None, None),
        P("row", "col", None, None),
        P("row", "col", None),
        P("row", "col", None, None),
        P("row", "col", None, None),
    )
    devices = mesh.shape["row"] * mesh.shape["col"]
    return jax.shard_map(
        slab_local if KZ % devices == 0 else pencil_local,
        mesh=mesh,
        in_specs=placed,
        out_specs=(P("row", "col", None, None, None), P("row", "col", None, None, None)),
        check_vma=False,
    )
```

```python
import math

import jax
import jax.numpy as jnp
import ml_dtypes
import numpy as np
from jax import lax
from jax.experimental import pallas as pl
from jax.experimental.pallas import tpu as pltpu
from jax.sharding import PartitionSpec as P

CX = 8
CY = 4
KZ = 256
TILE = 128
RHS = 2
ITERS = 2


ewald_beta = 0.4
thole_a = 0.39
self_coef = 4.0 * ewald_beta**3 / (3.0 * math.sqrt(math.pi))
highest = lax.Precision.HIGHEST


def with_halo(cells, sides, width):
    for axis, dim in sides:
        count = lax.axis_size(axis)
        head = lax.slice_in_dim(cells, 0, width, axis=dim)
        tail = lax.slice_in_dim(cells, cells.shape[dim] - width, cells.shape[dim], axis=dim)
        cells = jnp.concatenate(
            [
                lax.ppermute(tail, axis, [(i, (i + 1) % count) for i in range(count)]),
                cells,
                lax.ppermute(head, axis, [((i + 1) % count, i) for i in range(count)]),
            ],
            axis=dim,
        )
    return cells


def spline_table(fraction):
    previous = {0: jnp.ones_like(fraction)}
    fourth = previous
    for degree in range(2, 6):
        current = {}
        for offset in range(degree):
            abscissa = fraction + offset
            summed = abscissa * previous.get(offset, 0.0) + (degree - abscissa) * previous.get(
                offset - 1, 0.0
            )
            current[offset] = summed / (degree - 1)
        if degree == 4:
            fourth = current
        previous = current
    values = jnp.stack([previous[4 - stencil] for stencil in range(5)])
    slopes = jnp.stack(
        [fourth.get(4 - stencil, 0.0) - fourth.get(3 - stencil, 0.0) for stencil in range(5)]
    )
    return (values, slopes)


def spline_modulus(wave_index, length):
    spline_coef = (1.0 / 24.0, 11.0 / 24.0, 11.0 / 24.0, 1.0 / 24.0)
    cosine_sum = jnp.zeros(wave_index.shape, jnp.float32)
    sine_sum = jnp.zeros(wave_index.shape, jnp.float32)
    for offset in range(4):
        angles = 2.0 * math.pi / length * (wave_index * offset % length).astype(jnp.float32)
        cosine_sum = cosine_sum + spline_coef[offset] * jnp.cos(angles)
        sine_sum = sine_sum + spline_coef[offset] * jnp.sin(angles)
    return cosine_sum * cosine_sum + sine_sum * sine_sum


def folded_square(wave_index, length):
    nearest = jnp.minimum(wave_index, length - wave_index).astype(jnp.float32) / length
    return nearest * nearest


def influence(wave_x, wave_y, wave_z, length_x, length_y, length_z):
    wave_norm = (
        folded_square(wave_x, length_x)
        + folded_square(wave_y, length_y)
        + folded_square(wave_z, length_z)
    )
    modulus = (
        spline_modulus(wave_x, length_x)
        * spline_modulus(wave_y, length_y)
        * spline_modulus(wave_z, length_z)
    )
    excluded = (wave_x * 2 == length_x) | (wave_y * 2 == length_y) | (wave_z * 2 == length_z)
    excluded = excluded | (wave_x == 0) & (wave_y == 0) & (wave_z == 0)
    safe_norm = jnp.where(excluded, 1.0, wave_norm)
    safe_modulus = jnp.where(excluded, 1.0, modulus)
    result = jnp.exp(-(math.pi**2 / ewald_beta**2) * safe_norm) / (
        math.pi * safe_norm * safe_modulus
    )
    return jnp.where(excluded, 0.0, result)


def tile_field(own_static, near_static, near_dipole, box_spans):
    listed_count = near_static.shape[0]
    tile_width = own_static.shape[1]
    box_span = jnp.array(box_spans, dtype=jnp.float32)[None, :, None, None]
    separation = near_static[:, 0:3, None, :] - own_static[None, 0:3, :, None]
    separation = separation - box_span * jnp.floor(separation / box_span + 0.5)
    dist_sq = jnp.sum(separation * separation, axis=1)
    itself = (jnp.arange(listed_count)[:, None, None] == 0) & (
        jnp.arange(tile_width)[:, None] == jnp.arange(tile_width)[None, :]
    )[None]
    safe_sq = jnp.where(itself, 1.0, dist_sq)
    distance = jnp.sqrt(safe_sq)
    scaled = distance / (own_static[3][None, :, None] * near_static[:, 3][:, None, :])
    cubed = thole_a * scaled * scaled * scaled
    damping = jnp.exp(-cubed)
    screen = lax.erfc(ewald_beta * distance)
    gaussian = 2.0 * ewald_beta / math.sqrt(math.pi) * jnp.exp(-(ewald_beta * ewald_beta) * safe_sq)
    inverse_sq = 1.0 / safe_sq
    inverse_cube = inverse_sq / distance
    first_term = (screen - damping) * inverse_cube + gaussian * inverse_sq
    second = (
        3.0 * (screen - (1.0 + cubed) * damping) * inverse_cube * inverse_sq
        + gaussian * (2.0 * ewald_beta * ewald_beta + 3.0 * inverse_sq) * inverse_sq
    )
    first_term = jnp.where(itself, 0.0, first_term)
    second = jnp.where(itself, 0.0, second)
    projected = jnp.sum(near_dipole[:, :, :, None, :] * separation[:, None, :, :, :], axis=2)
    weighted = second[:, None] * projected
    outward = jnp.sum(weighted[:, :, None] * separation[:, None], axis=(0, 4))
    inward = jnp.sum(first_term[:, None, None] * near_dipole[:, :, :, None, :], axis=(0, 4))
    return outward - inward


def hartley(length):
    counter = jnp.arange(length, dtype=jnp.int32)
    angles = (
        2.0 * math.pi / length * (counter[:, None] * counter[None, :] % length).astype(jnp.float32)
    )
    return jnp.cos(angles) + jnp.sin(angles)


def placed_table(first_cell, weights, extent):
    slot_index = jnp.arange(extent, dtype=jnp.int32)[:, None]
    placed = jnp.zeros((extent, first_cell.shape[0]), jnp.float32)
    for stencil in range(5):
        placed = placed + jnp.where(
            slot_index == (first_cell[None, :] + stencil) % extent, weights[stencil][None, :], 0.0
        )
    return placed


def pad_axis(source, axis_pos, leading, trailing):
    widths = [(0, 0)] * source.ndim
    widths[axis_pos] = (leading, trailing)
    return jnp.pad(source, widths)


def fold_cycle(cycle_only, axis_pos, inner_len):
    middle = lax.slice_in_dim(cycle_only, 4, inner_len + 4, axis=axis_pos)
    lower_cycle = lax.slice_in_dim(cycle_only, 0, 2, axis=axis_pos)
    upper_cycle = lax.slice_in_dim(cycle_only, inner_len + 6, inner_len + 8, axis=axis_pos)
    return (
        middle
        + pad_axis(lower_cycle, axis_pos, 0, inner_len - 2)
        + pad_axis(upper_cycle, axis_pos, inner_len - 2, 0)
    )


def clear_inside(extended, extents):
    inside = None
    for axis_pos, inner_len in extents:
        slot_index = lax.broadcasted_iota(jnp.int32, extended.shape, axis_pos)
        within = (slot_index >= 2) & (slot_index < inner_len + 6)
        inside = within if inside is None else inside & within
    return jnp.where(inside, 0.0, extended)


def inner_sum(left_arr, right_arr):
    return lax.psum(jnp.sum(left_arr * right_arr, axis=(1, 2)), ("row", "col"))


def pencil_local(field_rhs, positions, polar, grid_base, tile_lists):
    rows_count = lax.axis_size("row")
    cols_count = lax.axis_size("col")
    grid_x = CX * rows_count
    grid_y = CY * cols_count
    atom_count = polar.shape[-1]
    tile_count = atom_count // TILE
    slab_depth = KZ // tile_count
    window_len = slab_depth + 4
    box_spans = (float(grid_x), float(grid_y), float(KZ))
    own_place = positions[0, 0]
    own_base = grid_base[0, 0]
    own_polar = polar[0, 0]
    lengths = jnp.array([grid_x, grid_y, KZ], dtype=jnp.int32)[:, None]
    cell_index = (own_base + 2) % lengths
    fraction = own_place - cell_index.astype(jnp.float32)
    values, slopes = spline_table(fraction)
    first_x = (own_base[0] - lax.axis_index("row") * CX + 2) % grid_x
    first_y = (own_base[1] - lax.axis_index("col") * CY + 2) % grid_y
    rows_x = placed_table(first_x, values[:, 0], CX + 4)
    slope_x = placed_table(first_x, slopes[:, 0], CX + 4)
    rows_y = placed_table(first_y, values[:, 1], CY + 4)
    slope_y = placed_table(first_y, slopes[:, 1], CY + 4)
    tile_start = jnp.arange(atom_count, dtype=jnp.int32) // TILE * slab_depth
    first_z = (own_base[2] + 2 - tile_start) % KZ
    rows_z = placed_table(first_z, values[:, 2], window_len)
    slope_z = placed_table(first_z, slopes[:, 2], window_len)
    plane_count = (CX + 4) * (CY + 4)
    plane_dx = (slope_x[:, None, :] * rows_y[None, :, :]).reshape(plane_count, atom_count)
    plane_dy = (rows_x[:, None, :] * slope_y[None, :, :]).reshape(plane_count, atom_count)
    plane_flat = (rows_x[:, None, :] * rows_y[None, :, :]).reshape(plane_count, atom_count)
    window_rows = jnp.moveaxis(rows_z.reshape(window_len, tile_count, TILE), 1, 0)
    window_slope = jnp.moveaxis(slope_z.reshape(window_len, tile_count, TILE), 1, 0)
    depth_table = jnp.concatenate([window_rows, window_slope], axis=2)
    grid_scale = 1.0 / (grid_x * grid_y * KZ)
    hartley_x = hartley(grid_x)
    hartley_y = hartley(grid_y)
    hartley_z = hartley(KZ)
    block_y = grid_y // rows_count
    block_z = KZ // cols_count
    wave_x = jnp.arange(grid_x, dtype=jnp.int32)[:, None, None]
    wave_y = (lax.axis_index("row") * block_y + jnp.arange(block_y, dtype=jnp.int32))[None, :, None]
    wave_z = (lax.axis_index("col") * block_z + jnp.arange(block_z, dtype=jnp.int32))[None, None, :]
    kernel = influence(wave_x, wave_y, wave_z, grid_x, grid_y, KZ) * grid_scale
    root_scale = jnp.power(own_polar, 1.0 / 6.0)
    own_static = jnp.concatenate([own_place, root_scale[None]], axis=0)
    near_static = with_halo(own_static[None, None], (("row", 0), ("col", 1)), 1)
    near_static = jnp.moveaxis(near_static.reshape(9, 4, tile_count, TILE), 2, 1).reshape(
        9 * tile_count, 4, TILE
    )
    own_tiles = jnp.moveaxis(own_static.reshape(4, tile_count, TILE), 1, 0)
    own_lists = tile_lists[0, 0]
    polar_wide = own_polar[None, None, :]
    solution = jnp.zeros_like(field_rhs[0, 0])
    residual = field_rhs[0, 0]
    scaled_res = polar_wide * residual
    direction = scaled_res
    progress = inner_sum(residual, scaled_res)
    for iteration in range(ITERS):
        near_dip = with_halo(direction[None, None], (("row", 0), ("col", 1)), 1)
        near_dip = jnp.moveaxis(near_dip.reshape(9, RHS, 3, tile_count, TILE), 3, 1).reshape(
            9 * tile_count, RHS, 3, TILE
        )

        def one_tile(tile_pos):
            picked = own_lists[tile_pos]
            return tile_field(own_tiles[tile_pos], near_static[picked], near_dip[picked], box_spans)

        fields = lax.map(one_tile, jnp.arange(tile_count, dtype=jnp.int32))
        direct = jnp.moveaxis(fields, 0, 2).reshape(RHS, 3, atom_count)
        slope_terms = (
            direction[:, 0, None, :] * plane_dx[None] + direction[:, 1, None, :] * plane_dy[None]
        )
        flat_terms = direction[:, 2, None, :] * plane_flat[None]
        spread_left = jnp.concatenate(
            [
                slope_terms.reshape(RHS, plane_count, tile_count, TILE),
                flat_terms.reshape(RHS, plane_count, tile_count, TILE),
            ],
            axis=3,
        )
        spread_windows = jnp.einsum("sptb,twb->sptw", spread_left, depth_table, precision=highest)
        main_part = spread_windows[..., :slab_depth].reshape(spread_windows.shape[:-2] + (KZ,))
        tail_part = pad_axis(
            spread_windows[..., slab_depth:], spread_windows.ndim - 1, 0, slab_depth - 4
        )
        tail_part = tail_part.reshape(spread_windows.shape[:-2] + (KZ,))[..., : KZ + 4 - slab_depth]
        last_axis = main_part.ndim - 1
        padded_line = pad_axis(main_part, last_axis, 0, 4) + pad_axis(
            tail_part, last_axis, slab_depth, 0
        )
        inner = padded_line[..., 2 : KZ + 2]
        spread_tile = (
            inner
            + pad_axis(padded_line[..., 0:2], last_axis, KZ - 2, 0)
            + pad_axis(padded_line[..., KZ + 2 : KZ + 4], last_axis, 0, KZ - 2)
        ).reshape(RHS, CX + 4, CY + 4, KZ)
        extended = with_halo(spread_tile, (("row", 1), ("col", 2)), 2)
        cycle_only = clear_inside(extended, ((1, CX), (2, CY)))
        folded = fold_cycle(fold_cycle(cycle_only, 1, CX), 2, CY)
        spectrum = jnp.einsum(
            "sxyz,zk->sxyk",
            spread_tile[:, 2 : CX + 2, 2 : CY + 2] + folded,
            hartley_z,
            precision=highest,
        )
        along_y = jnp.einsum(
            "sxyz,yk->sxkz",
            lax.all_to_all(spectrum, "col", split_axis=3, concat_axis=2, tiled=True),
            hartley_y,
            precision=highest,
        )
        along_x = (
            jnp.einsum(
                "sxyz,xk->skyz",
                lax.all_to_all(along_y, "row", split_axis=2, concat_axis=1, tiled=True),
                hartley_x,
                precision=highest,
            )
            * kernel[None]
        )
        mixed_part = jnp.einsum("sxyz,xk->skyz", along_x, hartley_x, precision=highest)
        returned = lax.all_to_all(mixed_part, "row", split_axis=1, concat_axis=2, tiled=True)
        swapped = jnp.einsum("sxyz,yk->sxkz", returned, hartley_y, precision=highest)
        restored = lax.all_to_all(swapped, "col", split_axis=2, concat_axis=3, tiled=True)
        padded = with_halo(
            jnp.einsum("sxyz,zk->sxyk", restored, hartley_z, precision=highest),
            (("row", 1), ("col", 2)),
            2,
        )
        line = padded.reshape(RHS, plane_count, KZ)
        extended_line = jnp.concatenate([line[..., KZ - 2 :], line, line[..., :2]], axis=-1)
        windows = jnp.stack(
            [
                extended_line[..., tile * slab_depth : tile * slab_depth + window_len]
                for tile in range(tile_count)
            ],
            axis=-2,
        )
        sampled = jnp.einsum("sptw,twb->sptb", windows, depth_table, precision=highest)
        with_flat = sampled[..., :TILE].reshape(RHS, plane_count, atom_count)
        with_slope = sampled[..., TILE:].reshape(RHS, plane_count, atom_count)
        recip_part = jnp.stack(
            [
                jnp.sum(with_flat * plane_dx[None], axis=1),
                jnp.sum(with_flat * plane_dy[None], axis=1),
                jnp.sum(with_slope * plane_flat[None], axis=1),
            ],
            axis=1,
        )
        image_field = direction / polar_wide - direct + recip_part - self_coef * direction
        step_size = (progress / inner_sum(direction, image_field))[:, None, None]
        solution = solution + step_size * direction
        residual = residual - step_size * image_field
        scaled_res = polar_wide * residual
        progress_next = inner_sum(residual, scaled_res)
        direction = scaled_res + (progress_next / progress)[:, None, None] * direction
        progress = progress_next
    return (solution[None, None], residual[None, None])


X_PAD = CX + 4
Y_PAD = CY + 4
SLOT_ROWS = 16
SPLIT = 2
VMEM_LIMIT = 60_000_000
PAIR_ROWS = 32
GROUP = 8
SCREEN_SCALE = 0.4
SCREEN_COEF = (
    0.22567588090896606,
    0.2256690263748169,
    0.20785020291805267,
    0.16849851608276367,
    0.14156343042850494,
    -0.005832736846059561,
    0.16930203139781952,
    -0.1830107867717743,
    0.05028456076979637,
)


def halves(value):
    high = value.astype(jnp.bfloat16)
    return high, (value - high.astype(jnp.float32)).astype(jnp.bfloat16)


def halves_np(value):
    value = value.astype(np.float32)
    high = value.astype(ml_dtypes.bfloat16)
    return high, (value - high.astype(np.float32)).astype(ml_dtypes.bfloat16)


def product(left, right, left_dim=1, right_dim=0):
    def one(first, second):
        return lax.dot_general(
            first,
            second,
            (((left_dim,), (right_dim,)), ((), ())),
            preferred_element_type=jnp.float32,
        )

    return one(left[0], right[0]) + (one(left[1], right[0]) + one(left[0], right[1]))


def cas_np(wave, place, length):
    angles = 2.0 * np.pi / length * (wave[:, None] * place[None, :] % length)
    return np.cos(angles) + np.sin(angles)


def modulus_np(wave, length):
    coef = np.array([1.0, 11.0, 11.0, 1.0]) / 24.0
    angles = 2.0 * np.pi / length * (wave[:, None] * np.arange(4)[None, :])
    return (coef * np.cos(angles)).sum(1) ** 2 + (coef * np.sin(angles)).sum(1) ** 2


def influence_np(length_x, length_y, length_z):
    total = np.zeros((length_x, length_y, length_z))
    modulus = np.ones((length_x, length_y, length_z))
    excluded = np.zeros((length_x, length_y, length_z), bool)
    for axis, length in enumerate((length_x, length_y, length_z)):
        wave = np.arange(length)
        shape = [1, 1, 1]
        shape[axis] = length
        total = total + ((np.minimum(wave, length - wave) / length) ** 2).reshape(shape)
        modulus = modulus * modulus_np(wave, length).reshape(shape)
        excluded = excluded | (wave * 2 == length).reshape(shape)
    excluded[0, 0, 0] = True
    safe = np.where(excluded, 1.0, total)
    result = np.exp(-(np.pi**2) / ewald_beta**2 * safe) / (
        np.pi * safe * np.where(excluded, 1.0, modulus)
    )
    return np.where(excluded, 0.0, result) / (length_x * length_y * length_z)


def slab_tables(rows_count, cols_count):
    grid_x = CX * rows_count
    grid_y = CY * cols_count
    devices = rows_count * cols_count
    chunk = KZ // devices
    wave_z = (np.arange(devices)[None, :] * chunk + np.arange(chunk)[:, None]).reshape(-1)
    along_z = cas_np(wave_z, np.arange(KZ), KZ)
    place_x = np.arange(rows_count)[:, None] * CX + np.arange(X_PAD)[None, :] - 2
    along_x = cas_np(np.arange(grid_x), place_x.reshape(-1) % grid_x, grid_x)
    padded_x = np.zeros((grid_x, rows_count, SLOT_ROWS))
    padded_x[:, :, :X_PAD] = along_x.reshape(grid_x, rows_count, X_PAD)
    padded_x = padded_x.reshape(grid_x, rows_count * SLOT_ROWS)
    x_high, x_low = halves_np(padded_x)
    forward_x = np.concatenate([x_high, x_low, x_high], axis=1)
    backward_x = np.concatenate([x_high.T, x_low.T, x_high.T], axis=1)
    place_y = (np.arange(cols_count)[:, None] * CY + np.arange(Y_PAD)[None, :] - 2) % grid_y
    along_y = cas_np(np.arange(grid_y), place_y.reshape(-1), grid_y)
    along_y = along_y.reshape(grid_y, cols_count, Y_PAD)
    units = chunk * RHS // SPLIT
    block = np.einsum("uv,kcy->cuyvk", np.eye(units), along_y)
    block = block.reshape(cols_count * units * Y_PAD, units * grid_y)
    kernel = influence_np(grid_x, grid_y, KZ).reshape(grid_x, grid_y, devices, chunk)
    kernel = np.transpose(kernel, (2, 0, 3, 1))[:, :, :, None, :]
    kernel = np.broadcast_to(kernel, (devices, grid_x, chunk, RHS, grid_y))
    kernel = kernel.reshape(devices, grid_x, SPLIT, units * grid_y)
    kernel = np.moveaxis(kernel, 2, 1).reshape(devices, SPLIT * grid_x, units * grid_y)
    kernel = kernel.astype(np.float32)
    return dict(
        along_z=halves_np(along_z),
        forward_x=forward_x,
        backward_x=backward_x,
        block=halves_np(block),
        block_back=halves_np(np.ascontiguousarray(block.T)),
        kernel=kernel,
    )


def pack_body(rhs_ref, place_ref, polar_ref, start_ref, payload_ref):
    polar = polar_ref[...]
    start = read_rows(rhs_ref) * polar
    start_ref[...] = start
    place = [place_ref[dim] for dim in range(3)]
    everything = jnp.concatenate(place + [1.0 / jnp.sqrt(polar), start], axis=0)
    store_payload(payload_ref, everything)


def read_rows(rows_ref):
    return jnp.concatenate([rows_ref[dim] for dim in range(3)], axis=0)


def store_payload(payload_ref, everything):
    tile_count = everything.shape[1] // TILE
    for quantity in range(everything.shape[0]):
        for tile in range(tile_count):
            row = quantity * tile_count + tile
            payload_ref[row : row + 1, :] = everything[
                quantity : quantity + 1, tile * TILE : (tile + 1) * TILE
            ]


def placed_rows(slot, weights, extent):
    slot_index = lax.broadcasted_iota(jnp.int32, (extent, slot.shape[1]), 0)
    placed = jnp.zeros((extent, slot.shape[1]), jnp.float32)
    for stencil in range(5):
        target = slot + stencil
        if extent == KZ:
            target = jnp.where(target >= KZ, target - KZ, target)
        placed = placed + jnp.where(slot_index == target, weights[stencil], 0.0)
    return placed


def spread_into(message_ref, moment, rows_x, slope_x, rows_y, slope_y, depth, devices):
    blocks = []
    for step in range(X_PAD):
        flat_x = rows_x[step : step + 1]
        tilt_x = slope_x[step : step + 1]
        for rhs in range(RHS):
            part_x = tilt_x * moment[rhs : rhs + 1]
            part_y = flat_x * moment[RHS + rhs : RHS + rhs + 1]
            part_z = flat_x * moment[2 * RHS + rhs : 2 * RHS + rhs + 1]
            blocks.append(
                jnp.concatenate([part_x * rows_y + part_y * slope_y, part_z * rows_y], axis=1)
            )
    charges = jnp.concatenate(blocks, axis=0)
    spectrum = product(depth, halves(charges), 1, 1)
    chunk = KZ // devices
    width = RHS * Y_PAD
    for step in range(X_PAD):
        message_ref[pl.ds(step, devices, stride=SLOT_ROWS), :] = jnp.concatenate(
            [
                spectrum[unit * devices : (unit + 1) * devices, step * width : (step + 1) * width]
                for unit in range(chunk)
            ],
            axis=1,
        )


def sample_from(message_ref, rows_x, slope_x, rows_y, slope_y, depth, devices):
    chunk = KZ // devices
    width = RHS * Y_PAD
    pieces = [
        message_ref[pl.ds(step, devices, stride=SLOT_ROWS), :] for step in range(X_PAD)
    ]
    spare = jnp.zeros((devices, KZ - X_PAD * width), jnp.float32)
    spectrum = jnp.concatenate(
        [
            jnp.concatenate(
                [piece[:, unit * width : (unit + 1) * width] for piece in pieces] + [spare], axis=1
            )
            for unit in range(chunk)
        ],
        axis=0,
    )
    spectrum = jnp.transpose(spectrum)[: X_PAD * width]
    sampled = product(halves(spectrum), depth, 1, 0)
    atoms = rows_x.shape[1]
    fields = [None] * (3 * RHS)
    for rhs in range(RHS):
        sum_x = sum_y = sum_z = None
        for step in range(X_PAD):
            first = step * width + rhs * Y_PAD
            flat = sampled[first : first + Y_PAD, :atoms]
            tilt = sampled[first : first + Y_PAD, atoms:]
            part_x = slope_x[step : step + 1] * flat
            part_y = rows_x[step : step + 1] * flat
            part_z = rows_x[step : step + 1] * tilt
            sum_x = part_x if sum_x is None else sum_x + part_x
            sum_y = part_y if sum_y is None else sum_y + part_y
            sum_z = part_z if sum_z is None else sum_z + part_z
        fields[rhs] = jnp.sum(sum_x * rows_y, axis=0, keepdims=True)
        fields[RHS + rhs] = jnp.sum(sum_y * slope_y, axis=0, keepdims=True)
        fields[2 * RHS + rhs] = jnp.sum(sum_z * rows_y, axis=0, keepdims=True)
    return jnp.concatenate(fields, axis=0)


def read_tables(tables_ref):
    return (
        tables_ref[0:X_PAD],
        tables_ref[SLOT_ROWS : SLOT_ROWS + X_PAD],
        tables_ref[2 * SLOT_ROWS : 2 * SLOT_ROWS + Y_PAD],
        tables_ref[2 * SLOT_ROWS + Y_PAD : 2 * SLOT_ROWS + 2 * Y_PAD],
    )


def clear_spare(message_ref, devices):
    spare = jnp.zeros((devices, message_ref.shape[1]), jnp.float32)
    for step in range(X_PAD, SLOT_ROWS):
        message_ref[pl.ds(step, devices, stride=SLOT_ROWS), :] = spare


def join_stack(stack_ref, up_ref, payload_ref, down_ref):
    rows = payload_ref.shape[0]
    stack_ref[0:rows] = up_ref[...]
    stack_ref[rows : 2 * rows] = payload_ref[...]
    stack_ref[2 * rows : 3 * rows] = down_ref[...]


def setup_body(
    lengths,
    devices,
    place_ref,
    base_ref,
    start_ref,
    z_high_ref,
    z_low_ref,
    up_ref,
    payload_ref,
    down_ref,
    message_ref,
    tables_ref,
    depth_high_ref,
    depth_low_ref,
    stack_ref,
):
    join_stack(stack_ref, up_ref, payload_ref, down_ref)
    base = [base_ref[dim] for dim in range(3)]
    fractions = []
    cells = []
    for dim in range(3):
        cell = base[dim] + 2
        cell = jnp.where(cell >= lengths[dim], cell - lengths[dim], cell)
        cells.append(cell)
        fractions.append(place_ref[dim] - cell.astype(jnp.float32))
    values, slopes = spline_table(jnp.concatenate(fractions, axis=0))
    values = [[values[stencil][dim : dim + 1] for stencil in range(5)] for dim in range(3)]
    slopes = [[slopes[stencil][dim : dim + 1] for stencil in range(5)] for dim in range(3)]
    slot_x = lax.rem(cells[0], CX)
    slot_y = lax.rem(cells[1], CY)
    tables_ref[0:SLOT_ROWS] = placed_rows(slot_x, values[0], SLOT_ROWS)
    tables_ref[SLOT_ROWS : 2 * SLOT_ROWS] = placed_rows(slot_x, slopes[0], SLOT_ROWS)
    tables_ref[2 * SLOT_ROWS : 2 * SLOT_ROWS + Y_PAD] = placed_rows(slot_y, values[1], Y_PAD)
    tables_ref[2 * SLOT_ROWS + Y_PAD : 2 * SLOT_ROWS + 2 * Y_PAD] = placed_rows(
        slot_y, slopes[1], Y_PAD
    )
    window = jnp.concatenate(
        [
            placed_rows(base[2], values[2], KZ),
            placed_rows(base[2], slopes[2], KZ),
        ],
        axis=1,
    )
    depth = product((z_high_ref[...], z_low_ref[...]), halves(window), 1, 0)
    depth = halves(depth)
    depth_high_ref[...] = depth[0]
    depth_low_ref[...] = depth[1]
    spread_into(message_ref, start_ref[...], *read_tables(tables_ref), depth, devices)
    clear_spare(message_ref, devices)


def transform_in(message_ref, forward_ref, block_high_ref, block_low_ref, rows_count, cols_count):
    gathered = jnp.concatenate(
        [
            jnp.concatenate(
                [
                    message_ref[(r * cols_count + c) * SLOT_ROWS :][:SLOT_ROWS]
                    for r in range(rows_count)
                ],
                axis=0,
            )
            for c in range(cols_count)
        ],
        axis=1,
    )
    high, low = halves(gathered)
    along = jnp.dot(
        forward_ref[...],
        jnp.concatenate([high, high, low], axis=0),
        preferred_element_type=jnp.float32,
    )
    part = along.shape[1] // cols_count // SPLIT
    along = jnp.concatenate(
        [
            jnp.concatenate(
                [
                    along[:, (c * SPLIT + half) * part : (c * SPLIT + half + 1) * part]
                    for c in range(cols_count)
                ],
                axis=1,
            )
            for half in range(SPLIT)
        ],
        axis=0,
    )
    return product(halves(along), (block_high_ref[...], block_low_ref[...]))


def transform_out(result_ref, values, backward_ref, block_high_ref, block_low_ref, counts):
    rows_count, cols_count = counts
    spread = product(halves(values), (block_high_ref[...], block_low_ref[...]))
    grid_x = spread.shape[0] // SPLIT
    part = spread.shape[1] // cols_count
    spread = jnp.concatenate(
        [
            spread[half * grid_x : (half + 1) * grid_x, c * part : (c + 1) * part]
            for c in range(cols_count)
            for half in range(SPLIT)
        ],
        axis=1,
    )
    high, low = halves(spread)
    along = jnp.dot(
        backward_ref[...],
        jnp.concatenate([high, high, low], axis=0),
        preferred_element_type=jnp.float32,
    )
    width = along.shape[1] // cols_count
    for r in range(rows_count):
        for c in range(cols_count):
            first = (r * cols_count + c) * SLOT_ROWS
            result_ref[first : first + SLOT_ROWS, :] = along[
                r * SLOT_ROWS : (r + 1) * SLOT_ROWS, c * width : (c + 1) * width
            ]


def middle_first_body(
    counts,
    position_ref,
    message_ref,
    kernel_ref,
    forward_ref,
    backward_ref,
    block_high_ref,
    block_low_ref,
    back_high_ref,
    back_low_ref,
    result_ref,
    wave_ref,
):
    wave = transform_in(message_ref, forward_ref, block_high_ref, block_low_ref, *counts)
    wave_ref[...] = wave
    transform_out(
        result_ref, wave * kernel_ref[0], backward_ref, back_high_ref, back_low_ref, counts
    )


def gather_rows(parts_ref):
    tiles = [parts_ref[8 * tile : 8 * tile + 8, :] for tile in range(parts_ref.shape[0] // 8)]
    return jnp.concatenate(tiles, axis=1)[0 : 3 * RHS]


def row_total(value, rhs):
    row = lax.broadcasted_iota(jnp.int32, value.shape, 0)
    return total(jnp.where(lax.rem(row, RHS) == rhs, value, 0.0))


def total(value):
    return jnp.sum(jnp.sum(value, axis=0, keepdims=True), axis=1, keepdims=True)


def middle_second_body(
    counts,
    position_ref,
    message_ref,
    kernel_ref,
    forward_ref,
    backward_ref,
    block_high_ref,
    block_low_ref,
    back_high_ref,
    back_low_ref,
    wave_ref,
    rhs_ref,
    start_ref,
    image_ref,
    second_ref,
    near_ref,
    polar_ref,
    result_ref,
):
    rhs_rows = read_rows(rhs_ref)
    near_rows = gather_rows(near_ref)
    wave = transform_in(message_ref, forward_ref, block_high_ref, block_low_ref, *counts)
    filtered = wave * kernel_ref[0]
    transform_out(result_ref, filtered, backward_ref, back_high_ref, back_low_ref, counts)
    before = wave_ref[...]
    grid_y = CY * counts[1]
    lane = lax.broadcasted_iota(jnp.int32, wave.shape, 1)
    own_rhs = lax.rem(lax.div(lane, grid_y), RHS)
    second = second_ref[...]
    start = start_ref[...]
    image = image_ref[...]
    local_part = second / polar_ref[...] - near_rows - self_coef * second
    slot = lax.broadcasted_iota(jnp.int32, (1, result_ref.shape[1]), 1)
    sums = jnp.zeros((1, result_ref.shape[1]), jnp.float32)
    for rhs in range(RHS):
        mine = own_rhs == rhs
        parts = (
            row_total(rhs_rows * start, rhs),
            row_total(start * image, rhs),
            row_total(second * image, rhs),
            row_total(start * local_part, rhs) + total(jnp.where(mine, before * filtered, 0.0)),
            row_total(second * local_part, rhs) + total(jnp.where(mine, wave * filtered, 0.0)),
        )
        for index, part in enumerate(parts):
            sums = jnp.where(slot == rhs * len(parts) + index, part, sums)
    devices = counts[0] * counts[1]
    result_ref[pl.ds(X_PAD, devices, stride=SLOT_ROWS), :] = jnp.broadcast_to(
        sums, (devices, sums.shape[1])
    )


def sample_body(
    devices,
    message_ref,
    tables_ref,
    depth_high_ref,
    depth_low_ref,
    start_ref,
    near_ref,
    polar_ref,
    image_ref,
    second_ref,
    payload_ref,
):
    tables = read_tables(tables_ref)
    depth = (depth_high_ref[...], depth_low_ref[...])
    field = sample_from(message_ref, *tables, depth, devices)
    start = start_ref[...]
    polar = polar_ref[...]
    image = start / polar - gather_rows(near_ref) + field - self_coef * start
    second = polar * image
    image_ref[...] = image
    second_ref[...] = second
    store_payload(payload_ref, second)


def spread_body(
    devices,
    tables_ref,
    depth_high_ref,
    depth_low_ref,
    second_ref,
    up_ref,
    payload_ref,
    down_ref,
    result_ref,
    stack_ref,
):
    join_stack(stack_ref, up_ref, payload_ref, down_ref)
    depth = (depth_high_ref[...], depth_low_ref[...])
    spread_into(result_ref, second_ref[...], *read_tables(tables_ref), depth, devices)
    clear_spare(result_ref, devices)


def final_body(
    devices,
    message_ref,
    tables_ref,
    depth_high_ref,
    depth_low_ref,
    rhs_ref,
    start_ref,
    image_ref,
    second_ref,
    near_ref,
    polar_ref,
    dipole_ref,
    residual_ref,
):
    tables = read_tables(tables_ref)
    depth = (depth_high_ref[...], depth_low_ref[...])
    field = sample_from(message_ref, *tables, depth, devices)
    second = second_ref[...]
    start = start_ref[...]
    image = image_ref[...]
    image_second = second / polar_ref[...] - gather_rows(near_ref) + field - self_coef * second
    sums = jnp.sum(
        message_ref[pl.ds(X_PAD, devices, stride=SLOT_ROWS), :], axis=0, keepdims=True
    )
    steps = []
    for rhs in range(RHS):
        progress, start_image, second_image, start_next, second_next = [
            sums[:, rhs * 5 + index : rhs * 5 + index + 1] for index in range(5)
        ]
        step = progress / start_image
        progress_next = progress - 2.0 * step * start_image + step * step * second_image
        grown = 1.0 + progress_next / progress
        curvature = (
            grown * grown * start_image
            - step * grown * (start_next + second_image)
            + step * step * second_next
        )
        steps.append((step, grown, progress_next / curvature))
    row = lax.broadcasted_iota(jnp.int32, (RHS, 1), 0)
    step, grown, step_next = [
        sum(jnp.where(row == rhs, steps[rhs][index], 0.0) for rhs in range(RHS))
        for index in range(3)
    ]
    for dim in range(3):
        rows = slice(dim * RHS, (dim + 1) * RHS)
        direction = grown * start[rows] - step * second[rows]
        image_direction = grown * image[rows] - step * image_second[rows]
        dipole_ref[dim] = step * start[rows] + step_next * direction
        residual_ref[dim] = rhs_ref[dim] - step * image[rows] - step_next * image_direction


def near_base(entry, brick_rows):
    return lax.shift_right_logical(entry, 2) * brick_rows + lax.bitwise_and(entry, 3)


def fill_near(scratch, left_ref, stack_ref, right_ref):
    rows = stack_ref.shape[0] // 3
    for row_step in range(3):
        for col_step, source in enumerate((left_ref, stack_ref, right_ref)):
            first = (row_step * 3 + col_step) * rows
            scratch[first : first + rows, :] = source[row_step * rows : (row_step + 1) * rows, :]


def nearest(places, origin, span):
    return places - span * jnp.floor((places - origin) * (1.0 / span) + 0.5)


def unwrap_near(near, stack_ref, tile_count, spans):
    rows = stack_ref.shape[0] // 3
    for dim in range(2):
        origin = stack_ref[rows + dim * tile_count : rows + dim * tile_count + 1, 0:1]
        for brick in range(9):
            first = brick * rows + dim * tile_count
            near[first : first + tile_count, :] = nearest(
                near[first : first + tile_count, :], origin, spans[dim]
            )


def pick_rows(picked, near, lists_ref, tile, tile_count, quantities, origin, span):
    rows = near.shape[0] // 9
    for entry in range(lists_ref.shape[1]):
        base = near_base(lists_ref[tile, entry], rows)
        for quantity in range(quantities):
            values = near[pl.ds(base + quantity * tile_count, 1), :]
            if quantity == 2 and span is not None:
                values = nearest(values, origin, span)
            first = (entry * quantities + quantity) * GROUP
            picked[first : first + GROUP, :] = jnp.broadcast_to(values, (GROUP, TILE))


def widen_own(stack_ref, quantities, tile_count, tile, square, wide):
    offset = stack_ref.shape[0] // 3
    for quantity in range(quantities):
        square[quantity : quantity + 1, :] = stack_ref[
            pl.ds(offset + quantity * tile_count + tile, 1), :
        ]
    columns = jnp.transpose(square[...])
    for quantity in range(quantities):
        wide[quantity * TILE : (quantity + 1) * TILE, :] = jnp.broadcast_to(
            columns[:, quantity : quantity + 1], (TILE, TILE)
        )


def add_field(sums, first_term, second_term, apart, moments):
    for rhs in range(RHS):
        moment = [moments[RHS * dim + rhs] for dim in range(3)]
        projected = moment[0] * apart[0] + moment[1] * apart[1] + moment[2] * apart[2]
        weighted = second_term * projected
        for dim in range(3):
            index = RHS * dim + rhs
            sums[index] = sums[index] + (weighted * apart[dim] - first_term * moment[dim])


def finish_sums(field_ref, sums_ref):
    lane = lax.broadcasted_iota(jnp.int32, (TILE, TILE), 1)
    merged = jnp.zeros((TILE, TILE), jnp.float32)
    for index in range(3 * RHS):
        column = jnp.sum(sums_ref[index * TILE : (index + 1) * TILE, :], axis=1, keepdims=True)
        merged = jnp.where(lane == index, column, merged)
    field_ref[...] = jnp.transpose(merged)[0:GROUP]


def pair_rows(start, group):
    return pl.ds(pl.multiple_of(start + group * GROUP, GROUP), GROUP)


def wide_rows(start, group, quantity):
    return pl.ds(pl.multiple_of(quantity * TILE + start + group * GROUP, GROUP), GROUP)


def pair_terms(square_dist, damp):
    inverse = lax.rsqrt(square_dist)
    distance = square_dist * inverse
    inverse_sq = inverse * inverse
    inverse_cube = inverse_sq * inverse
    cubed = damp * (distance * square_dist)
    damping = jnp.exp(-cubed)
    bell = jnp.exp(-(ewald_beta * ewald_beta) * square_dist)
    turned = 1.0 / (1.0 + (SCREEN_SCALE * ewald_beta) * distance)
    series = SCREEN_COEF[-1] * turned + SCREEN_COEF[-2]
    for coef in SCREEN_COEF[-3::-1]:
        series = series * turned + coef
    screen = bell * turned * series
    gaussian = (2.0 * ewald_beta / math.sqrt(math.pi)) * bell
    bare = screen - damping
    first_term = bare * inverse_cube + gaussian * inverse_sq
    second_term = (
        3.0 * (first_term - (cubed * damping) * inverse_cube)
        + (2.0 * ewald_beta * ewald_beta) * gaussian
    ) * inverse_sq
    return first_term, second_term


def pair_first_body(
    tile_count,
    spans,
    lists_ref,
    left_ref,
    stack_ref,
    right_ref,
    after_ref,
    first_ref,
    second_ref,
    field_ref,
    near,
    picked,
    square,
    wide,
    sums_ref,
):
    @pl.when(pl.program_id(0) == 0)
    def _():
        fill_near(near, left_ref, stack_ref, right_ref)
        unwrap_near(near, stack_ref, tile_count, spans)
        square[...] = jnp.zeros_like(square)

    tile = pl.program_id(0)
    quantities = stack_ref.shape[0] // 3 // tile_count
    widen_own(stack_ref, 4, tile_count, tile, square, wide)
    origin = wide[2 * TILE : 2 * TILE + 1, 0:1]
    pick_rows(picked, near, lists_ref, tile, tile_count, quantities, origin, spans[2])

    @pl.loop(0, TILE // PAIR_ROWS)
    def _(part):
        start = part * PAIR_ROWS
        for group in range(PAIR_ROWS // GROUP):
            own = [wide[wide_rows(start, group, dim), :] for dim in range(4)]
            own_damp = thole_a * own[3]
            sums = [jnp.zeros((GROUP, TILE), jnp.float32) for _ in range(3 * RHS)]
            itself = (
                lax.broadcasted_iota(jnp.int32, (GROUP, TILE), 0) + (start + group * GROUP)
            ) == lax.broadcasted_iota(jnp.int32, (GROUP, TILE), 1)
            for entry in range(lists_ref.shape[1]):
                first = entry * quantities * GROUP
                rows = [
                    picked[first + quantity * GROUP : first + (quantity + 1) * GROUP, :]
                    for quantity in range(quantities)
                ]
                apart = [rows[dim] - own[dim] for dim in range(3)]
                square_dist = apart[0] * apart[0] + apart[1] * apart[1] + apart[2] * apart[2]
                if entry == 0:
                    square_dist = jnp.where(itself, 1.0, square_dist)
                first_term, second_term = pair_terms(square_dist, own_damp * rows[3])
                if entry == 0:
                    first_term = jnp.where(itself, 0.0, first_term)
                    second_term = jnp.where(itself, 0.0, second_term)
                place = wide_rows(start, group, entry)
                first_ref[place, :] = first_term
                second_ref[place, :] = second_term
                add_field(sums, first_term, second_term, apart, rows[4:])
            for index, value in enumerate(sums):
                sums_ref[wide_rows(start, group, index), :] = value

    finish_sums(field_ref, sums_ref)


def pair_second_body(
    tile_count,
    spans,
    lists_ref,
    left_ref,
    stack_ref,
    right_ref,
    left_moment_ref,
    stack_moment_ref,
    right_moment_ref,
    first_ref,
    second_ref,
    field_ref,
    near,
    near_moment,
    picked,
    picked_moment,
    square,
    wide,
    sums_ref,
):
    @pl.when(pl.program_id(0) == 0)
    def _():
        fill_near(near, left_ref, stack_ref, right_ref)
        unwrap_near(near, stack_ref, tile_count, spans)
        fill_near(near_moment, left_moment_ref, stack_moment_ref, right_moment_ref)
        square[...] = jnp.zeros_like(square)

    tile = pl.program_id(0)
    widen_own(stack_ref, 3, tile_count, tile, square, wide)
    origin = wide[2 * TILE : 2 * TILE + 1, 0:1]
    pick_rows(picked, near, lists_ref, tile, tile_count, 3, origin, spans[2])
    pick_rows(picked_moment, near_moment, lists_ref, tile, tile_count, 3 * RHS, None, None)

    @pl.loop(0, TILE // PAIR_ROWS)
    def _(part):
        start = part * PAIR_ROWS
        for group in range(PAIR_ROWS // GROUP):
            own = [wide[wide_rows(start, group, dim), :] for dim in range(3)]
            sums = [jnp.zeros((GROUP, TILE), jnp.float32) for _ in range(3 * RHS)]
            for entry in range(lists_ref.shape[1]):
                first = entry * 3 * GROUP
                apart = [
                    picked[first + dim * GROUP : first + (dim + 1) * GROUP, :] - own[dim]
                    for dim in range(3)
                ]
                first = first * RHS
                moments = [
                    picked_moment[first + index * GROUP : first + (index + 1) * GROUP, :]
                    for index in range(3 * RHS)
                ]
                place = wide_rows(start, group, entry)
                add_field(sums, first_ref[place, :], second_ref[place, :], apart, moments)
            for index, value in enumerate(sums):
                sums_ref[wide_rows(start, group, index), :] = value

    finish_sums(field_ref, sums_ref)


def shift(source, axis, step):
    count = lax.axis_size(axis)
    return lax.ppermute(source, axis, [(i, (i + step) % count) for i in range(count)])


def both_ways(source, axis):
    return shift(source, axis, 1), source, shift(source, axis, -1)


def whole(shape):
    return pl.BlockSpec(shape, lambda *_: (0,) * len(shape))


def anywhere():
    return pl.BlockSpec(memory_space=pl.ANY)


def call(body, outs, *operands, after=()):
    def run(*refs):
        body(*refs[len(after) :])

    return pl.pallas_call(
        run,
        grid=(1,),
        in_specs=[anywhere()] * len(after) + [whole(operand.shape) for operand in operands],
        out_specs=[whole(shape) for shape, _ in outs],
        out_shape=[jax.ShapeDtypeStruct(shape, dtype) for shape, dtype in outs],
        compiler_params=pltpu.CompilerParams(vmem_limit_bytes=VMEM_LIMIT),
        cost_estimate=pl.CostEstimate(
            flops=200_000_000, bytes_accessed=4 << 20, transcendentals=0
        ),
    )(*after, *operands)


def middle_call(body, outs, position, message, kernel, *operands, after=()):
    def run(position_ref, *refs):
        body(position_ref, *refs[len(after) :])

    return pl.pallas_call(
        run,
        grid_spec=pltpu.PrefetchScalarGridSpec(
            num_scalar_prefetch=1,
            grid=(1,),
            in_specs=[anywhere()] * len(after)
            + [whole(message.shape)]
            + [pl.BlockSpec((1,) + kernel.shape[1:], lambda i, s: (s[0], 0, 0))]
            + [whole(operand.shape) for operand in operands],
            out_specs=[whole(shape) for shape in outs],
        ),
        out_shape=[jax.ShapeDtypeStruct(shape, jnp.float32) for shape in outs],
        compiler_params=pltpu.CompilerParams(vmem_limit_bytes=VMEM_LIMIT),
        cost_estimate=pl.CostEstimate(
            flops=200_000_000, bytes_accessed=4 << 20, transcendentals=0
        ),
    )(position, *after, message, kernel, *operands)


def pair_call(body, outs, tiles, blocked, scratch, lists, *operands, after=()):
    def block(operand):
        rows = operand.shape[0] // tiles
        return pl.BlockSpec((rows, operand.shape[1]), lambda i, s: (i, 0))

    out_shape = [jax.ShapeDtypeStruct(shape, jnp.float32) for shape in outs]
    plain = len(operands) - blocked
    return pl.pallas_call(
        body,
        out_shape=out_shape,
        grid_spec=pltpu.PrefetchScalarGridSpec(
            num_scalar_prefetch=1,
            grid=(tiles,),
            in_specs=[whole(operand.shape) for operand in operands[:plain]]
            + [block(operand) for operand in operands[plain:]]
            + [anywhere()] * len(after),
            out_specs=[block(shape) for shape in out_shape],
            scratch_shapes=[pltpu.VMEM(shape, jnp.float32) for shape in scratch],
        ),
        compiler_params=pltpu.CompilerParams(vmem_limit_bytes=VMEM_LIMIT),
        cost_estimate=pl.CostEstimate(
            flops=80_000_000, bytes_accessed=8 << 20, transcendentals=1 << 21
        ),
    )(lists, *operands, *after)


def exchange(message, devices):
    shape = message.shape
    sent = message.reshape(devices, 1, -1)
    return lax.all_to_all(sent, ("row", "col"), split_axis=0, concat_axis=0, tiled=True).reshape(
        shape
    )


def slab_local(field_rhs, positions, polar, grid_base, tile_lists):
    rows_count = lax.axis_size("row")
    cols_count = lax.axis_size("col")
    counts = (rows_count, cols_count)
    devices = rows_count * cols_count
    lengths = (CX * rows_count, CY * cols_count, KZ)
    spans = tuple(float(length) for length in lengths)
    atoms = polar.shape[-1]
    tile_count = atoms // TILE
    listed = tile_lists.shape[-1]
    tables = slab_tables(rows_count, cols_count)
    f32 = jnp.float32
    rhs = jnp.swapaxes(field_rhs[0, 0], 0, 1)
    place = jnp.swapaxes(positions[0], 0, 1)
    base = jnp.swapaxes(grid_base[0], 0, 1)
    polar = polar.reshape(1, atoms)
    lists = tile_lists[0, 0]
    quantities = 4 + 3 * RHS
    brick_rows = quantities * tile_count
    moment_rows = 3 * RHS * tile_count
    message_shape = (devices * SLOT_ROWS, KZ // devices * RHS * Y_PAD)
    row_shape = (3 * RHS, atoms)
    square = (TILE, TILE)
    wide = (4 * TILE, TILE)
    sums = (3 * RHS * TILE, TILE)

    start, payload = call(pack_body, [(row_shape, f32), ((brick_rows, TILE), f32)], rhs, place, polar)

    def setup(*refs):
        setup_body(lengths, devices, *refs)

    message, splines, depth_high, depth_low, stack = call(
        setup,
        [
            (message_shape, f32),
            ((2 * SLOT_ROWS + 2 * Y_PAD, atoms), f32),
            ((KZ, 2 * atoms), jnp.bfloat16),
            ((KZ, 2 * atoms), jnp.bfloat16),
            ((3 * brick_rows, TILE), f32),
        ],
        place,
        base,
        start,
        *[jnp.asarray(table) for table in tables["along_z"]],
        *both_ways(payload, "row"),
    )
    near = both_ways(stack, "col")
    position = (lax.axis_index("row") * cols_count + lax.axis_index("col")).reshape(1)
    constants = (
        jnp.asarray(tables["kernel"]),
        jnp.asarray(tables["forward_x"]),
        jnp.asarray(tables["backward_x"]),
        *[jnp.asarray(table) for table in tables["block"]],
        *[jnp.asarray(table) for table in tables["block_back"]],
    )
    arrived = exchange(message, devices)

    def middle_first(*refs):
        middle_first_body(counts, *refs)

    mixed, wave = middle_call(
        middle_first,
        [message_shape, tables["kernel"].shape[1:]],
        position,
        arrived,
        *constants,
        after=(near[0], near[2]),
    )
    returned = exchange(mixed, devices)

    def pair_first(*refs):
        pair_first_body(tile_count, spans, *refs)

    first_term, second_term, direct = pair_call(
        pair_first,
        [(tile_count * listed * TILE, TILE)] * 2 + [(tile_count * GROUP, TILE)],
        tile_count,
        0,
        [(9 * brick_rows, TILE), (listed * quantities * GROUP, TILE), square, wide, sums],
        lists,
        *near,
        after=(wave,),
    )

    def sample(*refs):
        sample_body(devices, *refs)

    image, second, moments = call(
        sample,
        [(row_shape, f32), (row_shape, f32), ((moment_rows, TILE), f32)],
        returned,
        splines,
        depth_high,
        depth_low,
        start,
        direct,
        polar,
    )

    def spread(*refs):
        spread_body(devices, *refs)

    message, stack = call(
        spread,
        [(message_shape, f32), ((3 * moment_rows, TILE), f32)],
        splines,
        depth_high,
        depth_low,
        second,
        *both_ways(moments, "row"),
    )
    near_moments = both_ways(stack, "col")
    arrived = exchange(message, devices)

    def pair_second(*refs):
        pair_second_body(tile_count, spans, *refs)

    (direct,) = pair_call(
        pair_second,
        [(tile_count * GROUP, TILE)],
        tile_count,
        2,
        [
            (9 * brick_rows, TILE),
            (9 * moment_rows, TILE),
            (listed * 3 * GROUP, TILE),
            (listed * 3 * RHS * GROUP, TILE),
            square,
            wide,
            sums,
        ],
        lists,
        *near,
        *near_moments,
        first_term,
        second_term,
    )

    def middle_second(*refs):
        middle_second_body(counts, *refs)

    (mixed,) = middle_call(
        middle_second,
        [message_shape],
        position,
        arrived,
        *constants,
        wave,
        rhs,
        start,
        image,
        second,
        direct,
        polar,
    )
    returned = exchange(mixed, devices)

    def final(*refs):
        final_body(devices, *refs)

    outs = call(
        final,
        [(rhs.shape, f32), (rhs.shape, f32)],
        returned,
        splines,
        depth_high,
        depth_low,
        rhs,
        start,
        image,
        second,
        direct,
        polar,
    )
    return tuple(jnp.swapaxes(out, 0, 1)[None, None] for out in outs)


def solution(mesh):
    placed = (
        P("row", "col", None, None, None),
        P("row", "col", None, None),
        P("row", "col", None),
        P("row", "col", None, None),
        P("row", "col", None, None),
    )
    devices = mesh.shape["row"] * mesh.shape["col"]
    return jax.shard_map(
        slab_local if KZ % devices == 0 else pencil_local,
        mesh=mesh,
        in_specs=placed,
        out_specs=(P("row", "col", None, None, None), P("row", "col", None, None, None)),
        check_vma=False,
    )
```

```python
import math

import jax
import jax.numpy as jnp
import ml_dtypes
import numpy as np
from jax import lax
from jax.experimental import pallas as pl
from jax.experimental.pallas import tpu as pltpu
from jax.sharding import PartitionSpec as P

CX = 8
CY = 4
KZ = 256
TILE = 128
RHS = 2
ITERS = 2


ewald_beta = 0.4
thole_a = 0.39
self_coef = 4.0 * ewald_beta**3 / (3.0 * math.sqrt(math.pi))
highest = lax.Precision.HIGHEST


def with_halo(cells, sides, width):
    for axis, dim in sides:
        count = lax.axis_size(axis)
        head = lax.slice_in_dim(cells, 0, width, axis=dim)
        tail = lax.slice_in_dim(cells, cells.shape[dim] - width, cells.shape[dim], axis=dim)
        cells = jnp.concatenate(
            [
                lax.ppermute(tail, axis, [(i, (i + 1) % count) for i in range(count)]),
                cells,
                lax.ppermute(head, axis, [((i + 1) % count, i) for i in range(count)]),
            ],
            axis=dim,
        )
    return cells


def spline_table(fraction):
    previous = {0: jnp.ones_like(fraction)}
    fourth = previous
    for degree in range(2, 6):
        current = {}
        for offset in range(degree):
            abscissa = fraction + offset
            summed = abscissa * previous.get(offset, 0.0) + (degree - abscissa) * previous.get(
                offset - 1, 0.0
            )
            current[offset] = summed / (degree - 1)
        if degree == 4:
            fourth = current
        previous = current
    values = jnp.stack([previous[4 - stencil] for stencil in range(5)])
    slopes = jnp.stack(
        [fourth.get(4 - stencil, 0.0) - fourth.get(3 - stencil, 0.0) for stencil in range(5)]
    )
    return (values, slopes)


def spline_modulus(wave_index, length):
    spline_coef = (1.0 / 24.0, 11.0 / 24.0, 11.0 / 24.0, 1.0 / 24.0)
    cosine_sum = jnp.zeros(wave_index.shape, jnp.float32)
    sine_sum = jnp.zeros(wave_index.shape, jnp.float32)
    for offset in range(4):
        angles = 2.0 * math.pi / length * (wave_index * offset % length).astype(jnp.float32)
        cosine_sum = cosine_sum + spline_coef[offset] * jnp.cos(angles)
        sine_sum = sine_sum + spline_coef[offset] * jnp.sin(angles)
    return cosine_sum * cosine_sum + sine_sum * sine_sum


def folded_square(wave_index, length):
    nearest = jnp.minimum(wave_index, length - wave_index).astype(jnp.float32) / length
    return nearest * nearest


def influence(wave_x, wave_y, wave_z, length_x, length_y, length_z):
    wave_norm = (
        folded_square(wave_x, length_x)
        + folded_square(wave_y, length_y)
        + folded_square(wave_z, length_z)
    )
    modulus = (
        spline_modulus(wave_x, length_x)
        * spline_modulus(wave_y, length_y)
        * spline_modulus(wave_z, length_z)
    )
    excluded = (wave_x * 2 == length_x) | (wave_y * 2 == length_y) | (wave_z * 2 == length_z)
    excluded = excluded | (wave_x == 0) & (wave_y == 0) & (wave_z == 0)
    safe_norm = jnp.where(excluded, 1.0, wave_norm)
    safe_modulus = jnp.where(excluded, 1.0, modulus)
    result = jnp.exp(-(math.pi**2 / ewald_beta**2) * safe_norm) / (
        math.pi * safe_norm * safe_modulus
    )
    return jnp.where(excluded, 0.0, result)


def tile_field(own_static, near_static, near_dipole, box_spans):
    listed_count = near_static.shape[0]
    tile_width = own_static.shape[1]
    box_span = jnp.array(box_spans, dtype=jnp.float32)[None, :, None, None]
    separation = near_static[:, 0:3, None, :] - own_static[None, 0:3, :, None]
    separation = separation - box_span * jnp.floor(separation / box_span + 0.5)
    dist_sq = jnp.sum(separation * separation, axis=1)
    itself = (jnp.arange(listed_count)[:, None, None] == 0) & (
        jnp.arange(tile_width)[:, None] == jnp.arange(tile_width)[None, :]
    )[None]
    safe_sq = jnp.where(itself, 1.0, dist_sq)
    distance = jnp.sqrt(safe_sq)
    scaled = distance / (own_static[3][None, :, None] * near_static[:, 3][:, None, :])
    cubed = thole_a * scaled * scaled * scaled
    damping = jnp.exp(-cubed)
    screen = lax.erfc(ewald_beta * distance)
    gaussian = 2.0 * ewald_beta / math.sqrt(math.pi) * jnp.exp(-(ewald_beta * ewald_beta) * safe_sq)
    inverse_sq = 1.0 / safe_sq
    inverse_cube = inverse_sq / distance
    first_term = (screen - damping) * inverse_cube + gaussian * inverse_sq
    second = (
        3.0 * (screen - (1.0 + cubed) * damping) * inverse_cube * inverse_sq
        + gaussian * (2.0 * ewald_beta * ewald_beta + 3.0 * inverse_sq) * inverse_sq
    )
    first_term = jnp.where(itself, 0.0, first_term)
    second = jnp.where(itself, 0.0, second)
    projected = jnp.sum(near_dipole[:, :, :, None, :] * separation[:, None, :, :, :], axis=2)
    weighted = second[:, None] * projected
    outward = jnp.sum(weighted[:, :, None] * separation[:, None], axis=(0, 4))
    inward = jnp.sum(first_term[:, None, None] * near_dipole[:, :, :, None, :], axis=(0, 4))
    return outward - inward


def hartley(length):
    counter = jnp.arange(length, dtype=jnp.int32)
    angles = (
        2.0 * math.pi / length * (counter[:, None] * counter[None, :] % length).astype(jnp.float32)
    )
    return jnp.cos(angles) + jnp.sin(angles)


def placed_table(first_cell, weights, extent):
    slot_index = jnp.arange(extent, dtype=jnp.int32)[:, None]
    placed = jnp.zeros((extent, first_cell.shape[0]), jnp.float32)
    for stencil in range(5):
        placed = placed + jnp.where(
            slot_index == (first_cell[None, :] + stencil) % extent, weights[stencil][None, :], 0.0
        )
    return placed


def pad_axis(source, axis_pos, leading, trailing):
    widths = [(0, 0)] * source.ndim
    widths[axis_pos] = (leading, trailing)
    return jnp.pad(source, widths)


def fold_cycle(cycle_only, axis_pos, inner_len):
    middle = lax.slice_in_dim(cycle_only, 4, inner_len + 4, axis=axis_pos)
    lower_cycle = lax.slice_in_dim(cycle_only, 0, 2, axis=axis_pos)
    upper_cycle = lax.slice_in_dim(cycle_only, inner_len + 6, inner_len + 8, axis=axis_pos)
    return (
        middle
        + pad_axis(lower_cycle, axis_pos, 0, inner_len - 2)
        + pad_axis(upper_cycle, axis_pos, inner_len - 2, 0)
    )


def clear_inside(extended, extents):
    inside = None
    for axis_pos, inner_len in extents:
        slot_index = lax.broadcasted_iota(jnp.int32, extended.shape, axis_pos)
        within = (slot_index >= 2) & (slot_index < inner_len + 6)
        inside = within if inside is None else inside & within
    return jnp.where(inside, 0.0, extended)


def inner_sum(left_arr, right_arr):
    return lax.psum(jnp.sum(left_arr * right_arr, axis=(1, 2)), ("row", "col"))


def pencil_local(field_rhs, positions, polar, grid_base, tile_lists):
    rows_count = lax.axis_size("row")
    cols_count = lax.axis_size("col")
    grid_x = CX * rows_count
    grid_y = CY * cols_count
    atom_count = polar.shape[-1]
    tile_count = atom_count // TILE
    slab_depth = KZ // tile_count
    window_len = slab_depth + 4
    box_spans = (float(grid_x), float(grid_y), float(KZ))
    own_place = positions[0, 0]
    own_base = grid_base[0, 0]
    own_polar = polar[0, 0]
    lengths = jnp.array([grid_x, grid_y, KZ], dtype=jnp.int32)[:, None]
    cell_index = (own_base + 2) % lengths
    fraction = own_place - cell_index.astype(jnp.float32)
    values, slopes = spline_table(fraction)
    first_x = (own_base[0] - lax.axis_index("row") * CX + 2) % grid_x
    first_y = (own_base[1] - lax.axis_index("col") * CY + 2) % grid_y
    rows_x = placed_table(first_x, values[:, 0], CX + 4)
    slope_x = placed_table(first_x, slopes[:, 0], CX + 4)
    rows_y = placed_table(first_y, values[:, 1], CY + 4)
    slope_y = placed_table(first_y, slopes[:, 1], CY + 4)
    tile_start = jnp.arange(atom_count, dtype=jnp.int32) // TILE * slab_depth
    first_z = (own_base[2] + 2 - tile_start) % KZ
    rows_z = placed_table(first_z, values[:, 2], window_len)
    slope_z = placed_table(first_z, slopes[:, 2], window_len)
    plane_count = (CX + 4) * (CY + 4)
    plane_dx = (slope_x[:, None, :] * rows_y[None, :, :]).reshape(plane_count, atom_count)
    plane_dy = (rows_x[:, None, :] * slope_y[None, :, :]).reshape(plane_count, atom_count)
    plane_flat = (rows_x[:, None, :] * rows_y[None, :, :]).reshape(plane_count, atom_count)
    window_rows = jnp.moveaxis(rows_z.reshape(window_len, tile_count, TILE), 1, 0)
    window_slope = jnp.moveaxis(slope_z.reshape(window_len, tile_count, TILE), 1, 0)
    depth_table = jnp.concatenate([window_rows, window_slope], axis=2)
    grid_scale = 1.0 / (grid_x * grid_y * KZ)
    hartley_x = hartley(grid_x)
    hartley_y = hartley(grid_y)
    hartley_z = hartley(KZ)
    block_y = grid_y // rows_count
    block_z = KZ // cols_count
    wave_x = jnp.arange(grid_x, dtype=jnp.int32)[:, None, None]
    wave_y = (lax.axis_index("row") * block_y + jnp.arange(block_y, dtype=jnp.int32))[None, :, None]
    wave_z = (lax.axis_index("col") * block_z + jnp.arange(block_z, dtype=jnp.int32))[None, None, :]
    kernel = influence(wave_x, wave_y, wave_z, grid_x, grid_y, KZ) * grid_scale
    root_scale = jnp.power(own_polar, 1.0 / 6.0)
    own_static = jnp.concatenate([own_place, root_scale[None]], axis=0)
    near_static = with_halo(own_static[None, None], (("row", 0), ("col", 1)), 1)
    near_static = jnp.moveaxis(near_static.reshape(9, 4, tile_count, TILE), 2, 1).reshape(
        9 * tile_count, 4, TILE
    )
    own_tiles = jnp.moveaxis(own_static.reshape(4, tile_count, TILE), 1, 0)
    own_lists = tile_lists[0, 0]
    polar_wide = own_polar[None, None, :]
    solution = jnp.zeros_like(field_rhs[0, 0])
    residual = field_rhs[0, 0]
    scaled_res = polar_wide * residual
    direction = scaled_res
    progress = inner_sum(residual, scaled_res)
    for iteration in range(ITERS):
        near_dip = with_halo(direction[None, None], (("row", 0), ("col", 1)), 1)
        near_dip = jnp.moveaxis(near_dip.reshape(9, RHS, 3, tile_count, TILE), 3, 1).reshape(
            9 * tile_count, RHS, 3, TILE
        )

        def one_tile(tile_pos):
            picked = own_lists[tile_pos]
            return tile_field(own_tiles[tile_pos], near_static[picked], near_dip[picked], box_spans)

        fields = lax.map(one_tile, jnp.arange(tile_count, dtype=jnp.int32))
        direct = jnp.moveaxis(fields, 0, 2).reshape(RHS, 3, atom_count)
        slope_terms = (
            direction[:, 0, None, :] * plane_dx[None] + direction[:, 1, None, :] * plane_dy[None]
        )
        flat_terms = direction[:, 2, None, :] * plane_flat[None]
        spread_left = jnp.concatenate(
            [
                slope_terms.reshape(RHS, plane_count, tile_count, TILE),
                flat_terms.reshape(RHS, plane_count, tile_count, TILE),
            ],
            axis=3,
        )
        spread_windows = jnp.einsum("sptb,twb->sptw", spread_left, depth_table, precision=highest)
        main_part = spread_windows[..., :slab_depth].reshape(spread_windows.shape[:-2] + (KZ,))
        tail_part = pad_axis(
            spread_windows[..., slab_depth:], spread_windows.ndim - 1, 0, slab_depth - 4
        )
        tail_part = tail_part.reshape(spread_windows.shape[:-2] + (KZ,))[..., : KZ + 4 - slab_depth]
        last_axis = main_part.ndim - 1
        padded_line = pad_axis(main_part, last_axis, 0, 4) + pad_axis(
            tail_part, last_axis, slab_depth, 0
        )
        inner = padded_line[..., 2 : KZ + 2]
        spread_tile = (
            inner
            + pad_axis(padded_line[..., 0:2], last_axis, KZ - 2, 0)
            + pad_axis(padded_line[..., KZ + 2 : KZ + 4], last_axis, 0, KZ - 2)
        ).reshape(RHS, CX + 4, CY + 4, KZ)
        extended = with_halo(spread_tile, (("row", 1), ("col", 2)), 2)
        cycle_only = clear_inside(extended, ((1, CX), (2, CY)))
        folded = fold_cycle(fold_cycle(cycle_only, 1, CX), 2, CY)
        spectrum = jnp.einsum(
            "sxyz,zk->sxyk",
            spread_tile[:, 2 : CX + 2, 2 : CY + 2] + folded,
            hartley_z,
            precision=highest,
        )
        along_y = jnp.einsum(
            "sxyz,yk->sxkz",
            lax.all_to_all(spectrum, "col", split_axis=3, concat_axis=2, tiled=True),
            hartley_y,
            precision=highest,
        )
        along_x = (
            jnp.einsum(
                "sxyz,xk->skyz",
                lax.all_to_all(along_y, "row", split_axis=2, concat_axis=1, tiled=True),
                hartley_x,
                precision=highest,
            )
            * kernel[None]
        )
        mixed_part = jnp.einsum("sxyz,xk->skyz", along_x, hartley_x, precision=highest)
        returned = lax.all_to_all(mixed_part, "row", split_axis=1, concat_axis=2, tiled=True)
        swapped = jnp.einsum("sxyz,yk->sxkz", returned, hartley_y, precision=highest)
        restored = lax.all_to_all(swapped, "col", split_axis=2, concat_axis=3, tiled=True)
        padded = with_halo(
            jnp.einsum("sxyz,zk->sxyk", restored, hartley_z, precision=highest),
            (("row", 1), ("col", 2)),
            2,
        )
        line = padded.reshape(RHS, plane_count, KZ)
        extended_line = jnp.concatenate([line[..., KZ - 2 :], line, line[..., :2]], axis=-1)
        windows = jnp.stack(
            [
                extended_line[..., tile * slab_depth : tile * slab_depth + window_len]
                for tile in range(tile_count)
            ],
            axis=-2,
        )
        sampled = jnp.einsum("sptw,twb->sptb", windows, depth_table, precision=highest)
        with_flat = sampled[..., :TILE].reshape(RHS, plane_count, atom_count)
        with_slope = sampled[..., TILE:].reshape(RHS, plane_count, atom_count)
        recip_part = jnp.stack(
            [
                jnp.sum(with_flat * plane_dx[None], axis=1),
                jnp.sum(with_flat * plane_dy[None], axis=1),
                jnp.sum(with_slope * plane_flat[None], axis=1),
            ],
            axis=1,
        )
        image_field = direction / polar_wide - direct + recip_part - self_coef * direction
        step_size = (progress / inner_sum(direction, image_field))[:, None, None]
        solution = solution + step_size * direction
        residual = residual - step_size * image_field
        scaled_res = polar_wide * residual
        progress_next = inner_sum(residual, scaled_res)
        direction = scaled_res + (progress_next / progress)[:, None, None] * direction
        progress = progress_next
    return (solution[None, None], residual[None, None])


X_PAD = CX + 4
Y_PAD = CY + 4
SLOT_ROWS = 16
SPLIT = 2
VMEM_LIMIT = 60_000_000
PAIR_ROWS = 32
GROUP = 8
SCREEN_SCALE = 0.4
SCREEN_COEF = (
    0.22567588090896606,
    0.2256690263748169,
    0.20785020291805267,
    0.16849851608276367,
    0.14156343042850494,
    -0.005832736846059561,
    0.16930203139781952,
    -0.1830107867717743,
    0.05028456076979637,
)


def halves(value):
    high = value.astype(jnp.bfloat16)
    return high, (value - high.astype(jnp.float32)).astype(jnp.bfloat16)


def halves_np(value):
    value = value.astype(np.float32)
    high = value.astype(ml_dtypes.bfloat16)
    return high, (value - high.astype(np.float32)).astype(ml_dtypes.bfloat16)


def product(left, right, left_dim=1, right_dim=0):
    def one(first, second):
        return lax.dot_general(
            first,
            second,
            (((left_dim,), (right_dim,)), ((), ())),
            preferred_element_type=jnp.float32,
        )

    return one(left[0], right[0]) + (one(left[1], right[0]) + one(left[0], right[1]))


def cas_np(wave, place, length):
    angles = 2.0 * np.pi / length * (wave[:, None] * place[None, :] % length)
    return np.cos(angles) + np.sin(angles)


def modulus_np(wave, length):
    coef = np.array([1.0, 11.0, 11.0, 1.0]) / 24.0
    angles = 2.0 * np.pi / length * (wave[:, None] * np.arange(4)[None, :])
    return (coef * np.cos(angles)).sum(1) ** 2 + (coef * np.sin(angles)).sum(1) ** 2


def influence_np(length_x, length_y, length_z):
    total = np.zeros((length_x, length_y, length_z))
    modulus = np.ones((length_x, length_y, length_z))
    excluded = np.zeros((length_x, length_y, length_z), bool)
    for axis, length in enumerate((length_x, length_y, length_z)):
        wave = np.arange(length)
        shape = [1, 1, 1]
        shape[axis] = length
        total = total + ((np.minimum(wave, length - wave) / length) ** 2).reshape(shape)
        modulus = modulus * modulus_np(wave, length).reshape(shape)
        excluded = excluded | (wave * 2 == length).reshape(shape)
    excluded[0, 0, 0] = True
    safe = np.where(excluded, 1.0, total)
    result = np.exp(-(np.pi**2) / ewald_beta**2 * safe) / (
        np.pi * safe * np.where(excluded, 1.0, modulus)
    )
    return np.where(excluded, 0.0, result) / (length_x * length_y * length_z)


def slab_tables(rows_count, cols_count):
    grid_x = CX * rows_count
    grid_y = CY * cols_count
    devices = rows_count * cols_count
    chunk = KZ // devices
    wave_z = (np.arange(devices)[None, :] * chunk + np.arange(chunk)[:, None]).reshape(-1)
    along_z = cas_np(wave_z, np.arange(KZ), KZ)
    place_x = np.arange(rows_count)[:, None] * CX + np.arange(X_PAD)[None, :] - 2
    along_x = cas_np(np.arange(grid_x), place_x.reshape(-1) % grid_x, grid_x)
    x_high, x_low = halves_np(along_x)
    forward_x = np.concatenate([x_high, x_low, x_high], axis=1)
    backward_x = np.concatenate([x_high.T, x_low.T, x_high.T], axis=1)
    place_y = (np.arange(cols_count)[:, None] * CY + np.arange(Y_PAD)[None, :] - 2) % grid_y
    along_y = cas_np(np.arange(grid_y), place_y.reshape(-1), grid_y)
    along_y = along_y.reshape(grid_y, cols_count, Y_PAD)
    units = chunk * RHS // SPLIT
    block = np.einsum("uv,kcy->cuyvk", np.eye(units), along_y)
    block = block.reshape(cols_count * units * Y_PAD, units * grid_y)
    kernel = influence_np(grid_x, grid_y, KZ).reshape(grid_x, grid_y, devices, chunk)
    kernel = np.transpose(kernel, (2, 0, 3, 1))[:, :, :, None, :]
    kernel = np.broadcast_to(kernel, (devices, grid_x, chunk, RHS, grid_y))
    kernel = kernel.reshape(devices, grid_x, SPLIT, units * grid_y)
    kernel = np.moveaxis(kernel, 2, 1).reshape(devices, SPLIT * grid_x, units * grid_y)
    kernel = kernel.astype(np.float32)
    return dict(
        along_z=halves_np(along_z),
        forward_x=forward_x,
        backward_x=backward_x,
        block=halves_np(block),
        block_back=halves_np(np.ascontiguousarray(block.T)),
        kernel=kernel,
    )


def pack_body(rhs_ref, place_ref, polar_ref, start_ref, payload_ref):
    polar = polar_ref[...]
    start = read_rows(rhs_ref) * polar
    start_ref[...] = start
    place = [place_ref[dim] for dim in range(3)]
    everything = jnp.concatenate(place + [1.0 / jnp.sqrt(polar), start], axis=0)
    store_payload(payload_ref, everything)


def read_rows(rows_ref):
    return jnp.concatenate([rows_ref[dim] for dim in range(3)], axis=0)


def store_payload(payload_ref, everything):
    tile_count = everything.shape[1] // TILE
    for quantity in range(everything.shape[0]):
        for tile in range(tile_count):
            row = quantity * tile_count + tile
            payload_ref[row : row + 1, :] = everything[
                quantity : quantity + 1, tile * TILE : (tile + 1) * TILE
            ]


def placed_rows(slot, weights, extent):
    slot_index = lax.broadcasted_iota(jnp.int32, (extent, slot.shape[1]), 0)
    placed = jnp.zeros((extent, slot.shape[1]), jnp.float32)
    for stencil in range(5):
        target = slot + stencil
        if extent == KZ:
            target = jnp.where(target >= KZ, target - KZ, target)
        placed = placed + jnp.where(slot_index == target, weights[stencil], 0.0)
    return placed


def spread_into(message_ref, moment, rows_x, slope_x, rows_y, slope_y, depth, devices):
    blocks = []
    for step in range(X_PAD):
        flat_x = rows_x[step : step + 1]
        tilt_x = slope_x[step : step + 1]
        for rhs in range(RHS):
            part_x = tilt_x * moment[rhs : rhs + 1]
            part_y = flat_x * moment[RHS + rhs : RHS + rhs + 1]
            part_z = flat_x * moment[2 * RHS + rhs : 2 * RHS + rhs + 1]
            blocks.append(
                jnp.concatenate([part_x * rows_y + part_y * slope_y, part_z * rows_y], axis=1)
            )
    charges = jnp.concatenate(blocks, axis=0)
    spectrum = product(depth, halves(charges), 1, 1)
    slot_rows = message_ref.shape[0] // devices
    chunk = KZ // devices
    width = RHS * Y_PAD
    for step in range(X_PAD):
        message_ref[pl.ds(step, devices, stride=slot_rows), :] = jnp.concatenate(
            [
                spectrum[unit * devices : (unit + 1) * devices, step * width : (step + 1) * width]
                for unit in range(chunk)
            ],
            axis=1,
        )


def sample_from(message_ref, rows_x, slope_x, rows_y, slope_y, depth, devices):
    chunk = KZ // devices
    width = RHS * Y_PAD
    slot_rows = message_ref.shape[0] // devices
    pieces = [
        message_ref[pl.ds(step, devices, stride=slot_rows), :] for step in range(X_PAD)
    ]
    spare = jnp.zeros((devices, KZ - X_PAD * width), jnp.float32)
    spectrum = jnp.concatenate(
        [
            jnp.concatenate(
                [piece[:, unit * width : (unit + 1) * width] for piece in pieces] + [spare], axis=1
            )
            for unit in range(chunk)
        ],
        axis=0,
    )
    spectrum = jnp.transpose(spectrum)[: X_PAD * width]
    sampled = product(halves(spectrum), depth, 1, 0)
    atoms = rows_x.shape[1]
    fields = [None] * (3 * RHS)
    for rhs in range(RHS):
        sum_x = sum_y = sum_z = None
        for step in range(X_PAD):
            first = step * width + rhs * Y_PAD
            flat = sampled[first : first + Y_PAD, :atoms]
            tilt = sampled[first : first + Y_PAD, atoms:]
            part_x = slope_x[step : step + 1] * flat
            part_y = rows_x[step : step + 1] * flat
            part_z = rows_x[step : step + 1] * tilt
            sum_x = part_x if sum_x is None else sum_x + part_x
            sum_y = part_y if sum_y is None else sum_y + part_y
            sum_z = part_z if sum_z is None else sum_z + part_z
        fields[rhs] = jnp.sum(sum_x * rows_y, axis=0, keepdims=True)
        fields[RHS + rhs] = jnp.sum(sum_y * slope_y, axis=0, keepdims=True)
        fields[2 * RHS + rhs] = jnp.sum(sum_z * rows_y, axis=0, keepdims=True)
    return jnp.concatenate(fields, axis=0)


def read_tables(tables_ref):
    return (
        tables_ref[0:X_PAD],
        tables_ref[SLOT_ROWS : SLOT_ROWS + X_PAD],
        tables_ref[2 * SLOT_ROWS : 2 * SLOT_ROWS + Y_PAD],
        tables_ref[2 * SLOT_ROWS + Y_PAD : 2 * SLOT_ROWS + 2 * Y_PAD],
    )


def join_stack(stack_ref, up_ref, payload_ref, down_ref):
    rows = payload_ref.shape[0]
    stack_ref[0:rows] = up_ref[...]
    stack_ref[rows : 2 * rows] = payload_ref[...]
    stack_ref[2 * rows : 3 * rows] = down_ref[...]


def setup_body(
    lengths,
    devices,
    place_ref,
    base_ref,
    start_ref,
    z_high_ref,
    z_low_ref,
    message_ref,
    tables_ref,
    depth_high_ref,
    depth_low_ref,
):
    base = [base_ref[dim] for dim in range(3)]
    fractions = []
    cells = []
    for dim in range(3):
        cell = base[dim] + 2
        cell = jnp.where(cell >= lengths[dim], cell - lengths[dim], cell)
        cells.append(cell)
        fractions.append(place_ref[dim] - cell.astype(jnp.float32))
    values, slopes = spline_table(jnp.concatenate(fractions, axis=0))
    values = [[values[stencil][dim : dim + 1] for stencil in range(5)] for dim in range(3)]
    slopes = [[slopes[stencil][dim : dim + 1] for stencil in range(5)] for dim in range(3)]
    slot_x = lax.rem(cells[0], CX)
    slot_y = lax.rem(cells[1], CY)
    tables_ref[0:SLOT_ROWS] = placed_rows(slot_x, values[0], SLOT_ROWS)
    tables_ref[SLOT_ROWS : 2 * SLOT_ROWS] = placed_rows(slot_x, slopes[0], SLOT_ROWS)
    tables_ref[2 * SLOT_ROWS : 2 * SLOT_ROWS + Y_PAD] = placed_rows(slot_y, values[1], Y_PAD)
    tables_ref[2 * SLOT_ROWS + Y_PAD : 2 * SLOT_ROWS + 2 * Y_PAD] = placed_rows(
        slot_y, slopes[1], Y_PAD
    )
    window = jnp.concatenate(
        [
            placed_rows(base[2], values[2], KZ),
            placed_rows(base[2], slopes[2], KZ),
        ],
        axis=1,
    )
    depth = product((z_high_ref[...], z_low_ref[...]), halves(window), 1, 0)
    depth = halves(depth)
    depth_high_ref[...] = depth[0]
    depth_low_ref[...] = depth[1]
    spread_into(message_ref, start_ref[...], *read_tables(tables_ref), depth, devices)


def transform_in(message_ref, forward_ref, block_high_ref, block_low_ref, rows_count, cols_count):
    gathered = jnp.concatenate(
        [
            jnp.concatenate(
                [
                    message_ref[(r * cols_count + c) * X_PAD : (r * cols_count + c + 1) * X_PAD]
                    for r in range(rows_count)
                ],
                axis=0,
            )
            for c in range(cols_count)
        ],
        axis=1,
    )
    high, low = halves(gathered)
    along = jnp.dot(
        forward_ref[...],
        jnp.concatenate([high, high, low], axis=0),
        preferred_element_type=jnp.float32,
    )
    part = along.shape[1] // cols_count // SPLIT
    along = jnp.concatenate(
        [
            jnp.concatenate(
                [
                    along[:, (c * SPLIT + half) * part : (c * SPLIT + half + 1) * part]
                    for c in range(cols_count)
                ],
                axis=1,
            )
            for half in range(SPLIT)
        ],
        axis=0,
    )
    return product(halves(along), (block_high_ref[...], block_low_ref[...]))


def transform_out(result_ref, values, backward_ref, block_high_ref, block_low_ref, counts):
    rows_count, cols_count = counts
    spread = product(halves(values), (block_high_ref[...], block_low_ref[...]))
    grid_x = spread.shape[0] // SPLIT
    part = spread.shape[1] // cols_count
    spread = jnp.concatenate(
        [
            spread[half * grid_x : (half + 1) * grid_x, c * part : (c + 1) * part]
            for c in range(cols_count)
            for half in range(SPLIT)
        ],
        axis=1,
    )
    high, low = halves(spread)
    along = jnp.dot(
        backward_ref[...],
        jnp.concatenate([high, high, low], axis=0),
        preferred_element_type=jnp.float32,
    )
    width = along.shape[1] // cols_count
    slot_rows = result_ref.shape[0] // (rows_count * cols_count)
    for r in range(rows_count):
        for c in range(cols_count):
            first = (r * cols_count + c) * slot_rows
            result_ref[first : first + X_PAD, :] = along[
                r * X_PAD : (r + 1) * X_PAD, c * width : (c + 1) * width
            ]


def middle_first_body(
    counts,
    position_ref,
    message_ref,
    kernel_ref,
    forward_ref,
    backward_ref,
    block_high_ref,
    block_low_ref,
    back_high_ref,
    back_low_ref,
    result_ref,
    wave_ref,
):
    wave = transform_in(message_ref, forward_ref, block_high_ref, block_low_ref, *counts)
    wave_ref[...] = wave
    transform_out(
        result_ref, wave * kernel_ref[0], backward_ref, back_high_ref, back_low_ref, counts
    )


def gather_rows(parts_ref):
    tiles = [parts_ref[8 * tile : 8 * tile + 8, :] for tile in range(parts_ref.shape[0] // 8)]
    return jnp.concatenate(tiles, axis=1)[0 : 3 * RHS]


def row_total(value, rhs):
    row = lax.broadcasted_iota(jnp.int32, value.shape, 0)
    return total(jnp.where(lax.rem(row, RHS) == rhs, value, 0.0))


def total(value):
    return jnp.sum(jnp.sum(value, axis=0, keepdims=True), axis=1, keepdims=True)


def middle_second_body(
    counts,
    position_ref,
    message_ref,
    kernel_ref,
    forward_ref,
    backward_ref,
    block_high_ref,
    block_low_ref,
    back_high_ref,
    back_low_ref,
    wave_ref,
    rhs_ref,
    start_ref,
    image_ref,
    second_ref,
    near_ref,
    polar_ref,
    result_ref,
):
    rhs_rows = read_rows(rhs_ref)
    near_rows = gather_rows(near_ref)
    wave = transform_in(message_ref, forward_ref, block_high_ref, block_low_ref, *counts)
    filtered = wave * kernel_ref[0]
    transform_out(result_ref, filtered, backward_ref, back_high_ref, back_low_ref, counts)
    before = wave_ref[...]
    grid_y = CY * counts[1]
    lane = lax.broadcasted_iota(jnp.int32, wave.shape, 1)
    own_rhs = lax.rem(lax.div(lane, grid_y), RHS)
    second = second_ref[...]
    start = start_ref[...]
    image = image_ref[...]
    local_part = second / polar_ref[...] - near_rows - self_coef * second
    slot = lax.broadcasted_iota(jnp.int32, (1, result_ref.shape[1]), 1)
    sums = jnp.zeros((1, result_ref.shape[1]), jnp.float32)
    for rhs in range(RHS):
        mine = own_rhs == rhs
        parts = (
            row_total(rhs_rows * start, rhs),
            row_total(start * image, rhs),
            row_total(second * image, rhs),
            row_total(start * local_part, rhs) + total(jnp.where(mine, before * filtered, 0.0)),
            row_total(second * local_part, rhs) + total(jnp.where(mine, wave * filtered, 0.0)),
        )
        for index, part in enumerate(parts):
            sums = jnp.where(slot == rhs * len(parts) + index, part, sums)
    devices = counts[0] * counts[1]
    result_ref[pl.ds(X_PAD, devices, stride=X_PAD + 1), :] = jnp.broadcast_to(
        sums, (devices, sums.shape[1])
    )


def sample_body(
    devices,
    message_ref,
    tables_ref,
    depth_high_ref,
    depth_low_ref,
    start_ref,
    near_ref,
    polar_ref,
    image_ref,
    second_ref,
    payload_ref,
):
    tables = read_tables(tables_ref)
    depth = (depth_high_ref[...], depth_low_ref[...])
    field = sample_from(message_ref, *tables, depth, devices)
    start = start_ref[...]
    polar = polar_ref[...]
    image = start / polar - gather_rows(near_ref) + field - self_coef * start
    second = polar * image
    image_ref[...] = image
    second_ref[...] = second
    store_payload(payload_ref, second)


def spread_body(
    devices,
    tables_ref,
    depth_high_ref,
    depth_low_ref,
    second_ref,
    up_ref,
    payload_ref,
    down_ref,
    result_ref,
    stack_ref,
):
    join_stack(stack_ref, up_ref, payload_ref, down_ref)
    depth = (depth_high_ref[...], depth_low_ref[...])
    spread_into(result_ref, second_ref[...], *read_tables(tables_ref), depth, devices)


def final_body(
    devices,
    message_ref,
    tables_ref,
    depth_high_ref,
    depth_low_ref,
    rhs_ref,
    start_ref,
    image_ref,
    second_ref,
    near_ref,
    polar_ref,
    dipole_ref,
    residual_ref,
):
    tables = read_tables(tables_ref)
    depth = (depth_high_ref[...], depth_low_ref[...])
    field = sample_from(message_ref, *tables, depth, devices)
    second = second_ref[...]
    start = start_ref[...]
    image = image_ref[...]
    image_second = second / polar_ref[...] - gather_rows(near_ref) + field - self_coef * second
    sums = jnp.sum(
        message_ref[pl.ds(X_PAD, devices, stride=X_PAD + 1), :], axis=0, keepdims=True
    )
    steps = []
    for rhs in range(RHS):
        progress, start_image, second_image, start_next, second_next = [
            sums[:, rhs * 5 + index : rhs * 5 + index + 1] for index in range(5)
        ]
        step = progress / start_image
        progress_next = progress - 2.0 * step * start_image + step * step * second_image
        grown = 1.0 + progress_next / progress
        curvature = (
            grown * grown * start_image
            - step * grown * (start_next + second_image)
            + step * step * second_next
        )
        steps.append((step, grown, progress_next / curvature))
    row = lax.broadcasted_iota(jnp.int32, (RHS, 1), 0)
    step, grown, step_next = [
        sum(jnp.where(row == rhs, steps[rhs][index], 0.0) for rhs in range(RHS))
        for index in range(3)
    ]
    for dim in range(3):
        rows = slice(dim * RHS, (dim + 1) * RHS)
        direction = grown * start[rows] - step * second[rows]
        image_direction = grown * image[rows] - step * image_second[rows]
        dipole_ref[dim] = step * start[rows] + step_next * direction
        residual_ref[dim] = rhs_ref[dim] - step * image[rows] - step_next * image_direction


def near_base(entry, brick_rows):
    return lax.shift_right_logical(entry, 2) * brick_rows + lax.bitwise_and(entry, 3)


def fill_near(scratch, left_ref, stack_ref, right_ref):
    rows = stack_ref.shape[0] // 3
    for row_step in range(3):
        for col_step, source in enumerate((left_ref, stack_ref, right_ref)):
            first = (row_step * 3 + col_step) * rows
            scratch[first : first + rows, :] = source[row_step * rows : (row_step + 1) * rows, :]


def fill_near_from_all(scratch, all_ref, counts):
    rows = scratch.shape[0] // 9
    for row_step in range(3):
        row = lax.rem(lax.axis_index("row") + (row_step + counts[0] - 1), counts[0])
        for col_step in range(3):
            col = lax.rem(lax.axis_index("col") + (col_step + counts[1] - 1), counts[1])
            first = (row_step * 3 + col_step) * rows
            source = pl.multiple_of((row * counts[1] + col) * rows, 8)
            scratch[first : first + rows, :] = all_ref[pl.ds(source, rows), :]


def nearest(places, origin, span):
    return places - span * jnp.floor((places - origin) * (1.0 / span) + 0.5)


def unwrap_near(near, tile_count, spans):
    rows = near.shape[0] // 9
    for dim in range(2):
        own = 4 * rows + dim * tile_count
        origin = near[own : own + 1, 0:1]
        for brick in range(9):
            first = brick * rows + dim * tile_count
            near[first : first + tile_count, :] = nearest(
                near[first : first + tile_count, :], origin, spans[dim]
            )


def pick_rows(picked, near, lists_ref, tile, tile_count, quantities, origin, span):
    rows = near.shape[0] // 9
    for entry in range(lists_ref.shape[1]):
        base = near_base(lists_ref[tile, entry], rows)
        for quantity in range(quantities):
            values = near[pl.ds(base + quantity * tile_count, 1), :]
            if quantity == 2 and span is not None:
                values = nearest(values, origin, span)
            first = (entry * quantities + quantity) * GROUP
            picked[first : first + GROUP, :] = jnp.broadcast_to(values, (GROUP, TILE))


def widen_own(near, quantities, tile_count, tile, square, wide):
    offset = near.shape[0] // 9 * 4
    for quantity in range(quantities):
        square[quantity : quantity + 1, :] = near[
            pl.ds(offset + quantity * tile_count + tile, 1), :
        ]
    columns = jnp.transpose(square[...])
    for quantity in range(quantities):
        wide[quantity * TILE : (quantity + 1) * TILE, :] = jnp.broadcast_to(
            columns[:, quantity : quantity + 1], (TILE, TILE)
        )


def add_field(sums, first_term, second_term, apart, moments):
    for rhs in range(RHS):
        moment = [moments[RHS * dim + rhs] for dim in range(3)]
        projected = moment[0] * apart[0] + moment[1] * apart[1] + moment[2] * apart[2]
        weighted = second_term * projected
        for dim in range(3):
            index = RHS * dim + rhs
            sums[index] = sums[index] + (weighted * apart[dim] - first_term * moment[dim])


def finish_sums(field_ref, sums_ref):
    lane = lax.broadcasted_iota(jnp.int32, (TILE, TILE), 1)
    merged = jnp.zeros((TILE, TILE), jnp.float32)
    for index in range(3 * RHS):
        column = jnp.sum(sums_ref[index * TILE : (index + 1) * TILE, :], axis=1, keepdims=True)
        merged = jnp.where(lane == index, column, merged)
    field_ref[...] = jnp.transpose(merged)[0:GROUP]


def pair_rows(start, group):
    return pl.ds(pl.multiple_of(start + group * GROUP, GROUP), GROUP)


def wide_rows(start, group, quantity):
    return pl.ds(pl.multiple_of(quantity * TILE + start + group * GROUP, GROUP), GROUP)


def pair_terms(square_dist, damp):
    inverse = lax.rsqrt(square_dist)
    distance = square_dist * inverse
    inverse_sq = inverse * inverse
    inverse_cube = inverse_sq * inverse
    cubed = damp * (distance * square_dist)
    damping = jnp.exp(cubed)
    bell = jnp.exp(-(ewald_beta * ewald_beta) * square_dist)
    stretched = 1.0 + (SCREEN_SCALE * ewald_beta) * distance
    turned = pl.reciprocal(stretched, approx=True)
    turned = turned * (2.0 - stretched * turned)
    series = SCREEN_COEF[-1] * turned + SCREEN_COEF[-2]
    for coef in SCREEN_COEF[-3::-1]:
        series = series * turned + coef
    screen = bell * turned * series
    gaussian = (2.0 * ewald_beta / math.sqrt(math.pi)) * bell
    bare = screen - damping
    first_term = bare * inverse_cube + gaussian * inverse_sq
    second_term = (
        3.0 * (first_term + (cubed * damping) * inverse_cube)
        + (2.0 * ewald_beta * ewald_beta) * gaussian
    ) * inverse_sq
    return first_term, second_term


def pair_first_body(
    counts,
    tile_count,
    spans,
    lists_ref,
    all_ref,
    after_ref,
    first_ref,
    second_ref,
    field_ref,
    near_ref,
    near,
    picked,
    square,
    wide,
    sums_ref,
):
    @pl.when(pl.program_id(0) == 0)
    def _():
        fill_near_from_all(near, all_ref, counts)
        unwrap_near(near, tile_count, spans)
        square[...] = jnp.zeros_like(square)
        rows = near.shape[0] // 9
        kept = 3 * tile_count
        for brick in range(9):
            near_ref[brick * kept : (brick + 1) * kept, :] = near[
                brick * rows : brick * rows + kept, :
            ]

    tile = pl.program_id(0)
    quantities = near.shape[0] // 9 // tile_count
    widen_own(near, 4, tile_count, tile, square, wide)
    origin = wide[2 * TILE : 2 * TILE + 1, 0:1]
    pick_rows(picked, near, lists_ref, tile, tile_count, quantities, origin, spans[2])

    @pl.loop(0, TILE // PAIR_ROWS)
    def _(part):
        start = part * PAIR_ROWS
        for group in range(PAIR_ROWS // GROUP):
            own = [wide[wide_rows(start, group, dim), :] for dim in range(4)]
            own_damp = -thole_a * own[3]
            sums = [jnp.zeros((GROUP, TILE), jnp.float32) for _ in range(3 * RHS)]
            itself = (
                lax.broadcasted_iota(jnp.int32, (GROUP, TILE), 0) + (start + group * GROUP)
            ) == lax.broadcasted_iota(jnp.int32, (GROUP, TILE), 1)
            for entry in range(lists_ref.shape[1]):
                first = entry * quantities * GROUP
                rows = [
                    picked[first + quantity * GROUP : first + (quantity + 1) * GROUP, :]
                    for quantity in range(quantities)
                ]
                apart = [rows[dim] - own[dim] for dim in range(3)]
                square_dist = apart[0] * apart[0] + apart[1] * apart[1] + apart[2] * apart[2]
                if entry == 0:
                    square_dist = jnp.where(itself, 1.0, square_dist)
                first_term, second_term = pair_terms(square_dist, own_damp * rows[3])
                if entry == 0:
                    first_term = jnp.where(itself, 0.0, first_term)
                    second_term = jnp.where(itself, 0.0, second_term)
                place = wide_rows(start, group, entry)
                first_ref[place, :] = first_term
                second_ref[place, :] = second_term
                add_field(sums, first_term, second_term, apart, rows[4:])
            for index, value in enumerate(sums):
                sums_ref[wide_rows(start, group, index), :] = value

    finish_sums(field_ref, sums_ref)


def pair_second_body(
    tile_count,
    spans,
    lists_ref,
    near,
    left_moment_ref,
    stack_moment_ref,
    right_moment_ref,
    first_ref,
    second_ref,
    field_ref,
    near_moment,
    picked,
    picked_moment,
    square,
    wide,
    sums_ref,
):
    @pl.when(pl.program_id(0) == 0)
    def _():
        fill_near(near_moment, left_moment_ref, stack_moment_ref, right_moment_ref)
        square[...] = jnp.zeros_like(square)

    tile = pl.program_id(0)
    widen_own(near, 3, tile_count, tile, square, wide)
    origin = wide[2 * TILE : 2 * TILE + 1, 0:1]
    pick_rows(picked, near, lists_ref, tile, tile_count, 3, origin, spans[2])
    pick_rows(picked_moment, near_moment, lists_ref, tile, tile_count, 3 * RHS, None, None)

    @pl.loop(0, TILE // PAIR_ROWS)
    def _(part):
        start = part * PAIR_ROWS
        for group in range(PAIR_ROWS // GROUP):
            own = [wide[wide_rows(start, group, dim), :] for dim in range(3)]
            sums = [jnp.zeros((GROUP, TILE), jnp.float32) for _ in range(3 * RHS)]
            for entry in range(lists_ref.shape[1]):
                first = entry * 3 * GROUP
                apart = [
                    picked[first + dim * GROUP : first + (dim + 1) * GROUP, :] - own[dim]
                    for dim in range(3)
                ]
                first = first * RHS
                moments = [
                    picked_moment[first + index * GROUP : first + (index + 1) * GROUP, :]
                    for index in range(3 * RHS)
                ]
                place = wide_rows(start, group, entry)
                add_field(sums, first_ref[place, :], second_ref[place, :], apart, moments)
            for index, value in enumerate(sums):
                sums_ref[wide_rows(start, group, index), :] = value

    finish_sums(field_ref, sums_ref)


def shift(source, axis, step):
    count = lax.axis_size(axis)
    return lax.ppermute(source, axis, [(i, (i + step) % count) for i in range(count)])


def both_ways(source, axis):
    return shift(source, axis, 1), source, shift(source, axis, -1)


def whole(shape):
    return pl.BlockSpec(shape, lambda *_: (0,) * len(shape))


def anywhere():
    return pl.BlockSpec(memory_space=pl.ANY)


def call(body, outs, *operands, after=()):
    def run(*refs):
        body(*refs[len(after) :])

    return pl.pallas_call(
        run,
        grid=(1,),
        in_specs=[anywhere()] * len(after) + [whole(operand.shape) for operand in operands],
        out_specs=[whole(shape) for shape, _ in outs],
        out_shape=[jax.ShapeDtypeStruct(shape, dtype) for shape, dtype in outs],
        compiler_params=pltpu.CompilerParams(vmem_limit_bytes=VMEM_LIMIT),
        cost_estimate=pl.CostEstimate(
            flops=200_000_000, bytes_accessed=4 << 20, transcendentals=0
        ),
    )(*after, *operands)


def middle_call(body, outs, position, message, kernel, *operands, after=()):
    def run(position_ref, *refs):
        body(position_ref, *refs[len(after) :])

    return pl.pallas_call(
        run,
        grid_spec=pltpu.PrefetchScalarGridSpec(
            num_scalar_prefetch=1,
            grid=(1,),
            in_specs=[anywhere()] * len(after)
            + [whole(message.shape)]
            + [pl.BlockSpec((1,) + kernel.shape[1:], lambda i, s: (s[0], 0, 0))]
            + [whole(operand.shape) for operand in operands],
            out_specs=[whole(shape) for shape in outs],
        ),
        out_shape=[jax.ShapeDtypeStruct(shape, jnp.float32) for shape in outs],
        compiler_params=pltpu.CompilerParams(vmem_limit_bytes=VMEM_LIMIT),
        cost_estimate=pl.CostEstimate(
            flops=200_000_000, bytes_accessed=4 << 20, transcendentals=0
        ),
    )(position, *after, message, kernel, *operands)


def pair_call(body, outs, kept, tiles, blocked, scratch, lists, *operands, after=()):
    def block(operand):
        rows = operand.shape[0] // tiles
        return pl.BlockSpec((rows, operand.shape[1]), lambda i, s: (i, 0))

    out_shape = [jax.ShapeDtypeStruct(shape, jnp.float32) for shape in outs + kept]
    plain = len(operands) - blocked
    return pl.pallas_call(
        body,
        out_shape=out_shape,
        grid_spec=pltpu.PrefetchScalarGridSpec(
            num_scalar_prefetch=1,
            grid=(tiles,),
            in_specs=[whole(operand.shape) for operand in operands[:plain]]
            + [block(operand) for operand in operands[plain:]]
            + [anywhere()] * len(after),
            out_specs=[block(shape) for shape in out_shape[: len(outs)]]
            + [whole(shape) for shape in kept],
            scratch_shapes=[pltpu.VMEM(shape, jnp.float32) for shape in scratch],
        ),
        compiler_params=pltpu.CompilerParams(vmem_limit_bytes=VMEM_LIMIT),
        cost_estimate=pl.CostEstimate(
            flops=80_000_000, bytes_accessed=8 << 20, transcendentals=1 << 21
        ),
    )(lists, *operands, *after)


def exchange(message, devices):
    shape = message.shape
    sent = message.reshape(devices, 1, -1)
    return lax.all_to_all(sent, ("row", "col"), split_axis=0, concat_axis=0, tiled=True).reshape(
        shape
    )


def slab_local(field_rhs, positions, polar, grid_base, tile_lists):
    rows_count = lax.axis_size("row")
    cols_count = lax.axis_size("col")
    counts = (rows_count, cols_count)
    devices = rows_count * cols_count
    lengths = (CX * rows_count, CY * cols_count, KZ)
    spans = tuple(float(length) for length in lengths)
    atoms = polar.shape[-1]
    tile_count = atoms // TILE
    listed = tile_lists.shape[-1]
    tables = slab_tables(rows_count, cols_count)
    f32 = jnp.float32
    rhs = jnp.swapaxes(field_rhs[0, 0], 0, 1)
    place = jnp.swapaxes(positions[0], 0, 1)
    base = jnp.swapaxes(grid_base[0], 0, 1)
    polar = polar.reshape(1, atoms)
    lists = tile_lists[0, 0]
    quantities = 4 + 3 * RHS
    brick_rows = quantities * tile_count
    moment_rows = 3 * RHS * tile_count
    message_shape = (devices * X_PAD, KZ // devices * RHS * Y_PAD)
    last_shape = (devices * (X_PAD + 1), message_shape[1])
    row_shape = (3 * RHS, atoms)
    square = (TILE, TILE)
    wide = (4 * TILE, TILE)
    sums = (3 * RHS * TILE, TILE)

    start, payload = call(pack_body, [(row_shape, f32), ((brick_rows, TILE), f32)], rhs, place, polar)

    def setup(*refs):
        setup_body(lengths, devices, *refs)

    everyone = lax.all_gather(payload, ("row", "col"), axis=0, tiled=True)
    message, splines, depth_high, depth_low = call(
        setup,
        [
            (message_shape, f32),
            ((2 * SLOT_ROWS + 2 * Y_PAD, atoms), f32),
            ((KZ, 2 * atoms), jnp.bfloat16),
            ((KZ, 2 * atoms), jnp.bfloat16),
        ],
        place,
        base,
        start,
        *[jnp.asarray(table) for table in tables["along_z"]],
    )
    position = (lax.axis_index("row") * cols_count + lax.axis_index("col")).reshape(1)
    constants = (
        jnp.asarray(tables["kernel"]),
        jnp.asarray(tables["forward_x"]),
        jnp.asarray(tables["backward_x"]),
        *[jnp.asarray(table) for table in tables["block"]],
        *[jnp.asarray(table) for table in tables["block_back"]],
    )
    arrived = exchange(message, devices)

    def middle_first(*refs):
        middle_first_body(counts, *refs)

    mixed, wave = middle_call(
        middle_first,
        [message_shape, tables["kernel"].shape[1:]],
        position,
        arrived,
        *constants,
    )
    returned = exchange(mixed, devices)

    def pair_first(*refs):
        pair_first_body(counts, tile_count, spans, *refs)

    first_term, second_term, direct, near = pair_call(
        pair_first,
        [(tile_count * listed * TILE, TILE)] * 2 + [(tile_count * GROUP, TILE)],
        [(9 * 3 * tile_count, TILE)],
        tile_count,
        0,
        [(9 * brick_rows, TILE), (listed * quantities * GROUP, TILE), square, wide, sums],
        lists,
        everyone,
        after=(wave,),
    )

    def sample(*refs):
        sample_body(devices, *refs)

    image, second, moments = call(
        sample,
        [(row_shape, f32), (row_shape, f32), ((moment_rows, TILE), f32)],
        returned,
        splines,
        depth_high,
        depth_low,
        start,
        direct,
        polar,
    )

    def spread(*refs):
        spread_body(devices, *refs)

    message, stack = call(
        spread,
        [(message_shape, f32), ((3 * moment_rows, TILE), f32)],
        splines,
        depth_high,
        depth_low,
        second,
        *both_ways(moments, "row"),
    )
    near_moments = both_ways(stack, "col")
    arrived = exchange(message, devices)

    def pair_second(*refs):
        pair_second_body(tile_count, spans, *refs)

    (direct,) = pair_call(
        pair_second,
        [(tile_count * GROUP, TILE)],
        [],
        tile_count,
        2,
        [
            (9 * moment_rows, TILE),
            (listed * 3 * GROUP, TILE),
            (listed * 3 * RHS * GROUP, TILE),
            square,
            wide,
            sums,
        ],
        lists,
        near,
        *near_moments,
        first_term,
        second_term,
    )

    def middle_second(*refs):
        middle_second_body(counts, *refs)

    (mixed,) = middle_call(
        middle_second,
        [last_shape],
        position,
        arrived,
        *constants,
        wave,
        rhs,
        start,
        image,
        second,
        direct,
        polar,
    )
    returned = exchange(mixed, devices)

    def final(*refs):
        final_body(devices, *refs)

    outs = call(
        final,
        [(rhs.shape, f32), (rhs.shape, f32)],
        returned,
        splines,
        depth_high,
        depth_low,
        rhs,
        start,
        image,
        second,
        direct,
        polar,
    )
    return tuple(jnp.swapaxes(out, 0, 1)[None, None] for out in outs)


def solution(mesh):
    placed = (
        P("row", "col", None, None, None),
        P("row", "col", None, None),
        P("row", "col", None),
        P("row", "col", None, None),
        P("row", "col", None, None),
    )
    devices = mesh.shape["row"] * mesh.shape["col"]
    return jax.shard_map(
        slab_local if KZ % devices == 0 else pencil_local,
        mesh=mesh,
        in_specs=placed,
        out_specs=(P("row", "col", None, None, None), P("row", "col", None, None, None)),
        check_vma=False,
    )
```

```python
import math

import jax
import jax.numpy as jnp
import ml_dtypes
import numpy as np
from jax import lax
from jax.experimental import pallas as pl
from jax.experimental.pallas import tpu as pltpu
from jax.sharding import PartitionSpec as P

CX = 8
CY = 4
KZ = 256
TILE = 128
RHS = 2
ITERS = 2


ewald_beta = 0.4
thole_a = 0.39
self_coef = 4.0 * ewald_beta**3 / (3.0 * math.sqrt(math.pi))
highest = lax.Precision.HIGHEST


def with_halo(cells, sides, width):
    for axis, dim in sides:
        count = lax.axis_size(axis)
        head = lax.slice_in_dim(cells, 0, width, axis=dim)
        tail = lax.slice_in_dim(cells, cells.shape[dim] - width, cells.shape[dim], axis=dim)
        cells = jnp.concatenate(
            [
                lax.ppermute(tail, axis, [(i, (i + 1) % count) for i in range(count)]),
                cells,
                lax.ppermute(head, axis, [((i + 1) % count, i) for i in range(count)]),
            ],
            axis=dim,
        )
    return cells


def spline_table(fraction):
    previous = {0: jnp.ones_like(fraction)}
    fourth = previous
    for degree in range(2, 6):
        current = {}
        for offset in range(degree):
            abscissa = fraction + offset
            summed = abscissa * previous.get(offset, 0.0) + (degree - abscissa) * previous.get(
                offset - 1, 0.0
            )
            current[offset] = summed / (degree - 1)
        if degree == 4:
            fourth = current
        previous = current
    values = jnp.stack([previous[4 - stencil] for stencil in range(5)])
    slopes = jnp.stack(
        [fourth.get(4 - stencil, 0.0) - fourth.get(3 - stencil, 0.0) for stencil in range(5)]
    )
    return (values, slopes)


def spline_modulus(wave_index, length):
    spline_coef = (1.0 / 24.0, 11.0 / 24.0, 11.0 / 24.0, 1.0 / 24.0)
    cosine_sum = jnp.zeros(wave_index.shape, jnp.float32)
    sine_sum = jnp.zeros(wave_index.shape, jnp.float32)
    for offset in range(4):
        angles = 2.0 * math.pi / length * (wave_index * offset % length).astype(jnp.float32)
        cosine_sum = cosine_sum + spline_coef[offset] * jnp.cos(angles)
        sine_sum = sine_sum + spline_coef[offset] * jnp.sin(angles)
    return cosine_sum * cosine_sum + sine_sum * sine_sum


def folded_square(wave_index, length):
    nearest = jnp.minimum(wave_index, length - wave_index).astype(jnp.float32) / length
    return nearest * nearest


def influence(wave_x, wave_y, wave_z, length_x, length_y, length_z):
    wave_norm = (
        folded_square(wave_x, length_x)
        + folded_square(wave_y, length_y)
        + folded_square(wave_z, length_z)
    )
    modulus = (
        spline_modulus(wave_x, length_x)
        * spline_modulus(wave_y, length_y)
        * spline_modulus(wave_z, length_z)
    )
    excluded = (wave_x * 2 == length_x) | (wave_y * 2 == length_y) | (wave_z * 2 == length_z)
    excluded = excluded | (wave_x == 0) & (wave_y == 0) & (wave_z == 0)
    safe_norm = jnp.where(excluded, 1.0, wave_norm)
    safe_modulus = jnp.where(excluded, 1.0, modulus)
    result = jnp.exp(-(math.pi**2 / ewald_beta**2) * safe_norm) / (
        math.pi * safe_norm * safe_modulus
    )
    return jnp.where(excluded, 0.0, result)


def tile_field(own_static, near_static, near_dipole, box_spans):
    listed_count = near_static.shape[0]
    tile_width = own_static.shape[1]
    box_span = jnp.array(box_spans, dtype=jnp.float32)[None, :, None, None]
    separation = near_static[:, 0:3, None, :] - own_static[None, 0:3, :, None]
    separation = separation - box_span * jnp.floor(separation / box_span + 0.5)
    dist_sq = jnp.sum(separation * separation, axis=1)
    itself = (jnp.arange(listed_count)[:, None, None] == 0) & (
        jnp.arange(tile_width)[:, None] == jnp.arange(tile_width)[None, :]
    )[None]
    safe_sq = jnp.where(itself, 1.0, dist_sq)
    distance = jnp.sqrt(safe_sq)
    scaled = distance / (own_static[3][None, :, None] * near_static[:, 3][:, None, :])
    cubed = thole_a * scaled * scaled * scaled
    damping = jnp.exp(-cubed)
    screen = lax.erfc(ewald_beta * distance)
    gaussian = 2.0 * ewald_beta / math.sqrt(math.pi) * jnp.exp(-(ewald_beta * ewald_beta) * safe_sq)
    inverse_sq = 1.0 / safe_sq
    inverse_cube = inverse_sq / distance
    first_term = (screen - damping) * inverse_cube + gaussian * inverse_sq
    second = (
        3.0 * (screen - (1.0 + cubed) * damping) * inverse_cube * inverse_sq
        + gaussian * (2.0 * ewald_beta * ewald_beta + 3.0 * inverse_sq) * inverse_sq
    )
    first_term = jnp.where(itself, 0.0, first_term)
    second = jnp.where(itself, 0.0, second)
    projected = jnp.sum(near_dipole[:, :, :, None, :] * separation[:, None, :, :, :], axis=2)
    weighted = second[:, None] * projected
    outward = jnp.sum(weighted[:, :, None] * separation[:, None], axis=(0, 4))
    inward = jnp.sum(first_term[:, None, None] * near_dipole[:, :, :, None, :], axis=(0, 4))
    return outward - inward


def hartley(length):
    counter = jnp.arange(length, dtype=jnp.int32)
    angles = (
        2.0 * math.pi / length * (counter[:, None] * counter[None, :] % length).astype(jnp.float32)
    )
    return jnp.cos(angles) + jnp.sin(angles)


def placed_table(first_cell, weights, extent):
    slot_index = jnp.arange(extent, dtype=jnp.int32)[:, None]
    placed = jnp.zeros((extent, first_cell.shape[0]), jnp.float32)
    for stencil in range(5):
        placed = placed + jnp.where(
            slot_index == (first_cell[None, :] + stencil) % extent, weights[stencil][None, :], 0.0
        )
    return placed


def pad_axis(source, axis_pos, leading, trailing):
    widths = [(0, 0)] * source.ndim
    widths[axis_pos] = (leading, trailing)
    return jnp.pad(source, widths)


def fold_cycle(cycle_only, axis_pos, inner_len):
    middle = lax.slice_in_dim(cycle_only, 4, inner_len + 4, axis=axis_pos)
    lower_cycle = lax.slice_in_dim(cycle_only, 0, 2, axis=axis_pos)
    upper_cycle = lax.slice_in_dim(cycle_only, inner_len + 6, inner_len + 8, axis=axis_pos)
    return (
        middle
        + pad_axis(lower_cycle, axis_pos, 0, inner_len - 2)
        + pad_axis(upper_cycle, axis_pos, inner_len - 2, 0)
    )


def clear_inside(extended, extents):
    inside = None
    for axis_pos, inner_len in extents:
        slot_index = lax.broadcasted_iota(jnp.int32, extended.shape, axis_pos)
        within = (slot_index >= 2) & (slot_index < inner_len + 6)
        inside = within if inside is None else inside & within
    return jnp.where(inside, 0.0, extended)


def inner_sum(left_arr, right_arr):
    return lax.psum(jnp.sum(left_arr * right_arr, axis=(1, 2)), ("row", "col"))


def pencil_local(field_rhs, positions, polar, grid_base, tile_lists):
    rows_count = lax.axis_size("row")
    cols_count = lax.axis_size("col")
    grid_x = CX * rows_count
    grid_y = CY * cols_count
    atom_count = polar.shape[-1]
    tile_count = atom_count // TILE
    slab_depth = KZ // tile_count
    window_len = slab_depth + 4
    box_spans = (float(grid_x), float(grid_y), float(KZ))
    own_place = positions[0, 0]
    own_base = grid_base[0, 0]
    own_polar = polar[0, 0]
    lengths = jnp.array([grid_x, grid_y, KZ], dtype=jnp.int32)[:, None]
    cell_index = (own_base + 2) % lengths
    fraction = own_place - cell_index.astype(jnp.float32)
    values, slopes = spline_table(fraction)
    first_x = (own_base[0] - lax.axis_index("row") * CX + 2) % grid_x
    first_y = (own_base[1] - lax.axis_index("col") * CY + 2) % grid_y
    rows_x = placed_table(first_x, values[:, 0], CX + 4)
    slope_x = placed_table(first_x, slopes[:, 0], CX + 4)
    rows_y = placed_table(first_y, values[:, 1], CY + 4)
    slope_y = placed_table(first_y, slopes[:, 1], CY + 4)
    tile_start = jnp.arange(atom_count, dtype=jnp.int32) // TILE * slab_depth
    first_z = (own_base[2] + 2 - tile_start) % KZ
    rows_z = placed_table(first_z, values[:, 2], window_len)
    slope_z = placed_table(first_z, slopes[:, 2], window_len)
    plane_count = (CX + 4) * (CY + 4)
    plane_dx = (slope_x[:, None, :] * rows_y[None, :, :]).reshape(plane_count, atom_count)
    plane_dy = (rows_x[:, None, :] * slope_y[None, :, :]).reshape(plane_count, atom_count)
    plane_flat = (rows_x[:, None, :] * rows_y[None, :, :]).reshape(plane_count, atom_count)
    window_rows = jnp.moveaxis(rows_z.reshape(window_len, tile_count, TILE), 1, 0)
    window_slope = jnp.moveaxis(slope_z.reshape(window_len, tile_count, TILE), 1, 0)
    depth_table = jnp.concatenate([window_rows, window_slope], axis=2)
    grid_scale = 1.0 / (grid_x * grid_y * KZ)
    hartley_x = hartley(grid_x)
    hartley_y = hartley(grid_y)
    hartley_z = hartley(KZ)
    block_y = grid_y // rows_count
    block_z = KZ // cols_count
    wave_x = jnp.arange(grid_x, dtype=jnp.int32)[:, None, None]
    wave_y = (lax.axis_index("row") * block_y + jnp.arange(block_y, dtype=jnp.int32))[None, :, None]
    wave_z = (lax.axis_index("col") * block_z + jnp.arange(block_z, dtype=jnp.int32))[None, None, :]
    kernel = influence(wave_x, wave_y, wave_z, grid_x, grid_y, KZ) * grid_scale
    root_scale = jnp.power(own_polar, 1.0 / 6.0)
    own_static = jnp.concatenate([own_place, root_scale[None]], axis=0)
    near_static = with_halo(own_static[None, None], (("row", 0), ("col", 1)), 1)
    near_static = jnp.moveaxis(near_static.reshape(9, 4, tile_count, TILE), 2, 1).reshape(
        9 * tile_count, 4, TILE
    )
    own_tiles = jnp.moveaxis(own_static.reshape(4, tile_count, TILE), 1, 0)
    own_lists = tile_lists[0, 0]
    polar_wide = own_polar[None, None, :]
    solution = jnp.zeros_like(field_rhs[0, 0])
    residual = field_rhs[0, 0]
    scaled_res = polar_wide * residual
    direction = scaled_res
    progress = inner_sum(residual, scaled_res)
    for iteration in range(ITERS):
        near_dip = with_halo(direction[None, None], (("row", 0), ("col", 1)), 1)
        near_dip = jnp.moveaxis(near_dip.reshape(9, RHS, 3, tile_count, TILE), 3, 1).reshape(
            9 * tile_count, RHS, 3, TILE
        )

        def one_tile(tile_pos):
            picked = own_lists[tile_pos]
            return tile_field(own_tiles[tile_pos], near_static[picked], near_dip[picked], box_spans)

        fields = lax.map(one_tile, jnp.arange(tile_count, dtype=jnp.int32))
        direct = jnp.moveaxis(fields, 0, 2).reshape(RHS, 3, atom_count)
        slope_terms = (
            direction[:, 0, None, :] * plane_dx[None] + direction[:, 1, None, :] * plane_dy[None]
        )
        flat_terms = direction[:, 2, None, :] * plane_flat[None]
        spread_left = jnp.concatenate(
            [
                slope_terms.reshape(RHS, plane_count, tile_count, TILE),
                flat_terms.reshape(RHS, plane_count, tile_count, TILE),
            ],
            axis=3,
        )
        spread_windows = jnp.einsum("sptb,twb->sptw", spread_left, depth_table, precision=highest)
        main_part = spread_windows[..., :slab_depth].reshape(spread_windows.shape[:-2] + (KZ,))
        tail_part = pad_axis(
            spread_windows[..., slab_depth:], spread_windows.ndim - 1, 0, slab_depth - 4
        )
        tail_part = tail_part.reshape(spread_windows.shape[:-2] + (KZ,))[..., : KZ + 4 - slab_depth]
        last_axis = main_part.ndim - 1
        padded_line = pad_axis(main_part, last_axis, 0, 4) + pad_axis(
            tail_part, last_axis, slab_depth, 0
        )
        inner = padded_line[..., 2 : KZ + 2]
        spread_tile = (
            inner
            + pad_axis(padded_line[..., 0:2], last_axis, KZ - 2, 0)
            + pad_axis(padded_line[..., KZ + 2 : KZ + 4], last_axis, 0, KZ - 2)
        ).reshape(RHS, CX + 4, CY + 4, KZ)
        extended = with_halo(spread_tile, (("row", 1), ("col", 2)), 2)
        cycle_only = clear_inside(extended, ((1, CX), (2, CY)))
        folded = fold_cycle(fold_cycle(cycle_only, 1, CX), 2, CY)
        spectrum = jnp.einsum(
            "sxyz,zk->sxyk",
            spread_tile[:, 2 : CX + 2, 2 : CY + 2] + folded,
            hartley_z,
            precision=highest,
        )
        along_y = jnp.einsum(
            "sxyz,yk->sxkz",
            lax.all_to_all(spectrum, "col", split_axis=3, concat_axis=2, tiled=True),
            hartley_y,
            precision=highest,
        )
        along_x = (
            jnp.einsum(
                "sxyz,xk->skyz",
                lax.all_to_all(along_y, "row", split_axis=2, concat_axis=1, tiled=True),
                hartley_x,
                precision=highest,
            )
            * kernel[None]
        )
        mixed_part = jnp.einsum("sxyz,xk->skyz", along_x, hartley_x, precision=highest)
        returned = lax.all_to_all(mixed_part, "row", split_axis=1, concat_axis=2, tiled=True)
        swapped = jnp.einsum("sxyz,yk->sxkz", returned, hartley_y, precision=highest)
        restored = lax.all_to_all(swapped, "col", split_axis=2, concat_axis=3, tiled=True)
        padded = with_halo(
            jnp.einsum("sxyz,zk->sxyk", restored, hartley_z, precision=highest),
            (("row", 1), ("col", 2)),
            2,
        )
        line = padded.reshape(RHS, plane_count, KZ)
        extended_line = jnp.concatenate([line[..., KZ - 2 :], line, line[..., :2]], axis=-1)
        windows = jnp.stack(
            [
                extended_line[..., tile * slab_depth : tile * slab_depth + window_len]
                for tile in range(tile_count)
            ],
            axis=-2,
        )
        sampled = jnp.einsum("sptw,twb->sptb", windows, depth_table, precision=highest)
        with_flat = sampled[..., :TILE].reshape(RHS, plane_count, atom_count)
        with_slope = sampled[..., TILE:].reshape(RHS, plane_count, atom_count)
        recip_part = jnp.stack(
            [
                jnp.sum(with_flat * plane_dx[None], axis=1),
                jnp.sum(with_flat * plane_dy[None], axis=1),
                jnp.sum(with_slope * plane_flat[None], axis=1),
            ],
            axis=1,
        )
        image_field = direction / polar_wide - direct + recip_part - self_coef * direction
        step_size = (progress / inner_sum(direction, image_field))[:, None, None]
        solution = solution + step_size * direction
        residual = residual - step_size * image_field
        scaled_res = polar_wide * residual
        progress_next = inner_sum(residual, scaled_res)
        direction = scaled_res + (progress_next / progress)[:, None, None] * direction
        progress = progress_next
    return (solution[None, None], residual[None, None])


X_PAD = CX + 4
Y_PAD = CY + 4
SLOT_ROWS = 16
SPLIT = 2
VMEM_LIMIT = 60_000_000
FINAL_VMEM_LIMIT = 24_000_000
EARLY_TILES = 1
PAIR_ROWS = 32
GROUP = 8
SCREEN_SCALE = 0.4
SCREEN_COEF = (
    0.22567588090896606,
    0.2256690263748169,
    0.20785020291805267,
    0.16849851608276367,
    0.14156343042850494,
    -0.005832736846059561,
    0.16930203139781952,
    -0.1830107867717743,
    0.05028456076979637,
)


def halves(value):
    high = value.astype(jnp.bfloat16)
    return high, (value - high.astype(jnp.float32)).astype(jnp.bfloat16)


def halves_np(value):
    value = value.astype(np.float32)
    high = value.astype(ml_dtypes.bfloat16)
    return high, (value - high.astype(np.float32)).astype(ml_dtypes.bfloat16)


def product(left, right, left_dim=1, right_dim=0):
    def one(first, second):
        return lax.dot_general(
            first,
            second,
            (((left_dim,), (right_dim,)), ((), ())),
            preferred_element_type=jnp.float32,
        )

    return one(left[0], right[0]) + (one(left[1], right[0]) + one(left[0], right[1]))


def cas_np(wave, place, length):
    angles = 2.0 * np.pi / length * (wave[:, None] * place[None, :] % length)
    return np.cos(angles) + np.sin(angles)


def modulus_np(wave, length):
    coef = np.array([1.0, 11.0, 11.0, 1.0]) / 24.0
    angles = 2.0 * np.pi / length * (wave[:, None] * np.arange(4)[None, :])
    return (coef * np.cos(angles)).sum(1) ** 2 + (coef * np.sin(angles)).sum(1) ** 2


def influence_np(length_x, length_y, length_z):
    total = np.zeros((length_x, length_y, length_z))
    modulus = np.ones((length_x, length_y, length_z))
    excluded = np.zeros((length_x, length_y, length_z), bool)
    for axis, length in enumerate((length_x, length_y, length_z)):
        wave = np.arange(length)
        shape = [1, 1, 1]
        shape[axis] = length
        total = total + ((np.minimum(wave, length - wave) / length) ** 2).reshape(shape)
        modulus = modulus * modulus_np(wave, length).reshape(shape)
        excluded = excluded | (wave * 2 == length).reshape(shape)
    excluded[0, 0, 0] = True
    safe = np.where(excluded, 1.0, total)
    result = np.exp(-(np.pi**2) / ewald_beta**2 * safe) / (
        np.pi * safe * np.where(excluded, 1.0, modulus)
    )
    return np.where(excluded, 0.0, result) / (length_x * length_y * length_z)


def slab_tables(rows_count, cols_count):
    grid_x = CX * rows_count
    grid_y = CY * cols_count
    devices = rows_count * cols_count
    chunk = KZ // devices
    wave_z = (np.arange(devices)[None, :] * chunk + np.arange(chunk)[:, None]).reshape(-1)
    along_z = cas_np(wave_z, np.arange(KZ), KZ)
    place_x = np.arange(rows_count)[:, None] * CX + np.arange(X_PAD)[None, :] - 2
    along_x = cas_np(np.arange(grid_x), place_x.reshape(-1) % grid_x, grid_x)
    x_high, x_low = halves_np(along_x)
    forward_x = np.concatenate([x_high, x_low, x_high], axis=1)
    backward_x = np.concatenate([x_high.T, x_low.T, x_high.T], axis=1)
    place_y = (np.arange(cols_count)[:, None] * CY + np.arange(Y_PAD)[None, :] - 2) % grid_y
    along_y = cas_np(np.arange(grid_y), place_y.reshape(-1), grid_y)
    along_y = along_y.reshape(grid_y, cols_count, Y_PAD)
    units = chunk * RHS // SPLIT
    block = np.einsum("uv,kcy->cuyvk", np.eye(units), along_y)
    block = block.reshape(cols_count * units * Y_PAD, units * grid_y)
    kernel = influence_np(grid_x, grid_y, KZ).reshape(grid_x, grid_y, devices, chunk)
    kernel = np.transpose(kernel, (2, 0, 3, 1))[:, :, :, None, :]
    kernel = np.broadcast_to(kernel, (devices, grid_x, chunk, RHS, grid_y))
    kernel = kernel.reshape(devices, grid_x, SPLIT, units * grid_y)
    kernel = np.moveaxis(kernel, 2, 1).reshape(devices, SPLIT * grid_x, units * grid_y)
    kernel = kernel.astype(np.float32)
    return dict(
        along_z=halves_np(along_z),
        forward_x=forward_x,
        backward_x=backward_x,
        block=halves_np(block),
        block_back=halves_np(np.ascontiguousarray(block.T)),
        kernel=kernel,
    )


def pack_body(rhs_ref, place_ref, polar_ref, start_ref, payload_ref):
    polar = polar_ref[...]
    start = read_rows(rhs_ref) * polar
    start_ref[...] = start
    place = [place_ref[dim] for dim in range(3)]
    everything = jnp.concatenate(place + [1.0 / jnp.sqrt(polar), start], axis=0)
    store_payload(payload_ref, everything)


def read_rows(rows_ref):
    return jnp.concatenate([rows_ref[dim] for dim in range(3)], axis=0)


def store_payload(payload_ref, everything):
    tile_count = everything.shape[1] // TILE
    for quantity in range(everything.shape[0]):
        for tile in range(tile_count):
            row = quantity * tile_count + tile
            payload_ref[row : row + 1, :] = everything[
                quantity : quantity + 1, tile * TILE : (tile + 1) * TILE
            ]


def placed_rows(slot, weights, extent):
    slot_index = lax.broadcasted_iota(jnp.int32, (extent, slot.shape[1]), 0)
    placed = jnp.zeros((extent, slot.shape[1]), jnp.float32)
    for stencil in range(5):
        target = slot + stencil
        if extent == KZ:
            target = jnp.where(target >= KZ, target - KZ, target)
        placed = placed + jnp.where(slot_index == target, weights[stencil], 0.0)
    return placed


def spread_into(message_ref, moment, rows_x, slope_x, rows_y, slope_y, depth, devices):
    blocks = []
    for step in range(X_PAD):
        flat_x = rows_x[step : step + 1]
        tilt_x = slope_x[step : step + 1]
        for rhs in range(RHS):
            part_x = tilt_x * moment[rhs : rhs + 1]
            part_y = flat_x * moment[RHS + rhs : RHS + rhs + 1]
            part_z = flat_x * moment[2 * RHS + rhs : 2 * RHS + rhs + 1]
            blocks.append(
                jnp.concatenate([part_x * rows_y + part_y * slope_y, part_z * rows_y], axis=1)
            )
    charges = jnp.concatenate(blocks, axis=0)
    spectrum = product(depth, halves(charges), 1, 1)
    slot_rows = message_ref.shape[0] // devices
    chunk = KZ // devices
    width = RHS * Y_PAD
    for step in range(X_PAD):
        message_ref[pl.ds(step, devices, stride=slot_rows), :] = jnp.concatenate(
            [
                spectrum[unit * devices : (unit + 1) * devices, step * width : (step + 1) * width]
                for unit in range(chunk)
            ],
            axis=1,
        )


def sample_from(message_ref, rows_x, slope_x, rows_y, slope_y, depth, devices):
    chunk = KZ // devices
    width = RHS * Y_PAD
    slot_rows = message_ref.shape[0] // devices
    pieces = [
        message_ref[pl.ds(step, devices, stride=slot_rows), :] for step in range(X_PAD)
    ]
    spare = jnp.zeros((devices, KZ - X_PAD * width), jnp.float32)
    spectrum = jnp.concatenate(
        [
            jnp.concatenate(
                [piece[:, unit * width : (unit + 1) * width] for piece in pieces] + [spare], axis=1
            )
            for unit in range(chunk)
        ],
        axis=0,
    )
    spectrum = jnp.transpose(spectrum)[: X_PAD * width]
    sampled = product(halves(spectrum), depth, 1, 0)
    atoms = rows_x.shape[1]
    fields = [None] * (3 * RHS)
    for rhs in range(RHS):
        sum_x = sum_y = sum_z = None
        for step in range(X_PAD):
            first = step * width + rhs * Y_PAD
            flat = sampled[first : first + Y_PAD, :atoms]
            tilt = sampled[first : first + Y_PAD, atoms:]
            part_x = slope_x[step : step + 1] * flat
            part_y = rows_x[step : step + 1] * flat
            part_z = rows_x[step : step + 1] * tilt
            sum_x = part_x if sum_x is None else sum_x + part_x
            sum_y = part_y if sum_y is None else sum_y + part_y
            sum_z = part_z if sum_z is None else sum_z + part_z
        fields[rhs] = jnp.sum(sum_x * rows_y, axis=0, keepdims=True)
        fields[RHS + rhs] = jnp.sum(sum_y * slope_y, axis=0, keepdims=True)
        fields[2 * RHS + rhs] = jnp.sum(sum_z * rows_y, axis=0, keepdims=True)
    return jnp.concatenate(fields, axis=0)


def read_tables(tables_ref):
    return (
        tables_ref[0:X_PAD],
        tables_ref[SLOT_ROWS : SLOT_ROWS + X_PAD],
        tables_ref[2 * SLOT_ROWS : 2 * SLOT_ROWS + Y_PAD],
        tables_ref[2 * SLOT_ROWS + Y_PAD : 2 * SLOT_ROWS + 2 * Y_PAD],
    )


def join_body(message_ref, left_ref, payload_ref, right_ref, passed_ref, stack_ref):
    rows = payload_ref.shape[0]
    stack_ref[0:rows] = left_ref[...]
    stack_ref[rows : 2 * rows] = payload_ref[...]
    stack_ref[2 * rows : 3 * rows] = right_ref[...]


def setup_body(
    lengths,
    devices,
    place_ref,
    base_ref,
    start_ref,
    z_high_ref,
    z_low_ref,
    message_ref,
    tables_ref,
    depth_high_ref,
    depth_low_ref,
):
    base = [base_ref[dim] for dim in range(3)]
    fractions = []
    cells = []
    for dim in range(3):
        cell = base[dim] + 2
        cell = jnp.where(cell >= lengths[dim], cell - lengths[dim], cell)
        cells.append(cell)
        fractions.append(place_ref[dim] - cell.astype(jnp.float32))
    values, slopes = spline_table(jnp.concatenate(fractions, axis=0))
    values = [[values[stencil][dim : dim + 1] for stencil in range(5)] for dim in range(3)]
    slopes = [[slopes[stencil][dim : dim + 1] for stencil in range(5)] for dim in range(3)]
    slot_x = lax.rem(cells[0], CX)
    slot_y = lax.rem(cells[1], CY)
    tables_ref[0:SLOT_ROWS] = placed_rows(slot_x, values[0], SLOT_ROWS)
    tables_ref[SLOT_ROWS : 2 * SLOT_ROWS] = placed_rows(slot_x, slopes[0], SLOT_ROWS)
    tables_ref[2 * SLOT_ROWS : 2 * SLOT_ROWS + Y_PAD] = placed_rows(slot_y, values[1], Y_PAD)
    tables_ref[2 * SLOT_ROWS + Y_PAD : 2 * SLOT_ROWS + 2 * Y_PAD] = placed_rows(
        slot_y, slopes[1], Y_PAD
    )
    window = jnp.concatenate(
        [
            placed_rows(base[2], values[2], KZ),
            placed_rows(base[2], slopes[2], KZ),
        ],
        axis=1,
    )
    depth = product((z_high_ref[...], z_low_ref[...]), halves(window), 1, 0)
    depth = halves(depth)
    depth_high_ref[...] = depth[0]
    depth_low_ref[...] = depth[1]
    spread_into(message_ref, start_ref[...], *read_tables(tables_ref), depth, devices)


def transform_in(message_ref, forward_ref, block_high_ref, block_low_ref, rows_count, cols_count):
    gathered = jnp.concatenate(
        [
            jnp.concatenate(
                [
                    message_ref[(r * cols_count + c) * X_PAD : (r * cols_count + c + 1) * X_PAD]
                    for r in range(rows_count)
                ],
                axis=0,
            )
            for c in range(cols_count)
        ],
        axis=1,
    )
    high, low = halves(gathered)
    along = jnp.dot(
        forward_ref[...],
        jnp.concatenate([high, high, low], axis=0),
        preferred_element_type=jnp.float32,
    )
    part = along.shape[1] // cols_count // SPLIT
    along = jnp.concatenate(
        [
            jnp.concatenate(
                [
                    along[:, (c * SPLIT + half) * part : (c * SPLIT + half + 1) * part]
                    for c in range(cols_count)
                ],
                axis=1,
            )
            for half in range(SPLIT)
        ],
        axis=0,
    )
    return product(halves(along), (block_high_ref[...], block_low_ref[...]))


def transform_out(result_ref, values, backward_ref, block_high_ref, block_low_ref, counts):
    rows_count, cols_count = counts
    spread = product(halves(values), (block_high_ref[...], block_low_ref[...]))
    grid_x = spread.shape[0] // SPLIT
    part = spread.shape[1] // cols_count
    spread = jnp.concatenate(
        [
            spread[half * grid_x : (half + 1) * grid_x, c * part : (c + 1) * part]
            for c in range(cols_count)
            for half in range(SPLIT)
        ],
        axis=1,
    )
    high, low = halves(spread)
    along = jnp.dot(
        backward_ref[...],
        jnp.concatenate([high, high, low], axis=0),
        preferred_element_type=jnp.float32,
    )
    width = along.shape[1] // cols_count
    slot_rows = result_ref.shape[0] // (rows_count * cols_count)
    for r in range(rows_count):
        for c in range(cols_count):
            first = (r * cols_count + c) * slot_rows
            result_ref[first : first + X_PAD, :] = along[
                r * X_PAD : (r + 1) * X_PAD, c * width : (c + 1) * width
            ]


def middle_first_body(
    counts,
    position_ref,
    message_ref,
    kernel_ref,
    forward_ref,
    backward_ref,
    block_high_ref,
    block_low_ref,
    back_high_ref,
    back_low_ref,
    result_ref,
    wave_ref,
):
    wave = transform_in(message_ref, forward_ref, block_high_ref, block_low_ref, *counts)
    wave_ref[...] = wave
    transform_out(
        result_ref, wave * kernel_ref[0], backward_ref, back_high_ref, back_low_ref, counts
    )


def gather_rows(parts):
    tiles = [
        parts[GROUP * tile : GROUP * tile + GROUP, :] for tile in range(parts.shape[0] // GROUP)
    ]
    return jnp.concatenate(tiles, axis=1)[0 : 3 * RHS]


def row_total(value, rhs):
    row = lax.broadcasted_iota(jnp.int32, value.shape, 0)
    return total(jnp.where(lax.rem(row, RHS) == rhs, value, 0.0))


def total(value):
    return jnp.sum(jnp.sum(value, axis=0, keepdims=True), axis=1, keepdims=True)


def middle_second_body(
    counts,
    position_ref,
    message_ref,
    kernel_ref,
    forward_ref,
    backward_ref,
    block_high_ref,
    block_low_ref,
    back_high_ref,
    back_low_ref,
    wave_ref,
    rhs_ref,
    start_ref,
    image_ref,
    second_ref,
    near_ref,
    polar_ref,
    result_ref,
):
    rhs_rows = read_rows(rhs_ref)
    near_rows = gather_rows(near_ref)
    wave = transform_in(message_ref, forward_ref, block_high_ref, block_low_ref, *counts)
    filtered = wave * kernel_ref[0]
    transform_out(result_ref, filtered, backward_ref, back_high_ref, back_low_ref, counts)
    before = wave_ref[...]
    grid_y = CY * counts[1]
    lane = lax.broadcasted_iota(jnp.int32, wave.shape, 1)
    own_rhs = lax.rem(lax.div(lane, grid_y), RHS)
    second = second_ref[...]
    start = start_ref[...]
    image = image_ref[...]
    local_part = second / polar_ref[...] - near_rows - self_coef * second
    slot = lax.broadcasted_iota(jnp.int32, (1, result_ref.shape[1]), 1)
    sums = jnp.zeros((1, result_ref.shape[1]), jnp.float32)
    for rhs in range(RHS):
        mine = own_rhs == rhs
        parts = (
            row_total(rhs_rows * start, rhs),
            row_total(start * image, rhs),
            row_total(second * image, rhs),
            row_total(start * local_part, rhs) + total(jnp.where(mine, before * filtered, 0.0)),
            row_total(second * local_part, rhs) + total(jnp.where(mine, wave * filtered, 0.0)),
        )
        for index, part in enumerate(parts):
            sums = jnp.where(slot == rhs * len(parts) + index, part, sums)
    devices = counts[0] * counts[1]
    result_ref[pl.ds(X_PAD, devices, stride=X_PAD + 1), :] = jnp.broadcast_to(
        sums, (devices, sums.shape[1])
    )


def sample_body(
    devices,
    message_ref,
    tables_ref,
    depth_high_ref,
    depth_low_ref,
    start_ref,
    near_ref,
    polar_ref,
    image_ref,
    second_ref,
    payload_ref,
):
    tables = read_tables(tables_ref)
    depth = (depth_high_ref[...], depth_low_ref[...])
    field = sample_from(message_ref, *tables, depth, devices)
    start = start_ref[...]
    polar = polar_ref[...]
    image = start / polar - gather_rows(near_ref) + field - self_coef * start
    second = polar * image
    image_ref[...] = image
    second_ref[...] = second
    store_payload(payload_ref, second)


def spread_body(
    devices,
    tables_ref,
    depth_high_ref,
    depth_low_ref,
    second_ref,
    result_ref,
):
    depth = (depth_high_ref[...], depth_low_ref[...])
    spread_into(result_ref, second_ref[...], *read_tables(tables_ref), depth, devices)


def final_body(
    devices,
    message_ref,
    tables_ref,
    depth_high_ref,
    depth_low_ref,
    rhs_ref,
    start_ref,
    image_ref,
    second_ref,
    near_ref,
    polar_ref,
    dipole_ref,
    residual_ref,
):
    tables = read_tables(tables_ref)
    depth = (depth_high_ref[...], depth_low_ref[...])
    field = sample_from(message_ref, *tables, depth, devices)
    second = second_ref[...]
    start = start_ref[...]
    image = image_ref[...]
    image_second = second / polar_ref[...] - gather_rows(near_ref) + field - self_coef * second
    sums = jnp.sum(
        message_ref[pl.ds(X_PAD, devices, stride=X_PAD + 1), :], axis=0, keepdims=True
    )
    steps = []
    for rhs in range(RHS):
        progress, start_image, second_image, start_next, second_next = [
            sums[:, rhs * 5 + index : rhs * 5 + index + 1] for index in range(5)
        ]
        step = progress / start_image
        progress_next = progress - 2.0 * step * start_image + step * step * second_image
        grown = 1.0 + progress_next / progress
        curvature = (
            grown * grown * start_image
            - step * grown * (start_next + second_image)
            + step * step * second_next
        )
        steps.append((step, grown, progress_next / curvature))
    row = lax.broadcasted_iota(jnp.int32, (RHS, 1), 0)
    step, grown, step_next = [
        sum(jnp.where(row == rhs, steps[rhs][index], 0.0) for rhs in range(RHS))
        for index in range(3)
    ]
    for dim in range(3):
        rows = slice(dim * RHS, (dim + 1) * RHS)
        direction = grown * start[rows] - step * second[rows]
        image_direction = grown * image[rows] - step * image_second[rows]
        dipole_ref[dim] = step * start[rows] + step_next * direction
        residual_ref[dim] = rhs_ref[dim] - step * image[rows] - step_next * image_direction


def near_base(entry, brick_rows):
    return lax.shift_right_logical(entry, 2) * brick_rows + lax.bitwise_and(entry, 3)


def fill_near(scratch, up_ref, stack_ref, down_ref):
    rows = stack_ref.shape[0]
    scratch[0:rows, :] = up_ref[...]
    scratch[rows : 2 * rows, :] = stack_ref[...]
    scratch[2 * rows : 3 * rows, :] = down_ref[...]


def nearest(places, origin, span):
    return places - span * jnp.floor((places - origin) * (1.0 / span) + 0.5)


def unwrap_near(near, tile_count, spans):
    rows = near.shape[0] // 9
    for dim in range(2):
        own = 4 * rows + dim * tile_count
        origin = near[own : own + 1, 0:1]
        for brick in range(9):
            first = brick * rows + dim * tile_count
            near[first : first + tile_count, :] = nearest(
                near[first : first + tile_count, :], origin, spans[dim]
            )


def pick_rows(picked, near, lists_ref, tile, tile_count, quantities, origin, span):
    rows = near.shape[0] // 9
    for entry in range(lists_ref.shape[1]):
        base = near_base(lists_ref[tile, entry], rows)
        for quantity in range(quantities):
            values = near[pl.ds(base + quantity * tile_count, 1), :]
            if quantity == 2 and span is not None:
                values = nearest(values, origin, span)
            first = (entry * quantities + quantity) * GROUP
            picked[first : first + GROUP, :] = jnp.broadcast_to(values, (GROUP, TILE))


def widen_own(near, quantities, tile_count, tile, square, wide):
    offset = near.shape[0] // 9 * 4
    for quantity in range(quantities):
        square[quantity : quantity + 1, :] = near[
            pl.ds(offset + quantity * tile_count + tile, 1), :
        ]
    columns = jnp.transpose(square[...])
    for quantity in range(quantities):
        wide[quantity * TILE : (quantity + 1) * TILE, :] = jnp.broadcast_to(
            columns[:, quantity : quantity + 1], (TILE, TILE)
        )


def add_field(sums, first_term, second_term, apart, moments):
    for rhs in range(RHS):
        moment = [moments[RHS * dim + rhs] for dim in range(3)]
        projected = moment[0] * apart[0] + moment[1] * apart[1] + moment[2] * apart[2]
        weighted = second_term * projected
        for dim in range(3):
            index = RHS * dim + rhs
            sums[index] = sums[index] + (weighted * apart[dim] - first_term * moment[dim])


def finish_sums(field_ref, sums_ref):
    lane = lax.broadcasted_iota(jnp.int32, (TILE, TILE), 1)
    merged = jnp.zeros((TILE, TILE), jnp.float32)
    for index in range(3 * RHS):
        column = jnp.sum(sums_ref[index * TILE : (index + 1) * TILE, :], axis=1, keepdims=True)
        merged = jnp.where(lane == index, column, merged)
    field_ref[...] = jnp.transpose(merged)[0:GROUP]


def pair_rows(start, group):
    return pl.ds(pl.multiple_of(start + group * GROUP, GROUP), GROUP)


def wide_rows(start, group, quantity):
    return pl.ds(pl.multiple_of(quantity * TILE + start + group * GROUP, GROUP), GROUP)


def pair_terms(square_dist, damp):
    inverse = lax.rsqrt(square_dist)
    distance = square_dist * inverse
    inverse_sq = inverse * inverse
    inverse_cube = inverse_sq * inverse
    cubed = damp * (distance * square_dist)
    damping = jnp.exp(cubed)
    bell = jnp.exp(-(ewald_beta * ewald_beta) * square_dist)
    stretched = 1.0 + (SCREEN_SCALE * ewald_beta) * distance
    turned = pl.reciprocal(stretched, approx=True)
    turned = turned * (2.0 - stretched * turned)
    series = SCREEN_COEF[-1] * turned + SCREEN_COEF[-2]
    for coef in SCREEN_COEF[-3::-1]:
        series = series * turned + coef
    screen = bell * turned * series
    gaussian = (2.0 * ewald_beta / math.sqrt(math.pi)) * bell
    bare = screen - damping
    first_term = bare * inverse_cube + gaussian * inverse_sq
    second_term = (
        3.0 * (first_term + (cubed * damping) * inverse_cube)
        + (2.0 * ewald_beta * ewald_beta) * gaussian
    ) * inverse_sq
    return first_term, second_term


def pair_first_body(
    first_tile,
    tile_count,
    spans,
    lists_ref,
    up_ref,
    stack_ref,
    down_ref,
    *others,
):
    first_ref, second_ref, field_ref, near_ref, near, picked, square, wide, sums_ref = others[-9:]

    @pl.when(pl.program_id(0) == 0)
    def _():
        fill_near(near, up_ref, stack_ref, down_ref)
        unwrap_near(near, tile_count, spans)
        square[...] = jnp.zeros_like(square)
        rows = near.shape[0] // 9
        kept = 3 * tile_count
        for brick in range(9):
            near_ref[brick * kept : (brick + 1) * kept, :] = near[
                brick * rows : brick * rows + kept, :
            ]

    tile = first_tile + pl.program_id(0)
    quantities = near.shape[0] // 9 // tile_count
    widen_own(near, 4, tile_count, tile, square, wide)
    origin = wide[2 * TILE : 2 * TILE + 1, 0:1]
    pick_rows(picked, near, lists_ref, tile, tile_count, quantities, origin, spans[2])

    @pl.loop(0, TILE // PAIR_ROWS)
    def _(part):
        start = part * PAIR_ROWS
        for group in range(PAIR_ROWS // GROUP):
            own = [wide[wide_rows(start, group, dim), :] for dim in range(4)]
            own_damp = -thole_a * own[3]
            sums = [jnp.zeros((GROUP, TILE), jnp.float32) for _ in range(3 * RHS)]
            itself = (
                lax.broadcasted_iota(jnp.int32, (GROUP, TILE), 0) + (start + group * GROUP)
            ) == lax.broadcasted_iota(jnp.int32, (GROUP, TILE), 1)
            for entry in range(lists_ref.shape[1]):
                first = entry * quantities * GROUP
                rows = [
                    picked[first + quantity * GROUP : first + (quantity + 1) * GROUP, :]
                    for quantity in range(quantities)
                ]
                apart = [rows[dim] - own[dim] for dim in range(3)]
                square_dist = apart[0] * apart[0] + apart[1] * apart[1] + apart[2] * apart[2]
                if entry == 0:
                    square_dist = jnp.where(itself, 1.0, square_dist)
                first_term, second_term = pair_terms(square_dist, own_damp * rows[3])
                if entry == 0:
                    first_term = jnp.where(itself, 0.0, first_term)
                    second_term = jnp.where(itself, 0.0, second_term)
                place = wide_rows(start, group, entry)
                first_ref[place, :] = first_term
                second_ref[place, :] = second_term
                add_field(sums, first_term, second_term, apart, rows[4:])
            for index, value in enumerate(sums):
                sums_ref[wide_rows(start, group, index), :] = value

    finish_sums(field_ref, sums_ref)


def pair_second_body(
    tile_count,
    spans,
    lists_ref,
    near,
    up_ref,
    stack_ref,
    down_ref,
    first_ref,
    second_ref,
    field_ref,
    near_moment,
    picked,
    picked_moment,
    square,
    wide,
    sums_ref,
):
    @pl.when(pl.program_id(0) == 0)
    def _():
        fill_near(near_moment, up_ref, stack_ref, down_ref)
        square[...] = jnp.zeros_like(square)

    tile = pl.program_id(0)
    widen_own(near, 3, tile_count, tile, square, wide)
    origin = wide[2 * TILE : 2 * TILE + 1, 0:1]
    pick_rows(picked, near, lists_ref, tile, tile_count, 3, origin, spans[2])
    pick_rows(picked_moment, near_moment, lists_ref, tile, tile_count, 3 * RHS, None, None)

    @pl.loop(0, TILE // PAIR_ROWS)
    def _(part):
        start = part * PAIR_ROWS
        for group in range(PAIR_ROWS // GROUP):
            own = [wide[wide_rows(start, group, dim), :] for dim in range(3)]
            sums = [jnp.zeros((GROUP, TILE), jnp.float32) for _ in range(3 * RHS)]
            for entry in range(lists_ref.shape[1]):
                first = entry * 3 * GROUP
                apart = [
                    picked[first + dim * GROUP : first + (dim + 1) * GROUP, :] - own[dim]
                    for dim in range(3)
                ]
                first = first * RHS
                moments = [
                    picked_moment[first + index * GROUP : first + (index + 1) * GROUP, :]
                    for index in range(3 * RHS)
                ]
                place = wide_rows(start, group, entry)
                add_field(sums, first_ref[place, :], second_ref[place, :], apart, moments)
            for index, value in enumerate(sums):
                sums_ref[wide_rows(start, group, index), :] = value

    finish_sums(field_ref, sums_ref)


def shift(source, axis, step):
    count = lax.axis_size(axis)
    return lax.ppermute(source, axis, [(i, (i + step) % count) for i in range(count)])


def both_ways(source, axis):
    return shift(source, axis, 1), source, shift(source, axis, -1)


def whole(shape):
    return pl.BlockSpec(shape, lambda *_: (0,) * len(shape))


def anywhere():
    return pl.BlockSpec(memory_space=pl.ANY)


def join(message, payload):
    left, _, right = both_ways(payload, "col")
    stack_shape = (3 * payload.shape[0], payload.shape[1])
    message, stack = pl.pallas_call(
        join_body,
        grid=(1,),
        in_specs=[anywhere()] + [whole(payload.shape)] * 3,
        out_specs=[anywhere(), whole(stack_shape)],
        out_shape=[
            jax.ShapeDtypeStruct(message.shape, message.dtype),
            jax.ShapeDtypeStruct(stack_shape, payload.dtype),
        ],
        input_output_aliases={0: 0},
        compiler_params=pltpu.CompilerParams(vmem_limit_bytes=VMEM_LIMIT),
    )(message, left, payload, right)
    return message, both_ways(stack, "row")


def call(body, outs, *operands, after=(), vmem=VMEM_LIMIT):
    def run(*refs):
        body(*refs[len(after) :])

    return pl.pallas_call(
        run,
        grid=(1,),
        in_specs=[anywhere()] * len(after) + [whole(operand.shape) for operand in operands],
        out_specs=[whole(shape) for shape, _ in outs],
        out_shape=[jax.ShapeDtypeStruct(shape, dtype) for shape, dtype in outs],
        compiler_params=pltpu.CompilerParams(vmem_limit_bytes=vmem),
        cost_estimate=pl.CostEstimate(
            flops=200_000_000, bytes_accessed=4 << 20, transcendentals=0
        ),
    )(*after, *operands)


def middle_call(body, outs, position, message, kernel, *operands, after=()):
    def run(position_ref, *refs):
        body(position_ref, *refs[len(after) :])

    return pl.pallas_call(
        run,
        grid_spec=pltpu.PrefetchScalarGridSpec(
            num_scalar_prefetch=1,
            grid=(1,),
            in_specs=[anywhere()] * len(after)
            + [whole(message.shape)]
            + [pl.BlockSpec((1,) + kernel.shape[1:], lambda i, s: (s[0], 0, 0))]
            + [whole(operand.shape) for operand in operands],
            out_specs=[whole(shape) for shape in outs],
        ),
        out_shape=[jax.ShapeDtypeStruct(shape, jnp.float32) for shape in outs],
        compiler_params=pltpu.CompilerParams(vmem_limit_bytes=VMEM_LIMIT),
        cost_estimate=pl.CostEstimate(
            flops=200_000_000, bytes_accessed=4 << 20, transcendentals=0
        ),
    )(position, *after, message, kernel, *operands)


def pair_call(body, outs, kept, first_tile, last_tile, blocked, scratch, lists, *operands, after=()):
    tiles = lists.shape[0]

    def block(operand):
        rows = operand.shape[0] // tiles
        return pl.BlockSpec((rows, operand.shape[1]), lambda i, s: (first_tile + i, 0))

    out_shape = [jax.ShapeDtypeStruct(shape, jnp.float32) for shape in outs + kept]
    plain = len(operands) - blocked
    aliases = {}
    if first_tile > 0:
        first = 1 + len(operands) + len(after) - len(outs)
        aliases = {first + index: index for index in range(len(outs))}
    return pl.pallas_call(
        body,
        out_shape=out_shape,
        grid_spec=pltpu.PrefetchScalarGridSpec(
            num_scalar_prefetch=1,
            grid=(last_tile - first_tile,),
            in_specs=[whole(operand.shape) for operand in operands[:plain]]
            + [block(operand) for operand in operands[plain:]]
            + [anywhere()] * len(after),
            out_specs=[block(shape) for shape in out_shape[: len(outs)]]
            + [whole(shape) for shape in kept],
            scratch_shapes=[pltpu.VMEM(shape, jnp.float32) for shape in scratch],
        ),
        input_output_aliases=aliases,
        compiler_params=pltpu.CompilerParams(vmem_limit_bytes=VMEM_LIMIT),
        cost_estimate=pl.CostEstimate(
            flops=80_000_000, bytes_accessed=8 << 20, transcendentals=1 << 21
        ),
    )(lists, *operands, *after)


def exchange(message, devices):
    shape = message.shape
    sent = message.reshape(devices, 1, -1)
    return lax.all_to_all(sent, ("row", "col"), split_axis=0, concat_axis=0, tiled=True).reshape(
        shape
    )


def slab_local(field_rhs, positions, polar, grid_base, tile_lists):
    rows_count = lax.axis_size("row")
    cols_count = lax.axis_size("col")
    counts = (rows_count, cols_count)
    devices = rows_count * cols_count
    lengths = (CX * rows_count, CY * cols_count, KZ)
    spans = tuple(float(length) for length in lengths)
    atoms = polar.shape[-1]
    tile_count = atoms // TILE
    listed = tile_lists.shape[-1]
    tables = slab_tables(rows_count, cols_count)
    f32 = jnp.float32
    rhs = jnp.swapaxes(field_rhs[0, 0], 0, 1)
    place = jnp.swapaxes(positions[0], 0, 1)
    base = jnp.swapaxes(grid_base[0], 0, 1)
    polar = polar.reshape(1, atoms)
    lists = tile_lists[0, 0]
    quantities = 4 + 3 * RHS
    brick_rows = quantities * tile_count
    moment_rows = 3 * RHS * tile_count
    message_shape = (devices * X_PAD, KZ // devices * RHS * Y_PAD)
    last_shape = (devices * (X_PAD + 1), message_shape[1])
    row_shape = (3 * RHS, atoms)
    square = (TILE, TILE)
    wide = (4 * TILE, TILE)
    sums = (3 * RHS * TILE, TILE)

    start, payload = call(pack_body, [(row_shape, f32), ((brick_rows, TILE), f32)], rhs, place, polar)

    def setup(*refs):
        setup_body(lengths, devices, *refs)

    message, splines, depth_high, depth_low = call(
        setup,
        [
            (message_shape, f32),
            ((2 * SLOT_ROWS + 2 * Y_PAD, atoms), f32),
            ((KZ, 2 * atoms), jnp.bfloat16),
            ((KZ, 2 * atoms), jnp.bfloat16),
        ],
        place,
        base,
        start,
        *[jnp.asarray(table) for table in tables["along_z"]],
    )
    position = (lax.axis_index("row") * cols_count + lax.axis_index("col")).reshape(1)
    constants = (
        jnp.asarray(tables["kernel"]),
        jnp.asarray(tables["forward_x"]),
        jnp.asarray(tables["backward_x"]),
        *[jnp.asarray(table) for table in tables["block"]],
        *[jnp.asarray(table) for table in tables["block_back"]],
    )
    message, near = join(message, payload)
    arrived = exchange(message, devices)

    def pair_first(first_tile, last_tile, *after):
        def body(*refs):
            pair_first_body(first_tile, tile_count, spans, *refs)

        return pair_call(
            body,
            [(tile_count * listed * TILE, TILE)] * 2 + [(tile_count * GROUP, TILE)],
            [(9 * 3 * tile_count, TILE)],
            first_tile,
            last_tile,
            0,
            [(9 * brick_rows, TILE), (listed * quantities * GROUP, TILE), square, wide, sums],
            lists,
            *near,
            after=after,
        )

    early = pair_first(0, EARLY_TILES, message)

    def middle_first(*refs):
        middle_first_body(counts, *refs)

    mixed, wave = middle_call(
        middle_first,
        [message_shape, tables["kernel"].shape[1:]],
        position,
        arrived,
        *constants,
        after=(early[2],),
    )
    returned = exchange(mixed, devices)
    first_term, second_term, direct, near = pair_first(EARLY_TILES, tile_count, wave, *early[:3])

    def sample(*refs):
        sample_body(devices, *refs)

    image, second, moments = call(
        sample,
        [(row_shape, f32), (row_shape, f32), ((moment_rows, TILE), f32)],
        returned,
        splines,
        depth_high,
        depth_low,
        start,
        direct,
        polar,
    )

    def spread(*refs):
        spread_body(devices, *refs)

    (message,) = call(spread, [(message_shape, f32)], splines, depth_high, depth_low, second)
    message, near_moments = join(message, moments)
    arrived = exchange(message, devices)

    def pair_second(*refs):
        pair_second_body(tile_count, spans, *refs)

    (direct,) = pair_call(
        pair_second,
        [(tile_count * GROUP, TILE)],
        [],
        0,
        tile_count,
        2,
        [
            (9 * moment_rows, TILE),
            (listed * 3 * GROUP, TILE),
            (listed * 3 * RHS * GROUP, TILE),
            square,
            wide,
            sums,
        ],
        lists,
        near,
        *near_moments,
        first_term,
        second_term,
    )

    def middle_second(*refs):
        middle_second_body(counts, *refs)

    (mixed,) = middle_call(
        middle_second,
        [last_shape],
        position,
        arrived,
        *constants,
        wave,
        rhs,
        start,
        image,
        second,
        direct,
        polar,
    )
    returned = exchange(mixed, devices)

    def final(*refs):
        final_body(devices, *refs)

    outs = call(
        final,
        [(rhs.shape, f32), (rhs.shape, f32)],
        returned,
        splines,
        depth_high,
        depth_low,
        rhs,
        start,
        image,
        second,
        direct,
        polar,
        vmem=FINAL_VMEM_LIMIT,
    )
    return tuple(jnp.swapaxes(out, 0, 1)[None, None] for out in outs)


def solution(mesh):
    placed = (
        P("row", "col", None, None, None),
        P("row", "col", None, None),
        P("row", "col", None),
        P("row", "col", None, None),
        P("row", "col", None, None),
    )
    devices = mesh.shape["row"] * mesh.shape["col"]
    return jax.shard_map(
        slab_local if KZ % devices == 0 else pencil_local,
        mesh=mesh,
        in_specs=placed,
        out_specs=(P("row", "col", None, None, None), P("row", "col", None, None, None)),
        check_vma=False,
    )
```

```python
import math

import jax
import jax.numpy as jnp
import ml_dtypes
import numpy as np
from jax import lax
from jax.experimental import pallas as pl
from jax.experimental.pallas import tpu as pltpu
from jax.sharding import PartitionSpec as P

CX = 8
CY = 4
KZ = 256
TILE = 128
RHS = 2
ITERS = 2


ewald_beta = 0.4
thole_a = 0.39
self_coef = 4.0 * ewald_beta**3 / (3.0 * math.sqrt(math.pi))
highest = lax.Precision.HIGHEST


def with_halo(cells, sides, width):
    for axis, dim in sides:
        count = lax.axis_size(axis)
        head = lax.slice_in_dim(cells, 0, width, axis=dim)
        tail = lax.slice_in_dim(cells, cells.shape[dim] - width, cells.shape[dim], axis=dim)
        cells = jnp.concatenate(
            [
                lax.ppermute(tail, axis, [(i, (i + 1) % count) for i in range(count)]),
                cells,
                lax.ppermute(head, axis, [((i + 1) % count, i) for i in range(count)]),
            ],
            axis=dim,
        )
    return cells


def spline_table(fraction):
    previous = {0: jnp.ones_like(fraction)}
    fourth = previous
    for degree in range(2, 6):
        current = {}
        for offset in range(degree):
            abscissa = fraction + offset
            summed = abscissa * previous.get(offset, 0.0) + (degree - abscissa) * previous.get(
                offset - 1, 0.0
            )
            current[offset] = summed / (degree - 1)
        if degree == 4:
            fourth = current
        previous = current
    values = jnp.stack([previous[4 - stencil] for stencil in range(5)])
    slopes = jnp.stack(
        [fourth.get(4 - stencil, 0.0) - fourth.get(3 - stencil, 0.0) for stencil in range(5)]
    )
    return (values, slopes)


def spline_modulus(wave_index, length):
    spline_coef = (1.0 / 24.0, 11.0 / 24.0, 11.0 / 24.0, 1.0 / 24.0)
    cosine_sum = jnp.zeros(wave_index.shape, jnp.float32)
    sine_sum = jnp.zeros(wave_index.shape, jnp.float32)
    for offset in range(4):
        angles = 2.0 * math.pi / length * (wave_index * offset % length).astype(jnp.float32)
        cosine_sum = cosine_sum + spline_coef[offset] * jnp.cos(angles)
        sine_sum = sine_sum + spline_coef[offset] * jnp.sin(angles)
    return cosine_sum * cosine_sum + sine_sum * sine_sum


def folded_square(wave_index, length):
    nearest = jnp.minimum(wave_index, length - wave_index).astype(jnp.float32) / length
    return nearest * nearest


def influence(wave_x, wave_y, wave_z, length_x, length_y, length_z):
    wave_norm = (
        folded_square(wave_x, length_x)
        + folded_square(wave_y, length_y)
        + folded_square(wave_z, length_z)
    )
    modulus = (
        spline_modulus(wave_x, length_x)
        * spline_modulus(wave_y, length_y)
        * spline_modulus(wave_z, length_z)
    )
    excluded = (wave_x * 2 == length_x) | (wave_y * 2 == length_y) | (wave_z * 2 == length_z)
    excluded = excluded | (wave_x == 0) & (wave_y == 0) & (wave_z == 0)
    safe_norm = jnp.where(excluded, 1.0, wave_norm)
    safe_modulus = jnp.where(excluded, 1.0, modulus)
    result = jnp.exp(-(math.pi**2 / ewald_beta**2) * safe_norm) / (
        math.pi * safe_norm * safe_modulus
    )
    return jnp.where(excluded, 0.0, result)


def tile_field(own_static, near_static, near_dipole, box_spans):
    listed_count = near_static.shape[0]
    tile_width = own_static.shape[1]
    box_span = jnp.array(box_spans, dtype=jnp.float32)[None, :, None, None]
    separation = near_static[:, 0:3, None, :] - own_static[None, 0:3, :, None]
    separation = separation - box_span * jnp.floor(separation / box_span + 0.5)
    dist_sq = jnp.sum(separation * separation, axis=1)
    itself = (jnp.arange(listed_count)[:, None, None] == 0) & (
        jnp.arange(tile_width)[:, None] == jnp.arange(tile_width)[None, :]
    )[None]
    safe_sq = jnp.where(itself, 1.0, dist_sq)
    distance = jnp.sqrt(safe_sq)
    scaled = distance / (own_static[3][None, :, None] * near_static[:, 3][:, None, :])
    cubed = thole_a * scaled * scaled * scaled
    damping = jnp.exp(-cubed)
    screen = lax.erfc(ewald_beta * distance)
    gaussian = 2.0 * ewald_beta / math.sqrt(math.pi) * jnp.exp(-(ewald_beta * ewald_beta) * safe_sq)
    inverse_sq = 1.0 / safe_sq
    inverse_cube = inverse_sq / distance
    first_term = (screen - damping) * inverse_cube + gaussian * inverse_sq
    second = (
        3.0 * (screen - (1.0 + cubed) * damping) * inverse_cube * inverse_sq
        + gaussian * (2.0 * ewald_beta * ewald_beta + 3.0 * inverse_sq) * inverse_sq
    )
    first_term = jnp.where(itself, 0.0, first_term)
    second = jnp.where(itself, 0.0, second)
    projected = jnp.sum(near_dipole[:, :, :, None, :] * separation[:, None, :, :, :], axis=2)
    weighted = second[:, None] * projected
    outward = jnp.sum(weighted[:, :, None] * separation[:, None], axis=(0, 4))
    inward = jnp.sum(first_term[:, None, None] * near_dipole[:, :, :, None, :], axis=(0, 4))
    return outward - inward


def hartley(length):
    counter = jnp.arange(length, dtype=jnp.int32)
    angles = (
        2.0 * math.pi / length * (counter[:, None] * counter[None, :] % length).astype(jnp.float32)
    )
    return jnp.cos(angles) + jnp.sin(angles)


def placed_table(first_cell, weights, extent):
    slot_index = jnp.arange(extent, dtype=jnp.int32)[:, None]
    placed = jnp.zeros((extent, first_cell.shape[0]), jnp.float32)
    for stencil in range(5):
        placed = placed + jnp.where(
            slot_index == (first_cell[None, :] + stencil) % extent, weights[stencil][None, :], 0.0
        )
    return placed


def pad_axis(source, axis_pos, leading, trailing):
    widths = [(0, 0)] * source.ndim
    widths[axis_pos] = (leading, trailing)
    return jnp.pad(source, widths)


def fold_cycle(cycle_only, axis_pos, inner_len):
    middle = lax.slice_in_dim(cycle_only, 4, inner_len + 4, axis=axis_pos)
    lower_cycle = lax.slice_in_dim(cycle_only, 0, 2, axis=axis_pos)
    upper_cycle = lax.slice_in_dim(cycle_only, inner_len + 6, inner_len + 8, axis=axis_pos)
    return (
        middle
        + pad_axis(lower_cycle, axis_pos, 0, inner_len - 2)
        + pad_axis(upper_cycle, axis_pos, inner_len - 2, 0)
    )


def clear_inside(extended, extents):
    inside = None
    for axis_pos, inner_len in extents:
        slot_index = lax.broadcasted_iota(jnp.int32, extended.shape, axis_pos)
        within = (slot_index >= 2) & (slot_index < inner_len + 6)
        inside = within if inside is None else inside & within
    return jnp.where(inside, 0.0, extended)


def inner_sum(left_arr, right_arr):
    return lax.psum(jnp.sum(left_arr * right_arr, axis=(1, 2)), ("row", "col"))


def pencil_local(field_rhs, positions, polar, grid_base, tile_lists):
    rows_count = lax.axis_size("row")
    cols_count = lax.axis_size("col")
    grid_x = CX * rows_count
    grid_y = CY * cols_count
    atom_count = polar.shape[-1]
    tile_count = atom_count // TILE
    slab_depth = KZ // tile_count
    window_len = slab_depth + 4
    box_spans = (float(grid_x), float(grid_y), float(KZ))
    own_place = positions[0, 0]
    own_base = grid_base[0, 0]
    own_polar = polar[0, 0]
    lengths = jnp.array([grid_x, grid_y, KZ], dtype=jnp.int32)[:, None]
    cell_index = (own_base + 2) % lengths
    fraction = own_place - cell_index.astype(jnp.float32)
    values, slopes = spline_table(fraction)
    first_x = (own_base[0] - lax.axis_index("row") * CX + 2) % grid_x
    first_y = (own_base[1] - lax.axis_index("col") * CY + 2) % grid_y
    rows_x = placed_table(first_x, values[:, 0], CX + 4)
    slope_x = placed_table(first_x, slopes[:, 0], CX + 4)
    rows_y = placed_table(first_y, values[:, 1], CY + 4)
    slope_y = placed_table(first_y, slopes[:, 1], CY + 4)
    tile_start = jnp.arange(atom_count, dtype=jnp.int32) // TILE * slab_depth
    first_z = (own_base[2] + 2 - tile_start) % KZ
    rows_z = placed_table(first_z, values[:, 2], window_len)
    slope_z = placed_table(first_z, slopes[:, 2], window_len)
    plane_count = (CX + 4) * (CY + 4)
    plane_dx = (slope_x[:, None, :] * rows_y[None, :, :]).reshape(plane_count, atom_count)
    plane_dy = (rows_x[:, None, :] * slope_y[None, :, :]).reshape(plane_count, atom_count)
    plane_flat = (rows_x[:, None, :] * rows_y[None, :, :]).reshape(plane_count, atom_count)
    window_rows = jnp.moveaxis(rows_z.reshape(window_len, tile_count, TILE), 1, 0)
    window_slope = jnp.moveaxis(slope_z.reshape(window_len, tile_count, TILE), 1, 0)
    depth_table = jnp.concatenate([window_rows, window_slope], axis=2)
    grid_scale = 1.0 / (grid_x * grid_y * KZ)
    hartley_x = hartley(grid_x)
    hartley_y = hartley(grid_y)
    hartley_z = hartley(KZ)
    block_y = grid_y // rows_count
    block_z = KZ // cols_count
    wave_x = jnp.arange(grid_x, dtype=jnp.int32)[:, None, None]
    wave_y = (lax.axis_index("row") * block_y + jnp.arange(block_y, dtype=jnp.int32))[None, :, None]
    wave_z = (lax.axis_index("col") * block_z + jnp.arange(block_z, dtype=jnp.int32))[None, None, :]
    kernel = influence(wave_x, wave_y, wave_z, grid_x, grid_y, KZ) * grid_scale
    root_scale = jnp.power(own_polar, 1.0 / 6.0)
    own_static = jnp.concatenate([own_place, root_scale[None]], axis=0)
    near_static = with_halo(own_static[None, None], (("row", 0), ("col", 1)), 1)
    near_static = jnp.moveaxis(near_static.reshape(9, 4, tile_count, TILE), 2, 1).reshape(
        9 * tile_count, 4, TILE
    )
    own_tiles = jnp.moveaxis(own_static.reshape(4, tile_count, TILE), 1, 0)
    own_lists = tile_lists[0, 0]
    polar_wide = own_polar[None, None, :]
    solution = jnp.zeros_like(field_rhs[0, 0])
    residual = field_rhs[0, 0]
    scaled_res = polar_wide * residual
    direction = scaled_res
    progress = inner_sum(residual, scaled_res)
    for iteration in range(ITERS):
        near_dip = with_halo(direction[None, None], (("row", 0), ("col", 1)), 1)
        near_dip = jnp.moveaxis(near_dip.reshape(9, RHS, 3, tile_count, TILE), 3, 1).reshape(
            9 * tile_count, RHS, 3, TILE
        )

        def one_tile(tile_pos):
            picked = own_lists[tile_pos]
            return tile_field(own_tiles[tile_pos], near_static[picked], near_dip[picked], box_spans)

        fields = lax.map(one_tile, jnp.arange(tile_count, dtype=jnp.int32))
        direct = jnp.moveaxis(fields, 0, 2).reshape(RHS, 3, atom_count)
        slope_terms = (
            direction[:, 0, None, :] * plane_dx[None] + direction[:, 1, None, :] * plane_dy[None]
        )
        flat_terms = direction[:, 2, None, :] * plane_flat[None]
        spread_left = jnp.concatenate(
            [
                slope_terms.reshape(RHS, plane_count, tile_count, TILE),
                flat_terms.reshape(RHS, plane_count, tile_count, TILE),
            ],
            axis=3,
        )
        spread_windows = jnp.einsum("sptb,twb->sptw", spread_left, depth_table, precision=highest)
        main_part = spread_windows[..., :slab_depth].reshape(spread_windows.shape[:-2] + (KZ,))
        tail_part = pad_axis(
            spread_windows[..., slab_depth:], spread_windows.ndim - 1, 0, slab_depth - 4
        )
        tail_part = tail_part.reshape(spread_windows.shape[:-2] + (KZ,))[..., : KZ + 4 - slab_depth]
        last_axis = main_part.ndim - 1
        padded_line = pad_axis(main_part, last_axis, 0, 4) + pad_axis(
            tail_part, last_axis, slab_depth, 0
        )
        inner = padded_line[..., 2 : KZ + 2]
        spread_tile = (
            inner
            + pad_axis(padded_line[..., 0:2], last_axis, KZ - 2, 0)
            + pad_axis(padded_line[..., KZ + 2 : KZ + 4], last_axis, 0, KZ - 2)
        ).reshape(RHS, CX + 4, CY + 4, KZ)
        extended = with_halo(spread_tile, (("row", 1), ("col", 2)), 2)
        cycle_only = clear_inside(extended, ((1, CX), (2, CY)))
        folded = fold_cycle(fold_cycle(cycle_only, 1, CX), 2, CY)
        spectrum = jnp.einsum(
            "sxyz,zk->sxyk",
            spread_tile[:, 2 : CX + 2, 2 : CY + 2] + folded,
            hartley_z,
            precision=highest,
        )
        along_y = jnp.einsum(
            "sxyz,yk->sxkz",
            lax.all_to_all(spectrum, "col", split_axis=3, concat_axis=2, tiled=True),
            hartley_y,
            precision=highest,
        )
        along_x = (
            jnp.einsum(
                "sxyz,xk->skyz",
                lax.all_to_all(along_y, "row", split_axis=2, concat_axis=1, tiled=True),
                hartley_x,
                precision=highest,
            )
            * kernel[None]
        )
        mixed_part = jnp.einsum("sxyz,xk->skyz", along_x, hartley_x, precision=highest)
        returned = lax.all_to_all(mixed_part, "row", split_axis=1, concat_axis=2, tiled=True)
        swapped = jnp.einsum("sxyz,yk->sxkz", returned, hartley_y, precision=highest)
        restored = lax.all_to_all(swapped, "col", split_axis=2, concat_axis=3, tiled=True)
        padded = with_halo(
            jnp.einsum("sxyz,zk->sxyk", restored, hartley_z, precision=highest),
            (("row", 1), ("col", 2)),
            2,
        )
        line = padded.reshape(RHS, plane_count, KZ)
        extended_line = jnp.concatenate([line[..., KZ - 2 :], line, line[..., :2]], axis=-1)
        windows = jnp.stack(
            [
                extended_line[..., tile * slab_depth : tile * slab_depth + window_len]
                for tile in range(tile_count)
            ],
            axis=-2,
        )
        sampled = jnp.einsum("sptw,twb->sptb", windows, depth_table, precision=highest)
        with_flat = sampled[..., :TILE].reshape(RHS, plane_count, atom_count)
        with_slope = sampled[..., TILE:].reshape(RHS, plane_count, atom_count)
        recip_part = jnp.stack(
            [
                jnp.sum(with_flat * plane_dx[None], axis=1),
                jnp.sum(with_flat * plane_dy[None], axis=1),
                jnp.sum(with_slope * plane_flat[None], axis=1),
            ],
            axis=1,
        )
        image_field = direction / polar_wide - direct + recip_part - self_coef * direction
        step_size = (progress / inner_sum(direction, image_field))[:, None, None]
        solution = solution + step_size * direction
        residual = residual - step_size * image_field
        scaled_res = polar_wide * residual
        progress_next = inner_sum(residual, scaled_res)
        direction = scaled_res + (progress_next / progress)[:, None, None] * direction
        progress = progress_next
    return (solution[None, None], residual[None, None])


X_PAD = CX + 4
Y_PAD = CY + 4
SLOT_ROWS = 16
SPLIT = 2
VMEM_LIMIT = 60_000_000
SMALL_VMEM_LIMIT = 24_000_000
EARLY_TILES = 1
PAIR_ROWS = 32
GROUP = 8
SCREEN_SCALE = 0.4
SCREEN_COEF = (
    0.22567588090896606,
    0.2256690263748169,
    0.20785020291805267,
    0.16849851608276367,
    0.14156343042850494,
    -0.005832736846059561,
    0.16930203139781952,
    -0.1830107867717743,
    0.05028456076979637,
)


def halves(value):
    high = value.astype(jnp.bfloat16)
    return high, (value - high.astype(jnp.float32)).astype(jnp.bfloat16)


def halves_np(value):
    value = value.astype(np.float32)
    high = value.astype(ml_dtypes.bfloat16)
    return high, (value - high.astype(np.float32)).astype(ml_dtypes.bfloat16)


def product(left, right, left_dim=1, right_dim=0):
    def one(first, second):
        return lax.dot_general(
            first,
            second,
            (((left_dim,), (right_dim,)), ((), ())),
            preferred_element_type=jnp.float32,
        )

    return one(left[0], right[0]) + (one(left[1], right[0]) + one(left[0], right[1]))


def cas_np(wave, place, length):
    angles = 2.0 * np.pi / length * (wave[:, None] * place[None, :] % length)
    return np.cos(angles) + np.sin(angles)


def modulus_np(wave, length):
    coef = np.array([1.0, 11.0, 11.0, 1.0]) / 24.0
    angles = 2.0 * np.pi / length * (wave[:, None] * np.arange(4)[None, :])
    return (coef * np.cos(angles)).sum(1) ** 2 + (coef * np.sin(angles)).sum(1) ** 2


def influence_np(length_x, length_y, length_z):
    total = np.zeros((length_x, length_y, length_z))
    modulus = np.ones((length_x, length_y, length_z))
    excluded = np.zeros((length_x, length_y, length_z), bool)
    for axis, length in enumerate((length_x, length_y, length_z)):
        wave = np.arange(length)
        shape = [1, 1, 1]
        shape[axis] = length
        total = total + ((np.minimum(wave, length - wave) / length) ** 2).reshape(shape)
        modulus = modulus * modulus_np(wave, length).reshape(shape)
        excluded = excluded | (wave * 2 == length).reshape(shape)
    excluded[0, 0, 0] = True
    safe = np.where(excluded, 1.0, total)
    result = np.exp(-(np.pi**2) / ewald_beta**2 * safe) / (
        np.pi * safe * np.where(excluded, 1.0, modulus)
    )
    return np.where(excluded, 0.0, result) / (length_x * length_y * length_z)


def slab_tables(rows_count, cols_count):
    grid_x = CX * rows_count
    grid_y = CY * cols_count
    devices = rows_count * cols_count
    chunk = KZ // devices
    wave_z = (np.arange(devices)[None, :] * chunk + np.arange(chunk)[:, None]).reshape(-1)
    along_z = cas_np(wave_z, np.arange(KZ), KZ)
    place_x = np.arange(rows_count)[:, None] * CX + np.arange(X_PAD)[None, :] - 2
    along_x = cas_np(np.arange(grid_x), place_x.reshape(-1) % grid_x, grid_x)
    x_high, x_low = halves_np(along_x)
    forward_x = np.concatenate([x_high, x_low, x_high], axis=1)
    backward_x = np.concatenate([x_high.T, x_low.T, x_high.T], axis=1)
    place_y = (np.arange(cols_count)[:, None] * CY + np.arange(Y_PAD)[None, :] - 2) % grid_y
    along_y = cas_np(np.arange(grid_y), place_y.reshape(-1), grid_y)
    along_y = along_y.reshape(grid_y, cols_count, Y_PAD)
    units = chunk * RHS // SPLIT
    block = np.einsum("uv,kcy->cuyvk", np.eye(units), along_y)
    block = block.reshape(cols_count * units * Y_PAD, units * grid_y)
    kernel = influence_np(grid_x, grid_y, KZ).reshape(grid_x, grid_y, devices, chunk)
    kernel = np.transpose(kernel, (2, 0, 3, 1))[:, :, :, None, :]
    kernel = np.broadcast_to(kernel, (devices, grid_x, chunk, RHS, grid_y))
    kernel = kernel.reshape(devices, grid_x, SPLIT, units * grid_y)
    kernel = np.moveaxis(kernel, 2, 1).reshape(devices, SPLIT * grid_x, units * grid_y)
    kernel = kernel.astype(np.float32)
    return dict(
        along_z=halves_np(along_z),
        forward_x=forward_x,
        backward_x=backward_x,
        block=halves_np(block),
        kernel=kernel,
    )


def pack_body(rhs_ref, place_ref, polar_ref, start_ref, payload_ref):
    polar = polar_ref[...]
    start = read_rows(rhs_ref) * polar
    start_ref[...] = start
    place = [place_ref[dim] for dim in range(3)]
    everything = jnp.concatenate(place + [1.0 / jnp.sqrt(polar), start], axis=0)
    store_payload(payload_ref, everything)


def read_rows(rows_ref):
    return jnp.concatenate([rows_ref[dim] for dim in range(3)], axis=0)


def store_payload(payload_ref, everything):
    tile_count = everything.shape[1] // TILE
    for quantity in range(everything.shape[0]):
        for tile in range(tile_count):
            row = quantity * tile_count + tile
            payload_ref[row : row + 1, :] = everything[
                quantity : quantity + 1, tile * TILE : (tile + 1) * TILE
            ]


def placed_rows(slot, weights, extent):
    slot_index = lax.broadcasted_iota(jnp.int32, (extent, slot.shape[1]), 0)
    placed = jnp.zeros((extent, slot.shape[1]), jnp.float32)
    for stencil in range(5):
        target = slot + stencil
        if extent == KZ:
            target = jnp.where(target >= KZ, target - KZ, target)
        placed = placed + jnp.where(slot_index == target, weights[stencil], 0.0)
    return placed


def spread_into(message_ref, moment, rows_x, slope_x, rows_y, slope_y, depth, devices):
    blocks = []
    for step in range(X_PAD):
        flat_x = rows_x[step : step + 1]
        tilt_x = slope_x[step : step + 1]
        for rhs in range(RHS):
            part_x = tilt_x * moment[rhs : rhs + 1]
            part_y = flat_x * moment[RHS + rhs : RHS + rhs + 1]
            part_z = flat_x * moment[2 * RHS + rhs : 2 * RHS + rhs + 1]
            blocks.append(
                jnp.concatenate([part_x * rows_y + part_y * slope_y, part_z * rows_y], axis=1)
            )
    charges = jnp.concatenate(blocks, axis=0)
    spectrum = product(depth, halves(charges), 1, 1)
    slot_rows = message_ref.shape[0] // devices
    chunk = KZ // devices
    width = RHS * Y_PAD
    for step in range(X_PAD):
        message_ref[pl.ds(step, devices, stride=slot_rows), :] = jnp.concatenate(
            [
                spectrum[unit * devices : (unit + 1) * devices, step * width : (step + 1) * width]
                for unit in range(chunk)
            ],
            axis=1,
        )


def sample_from(message_ref, rows_x, slope_x, rows_y, slope_y, depth, devices):
    chunk = KZ // devices
    width = RHS * Y_PAD
    slot_rows = message_ref.shape[0] // devices
    pieces = [
        message_ref[pl.ds(step, devices, stride=slot_rows), :] for step in range(X_PAD)
    ]
    spare = jnp.zeros((devices, KZ - X_PAD * width), jnp.float32)
    spectrum = jnp.concatenate(
        [
            jnp.concatenate(
                [piece[:, unit * width : (unit + 1) * width] for piece in pieces] + [spare], axis=1
            )
            for unit in range(chunk)
        ],
        axis=0,
    )
    spectrum = jnp.transpose(spectrum)[: X_PAD * width]
    sampled = product(halves(spectrum), depth, 1, 0)
    atoms = rows_x.shape[1]
    fields = [None] * (3 * RHS)
    for rhs in range(RHS):
        sum_x = sum_y = sum_z = None
        for step in range(X_PAD):
            first = step * width + rhs * Y_PAD
            flat = sampled[first : first + Y_PAD, :atoms]
            tilt = sampled[first : first + Y_PAD, atoms:]
            part_x = slope_x[step : step + 1] * flat
            part_y = rows_x[step : step + 1] * flat
            part_z = rows_x[step : step + 1] * tilt
            sum_x = part_x if sum_x is None else sum_x + part_x
            sum_y = part_y if sum_y is None else sum_y + part_y
            sum_z = part_z if sum_z is None else sum_z + part_z
        fields[rhs] = jnp.sum(sum_x * rows_y, axis=0, keepdims=True)
        fields[RHS + rhs] = jnp.sum(sum_y * slope_y, axis=0, keepdims=True)
        fields[2 * RHS + rhs] = jnp.sum(sum_z * rows_y, axis=0, keepdims=True)
    return jnp.concatenate(fields, axis=0)


def read_tables(tables_ref):
    return (
        tables_ref[0:X_PAD],
        tables_ref[SLOT_ROWS : SLOT_ROWS + X_PAD],
        tables_ref[2 * SLOT_ROWS : 2 * SLOT_ROWS + Y_PAD],
        tables_ref[2 * SLOT_ROWS + Y_PAD : 2 * SLOT_ROWS + 2 * Y_PAD],
    )


def setup_body(
    lengths,
    devices,
    place_ref,
    base_ref,
    start_ref,
    z_high_ref,
    z_low_ref,
    message_ref,
    tables_ref,
    depth_high_ref,
    depth_low_ref,
):
    base = [base_ref[dim] for dim in range(3)]
    fractions = []
    cells = []
    for dim in range(3):
        cell = base[dim] + 2
        cell = jnp.where(cell >= lengths[dim], cell - lengths[dim], cell)
        cells.append(cell)
        fractions.append(place_ref[dim] - cell.astype(jnp.float32))
    values, slopes = spline_table(jnp.concatenate(fractions, axis=0))
    values = [[values[stencil][dim : dim + 1] for stencil in range(5)] for dim in range(3)]
    slopes = [[slopes[stencil][dim : dim + 1] for stencil in range(5)] for dim in range(3)]
    slot_x = lax.rem(cells[0], CX)
    slot_y = lax.rem(cells[1], CY)
    tables_ref[0:SLOT_ROWS] = placed_rows(slot_x, values[0], SLOT_ROWS)
    tables_ref[SLOT_ROWS : 2 * SLOT_ROWS] = placed_rows(slot_x, slopes[0], SLOT_ROWS)
    tables_ref[2 * SLOT_ROWS : 2 * SLOT_ROWS + Y_PAD] = placed_rows(slot_y, values[1], Y_PAD)
    tables_ref[2 * SLOT_ROWS + Y_PAD : 2 * SLOT_ROWS + 2 * Y_PAD] = placed_rows(
        slot_y, slopes[1], Y_PAD
    )
    window = jnp.concatenate(
        [
            placed_rows(base[2], values[2], KZ),
            placed_rows(base[2], slopes[2], KZ),
        ],
        axis=1,
    )
    depth = product((z_high_ref[...], z_low_ref[...]), halves(window), 1, 0)
    depth = halves(depth)
    depth_high_ref[...] = depth[0]
    depth_low_ref[...] = depth[1]
    spread_into(message_ref, start_ref[...], *read_tables(tables_ref), depth, devices)


def transform_in(message_ref, forward_ref, block_high_ref, block_low_ref, rows_count, cols_count):
    gathered = jnp.concatenate(
        [
            jnp.concatenate(
                [
                    message_ref[(r * cols_count + c) * X_PAD : (r * cols_count + c + 1) * X_PAD]
                    for r in range(rows_count)
                ],
                axis=0,
            )
            for c in range(cols_count)
        ],
        axis=1,
    )
    high, low = halves(gathered)
    along = jnp.dot(
        forward_ref[...],
        jnp.concatenate([high, high, low], axis=0),
        preferred_element_type=jnp.float32,
    )
    part = along.shape[1] // cols_count // SPLIT
    along = jnp.concatenate(
        [
            jnp.concatenate(
                [
                    along[:, (c * SPLIT + half) * part : (c * SPLIT + half + 1) * part]
                    for c in range(cols_count)
                ],
                axis=1,
            )
            for half in range(SPLIT)
        ],
        axis=0,
    )
    return product(halves(along), (block_high_ref[...], block_low_ref[...]))


def transform_out(result_ref, values, backward_ref, block_high_ref, block_low_ref, counts):
    rows_count, cols_count = counts
    spread = product(halves(values), (block_high_ref[...], block_low_ref[...]), 1, 1)
    grid_x = spread.shape[0] // SPLIT
    part = spread.shape[1] // cols_count
    spread = jnp.concatenate(
        [
            spread[half * grid_x : (half + 1) * grid_x, c * part : (c + 1) * part]
            for c in range(cols_count)
            for half in range(SPLIT)
        ],
        axis=1,
    )
    high, low = halves(spread)
    along = jnp.dot(
        backward_ref[...],
        jnp.concatenate([high, high, low], axis=0),
        preferred_element_type=jnp.float32,
    )
    width = along.shape[1] // cols_count
    slot_rows = result_ref.shape[0] // (rows_count * cols_count)
    for r in range(rows_count):
        for c in range(cols_count):
            first = (r * cols_count + c) * slot_rows
            result_ref[first : first + X_PAD, :] = along[
                r * X_PAD : (r + 1) * X_PAD, c * width : (c + 1) * width
            ]


def middle_first_body(
    counts,
    message_ref,
    kernel_ref,
    forward_ref,
    backward_ref,
    block_high_ref,
    block_low_ref,
    result_ref,
    wave_ref,
):
    wave = transform_in(message_ref, forward_ref, block_high_ref, block_low_ref, *counts)
    wave_ref[...] = wave
    transform_out(
        result_ref, wave * kernel_ref[...], backward_ref, block_high_ref, block_low_ref, counts
    )


def gather_rows(parts):
    tiles = [
        parts[GROUP * tile : GROUP * tile + GROUP, :] for tile in range(parts.shape[0] // GROUP)
    ]
    return jnp.concatenate(tiles, axis=1)[0 : 3 * RHS]


def row_total(value, rhs):
    row = lax.broadcasted_iota(jnp.int32, value.shape, 0)
    return total(jnp.where(lax.rem(row, RHS) == rhs, value, 0.0))


def total(value):
    return jnp.sum(jnp.sum(value, axis=0, keepdims=True), axis=1, keepdims=True)


def middle_second_body(
    counts,
    message_ref,
    kernel_ref,
    forward_ref,
    backward_ref,
    block_high_ref,
    block_low_ref,
    wave_ref,
    rhs_ref,
    start_ref,
    image_ref,
    second_ref,
    near_ref,
    polar_ref,
    result_ref,
):
    rhs_rows = read_rows(rhs_ref)
    near_rows = gather_rows(near_ref)
    wave = transform_in(message_ref, forward_ref, block_high_ref, block_low_ref, *counts)
    filtered = wave * kernel_ref[...]
    transform_out(result_ref, filtered, backward_ref, block_high_ref, block_low_ref, counts)
    before = wave_ref[...]
    grid_y = CY * counts[1]
    lane = lax.broadcasted_iota(jnp.int32, wave.shape, 1)
    own_rhs = lax.rem(lax.div(lane, grid_y), RHS)
    second = second_ref[...]
    start = start_ref[...]
    image = image_ref[...]
    local_part = second / polar_ref[...] - near_rows - self_coef * second
    slot = lax.broadcasted_iota(jnp.int32, (1, result_ref.shape[1]), 1)
    sums = jnp.zeros((1, result_ref.shape[1]), jnp.float32)
    for rhs in range(RHS):
        mine = own_rhs == rhs
        parts = (
            row_total(rhs_rows * start, rhs),
            row_total(start * image, rhs),
            row_total(second * image, rhs),
            row_total(start * local_part, rhs) + total(jnp.where(mine, before * filtered, 0.0)),
            row_total(second * local_part, rhs) + total(jnp.where(mine, wave * filtered, 0.0)),
        )
        for index, part in enumerate(parts):
            sums = jnp.where(slot == rhs * len(parts) + index, part, sums)
    devices = counts[0] * counts[1]
    result_ref[pl.ds(X_PAD, devices, stride=X_PAD + 1), :] = jnp.broadcast_to(
        sums, (devices, sums.shape[1])
    )


def sample_body(
    devices,
    message_ref,
    tables_ref,
    depth_high_ref,
    depth_low_ref,
    start_ref,
    near_ref,
    polar_ref,
    image_ref,
    second_ref,
    payload_ref,
):
    tables = read_tables(tables_ref)
    depth = (depth_high_ref[...], depth_low_ref[...])
    field = sample_from(message_ref, *tables, depth, devices)
    start = start_ref[...]
    polar = polar_ref[...]
    image = start / polar - gather_rows(near_ref) + field - self_coef * start
    second = polar * image
    image_ref[...] = image
    second_ref[...] = second
    store_payload(payload_ref, second)


def spread_body(
    devices,
    tables_ref,
    depth_high_ref,
    depth_low_ref,
    second_ref,
    result_ref,
):
    depth = (depth_high_ref[...], depth_low_ref[...])
    spread_into(result_ref, second_ref[...], *read_tables(tables_ref), depth, devices)


def final_body(
    devices,
    message_ref,
    tables_ref,
    depth_high_ref,
    depth_low_ref,
    rhs_ref,
    start_ref,
    image_ref,
    second_ref,
    near_ref,
    polar_ref,
    dipole_ref,
    residual_ref,
):
    tables = read_tables(tables_ref)
    depth = (depth_high_ref[...], depth_low_ref[...])
    field = sample_from(message_ref, *tables, depth, devices)
    second = second_ref[...]
    start = start_ref[...]
    image = image_ref[...]
    image_second = second / polar_ref[...] - gather_rows(near_ref) + field - self_coef * second
    sums = jnp.sum(
        message_ref[pl.ds(X_PAD, devices, stride=X_PAD + 1), :], axis=0, keepdims=True
    )
    steps = []
    for rhs in range(RHS):
        progress, start_image, second_image, start_next, second_next = [
            sums[:, rhs * 5 + index : rhs * 5 + index + 1] for index in range(5)
        ]
        step = progress / start_image
        progress_next = progress - 2.0 * step * start_image + step * step * second_image
        grown = 1.0 + progress_next / progress
        curvature = (
            grown * grown * start_image
            - step * grown * (start_next + second_image)
            + step * step * second_next
        )
        steps.append((step, grown, progress_next / curvature))
    row = lax.broadcasted_iota(jnp.int32, (RHS, 1), 0)
    step, grown, step_next = [
        sum(jnp.where(row == rhs, steps[rhs][index], 0.0) for rhs in range(RHS))
        for index in range(3)
    ]
    for dim in range(3):
        rows = slice(dim * RHS, (dim + 1) * RHS)
        direction = grown * start[rows] - step * second[rows]
        image_direction = grown * image[rows] - step * image_second[rows]
        dipole_ref[dim] = step * start[rows] + step_next * direction
        residual_ref[dim] = rhs_ref[dim] - step * image[rows] - step_next * image_direction


def near_base(entry, brick_rows):
    return lax.shift_right_logical(entry, 2) * brick_rows + lax.bitwise_and(entry, 3)


def fill_near(scratch, up_ref, stack_ref, down_ref):
    rows = stack_ref.shape[0]
    scratch[0:rows, :] = up_ref[...]
    scratch[rows : 2 * rows, :] = stack_ref[...]
    scratch[2 * rows : 3 * rows, :] = down_ref[...]


def nearest(places, origin, span):
    return places - span * jnp.floor((places - origin) * (1.0 / span) + 0.5)


def unwrap_near(near, tile_count, spans):
    rows = near.shape[0] // 9
    for dim in range(2):
        own = 4 * rows + dim * tile_count
        origin = near[own : own + 1, 0:1]
        for brick in range(9):
            first = brick * rows + dim * tile_count
            near[first : first + tile_count, :] = nearest(
                near[first : first + tile_count, :], origin, spans[dim]
            )


def pick_rows(picked, near, lists_ref, tile, tile_count, quantities, origin, span):
    rows = near.shape[0] // 9
    for entry in range(lists_ref.shape[1]):
        base = near_base(lists_ref[tile, entry], rows)
        for quantity in range(quantities):
            values = near[pl.ds(base + quantity * tile_count, 1), :]
            if quantity == 2 and span is not None:
                values = nearest(values, origin, span)
            first = (entry * quantities + quantity) * GROUP
            picked[first : first + GROUP, :] = jnp.broadcast_to(values, (GROUP, TILE))


def widen_own(near, quantities, tile_count, tile, square, wide):
    offset = near.shape[0] // 9 * 4
    for quantity in range(quantities):
        square[quantity : quantity + 1, :] = near[
            pl.ds(offset + quantity * tile_count + tile, 1), :
        ]
    columns = jnp.transpose(square[...])
    for quantity in range(quantities):
        wide[quantity * TILE : (quantity + 1) * TILE, :] = jnp.broadcast_to(
            columns[:, quantity : quantity + 1], (TILE, TILE)
        )


def add_field(sums, first_term, second_term, apart, moments):
    for rhs in range(RHS):
        moment = [moments[RHS * dim + rhs] for dim in range(3)]
        projected = moment[0] * apart[0] + moment[1] * apart[1] + moment[2] * apart[2]
        weighted = second_term * projected
        for dim in range(3):
            index = RHS * dim + rhs
            sums[index] = sums[index] + (weighted * apart[dim] - first_term * moment[dim])


def finish_sums(field_ref, sums_ref):
    lane = lax.broadcasted_iota(jnp.int32, (TILE, TILE), 1)
    merged = jnp.zeros((TILE, TILE), jnp.float32)
    for index in range(3 * RHS):
        column = jnp.sum(sums_ref[index * TILE : (index + 1) * TILE, :], axis=1, keepdims=True)
        merged = jnp.where(lane == index, column, merged)
    field_ref[...] = jnp.transpose(merged)[0:GROUP]


def pair_rows(start, group):
    return pl.ds(pl.multiple_of(start + group * GROUP, GROUP), GROUP)


def wide_rows(start, group, quantity):
    return pl.ds(pl.multiple_of(quantity * TILE + start + group * GROUP, GROUP), GROUP)


def pair_terms(square_dist, damp):
    inverse = lax.rsqrt(square_dist)
    distance = square_dist * inverse
    inverse_sq = inverse * inverse
    inverse_cube = inverse_sq * inverse
    cubed = damp * (distance * square_dist)
    damping = jnp.exp(cubed)
    bell = jnp.exp(-(ewald_beta * ewald_beta) * square_dist)
    stretched = 1.0 + (SCREEN_SCALE * ewald_beta) * distance
    turned = pl.reciprocal(stretched, approx=True)
    turned = turned * (2.0 - stretched * turned)
    series = SCREEN_COEF[-1] * turned + SCREEN_COEF[-2]
    for coef in SCREEN_COEF[-3::-1]:
        series = series * turned + coef
    screen = bell * turned * series
    gaussian = (2.0 * ewald_beta / math.sqrt(math.pi)) * bell
    bare = screen - damping
    first_term = bare * inverse_cube + gaussian * inverse_sq
    second_term = (
        3.0 * (first_term + (cubed * damping) * inverse_cube)
        + (2.0 * ewald_beta * ewald_beta) * gaussian
    ) * inverse_sq
    return first_term, second_term


def pair_first_body(
    first_tile,
    tile_count,
    spans,
    lists_ref,
    up_ref,
    stack_ref,
    down_ref,
    *others,
):
    first_ref, second_ref, field_ref, near_ref, near, picked, square, wide, sums_ref = others[-9:]

    @pl.when(pl.program_id(0) == 0)
    def _():
        fill_near(near, up_ref, stack_ref, down_ref)
        unwrap_near(near, tile_count, spans)
        square[...] = jnp.zeros_like(square)
        rows = near.shape[0] // 9
        kept = 3 * tile_count
        for brick in range(9):
            near_ref[brick * kept : (brick + 1) * kept, :] = near[
                brick * rows : brick * rows + kept, :
            ]

    tile = first_tile + pl.program_id(0)
    quantities = near.shape[0] // 9 // tile_count
    widen_own(near, 4, tile_count, tile, square, wide)
    origin = wide[2 * TILE : 2 * TILE + 1, 0:1]
    pick_rows(picked, near, lists_ref, tile, tile_count, quantities, origin, spans[2])

    @pl.loop(0, TILE // PAIR_ROWS)
    def _(part):
        start = part * PAIR_ROWS
        for group in range(PAIR_ROWS // GROUP):
            own = [wide[wide_rows(start, group, dim), :] for dim in range(4)]
            own_damp = -thole_a * own[3]
            sums = [jnp.zeros((GROUP, TILE), jnp.float32) for _ in range(3 * RHS)]
            itself = (
                lax.broadcasted_iota(jnp.int32, (GROUP, TILE), 0) + (start + group * GROUP)
            ) == lax.broadcasted_iota(jnp.int32, (GROUP, TILE), 1)
            for entry in range(lists_ref.shape[1]):
                first = entry * quantities * GROUP
                rows = [
                    picked[first + quantity * GROUP : first + (quantity + 1) * GROUP, :]
                    for quantity in range(quantities)
                ]
                apart = [rows[dim] - own[dim] for dim in range(3)]
                square_dist = apart[0] * apart[0] + apart[1] * apart[1] + apart[2] * apart[2]
                if entry == 0:
                    square_dist = jnp.where(itself, 1.0, square_dist)
                first_term, second_term = pair_terms(square_dist, own_damp * rows[3])
                if entry == 0:
                    first_term = jnp.where(itself, 0.0, first_term)
                    second_term = jnp.where(itself, 0.0, second_term)
                place = wide_rows(start, group, entry)
                first_ref[place, :] = first_term
                second_ref[place, :] = second_term
                add_field(sums, first_term, second_term, apart, rows[4:])
            for index, value in enumerate(sums):
                sums_ref[wide_rows(start, group, index), :] = value

    finish_sums(field_ref, sums_ref)


def pair_second_body(
    tile_count,
    spans,
    lists_ref,
    near,
    up_ref,
    stack_ref,
    down_ref,
    first_ref,
    second_ref,
    field_ref,
    near_moment,
    picked,
    picked_moment,
    square,
    wide,
    sums_ref,
):
    @pl.when(pl.program_id(0) == 0)
    def _():
        fill_near(near_moment, up_ref, stack_ref, down_ref)
        square[...] = jnp.zeros_like(square)

    tile = pl.program_id(0)
    widen_own(near, 3, tile_count, tile, square, wide)
    origin = wide[2 * TILE : 2 * TILE + 1, 0:1]
    pick_rows(picked, near, lists_ref, tile, tile_count, 3, origin, spans[2])
    pick_rows(picked_moment, near_moment, lists_ref, tile, tile_count, 3 * RHS, None, None)

    @pl.loop(0, TILE // PAIR_ROWS)
    def _(part):
        start = part * PAIR_ROWS
        for group in range(PAIR_ROWS // GROUP):
            own = [wide[wide_rows(start, group, dim), :] for dim in range(3)]
            sums = [jnp.zeros((GROUP, TILE), jnp.float32) for _ in range(3 * RHS)]
            for entry in range(lists_ref.shape[1]):
                first = entry * 3 * GROUP
                apart = [
                    picked[first + dim * GROUP : first + (dim + 1) * GROUP, :] - own[dim]
                    for dim in range(3)
                ]
                first = first * RHS
                moments = [
                    picked_moment[first + index * GROUP : first + (index + 1) * GROUP, :]
                    for index in range(3 * RHS)
                ]
                place = wide_rows(start, group, entry)
                add_field(sums, first_ref[place, :], second_ref[place, :], apart, moments)
            for index, value in enumerate(sums):
                sums_ref[wide_rows(start, group, index), :] = value

    finish_sums(field_ref, sums_ref)


def shift(source, axis, step):
    count = lax.axis_size(axis)
    return lax.ppermute(source, axis, [(i, (i + step) % count) for i in range(count)])


def both_ways(source, axis):
    return shift(source, axis, 1), source, shift(source, axis, -1)


def whole(shape):
    return pl.BlockSpec(shape, lambda *_: (0,) * len(shape))


def anywhere():
    return pl.BlockSpec(memory_space=pl.ANY)


def join(message, payload):
    left, _, right = both_ways(payload, "col")
    message, left, right = lax.optimization_barrier((message, left, right))
    return message, both_ways(jnp.concatenate([left, payload, right], axis=0), "row")


class Fetched:
    def __init__(self, source, scratch, semaphore):
        self.copy = pltpu.make_async_copy(source, scratch, semaphore)
        self.copy.start()
        self.scratch = scratch
        self.shape = scratch.shape
        self.waiting = True

    def wait(self):
        if self.waiting:
            self.copy.wait()
            self.waiting = False

    def __getitem__(self, index):
        self.wait()
        return self.scratch[index]


def call(body, outs, *operands, after=(), own_block=None):
    fetched = [
        pltpu.VMEM(operand.shape[1:] if index == own_block else operand.shape, operand.dtype)
        for index, operand in enumerate(operands)
    ]
    count = len(operands)

    def run(*refs):
        refs = refs[len(after) :]
        sources, refs = refs[:count], refs[count:]
        results, refs = refs[: len(outs)], refs[len(outs) :]
        targets, written, semaphore = refs[:count], refs[count:-1], refs[-1]
        inputs = []
        for index, source in enumerate(sources):
            if index == own_block:
                place = lax.axis_index("row") * lax.axis_size("col") + lax.axis_index("col")
                source = source.at[place]
            inputs.append(Fetched(source, targets[index], semaphore.at[index]))
        body(*inputs, *written)
        for operand in inputs:
            operand.wait()
        copies = [
            pltpu.make_async_copy(value, result, semaphore.at[count + index])
            for index, (value, result) in enumerate(zip(written, results))
        ]
        for copy in copies:
            copy.start()
        for copy in copies:
            copy.wait()

    return pl.pallas_call(
        run,
        in_specs=[anywhere()] * (len(after) + count),
        out_specs=[anywhere()] * len(outs),
        out_shape=[jax.ShapeDtypeStruct(shape, dtype) for shape, dtype in outs],
        scratch_shapes=fetched
        + [pltpu.VMEM(shape, dtype) for shape, dtype in outs]
        + [pltpu.SemaphoreType.DMA((count + len(outs),))],
        compiler_params=pltpu.CompilerParams(vmem_limit_bytes=VMEM_LIMIT),
        cost_estimate=pl.CostEstimate(
            flops=200_000_000, bytes_accessed=4 << 20, transcendentals=0
        ),
    )(*after, *operands)


def final_call(body, outs, *operands):
    return pl.pallas_call(
        body,
        grid=(1,),
        in_specs=[whole(operand.shape) for operand in operands],
        out_specs=[whole(shape) for shape, _ in outs],
        out_shape=[jax.ShapeDtypeStruct(shape, dtype) for shape, dtype in outs],
        compiler_params=pltpu.CompilerParams(vmem_limit_bytes=SMALL_VMEM_LIMIT),
    )(*operands)


def pair_call(body, outs, kept, first_tile, last_tile, blocked, scratch, lists, *operands, after=()):
    tiles = lists.shape[0]

    def block(operand):
        rows = operand.shape[0] // tiles
        return pl.BlockSpec((rows, operand.shape[1]), lambda i, s: (first_tile + i, 0))

    out_shape = [jax.ShapeDtypeStruct(shape, jnp.float32) for shape in outs + kept]
    plain = len(operands) - blocked
    aliases = {}
    if first_tile > 0:
        first = 1 + len(operands) + len(after) - len(outs)
        aliases = {first + index: index for index in range(len(outs))}
    return pl.pallas_call(
        body,
        out_shape=out_shape,
        grid_spec=pltpu.PrefetchScalarGridSpec(
            num_scalar_prefetch=1,
            grid=(last_tile - first_tile,),
            in_specs=[whole(operand.shape) for operand in operands[:plain]]
            + [block(operand) for operand in operands[plain:]]
            + [anywhere()] * len(after),
            out_specs=[block(shape) for shape in out_shape[: len(outs)]]
            + [whole(shape) for shape in kept],
            scratch_shapes=[pltpu.VMEM(shape, jnp.float32) for shape in scratch],
        ),
        input_output_aliases=aliases,
        compiler_params=pltpu.CompilerParams(vmem_limit_bytes=VMEM_LIMIT),
        cost_estimate=pl.CostEstimate(
            flops=80_000_000, bytes_accessed=8 << 20, transcendentals=1 << 21
        ),
    )(lists, *operands, *after)


def exchange(message, devices):
    shape = message.shape
    sent = message.reshape(devices, 1, -1)
    return lax.all_to_all(sent, ("row", "col"), split_axis=0, concat_axis=0, tiled=True).reshape(
        shape
    )


def slab_local(field_rhs, positions, polar, grid_base, tile_lists):
    rows_count = lax.axis_size("row")
    cols_count = lax.axis_size("col")
    counts = (rows_count, cols_count)
    devices = rows_count * cols_count
    lengths = (CX * rows_count, CY * cols_count, KZ)
    spans = tuple(float(length) for length in lengths)
    atoms = polar.shape[-1]
    tile_count = atoms // TILE
    listed = tile_lists.shape[-1]
    tables = slab_tables(rows_count, cols_count)
    f32 = jnp.float32
    rhs = jnp.swapaxes(field_rhs[0, 0], 0, 1)
    place = jnp.swapaxes(positions[0], 0, 1)
    base = jnp.swapaxes(grid_base[0], 0, 1)
    polar = polar.reshape(1, atoms)
    lists = tile_lists[0, 0]
    quantities = 4 + 3 * RHS
    brick_rows = quantities * tile_count
    moment_rows = 3 * RHS * tile_count
    message_shape = (devices * X_PAD, KZ // devices * RHS * Y_PAD)
    last_shape = (devices * (X_PAD + 1), message_shape[1])
    row_shape = (3 * RHS, atoms)
    square = (TILE, TILE)
    wide = (4 * TILE, TILE)
    sums = (3 * RHS * TILE, TILE)

    start, payload = call(pack_body, [(row_shape, f32), ((brick_rows, TILE), f32)], rhs, place, polar)

    def setup(*refs):
        setup_body(lengths, devices, *refs)

    message, splines, depth_high, depth_low = call(
        setup,
        [
            (message_shape, f32),
            ((2 * SLOT_ROWS + 2 * Y_PAD, atoms), f32),
            ((KZ, 2 * atoms), jnp.bfloat16),
            ((KZ, 2 * atoms), jnp.bfloat16),
        ],
        place,
        base,
        start,
        *[jnp.asarray(table) for table in tables["along_z"]],
    )
    constants = (
        jnp.asarray(tables["kernel"]),
        jnp.asarray(tables["forward_x"]),
        jnp.asarray(tables["backward_x"]),
        *[jnp.asarray(table) for table in tables["block"]],
    )
    message, near = join(message, payload)
    arrived = exchange(message, devices)

    def pair_first(first_tile, last_tile, *after):
        def body(*refs):
            pair_first_body(first_tile, tile_count, spans, *refs)

        return pair_call(
            body,
            [(tile_count * listed * TILE, TILE)] * 2 + [(tile_count * GROUP, TILE)],
            [(9 * 3 * tile_count, TILE)],
            first_tile,
            last_tile,
            0,
            [(9 * brick_rows, TILE), (listed * quantities * GROUP, TILE), square, wide, sums],
            lists,
            *near,
            after=after,
        )

    early = pair_first(0, EARLY_TILES, message)

    def middle_first(*refs):
        middle_first_body(counts, *refs)

    mixed, wave = call(
        middle_first,
        [(message_shape, f32), (tables["kernel"].shape[1:], f32)],
        arrived,
        *constants,
        after=(early[2],),
        own_block=1,
    )
    returned = exchange(mixed, devices)
    first_term, second_term, direct, near = pair_first(EARLY_TILES, tile_count, wave, *early[:3])

    def sample(*refs):
        sample_body(devices, *refs)

    image, second, moments = call(
        sample,
        [(row_shape, f32), (row_shape, f32), ((moment_rows, TILE), f32)],
        returned,
        splines,
        depth_high,
        depth_low,
        start,
        direct,
        polar,
    )

    def spread(*refs):
        spread_body(devices, *refs)

    (message,) = call(spread, [(message_shape, f32)], splines, depth_high, depth_low, second)
    message, near_moments = join(message, moments)
    arrived = exchange(message, devices)

    def pair_second(*refs):
        pair_second_body(tile_count, spans, *refs)

    (direct,) = pair_call(
        pair_second,
        [(tile_count * GROUP, TILE)],
        [],
        0,
        tile_count,
        2,
        [
            (9 * moment_rows, TILE),
            (listed * 3 * GROUP, TILE),
            (listed * 3 * RHS * GROUP, TILE),
            square,
            wide,
            sums,
        ],
        lists,
        near,
        *near_moments,
        first_term,
        second_term,
    )

    def middle_second(*refs):
        middle_second_body(counts, *refs)

    (mixed,) = call(
        middle_second,
        [(last_shape, f32)],
        arrived,
        *constants,
        wave,
        rhs,
        start,
        image,
        second,
        direct,
        polar,
        own_block=1,
    )
    returned = exchange(mixed, devices)

    def final(*refs):
        final_body(devices, *refs)

    outs = final_call(
        final,
        [(rhs.shape, f32), (rhs.shape, f32)],
        returned,
        splines,
        depth_high,
        depth_low,
        rhs,
        start,
        image,
        second,
        direct,
        polar,
    )
    return tuple(jnp.swapaxes(out, 0, 1)[None, None] for out in outs)


def solution(mesh):
    placed = (
        P("row", "col", None, None, None),
        P("row", "col", None, None),
        P("row", "col", None),
        P("row", "col", None, None),
        P("row", "col", None, None),
    )
    devices = mesh.shape["row"] * mesh.shape["col"]
    return jax.shard_map(
        slab_local if KZ % devices == 0 else pencil_local,
        mesh=mesh,
        in_specs=placed,
        out_specs=(P("row", "col", None, None, None), P("row", "col", None, None, None)),
        check_vma=False,
    )
```

```python
import math

import jax
import jax.numpy as jnp
import ml_dtypes
import numpy as np
from jax import lax
from jax.experimental import pallas as pl
from jax.experimental.pallas import tpu as pltpu
from jax.sharding import PartitionSpec as P

CX = 8
CY = 4
KZ = 256
TILE = 128
RHS = 2
ITERS = 2


ewald_beta = 0.4
thole_a = 0.39
self_coef = 4.0 * ewald_beta**3 / (3.0 * math.sqrt(math.pi))
highest = lax.Precision.HIGHEST


def with_halo(cells, sides, width):
    for axis, dim in sides:
        count = lax.axis_size(axis)
        head = lax.slice_in_dim(cells, 0, width, axis=dim)
        tail = lax.slice_in_dim(cells, cells.shape[dim] - width, cells.shape[dim], axis=dim)
        cells = jnp.concatenate(
            [
                lax.ppermute(tail, axis, [(i, (i + 1) % count) for i in range(count)]),
                cells,
                lax.ppermute(head, axis, [((i + 1) % count, i) for i in range(count)]),
            ],
            axis=dim,
        )
    return cells


def spline_table(fraction):
    previous = {0: jnp.ones_like(fraction)}
    fourth = previous
    for degree in range(2, 6):
        current = {}
        for offset in range(degree):
            abscissa = fraction + offset
            summed = abscissa * previous.get(offset, 0.0) + (degree - abscissa) * previous.get(
                offset - 1, 0.0
            )
            current[offset] = summed / (degree - 1)
        if degree == 4:
            fourth = current
        previous = current
    values = jnp.stack([previous[4 - stencil] for stencil in range(5)])
    slopes = jnp.stack(
        [fourth.get(4 - stencil, 0.0) - fourth.get(3 - stencil, 0.0) for stencil in range(5)]
    )
    return (values, slopes)


def spline_modulus(wave_index, length):
    spline_coef = (1.0 / 24.0, 11.0 / 24.0, 11.0 / 24.0, 1.0 / 24.0)
    cosine_sum = jnp.zeros(wave_index.shape, jnp.float32)
    sine_sum = jnp.zeros(wave_index.shape, jnp.float32)
    for offset in range(4):
        angles = 2.0 * math.pi / length * (wave_index * offset % length).astype(jnp.float32)
        cosine_sum = cosine_sum + spline_coef[offset] * jnp.cos(angles)
        sine_sum = sine_sum + spline_coef[offset] * jnp.sin(angles)
    return cosine_sum * cosine_sum + sine_sum * sine_sum


def folded_square(wave_index, length):
    nearest = jnp.minimum(wave_index, length - wave_index).astype(jnp.float32) / length
    return nearest * nearest


def influence(wave_x, wave_y, wave_z, length_x, length_y, length_z):
    wave_norm = (
        folded_square(wave_x, length_x)
        + folded_square(wave_y, length_y)
        + folded_square(wave_z, length_z)
    )
    modulus = (
        spline_modulus(wave_x, length_x)
        * spline_modulus(wave_y, length_y)
        * spline_modulus(wave_z, length_z)
    )
    excluded = (wave_x * 2 == length_x) | (wave_y * 2 == length_y) | (wave_z * 2 == length_z)
    excluded = excluded | (wave_x == 0) & (wave_y == 0) & (wave_z == 0)
    safe_norm = jnp.where(excluded, 1.0, wave_norm)
    safe_modulus = jnp.where(excluded, 1.0, modulus)
    result = jnp.exp(-(math.pi**2 / ewald_beta**2) * safe_norm) / (
        math.pi * safe_norm * safe_modulus
    )
    return jnp.where(excluded, 0.0, result)


def tile_field(own_static, near_static, near_dipole, box_spans):
    listed_count = near_static.shape[0]
    tile_width = own_static.shape[1]
    box_span = jnp.array(box_spans, dtype=jnp.float32)[None, :, None, None]
    separation = near_static[:, 0:3, None, :] - own_static[None, 0:3, :, None]
    separation = separation - box_span * jnp.floor(separation / box_span + 0.5)
    dist_sq = jnp.sum(separation * separation, axis=1)
    itself = (jnp.arange(listed_count)[:, None, None] == 0) & (
        jnp.arange(tile_width)[:, None] == jnp.arange(tile_width)[None, :]
    )[None]
    safe_sq = jnp.where(itself, 1.0, dist_sq)
    distance = jnp.sqrt(safe_sq)
    scaled = distance / (own_static[3][None, :, None] * near_static[:, 3][:, None, :])
    cubed = thole_a * scaled * scaled * scaled
    damping = jnp.exp(-cubed)
    screen = lax.erfc(ewald_beta * distance)
    gaussian = 2.0 * ewald_beta / math.sqrt(math.pi) * jnp.exp(-(ewald_beta * ewald_beta) * safe_sq)
    inverse_sq = 1.0 / safe_sq
    inverse_cube = inverse_sq / distance
    first_term = (screen - damping) * inverse_cube + gaussian * inverse_sq
    second = (
        3.0 * (screen - (1.0 + cubed) * damping) * inverse_cube * inverse_sq
        + gaussian * (2.0 * ewald_beta * ewald_beta + 3.0 * inverse_sq) * inverse_sq
    )
    first_term = jnp.where(itself, 0.0, first_term)
    second = jnp.where(itself, 0.0, second)
    projected = jnp.sum(near_dipole[:, :, :, None, :] * separation[:, None, :, :, :], axis=2)
    weighted = second[:, None] * projected
    outward = jnp.sum(weighted[:, :, None] * separation[:, None], axis=(0, 4))
    inward = jnp.sum(first_term[:, None, None] * near_dipole[:, :, :, None, :], axis=(0, 4))
    return outward - inward


def hartley(length):
    counter = jnp.arange(length, dtype=jnp.int32)
    angles = (
        2.0 * math.pi / length * (counter[:, None] * counter[None, :] % length).astype(jnp.float32)
    )
    return jnp.cos(angles) + jnp.sin(angles)


def placed_table(first_cell, weights, extent):
    slot_index = jnp.arange(extent, dtype=jnp.int32)[:, None]
    placed = jnp.zeros((extent, first_cell.shape[0]), jnp.float32)
    for stencil in range(5):
        placed = placed + jnp.where(
            slot_index == (first_cell[None, :] + stencil) % extent, weights[stencil][None, :], 0.0
        )
    return placed


def pad_axis(source, axis_pos, leading, trailing):
    widths = [(0, 0)] * source.ndim
    widths[axis_pos] = (leading, trailing)
    return jnp.pad(source, widths)


def fold_cycle(cycle_only, axis_pos, inner_len):
    middle = lax.slice_in_dim(cycle_only, 4, inner_len + 4, axis=axis_pos)
    lower_cycle = lax.slice_in_dim(cycle_only, 0, 2, axis=axis_pos)
    upper_cycle = lax.slice_in_dim(cycle_only, inner_len + 6, inner_len + 8, axis=axis_pos)
    return (
        middle
        + pad_axis(lower_cycle, axis_pos, 0, inner_len - 2)
        + pad_axis(upper_cycle, axis_pos, inner_len - 2, 0)
    )


def clear_inside(extended, extents):
    inside = None
    for axis_pos, inner_len in extents:
        slot_index = lax.broadcasted_iota(jnp.int32, extended.shape, axis_pos)
        within = (slot_index >= 2) & (slot_index < inner_len + 6)
        inside = within if inside is None else inside & within
    return jnp.where(inside, 0.0, extended)


def inner_sum(left_arr, right_arr):
    return lax.psum(jnp.sum(left_arr * right_arr, axis=(1, 2)), ("row", "col"))


def pencil_local(field_rhs, positions, polar, grid_base, tile_lists):
    rows_count = lax.axis_size("row")
    cols_count = lax.axis_size("col")
    grid_x = CX * rows_count
    grid_y = CY * cols_count
    atom_count = polar.shape[-1]
    tile_count = atom_count // TILE
    slab_depth = KZ // tile_count
    window_len = slab_depth + 4
    box_spans = (float(grid_x), float(grid_y), float(KZ))
    own_place = positions[0, 0]
    own_base = grid_base[0, 0]
    own_polar = polar[0, 0]
    lengths = jnp.array([grid_x, grid_y, KZ], dtype=jnp.int32)[:, None]
    cell_index = (own_base + 2) % lengths
    fraction = own_place - cell_index.astype(jnp.float32)
    values, slopes = spline_table(fraction)
    first_x = (own_base[0] - lax.axis_index("row") * CX + 2) % grid_x
    first_y = (own_base[1] - lax.axis_index("col") * CY + 2) % grid_y
    rows_x = placed_table(first_x, values[:, 0], CX + 4)
    slope_x = placed_table(first_x, slopes[:, 0], CX + 4)
    rows_y = placed_table(first_y, values[:, 1], CY + 4)
    slope_y = placed_table(first_y, slopes[:, 1], CY + 4)
    tile_start = jnp.arange(atom_count, dtype=jnp.int32) // TILE * slab_depth
    first_z = (own_base[2] + 2 - tile_start) % KZ
    rows_z = placed_table(first_z, values[:, 2], window_len)
    slope_z = placed_table(first_z, slopes[:, 2], window_len)
    plane_count = (CX + 4) * (CY + 4)
    plane_dx = (slope_x[:, None, :] * rows_y[None, :, :]).reshape(plane_count, atom_count)
    plane_dy = (rows_x[:, None, :] * slope_y[None, :, :]).reshape(plane_count, atom_count)
    plane_flat = (rows_x[:, None, :] * rows_y[None, :, :]).reshape(plane_count, atom_count)
    window_rows = jnp.moveaxis(rows_z.reshape(window_len, tile_count, TILE), 1, 0)
    window_slope = jnp.moveaxis(slope_z.reshape(window_len, tile_count, TILE), 1, 0)
    depth_table = jnp.concatenate([window_rows, window_slope], axis=2)
    grid_scale = 1.0 / (grid_x * grid_y * KZ)
    hartley_x = hartley(grid_x)
    hartley_y = hartley(grid_y)
    hartley_z = hartley(KZ)
    block_y = grid_y // rows_count
    block_z = KZ // cols_count
    wave_x = jnp.arange(grid_x, dtype=jnp.int32)[:, None, None]
    wave_y = (lax.axis_index("row") * block_y + jnp.arange(block_y, dtype=jnp.int32))[None, :, None]
    wave_z = (lax.axis_index("col") * block_z + jnp.arange(block_z, dtype=jnp.int32))[None, None, :]
    kernel = influence(wave_x, wave_y, wave_z, grid_x, grid_y, KZ) * grid_scale
    root_scale = jnp.power(own_polar, 1.0 / 6.0)
    own_static = jnp.concatenate([own_place, root_scale[None]], axis=0)
    near_static = with_halo(own_static[None, None], (("row", 0), ("col", 1)), 1)
    near_static = jnp.moveaxis(near_static.reshape(9, 4, tile_count, TILE), 2, 1).reshape(
        9 * tile_count, 4, TILE
    )
    own_tiles = jnp.moveaxis(own_static.reshape(4, tile_count, TILE), 1, 0)
    own_lists = tile_lists[0, 0]
    polar_wide = own_polar[None, None, :]
    solution = jnp.zeros_like(field_rhs[0, 0])
    residual = field_rhs[0, 0]
    scaled_res = polar_wide * residual
    direction = scaled_res
    progress = inner_sum(residual, scaled_res)
    for iteration in range(ITERS):
        near_dip = with_halo(direction[None, None], (("row", 0), ("col", 1)), 1)
        near_dip = jnp.moveaxis(near_dip.reshape(9, RHS, 3, tile_count, TILE), 3, 1).reshape(
            9 * tile_count, RHS, 3, TILE
        )

        def one_tile(tile_pos):
            picked = own_lists[tile_pos]
            return tile_field(own_tiles[tile_pos], near_static[picked], near_dip[picked], box_spans)

        fields = lax.map(one_tile, jnp.arange(tile_count, dtype=jnp.int32))
        direct = jnp.moveaxis(fields, 0, 2).reshape(RHS, 3, atom_count)
        slope_terms = (
            direction[:, 0, None, :] * plane_dx[None] + direction[:, 1, None, :] * plane_dy[None]
        )
        flat_terms = direction[:, 2, None, :] * plane_flat[None]
        spread_left = jnp.concatenate(
            [
                slope_terms.reshape(RHS, plane_count, tile_count, TILE),
                flat_terms.reshape(RHS, plane_count, tile_count, TILE),
            ],
            axis=3,
        )
        spread_windows = jnp.einsum("sptb,twb->sptw", spread_left, depth_table, precision=highest)
        main_part = spread_windows[..., :slab_depth].reshape(spread_windows.shape[:-2] + (KZ,))
        tail_part = pad_axis(
            spread_windows[..., slab_depth:], spread_windows.ndim - 1, 0, slab_depth - 4
        )
        tail_part = tail_part.reshape(spread_windows.shape[:-2] + (KZ,))[..., : KZ + 4 - slab_depth]
        last_axis = main_part.ndim - 1
        padded_line = pad_axis(main_part, last_axis, 0, 4) + pad_axis(
            tail_part, last_axis, slab_depth, 0
        )
        inner = padded_line[..., 2 : KZ + 2]
        spread_tile = (
            inner
            + pad_axis(padded_line[..., 0:2], last_axis, KZ - 2, 0)
            + pad_axis(padded_line[..., KZ + 2 : KZ + 4], last_axis, 0, KZ - 2)
        ).reshape(RHS, CX + 4, CY + 4, KZ)
        extended = with_halo(spread_tile, (("row", 1), ("col", 2)), 2)
        cycle_only = clear_inside(extended, ((1, CX), (2, CY)))
        folded = fold_cycle(fold_cycle(cycle_only, 1, CX), 2, CY)
        spectrum = jnp.einsum(
            "sxyz,zk->sxyk",
            spread_tile[:, 2 : CX + 2, 2 : CY + 2] + folded,
            hartley_z,
            precision=highest,
        )
        along_y = jnp.einsum(
            "sxyz,yk->sxkz",
            lax.all_to_all(spectrum, "col", split_axis=3, concat_axis=2, tiled=True),
            hartley_y,
            precision=highest,
        )
        along_x = (
            jnp.einsum(
                "sxyz,xk->skyz",
                lax.all_to_all(along_y, "row", split_axis=2, concat_axis=1, tiled=True),
                hartley_x,
                precision=highest,
            )
            * kernel[None]
        )
        mixed_part = jnp.einsum("sxyz,xk->skyz", along_x, hartley_x, precision=highest)
        returned = lax.all_to_all(mixed_part, "row", split_axis=1, concat_axis=2, tiled=True)
        swapped = jnp.einsum("sxyz,yk->sxkz", returned, hartley_y, precision=highest)
        restored = lax.all_to_all(swapped, "col", split_axis=2, concat_axis=3, tiled=True)
        padded = with_halo(
            jnp.einsum("sxyz,zk->sxyk", restored, hartley_z, precision=highest),
            (("row", 1), ("col", 2)),
            2,
        )
        line = padded.reshape(RHS, plane_count, KZ)
        extended_line = jnp.concatenate([line[..., KZ - 2 :], line, line[..., :2]], axis=-1)
        windows = jnp.stack(
            [
                extended_line[..., tile * slab_depth : tile * slab_depth + window_len]
                for tile in range(tile_count)
            ],
            axis=-2,
        )
        sampled = jnp.einsum("sptw,twb->sptb", windows, depth_table, precision=highest)
        with_flat = sampled[..., :TILE].reshape(RHS, plane_count, atom_count)
        with_slope = sampled[..., TILE:].reshape(RHS, plane_count, atom_count)
        recip_part = jnp.stack(
            [
                jnp.sum(with_flat * plane_dx[None], axis=1),
                jnp.sum(with_flat * plane_dy[None], axis=1),
                jnp.sum(with_slope * plane_flat[None], axis=1),
            ],
            axis=1,
        )
        image_field = direction / polar_wide - direct + recip_part - self_coef * direction
        step_size = (progress / inner_sum(direction, image_field))[:, None, None]
        solution = solution + step_size * direction
        residual = residual - step_size * image_field
        scaled_res = polar_wide * residual
        progress_next = inner_sum(residual, scaled_res)
        direction = scaled_res + (progress_next / progress)[:, None, None] * direction
        progress = progress_next
    return (solution[None, None], residual[None, None])


X_PAD = CX + 4
Y_PAD = CY + 4
SLOT_ROWS = 16
SPLIT = 2
VMEM_LIMIT = 60_000_000
SMALL_VMEM_LIMIT = 24_000_000
EARLY_TILES = 1
PAIR_ROWS = 32
GROUP = 16
BLOCK = 8
FIXED = 4
DEPTH = 6 * BLOCK
SCREEN_SCALE = 0.4
SCREEN_COEF = (
    0.22567588090896606,
    0.2256690263748169,
    0.20785020291805267,
    0.16849851608276367,
    0.14156343042850494,
    -0.005832736846059561,
    0.16930203139781952,
    -0.1830107867717743,
    0.05028456076979637,
)


def halves(value):
    high = value.astype(jnp.bfloat16)
    return high, (value - high.astype(jnp.float32)).astype(jnp.bfloat16)


def halves_np(value):
    value = value.astype(np.float32)
    high = value.astype(ml_dtypes.bfloat16)
    return high, (value - high.astype(np.float32)).astype(ml_dtypes.bfloat16)


def product(left, right, left_dim=1, right_dim=0):
    def one(first, second):
        return lax.dot_general(
            first,
            second,
            (((left_dim,), (right_dim,)), ((), ())),
            preferred_element_type=jnp.float32,
        )

    return one(left[0], right[0]) + (one(left[1], right[0]) + one(left[0], right[1]))


def cas_np(wave, place, length):
    angles = 2.0 * np.pi / length * (wave[:, None] * place[None, :] % length)
    return np.cos(angles) + np.sin(angles)


def modulus_np(wave, length):
    coef = np.array([1.0, 11.0, 11.0, 1.0]) / 24.0
    angles = 2.0 * np.pi / length * (wave[:, None] * np.arange(4)[None, :])
    return (coef * np.cos(angles)).sum(1) ** 2 + (coef * np.sin(angles)).sum(1) ** 2


def influence_np(length_x, length_y, length_z):
    total = np.zeros((length_x, length_y, length_z))
    modulus = np.ones((length_x, length_y, length_z))
    excluded = np.zeros((length_x, length_y, length_z), bool)
    for axis, length in enumerate((length_x, length_y, length_z)):
        wave = np.arange(length)
        shape = [1, 1, 1]
        shape[axis] = length
        total = total + ((np.minimum(wave, length - wave) / length) ** 2).reshape(shape)
        modulus = modulus * modulus_np(wave, length).reshape(shape)
        excluded = excluded | (wave * 2 == length).reshape(shape)
    excluded[0, 0, 0] = True
    safe = np.where(excluded, 1.0, total)
    result = np.exp(-(np.pi**2) / ewald_beta**2 * safe) / (
        np.pi * safe * np.where(excluded, 1.0, modulus)
    )
    return np.where(excluded, 0.0, result) / (length_x * length_y * length_z)


def slab_tables(rows_count, cols_count):
    grid_x = CX * rows_count
    grid_y = CY * cols_count
    devices = rows_count * cols_count
    chunk = KZ // devices
    wave_z = (np.arange(devices)[None, :] * chunk + np.arange(chunk)[:, None]).reshape(-1)
    along_z = cas_np(wave_z, np.arange(KZ), KZ)
    place_x = np.arange(rows_count)[:, None] * CX + np.arange(X_PAD)[None, :] - 2
    along_x = cas_np(np.arange(grid_x), place_x.reshape(-1) % grid_x, grid_x)
    x_high, x_low = halves_np(along_x)
    forward_x = np.concatenate([x_high, x_low, x_high], axis=1)
    backward_x = np.concatenate([x_high.T, x_low.T, x_high.T], axis=1)
    place_y = (np.arange(cols_count)[:, None] * CY + np.arange(Y_PAD)[None, :] - 2) % grid_y
    along_y = cas_np(np.arange(grid_y), place_y.reshape(-1), grid_y)
    along_y = along_y.reshape(grid_y, cols_count, Y_PAD)
    units = chunk * RHS // SPLIT
    block = np.einsum("uv,kcy->cuyvk", np.eye(units), along_y)
    block = block.reshape(cols_count * units * Y_PAD, units * grid_y)
    kernel = influence_np(grid_x, grid_y, KZ).reshape(grid_x, grid_y, devices, chunk)
    kernel = np.transpose(kernel, (2, 0, 3, 1))[:, :, :, None, :]
    kernel = np.broadcast_to(kernel, (devices, grid_x, chunk, RHS, grid_y))
    kernel = kernel.reshape(devices, grid_x, SPLIT, units * grid_y)
    kernel = np.moveaxis(kernel, 2, 1).reshape(devices, SPLIT * grid_x, units * grid_y)
    kernel = kernel.astype(np.float32)
    return dict(
        along_z=halves_np(along_z),
        forward_x=forward_x,
        backward_x=backward_x,
        block=halves_np(block),
        kernel=kernel,
    )


def pack_body(rhs_ref, place_ref, polar_ref, start_ref, payload_ref):
    polar = polar_ref[...]
    start = read_rows(rhs_ref) * polar
    start_ref[...] = start
    store_moments(payload_ref, start)
    place = [place_ref[dim] for dim in range(3)]
    fixed = jnp.concatenate(place + [1.0 / jnp.sqrt(polar)], axis=0)
    tile_count = fixed.shape[1] // TILE
    for tile in range(tile_count):
        first = tile_count * BLOCK + tile * FIXED
        payload_ref[first : first + FIXED, :] = fixed[:, tile * TILE : (tile + 1) * TILE]


def read_rows(rows_ref):
    return jnp.concatenate([rows_ref[dim] for dim in range(3)], axis=0)


def store_moments(payload_ref, moments):
    spare = jnp.zeros((BLOCK - moments.shape[0], TILE), jnp.float32)
    for tile in range(moments.shape[1] // TILE):
        payload_ref[tile * BLOCK : (tile + 1) * BLOCK, :] = jnp.concatenate(
            [moments[:, tile * TILE : (tile + 1) * TILE], spare], axis=0
        )


def placed_rows(slot, weights, extent):
    slot_index = lax.broadcasted_iota(jnp.int32, (extent, slot.shape[1]), 0)
    placed = jnp.zeros((extent, slot.shape[1]), jnp.float32)
    for stencil in range(5):
        target = slot + stencil
        if extent == KZ:
            target = jnp.where(target >= KZ, target - KZ, target)
        placed = placed + jnp.where(slot_index == target, weights[stencil], 0.0)
    return placed


def spread_into(message_ref, moment, rows_x, slope_x, rows_y, slope_y, depth, devices):
    blocks = []
    for step in range(X_PAD):
        flat_x = rows_x[step : step + 1]
        tilt_x = slope_x[step : step + 1]
        for rhs in range(RHS):
            part_x = tilt_x * moment[rhs : rhs + 1]
            part_y = flat_x * moment[RHS + rhs : RHS + rhs + 1]
            part_z = flat_x * moment[2 * RHS + rhs : 2 * RHS + rhs + 1]
            blocks.append(
                jnp.concatenate([part_x * rows_y + part_y * slope_y, part_z * rows_y], axis=1)
            )
    charges = jnp.concatenate(blocks, axis=0)
    spectrum = product(depth, halves(charges), 1, 1)
    slot_rows = message_ref.shape[0] // devices
    chunk = KZ // devices
    width = RHS * Y_PAD
    for step in range(X_PAD):
        message_ref[pl.ds(step, devices, stride=slot_rows), :] = jnp.concatenate(
            [
                spectrum[unit * devices : (unit + 1) * devices, step * width : (step + 1) * width]
                for unit in range(chunk)
            ],
            axis=1,
        )


def sample_from(message_ref, rows_x, slope_x, rows_y, slope_y, depth, devices):
    chunk = KZ // devices
    width = RHS * Y_PAD
    slot_rows = message_ref.shape[0] // devices
    pieces = [
        message_ref[pl.ds(step, devices, stride=slot_rows), :] for step in range(X_PAD)
    ]
    spare = jnp.zeros((devices, KZ - X_PAD * width), jnp.float32)
    spectrum = jnp.concatenate(
        [
            jnp.concatenate(
                [piece[:, unit * width : (unit + 1) * width] for piece in pieces] + [spare], axis=1
            )
            for unit in range(chunk)
        ],
        axis=0,
    )
    spectrum = jnp.transpose(spectrum)[: X_PAD * width]
    sampled = product(halves(spectrum), depth, 1, 0)
    atoms = rows_x.shape[1]
    fields = [None] * (3 * RHS)
    for rhs in range(RHS):
        sum_x = sum_y = sum_z = None
        for step in range(X_PAD):
            first = step * width + rhs * Y_PAD
            flat = sampled[first : first + Y_PAD, :atoms]
            tilt = sampled[first : first + Y_PAD, atoms:]
            part_x = slope_x[step : step + 1] * flat
            part_y = rows_x[step : step + 1] * flat
            part_z = rows_x[step : step + 1] * tilt
            sum_x = part_x if sum_x is None else sum_x + part_x
            sum_y = part_y if sum_y is None else sum_y + part_y
            sum_z = part_z if sum_z is None else sum_z + part_z
        fields[rhs] = jnp.sum(sum_x * rows_y, axis=0, keepdims=True)
        fields[RHS + rhs] = jnp.sum(sum_y * slope_y, axis=0, keepdims=True)
        fields[2 * RHS + rhs] = jnp.sum(sum_z * rows_y, axis=0, keepdims=True)
    return jnp.concatenate(fields, axis=0)


def read_tables(tables_ref):
    return (
        tables_ref[0:X_PAD],
        tables_ref[SLOT_ROWS : SLOT_ROWS + X_PAD],
        tables_ref[2 * SLOT_ROWS : 2 * SLOT_ROWS + Y_PAD],
        tables_ref[2 * SLOT_ROWS + Y_PAD : 2 * SLOT_ROWS + 2 * Y_PAD],
    )


def setup_body(
    lengths,
    devices,
    place_ref,
    base_ref,
    start_ref,
    z_high_ref,
    z_low_ref,
    message_ref,
    tables_ref,
    depth_high_ref,
    depth_low_ref,
):
    base = [base_ref[dim] for dim in range(3)]
    fractions = []
    cells = []
    for dim in range(3):
        cell = base[dim] + 2
        cell = jnp.where(cell >= lengths[dim], cell - lengths[dim], cell)
        cells.append(cell)
        fractions.append(place_ref[dim] - cell.astype(jnp.float32))
    values, slopes = spline_table(jnp.concatenate(fractions, axis=0))
    values = [[values[stencil][dim : dim + 1] for stencil in range(5)] for dim in range(3)]
    slopes = [[slopes[stencil][dim : dim + 1] for stencil in range(5)] for dim in range(3)]
    slot_x = lax.rem(cells[0], CX)
    slot_y = lax.rem(cells[1], CY)
    tables_ref[0:SLOT_ROWS] = placed_rows(slot_x, values[0], SLOT_ROWS)
    tables_ref[SLOT_ROWS : 2 * SLOT_ROWS] = placed_rows(slot_x, slopes[0], SLOT_ROWS)
    tables_ref[2 * SLOT_ROWS : 2 * SLOT_ROWS + Y_PAD] = placed_rows(slot_y, values[1], Y_PAD)
    tables_ref[2 * SLOT_ROWS + Y_PAD : 2 * SLOT_ROWS + 2 * Y_PAD] = placed_rows(
        slot_y, slopes[1], Y_PAD
    )
    window = jnp.concatenate(
        [
            placed_rows(base[2], values[2], KZ),
            placed_rows(base[2], slopes[2], KZ),
        ],
        axis=1,
    )
    depth = product((z_high_ref[...], z_low_ref[...]), halves(window), 1, 0)
    depth = halves(depth)
    depth_high_ref[...] = depth[0]
    depth_low_ref[...] = depth[1]
    spread_into(message_ref, start_ref[...], *read_tables(tables_ref), depth, devices)


def transform_in(message_ref, forward_ref, block_high_ref, block_low_ref, rows_count, cols_count):
    gathered = jnp.concatenate(
        [
            jnp.concatenate(
                [
                    message_ref[(r * cols_count + c) * X_PAD : (r * cols_count + c + 1) * X_PAD]
                    for r in range(rows_count)
                ],
                axis=0,
            )
            for c in range(cols_count)
        ],
        axis=1,
    )
    high, low = halves(gathered)
    along = jnp.dot(
        forward_ref[...],
        jnp.concatenate([high, high, low], axis=0),
        preferred_element_type=jnp.float32,
    )
    part = along.shape[1] // cols_count // SPLIT
    along = jnp.concatenate(
        [
            jnp.concatenate(
                [
                    along[:, (c * SPLIT + half) * part : (c * SPLIT + half + 1) * part]
                    for c in range(cols_count)
                ],
                axis=1,
            )
            for half in range(SPLIT)
        ],
        axis=0,
    )
    return product(halves(along), (block_high_ref[...], block_low_ref[...]))


def transform_out(result_ref, values, backward_ref, block_high_ref, block_low_ref, counts):
    rows_count, cols_count = counts
    spread = product(halves(values), (block_high_ref[...], block_low_ref[...]), 1, 1)
    grid_x = spread.shape[0] // SPLIT
    part = spread.shape[1] // cols_count
    spread = jnp.concatenate(
        [
            spread[half * grid_x : (half + 1) * grid_x, c * part : (c + 1) * part]
            for c in range(cols_count)
            for half in range(SPLIT)
        ],
        axis=1,
    )
    high, low = halves(spread)
    along = jnp.dot(
        backward_ref[...],
        jnp.concatenate([high, high, low], axis=0),
        preferred_element_type=jnp.float32,
    )
    width = along.shape[1] // cols_count
    slot_rows = result_ref.shape[0] // (rows_count * cols_count)
    for r in range(rows_count):
        for c in range(cols_count):
            first = (r * cols_count + c) * slot_rows
            result_ref[first : first + X_PAD, :] = along[
                r * X_PAD : (r + 1) * X_PAD, c * width : (c + 1) * width
            ]


def middle_first_body(
    counts,
    message_ref,
    kernel_ref,
    forward_ref,
    backward_ref,
    block_high_ref,
    block_low_ref,
    result_ref,
    wave_ref,
):
    wave = transform_in(message_ref, forward_ref, block_high_ref, block_low_ref, *counts)
    wave_ref[...] = wave
    transform_out(
        result_ref, wave * kernel_ref[...], backward_ref, block_high_ref, block_low_ref, counts
    )


def gather_rows(parts):
    tiles = [
        parts[BLOCK * tile : BLOCK * tile + BLOCK, :] for tile in range(parts.shape[0] // BLOCK)
    ]
    return jnp.concatenate(tiles, axis=1)[0 : 3 * RHS]


def row_total(value, rhs):
    row = lax.broadcasted_iota(jnp.int32, value.shape, 0)
    return total(jnp.where(lax.rem(row, RHS) == rhs, value, 0.0))


def total(value):
    return jnp.sum(jnp.sum(value, axis=0, keepdims=True), axis=1, keepdims=True)


def middle_second_body(
    counts,
    message_ref,
    kernel_ref,
    forward_ref,
    backward_ref,
    block_high_ref,
    block_low_ref,
    wave_ref,
    rhs_ref,
    start_ref,
    image_ref,
    second_ref,
    near_ref,
    polar_ref,
    result_ref,
):
    rhs_rows = read_rows(rhs_ref)
    near_rows = gather_rows(near_ref)
    wave = transform_in(message_ref, forward_ref, block_high_ref, block_low_ref, *counts)
    filtered = wave * kernel_ref[...]
    transform_out(result_ref, filtered, backward_ref, block_high_ref, block_low_ref, counts)
    before = wave_ref[...]
    grid_y = CY * counts[1]
    lane = lax.broadcasted_iota(jnp.int32, wave.shape, 1)
    own_rhs = lax.rem(lax.div(lane, grid_y), RHS)
    second = second_ref[...]
    start = start_ref[...]
    image = image_ref[...]
    local_part = second / polar_ref[...] - near_rows - self_coef * second
    slot = lax.broadcasted_iota(jnp.int32, (1, result_ref.shape[1]), 1)
    sums = jnp.zeros((1, result_ref.shape[1]), jnp.float32)
    for rhs in range(RHS):
        mine = own_rhs == rhs
        parts = (
            row_total(rhs_rows * start, rhs),
            row_total(start * image, rhs),
            row_total(second * image, rhs),
            row_total(start * local_part, rhs) + total(jnp.where(mine, before * filtered, 0.0)),
            row_total(second * local_part, rhs) + total(jnp.where(mine, wave * filtered, 0.0)),
        )
        for index, part in enumerate(parts):
            sums = jnp.where(slot == rhs * len(parts) + index, part, sums)
    devices = counts[0] * counts[1]
    result_ref[pl.ds(X_PAD, devices, stride=X_PAD + 1), :] = jnp.broadcast_to(
        sums, (devices, sums.shape[1])
    )


def sample_body(
    devices,
    message_ref,
    tables_ref,
    depth_high_ref,
    depth_low_ref,
    start_ref,
    near_ref,
    polar_ref,
    image_ref,
    second_ref,
    payload_ref,
):
    tables = read_tables(tables_ref)
    depth = (depth_high_ref[...], depth_low_ref[...])
    field = sample_from(message_ref, *tables, depth, devices)
    start = start_ref[...]
    polar = polar_ref[...]
    image = start / polar - gather_rows(near_ref) + field - self_coef * start
    second = polar * image
    image_ref[...] = image
    second_ref[...] = second
    store_moments(payload_ref, second)


def spread_body(
    devices,
    tables_ref,
    depth_high_ref,
    depth_low_ref,
    second_ref,
    result_ref,
):
    depth = (depth_high_ref[...], depth_low_ref[...])
    spread_into(result_ref, second_ref[...], *read_tables(tables_ref), depth, devices)


def final_body(
    devices,
    message_ref,
    tables_ref,
    depth_high_ref,
    depth_low_ref,
    rhs_ref,
    start_ref,
    image_ref,
    second_ref,
    near_ref,
    polar_ref,
    dipole_ref,
    residual_ref,
):
    tables = read_tables(tables_ref)
    depth = (depth_high_ref[...], depth_low_ref[...])
    field = sample_from(message_ref, *tables, depth, devices)
    second = second_ref[...]
    start = start_ref[...]
    image = image_ref[...]
    image_second = second / polar_ref[...] - gather_rows(near_ref) + field - self_coef * second
    sums = jnp.sum(
        message_ref[pl.ds(X_PAD, devices, stride=X_PAD + 1), :], axis=0, keepdims=True
    )
    steps = []
    for rhs in range(RHS):
        progress, start_image, second_image, start_next, second_next = [
            sums[:, rhs * 5 + index : rhs * 5 + index + 1] for index in range(5)
        ]
        step = progress / start_image
        progress_next = progress - 2.0 * step * start_image + step * step * second_image
        grown = 1.0 + progress_next / progress
        curvature = (
            grown * grown * start_image
            - step * grown * (start_next + second_image)
            + step * step * second_next
        )
        steps.append((step, grown, progress_next / curvature))
    row = lax.broadcasted_iota(jnp.int32, (RHS, 1), 0)
    step, grown, step_next = [
        sum(jnp.where(row == rhs, steps[rhs][index], 0.0) for rhs in range(RHS))
        for index in range(3)
    ]
    for dim in range(3):
        rows = slice(dim * RHS, (dim + 1) * RHS)
        direction = grown * start[rows] - step * second[rows]
        image_direction = grown * image[rows] - step * image_second[rows]
        dipole_ref[dim] = step * start[rows] + step_next * direction
        residual_ref[dim] = rhs_ref[dim] - step * image[rows] - step_next * image_direction


def block_rows(entry):
    return pl.ds(pl.multiple_of(entry * BLOCK, BLOCK), BLOCK)


def nearest(places, origin, span):
    return places - span * jnp.floor((places - origin) / span + 0.5)


def row_index(shape):
    return lax.broadcasted_iota(jnp.int32, shape, 0)


def fill_first(near_fixed, near_moment, sources, tile_count, spans):
    rows = sources[0].shape[0] // 3
    near_fixed[...] = jnp.zeros_like(near_fixed)
    for row_step, source in enumerate(sources):
        for col_step in range(3):
            brick = row_step * 3 + col_step
            first = col_step * rows
            near_moment[brick * tile_count * BLOCK : (brick + 1) * tile_count * BLOCK, :] = source[
                first : first + tile_count * BLOCK, :
            ]
            for tile in range(tile_count):
                place = (brick * tile_count + tile) * BLOCK
                begin = first + tile_count * BLOCK + tile * FIXED
                near_fixed[place : place + FIXED, :] = source[begin : begin + FIXED, :]
    own = 4 * tile_count * BLOCK
    origin = near_fixed[own : own + BLOCK, 0:1]
    row = row_index((BLOCK, 1))
    span = jnp.where(row == 0, spans[0], jnp.where(row == 1, spans[1], 1.0e30))
    for entry in range(9 * tile_count):
        place = slice(entry * BLOCK, (entry + 1) * BLOCK)
        near_fixed[place, :] = nearest(near_fixed[place, :], origin, span)


def thirds(value):
    high = value.astype(jnp.bfloat16).astype(jnp.float32)
    rest = value - high
    middle = rest.astype(jnp.bfloat16).astype(jnp.float32)
    return high, middle, rest - middle


def prepare(tile, tile_count, lists_ref, span, near_fixed, near_moment, scratch, quantities):
    picked, wide, square, own_side, near_side, moment_high, moment_low = scratch
    own = near_fixed[block_rows(4 * tile_count + tile), :]
    origin = own[:, 0:1]
    square[0:BLOCK, :] = own
    columns = jnp.transpose(square[...])
    for quantity in range(quantities):
        wide[quantity * TILE : (quantity + 1) * TILE, :] = jnp.broadcast_to(
            columns[:, quantity : quantity + 1], (TILE, TILE)
        )
    row = row_index((BLOCK, TILE))
    local_own = own - origin
    doubled = jnp.concatenate(
        [local_own[dim : dim + 1] for dim in range(3) for _ in range(RHS)]
        + [jnp.zeros((BLOCK - 3 * RHS, TILE), jnp.float32)],
        axis=0,
    )
    high, middle, low = thirds(doubled)
    sides = []
    for rhs in range(RHS):
        mine = lax.rem(row, RHS) == rhs
        one = jnp.where(row == 3 * RHS + rhs, 1.0, 0.0)
        first, second, third = [jnp.where(mine, -part, 0.0) for part in (high, middle, low)]
        sides.append(
            jnp.concatenate([first + one, second, third, first + one, second, first + one], axis=0)
        )
    own_side[...] = jnp.concatenate(sides, axis=1).astype(jnp.bfloat16)
    span_rows = jnp.where(row_index((BLOCK, 1)) == 2, span, 1.0e30)
    spare = jnp.zeros((BLOCK, TILE), jnp.float32)
    for entry in range(lists_ref.shape[1]):
        listing = lists_ref[tile, entry]
        fixed = nearest(near_fixed[block_rows(listing), :], origin, span_rows)
        for quantity in range(quantities):
            first = (entry * quantities + quantity) * GROUP
            picked[first : first + GROUP, :] = jnp.broadcast_to(
                fixed[quantity : quantity + 1], (GROUP, TILE)
            )
        moment = near_moment[block_rows(listing), :]
        local = fixed - origin
        offset = sum(
            moment[RHS * dim : RHS * dim + RHS] * local[dim : dim + 1] for dim in range(3)
        )
        high, middle, low = thirds(jnp.concatenate([moment[0 : 3 * RHS], offset], axis=0))
        near_side[entry * DEPTH : (entry + 1) * DEPTH, :] = jnp.concatenate(
            [high, high, high, middle, middle, low], axis=0
        ).astype(jnp.bfloat16)
        lanes = slice(entry * TILE, (entry + 1) * TILE)
        moment_high[:, lanes] = jnp.concatenate([high, spare], axis=0).astype(jnp.bfloat16)
        moment_low[:, lanes] = jnp.concatenate([middle, spare], axis=0).astype(jnp.bfloat16)


def project(projected, own_side, near_side, entries):
    side = own_side[...]
    for entry in range(entries):
        projected[entry * RHS * TILE : (entry + 1) * RHS * TILE, :] = lax.dot_general(
            side,
            near_side[entry * DEPTH : (entry + 1) * DEPTH, :],
            (((0,), (0,)), ((), ())),
            preferred_element_type=jnp.float32,
        )


def add_outward(sums, second_term, apart, projected):
    for rhs in range(RHS):
        weighted = second_term * projected[rhs]
        for dim in range(3):
            index = RHS * dim + rhs
            sums[index] = sums[index] + weighted * apart[dim]


def finish_sums(field_ref, sums_ref, high_ref, low_ref, moment_high, moment_low, entries):
    def lines(source):
        return jnp.concatenate(
            [source[entry * TILE : (entry + 1) * TILE, :] for entry in range(entries)], axis=1
        )

    high = lines(high_ref)
    near = (moment_high[...], moment_low[...])
    inward = product((high, lines(low_ref)), near, 1, 1)
    lane = lax.broadcasted_iota(jnp.int32, (TILE, TILE), 1)
    merged = jnp.zeros((TILE, TILE), jnp.float32)
    for index in range(3 * RHS):
        column = jnp.sum(sums_ref[index * TILE : (index + 1) * TILE, :], axis=1, keepdims=True)
        merged = jnp.where(lane == index, column - inward[:, index : index + 1], merged)
    field_ref[...] = jnp.transpose(merged)[0:BLOCK]


def wide_rows(start, quantity):
    return pl.ds(pl.multiple_of(quantity * TILE + start, GROUP), GROUP)


def pair_terms(square_dist, damp):
    inverse = lax.rsqrt(square_dist)
    distance = square_dist * inverse
    inverse_sq = inverse * inverse
    inverse_cube = inverse_sq * inverse
    cubed = damp * (distance * square_dist)
    damping = jnp.exp(cubed)
    bell = jnp.exp(-(ewald_beta * ewald_beta) * square_dist)
    stretched = 1.0 + (SCREEN_SCALE * ewald_beta) * distance
    turned = pl.reciprocal(stretched, approx=True)
    turned = turned * (2.0 - stretched * turned)
    series = SCREEN_COEF[-1] * turned + SCREEN_COEF[-2]
    for coef in SCREEN_COEF[-3::-1]:
        series = series * turned + coef
    screen = bell * turned * series
    gaussian = (2.0 * ewald_beta / math.sqrt(math.pi)) * bell
    bare = screen - damping
    first_term = bare * inverse_cube + gaussian * inverse_sq
    second_term = (
        3.0 * (first_term + (cubed * damping) * inverse_cube)
        + (2.0 * ewald_beta * ewald_beta) * gaussian
    ) * inverse_sq
    return first_term, second_term


def pair_first_body(
    first_tile,
    tile_count,
    spans,
    lists_ref,
    up_ref,
    stack_ref,
    down_ref,
    *others,
):
    high_ref, low_ref, second_ref, field_ref, near_ref = others[-15:-10]
    near_moment, sums_ref, projected_ref = others[-10:-7]
    scratch = others[-7:]
    picked, wide, square, own_side, near_side, moment_high, moment_low = scratch

    @pl.when(pl.program_id(0) == 0)
    def _():
        fill_first(near_ref, near_moment, (up_ref, stack_ref, down_ref), tile_count, spans)
        square[...] = jnp.zeros_like(square)

    tile = first_tile + pl.program_id(0)
    entries = lists_ref.shape[1]
    prepare(tile, tile_count, lists_ref, spans[2], near_ref, near_moment, scratch, FIXED)
    project(projected_ref, own_side, near_side, entries)

    @pl.loop(0, TILE // PAIR_ROWS)
    def _(part):
        for group in range(PAIR_ROWS // GROUP):
            start = part * PAIR_ROWS + group * GROUP
            own = [wide[wide_rows(start, dim), :] for dim in range(FIXED)]
            own_damp = -thole_a * own[3]
            sums = [jnp.zeros((GROUP, TILE), jnp.float32) for _ in range(3 * RHS)]
            itself = (row_index((GROUP, TILE)) + start) == lax.broadcasted_iota(
                jnp.int32, (GROUP, TILE), 1
            )
            for entry in range(entries):
                rows = [
                    picked[(entry * FIXED + index) * GROUP : (entry * FIXED + index + 1) * GROUP, :]
                    for index in range(FIXED)
                ]
                apart = [rows[dim] - own[dim] for dim in range(3)]
                square_dist = apart[0] * apart[0] + apart[1] * apart[1] + apart[2] * apart[2]
                if entry == 0:
                    square_dist = jnp.where(itself, 1.0, square_dist)
                first_term, second_term = pair_terms(square_dist, own_damp * rows[3])
                if entry == 0:
                    first_term = jnp.where(itself, 0.0, first_term)
                    second_term = jnp.where(itself, 0.0, second_term)
                place = wide_rows(start, entry)
                high, low = halves(first_term)
                high_ref[place, :] = high
                low_ref[place, :] = low
                second_ref[place, :] = second_term
                projected = [
                    projected_ref[wide_rows(start, entry * RHS + rhs), :] for rhs in range(RHS)
                ]
                add_outward(sums, second_term, apart, projected)
            for index, value in enumerate(sums):
                sums_ref[wide_rows(start, index), :] = value

    finish_sums(field_ref, sums_ref, high_ref, low_ref, moment_high, moment_low, entries)


def pair_second_body(
    tile_count,
    spans,
    lists_ref,
    near_ref,
    up_ref,
    stack_ref,
    down_ref,
    high_ref,
    low_ref,
    second_ref,
    field_ref,
    near_moment,
    sums_ref,
    projected_ref,
    *scratch,
):
    picked, wide, square, own_side, near_side, moment_high, moment_low = scratch

    @pl.when(pl.program_id(0) == 0)
    def _():
        rows = stack_ref.shape[0]
        for row_step, source in enumerate((up_ref, stack_ref, down_ref)):
            near_moment[row_step * rows : (row_step + 1) * rows, :] = source[...]
        square[...] = jnp.zeros_like(square)

    tile = pl.program_id(0)
    entries = lists_ref.shape[1]
    prepare(tile, tile_count, lists_ref, spans[2], near_ref, near_moment, scratch, 3)
    project(projected_ref, own_side, near_side, entries)

    @pl.loop(0, TILE // PAIR_ROWS)
    def _(part):
        for group in range(PAIR_ROWS // GROUP):
            start = part * PAIR_ROWS + group * GROUP
            own = [wide[wide_rows(start, dim), :] for dim in range(3)]
            sums = [jnp.zeros((GROUP, TILE), jnp.float32) for _ in range(3 * RHS)]
            for entry in range(entries):
                apart = [
                    picked[(entry * 3 + dim) * GROUP : (entry * 3 + dim + 1) * GROUP, :] - own[dim]
                    for dim in range(3)
                ]
                projected = [
                    projected_ref[wide_rows(start, entry * RHS + rhs), :] for rhs in range(RHS)
                ]
                add_outward(sums, second_ref[wide_rows(start, entry), :], apart, projected)
            for index, value in enumerate(sums):
                sums_ref[wide_rows(start, index), :] = value

    finish_sums(field_ref, sums_ref, high_ref, low_ref, moment_high, moment_low, entries)


def shift(source, axis, step):
    count = lax.axis_size(axis)
    return lax.ppermute(source, axis, [(i, (i + step) % count) for i in range(count)])


def both_ways(source, axis):
    return shift(source, axis, 1), source, shift(source, axis, -1)


def whole(shape):
    return pl.BlockSpec(shape, lambda *_: (0,) * len(shape))


def anywhere():
    return pl.BlockSpec(memory_space=pl.ANY)


def join(message, payload):
    left, _, right = both_ways(payload, "col")
    message, left, right = lax.optimization_barrier((message, left, right))
    return message, both_ways(jnp.concatenate([left, payload, right], axis=0), "row")


class Fetched:
    def __init__(self, source, scratch, semaphore):
        self.copy = pltpu.make_async_copy(source, scratch, semaphore)
        self.copy.start()
        self.scratch = scratch
        self.shape = scratch.shape
        self.waiting = True

    def wait(self):
        if self.waiting:
            self.copy.wait()
            self.waiting = False

    def __getitem__(self, index):
        self.wait()
        return self.scratch[index]


def call(body, outs, *operands, after=(), own_block=None, near=0, vmem=VMEM_LIMIT):
    fetched = [
        pltpu.VMEM(operand.shape[1:] if index == own_block else operand.shape, operand.dtype)
        for index, operand in enumerate(operands)
        if index >= near
    ]
    count = len(operands)

    def run(*refs):
        refs = refs[len(after) :]
        sources, refs = refs[:count], refs[count:]
        results, refs = refs[: len(outs)], refs[len(outs) :]
        targets = sources[:near] + refs[: count - near]
        written, semaphore = refs[count - near : -1], refs[-1]
        inputs = []
        for index, source in enumerate(sources):
            if index < near:
                inputs.append(source)
                continue
            if index == own_block:
                place = lax.axis_index("row") * lax.axis_size("col") + lax.axis_index("col")
                source = source.at[place]
            inputs.append(Fetched(source, targets[index], semaphore.at[index]))
        body(*inputs, *written)
        for operand in inputs[near:]:
            operand.wait()
        copies = [
            pltpu.make_async_copy(value, result, semaphore.at[count + index])
            for index, (value, result) in enumerate(zip(written, results))
        ]
        for copy in copies:
            copy.start()
        for copy in copies:
            copy.wait()

    return pl.pallas_call(
        run,
        in_specs=[anywhere()] * len(after)
        + [pl.BlockSpec(memory_space=pltpu.VMEM)] * near
        + [anywhere()] * (count - near),
        out_specs=[anywhere()] * len(outs),
        out_shape=[jax.ShapeDtypeStruct(shape, dtype) for shape, dtype in outs],
        scratch_shapes=fetched
        + [pltpu.VMEM(shape, dtype) for shape, dtype in outs]
        + [pltpu.SemaphoreType.DMA((count + len(outs),))],
        compiler_params=pltpu.CompilerParams(vmem_limit_bytes=vmem),
        cost_estimate=pl.CostEstimate(
            flops=200_000_000, bytes_accessed=4 << 20, transcendentals=0
        ),
    )(*after, *operands)


def final_call(body, outs, *operands):
    return pl.pallas_call(
        body,
        grid=(1,),
        in_specs=[whole(operand.shape) for operand in operands],
        out_specs=[whole(shape) for shape, _ in outs],
        out_shape=[jax.ShapeDtypeStruct(shape, dtype) for shape, dtype in outs],
        compiler_params=pltpu.CompilerParams(vmem_limit_bytes=SMALL_VMEM_LIMIT),
    )(*operands)


def pair_call(body, outs, kept, first_tile, last_tile, blocked, scratch, lists, *operands, after=()):
    tiles = lists.shape[0]

    def block(operand):
        rows = operand.shape[0] // tiles
        return pl.BlockSpec((rows, operand.shape[1]), lambda i, s: (first_tile + i, 0))

    out_shape = [jax.ShapeDtypeStruct(shape, dtype) for shape, dtype in outs + kept]
    plain = len(operands) - blocked
    aliases = {}
    if first_tile > 0:
        first = 1 + len(operands) + len(after) - len(outs)
        aliases = {first + index: index for index in range(len(outs))}
    return pl.pallas_call(
        body,
        out_shape=out_shape,
        grid_spec=pltpu.PrefetchScalarGridSpec(
            num_scalar_prefetch=1,
            grid=(last_tile - first_tile,),
            in_specs=[whole(operand.shape) for operand in operands[:plain]]
            + [block(operand) for operand in operands[plain:]]
            + [anywhere()] * len(after),
            out_specs=[block(shape) for shape in out_shape[: len(outs)]]
            + [whole(shape) for shape, _ in kept],
            scratch_shapes=[pltpu.VMEM(shape, dtype) for shape, dtype in scratch],
        ),
        input_output_aliases=aliases,
        compiler_params=pltpu.CompilerParams(vmem_limit_bytes=VMEM_LIMIT),
        cost_estimate=pl.CostEstimate(
            flops=80_000_000, bytes_accessed=8 << 20, transcendentals=1 << 21
        ),
    )(lists, *operands, *after)


def exchange(message, devices):
    shape = message.shape
    sent = message.reshape(devices, 1, -1)
    return lax.all_to_all(sent, ("row", "col"), split_axis=0, concat_axis=0, tiled=True).reshape(
        shape
    )


def slab_local(field_rhs, positions, polar, grid_base, tile_lists):
    rows_count = lax.axis_size("row")
    cols_count = lax.axis_size("col")
    counts = (rows_count, cols_count)
    devices = rows_count * cols_count
    lengths = (CX * rows_count, CY * cols_count, KZ)
    spans = tuple(float(length) for length in lengths)
    atoms = polar.shape[-1]
    tile_count = atoms // TILE
    listed = tile_lists.shape[-1]
    tables = slab_tables(rows_count, cols_count)
    f32 = jnp.float32
    rhs = jnp.swapaxes(field_rhs[0, 0], 0, 1)
    place = jnp.swapaxes(positions[0], 0, 1)
    base = jnp.swapaxes(grid_base[0], 0, 1)
    polar = polar.reshape(1, atoms)
    lists = tile_lists[0, 0]
    payload_shape = (tile_count * (BLOCK + FIXED), TILE)
    moment_shape = (tile_count * BLOCK, TILE)
    near_shape = (9 * tile_count * BLOCK, TILE)
    term_shape = (tile_count * listed * TILE, TILE)
    bf16 = jnp.bfloat16

    def pair_scratch(quantities):
        return [
            (near_shape, f32),
            ((3 * RHS * TILE, TILE), f32),
            ((listed * RHS * TILE, TILE), f32),
            ((listed * quantities * GROUP, TILE), f32),
            ((quantities * TILE, TILE), f32),
            ((TILE, TILE), f32),
            ((DEPTH, RHS * TILE), bf16),
            ((listed * DEPTH, TILE), bf16),
            ((2 * BLOCK, listed * TILE), bf16),
            ((2 * BLOCK, listed * TILE), bf16),
        ]

    message_shape = (devices * X_PAD, KZ // devices * RHS * Y_PAD)
    last_shape = (devices * (X_PAD + 1), message_shape[1])
    row_shape = (3 * RHS, atoms)

    start, payload = call(pack_body, [(row_shape, f32), (payload_shape, f32)], rhs, place, polar)

    def setup(*refs):
        setup_body(lengths, devices, *refs)

    message, splines, depth_high, depth_low = call(
        setup,
        [
            (message_shape, f32),
            ((2 * SLOT_ROWS + 2 * Y_PAD, atoms), f32),
            ((KZ, 2 * atoms), jnp.bfloat16),
            ((KZ, 2 * atoms), jnp.bfloat16),
        ],
        place,
        base,
        start,
        *[jnp.asarray(table) for table in tables["along_z"]],
    )
    constants = (
        jnp.asarray(tables["kernel"]),
        jnp.asarray(tables["forward_x"]),
        jnp.asarray(tables["backward_x"]),
        *[jnp.asarray(table) for table in tables["block"]],
    )
    message, near = join(message, payload)
    arrived = exchange(message, devices)

    def pair_first(first_tile, last_tile, *after):
        def body(*refs):
            pair_first_body(first_tile, tile_count, spans, *refs)

        return pair_call(
            body,
            [(term_shape, bf16), (term_shape, bf16), (term_shape, f32), (moment_shape, f32)],
            [(near_shape, f32)],
            first_tile,
            last_tile,
            0,
            pair_scratch(FIXED),
            lists,
            *near,
            after=after,
        )

    early = pair_first(0, EARLY_TILES, message)

    def middle_first(*refs):
        middle_first_body(counts, *refs)

    mixed, wave = call(
        middle_first,
        [(message_shape, f32), (tables["kernel"].shape[1:], f32)],
        arrived,
        *constants,
        after=(early[3],),
        own_block=1,
    )
    returned = exchange(mixed, devices)
    *terms, direct, near = pair_first(EARLY_TILES, tile_count, wave, *early[:4])

    def sample(*refs):
        sample_body(devices, *refs)

    image, second, moments = call(
        sample,
        [(row_shape, f32), (row_shape, f32), (moment_shape, f32)],
        returned,
        splines,
        depth_high,
        depth_low,
        start,
        direct,
        polar,
    )

    def spread(*refs):
        spread_body(devices, *refs)

    (message,) = call(spread, [(message_shape, f32)], splines, depth_high, depth_low, second)
    message, near_moments = join(message, moments)
    arrived = exchange(message, devices)

    def pair_second(*refs):
        pair_second_body(tile_count, spans, *refs)

    (direct,) = pair_call(
        pair_second,
        [(moment_shape, f32)],
        [],
        0,
        tile_count,
        3,
        pair_scratch(3),
        lists,
        near,
        *near_moments,
        *terms,
    )

    def middle_second(*refs):
        middle_second_body(counts, *refs)

    (mixed,) = call(
        middle_second,
        [(last_shape, f32)],
        arrived,
        *constants,
        wave,
        rhs,
        start,
        image,
        second,
        direct,
        polar,
        own_block=1,
    )
    returned = exchange(mixed, devices)

    def final(*refs):
        final_body(devices, *refs)

    outs = final_call(
        final,
        [(rhs.shape, f32), (rhs.shape, f32)],
        returned,
        splines,
        depth_high,
        depth_low,
        rhs,
        start,
        image,
        second,
        direct,
        polar,
    )
    return tuple(jnp.swapaxes(out, 0, 1)[None, None] for out in outs)


def solution(mesh):
    placed = (
        P("row", "col", None, None, None),
        P("row", "col", None, None),
        P("row", "col", None),
        P("row", "col", None, None),
        P("row", "col", None, None),
    )
    devices = mesh.shape["row"] * mesh.shape["col"]
    return jax.shard_map(
        slab_local if KZ % devices == 0 else pencil_local,
        mesh=mesh,
        in_specs=placed,
        out_specs=(P("row", "col", None, None, None), P("row", "col", None, None, None)),
        check_vma=False,
    )
```

```python
import math

import jax
import jax.numpy as jnp
import ml_dtypes
import numpy as np
from jax import lax
from jax.experimental import pallas as pl
from jax.experimental.pallas import tpu as pltpu
from jax.sharding import PartitionSpec as P

CX = 8
CY = 4
KZ = 256
TILE = 128
RHS = 2
ITERS = 2


ewald_beta = 0.4
thole_a = 0.39
self_coef = 4.0 * ewald_beta**3 / (3.0 * math.sqrt(math.pi))
highest = lax.Precision.HIGHEST


def with_halo(cells, sides, width):
    for axis, dim in sides:
        count = lax.axis_size(axis)
        head = lax.slice_in_dim(cells, 0, width, axis=dim)
        tail = lax.slice_in_dim(cells, cells.shape[dim] - width, cells.shape[dim], axis=dim)
        cells = jnp.concatenate(
            [
                lax.ppermute(tail, axis, [(i, (i + 1) % count) for i in range(count)]),
                cells,
                lax.ppermute(head, axis, [((i + 1) % count, i) for i in range(count)]),
            ],
            axis=dim,
        )
    return cells


def spline_table(fraction):
    previous = {0: jnp.ones_like(fraction)}
    fourth = previous
    for degree in range(2, 6):
        current = {}
        for offset in range(degree):
            abscissa = fraction + offset
            summed = abscissa * previous.get(offset, 0.0) + (degree - abscissa) * previous.get(
                offset - 1, 0.0
            )
            current[offset] = summed / (degree - 1)
        if degree == 4:
            fourth = current
        previous = current
    values = jnp.stack([previous[4 - stencil] for stencil in range(5)])
    slopes = jnp.stack(
        [fourth.get(4 - stencil, 0.0) - fourth.get(3 - stencil, 0.0) for stencil in range(5)]
    )
    return (values, slopes)


def spline_modulus(wave_index, length):
    spline_coef = (1.0 / 24.0, 11.0 / 24.0, 11.0 / 24.0, 1.0 / 24.0)
    cosine_sum = jnp.zeros(wave_index.shape, jnp.float32)
    sine_sum = jnp.zeros(wave_index.shape, jnp.float32)
    for offset in range(4):
        angles = 2.0 * math.pi / length * (wave_index * offset % length).astype(jnp.float32)
        cosine_sum = cosine_sum + spline_coef[offset] * jnp.cos(angles)
        sine_sum = sine_sum + spline_coef[offset] * jnp.sin(angles)
    return cosine_sum * cosine_sum + sine_sum * sine_sum


def folded_square(wave_index, length):
    nearest = jnp.minimum(wave_index, length - wave_index).astype(jnp.float32) / length
    return nearest * nearest


def influence(wave_x, wave_y, wave_z, length_x, length_y, length_z):
    wave_norm = (
        folded_square(wave_x, length_x)
        + folded_square(wave_y, length_y)
        + folded_square(wave_z, length_z)
    )
    modulus = (
        spline_modulus(wave_x, length_x)
        * spline_modulus(wave_y, length_y)
        * spline_modulus(wave_z, length_z)
    )
    excluded = (wave_x * 2 == length_x) | (wave_y * 2 == length_y) | (wave_z * 2 == length_z)
    excluded = excluded | (wave_x == 0) & (wave_y == 0) & (wave_z == 0)
    safe_norm = jnp.where(excluded, 1.0, wave_norm)
    safe_modulus = jnp.where(excluded, 1.0, modulus)
    result = jnp.exp(-(math.pi**2 / ewald_beta**2) * safe_norm) / (
        math.pi * safe_norm * safe_modulus
    )
    return jnp.where(excluded, 0.0, result)


def tile_field(own_static, near_static, near_dipole, box_spans):
    listed_count = near_static.shape[0]
    tile_width = own_static.shape[1]
    box_span = jnp.array(box_spans, dtype=jnp.float32)[None, :, None, None]
    separation = near_static[:, 0:3, None, :] - own_static[None, 0:3, :, None]
    separation = separation - box_span * jnp.floor(separation / box_span + 0.5)
    dist_sq = jnp.sum(separation * separation, axis=1)
    itself = (jnp.arange(listed_count)[:, None, None] == 0) & (
        jnp.arange(tile_width)[:, None] == jnp.arange(tile_width)[None, :]
    )[None]
    safe_sq = jnp.where(itself, 1.0, dist_sq)
    distance = jnp.sqrt(safe_sq)
    scaled = distance / (own_static[3][None, :, None] * near_static[:, 3][:, None, :])
    cubed = thole_a * scaled * scaled * scaled
    damping = jnp.exp(-cubed)
    screen = lax.erfc(ewald_beta * distance)
    gaussian = 2.0 * ewald_beta / math.sqrt(math.pi) * jnp.exp(-(ewald_beta * ewald_beta) * safe_sq)
    inverse_sq = 1.0 / safe_sq
    inverse_cube = inverse_sq / distance
    first_term = (screen - damping) * inverse_cube + gaussian * inverse_sq
    second = (
        3.0 * (screen - (1.0 + cubed) * damping) * inverse_cube * inverse_sq
        + gaussian * (2.0 * ewald_beta * ewald_beta + 3.0 * inverse_sq) * inverse_sq
    )
    first_term = jnp.where(itself, 0.0, first_term)
    second = jnp.where(itself, 0.0, second)
    projected = jnp.sum(near_dipole[:, :, :, None, :] * separation[:, None, :, :, :], axis=2)
    weighted = second[:, None] * projected
    outward = jnp.sum(weighted[:, :, None] * separation[:, None], axis=(0, 4))
    inward = jnp.sum(first_term[:, None, None] * near_dipole[:, :, :, None, :], axis=(0, 4))
    return outward - inward


def hartley(length):
    counter = jnp.arange(length, dtype=jnp.int32)
    angles = (
        2.0 * math.pi / length * (counter[:, None] * counter[None, :] % length).astype(jnp.float32)
    )
    return jnp.cos(angles) + jnp.sin(angles)


def placed_table(first_cell, weights, extent):
    slot_index = jnp.arange(extent, dtype=jnp.int32)[:, None]
    placed = jnp.zeros((extent, first_cell.shape[0]), jnp.float32)
    for stencil in range(5):
        placed = placed + jnp.where(
            slot_index == (first_cell[None, :] + stencil) % extent, weights[stencil][None, :], 0.0
        )
    return placed


def pad_axis(source, axis_pos, leading, trailing):
    widths = [(0, 0)] * source.ndim
    widths[axis_pos] = (leading, trailing)
    return jnp.pad(source, widths)


def fold_cycle(cycle_only, axis_pos, inner_len):
    middle = lax.slice_in_dim(cycle_only, 4, inner_len + 4, axis=axis_pos)
    lower_cycle = lax.slice_in_dim(cycle_only, 0, 2, axis=axis_pos)
    upper_cycle = lax.slice_in_dim(cycle_only, inner_len + 6, inner_len + 8, axis=axis_pos)
    return (
        middle
        + pad_axis(lower_cycle, axis_pos, 0, inner_len - 2)
        + pad_axis(upper_cycle, axis_pos, inner_len - 2, 0)
    )


def clear_inside(extended, extents):
    inside = None
    for axis_pos, inner_len in extents:
        slot_index = lax.broadcasted_iota(jnp.int32, extended.shape, axis_pos)
        within = (slot_index >= 2) & (slot_index < inner_len + 6)
        inside = within if inside is None else inside & within
    return jnp.where(inside, 0.0, extended)


def inner_sum(left_arr, right_arr):
    return lax.psum(jnp.sum(left_arr * right_arr, axis=(1, 2)), ("row", "col"))


def pencil_local(field_rhs, positions, polar, grid_base, tile_lists):
    rows_count = lax.axis_size("row")
    cols_count = lax.axis_size("col")
    grid_x = CX * rows_count
    grid_y = CY * cols_count
    atom_count = polar.shape[-1]
    tile_count = atom_count // TILE
    slab_depth = KZ // tile_count
    window_len = slab_depth + 4
    box_spans = (float(grid_x), float(grid_y), float(KZ))
    own_place = positions[0, 0]
    own_base = grid_base[0, 0]
    own_polar = polar[0, 0]
    lengths = jnp.array([grid_x, grid_y, KZ], dtype=jnp.int32)[:, None]
    cell_index = (own_base + 2) % lengths
    fraction = own_place - cell_index.astype(jnp.float32)
    values, slopes = spline_table(fraction)
    first_x = (own_base[0] - lax.axis_index("row") * CX + 2) % grid_x
    first_y = (own_base[1] - lax.axis_index("col") * CY + 2) % grid_y
    rows_x = placed_table(first_x, values[:, 0], CX + 4)
    slope_x = placed_table(first_x, slopes[:, 0], CX + 4)
    rows_y = placed_table(first_y, values[:, 1], CY + 4)
    slope_y = placed_table(first_y, slopes[:, 1], CY + 4)
    tile_start = jnp.arange(atom_count, dtype=jnp.int32) // TILE * slab_depth
    first_z = (own_base[2] + 2 - tile_start) % KZ
    rows_z = placed_table(first_z, values[:, 2], window_len)
    slope_z = placed_table(first_z, slopes[:, 2], window_len)
    plane_count = (CX + 4) * (CY + 4)
    plane_dx = (slope_x[:, None, :] * rows_y[None, :, :]).reshape(plane_count, atom_count)
    plane_dy = (rows_x[:, None, :] * slope_y[None, :, :]).reshape(plane_count, atom_count)
    plane_flat = (rows_x[:, None, :] * rows_y[None, :, :]).reshape(plane_count, atom_count)
    window_rows = jnp.moveaxis(rows_z.reshape(window_len, tile_count, TILE), 1, 0)
    window_slope = jnp.moveaxis(slope_z.reshape(window_len, tile_count, TILE), 1, 0)
    depth_table = jnp.concatenate([window_rows, window_slope], axis=2)
    grid_scale = 1.0 / (grid_x * grid_y * KZ)
    hartley_x = hartley(grid_x)
    hartley_y = hartley(grid_y)
    hartley_z = hartley(KZ)
    block_y = grid_y // rows_count
    block_z = KZ // cols_count
    wave_x = jnp.arange(grid_x, dtype=jnp.int32)[:, None, None]
    wave_y = (lax.axis_index("row") * block_y + jnp.arange(block_y, dtype=jnp.int32))[None, :, None]
    wave_z = (lax.axis_index("col") * block_z + jnp.arange(block_z, dtype=jnp.int32))[None, None, :]
    kernel = influence(wave_x, wave_y, wave_z, grid_x, grid_y, KZ) * grid_scale
    root_scale = jnp.power(own_polar, 1.0 / 6.0)
    own_static = jnp.concatenate([own_place, root_scale[None]], axis=0)
    near_static = with_halo(own_static[None, None], (("row", 0), ("col", 1)), 1)
    near_static = jnp.moveaxis(near_static.reshape(9, 4, tile_count, TILE), 2, 1).reshape(
        9 * tile_count, 4, TILE
    )
    own_tiles = jnp.moveaxis(own_static.reshape(4, tile_count, TILE), 1, 0)
    own_lists = tile_lists[0, 0]
    polar_wide = own_polar[None, None, :]
    solution = jnp.zeros_like(field_rhs[0, 0])
    residual = field_rhs[0, 0]
    scaled_res = polar_wide * residual
    direction = scaled_res
    progress = inner_sum(residual, scaled_res)
    for iteration in range(ITERS):
        near_dip = with_halo(direction[None, None], (("row", 0), ("col", 1)), 1)
        near_dip = jnp.moveaxis(near_dip.reshape(9, RHS, 3, tile_count, TILE), 3, 1).reshape(
            9 * tile_count, RHS, 3, TILE
        )

        def one_tile(tile_pos):
            picked = own_lists[tile_pos]
            return tile_field(own_tiles[tile_pos], near_static[picked], near_dip[picked], box_spans)

        fields = lax.map(one_tile, jnp.arange(tile_count, dtype=jnp.int32))
        direct = jnp.moveaxis(fields, 0, 2).reshape(RHS, 3, atom_count)
        slope_terms = (
            direction[:, 0, None, :] * plane_dx[None] + direction[:, 1, None, :] * plane_dy[None]
        )
        flat_terms = direction[:, 2, None, :] * plane_flat[None]
        spread_left = jnp.concatenate(
            [
                slope_terms.reshape(RHS, plane_count, tile_count, TILE),
                flat_terms.reshape(RHS, plane_count, tile_count, TILE),
            ],
            axis=3,
        )
        spread_windows = jnp.einsum("sptb,twb->sptw", spread_left, depth_table, precision=highest)
        main_part = spread_windows[..., :slab_depth].reshape(spread_windows.shape[:-2] + (KZ,))
        tail_part = pad_axis(
            spread_windows[..., slab_depth:], spread_windows.ndim - 1, 0, slab_depth - 4
        )
        tail_part = tail_part.reshape(spread_windows.shape[:-2] + (KZ,))[..., : KZ + 4 - slab_depth]
        last_axis = main_part.ndim - 1
        padded_line = pad_axis(main_part, last_axis, 0, 4) + pad_axis(
            tail_part, last_axis, slab_depth, 0
        )
        inner = padded_line[..., 2 : KZ + 2]
        spread_tile = (
            inner
            + pad_axis(padded_line[..., 0:2], last_axis, KZ - 2, 0)
            + pad_axis(padded_line[..., KZ + 2 : KZ + 4], last_axis, 0, KZ - 2)
        ).reshape(RHS, CX + 4, CY + 4, KZ)
        extended = with_halo(spread_tile, (("row", 1), ("col", 2)), 2)
        cycle_only = clear_inside(extended, ((1, CX), (2, CY)))
        folded = fold_cycle(fold_cycle(cycle_only, 1, CX), 2, CY)
        spectrum = jnp.einsum(
            "sxyz,zk->sxyk",
            spread_tile[:, 2 : CX + 2, 2 : CY + 2] + folded,
            hartley_z,
            precision=highest,
        )
        along_y = jnp.einsum(
            "sxyz,yk->sxkz",
            lax.all_to_all(spectrum, "col", split_axis=3, concat_axis=2, tiled=True),
            hartley_y,
            precision=highest,
        )
        along_x = (
            jnp.einsum(
                "sxyz,xk->skyz",
                lax.all_to_all(along_y, "row", split_axis=2, concat_axis=1, tiled=True),
                hartley_x,
                precision=highest,
            )
            * kernel[None]
        )
        mixed_part = jnp.einsum("sxyz,xk->skyz", along_x, hartley_x, precision=highest)
        returned = lax.all_to_all(mixed_part, "row", split_axis=1, concat_axis=2, tiled=True)
        swapped = jnp.einsum("sxyz,yk->sxkz", returned, hartley_y, precision=highest)
        restored = lax.all_to_all(swapped, "col", split_axis=2, concat_axis=3, tiled=True)
        padded = with_halo(
            jnp.einsum("sxyz,zk->sxyk", restored, hartley_z, precision=highest),
            (("row", 1), ("col", 2)),
            2,
        )
        line = padded.reshape(RHS, plane_count, KZ)
        extended_line = jnp.concatenate([line[..., KZ - 2 :], line, line[..., :2]], axis=-1)
        windows = jnp.stack(
            [
                extended_line[..., tile * slab_depth : tile * slab_depth + window_len]
                for tile in range(tile_count)
            ],
            axis=-2,
        )
        sampled = jnp.einsum("sptw,twb->sptb", windows, depth_table, precision=highest)
        with_flat = sampled[..., :TILE].reshape(RHS, plane_count, atom_count)
        with_slope = sampled[..., TILE:].reshape(RHS, plane_count, atom_count)
        recip_part = jnp.stack(
            [
                jnp.sum(with_flat * plane_dx[None], axis=1),
                jnp.sum(with_flat * plane_dy[None], axis=1),
                jnp.sum(with_slope * plane_flat[None], axis=1),
            ],
            axis=1,
        )
        image_field = direction / polar_wide - direct + recip_part - self_coef * direction
        step_size = (progress / inner_sum(direction, image_field))[:, None, None]
        solution = solution + step_size * direction
        residual = residual - step_size * image_field
        scaled_res = polar_wide * residual
        progress_next = inner_sum(residual, scaled_res)
        direction = scaled_res + (progress_next / progress)[:, None, None] * direction
        progress = progress_next
    return (solution[None, None], residual[None, None])


X_PAD = CX + 4
Y_PAD = CY + 4
SLOT_ROWS = 16
SPLIT = 2
VMEM_LIMIT = 60_000_000
SMALL_VMEM_LIMIT = 24_000_000
MIDDLE_VMEM_LIMIT = 56_000_000
EARLY_TILES = 1
PAIR_ROWS = 32
GROUP = 8
SCREEN_SCALE = 0.4
SCREEN_COEF = (
    0.22567588090896606,
    0.2256690263748169,
    0.20785020291805267,
    0.16849851608276367,
    0.14156343042850494,
    -0.005832736846059561,
    0.16930203139781952,
    -0.1830107867717743,
    0.05028456076979637,
)


def halves(value):
    high = value.astype(jnp.bfloat16)
    return high, (value - high.astype(jnp.float32)).astype(jnp.bfloat16)


def halves_np(value):
    value = value.astype(np.float32)
    high = value.astype(ml_dtypes.bfloat16)
    return high, (value - high.astype(np.float32)).astype(ml_dtypes.bfloat16)


def product(left, right, left_dim=1, right_dim=0):
    def one(first, second):
        return lax.dot_general(
            first,
            second,
            (((left_dim,), (right_dim,)), ((), ())),
            preferred_element_type=jnp.float32,
        )

    return one(left[0], right[0]) + (one(left[1], right[0]) + one(left[0], right[1]))


def cas_np(wave, place, length):
    angles = 2.0 * np.pi / length * (wave[:, None] * place[None, :] % length)
    return np.cos(angles) + np.sin(angles)


def modulus_np(wave, length):
    coef = np.array([1.0, 11.0, 11.0, 1.0]) / 24.0
    angles = 2.0 * np.pi / length * (wave[:, None] * np.arange(4)[None, :])
    return (coef * np.cos(angles)).sum(1) ** 2 + (coef * np.sin(angles)).sum(1) ** 2


def influence_np(length_x, length_y, length_z):
    total = np.zeros((length_x, length_y, length_z))
    modulus = np.ones((length_x, length_y, length_z))
    excluded = np.zeros((length_x, length_y, length_z), bool)
    for axis, length in enumerate((length_x, length_y, length_z)):
        wave = np.arange(length)
        shape = [1, 1, 1]
        shape[axis] = length
        total = total + ((np.minimum(wave, length - wave) / length) ** 2).reshape(shape)
        modulus = modulus * modulus_np(wave, length).reshape(shape)
        excluded = excluded | (wave * 2 == length).reshape(shape)
    excluded[0, 0, 0] = True
    safe = np.where(excluded, 1.0, total)
    result = np.exp(-(np.pi**2) / ewald_beta**2 * safe) / (
        np.pi * safe * np.where(excluded, 1.0, modulus)
    )
    return np.where(excluded, 0.0, result) / (length_x * length_y * length_z)


def slab_tables(rows_count, cols_count):
    grid_x = CX * rows_count
    grid_y = CY * cols_count
    devices = rows_count * cols_count
    chunk = KZ // devices
    wave_z = (np.arange(devices)[None, :] * chunk + np.arange(chunk)[:, None]).reshape(-1)
    along_z = cas_np(wave_z, np.arange(KZ), KZ)
    place_x = np.arange(rows_count)[:, None] * CX + np.arange(X_PAD)[None, :] - 2
    along_x = cas_np(np.arange(grid_x), place_x.reshape(-1) % grid_x, grid_x)
    x_high, x_low = halves_np(along_x)
    forward_x = np.concatenate([x_high, x_low, x_high], axis=1)
    backward_x = np.concatenate([x_high.T, x_low.T, x_high.T], axis=1)
    place_y = (np.arange(cols_count)[:, None] * CY + np.arange(Y_PAD)[None, :] - 2) % grid_y
    along_y = cas_np(np.arange(grid_y), place_y.reshape(-1), grid_y)
    along_y = along_y.reshape(grid_y, cols_count, Y_PAD)
    units = chunk * RHS // SPLIT
    block = np.einsum("uv,kcy->cuyvk", np.eye(units), along_y)
    block = block.reshape(cols_count * units * Y_PAD, units * grid_y)
    kernel = influence_np(grid_x, grid_y, KZ).reshape(grid_x, grid_y, devices, chunk)
    kernel = np.transpose(kernel, (2, 0, 3, 1))[:, :, :, None, :]
    kernel = np.broadcast_to(kernel, (devices, grid_x, chunk, RHS, grid_y))
    kernel = kernel.reshape(devices, grid_x, SPLIT, units * grid_y)
    kernel = np.moveaxis(kernel, 2, 1).reshape(devices, SPLIT * grid_x, units * grid_y)
    kernel = kernel.astype(np.float32)
    return dict(
        along_z=halves_np(along_z),
        forward_x=forward_x,
        backward_x=backward_x,
        block=halves_np(block),
        kernel=kernel,
    )


def pack_body(rhs_ref, place_ref, polar_ref, start_ref, payload_ref):
    polar = polar_ref[...]
    start = read_rows(rhs_ref) * polar
    start_ref[...] = start
    place = [place_ref[dim] for dim in range(3)]
    everything = jnp.concatenate(place + [1.0 / jnp.sqrt(polar), start], axis=0)
    store_payload(payload_ref, everything)


def read_rows(rows_ref):
    return jnp.concatenate([rows_ref[dim] for dim in range(3)], axis=0)


def store_payload(payload_ref, everything):
    tile_count = everything.shape[1] // TILE
    for quantity in range(everything.shape[0]):
        for tile in range(tile_count):
            row = quantity * tile_count + tile
            payload_ref[row : row + 1, :] = everything[
                quantity : quantity + 1, tile * TILE : (tile + 1) * TILE
            ]


def placed_rows(slot, weights, extent):
    slot_index = lax.broadcasted_iota(jnp.int32, (extent, slot.shape[1]), 0)
    placed = jnp.zeros((extent, slot.shape[1]), jnp.float32)
    for stencil in range(5):
        target = slot + stencil
        if extent == KZ:
            target = jnp.where(target >= KZ, target - KZ, target)
        placed = placed + jnp.where(slot_index == target, weights[stencil], 0.0)
    return placed


def spread_into(message_ref, moment, rows_x, slope_x, rows_y, slope_y, depth, devices):
    blocks = []
    for step in range(X_PAD):
        flat_x = rows_x[step : step + 1]
        tilt_x = slope_x[step : step + 1]
        for rhs in range(RHS):
            part_x = tilt_x * moment[rhs : rhs + 1]
            part_y = flat_x * moment[RHS + rhs : RHS + rhs + 1]
            part_z = flat_x * moment[2 * RHS + rhs : 2 * RHS + rhs + 1]
            blocks.append(
                jnp.concatenate([part_x * rows_y + part_y * slope_y, part_z * rows_y], axis=1)
            )
    charges = jnp.concatenate(blocks, axis=0)
    spectrum = product(depth, halves(charges), 1, 1)
    slot_rows = message_ref.shape[0] // devices
    chunk = KZ // devices
    width = RHS * Y_PAD
    for step in range(X_PAD):
        message_ref[pl.ds(step, devices, stride=slot_rows), :] = jnp.concatenate(
            [
                spectrum[unit * devices : (unit + 1) * devices, step * width : (step + 1) * width]
                for unit in range(chunk)
            ],
            axis=1,
        )


def sample_from(message_ref, rows_x, slope_x, rows_y, slope_y, depth, devices):
    chunk = KZ // devices
    width = RHS * Y_PAD
    slot_rows = message_ref.shape[0] // devices
    pieces = [
        message_ref[pl.ds(step, devices, stride=slot_rows), :] for step in range(X_PAD)
    ]
    spare = jnp.zeros((devices, KZ - X_PAD * width), jnp.float32)
    spectrum = jnp.concatenate(
        [
            jnp.concatenate(
                [piece[:, unit * width : (unit + 1) * width] for piece in pieces] + [spare], axis=1
            )
            for unit in range(chunk)
        ],
        axis=0,
    )
    spectrum = jnp.transpose(spectrum)[: X_PAD * width]
    sampled = product(halves(spectrum), depth, 1, 0)
    atoms = rows_x.shape[1]
    fields = [None] * (3 * RHS)
    for rhs in range(RHS):
        sum_x = sum_y = sum_z = None
        for step in range(X_PAD):
            first = step * width + rhs * Y_PAD
            flat = sampled[first : first + Y_PAD, :atoms]
            tilt = sampled[first : first + Y_PAD, atoms:]
            part_x = slope_x[step : step + 1] * flat
            part_y = rows_x[step : step + 1] * flat
            part_z = rows_x[step : step + 1] * tilt
            sum_x = part_x if sum_x is None else sum_x + part_x
            sum_y = part_y if sum_y is None else sum_y + part_y
            sum_z = part_z if sum_z is None else sum_z + part_z
        fields[rhs] = jnp.sum(sum_x * rows_y, axis=0, keepdims=True)
        fields[RHS + rhs] = jnp.sum(sum_y * slope_y, axis=0, keepdims=True)
        fields[2 * RHS + rhs] = jnp.sum(sum_z * rows_y, axis=0, keepdims=True)
    return jnp.concatenate(fields, axis=0)


def read_tables(tables_ref):
    return (
        tables_ref[0:X_PAD],
        tables_ref[SLOT_ROWS : SLOT_ROWS + X_PAD],
        tables_ref[2 * SLOT_ROWS : 2 * SLOT_ROWS + Y_PAD],
        tables_ref[2 * SLOT_ROWS + Y_PAD : 2 * SLOT_ROWS + 2 * Y_PAD],
    )


def setup_body(
    lengths,
    devices,
    place_ref,
    base_ref,
    start_ref,
    z_high_ref,
    z_low_ref,
    message_ref,
    tables_ref,
    depth_high_ref,
    depth_low_ref,
):
    base = [base_ref[dim] for dim in range(3)]
    fractions = []
    cells = []
    for dim in range(3):
        cell = base[dim] + 2
        cell = jnp.where(cell >= lengths[dim], cell - lengths[dim], cell)
        cells.append(cell)
        fractions.append(place_ref[dim] - cell.astype(jnp.float32))
    values, slopes = spline_table(jnp.concatenate(fractions, axis=0))
    values = [[values[stencil][dim : dim + 1] for stencil in range(5)] for dim in range(3)]
    slopes = [[slopes[stencil][dim : dim + 1] for stencil in range(5)] for dim in range(3)]
    slot_x = lax.rem(cells[0], CX)
    slot_y = lax.rem(cells[1], CY)
    tables_ref[0:SLOT_ROWS] = placed_rows(slot_x, values[0], SLOT_ROWS)
    tables_ref[SLOT_ROWS : 2 * SLOT_ROWS] = placed_rows(slot_x, slopes[0], SLOT_ROWS)
    tables_ref[2 * SLOT_ROWS : 2 * SLOT_ROWS + Y_PAD] = placed_rows(slot_y, values[1], Y_PAD)
    tables_ref[2 * SLOT_ROWS + Y_PAD : 2 * SLOT_ROWS + 2 * Y_PAD] = placed_rows(
        slot_y, slopes[1], Y_PAD
    )
    window = jnp.concatenate(
        [
            placed_rows(base[2], values[2], KZ),
            placed_rows(base[2], slopes[2], KZ),
        ],
        axis=1,
    )
    depth = product((z_high_ref[...], z_low_ref[...]), halves(window), 1, 0)
    depth = halves(depth)
    depth_high_ref[...] = depth[0]
    depth_low_ref[...] = depth[1]
    spread_into(message_ref, start_ref[...], *read_tables(tables_ref), depth, devices)


def transform_in(message_ref, forward_ref, block_high_ref, block_low_ref, rows_count, cols_count):
    gathered = jnp.concatenate(
        [
            jnp.concatenate(
                [
                    message_ref[(r * cols_count + c) * X_PAD : (r * cols_count + c + 1) * X_PAD]
                    for r in range(rows_count)
                ],
                axis=0,
            )
            for c in range(cols_count)
        ],
        axis=1,
    )
    high, low = halves(gathered)
    along = jnp.dot(
        forward_ref[...],
        jnp.concatenate([high, high, low], axis=0),
        preferred_element_type=jnp.float32,
    )
    part = along.shape[1] // cols_count // SPLIT
    along = jnp.concatenate(
        [
            jnp.concatenate(
                [
                    along[:, (c * SPLIT + half) * part : (c * SPLIT + half + 1) * part]
                    for c in range(cols_count)
                ],
                axis=1,
            )
            for half in range(SPLIT)
        ],
        axis=0,
    )
    return product(halves(along), (block_high_ref[...], block_low_ref[...]))


def transform_out(result_ref, values, backward_ref, block_high_ref, block_low_ref, counts):
    rows_count, cols_count = counts
    spread = product(halves(values), (block_high_ref[...], block_low_ref[...]), 1, 1)
    grid_x = spread.shape[0] // SPLIT
    part = spread.shape[1] // cols_count
    spread = jnp.concatenate(
        [
            spread[half * grid_x : (half + 1) * grid_x, c * part : (c + 1) * part]
            for c in range(cols_count)
            for half in range(SPLIT)
        ],
        axis=1,
    )
    high, low = halves(spread)
    along = jnp.dot(
        backward_ref[...],
        jnp.concatenate([high, high, low], axis=0),
        preferred_element_type=jnp.float32,
    )
    width = along.shape[1] // cols_count
    slot_rows = result_ref.shape[0] // (rows_count * cols_count)
    for r in range(rows_count):
        for c in range(cols_count):
            first = (r * cols_count + c) * slot_rows
            result_ref[first : first + X_PAD, :] = along[
                r * X_PAD : (r + 1) * X_PAD, c * width : (c + 1) * width
            ]


def middle_first_body(
    counts,
    message_ref,
    kernel_ref,
    forward_ref,
    backward_ref,
    block_high_ref,
    block_low_ref,
    result_ref,
    wave_ref,
):
    wave = transform_in(message_ref, forward_ref, block_high_ref, block_low_ref, *counts)
    wave_ref[...] = wave
    transform_out(
        result_ref, wave * kernel_ref[...], backward_ref, block_high_ref, block_low_ref, counts
    )


def gather_rows(parts):
    tiles = [
        parts[GROUP * tile : GROUP * tile + GROUP, :] for tile in range(parts.shape[0] // GROUP)
    ]
    return jnp.concatenate(tiles, axis=1)[0 : 3 * RHS]


def row_total(value, rhs):
    row = lax.broadcasted_iota(jnp.int32, value.shape, 0)
    return total(jnp.where(lax.rem(row, RHS) == rhs, value, 0.0))


def total(value):
    return jnp.sum(jnp.sum(value, axis=0, keepdims=True), axis=1, keepdims=True)


def middle_second_body(
    counts,
    message_ref,
    kernel_ref,
    forward_ref,
    backward_ref,
    block_high_ref,
    block_low_ref,
    wave_ref,
    rhs_ref,
    start_ref,
    image_ref,
    second_ref,
    near_ref,
    polar_ref,
    result_ref,
):
    rhs_rows = read_rows(rhs_ref)
    near_rows = gather_rows(near_ref)
    wave = transform_in(message_ref, forward_ref, block_high_ref, block_low_ref, *counts)
    filtered = wave * kernel_ref[...]
    transform_out(result_ref, filtered, backward_ref, block_high_ref, block_low_ref, counts)
    before = wave_ref[...]
    grid_y = CY * counts[1]
    lane = lax.broadcasted_iota(jnp.int32, wave.shape, 1)
    own_rhs = lax.rem(lax.div(lane, grid_y), RHS)
    second = second_ref[...]
    start = start_ref[...]
    image = image_ref[...]
    local_part = second / polar_ref[...] - near_rows - self_coef * second
    slot = lax.broadcasted_iota(jnp.int32, (1, result_ref.shape[1]), 1)
    sums = jnp.zeros((1, result_ref.shape[1]), jnp.float32)
    for rhs in range(RHS):
        mine = own_rhs == rhs
        parts = (
            row_total(rhs_rows * start, rhs),
            row_total(start * image, rhs),
            row_total(second * image, rhs),
            row_total(start * local_part, rhs) + total(jnp.where(mine, before * filtered, 0.0)),
            row_total(second * local_part, rhs) + total(jnp.where(mine, wave * filtered, 0.0)),
        )
        for index, part in enumerate(parts):
            sums = jnp.where(slot == rhs * len(parts) + index, part, sums)
    devices = counts[0] * counts[1]
    result_ref[pl.ds(X_PAD, devices, stride=X_PAD + 1), :] = jnp.broadcast_to(
        sums, (devices, sums.shape[1])
    )


def sample_body(
    devices,
    message_ref,
    tables_ref,
    depth_high_ref,
    depth_low_ref,
    start_ref,
    near_ref,
    polar_ref,
    image_ref,
    second_ref,
    payload_ref,
):
    tables = read_tables(tables_ref)
    depth = (depth_high_ref[...], depth_low_ref[...])
    field = sample_from(message_ref, *tables, depth, devices)
    start = start_ref[...]
    polar = polar_ref[...]
    image = start / polar - gather_rows(near_ref) + field - self_coef * start
    second = polar * image
    image_ref[...] = image
    second_ref[...] = second
    store_payload(payload_ref, second)


def spread_body(
    devices,
    tables_ref,
    depth_high_ref,
    depth_low_ref,
    second_ref,
    result_ref,
):
    depth = (depth_high_ref[...], depth_low_ref[...])
    spread_into(result_ref, second_ref[...], *read_tables(tables_ref), depth, devices)


def final_body(
    devices,
    message_ref,
    tables_ref,
    depth_high_ref,
    depth_low_ref,
    rhs_ref,
    start_ref,
    image_ref,
    second_ref,
    near_ref,
    polar_ref,
    dipole_ref,
    residual_ref,
):
    tables = read_tables(tables_ref)
    depth = (depth_high_ref[...], depth_low_ref[...])
    field = sample_from(message_ref, *tables, depth, devices)
    second = second_ref[...]
    start = start_ref[...]
    image = image_ref[...]
    image_second = second / polar_ref[...] - gather_rows(near_ref) + field - self_coef * second
    sums = jnp.sum(
        message_ref[pl.ds(X_PAD, devices, stride=X_PAD + 1), :], axis=0, keepdims=True
    )
    steps = []
    for rhs in range(RHS):
        progress, start_image, second_image, start_next, second_next = [
            sums[:, rhs * 5 + index : rhs * 5 + index + 1] for index in range(5)
        ]
        step = progress / start_image
        progress_next = progress - 2.0 * step * start_image + step * step * second_image
        grown = 1.0 + progress_next / progress
        curvature = (
            grown * grown * start_image
            - step * grown * (start_next + second_image)
            + step * step * second_next
        )
        steps.append((step, grown, progress_next / curvature))
    row = lax.broadcasted_iota(jnp.int32, (RHS, 1), 0)
    step, grown, step_next = [
        sum(jnp.where(row == rhs, steps[rhs][index], 0.0) for rhs in range(RHS))
        for index in range(3)
    ]
    for dim in range(3):
        rows = slice(dim * RHS, (dim + 1) * RHS)
        direction = grown * start[rows] - step * second[rows]
        image_direction = grown * image[rows] - step * image_second[rows]
        dipole_ref[dim] = step * start[rows] + step_next * direction
        residual_ref[dim] = rhs_ref[dim] - step * image[rows] - step_next * image_direction


def near_base(entry, brick_rows):
    return lax.shift_right_logical(entry, 2) * brick_rows + lax.bitwise_and(entry, 3)


def fill_near(scratch, up_ref, stack_ref, down_ref):
    rows = stack_ref.shape[0]
    scratch[0:rows, :] = up_ref[...]
    scratch[rows : 2 * rows, :] = stack_ref[...]
    scratch[2 * rows : 3 * rows, :] = down_ref[...]


def nearest(places, origin, span):
    return places - span * jnp.floor((places - origin) * (1.0 / span) + 0.5)


def unwrap_near(near, tile_count, spans):
    rows = near.shape[0] // 9
    for dim in range(2):
        own = 4 * rows + dim * tile_count
        origin = near[own : own + 1, 0:1]
        for brick in range(9):
            first = brick * rows + dim * tile_count
            near[first : first + tile_count, :] = nearest(
                near[first : first + tile_count, :], origin, spans[dim]
            )


def pick_rows(picked, near, lists_ref, tile, tile_count, quantities, origin, span):
    rows = near.shape[0] // 9
    for entry in range(lists_ref.shape[1]):
        base = near_base(lists_ref[tile, entry], rows)
        for quantity in range(quantities):
            values = near[pl.ds(base + quantity * tile_count, 1), :]
            if quantity == 2 and span is not None:
                values = nearest(values, origin, span)
            first = (entry * quantities + quantity) * GROUP
            picked[first : first + GROUP, :] = jnp.broadcast_to(values, (GROUP, TILE))


def widen_own(near, quantities, tile_count, tile, square, wide):
    offset = near.shape[0] // 9 * 4
    for quantity in range(quantities):
        square[quantity : quantity + 1, :] = near[
            pl.ds(offset + quantity * tile_count + tile, 1), :
        ]
    columns = jnp.transpose(square[...])
    for quantity in range(quantities):
        wide[quantity * TILE : (quantity + 1) * TILE, :] = jnp.broadcast_to(
            columns[:, quantity : quantity + 1], (TILE, TILE)
        )


def add_field(sums, first_term, second_term, apart, moments):
    for rhs in range(RHS):
        moment = [moments[RHS * dim + rhs] for dim in range(3)]
        projected = moment[0] * apart[0] + moment[1] * apart[1] + moment[2] * apart[2]
        weighted = second_term * projected
        for dim in range(3):
            index = RHS * dim + rhs
            sums[index] = sums[index] + (weighted * apart[dim] - first_term * moment[dim])


def finish_sums(field_ref, sums_ref):
    lane = lax.broadcasted_iota(jnp.int32, (TILE, TILE), 1)
    merged = jnp.zeros((TILE, TILE), jnp.float32)
    for index in range(3 * RHS):
        column = jnp.sum(sums_ref[index * TILE : (index + 1) * TILE, :], axis=1, keepdims=True)
        merged = jnp.where(lane == index, column, merged)
    field_ref[...] = jnp.transpose(merged)[0:GROUP]


def pair_rows(start, group):
    return pl.ds(pl.multiple_of(start + group * GROUP, GROUP), GROUP)


def wide_rows(start, group, quantity):
    return pl.ds(pl.multiple_of(quantity * TILE + start + group * GROUP, GROUP), GROUP)


def pair_terms(square_dist, damp):
    inverse = lax.rsqrt(square_dist)
    distance = square_dist * inverse
    inverse_sq = inverse * inverse
    inverse_cube = inverse_sq * inverse
    cubed = damp * (distance * square_dist)
    damping = jnp.exp(cubed)
    bell = jnp.exp(-(ewald_beta * ewald_beta) * square_dist)
    stretched = 1.0 + (SCREEN_SCALE * ewald_beta) * distance
    turned = pl.reciprocal(stretched, approx=True)
    turned = turned * (2.0 - stretched * turned)
    series = SCREEN_COEF[-1] * turned + SCREEN_COEF[-2]
    for coef in SCREEN_COEF[-3::-1]:
        series = series * turned + coef
    screen = bell * turned * series
    gaussian = (2.0 * ewald_beta / math.sqrt(math.pi)) * bell
    bare = screen - damping
    first_term = bare * inverse_cube + gaussian * inverse_sq
    second_term = (
        3.0 * (first_term + (cubed * damping) * inverse_cube)
        + (2.0 * ewald_beta * ewald_beta) * gaussian
    ) * inverse_sq
    return first_term, second_term


def pair_first_body(
    first_tile,
    tile_count,
    spans,
    lists_ref,
    up_ref,
    stack_ref,
    down_ref,
    *others,
):
    first_ref, second_ref, field_ref, near_ref, near, picked, square, wide, sums_ref = others[-9:]

    @pl.when(pl.program_id(0) == 0)
    def _():
        fill_near(near, up_ref, stack_ref, down_ref)
        unwrap_near(near, tile_count, spans)
        square[...] = jnp.zeros_like(square)
        rows = near.shape[0] // 9
        kept = 3 * tile_count
        for brick in range(9):
            near_ref[brick * kept : (brick + 1) * kept, :] = near[
                brick * rows : brick * rows + kept, :
            ]

    tile = first_tile + pl.program_id(0)
    quantities = near.shape[0] // 9 // tile_count
    widen_own(near, 4, tile_count, tile, square, wide)
    origin = wide[2 * TILE : 2 * TILE + 1, 0:1]
    pick_rows(picked, near, lists_ref, tile, tile_count, quantities, origin, spans[2])

    @pl.loop(0, TILE // PAIR_ROWS)
    def _(part):
        start = part * PAIR_ROWS
        for group in range(PAIR_ROWS // GROUP):
            own = [wide[wide_rows(start, group, dim), :] for dim in range(4)]
            own_damp = -thole_a * own[3]
            sums = [jnp.zeros((GROUP, TILE), jnp.float32) for _ in range(3 * RHS)]
            itself = (
                lax.broadcasted_iota(jnp.int32, (GROUP, TILE), 0) + (start + group * GROUP)
            ) == lax.broadcasted_iota(jnp.int32, (GROUP, TILE), 1)
            for entry in range(lists_ref.shape[1]):
                first = entry * quantities * GROUP
                rows = [
                    picked[first + quantity * GROUP : first + (quantity + 1) * GROUP, :]
                    for quantity in range(quantities)
                ]
                apart = [rows[dim] - own[dim] for dim in range(3)]
                square_dist = apart[0] * apart[0] + apart[1] * apart[1] + apart[2] * apart[2]
                if entry == 0:
                    square_dist = jnp.where(itself, 1.0, square_dist)
                first_term, second_term = pair_terms(square_dist, own_damp * rows[3])
                if entry == 0:
                    first_term = jnp.where(itself, 0.0, first_term)
                    second_term = jnp.where(itself, 0.0, second_term)
                place = wide_rows(start, group, entry)
                first_ref[place, :] = first_term
                second_ref[place, :] = second_term
                add_field(sums, first_term, second_term, apart, rows[4:])
            for index, value in enumerate(sums):
                sums_ref[wide_rows(start, group, index), :] = value

    finish_sums(field_ref, sums_ref)


def pair_second_body(
    tile_count,
    spans,
    lists_ref,
    near,
    up_ref,
    stack_ref,
    down_ref,
    first_ref,
    second_ref,
    field_ref,
    near_moment,
    picked,
    picked_moment,
    square,
    wide,
    sums_ref,
):
    @pl.when(pl.program_id(0) == 0)
    def _():
        fill_near(near_moment, up_ref, stack_ref, down_ref)
        square[...] = jnp.zeros_like(square)

    tile = pl.program_id(0)
    widen_own(near, 3, tile_count, tile, square, wide)
    origin = wide[2 * TILE : 2 * TILE + 1, 0:1]
    pick_rows(picked, near, lists_ref, tile, tile_count, 3, origin, spans[2])
    pick_rows(picked_moment, near_moment, lists_ref, tile, tile_count, 3 * RHS, None, None)

    @pl.loop(0, TILE // PAIR_ROWS)
    def _(part):
        start = part * PAIR_ROWS
        for group in range(PAIR_ROWS // GROUP):
            own = [wide[wide_rows(start, group, dim), :] for dim in range(3)]
            sums = [jnp.zeros((GROUP, TILE), jnp.float32) for _ in range(3 * RHS)]
            for entry in range(lists_ref.shape[1]):
                first = entry * 3 * GROUP
                apart = [
                    picked[first + dim * GROUP : first + (dim + 1) * GROUP, :] - own[dim]
                    for dim in range(3)
                ]
                first = first * RHS
                moments = [
                    picked_moment[first + index * GROUP : first + (index + 1) * GROUP, :]
                    for index in range(3 * RHS)
                ]
                place = wide_rows(start, group, entry)
                add_field(sums, first_ref[place, :], second_ref[place, :], apart, moments)
            for index, value in enumerate(sums):
                sums_ref[wide_rows(start, group, index), :] = value

    finish_sums(field_ref, sums_ref)


def shift(source, axis, step):
    count = lax.axis_size(axis)
    return lax.ppermute(source, axis, [(i, (i + step) % count) for i in range(count)])


def both_ways(source, axis):
    return shift(source, axis, 1), source, shift(source, axis, -1)


def whole(shape):
    return pl.BlockSpec(shape, lambda *_: (0,) * len(shape))


def anywhere():
    return pl.BlockSpec(memory_space=pl.ANY)


def join(message, payload):
    left, _, right = both_ways(payload, "col")
    message, left, right = lax.optimization_barrier((message, left, right))
    return message, both_ways(jnp.concatenate([left, payload, right], axis=0), "row")


class Fetched:
    def __init__(self, source, scratch, semaphore):
        self.copy = pltpu.make_async_copy(source, scratch, semaphore)
        self.copy.start()
        self.scratch = scratch
        self.shape = scratch.shape
        self.waiting = True

    def wait(self):
        if self.waiting:
            self.copy.wait()
            self.waiting = False

    def __getitem__(self, index):
        self.wait()
        return self.scratch[index]


def call(body, outs, *operands, after=(), own_block=None, near=0, vmem=VMEM_LIMIT):
    fetched = [
        pltpu.VMEM(operand.shape[1:] if index == own_block else operand.shape, operand.dtype)
        for index, operand in enumerate(operands)
        if index >= near
    ]
    count = len(operands)

    def run(*refs):
        refs = refs[len(after) :]
        sources, refs = refs[:count], refs[count:]
        results, refs = refs[: len(outs)], refs[len(outs) :]
        targets = sources[:near] + refs[: count - near]
        written, semaphore = refs[count - near : -1], refs[-1]
        inputs = []
        for index, source in enumerate(sources):
            if index < near:
                inputs.append(source)
                continue
            if index == own_block:
                place = lax.axis_index("row") * lax.axis_size("col") + lax.axis_index("col")
                source = source.at[place]
            inputs.append(Fetched(source, targets[index], semaphore.at[index]))
        body(*inputs, *written)
        for operand in inputs[near:]:
            operand.wait()
        copies = [
            pltpu.make_async_copy(value, result, semaphore.at[count + index])
            for index, (value, result) in enumerate(zip(written, results))
        ]
        for copy in copies:
            copy.start()
        for copy in copies:
            copy.wait()

    return pl.pallas_call(
        run,
        in_specs=[anywhere()] * len(after)
        + [pl.BlockSpec(memory_space=pltpu.VMEM)] * near
        + [anywhere()] * (count - near),
        out_specs=[anywhere()] * len(outs),
        out_shape=[jax.ShapeDtypeStruct(shape, dtype) for shape, dtype in outs],
        scratch_shapes=fetched
        + [pltpu.VMEM(shape, dtype) for shape, dtype in outs]
        + [pltpu.SemaphoreType.DMA((count + len(outs),))],
        compiler_params=pltpu.CompilerParams(vmem_limit_bytes=vmem),
        cost_estimate=pl.CostEstimate(
            flops=200_000_000, bytes_accessed=4 << 20, transcendentals=0
        ),
    )(*after, *operands)


def final_call(body, outs, *operands):
    return pl.pallas_call(
        body,
        grid=(1,),
        in_specs=[whole(operand.shape) for operand in operands],
        out_specs=[whole(shape) for shape, _ in outs],
        out_shape=[jax.ShapeDtypeStruct(shape, dtype) for shape, dtype in outs],
        compiler_params=pltpu.CompilerParams(vmem_limit_bytes=SMALL_VMEM_LIMIT),
    )(*operands)


def pair_call(body, outs, kept, first_tile, last_tile, blocked, scratch, lists, *operands, after=()):
    tiles = lists.shape[0]

    def block(operand):
        rows = operand.shape[0] // tiles
        return pl.BlockSpec((rows, operand.shape[1]), lambda i, s: (first_tile + i, 0))

    out_shape = [jax.ShapeDtypeStruct(shape, jnp.float32) for shape in outs + kept]
    plain = len(operands) - blocked
    aliases = {}
    if first_tile > 0:
        first = 1 + len(operands) + len(after) - len(outs)
        aliases = {first + index: index for index in range(len(outs))}
    return pl.pallas_call(
        body,
        out_shape=out_shape,
        grid_spec=pltpu.PrefetchScalarGridSpec(
            num_scalar_prefetch=1,
            grid=(last_tile - first_tile,),
            in_specs=[whole(operand.shape) for operand in operands[:plain]]
            + [block(operand) for operand in operands[plain:]]
            + [anywhere()] * len(after),
            out_specs=[block(shape) for shape in out_shape[: len(outs)]]
            + [whole(shape) for shape in kept],
            scratch_shapes=[pltpu.VMEM(shape, jnp.float32) for shape in scratch],
        ),
        input_output_aliases=aliases,
        compiler_params=pltpu.CompilerParams(vmem_limit_bytes=VMEM_LIMIT),
        cost_estimate=pl.CostEstimate(
            flops=80_000_000, bytes_accessed=8 << 20, transcendentals=1 << 21
        ),
    )(lists, *operands, *after)


def exchange(message, devices):
    shape = message.shape
    sent = message.reshape(devices, 1, -1)
    return lax.all_to_all(sent, ("row", "col"), split_axis=0, concat_axis=0, tiled=True).reshape(
        shape
    )


def slab_local(field_rhs, positions, polar, grid_base, tile_lists):
    rows_count = lax.axis_size("row")
    cols_count = lax.axis_size("col")
    counts = (rows_count, cols_count)
    devices = rows_count * cols_count
    lengths = (CX * rows_count, CY * cols_count, KZ)
    spans = tuple(float(length) for length in lengths)
    atoms = polar.shape[-1]
    tile_count = atoms // TILE
    listed = tile_lists.shape[-1]
    tables = slab_tables(rows_count, cols_count)
    f32 = jnp.float32
    rhs = jnp.swapaxes(field_rhs[0, 0], 0, 1)
    place = jnp.swapaxes(positions[0], 0, 1)
    base = jnp.swapaxes(grid_base[0], 0, 1)
    polar = polar.reshape(1, atoms)
    lists = tile_lists[0, 0]
    quantities = 4 + 3 * RHS
    brick_rows = quantities * tile_count
    moment_rows = 3 * RHS * tile_count
    message_shape = (devices * X_PAD, KZ // devices * RHS * Y_PAD)
    last_shape = (devices * (X_PAD + 1), message_shape[1])
    row_shape = (3 * RHS, atoms)
    square = (TILE, TILE)
    wide = (4 * TILE, TILE)
    sums = (3 * RHS * TILE, TILE)

    start, payload = call(pack_body, [(row_shape, f32), ((brick_rows, TILE), f32)], rhs, place, polar)

    def setup(*refs):
        setup_body(lengths, devices, *refs)

    message, splines, depth_high, depth_low = call(
        setup,
        [
            (message_shape, f32),
            ((2 * SLOT_ROWS + 2 * Y_PAD, atoms), f32),
            ((KZ, 2 * atoms), jnp.bfloat16),
            ((KZ, 2 * atoms), jnp.bfloat16),
        ],
        place,
        base,
        start,
        *[jnp.asarray(table) for table in tables["along_z"]],
    )
    constants = (
        jnp.asarray(tables["kernel"]),
        jnp.asarray(tables["forward_x"]),
        jnp.asarray(tables["backward_x"]),
        *[jnp.asarray(table) for table in tables["block"]],
    )
    message, near = join(message, payload)
    arrived = exchange(message, devices)

    def pair_first(first_tile, last_tile, *after):
        def body(*refs):
            pair_first_body(first_tile, tile_count, spans, *refs)

        return pair_call(
            body,
            [(tile_count * listed * TILE, TILE)] * 2 + [(tile_count * GROUP, TILE)],
            [(9 * 3 * tile_count, TILE)],
            first_tile,
            last_tile,
            0,
            [(9 * brick_rows, TILE), (listed * quantities * GROUP, TILE), square, wide, sums],
            lists,
            *near,
            after=after,
        )

    early = pair_first(0, EARLY_TILES, message)

    def middle_first(*refs):
        middle_first_body(counts, *refs)

    mixed, wave = call(
        middle_first,
        [(message_shape, f32), (tables["kernel"].shape[1:], f32)],
        arrived,
        *constants,
        after=(early[2],),
        own_block=1,
        near=1,
        vmem=MIDDLE_VMEM_LIMIT,
    )
    returned = exchange(mixed, devices)
    first_term, second_term, direct, near = pair_first(EARLY_TILES, tile_count, wave, *early[:3])

    def sample(*refs):
        sample_body(devices, *refs)

    image, second, moments = call(
        sample,
        [(row_shape, f32), (row_shape, f32), ((moment_rows, TILE), f32)],
        returned,
        splines,
        depth_high,
        depth_low,
        start,
        direct,
        polar,
        near=1,
        vmem=MIDDLE_VMEM_LIMIT,
    )

    def spread(*refs):
        spread_body(devices, *refs)

    (message,) = call(spread, [(message_shape, f32)], splines, depth_high, depth_low, second)
    message, near_moments = join(message, moments)
    arrived = exchange(message, devices)

    def pair_second(*refs):
        pair_second_body(tile_count, spans, *refs)

    (direct,) = pair_call(
        pair_second,
        [(tile_count * GROUP, TILE)],
        [],
        0,
        tile_count,
        2,
        [
            (9 * moment_rows, TILE),
            (listed * 3 * GROUP, TILE),
            (listed * 3 * RHS * GROUP, TILE),
            square,
            wide,
            sums,
        ],
        lists,
        near,
        *near_moments,
        first_term,
        second_term,
    )

    def middle_second(*refs):
        middle_second_body(counts, *refs)

    (mixed,) = call(
        middle_second,
        [(last_shape, f32)],
        arrived,
        *constants,
        wave,
        rhs,
        start,
        image,
        second,
        direct,
        polar,
        own_block=1,
        near=1,
        vmem=MIDDLE_VMEM_LIMIT,
    )
    returned = exchange(mixed, devices)

    def final(*refs):
        final_body(devices, *refs)

    outs = final_call(
        final,
        [(rhs.shape, f32), (rhs.shape, f32)],
        returned,
        splines,
        depth_high,
        depth_low,
        rhs,
        start,
        image,
        second,
        direct,
        polar,
    )
    return tuple(jnp.swapaxes(out, 0, 1)[None, None] for out in outs)


def solution(mesh):
    placed = (
        P("row", "col", None, None, None),
        P("row", "col", None, None),
        P("row", "col", None),
        P("row", "col", None, None),
        P("row", "col", None, None),
    )
    devices = mesh.shape["row"] * mesh.shape["col"]
    return jax.shard_map(
        slab_local if KZ % devices == 0 else pencil_local,
        mesh=mesh,
        in_specs=placed,
        out_specs=(P("row", "col", None, None, None), P("row", "col", None, None, None)),
        check_vma=False,
    )
```

```python
import math

import jax
import jax.numpy as jnp
import ml_dtypes
import numpy as np
from jax import lax
from jax.experimental import pallas as pl
from jax.experimental.pallas import tpu as pltpu
from jax.sharding import PartitionSpec as P

CX = 8
CY = 4
KZ = 256
TILE = 128
RHS = 2
ITERS = 2


ewald_beta = 0.4
thole_a = 0.39
self_coef = 4.0 * ewald_beta**3 / (3.0 * math.sqrt(math.pi))
highest = lax.Precision.HIGHEST


def with_halo(cells, sides, width):
    for axis, dim in sides:
        count = lax.axis_size(axis)
        head = lax.slice_in_dim(cells, 0, width, axis=dim)
        tail = lax.slice_in_dim(cells, cells.shape[dim] - width, cells.shape[dim], axis=dim)
        cells = jnp.concatenate(
            [
                lax.ppermute(tail, axis, [(i, (i + 1) % count) for i in range(count)]),
                cells,
                lax.ppermute(head, axis, [((i + 1) % count, i) for i in range(count)]),
            ],
            axis=dim,
        )
    return cells


def spline_table(fraction):
    previous = {0: jnp.ones_like(fraction)}
    fourth = previous
    for degree in range(2, 6):
        current = {}
        for offset in range(degree):
            abscissa = fraction + offset
            summed = abscissa * previous.get(offset, 0.0) + (degree - abscissa) * previous.get(
                offset - 1, 0.0
            )
            current[offset] = summed / (degree - 1)
        if degree == 4:
            fourth = current
        previous = current
    values = jnp.stack([previous[4 - stencil] for stencil in range(5)])
    slopes = jnp.stack(
        [fourth.get(4 - stencil, 0.0) - fourth.get(3 - stencil, 0.0) for stencil in range(5)]
    )
    return (values, slopes)


def spline_modulus(wave_index, length):
    spline_coef = (1.0 / 24.0, 11.0 / 24.0, 11.0 / 24.0, 1.0 / 24.0)
    cosine_sum = jnp.zeros(wave_index.shape, jnp.float32)
    sine_sum = jnp.zeros(wave_index.shape, jnp.float32)
    for offset in range(4):
        angles = 2.0 * math.pi / length * (wave_index * offset % length).astype(jnp.float32)
        cosine_sum = cosine_sum + spline_coef[offset] * jnp.cos(angles)
        sine_sum = sine_sum + spline_coef[offset] * jnp.sin(angles)
    return cosine_sum * cosine_sum + sine_sum * sine_sum


def folded_square(wave_index, length):
    nearest = jnp.minimum(wave_index, length - wave_index).astype(jnp.float32) / length
    return nearest * nearest


def influence(wave_x, wave_y, wave_z, length_x, length_y, length_z):
    wave_norm = (
        folded_square(wave_x, length_x)
        + folded_square(wave_y, length_y)
        + folded_square(wave_z, length_z)
    )
    modulus = (
        spline_modulus(wave_x, length_x)
        * spline_modulus(wave_y, length_y)
        * spline_modulus(wave_z, length_z)
    )
    excluded = (wave_x * 2 == length_x) | (wave_y * 2 == length_y) | (wave_z * 2 == length_z)
    excluded = excluded | (wave_x == 0) & (wave_y == 0) & (wave_z == 0)
    safe_norm = jnp.where(excluded, 1.0, wave_norm)
    safe_modulus = jnp.where(excluded, 1.0, modulus)
    result = jnp.exp(-(math.pi**2 / ewald_beta**2) * safe_norm) / (
        math.pi * safe_norm * safe_modulus
    )
    return jnp.where(excluded, 0.0, result)


def tile_field(own_static, near_static, near_dipole, box_spans):
    listed_count = near_static.shape[0]
    tile_width = own_static.shape[1]
    box_span = jnp.array(box_spans, dtype=jnp.float32)[None, :, None, None]
    separation = near_static[:, 0:3, None, :] - own_static[None, 0:3, :, None]
    separation = separation - box_span * jnp.floor(separation / box_span + 0.5)
    dist_sq = jnp.sum(separation * separation, axis=1)
    itself = (jnp.arange(listed_count)[:, None, None] == 0) & (
        jnp.arange(tile_width)[:, None] == jnp.arange(tile_width)[None, :]
    )[None]
    safe_sq = jnp.where(itself, 1.0, dist_sq)
    distance = jnp.sqrt(safe_sq)
    scaled = distance / (own_static[3][None, :, None] * near_static[:, 3][:, None, :])
    cubed = thole_a * scaled * scaled * scaled
    damping = jnp.exp(-cubed)
    screen = lax.erfc(ewald_beta * distance)
    gaussian = 2.0 * ewald_beta / math.sqrt(math.pi) * jnp.exp(-(ewald_beta * ewald_beta) * safe_sq)
    inverse_sq = 1.0 / safe_sq
    inverse_cube = inverse_sq / distance
    first_term = (screen - damping) * inverse_cube + gaussian * inverse_sq
    second = (
        3.0 * (screen - (1.0 + cubed) * damping) * inverse_cube * inverse_sq
        + gaussian * (2.0 * ewald_beta * ewald_beta + 3.0 * inverse_sq) * inverse_sq
    )
    first_term = jnp.where(itself, 0.0, first_term)
    second = jnp.where(itself, 0.0, second)
    projected = jnp.sum(near_dipole[:, :, :, None, :] * separation[:, None, :, :, :], axis=2)
    weighted = second[:, None] * projected
    outward = jnp.sum(weighted[:, :, None] * separation[:, None], axis=(0, 4))
    inward = jnp.sum(first_term[:, None, None] * near_dipole[:, :, :, None, :], axis=(0, 4))
    return outward - inward


def hartley(length):
    counter = jnp.arange(length, dtype=jnp.int32)
    angles = (
        2.0 * math.pi / length * (counter[:, None] * counter[None, :] % length).astype(jnp.float32)
    )
    return jnp.cos(angles) + jnp.sin(angles)


def placed_table(first_cell, weights, extent):
    slot_index = jnp.arange(extent, dtype=jnp.int32)[:, None]
    placed = jnp.zeros((extent, first_cell.shape[0]), jnp.float32)
    for stencil in range(5):
        placed = placed + jnp.where(
            slot_index == (first_cell[None, :] + stencil) % extent, weights[stencil][None, :], 0.0
        )
    return placed


def pad_axis(source, axis_pos, leading, trailing):
    widths = [(0, 0)] * source.ndim
    widths[axis_pos] = (leading, trailing)
    return jnp.pad(source, widths)


def fold_cycle(cycle_only, axis_pos, inner_len):
    middle = lax.slice_in_dim(cycle_only, 4, inner_len + 4, axis=axis_pos)
    lower_cycle = lax.slice_in_dim(cycle_only, 0, 2, axis=axis_pos)
    upper_cycle = lax.slice_in_dim(cycle_only, inner_len + 6, inner_len + 8, axis=axis_pos)
    return (
        middle
        + pad_axis(lower_cycle, axis_pos, 0, inner_len - 2)
        + pad_axis(upper_cycle, axis_pos, inner_len - 2, 0)
    )


def clear_inside(extended, extents):
    inside = None
    for axis_pos, inner_len in extents:
        slot_index = lax.broadcasted_iota(jnp.int32, extended.shape, axis_pos)
        within = (slot_index >= 2) & (slot_index < inner_len + 6)
        inside = within if inside is None else inside & within
    return jnp.where(inside, 0.0, extended)


def inner_sum(left_arr, right_arr):
    return lax.psum(jnp.sum(left_arr * right_arr, axis=(1, 2)), ("row", "col"))


def pencil_local(field_rhs, positions, polar, grid_base, tile_lists):
    rows_count = lax.axis_size("row")
    cols_count = lax.axis_size("col")
    grid_x = CX * rows_count
    grid_y = CY * cols_count
    atom_count = polar.shape[-1]
    tile_count = atom_count // TILE
    slab_depth = KZ // tile_count
    window_len = slab_depth + 4
    box_spans = (float(grid_x), float(grid_y), float(KZ))
    own_place = positions[0, 0]
    own_base = grid_base[0, 0]
    own_polar = polar[0, 0]
    lengths = jnp.array([grid_x, grid_y, KZ], dtype=jnp.int32)[:, None]
    cell_index = (own_base + 2) % lengths
    fraction = own_place - cell_index.astype(jnp.float32)
    values, slopes = spline_table(fraction)
    first_x = (own_base[0] - lax.axis_index("row") * CX + 2) % grid_x
    first_y = (own_base[1] - lax.axis_index("col") * CY + 2) % grid_y
    rows_x = placed_table(first_x, values[:, 0], CX + 4)
    slope_x = placed_table(first_x, slopes[:, 0], CX + 4)
    rows_y = placed_table(first_y, values[:, 1], CY + 4)
    slope_y = placed_table(first_y, slopes[:, 1], CY + 4)
    tile_start = jnp.arange(atom_count, dtype=jnp.int32) // TILE * slab_depth
    first_z = (own_base[2] + 2 - tile_start) % KZ
    rows_z = placed_table(first_z, values[:, 2], window_len)
    slope_z = placed_table(first_z, slopes[:, 2], window_len)
    plane_count = (CX + 4) * (CY + 4)
    plane_dx = (slope_x[:, None, :] * rows_y[None, :, :]).reshape(plane_count, atom_count)
    plane_dy = (rows_x[:, None, :] * slope_y[None, :, :]).reshape(plane_count, atom_count)
    plane_flat = (rows_x[:, None, :] * rows_y[None, :, :]).reshape(plane_count, atom_count)
    window_rows = jnp.moveaxis(rows_z.reshape(window_len, tile_count, TILE), 1, 0)
    window_slope = jnp.moveaxis(slope_z.reshape(window_len, tile_count, TILE), 1, 0)
    depth_table = jnp.concatenate([window_rows, window_slope], axis=2)
    grid_scale = 1.0 / (grid_x * grid_y * KZ)
    hartley_x = hartley(grid_x)
    hartley_y = hartley(grid_y)
    hartley_z = hartley(KZ)
    block_y = grid_y // rows_count
    block_z = KZ // cols_count
    wave_x = jnp.arange(grid_x, dtype=jnp.int32)[:, None, None]
    wave_y = (lax.axis_index("row") * block_y + jnp.arange(block_y, dtype=jnp.int32))[None, :, None]
    wave_z = (lax.axis_index("col") * block_z + jnp.arange(block_z, dtype=jnp.int32))[None, None, :]
    kernel = influence(wave_x, wave_y, wave_z, grid_x, grid_y, KZ) * grid_scale
    root_scale = jnp.power(own_polar, 1.0 / 6.0)
    own_static = jnp.concatenate([own_place, root_scale[None]], axis=0)
    near_static = with_halo(own_static[None, None], (("row", 0), ("col", 1)), 1)
    near_static = jnp.moveaxis(near_static.reshape(9, 4, tile_count, TILE), 2, 1).reshape(
        9 * tile_count, 4, TILE
    )
    own_tiles = jnp.moveaxis(own_static.reshape(4, tile_count, TILE), 1, 0)
    own_lists = tile_lists[0, 0]
    polar_wide = own_polar[None, None, :]
    solution = jnp.zeros_like(field_rhs[0, 0])
    residual = field_rhs[0, 0]
    scaled_res = polar_wide * residual
    direction = scaled_res
    progress = inner_sum(residual, scaled_res)
    for iteration in range(ITERS):
        near_dip = with_halo(direction[None, None], (("row", 0), ("col", 1)), 1)
        near_dip = jnp.moveaxis(near_dip.reshape(9, RHS, 3, tile_count, TILE), 3, 1).reshape(
            9 * tile_count, RHS, 3, TILE
        )

        def one_tile(tile_pos):
            picked = own_lists[tile_pos]
            return tile_field(own_tiles[tile_pos], near_static[picked], near_dip[picked], box_spans)

        fields = lax.map(one_tile, jnp.arange(tile_count, dtype=jnp.int32))
        direct = jnp.moveaxis(fields, 0, 2).reshape(RHS, 3, atom_count)
        slope_terms = (
            direction[:, 0, None, :] * plane_dx[None] + direction[:, 1, None, :] * plane_dy[None]
        )
        flat_terms = direction[:, 2, None, :] * plane_flat[None]
        spread_left = jnp.concatenate(
            [
                slope_terms.reshape(RHS, plane_count, tile_count, TILE),
                flat_terms.reshape(RHS, plane_count, tile_count, TILE),
            ],
            axis=3,
        )
        spread_windows = jnp.einsum("sptb,twb->sptw", spread_left, depth_table, precision=highest)
        main_part = spread_windows[..., :slab_depth].reshape(spread_windows.shape[:-2] + (KZ,))
        tail_part = pad_axis(
            spread_windows[..., slab_depth:], spread_windows.ndim - 1, 0, slab_depth - 4
        )
        tail_part = tail_part.reshape(spread_windows.shape[:-2] + (KZ,))[..., : KZ + 4 - slab_depth]
        last_axis = main_part.ndim - 1
        padded_line = pad_axis(main_part, last_axis, 0, 4) + pad_axis(
            tail_part, last_axis, slab_depth, 0
        )
        inner = padded_line[..., 2 : KZ + 2]
        spread_tile = (
            inner
            + pad_axis(padded_line[..., 0:2], last_axis, KZ - 2, 0)
            + pad_axis(padded_line[..., KZ + 2 : KZ + 4], last_axis, 0, KZ - 2)
        ).reshape(RHS, CX + 4, CY + 4, KZ)
        extended = with_halo(spread_tile, (("row", 1), ("col", 2)), 2)
        cycle_only = clear_inside(extended, ((1, CX), (2, CY)))
        folded = fold_cycle(fold_cycle(cycle_only, 1, CX), 2, CY)
        spectrum = jnp.einsum(
            "sxyz,zk->sxyk",
            spread_tile[:, 2 : CX + 2, 2 : CY + 2] + folded,
            hartley_z,
            precision=highest,
        )
        along_y = jnp.einsum(
            "sxyz,yk->sxkz",
            lax.all_to_all(spectrum, "col", split_axis=3, concat_axis=2, tiled=True),
            hartley_y,
            precision=highest,
        )
        along_x = (
            jnp.einsum(
                "sxyz,xk->skyz",
                lax.all_to_all(along_y, "row", split_axis=2, concat_axis=1, tiled=True),
                hartley_x,
                precision=highest,
            )
            * kernel[None]
        )
        mixed_part = jnp.einsum("sxyz,xk->skyz", along_x, hartley_x, precision=highest)
        returned = lax.all_to_all(mixed_part, "row", split_axis=1, concat_axis=2, tiled=True)
        swapped = jnp.einsum("sxyz,yk->sxkz", returned, hartley_y, precision=highest)
        restored = lax.all_to_all(swapped, "col", split_axis=2, concat_axis=3, tiled=True)
        padded = with_halo(
            jnp.einsum("sxyz,zk->sxyk", restored, hartley_z, precision=highest),
            (("row", 1), ("col", 2)),
            2,
        )
        line = padded.reshape(RHS, plane_count, KZ)
        extended_line = jnp.concatenate([line[..., KZ - 2 :], line, line[..., :2]], axis=-1)
        windows = jnp.stack(
            [
                extended_line[..., tile * slab_depth : tile * slab_depth + window_len]
                for tile in range(tile_count)
            ],
            axis=-2,
        )
        sampled = jnp.einsum("sptw,twb->sptb", windows, depth_table, precision=highest)
        with_flat = sampled[..., :TILE].reshape(RHS, plane_count, atom_count)
        with_slope = sampled[..., TILE:].reshape(RHS, plane_count, atom_count)
        recip_part = jnp.stack(
            [
                jnp.sum(with_flat * plane_dx[None], axis=1),
                jnp.sum(with_flat * plane_dy[None], axis=1),
                jnp.sum(with_slope * plane_flat[None], axis=1),
            ],
            axis=1,
        )
        image_field = direction / polar_wide - direct + recip_part - self_coef * direction
        step_size = (progress / inner_sum(direction, image_field))[:, None, None]
        solution = solution + step_size * direction
        residual = residual - step_size * image_field
        scaled_res = polar_wide * residual
        progress_next = inner_sum(residual, scaled_res)
        direction = scaled_res + (progress_next / progress)[:, None, None] * direction
        progress = progress_next
    return (solution[None, None], residual[None, None])


X_PAD = CX + 4
Y_PAD = CY + 4
SLOT_ROWS = 16
SPLIT = 2
VMEM_LIMIT = 60_000_000
SMALL_VMEM_LIMIT = 24_000_000
EARLY_TILES = 1
PAIR_ROWS = 32
GROUP = 8
SCREEN_SCALE = 0.4
SCREEN_COEF = (
    0.22567588090896606,
    0.2256690263748169,
    0.20785020291805267,
    0.16849851608276367,
    0.14156343042850494,
    -0.005832736846059561,
    0.16930203139781952,
    -0.1830107867717743,
    0.05028456076979637,
)


def halves(value):
    high = value.astype(jnp.bfloat16)
    return high, (value - high.astype(jnp.float32)).astype(jnp.bfloat16)


def halves_np(value):
    value = value.astype(np.float32)
    high = value.astype(ml_dtypes.bfloat16)
    return high, (value - high.astype(np.float32)).astype(ml_dtypes.bfloat16)


def product(left, right, left_dim=1, right_dim=0):
    def one(first, second):
        return lax.dot_general(
            first,
            second,
            (((left_dim,), (right_dim,)), ((), ())),
            preferred_element_type=jnp.float32,
        )

    return one(left[0], right[0]) + (one(left[1], right[0]) + one(left[0], right[1]))


def cas_np(wave, place, length):
    angles = 2.0 * np.pi / length * (wave[:, None] * place[None, :] % length)
    return np.cos(angles) + np.sin(angles)


def modulus_np(wave, length):
    coef = np.array([1.0, 11.0, 11.0, 1.0]) / 24.0
    angles = 2.0 * np.pi / length * (wave[:, None] * np.arange(4)[None, :])
    return (coef * np.cos(angles)).sum(1) ** 2 + (coef * np.sin(angles)).sum(1) ** 2


def influence_np(length_x, length_y, length_z):
    total = np.zeros((length_x, length_y, length_z))
    modulus = np.ones((length_x, length_y, length_z))
    excluded = np.zeros((length_x, length_y, length_z), bool)
    for axis, length in enumerate((length_x, length_y, length_z)):
        wave = np.arange(length)
        shape = [1, 1, 1]
        shape[axis] = length
        total = total + ((np.minimum(wave, length - wave) / length) ** 2).reshape(shape)
        modulus = modulus * modulus_np(wave, length).reshape(shape)
        excluded = excluded | (wave * 2 == length).reshape(shape)
    excluded[0, 0, 0] = True
    safe = np.where(excluded, 1.0, total)
    result = np.exp(-(np.pi**2) / ewald_beta**2 * safe) / (
        np.pi * safe * np.where(excluded, 1.0, modulus)
    )
    return np.where(excluded, 0.0, result) / (length_x * length_y * length_z)


def slab_tables(rows_count, cols_count):
    grid_x = CX * rows_count
    grid_y = CY * cols_count
    devices = rows_count * cols_count
    chunk = KZ // devices
    wave_z = (np.arange(devices)[None, :] * chunk + np.arange(chunk)[:, None]).reshape(-1)
    along_z = cas_np(wave_z, np.arange(KZ), KZ)
    place_x = np.arange(rows_count)[:, None] * CX + np.arange(X_PAD)[None, :] - 2
    along_x = cas_np(np.arange(grid_x), place_x.reshape(-1) % grid_x, grid_x)
    x_high, x_low = halves_np(along_x)
    forward_x = np.concatenate([x_high, x_low, x_high], axis=1)
    backward_x = np.concatenate([x_high.T, x_low.T, x_high.T], axis=1)
    place_y = (np.arange(cols_count)[:, None] * CY + np.arange(Y_PAD)[None, :] - 2) % grid_y
    along_y = cas_np(np.arange(grid_y), place_y.reshape(-1), grid_y)
    along_y = along_y.reshape(grid_y, cols_count, Y_PAD)
    units = chunk * RHS // SPLIT
    block = np.einsum("uv,kcy->cuyvk", np.eye(units), along_y)
    block = block.reshape(cols_count * units * Y_PAD, units * grid_y)
    kernel = influence_np(grid_x, grid_y, KZ).reshape(grid_x, grid_y, devices, chunk)
    kernel = np.transpose(kernel, (2, 0, 3, 1))[:, :, :, None, :]
    kernel = np.broadcast_to(kernel, (devices, grid_x, chunk, RHS, grid_y))
    kernel = kernel.reshape(devices, grid_x, SPLIT, units * grid_y)
    kernel = np.moveaxis(kernel, 2, 1).reshape(devices, SPLIT * grid_x, units * grid_y)
    kernel = kernel.astype(np.float32)
    return dict(
        along_z=halves_np(along_z),
        forward_x=forward_x,
        backward_x=backward_x,
        block=halves_np(block),
        kernel=kernel,
    )


def pack_body(rhs_ref, place_ref, polar_ref, start_ref, payload_ref):
    polar = polar_ref[...]
    start = read_rows(rhs_ref) * polar
    start_ref[...] = start
    place = [place_ref[dim] for dim in range(3)]
    everything = jnp.concatenate(place + [1.0 / jnp.sqrt(polar), start], axis=0)
    store_payload(payload_ref, everything)


def read_rows(rows_ref):
    return jnp.concatenate([rows_ref[dim] for dim in range(3)], axis=0)


def store_payload(payload_ref, everything):
    tile_count = everything.shape[1] // TILE
    for quantity in range(everything.shape[0]):
        for tile in range(tile_count):
            row = quantity * tile_count + tile
            payload_ref[row : row + 1, :] = everything[
                quantity : quantity + 1, tile * TILE : (tile + 1) * TILE
            ]


def placed_rows(slot, weights, extent):
    slot_index = lax.broadcasted_iota(jnp.int32, (extent, slot.shape[1]), 0)
    placed = jnp.zeros((extent, slot.shape[1]), jnp.float32)
    for stencil in range(5):
        target = slot + stencil
        if extent == KZ:
            target = jnp.where(target >= KZ, target - KZ, target)
        placed = placed + jnp.where(slot_index == target, weights[stencil], 0.0)
    return placed


def spread_into(message_ref, moment, rows_x, slope_x, rows_y, slope_y, depth, devices):
    blocks = []
    for step in range(X_PAD):
        flat_x = rows_x[step : step + 1]
        tilt_x = slope_x[step : step + 1]
        for rhs in range(RHS):
            part_x = tilt_x * moment[rhs : rhs + 1]
            part_y = flat_x * moment[RHS + rhs : RHS + rhs + 1]
            part_z = flat_x * moment[2 * RHS + rhs : 2 * RHS + rhs + 1]
            blocks.append(
                jnp.concatenate([part_x * rows_y + part_y * slope_y, part_z * rows_y], axis=1)
            )
    charges = jnp.concatenate(blocks, axis=0)
    spectrum = product(depth, halves(charges), 1, 1)
    slot_rows = message_ref.shape[0] // devices
    chunk = KZ // devices
    width = RHS * Y_PAD
    for step in range(X_PAD):
        message_ref[pl.ds(step, devices, stride=slot_rows), :] = jnp.concatenate(
            [
                spectrum[unit * devices : (unit + 1) * devices, step * width : (step + 1) * width]
                for unit in range(chunk)
            ],
            axis=1,
        )


def sample_from(message_ref, rows_x, slope_x, rows_y, slope_y, depth, devices):
    chunk = KZ // devices
    width = RHS * Y_PAD
    slot_rows = message_ref.shape[0] // devices
    pieces = [
        message_ref[pl.ds(step, devices, stride=slot_rows), :] for step in range(X_PAD)
    ]
    spare = jnp.zeros((devices, KZ - X_PAD * width), jnp.float32)
    spectrum = jnp.concatenate(
        [
            jnp.concatenate(
                [piece[:, unit * width : (unit + 1) * width] for piece in pieces] + [spare], axis=1
            )
            for unit in range(chunk)
        ],
        axis=0,
    )
    spectrum = jnp.transpose(spectrum)[: X_PAD * width]
    sampled = product(halves(spectrum), depth, 1, 0)
    atoms = rows_x.shape[1]
    fields = [None] * (3 * RHS)
    for rhs in range(RHS):
        sum_x = sum_y = sum_z = None
        for step in range(X_PAD):
            first = step * width + rhs * Y_PAD
            flat = sampled[first : first + Y_PAD, :atoms]
            tilt = sampled[first : first + Y_PAD, atoms:]
            part_x = slope_x[step : step + 1] * flat
            part_y = rows_x[step : step + 1] * flat
            part_z = rows_x[step : step + 1] * tilt
            sum_x = part_x if sum_x is None else sum_x + part_x
            sum_y = part_y if sum_y is None else sum_y + part_y
            sum_z = part_z if sum_z is None else sum_z + part_z
        fields[rhs] = jnp.sum(sum_x * rows_y, axis=0, keepdims=True)
        fields[RHS + rhs] = jnp.sum(sum_y * slope_y, axis=0, keepdims=True)
        fields[2 * RHS + rhs] = jnp.sum(sum_z * rows_y, axis=0, keepdims=True)
    return jnp.concatenate(fields, axis=0)


def read_tables(tables_ref):
    return (
        tables_ref[0:X_PAD],
        tables_ref[SLOT_ROWS : SLOT_ROWS + X_PAD],
        tables_ref[2 * SLOT_ROWS : 2 * SLOT_ROWS + Y_PAD],
        tables_ref[2 * SLOT_ROWS + Y_PAD : 2 * SLOT_ROWS + 2 * Y_PAD],
    )


def setup_body(
    lengths,
    devices,
    place_ref,
    base_ref,
    start_ref,
    z_high_ref,
    z_low_ref,
    message_ref,
    tables_ref,
    depth_high_ref,
    depth_low_ref,
):
    base = [base_ref[dim] for dim in range(3)]
    fractions = []
    cells = []
    for dim in range(3):
        cell = base[dim] + 2
        cell = jnp.where(cell >= lengths[dim], cell - lengths[dim], cell)
        cells.append(cell)
        fractions.append(place_ref[dim] - cell.astype(jnp.float32))
    values, slopes = spline_table(jnp.concatenate(fractions, axis=0))
    values = [[values[stencil][dim : dim + 1] for stencil in range(5)] for dim in range(3)]
    slopes = [[slopes[stencil][dim : dim + 1] for stencil in range(5)] for dim in range(3)]
    slot_x = lax.rem(cells[0], CX)
    slot_y = lax.rem(cells[1], CY)
    tables_ref[0:SLOT_ROWS] = placed_rows(slot_x, values[0], SLOT_ROWS)
    tables_ref[SLOT_ROWS : 2 * SLOT_ROWS] = placed_rows(slot_x, slopes[0], SLOT_ROWS)
    tables_ref[2 * SLOT_ROWS : 2 * SLOT_ROWS + Y_PAD] = placed_rows(slot_y, values[1], Y_PAD)
    tables_ref[2 * SLOT_ROWS + Y_PAD : 2 * SLOT_ROWS + 2 * Y_PAD] = placed_rows(
        slot_y, slopes[1], Y_PAD
    )
    window = jnp.concatenate(
        [
            placed_rows(base[2], values[2], KZ),
            placed_rows(base[2], slopes[2], KZ),
        ],
        axis=1,
    )
    depth = product((z_high_ref[...], z_low_ref[...]), halves(window), 1, 0)
    depth = halves(depth)
    depth_high_ref[...] = depth[0]
    depth_low_ref[...] = depth[1]
    spread_into(message_ref, start_ref[...], *read_tables(tables_ref), depth, devices)


def transform_in(message_ref, forward_ref, block_high_ref, block_low_ref, rows_count, cols_count):
    gathered = jnp.concatenate(
        [
            jnp.concatenate(
                [
                    message_ref[(r * cols_count + c) * X_PAD : (r * cols_count + c + 1) * X_PAD]
                    for r in range(rows_count)
                ],
                axis=0,
            )
            for c in range(cols_count)
        ],
        axis=1,
    )
    high, low = halves(gathered)
    along = jnp.dot(
        forward_ref[...],
        jnp.concatenate([high, high, low], axis=0),
        preferred_element_type=jnp.float32,
    )
    part = along.shape[1] // cols_count // SPLIT
    along = jnp.concatenate(
        [
            jnp.concatenate(
                [
                    along[:, (c * SPLIT + half) * part : (c * SPLIT + half + 1) * part]
                    for c in range(cols_count)
                ],
                axis=1,
            )
            for half in range(SPLIT)
        ],
        axis=0,
    )
    return product(halves(along), (block_high_ref[...], block_low_ref[...]))


def transform_out(result_ref, values, backward_ref, block_high_ref, block_low_ref, counts):
    rows_count, cols_count = counts
    spread = product(halves(values), (block_high_ref[...], block_low_ref[...]), 1, 1)
    grid_x = spread.shape[0] // SPLIT
    part = spread.shape[1] // cols_count
    spread = jnp.concatenate(
        [
            spread[half * grid_x : (half + 1) * grid_x, c * part : (c + 1) * part]
            for c in range(cols_count)
            for half in range(SPLIT)
        ],
        axis=1,
    )
    high, low = halves(spread)
    along = jnp.dot(
        backward_ref[...],
        jnp.concatenate([high, high, low], axis=0),
        preferred_element_type=jnp.float32,
    )
    width = along.shape[1] // cols_count
    slot_rows = result_ref.shape[0] // (rows_count * cols_count)
    for r in range(rows_count):
        for c in range(cols_count):
            first = (r * cols_count + c) * slot_rows
            result_ref[first : first + X_PAD, :] = along[
                r * X_PAD : (r + 1) * X_PAD, c * width : (c + 1) * width
            ]


def middle_first_body(
    counts,
    message_ref,
    kernel_ref,
    forward_ref,
    backward_ref,
    block_high_ref,
    block_low_ref,
    result_ref,
    wave_ref,
):
    wave = transform_in(message_ref, forward_ref, block_high_ref, block_low_ref, *counts)
    wave_ref[...] = wave
    transform_out(
        result_ref, wave * kernel_ref[...], backward_ref, block_high_ref, block_low_ref, counts
    )


def gather_rows(parts):
    tiles = [
        parts[GROUP * tile : GROUP * tile + GROUP, :] for tile in range(parts.shape[0] // GROUP)
    ]
    return jnp.concatenate(tiles, axis=1)[0 : 3 * RHS]


def row_total(value, rhs):
    row = lax.broadcasted_iota(jnp.int32, value.shape, 0)
    return total(jnp.where(lax.rem(row, RHS) == rhs, value, 0.0))


def total(value):
    return jnp.sum(jnp.sum(value, axis=0, keepdims=True), axis=1, keepdims=True)


def middle_second_body(
    counts,
    message_ref,
    kernel_ref,
    forward_ref,
    backward_ref,
    block_high_ref,
    block_low_ref,
    wave_ref,
    rhs_ref,
    start_ref,
    image_ref,
    second_ref,
    near_ref,
    polar_ref,
    result_ref,
):
    rhs_rows = read_rows(rhs_ref)
    near_rows = gather_rows(near_ref)
    wave = transform_in(message_ref, forward_ref, block_high_ref, block_low_ref, *counts)
    filtered = wave * kernel_ref[...]
    transform_out(result_ref, filtered, backward_ref, block_high_ref, block_low_ref, counts)
    before = wave_ref[...]
    grid_y = CY * counts[1]
    lane = lax.broadcasted_iota(jnp.int32, wave.shape, 1)
    own_rhs = lax.rem(lax.div(lane, grid_y), RHS)
    second = second_ref[...]
    start = start_ref[...]
    image = image_ref[...]
    local_part = second / polar_ref[...] - near_rows - self_coef * second
    slot = lax.broadcasted_iota(jnp.int32, (1, result_ref.shape[1]), 1)
    sums = jnp.zeros((1, result_ref.shape[1]), jnp.float32)
    for rhs in range(RHS):
        mine = own_rhs == rhs
        parts = (
            row_total(rhs_rows * start, rhs),
            row_total(start * image, rhs),
            row_total(second * image, rhs),
            row_total(start * local_part, rhs) + total(jnp.where(mine, before * filtered, 0.0)),
            row_total(second * local_part, rhs) + total(jnp.where(mine, wave * filtered, 0.0)),
        )
        for index, part in enumerate(parts):
            sums = jnp.where(slot == rhs * len(parts) + index, part, sums)
    devices = counts[0] * counts[1]
    result_ref[pl.ds(X_PAD, devices, stride=X_PAD + 1), :] = jnp.broadcast_to(
        sums, (devices, sums.shape[1])
    )


def sample_body(
    devices,
    message_ref,
    tables_ref,
    depth_high_ref,
    depth_low_ref,
    start_ref,
    near_ref,
    polar_ref,
    image_ref,
    second_ref,
    payload_ref,
):
    tables = read_tables(tables_ref)
    depth = (depth_high_ref[...], depth_low_ref[...])
    field = sample_from(message_ref, *tables, depth, devices)
    start = start_ref[...]
    polar = polar_ref[...]
    image = start / polar - gather_rows(near_ref) + field - self_coef * start
    second = polar * image
    image_ref[...] = image
    second_ref[...] = second
    store_payload(payload_ref, second)


def spread_body(
    devices,
    tables_ref,
    depth_high_ref,
    depth_low_ref,
    second_ref,
    result_ref,
):
    depth = (depth_high_ref[...], depth_low_ref[...])
    spread_into(result_ref, second_ref[...], *read_tables(tables_ref), depth, devices)


def final_body(
    devices,
    message_ref,
    tables_ref,
    depth_high_ref,
    depth_low_ref,
    rhs_ref,
    start_ref,
    image_ref,
    second_ref,
    near_ref,
    polar_ref,
    dipole_ref,
    residual_ref,
):
    tables = read_tables(tables_ref)
    depth = (depth_high_ref[...], depth_low_ref[...])
    field = sample_from(message_ref, *tables, depth, devices)
    second = second_ref[...]
    start = start_ref[...]
    image = image_ref[...]
    image_second = second / polar_ref[...] - gather_rows(near_ref) + field - self_coef * second
    sums = jnp.sum(
        message_ref[pl.ds(X_PAD, devices, stride=X_PAD + 1), :], axis=0, keepdims=True
    )
    steps = []
    for rhs in range(RHS):
        progress, start_image, second_image, start_next, second_next = [
            sums[:, rhs * 5 + index : rhs * 5 + index + 1] for index in range(5)
        ]
        step = progress / start_image
        progress_next = progress - 2.0 * step * start_image + step * step * second_image
        grown = 1.0 + progress_next / progress
        curvature = (
            grown * grown * start_image
            - step * grown * (start_next + second_image)
            + step * step * second_next
        )
        steps.append((step, grown, progress_next / curvature))
    row = lax.broadcasted_iota(jnp.int32, (RHS, 1), 0)
    step, grown, step_next = [
        sum(jnp.where(row == rhs, steps[rhs][index], 0.0) for rhs in range(RHS))
        for index in range(3)
    ]
    for dim in range(3):
        rows = slice(dim * RHS, (dim + 1) * RHS)
        direction = grown * start[rows] - step * second[rows]
        image_direction = grown * image[rows] - step * image_second[rows]
        dipole_ref[dim] = step * start[rows] + step_next * direction
        residual_ref[dim] = rhs_ref[dim] - step * image[rows] - step_next * image_direction


def near_base(entry, brick_rows):
    return lax.shift_right_logical(entry, 2) * brick_rows + lax.bitwise_and(entry, 3)


def fill_near(scratch, up_ref, stack_ref, down_ref):
    rows = stack_ref.shape[0]
    scratch[0:rows, :] = up_ref[...]
    scratch[rows : 2 * rows, :] = stack_ref[...]
    scratch[2 * rows : 3 * rows, :] = down_ref[...]


def nearest(places, origin, span):
    return places - span * jnp.floor((places - origin) * (1.0 / span) + 0.5)


def unwrap_near(near, tile_count, spans):
    rows = near.shape[0] // 9
    for dim in range(2):
        own = 4 * rows + dim * tile_count
        origin = near[own : own + 1, 0:1]
        for brick in range(9):
            first = brick * rows + dim * tile_count
            near[first : first + tile_count, :] = nearest(
                near[first : first + tile_count, :], origin, spans[dim]
            )


def pick_rows(picked, near, lists_ref, tile, place, tile_count, quantities, origin, span):
    rows = near.shape[0] // 9
    place = place * lists_ref.shape[1] * quantities * GROUP
    for entry in range(lists_ref.shape[1]):
        base = near_base(lists_ref[tile, entry], rows)
        for quantity in range(quantities):
            values = near[pl.ds(base + quantity * tile_count, 1), :]
            if quantity == 2 and span is not None:
                values = nearest(values, origin, span)
            first = place + (entry * quantities + quantity) * GROUP
            picked[first : first + GROUP, :] = jnp.broadcast_to(values, (GROUP, TILE))


def widen_own(near, quantities, tile_count, tile, place, wide):
    offset = near.shape[0] // 9 * 4
    rows = [
        near[offset + quantity * tile_count + tile : offset + quantity * tile_count + tile + 1, :]
        for quantity in range(quantities)
    ]
    spare = jnp.zeros((TILE - quantities, TILE), jnp.float32)
    columns = jnp.transpose(jnp.concatenate(rows + [spare], axis=0))
    for quantity in range(quantities):
        first = (place * quantities + quantity) * TILE
        wide[first : first + TILE, :] = jnp.broadcast_to(
            columns[:, quantity : quantity + 1], (TILE, TILE)
        )


def add_field(sums, first_term, second_term, apart, moments):
    for rhs in range(RHS):
        moment = [moments[RHS * dim + rhs] for dim in range(3)]
        projected = moment[0] * apart[0] + moment[1] * apart[1] + moment[2] * apart[2]
        weighted = second_term * projected
        for dim in range(3):
            index = RHS * dim + rhs
            sums[index] = sums[index] + (weighted * apart[dim] - first_term * moment[dim])


def finish_sums(field_ref, sums_ref, first_tile, place):
    place = place * 3 * RHS
    lane = lax.broadcasted_iota(jnp.int32, (TILE, TILE), 1)
    merged = jnp.zeros((TILE, TILE), jnp.float32)
    for index in range(3 * RHS):
        first = (place + index) * TILE
        column = jnp.sum(sums_ref[first : first + TILE, :], axis=1, keepdims=True)
        merged = jnp.where(lane == index, column, merged)
    first = (first_tile + place // (3 * RHS)) * GROUP
    field_ref[first : first + GROUP, :] = jnp.transpose(merged)[0:GROUP]


def pair_rows(start, group):
    return pl.ds(pl.multiple_of(start + group * GROUP, GROUP), GROUP)


def wide_rows(start, group, quantity):
    return pl.ds(pl.multiple_of(quantity * TILE + start + group * GROUP, GROUP), GROUP)


def pair_terms(square_dist, damp):
    inverse = lax.rsqrt(square_dist)
    distance = square_dist * inverse
    inverse_sq = inverse * inverse
    inverse_cube = inverse_sq * inverse
    cubed = damp * (distance * square_dist)
    damping = jnp.exp(cubed)
    bell = jnp.exp(-(ewald_beta * ewald_beta) * square_dist)
    stretched = 1.0 + (SCREEN_SCALE * ewald_beta) * distance
    turned = pl.reciprocal(stretched, approx=True)
    turned = turned * (2.0 - stretched * turned)
    series = SCREEN_COEF[-1] * turned + SCREEN_COEF[-2]
    for coef in SCREEN_COEF[-3::-1]:
        series = series * turned + coef
    screen = bell * turned * series
    gaussian = (2.0 * ewald_beta / math.sqrt(math.pi)) * bell
    bare = screen - damping
    first_term = bare * inverse_cube + gaussian * inverse_sq
    second_term = (
        3.0 * (first_term + (cubed * damping) * inverse_cube)
        + (2.0 * ewald_beta * ewald_beta) * gaussian
    ) * inverse_sq
    return first_term, second_term


def pair_first_body(
    first_tile,
    last_tile,
    tile_count,
    spans,
    lists_ref,
    up_ref,
    stack_ref,
    down_ref,
    *others,
):
    first_ref, second_ref, field_ref, near_ref, near, picked, wide, sums_ref = others[-8:]
    quantities = near.shape[0] // 9 // tile_count
    step = pl.program_id(0)
    entries = lists_ref.shape[1]

    @pl.when(step == 0)
    def _():
        fill_near(near, up_ref, stack_ref, down_ref)
        unwrap_near(near, tile_count, spans)
        rows = near.shape[0] // 9
        kept = 3 * tile_count
        for brick in range(9):
            near_ref[brick * kept : (brick + 1) * kept, :] = near[
                brick * rows : brick * rows + kept, :
            ]
        for place, tile in enumerate(range(first_tile, last_tile)):
            widen_own(near, 4, tile_count, tile, place, wide)
            own = near.shape[0] // 9 * 4 + 2 * tile_count + tile
            origin = near[own : own + 1, 0:1]
            pick_rows(
                picked, near, lists_ref, tile, place, tile_count, quantities, origin, spans[2]
            )
        if first_tile > 0:
            field_ref[0 : first_tile * GROUP, :] = others[0][...]

    picked = picked.at[tile_rows(step, entries * quantities * GROUP), :]
    wide = wide.at[tile_rows(step, 4 * TILE), :]
    step_sums = sums_ref.at[tile_rows(step, 3 * RHS * TILE), :]

    @pl.loop(0, TILE // PAIR_ROWS)
    def _(part):
        start = part * PAIR_ROWS
        for group in range(PAIR_ROWS // GROUP):
            own = [wide[wide_rows(start, group, dim), :] for dim in range(4)]
            own_damp = -thole_a * own[3]
            sums = [jnp.zeros((GROUP, TILE), jnp.float32) for _ in range(3 * RHS)]
            itself = (
                lax.broadcasted_iota(jnp.int32, (GROUP, TILE), 0) + (start + group * GROUP)
            ) == lax.broadcasted_iota(jnp.int32, (GROUP, TILE), 1)
            for entry in range(entries):
                first = entry * quantities * GROUP
                rows = [
                    picked[first + quantity * GROUP : first + (quantity + 1) * GROUP, :]
                    for quantity in range(quantities)
                ]
                apart = [rows[dim] - own[dim] for dim in range(3)]
                square_dist = apart[0] * apart[0] + apart[1] * apart[1] + apart[2] * apart[2]
                if entry == 0:
                    square_dist = jnp.where(itself, 1.0, square_dist)
                first_term, second_term = pair_terms(square_dist, own_damp * rows[3])
                if entry == 0:
                    first_term = jnp.where(itself, 0.0, first_term)
                    second_term = jnp.where(itself, 0.0, second_term)
                place = wide_rows(start, group, entry)
                first_ref[place, :] = first_term
                second_ref[place, :] = second_term
                add_field(sums, first_term, second_term, apart, rows[4:])
            for index, value in enumerate(sums):
                step_sums[wide_rows(start, group, index), :] = value

    @pl.when(step == last_tile - first_tile - 1)
    def _():
        for place in range(last_tile - first_tile):
            finish_sums(field_ref, sums_ref, first_tile, place)


def tile_rows(step, rows):
    return pl.ds(pl.multiple_of(step * rows, GROUP), rows)


def pair_second_body(
    tile_count,
    spans,
    lists_ref,
    near,
    up_ref,
    stack_ref,
    down_ref,
    first_ref,
    second_ref,
    field_ref,
    near_moment,
    picked,
    picked_moment,
    wide,
    sums_ref,
):
    step = pl.program_id(0)
    entries = lists_ref.shape[1]

    @pl.when(step == 0)
    def _():
        fill_near(near_moment, up_ref, stack_ref, down_ref)
        for tile in range(tile_count):
            widen_own(near, 3, tile_count, tile, tile, wide)
            own = near.shape[0] // 9 * 4 + 2 * tile_count + tile
            origin = near[own : own + 1, 0:1]
            pick_rows(picked, near, lists_ref, tile, tile, tile_count, 3, origin, spans[2])
            pick_rows(
                picked_moment, near_moment, lists_ref, tile, tile, tile_count, 3 * RHS, None, None
            )

    picked = picked.at[tile_rows(step, entries * 3 * GROUP), :]
    picked_moment = picked_moment.at[tile_rows(step, entries * 3 * RHS * GROUP), :]
    wide = wide.at[tile_rows(step, 3 * TILE), :]
    step_sums = sums_ref.at[tile_rows(step, 3 * RHS * TILE), :]

    @pl.loop(0, TILE // PAIR_ROWS)
    def _(part):
        start = part * PAIR_ROWS
        for group in range(PAIR_ROWS // GROUP):
            own = [wide[wide_rows(start, group, dim), :] for dim in range(3)]
            sums = [jnp.zeros((GROUP, TILE), jnp.float32) for _ in range(3 * RHS)]
            for entry in range(entries):
                first = entry * 3 * GROUP
                apart = [
                    picked[first + dim * GROUP : first + (dim + 1) * GROUP, :] - own[dim]
                    for dim in range(3)
                ]
                first = first * RHS
                moments = [
                    picked_moment[first + index * GROUP : first + (index + 1) * GROUP, :]
                    for index in range(3 * RHS)
                ]
                place = wide_rows(start, group, entry)
                add_field(sums, first_ref[place, :], second_ref[place, :], apart, moments)
            for index, value in enumerate(sums):
                step_sums[wide_rows(start, group, index), :] = value

    @pl.when(step == tile_count - 1)
    def _():
        for place in range(tile_count):
            finish_sums(field_ref, sums_ref, 0, place)


def shift(source, axis, step):
    count = lax.axis_size(axis)
    return lax.ppermute(source, axis, [(i, (i + step) % count) for i in range(count)])


def both_ways(source, axis):
    return shift(source, axis, 1), source, shift(source, axis, -1)


def whole(shape):
    return pl.BlockSpec(shape, lambda *_: (0,) * len(shape))


def anywhere():
    return pl.BlockSpec(memory_space=pl.ANY)


def pairwise(source, axis):
    count = lax.axis_size(axis)
    first = lax.ppermute(source, axis, [(i, i ^ 1) for i in range(count)])
    second = lax.ppermute(
        source, axis, [(i, (i + 1 if i % 2 else i - 1) % count) for i in range(count)]
    )
    return first, second


def join(message, payload):
    first, second = pairwise(payload, "col")
    even = lax.rem(lax.axis_index("col"), 2) == 0
    left = jnp.where(even, second, first)
    right = jnp.where(even, first, second)
    message, left, right = lax.optimization_barrier((message, left, right))
    return message, both_ways(jnp.concatenate([left, payload, right], axis=0), "row")


class Fetched:
    def __init__(self, source, scratch, semaphore):
        self.copy = pltpu.make_async_copy(source, scratch, semaphore)
        self.copy.start()
        self.scratch = scratch
        self.shape = scratch.shape
        self.waiting = True

    def wait(self):
        if self.waiting:
            self.copy.wait()
            self.waiting = False

    def __getitem__(self, index):
        self.wait()
        return self.scratch[index]


def call(body, outs, *operands, after=(), own_block=None):
    fetched = [
        pltpu.VMEM(operand.shape[1:] if index == own_block else operand.shape, operand.dtype)
        for index, operand in enumerate(operands)
    ]
    count = len(operands)

    def run(*refs):
        refs = refs[len(after) :]
        sources, refs = refs[:count], refs[count:]
        results, refs = refs[: len(outs)], refs[len(outs) :]
        targets, written, semaphore = refs[:count], refs[count:-1], refs[-1]
        inputs = []
        for index, source in enumerate(sources):
            if index == own_block:
                place = lax.axis_index("row") * lax.axis_size("col") + lax.axis_index("col")
                source = source.at[place]
            inputs.append(Fetched(source, targets[index], semaphore.at[index]))
        body(*inputs, *written)
        for operand in inputs:
            operand.wait()
        copies = [
            pltpu.make_async_copy(value, result, semaphore.at[count + index])
            for index, (value, result) in enumerate(zip(written, results))
        ]
        for copy in copies:
            copy.start()
        for copy in copies:
            copy.wait()

    return pl.pallas_call(
        run,
        in_specs=[anywhere()] * (len(after) + count),
        out_specs=[anywhere()] * len(outs),
        out_shape=[jax.ShapeDtypeStruct(shape, dtype) for shape, dtype in outs],
        scratch_shapes=fetched
        + [pltpu.VMEM(shape, dtype) for shape, dtype in outs]
        + [pltpu.SemaphoreType.DMA((count + len(outs),))],
        compiler_params=pltpu.CompilerParams(vmem_limit_bytes=VMEM_LIMIT),
        cost_estimate=pl.CostEstimate(
            flops=200_000_000, bytes_accessed=4 << 20, transcendentals=0
        ),
    )(*after, *operands)


def final_call(body, outs, *operands):
    return pl.pallas_call(
        body,
        grid=(1,),
        in_specs=[whole(operand.shape) for operand in operands],
        out_specs=[whole(shape) for shape, _ in outs],
        out_shape=[jax.ShapeDtypeStruct(shape, dtype) for shape, dtype in outs],
        compiler_params=pltpu.CompilerParams(vmem_limit_bytes=SMALL_VMEM_LIMIT),
    )(*operands)


def pair_call(body, outs, kept, first_tile, last_tile, blocked, scratch, lists, *operands, after=()):
    tiles = lists.shape[0]

    def block(operand):
        rows = operand.shape[0] // tiles
        return pl.BlockSpec((rows, operand.shape[1]), lambda i, s: (first_tile + i, 0))

    out_shape = [jax.ShapeDtypeStruct(shape, jnp.float32) for shape in outs + kept]
    plain = len(operands) - blocked
    aliases = {}
    if first_tile > 0:
        first = 1 + len(operands) + len(after) - len(outs)
        aliases = {first + index: index for index in range(len(outs))}
    return pl.pallas_call(
        body,
        out_shape=out_shape,
        grid_spec=pltpu.PrefetchScalarGridSpec(
            num_scalar_prefetch=1,
            grid=(last_tile - first_tile,),
            in_specs=[whole(operand.shape) for operand in operands[:plain]]
            + [block(operand) for operand in operands[plain:]]
            + [anywhere()] * len(after),
            out_specs=[block(shape) for shape in out_shape[: len(outs)]]
            + [whole(shape) for shape in kept],
            scratch_shapes=[pltpu.VMEM(shape, jnp.float32) for shape in scratch],
        ),
        input_output_aliases=aliases,
        compiler_params=pltpu.CompilerParams(vmem_limit_bytes=VMEM_LIMIT),
        cost_estimate=pl.CostEstimate(
            flops=80_000_000, bytes_accessed=8 << 20, transcendentals=1 << 21
        ),
    )(lists, *operands, *after)


def exchange(message, devices):
    shape = message.shape
    sent = message.reshape(devices, 1, -1)
    return lax.all_to_all(sent, ("row", "col"), split_axis=0, concat_axis=0, tiled=True).reshape(
        shape
    )


def slab_local(field_rhs, positions, polar, grid_base, tile_lists):
    rows_count = lax.axis_size("row")
    cols_count = lax.axis_size("col")
    counts = (rows_count, cols_count)
    devices = rows_count * cols_count
    lengths = (CX * rows_count, CY * cols_count, KZ)
    spans = tuple(float(length) for length in lengths)
    atoms = polar.shape[-1]
    tile_count = atoms // TILE
    listed = tile_lists.shape[-1]
    tables = slab_tables(rows_count, cols_count)
    f32 = jnp.float32
    rhs = jnp.swapaxes(field_rhs[0, 0], 0, 1)
    place = jnp.swapaxes(positions[0], 0, 1)
    base = jnp.swapaxes(grid_base[0], 0, 1)
    polar = polar.reshape(1, atoms)
    lists = tile_lists[0, 0]
    quantities = 4 + 3 * RHS
    brick_rows = quantities * tile_count
    moment_rows = 3 * RHS * tile_count
    message_shape = (devices * X_PAD, KZ // devices * RHS * Y_PAD)
    last_shape = (devices * (X_PAD + 1), message_shape[1])
    row_shape = (3 * RHS, atoms)

    start, payload = call(pack_body, [(row_shape, f32), ((brick_rows, TILE), f32)], rhs, place, polar)

    def setup(*refs):
        setup_body(lengths, devices, *refs)

    message, splines, depth_high, depth_low = call(
        setup,
        [
            (message_shape, f32),
            ((2 * SLOT_ROWS + 2 * Y_PAD, atoms), f32),
            ((KZ, 2 * atoms), jnp.bfloat16),
            ((KZ, 2 * atoms), jnp.bfloat16),
        ],
        place,
        base,
        start,
        *[jnp.asarray(table) for table in tables["along_z"]],
    )
    constants = (
        jnp.asarray(tables["kernel"]),
        jnp.asarray(tables["forward_x"]),
        jnp.asarray(tables["backward_x"]),
        *[jnp.asarray(table) for table in tables["block"]],
    )
    message, near = join(message, payload)
    arrived = exchange(message, devices)

    def pair_first(first_tile, last_tile, fields, *after):
        def body(*refs):
            pair_first_body(first_tile, last_tile, tile_count, spans, *refs)

        tiles = last_tile - first_tile
        return pair_call(
            body,
            [(tile_count * listed * TILE, TILE)] * 2,
            [(last_tile * GROUP, TILE), (9 * 3 * tile_count, TILE)],
            first_tile,
            last_tile,
            0,
            [
                (9 * brick_rows, TILE),
                (tiles * listed * quantities * GROUP, TILE),
                (tiles * 4 * TILE, TILE),
                (tiles * 3 * RHS * TILE, TILE),
            ],
            lists,
            *near,
            *fields,
            after=after,
        )

    early = pair_first(0, EARLY_TILES, (), message)

    def middle_first(*refs):
        middle_first_body(counts, *refs)

    mixed, wave = call(
        middle_first,
        [(message_shape, f32), (tables["kernel"].shape[1:], f32)],
        arrived,
        *constants,
        after=(early[2],),
        own_block=1,
    )
    returned = exchange(mixed, devices)
    first_term, second_term, direct, near = pair_first(
        EARLY_TILES, tile_count, (early[2],), wave, *early[:2]
    )

    def sample(*refs):
        sample_body(devices, *refs)

    image, second, moments = call(
        sample,
        [(row_shape, f32), (row_shape, f32), ((moment_rows, TILE), f32)],
        returned,
        splines,
        depth_high,
        depth_low,
        start,
        direct,
        polar,
    )

    def spread(*refs):
        spread_body(devices, *refs)

    (message,) = call(spread, [(message_shape, f32)], splines, depth_high, depth_low, second)
    message, near_moments = join(message, moments)
    arrived = exchange(message, devices)

    def pair_second(*refs):
        pair_second_body(tile_count, spans, *refs)

    (direct,) = pair_call(
        pair_second,
        [],
        [(tile_count * GROUP, TILE)],
        0,
        tile_count,
        2,
        [
            (9 * moment_rows, TILE),
            (tile_count * listed * 3 * GROUP, TILE),
            (tile_count * listed * 3 * RHS * GROUP, TILE),
            (tile_count * 3 * TILE, TILE),
            (tile_count * 3 * RHS * TILE, TILE),
        ],
        lists,
        near,
        *near_moments,
        first_term,
        second_term,
    )

    def middle_second(*refs):
        middle_second_body(counts, *refs)

    (mixed,) = call(
        middle_second,
        [(last_shape, f32)],
        arrived,
        *constants,
        wave,
        rhs,
        start,
        image,
        second,
        direct,
        polar,
        own_block=1,
    )
    returned = exchange(mixed, devices)

    def final(*refs):
        final_body(devices, *refs)

    outs = final_call(
        final,
        [(rhs.shape, f32), (rhs.shape, f32)],
        returned,
        splines,
        depth_high,
        depth_low,
        rhs,
        start,
        image,
        second,
        direct,
        polar,
    )
    return tuple(jnp.swapaxes(out, 0, 1)[None, None] for out in outs)


def solution(mesh):
    placed = (
        P("row", "col", None, None, None),
        P("row", "col", None, None),
        P("row", "col", None),
        P("row", "col", None, None),
        P("row", "col", None, None),
    )
    devices = mesh.shape["row"] * mesh.shape["col"]
    return jax.shard_map(
        slab_local if KZ % devices == 0 else pencil_local,
        mesh=mesh,
        in_specs=placed,
        out_specs=(P("row", "col", None, None, None), P("row", "col", None, None, None)),
        check_vma=False,
    )
```

```python
import math

import jax
import jax.numpy as jnp
import ml_dtypes
import numpy as np
from jax import lax
from jax.experimental import pallas as pl
from jax.experimental.pallas import tpu as pltpu
from jax.sharding import PartitionSpec as P

CX = 8
CY = 4
KZ = 256
TILE = 128
RHS = 2
ITERS = 2


ewald_beta = 0.4
thole_a = 0.39
self_coef = 4.0 * ewald_beta**3 / (3.0 * math.sqrt(math.pi))
highest = lax.Precision.HIGHEST


def with_halo(cells, sides, width):
    for axis, dim in sides:
        count = lax.axis_size(axis)
        head = lax.slice_in_dim(cells, 0, width, axis=dim)
        tail = lax.slice_in_dim(cells, cells.shape[dim] - width, cells.shape[dim], axis=dim)
        cells = jnp.concatenate(
            [
                lax.ppermute(tail, axis, [(i, (i + 1) % count) for i in range(count)]),
                cells,
                lax.ppermute(head, axis, [((i + 1) % count, i) for i in range(count)]),
            ],
            axis=dim,
        )
    return cells


def spline_table(fraction):
    previous = {0: jnp.ones_like(fraction)}
    fourth = previous
    for degree in range(2, 6):
        current = {}
        for offset in range(degree):
            abscissa = fraction + offset
            summed = abscissa * previous.get(offset, 0.0) + (degree - abscissa) * previous.get(
                offset - 1, 0.0
            )
            current[offset] = summed / (degree - 1)
        if degree == 4:
            fourth = current
        previous = current
    values = jnp.stack([previous[4 - stencil] for stencil in range(5)])
    slopes = jnp.stack(
        [fourth.get(4 - stencil, 0.0) - fourth.get(3 - stencil, 0.0) for stencil in range(5)]
    )
    return (values, slopes)


def spline_modulus(wave_index, length):
    spline_coef = (1.0 / 24.0, 11.0 / 24.0, 11.0 / 24.0, 1.0 / 24.0)
    cosine_sum = jnp.zeros(wave_index.shape, jnp.float32)
    sine_sum = jnp.zeros(wave_index.shape, jnp.float32)
    for offset in range(4):
        angles = 2.0 * math.pi / length * (wave_index * offset % length).astype(jnp.float32)
        cosine_sum = cosine_sum + spline_coef[offset] * jnp.cos(angles)
        sine_sum = sine_sum + spline_coef[offset] * jnp.sin(angles)
    return cosine_sum * cosine_sum + sine_sum * sine_sum


def folded_square(wave_index, length):
    nearest = jnp.minimum(wave_index, length - wave_index).astype(jnp.float32) / length
    return nearest * nearest


def influence(wave_x, wave_y, wave_z, length_x, length_y, length_z):
    wave_norm = (
        folded_square(wave_x, length_x)
        + folded_square(wave_y, length_y)
        + folded_square(wave_z, length_z)
    )
    modulus = (
        spline_modulus(wave_x, length_x)
        * spline_modulus(wave_y, length_y)
        * spline_modulus(wave_z, length_z)
    )
    excluded = (wave_x * 2 == length_x) | (wave_y * 2 == length_y) | (wave_z * 2 == length_z)
    excluded = excluded | (wave_x == 0) & (wave_y == 0) & (wave_z == 0)
    safe_norm = jnp.where(excluded, 1.0, wave_norm)
    safe_modulus = jnp.where(excluded, 1.0, modulus)
    result = jnp.exp(-(math.pi**2 / ewald_beta**2) * safe_norm) / (
        math.pi * safe_norm * safe_modulus
    )
    return jnp.where(excluded, 0.0, result)


def tile_field(own_static, near_static, near_dipole, box_spans):
    listed_count = near_static.shape[0]
    tile_width = own_static.shape[1]
    box_span = jnp.array(box_spans, dtype=jnp.float32)[None, :, None, None]
    separation = near_static[:, 0:3, None, :] - own_static[None, 0:3, :, None]
    separation = separation - box_span * jnp.floor(separation / box_span + 0.5)
    dist_sq = jnp.sum(separation * separation, axis=1)
    itself = (jnp.arange(listed_count)[:, None, None] == 0) & (
        jnp.arange(tile_width)[:, None] == jnp.arange(tile_width)[None, :]
    )[None]
    safe_sq = jnp.where(itself, 1.0, dist_sq)
    distance = jnp.sqrt(safe_sq)
    scaled = distance / (own_static[3][None, :, None] * near_static[:, 3][:, None, :])
    cubed = thole_a * scaled * scaled * scaled
    damping = jnp.exp(-cubed)
    screen = lax.erfc(ewald_beta * distance)
    gaussian = 2.0 * ewald_beta / math.sqrt(math.pi) * jnp.exp(-(ewald_beta * ewald_beta) * safe_sq)
    inverse_sq = 1.0 / safe_sq
    inverse_cube = inverse_sq / distance
    first_term = (screen - damping) * inverse_cube + gaussian * inverse_sq
    second = (
        3.0 * (screen - (1.0 + cubed) * damping) * inverse_cube * inverse_sq
        + gaussian * (2.0 * ewald_beta * ewald_beta + 3.0 * inverse_sq) * inverse_sq
    )
    first_term = jnp.where(itself, 0.0, first_term)
    second = jnp.where(itself, 0.0, second)
    projected = jnp.sum(near_dipole[:, :, :, None, :] * separation[:, None, :, :, :], axis=2)
    weighted = second[:, None] * projected
    outward = jnp.sum(weighted[:, :, None] * separation[:, None], axis=(0, 4))
    inward = jnp.sum(first_term[:, None, None] * near_dipole[:, :, :, None, :], axis=(0, 4))
    return outward - inward


def hartley(length):
    counter = jnp.arange(length, dtype=jnp.int32)
    angles = (
        2.0 * math.pi / length * (counter[:, None] * counter[None, :] % length).astype(jnp.float32)
    )
    return jnp.cos(angles) + jnp.sin(angles)


def placed_table(first_cell, weights, extent):
    slot_index = jnp.arange(extent, dtype=jnp.int32)[:, None]
    placed = jnp.zeros((extent, first_cell.shape[0]), jnp.float32)
    for stencil in range(5):
        placed = placed + jnp.where(
            slot_index == (first_cell[None, :] + stencil) % extent, weights[stencil][None, :], 0.0
        )
    return placed


def pad_axis(source, axis_pos, leading, trailing):
    widths = [(0, 0)] * source.ndim
    widths[axis_pos] = (leading, trailing)
    return jnp.pad(source, widths)


def fold_cycle(cycle_only, axis_pos, inner_len):
    middle = lax.slice_in_dim(cycle_only, 4, inner_len + 4, axis=axis_pos)
    lower_cycle = lax.slice_in_dim(cycle_only, 0, 2, axis=axis_pos)
    upper_cycle = lax.slice_in_dim(cycle_only, inner_len + 6, inner_len + 8, axis=axis_pos)
    return (
        middle
        + pad_axis(lower_cycle, axis_pos, 0, inner_len - 2)
        + pad_axis(upper_cycle, axis_pos, inner_len - 2, 0)
    )


def clear_inside(extended, extents):
    inside = None
    for axis_pos, inner_len in extents:
        slot_index = lax.broadcasted_iota(jnp.int32, extended.shape, axis_pos)
        within = (slot_index >= 2) & (slot_index < inner_len + 6)
        inside = within if inside is None else inside & within
    return jnp.where(inside, 0.0, extended)


def inner_sum(left_arr, right_arr):
    return lax.psum(jnp.sum(left_arr * right_arr, axis=(1, 2)), ("row", "col"))


def pencil_local(field_rhs, positions, polar, grid_base, tile_lists):
    rows_count = lax.axis_size("row")
    cols_count = lax.axis_size("col")
    grid_x = CX * rows_count
    grid_y = CY * cols_count
    atom_count = polar.shape[-1]
    tile_count = atom_count // TILE
    slab_depth = KZ // tile_count
    window_len = slab_depth + 4
    box_spans = (float(grid_x), float(grid_y), float(KZ))
    own_place = positions[0, 0]
    own_base = grid_base[0, 0]
    own_polar = polar[0, 0]
    lengths = jnp.array([grid_x, grid_y, KZ], dtype=jnp.int32)[:, None]
    cell_index = (own_base + 2) % lengths
    fraction = own_place - cell_index.astype(jnp.float32)
    values, slopes = spline_table(fraction)
    first_x = (own_base[0] - lax.axis_index("row") * CX + 2) % grid_x
    first_y = (own_base[1] - lax.axis_index("col") * CY + 2) % grid_y
    rows_x = placed_table(first_x, values[:, 0], CX + 4)
    slope_x = placed_table(first_x, slopes[:, 0], CX + 4)
    rows_y = placed_table(first_y, values[:, 1], CY + 4)
    slope_y = placed_table(first_y, slopes[:, 1], CY + 4)
    tile_start = jnp.arange(atom_count, dtype=jnp.int32) // TILE * slab_depth
    first_z = (own_base[2] + 2 - tile_start) % KZ
    rows_z = placed_table(first_z, values[:, 2], window_len)
    slope_z = placed_table(first_z, slopes[:, 2], window_len)
    plane_count = (CX + 4) * (CY + 4)
    plane_dx = (slope_x[:, None, :] * rows_y[None, :, :]).reshape(plane_count, atom_count)
    plane_dy = (rows_x[:, None, :] * slope_y[None, :, :]).reshape(plane_count, atom_count)
    plane_flat = (rows_x[:, None, :] * rows_y[None, :, :]).reshape(plane_count, atom_count)
    window_rows = jnp.moveaxis(rows_z.reshape(window_len, tile_count, TILE), 1, 0)
    window_slope = jnp.moveaxis(slope_z.reshape(window_len, tile_count, TILE), 1, 0)
    depth_table = jnp.concatenate([window_rows, window_slope], axis=2)
    grid_scale = 1.0 / (grid_x * grid_y * KZ)
    hartley_x = hartley(grid_x)
    hartley_y = hartley(grid_y)
    hartley_z = hartley(KZ)
    block_y = grid_y // rows_count
    block_z = KZ // cols_count
    wave_x = jnp.arange(grid_x, dtype=jnp.int32)[:, None, None]
    wave_y = (lax.axis_index("row") * block_y + jnp.arange(block_y, dtype=jnp.int32))[None, :, None]
    wave_z = (lax.axis_index("col") * block_z + jnp.arange(block_z, dtype=jnp.int32))[None, None, :]
    kernel = influence(wave_x, wave_y, wave_z, grid_x, grid_y, KZ) * grid_scale
    root_scale = jnp.power(own_polar, 1.0 / 6.0)
    own_static = jnp.concatenate([own_place, root_scale[None]], axis=0)
    near_static = with_halo(own_static[None, None], (("row", 0), ("col", 1)), 1)
    near_static = jnp.moveaxis(near_static.reshape(9, 4, tile_count, TILE), 2, 1).reshape(
        9 * tile_count, 4, TILE
    )
    own_tiles = jnp.moveaxis(own_static.reshape(4, tile_count, TILE), 1, 0)
    own_lists = tile_lists[0, 0]
    polar_wide = own_polar[None, None, :]
    solution = jnp.zeros_like(field_rhs[0, 0])
    residual = field_rhs[0, 0]
    scaled_res = polar_wide * residual
    direction = scaled_res
    progress = inner_sum(residual, scaled_res)
    for iteration in range(ITERS):
        near_dip = with_halo(direction[None, None], (("row", 0), ("col", 1)), 1)
        near_dip = jnp.moveaxis(near_dip.reshape(9, RHS, 3, tile_count, TILE), 3, 1).reshape(
            9 * tile_count, RHS, 3, TILE
        )

        def one_tile(tile_pos):
            picked = own_lists[tile_pos]
            return tile_field(own_tiles[tile_pos], near_static[picked], near_dip[picked], box_spans)

        fields = lax.map(one_tile, jnp.arange(tile_count, dtype=jnp.int32))
        direct = jnp.moveaxis(fields, 0, 2).reshape(RHS, 3, atom_count)
        slope_terms = (
            direction[:, 0, None, :] * plane_dx[None] + direction[:, 1, None, :] * plane_dy[None]
        )
        flat_terms = direction[:, 2, None, :] * plane_flat[None]
        spread_left = jnp.concatenate(
            [
                slope_terms.reshape(RHS, plane_count, tile_count, TILE),
                flat_terms.reshape(RHS, plane_count, tile_count, TILE),
            ],
            axis=3,
        )
        spread_windows = jnp.einsum("sptb,twb->sptw", spread_left, depth_table, precision=highest)
        main_part = spread_windows[..., :slab_depth].reshape(spread_windows.shape[:-2] + (KZ,))
        tail_part = pad_axis(
            spread_windows[..., slab_depth:], spread_windows.ndim - 1, 0, slab_depth - 4
        )
        tail_part = tail_part.reshape(spread_windows.shape[:-2] + (KZ,))[..., : KZ + 4 - slab_depth]
        last_axis = main_part.ndim - 1
        padded_line = pad_axis(main_part, last_axis, 0, 4) + pad_axis(
            tail_part, last_axis, slab_depth, 0
        )
        inner = padded_line[..., 2 : KZ + 2]
        spread_tile = (
            inner
            + pad_axis(padded_line[..., 0:2], last_axis, KZ - 2, 0)
            + pad_axis(padded_line[..., KZ + 2 : KZ + 4], last_axis, 0, KZ - 2)
        ).reshape(RHS, CX + 4, CY + 4, KZ)
        extended = with_halo(spread_tile, (("row", 1), ("col", 2)), 2)
        cycle_only = clear_inside(extended, ((1, CX), (2, CY)))
        folded = fold_cycle(fold_cycle(cycle_only, 1, CX), 2, CY)
        spectrum = jnp.einsum(
            "sxyz,zk->sxyk",
            spread_tile[:, 2 : CX + 2, 2 : CY + 2] + folded,
            hartley_z,
            precision=highest,
        )
        along_y = jnp.einsum(
            "sxyz,yk->sxkz",
            lax.all_to_all(spectrum, "col", split_axis=3, concat_axis=2, tiled=True),
            hartley_y,
            precision=highest,
        )
        along_x = (
            jnp.einsum(
                "sxyz,xk->skyz",
                lax.all_to_all(along_y, "row", split_axis=2, concat_axis=1, tiled=True),
                hartley_x,
                precision=highest,
            )
            * kernel[None]
        )
        mixed_part = jnp.einsum("sxyz,xk->skyz", along_x, hartley_x, precision=highest)
        returned = lax.all_to_all(mixed_part, "row", split_axis=1, concat_axis=2, tiled=True)
        swapped = jnp.einsum("sxyz,yk->sxkz", returned, hartley_y, precision=highest)
        restored = lax.all_to_all(swapped, "col", split_axis=2, concat_axis=3, tiled=True)
        padded = with_halo(
            jnp.einsum("sxyz,zk->sxyk", restored, hartley_z, precision=highest),
            (("row", 1), ("col", 2)),
            2,
        )
        line = padded.reshape(RHS, plane_count, KZ)
        extended_line = jnp.concatenate([line[..., KZ - 2 :], line, line[..., :2]], axis=-1)
        windows = jnp.stack(
            [
                extended_line[..., tile * slab_depth : tile * slab_depth + window_len]
                for tile in range(tile_count)
            ],
            axis=-2,
        )
        sampled = jnp.einsum("sptw,twb->sptb", windows, depth_table, precision=highest)
        with_flat = sampled[..., :TILE].reshape(RHS, plane_count, atom_count)
        with_slope = sampled[..., TILE:].reshape(RHS, plane_count, atom_count)
        recip_part = jnp.stack(
            [
                jnp.sum(with_flat * plane_dx[None], axis=1),
                jnp.sum(with_flat * plane_dy[None], axis=1),
                jnp.sum(with_slope * plane_flat[None], axis=1),
            ],
            axis=1,
        )
        image_field = direction / polar_wide - direct + recip_part - self_coef * direction
        step_size = (progress / inner_sum(direction, image_field))[:, None, None]
        solution = solution + step_size * direction
        residual = residual - step_size * image_field
        scaled_res = polar_wide * residual
        progress_next = inner_sum(residual, scaled_res)
        direction = scaled_res + (progress_next / progress)[:, None, None] * direction
        progress = progress_next
    return (solution[None, None], residual[None, None])


X_PAD = CX + 4
Y_PAD = CY + 4
SLOT_ROWS = 16
SPLIT = 2
VMEM_LIMIT = 60_000_000
SMALL_VMEM_LIMIT = 24_000_000
EARLY_TILES = 1
PAIR_ROWS = 32
GROUP = 8
SCREEN_SCALE = 0.4
SCREEN_COEF = (
    0.22567588090896606,
    0.2256690263748169,
    0.20785020291805267,
    0.16849851608276367,
    0.14156343042850494,
    -0.005832736846059561,
    0.16930203139781952,
    -0.1830107867717743,
    0.05028456076979637,
)


def halves(value):
    high = value.astype(jnp.bfloat16)
    return high, (value - high.astype(jnp.float32)).astype(jnp.bfloat16)


def halves_np(value):
    value = value.astype(np.float32)
    high = value.astype(ml_dtypes.bfloat16)
    return high, (value - high.astype(np.float32)).astype(ml_dtypes.bfloat16)


def product(left, right, left_dim=1, right_dim=0):
    def one(first, second):
        return lax.dot_general(
            first,
            second,
            (((left_dim,), (right_dim,)), ((), ())),
            preferred_element_type=jnp.float32,
        )

    return one(left[0], right[0]) + (one(left[1], right[0]) + one(left[0], right[1]))


def cas_np(wave, place, length):
    angles = 2.0 * np.pi / length * (wave[:, None] * place[None, :] % length)
    return np.cos(angles) + np.sin(angles)


def modulus_np(wave, length):
    coef = np.array([1.0, 11.0, 11.0, 1.0]) / 24.0
    angles = 2.0 * np.pi / length * (wave[:, None] * np.arange(4)[None, :])
    return (coef * np.cos(angles)).sum(1) ** 2 + (coef * np.sin(angles)).sum(1) ** 2


def influence_np(length_x, length_y, length_z):
    total = np.zeros((length_x, length_y, length_z))
    modulus = np.ones((length_x, length_y, length_z))
    excluded = np.zeros((length_x, length_y, length_z), bool)
    for axis, length in enumerate((length_x, length_y, length_z)):
        wave = np.arange(length)
        shape = [1, 1, 1]
        shape[axis] = length
        total = total + ((np.minimum(wave, length - wave) / length) ** 2).reshape(shape)
        modulus = modulus * modulus_np(wave, length).reshape(shape)
        excluded = excluded | (wave * 2 == length).reshape(shape)
    excluded[0, 0, 0] = True
    safe = np.where(excluded, 1.0, total)
    result = np.exp(-(np.pi**2) / ewald_beta**2 * safe) / (
        np.pi * safe * np.where(excluded, 1.0, modulus)
    )
    return np.where(excluded, 0.0, result) / (length_x * length_y * length_z)


def slab_tables(rows_count, cols_count):
    grid_x = CX * rows_count
    grid_y = CY * cols_count
    devices = rows_count * cols_count
    chunk = KZ // devices
    wave_z = (np.arange(devices)[None, :] * chunk + np.arange(chunk)[:, None]).reshape(-1)
    along_z = cas_np(wave_z, np.arange(KZ), KZ)
    place_x = np.arange(rows_count)[:, None] * CX + np.arange(X_PAD)[None, :] - 2
    along_x = cas_np(np.arange(grid_x), place_x.reshape(-1) % grid_x, grid_x)
    x_high, x_low = halves_np(along_x)
    forward_x = np.concatenate([x_high, x_low, x_high], axis=1)
    backward_x = np.concatenate([x_high.T, x_low.T, x_high.T], axis=1)
    place_y = (np.arange(cols_count)[:, None] * CY + np.arange(Y_PAD)[None, :] - 2) % grid_y
    along_y = cas_np(np.arange(grid_y), place_y.reshape(-1), grid_y)
    along_y = along_y.reshape(grid_y, cols_count, Y_PAD)
    units = chunk * RHS // SPLIT
    block = np.einsum("uv,kcy->cuyvk", np.eye(units), along_y)
    block = block.reshape(cols_count * units * Y_PAD, units * grid_y)
    kernel = influence_np(grid_x, grid_y, KZ).reshape(grid_x, grid_y, devices, chunk)
    kernel = np.transpose(kernel, (2, 0, 3, 1))[:, :, :, None, :]
    kernel = np.broadcast_to(kernel, (devices, grid_x, chunk, RHS, grid_y))
    kernel = kernel.reshape(devices, grid_x, SPLIT, units * grid_y)
    kernel = np.moveaxis(kernel, 2, 1).reshape(devices, SPLIT * grid_x, units * grid_y)
    kernel = kernel.astype(np.float32)
    return dict(
        along_z=halves_np(along_z),
        forward_x=forward_x,
        backward_x=backward_x,
        block=halves_np(block),
        kernel=kernel,
    )


def pack_body(rhs_ref, place_ref, polar_ref, start_ref, payload_ref):
    polar = polar_ref[...]
    start = read_rows(rhs_ref) * polar
    start_ref[...] = start
    place = [place_ref[dim] for dim in range(3)]
    everything = jnp.concatenate(place + [1.0 / jnp.sqrt(polar), start], axis=0)
    store_payload(payload_ref, everything)


def read_rows(rows_ref):
    return jnp.concatenate([rows_ref[dim] for dim in range(3)], axis=0)


def store_payload(payload_ref, everything):
    tile_count = everything.shape[1] // TILE
    for quantity in range(everything.shape[0]):
        for tile in range(tile_count):
            row = quantity * tile_count + tile
            payload_ref[row : row + 1, :] = everything[
                quantity : quantity + 1, tile * TILE : (tile + 1) * TILE
            ]


def placed_rows(slot, weights, extent):
    slot_index = lax.broadcasted_iota(jnp.int32, (extent, slot.shape[1]), 0)
    placed = jnp.zeros((extent, slot.shape[1]), jnp.float32)
    for stencil in range(5):
        target = slot + stencil
        if extent == KZ:
            target = jnp.where(target >= KZ, target - KZ, target)
        placed = placed + jnp.where(slot_index == target, weights[stencil], 0.0)
    return placed


def spread_into(message_ref, moment, rows_x, slope_x, rows_y, slope_y, depth, devices):
    blocks = []
    for step in range(X_PAD):
        flat_x = rows_x[step : step + 1]
        tilt_x = slope_x[step : step + 1]
        for rhs in range(RHS):
            part_x = tilt_x * moment[rhs : rhs + 1]
            part_y = flat_x * moment[RHS + rhs : RHS + rhs + 1]
            part_z = flat_x * moment[2 * RHS + rhs : 2 * RHS + rhs + 1]
            blocks.append(
                jnp.concatenate([part_x * rows_y + part_y * slope_y, part_z * rows_y], axis=1)
            )
    charges = jnp.concatenate(blocks, axis=0)
    spectrum = product(depth, halves(charges), 1, 1)
    slot_rows = message_ref.shape[0] // devices
    chunk = KZ // devices
    width = RHS * Y_PAD
    for step in range(X_PAD):
        message_ref[pl.ds(step, devices, stride=slot_rows), :] = jnp.concatenate(
            [
                spectrum[unit * devices : (unit + 1) * devices, step * width : (step + 1) * width]
                for unit in range(chunk)
            ],
            axis=1,
        )


def sample_from(message_ref, rows_x, slope_x, rows_y, slope_y, depth, devices):
    chunk = KZ // devices
    width = RHS * Y_PAD
    slot_rows = message_ref.shape[0] // devices
    pieces = [
        message_ref[pl.ds(step, devices, stride=slot_rows), :] for step in range(X_PAD)
    ]
    spare = jnp.zeros((devices, KZ - X_PAD * width), jnp.float32)
    spectrum = jnp.concatenate(
        [
            jnp.concatenate(
                [piece[:, unit * width : (unit + 1) * width] for piece in pieces] + [spare], axis=1
            )
            for unit in range(chunk)
        ],
        axis=0,
    )
    spectrum = jnp.transpose(spectrum)[: X_PAD * width]
    sampled = product(halves(spectrum), depth, 1, 0)
    atoms = rows_x.shape[1]
    fields = [None] * (3 * RHS)
    for rhs in range(RHS):
        sum_x = sum_y = sum_z = None
        for step in range(X_PAD):
            first = step * width + rhs * Y_PAD
            flat = sampled[first : first + Y_PAD, :atoms]
            tilt = sampled[first : first + Y_PAD, atoms:]
            part_x = slope_x[step : step + 1] * flat
            part_y = rows_x[step : step + 1] * flat
            part_z = rows_x[step : step + 1] * tilt
            sum_x = part_x if sum_x is None else sum_x + part_x
            sum_y = part_y if sum_y is None else sum_y + part_y
            sum_z = part_z if sum_z is None else sum_z + part_z
        fields[rhs] = jnp.sum(sum_x * rows_y, axis=0, keepdims=True)
        fields[RHS + rhs] = jnp.sum(sum_y * slope_y, axis=0, keepdims=True)
        fields[2 * RHS + rhs] = jnp.sum(sum_z * rows_y, axis=0, keepdims=True)
    return jnp.concatenate(fields, axis=0)


def read_tables(tables_ref):
    return (
        tables_ref[0:X_PAD],
        tables_ref[SLOT_ROWS : SLOT_ROWS + X_PAD],
        tables_ref[2 * SLOT_ROWS : 2 * SLOT_ROWS + Y_PAD],
        tables_ref[2 * SLOT_ROWS + Y_PAD : 2 * SLOT_ROWS + 2 * Y_PAD],
    )


def setup_body(
    lengths,
    devices,
    place_ref,
    base_ref,
    start_ref,
    z_high_ref,
    z_low_ref,
    message_ref,
    tables_ref,
    depth_high_ref,
    depth_low_ref,
):
    base = [base_ref[dim] for dim in range(3)]
    fractions = []
    cells = []
    for dim in range(3):
        cell = base[dim] + 2
        cell = jnp.where(cell >= lengths[dim], cell - lengths[dim], cell)
        cells.append(cell)
        fractions.append(place_ref[dim] - cell.astype(jnp.float32))
    values, slopes = spline_table(jnp.concatenate(fractions, axis=0))
    values = [[values[stencil][dim : dim + 1] for stencil in range(5)] for dim in range(3)]
    slopes = [[slopes[stencil][dim : dim + 1] for stencil in range(5)] for dim in range(3)]
    slot_x = lax.rem(cells[0], CX)
    slot_y = lax.rem(cells[1], CY)
    tables_ref[0:SLOT_ROWS] = placed_rows(slot_x, values[0], SLOT_ROWS)
    tables_ref[SLOT_ROWS : 2 * SLOT_ROWS] = placed_rows(slot_x, slopes[0], SLOT_ROWS)
    tables_ref[2 * SLOT_ROWS : 2 * SLOT_ROWS + Y_PAD] = placed_rows(slot_y, values[1], Y_PAD)
    tables_ref[2 * SLOT_ROWS + Y_PAD : 2 * SLOT_ROWS + 2 * Y_PAD] = placed_rows(
        slot_y, slopes[1], Y_PAD
    )
    window = jnp.concatenate(
        [
            placed_rows(base[2], values[2], KZ),
            placed_rows(base[2], slopes[2], KZ),
        ],
        axis=1,
    )
    depth = product((z_high_ref[...], z_low_ref[...]), halves(window), 1, 0)
    depth = halves(depth)
    depth_high_ref[...] = depth[0]
    depth_low_ref[...] = depth[1]
    spread_into(message_ref, start_ref[...], *read_tables(tables_ref), depth, devices)


def transform_in(message_ref, forward_ref, block_high_ref, block_low_ref, rows_count, cols_count):
    gathered = jnp.concatenate(
        [
            jnp.concatenate(
                [
                    message_ref[(r * cols_count + c) * X_PAD : (r * cols_count + c + 1) * X_PAD]
                    for r in range(rows_count)
                ],
                axis=0,
            )
            for c in range(cols_count)
        ],
        axis=1,
    )
    high, low = halves(gathered)
    along = jnp.dot(
        forward_ref[...],
        jnp.concatenate([high, high, low], axis=0),
        preferred_element_type=jnp.float32,
    )
    part = along.shape[1] // cols_count // SPLIT
    along = jnp.concatenate(
        [
            jnp.concatenate(
                [
                    along[:, (c * SPLIT + half) * part : (c * SPLIT + half + 1) * part]
                    for c in range(cols_count)
                ],
                axis=1,
            )
            for half in range(SPLIT)
        ],
        axis=0,
    )
    return product(halves(along), (block_high_ref[...], block_low_ref[...]))


def transform_out(result_ref, values, backward_ref, block_high_ref, block_low_ref, counts):
    rows_count, cols_count = counts
    spread = product(halves(values), (block_high_ref[...], block_low_ref[...]), 1, 1)
    grid_x = spread.shape[0] // SPLIT
    part = spread.shape[1] // cols_count
    spread = jnp.concatenate(
        [
            spread[half * grid_x : (half + 1) * grid_x, c * part : (c + 1) * part]
            for c in range(cols_count)
            for half in range(SPLIT)
        ],
        axis=1,
    )
    high, low = halves(spread)
    along = jnp.dot(
        backward_ref[...],
        jnp.concatenate([high, high, low], axis=0),
        preferred_element_type=jnp.float32,
    )
    width = along.shape[1] // cols_count
    slot_rows = result_ref.shape[0] // (rows_count * cols_count)
    for r in range(rows_count):
        for c in range(cols_count):
            first = (r * cols_count + c) * slot_rows
            result_ref[first : first + X_PAD, :] = along[
                r * X_PAD : (r + 1) * X_PAD, c * width : (c + 1) * width
            ]


def middle_first_body(
    counts,
    message_ref,
    kernel_ref,
    forward_ref,
    backward_ref,
    block_high_ref,
    block_low_ref,
    result_ref,
    wave_ref,
):
    wave = transform_in(message_ref, forward_ref, block_high_ref, block_low_ref, *counts)
    wave_ref[...] = wave
    transform_out(
        result_ref, wave * kernel_ref[...], backward_ref, block_high_ref, block_low_ref, counts
    )


def gather_rows(parts):
    tiles = [
        parts[GROUP * tile : GROUP * tile + GROUP, :] for tile in range(parts.shape[0] // GROUP)
    ]
    return jnp.concatenate(tiles, axis=1)[0 : 3 * RHS]


def row_total(value, rhs):
    row = lax.broadcasted_iota(jnp.int32, value.shape, 0)
    return total(jnp.where(lax.rem(row, RHS) == rhs, value, 0.0))


def total(value):
    return jnp.sum(jnp.sum(value, axis=0, keepdims=True), axis=1, keepdims=True)


def middle_second_body(
    counts,
    message_ref,
    kernel_ref,
    forward_ref,
    backward_ref,
    block_high_ref,
    block_low_ref,
    wave_ref,
    rhs_ref,
    start_ref,
    image_ref,
    second_ref,
    near_ref,
    polar_ref,
    result_ref,
):
    rhs_rows = read_rows(rhs_ref)
    near_rows = gather_rows(near_ref)
    wave = transform_in(message_ref, forward_ref, block_high_ref, block_low_ref, *counts)
    filtered = wave * kernel_ref[...]
    transform_out(result_ref, filtered, backward_ref, block_high_ref, block_low_ref, counts)
    before = wave_ref[...]
    grid_y = CY * counts[1]
    lane = lax.broadcasted_iota(jnp.int32, wave.shape, 1)
    own_rhs = lax.rem(lax.div(lane, grid_y), RHS)
    second = second_ref[...]
    start = start_ref[...]
    image = image_ref[...]
    local_part = second / polar_ref[...] - near_rows - self_coef * second
    slot = lax.broadcasted_iota(jnp.int32, (1, result_ref.shape[1]), 1)
    sums = jnp.zeros((1, result_ref.shape[1]), jnp.float32)
    for rhs in range(RHS):
        mine = own_rhs == rhs
        parts = (
            row_total(rhs_rows * start, rhs),
            row_total(start * image, rhs),
            row_total(second * image, rhs),
            row_total(start * local_part, rhs) + total(jnp.where(mine, before * filtered, 0.0)),
            row_total(second * local_part, rhs) + total(jnp.where(mine, wave * filtered, 0.0)),
        )
        for index, part in enumerate(parts):
            sums = jnp.where(slot == rhs * len(parts) + index, part, sums)
    devices = counts[0] * counts[1]
    result_ref[pl.ds(X_PAD, devices, stride=X_PAD + 1), :] = jnp.broadcast_to(
        sums, (devices, sums.shape[1])
    )


def sample_body(
    devices,
    message_ref,
    tables_ref,
    depth_high_ref,
    depth_low_ref,
    start_ref,
    near_ref,
    polar_ref,
    image_ref,
    second_ref,
    payload_ref,
):
    tables = read_tables(tables_ref)
    depth = (depth_high_ref[...], depth_low_ref[...])
    field = sample_from(message_ref, *tables, depth, devices)
    start = start_ref[...]
    polar = polar_ref[...]
    image = start / polar - gather_rows(near_ref) + field - self_coef * start
    second = polar * image
    image_ref[...] = image
    second_ref[...] = second
    store_payload(payload_ref, second)


def spread_body(
    devices,
    tables_ref,
    depth_high_ref,
    depth_low_ref,
    second_ref,
    result_ref,
):
    depth = (depth_high_ref[...], depth_low_ref[...])
    spread_into(result_ref, second_ref[...], *read_tables(tables_ref), depth, devices)


def final_body(
    devices,
    message_ref,
    tables_ref,
    depth_high_ref,
    depth_low_ref,
    rhs_ref,
    start_ref,
    image_ref,
    second_ref,
    near_ref,
    polar_ref,
    dipole_ref,
    residual_ref,
):
    tables = read_tables(tables_ref)
    depth = (depth_high_ref[...], depth_low_ref[...])
    field = sample_from(message_ref, *tables, depth, devices)
    second = second_ref[...]
    start = start_ref[...]
    image = image_ref[...]
    image_second = second / polar_ref[...] - gather_rows(near_ref) + field - self_coef * second
    sums = jnp.sum(
        message_ref[pl.ds(X_PAD, devices, stride=X_PAD + 1), :], axis=0, keepdims=True
    )
    steps = []
    for rhs in range(RHS):
        progress, start_image, second_image, start_next, second_next = [
            sums[:, rhs * 5 + index : rhs * 5 + index + 1] for index in range(5)
        ]
        step = progress / start_image
        progress_next = progress - 2.0 * step * start_image + step * step * second_image
        grown = 1.0 + progress_next / progress
        curvature = (
            grown * grown * start_image
            - step * grown * (start_next + second_image)
            + step * step * second_next
        )
        steps.append((step, grown, progress_next / curvature))
    row = lax.broadcasted_iota(jnp.int32, (RHS, 1), 0)
    step, grown, step_next = [
        sum(jnp.where(row == rhs, steps[rhs][index], 0.0) for rhs in range(RHS))
        for index in range(3)
    ]
    for dim in range(3):
        rows = slice(dim * RHS, (dim + 1) * RHS)
        direction = grown * start[rows] - step * second[rows]
        image_direction = grown * image[rows] - step * image_second[rows]
        dipole_ref[dim] = step * start[rows] + step_next * direction
        residual_ref[dim] = rhs_ref[dim] - step * image[rows] - step_next * image_direction


def near_base(entry, brick_rows):
    return lax.shift_right_logical(entry, 2) * brick_rows + lax.bitwise_and(entry, 3)


def nearest(places, origin, span):
    return places - span * jnp.floor((places - origin) * (1.0 / span) + 0.5)


def unwrap_near(near, tile_count, spans):
    rows = near.shape[0] // 9
    for dim in range(2):
        own = 4 * rows + dim * tile_count
        origin = near[own : own + 1, 0:1]
        for brick in range(9):
            first = brick * rows + dim * tile_count
            near[first : first + tile_count, :] = nearest(
                near[first : first + tile_count, :], origin, spans[dim]
            )


def pick_rows(picked, near, lists_ref, tile, place, tile_count, quantities, origin, span):
    rows = near.shape[0] // 9
    place = place * lists_ref.shape[1] * quantities * GROUP
    for entry in range(lists_ref.shape[1]):
        base = near_base(lists_ref[tile, entry], rows)
        for quantity in range(quantities):
            values = near[pl.ds(base + quantity * tile_count, 1), :]
            if quantity == 2 and span is not None:
                values = nearest(values, origin, span)
            first = place + (entry * quantities + quantity) * GROUP
            picked[first : first + GROUP, :] = jnp.broadcast_to(values, (GROUP, TILE))


def widen_own(near, quantities, tile_count, tile, place, wide):
    offset = near.shape[0] // 9 * 4
    rows = [
        near[offset + quantity * tile_count + tile : offset + quantity * tile_count + tile + 1, :]
        for quantity in range(quantities)
    ]
    spare = jnp.zeros((TILE - quantities, TILE), jnp.float32)
    columns = jnp.transpose(jnp.concatenate(rows + [spare], axis=0))
    for quantity in range(quantities):
        first = (place * quantities + quantity) * TILE
        wide[first : first + TILE, :] = jnp.broadcast_to(
            columns[:, quantity : quantity + 1], (TILE, TILE)
        )


def add_field(sums, first_term, second_term, apart, moments):
    for rhs in range(RHS):
        moment = [moments[RHS * dim + rhs] for dim in range(3)]
        projected = moment[0] * apart[0] + moment[1] * apart[1] + moment[2] * apart[2]
        weighted = second_term * projected
        for dim in range(3):
            index = RHS * dim + rhs
            sums[index] = sums[index] + (weighted * apart[dim] - first_term * moment[dim])


def finish_sums(field_ref, sums_ref, first_tile, place):
    place = place * 3 * RHS
    lane = lax.broadcasted_iota(jnp.int32, (TILE, TILE), 1)
    merged = jnp.zeros((TILE, TILE), jnp.float32)
    for index in range(3 * RHS):
        first = (place + index) * TILE
        column = jnp.sum(sums_ref[first : first + TILE, :], axis=1, keepdims=True)
        merged = jnp.where(lane == index, column, merged)
    first = (first_tile + place // (3 * RHS)) * GROUP
    field_ref[first : first + GROUP, :] = jnp.transpose(merged)[0:GROUP]


def pair_rows(start, group):
    return pl.ds(pl.multiple_of(start + group * GROUP, GROUP), GROUP)


def wide_rows(start, group, quantity):
    return pl.ds(pl.multiple_of(quantity * TILE + start + group * GROUP, GROUP), GROUP)


def pair_terms(square_dist, damp):
    inverse = lax.rsqrt(square_dist)
    distance = square_dist * inverse
    inverse_sq = inverse * inverse
    inverse_cube = inverse_sq * inverse
    cubed = damp * (distance * square_dist)
    damping = jnp.exp(cubed)
    bell = jnp.exp(-(ewald_beta * ewald_beta) * square_dist)
    stretched = 1.0 + (SCREEN_SCALE * ewald_beta) * distance
    turned = pl.reciprocal(stretched, approx=True)
    turned = turned * (2.0 - stretched * turned)
    series = SCREEN_COEF[-1] * turned + SCREEN_COEF[-2]
    for coef in SCREEN_COEF[-3::-1]:
        series = series * turned + coef
    screen = bell * turned * series
    gaussian = (2.0 * ewald_beta / math.sqrt(math.pi)) * bell
    bare = screen - damping
    first_term = bare * inverse_cube + gaussian * inverse_sq
    second_term = (
        3.0 * (first_term + (cubed * damping) * inverse_cube)
        + (2.0 * ewald_beta * ewald_beta) * gaussian
    ) * inverse_sq
    return first_term, second_term


def tile_rows(step, rows):
    return pl.ds(pl.multiple_of(step * rows, GROUP), rows)


def start_all(copies):
    for copy in copies:
        copy.start()


def wait_all(copies):
    for copy in copies:
        copy.wait()


def near_copies(sources, near, semaphore):
    rows = sources[0].shape[0]
    return [
        pltpu.make_async_copy(
            source, near.at[index * rows : (index + 1) * rows, :], semaphore.at[index]
        )
        for index, source in enumerate(sources)
    ]


def term_copies(terms, buffers, semaphore, step, slot, inward):
    size = buffers[0].shape[1]
    rows = pl.ds(pl.multiple_of(step * size, GROUP), size)
    copies = []
    for index in range(2):
        far, here = terms[index].at[rows, :], buffers[index].at[slot]
        ends = (far, here) if inward else (here, far)
        copies.append(pltpu.make_async_copy(*ends, semaphore.at[index, slot]))
    return copies


def pair_first_body(
    first_tile,
    last_tile,
    tile_count,
    spans,
    lists_ref,
    up_ref,
    stack_ref,
    down_ref,
    *others,
):
    first_ref, second_ref, field_ref, near_ref = others[-13:-9]
    near, picked, wide, sums_ref, kept, field, first_buffer, second_buffer, semaphore = others[-9:]
    terms = (first_ref, second_ref)
    buffers = (first_buffer, second_buffer)
    copies = near_copies((up_ref, stack_ref, down_ref), near, semaphore.at[0])
    if first_tile > 0:
        copies.append(
            pltpu.make_async_copy(
                others[0], field.at[0 : first_tile * GROUP, :], semaphore.at[0, 3]
            )
        )
    start_all(copies)
    wait_all(copies)
    entries = lists_ref.shape[1]
    rows = near.shape[0] // 9
    quantities = rows // tile_count
    unwrap_near(near, tile_count, spans)
    for brick in range(9):
        kept[brick * 3 * tile_count : (brick + 1) * 3 * tile_count, :] = near[
            brick * rows : brick * rows + 3 * tile_count, :
        ]
    keep = pltpu.make_async_copy(kept, near_ref, semaphore.at[1, 3])
    keep.start()
    for place, tile in enumerate(range(first_tile, last_tile)):
        widen_own(near, 4, tile_count, tile, place, wide)
        own = rows * 4 + 2 * tile_count + tile
        origin = near[own : own + 1, 0:1]
        pick_rows(picked, near, lists_ref, tile, place, tile_count, quantities, origin, spans[2])
    parts = TILE // PAIR_ROWS
    steps = (last_tile - first_tile) * parts

    def sent(step, slot):
        return term_copies(terms, buffers, semaphore, first_tile * parts + step, slot, False)

    @pl.loop(0, steps)
    def _(step):
        slot = lax.rem(step, 2)

        @pl.when(step >= 2)
        def _():
            wait_all(sent(step - 2, slot))

        tile = lax.div(step, parts)
        start = lax.rem(step, parts) * PAIR_ROWS
        step_picked = picked.at[tile_rows(tile, entries * quantities * GROUP), :]
        step_wide = wide.at[tile_rows(tile, 4 * TILE), :]
        step_sums = sums_ref.at[tile_rows(tile, 3 * RHS * TILE), :]
        for group in range(PAIR_ROWS // GROUP):
            own = [step_wide[wide_rows(start, group, dim), :] for dim in range(4)]
            own_damp = -thole_a * own[3]
            sums = [jnp.zeros((GROUP, TILE), jnp.float32) for _ in range(3 * RHS)]
            itself = (
                lax.broadcasted_iota(jnp.int32, (GROUP, TILE), 0) + (start + group * GROUP)
            ) == lax.broadcasted_iota(jnp.int32, (GROUP, TILE), 1)
            for entry in range(entries):
                first = entry * quantities * GROUP
                rows = [
                    step_picked[first + quantity * GROUP : first + (quantity + 1) * GROUP, :]
                    for quantity in range(quantities)
                ]
                apart = [rows[dim] - own[dim] for dim in range(3)]
                square_dist = apart[0] * apart[0] + apart[1] * apart[1] + apart[2] * apart[2]
                if entry == 0:
                    square_dist = jnp.where(itself, 1.0, square_dist)
                first_term, second_term = pair_terms(square_dist, own_damp * rows[3])
                if entry == 0:
                    first_term = jnp.where(itself, 0.0, first_term)
                    second_term = jnp.where(itself, 0.0, second_term)
                place = entry * PAIR_ROWS + group * GROUP
                first_buffer[slot, place : place + GROUP, :] = first_term
                second_buffer[slot, place : place + GROUP, :] = second_term
                add_field(sums, first_term, second_term, apart, rows[4:])
            for index, value in enumerate(sums):
                step_sums[wide_rows(start, group, index), :] = value
        start_all(sent(step, slot))

    for place in range(last_tile - first_tile):
        finish_sums(field, sums_ref, first_tile, place)
    result = pltpu.make_async_copy(field, field_ref, semaphore.at[1, 2])
    result.start()
    wait_all(sent(steps - 2, (steps - 2) % 2))
    wait_all(sent(steps - 1, (steps - 1) % 2))
    keep.wait()
    result.wait()


def pair_second_body(
    tile_count,
    spans,
    lists_ref,
    near_ref,
    up_ref,
    stack_ref,
    down_ref,
    first_ref,
    second_ref,
    field_ref,
    near,
    near_moment,
    picked,
    picked_moment,
    wide,
    sums_ref,
    field,
    first_buffer,
    second_buffer,
    semaphore,
):
    terms = (first_ref, second_ref)
    buffers = (first_buffer, second_buffer)
    parts = TILE // PAIR_ROWS
    steps = tile_count * parts

    def fetched(step, slot):
        return term_copies(terms, buffers, semaphore, step, slot, True)

    places = pltpu.make_async_copy(near_ref, near, semaphore.at[1, 3])
    places.start()
    copies = near_copies((up_ref, stack_ref, down_ref), near_moment, semaphore.at[2])
    start_all(copies)
    start_all(fetched(0, 0))
    entries = lists_ref.shape[1]
    places.wait()
    for tile in range(tile_count):
        widen_own(near, 3, tile_count, tile, tile, wide)
        own = near.shape[0] // 9 * 4 + 2 * tile_count + tile
        origin = near[own : own + 1, 0:1]
        pick_rows(picked, near, lists_ref, tile, tile, tile_count, 3, origin, spans[2])
    wait_all(copies)
    for tile in range(tile_count):
        pick_rows(
            picked_moment, near_moment, lists_ref, tile, tile, tile_count, 3 * RHS, None, None
        )

    @pl.loop(0, steps)
    def _(step):
        slot = lax.rem(step, 2)

        @pl.when(step + 1 < steps)
        def _():
            start_all(fetched(step + 1, 1 - slot))

        wait_all(fetched(step, slot))
        tile = lax.div(step, parts)
        start = lax.rem(step, parts) * PAIR_ROWS
        step_picked = picked.at[tile_rows(tile, entries * 3 * GROUP), :]
        step_moment = picked_moment.at[tile_rows(tile, entries * 3 * RHS * GROUP), :]
        step_wide = wide.at[tile_rows(tile, 3 * TILE), :]
        step_sums = sums_ref.at[tile_rows(tile, 3 * RHS * TILE), :]
        for group in range(PAIR_ROWS // GROUP):
            own = [step_wide[wide_rows(start, group, dim), :] for dim in range(3)]
            sums = [jnp.zeros((GROUP, TILE), jnp.float32) for _ in range(3 * RHS)]
            for entry in range(entries):
                first = entry * 3 * GROUP
                apart = [
                    step_picked[first + dim * GROUP : first + (dim + 1) * GROUP, :] - own[dim]
                    for dim in range(3)
                ]
                first = first * RHS
                moments = [
                    step_moment[first + index * GROUP : first + (index + 1) * GROUP, :]
                    for index in range(3 * RHS)
                ]
                place = entry * PAIR_ROWS + group * GROUP
                add_field(
                    sums,
                    first_buffer[slot, place : place + GROUP, :],
                    second_buffer[slot, place : place + GROUP, :],
                    apart,
                    moments,
                )
            for index, value in enumerate(sums):
                step_sums[wide_rows(start, group, index), :] = value

    for place in range(tile_count):
        finish_sums(field, sums_ref, 0, place)
    result = pltpu.make_async_copy(field, field_ref, semaphore.at[1, 2])
    result.start()
    result.wait()


def shift(source, axis, step):
    count = lax.axis_size(axis)
    return lax.ppermute(source, axis, [(i, (i + step) % count) for i in range(count)])


def both_ways(source, axis):
    return shift(source, axis, 1), source, shift(source, axis, -1)


def whole(shape):
    return pl.BlockSpec(shape, lambda *_: (0,) * len(shape))


def anywhere():
    return pl.BlockSpec(memory_space=pl.ANY)


def join(message, payload):
    left, _, right = both_ways(payload, "col")
    message, left, right = lax.optimization_barrier((message, left, right))
    return message, both_ways(jnp.concatenate([left, payload, right], axis=0), "row")


class Fetched:
    def __init__(self, source, scratch, semaphore):
        self.copy = pltpu.make_async_copy(source, scratch, semaphore)
        self.copy.start()
        self.scratch = scratch
        self.shape = scratch.shape
        self.waiting = True

    def wait(self):
        if self.waiting:
            self.copy.wait()
            self.waiting = False

    def __getitem__(self, index):
        self.wait()
        return self.scratch[index]


def call(body, outs, *operands, after=(), own_block=None):
    fetched = [
        pltpu.VMEM(operand.shape[1:] if index == own_block else operand.shape, operand.dtype)
        for index, operand in enumerate(operands)
    ]
    count = len(operands)

    def run(*refs):
        refs = refs[len(after) :]
        sources, refs = refs[:count], refs[count:]
        results, refs = refs[: len(outs)], refs[len(outs) :]
        targets, written, semaphore = refs[:count], refs[count:-1], refs[-1]
        inputs = []
        for index, source in enumerate(sources):
            if index == own_block:
                place = lax.axis_index("row") * lax.axis_size("col") + lax.axis_index("col")
                source = source.at[place]
            inputs.append(Fetched(source, targets[index], semaphore.at[index]))
        body(*inputs, *written)
        for operand in inputs:
            operand.wait()
        copies = [
            pltpu.make_async_copy(value, result, semaphore.at[count + index])
            for index, (value, result) in enumerate(zip(written, results))
        ]
        for copy in copies:
            copy.start()
        for copy in copies:
            copy.wait()

    return pl.pallas_call(
        run,
        in_specs=[anywhere()] * (len(after) + count),
        out_specs=[anywhere()] * len(outs),
        out_shape=[jax.ShapeDtypeStruct(shape, dtype) for shape, dtype in outs],
        scratch_shapes=fetched
        + [pltpu.VMEM(shape, dtype) for shape, dtype in outs]
        + [pltpu.SemaphoreType.DMA((count + len(outs),))],
        compiler_params=pltpu.CompilerParams(vmem_limit_bytes=VMEM_LIMIT),
        cost_estimate=pl.CostEstimate(
            flops=200_000_000, bytes_accessed=4 << 20, transcendentals=0
        ),
    )(*after, *operands)


def final_call(body, outs, *operands):
    return pl.pallas_call(
        body,
        grid=(1,),
        in_specs=[whole(operand.shape) for operand in operands],
        out_specs=[whole(shape) for shape, _ in outs],
        out_shape=[jax.ShapeDtypeStruct(shape, dtype) for shape, dtype in outs],
        compiler_params=pltpu.CompilerParams(vmem_limit_bytes=SMALL_VMEM_LIMIT),
    )(*operands)


def pair_call(body, outs, scratch, lists, *operands, aliased=0):
    buffers = (2, lists.shape[1] * PAIR_ROWS, TILE)
    first = 1 + len(operands) - aliased
    return pl.pallas_call(
        body,
        in_specs=[pl.BlockSpec(memory_space=pltpu.SMEM)] + [anywhere()] * len(operands),
        out_specs=[anywhere()] * len(outs),
        out_shape=[jax.ShapeDtypeStruct(shape, jnp.float32) for shape in outs],
        scratch_shapes=[pltpu.VMEM(shape, jnp.float32) for shape in scratch + [buffers] * 2]
        + [pltpu.SemaphoreType.DMA((3, 4))],
        input_output_aliases={first + index: index for index in range(aliased)},
        compiler_params=pltpu.CompilerParams(vmem_limit_bytes=VMEM_LIMIT),
        cost_estimate=pl.CostEstimate(
            flops=80_000_000, bytes_accessed=8 << 20, transcendentals=1 << 21
        ),
    )(lists, *operands)


def exchange(message, devices):
    shape = message.shape
    sent = message.reshape(devices, 1, -1)
    return lax.all_to_all(sent, ("row", "col"), split_axis=0, concat_axis=0, tiled=True).reshape(
        shape
    )


def slab_local(field_rhs, positions, polar, grid_base, tile_lists):
    rows_count = lax.axis_size("row")
    cols_count = lax.axis_size("col")
    counts = (rows_count, cols_count)
    devices = rows_count * cols_count
    lengths = (CX * rows_count, CY * cols_count, KZ)
    spans = tuple(float(length) for length in lengths)
    atoms = polar.shape[-1]
    tile_count = atoms // TILE
    listed = tile_lists.shape[-1]
    tables = slab_tables(rows_count, cols_count)
    f32 = jnp.float32
    rhs = jnp.swapaxes(field_rhs[0, 0], 0, 1)
    place = jnp.swapaxes(positions[0], 0, 1)
    base = jnp.swapaxes(grid_base[0], 0, 1)
    polar = polar.reshape(1, atoms)
    lists = tile_lists[0, 0]
    quantities = 4 + 3 * RHS
    brick_rows = quantities * tile_count
    moment_rows = 3 * RHS * tile_count
    message_shape = (devices * X_PAD, KZ // devices * RHS * Y_PAD)
    last_shape = (devices * (X_PAD + 1), message_shape[1])
    row_shape = (3 * RHS, atoms)

    start, payload = call(pack_body, [(row_shape, f32), ((brick_rows, TILE), f32)], rhs, place, polar)

    def setup(*refs):
        setup_body(lengths, devices, *refs)

    message, splines, depth_high, depth_low = call(
        setup,
        [
            (message_shape, f32),
            ((2 * SLOT_ROWS + 2 * Y_PAD, atoms), f32),
            ((KZ, 2 * atoms), jnp.bfloat16),
            ((KZ, 2 * atoms), jnp.bfloat16),
        ],
        place,
        base,
        start,
        *[jnp.asarray(table) for table in tables["along_z"]],
    )
    constants = (
        jnp.asarray(tables["kernel"]),
        jnp.asarray(tables["forward_x"]),
        jnp.asarray(tables["backward_x"]),
        *[jnp.asarray(table) for table in tables["block"]],
    )
    message, near = join(message, payload)
    arrived = exchange(message, devices)

    def pair_first(first_tile, last_tile, fields, *after):
        def body(*refs):
            pair_first_body(first_tile, last_tile, tile_count, spans, *refs)

        tiles = last_tile - first_tile
        return pair_call(
            body,
            [(tile_count * listed * TILE, TILE)] * 2
            + [(last_tile * GROUP, TILE), (9 * 3 * tile_count, TILE)],
            [
                (9 * brick_rows, TILE),
                (tiles * listed * quantities * GROUP, TILE),
                (tiles * 4 * TILE, TILE),
                (tiles * 3 * RHS * TILE, TILE),
                (9 * 3 * tile_count, TILE),
                (last_tile * GROUP, TILE),
            ],
            lists,
            *near,
            *fields,
            *after,
            aliased=2 if first_tile > 0 else 0,
        )

    early = pair_first(0, EARLY_TILES, (), message)

    def middle_first(*refs):
        middle_first_body(counts, *refs)

    mixed, wave = call(
        middle_first,
        [(message_shape, f32), (tables["kernel"].shape[1:], f32)],
        arrived,
        *constants,
        after=(early[2],),
        own_block=1,
    )
    returned = exchange(mixed, devices)
    first_term, second_term, direct, near = pair_first(
        EARLY_TILES, tile_count, (early[2],), wave, *early[:2]
    )

    def sample(*refs):
        sample_body(devices, *refs)

    image, second, moments = call(
        sample,
        [(row_shape, f32), (row_shape, f32), ((moment_rows, TILE), f32)],
        returned,
        splines,
        depth_high,
        depth_low,
        start,
        direct,
        polar,
    )

    def spread(*refs):
        spread_body(devices, *refs)

    (message,) = call(spread, [(message_shape, f32)], splines, depth_high, depth_low, second)
    message, near_moments = join(message, moments)
    arrived = exchange(message, devices)

    def pair_second(*refs):
        pair_second_body(tile_count, spans, *refs)

    (direct,) = pair_call(
        pair_second,
        [(tile_count * GROUP, TILE)],
        [
            (9 * 3 * tile_count, TILE),
            (9 * moment_rows, TILE),
            (tile_count * listed * 3 * GROUP, TILE),
            (tile_count * listed * 3 * RHS * GROUP, TILE),
            (tile_count * 3 * TILE, TILE),
            (tile_count * 3 * RHS * TILE, TILE),
            (tile_count * GROUP, TILE),
        ],
        lists,
        near,
        *near_moments,
        first_term,
        second_term,
    )

    def middle_second(*refs):
        middle_second_body(counts, *refs)

    (mixed,) = call(
        middle_second,
        [(last_shape, f32)],
        arrived,
        *constants,
        wave,
        rhs,
        start,
        image,
        second,
        direct,
        polar,
        own_block=1,
    )
    returned = exchange(mixed, devices)

    def final(*refs):
        final_body(devices, *refs)

    outs = final_call(
        final,
        [(rhs.shape, f32), (rhs.shape, f32)],
        returned,
        splines,
        depth_high,
        depth_low,
        rhs,
        start,
        image,
        second,
        direct,
        polar,
    )
    return tuple(jnp.swapaxes(out, 0, 1)[None, None] for out in outs)


def solution(mesh):
    placed = (
        P("row", "col", None, None, None),
        P("row", "col", None, None),
        P("row", "col", None),
        P("row", "col", None, None),
        P("row", "col", None, None),
    )
    devices = mesh.shape["row"] * mesh.shape["col"]
    return jax.shard_map(
        slab_local if KZ % devices == 0 else pencil_local,
        mesh=mesh,
        in_specs=placed,
        out_specs=(P("row", "col", None, None, None), P("row", "col", None, None, None)),
        check_vma=False,
    )
```

```python
import math

import jax
import jax.numpy as jnp
import ml_dtypes
import numpy as np
from jax import lax
from jax.experimental import pallas as pl
from jax.experimental.pallas import tpu as pltpu
from jax.sharding import PartitionSpec as P

CX = 8
CY = 4
KZ = 256
TILE = 128
RHS = 2
ITERS = 2


ewald_beta = 0.4
thole_a = 0.39
self_coef = 4.0 * ewald_beta**3 / (3.0 * math.sqrt(math.pi))
highest = lax.Precision.HIGHEST


def with_halo(cells, sides, width):
    for axis, dim in sides:
        count = lax.axis_size(axis)
        head = lax.slice_in_dim(cells, 0, width, axis=dim)
        tail = lax.slice_in_dim(cells, cells.shape[dim] - width, cells.shape[dim], axis=dim)
        cells = jnp.concatenate(
            [
                lax.ppermute(tail, axis, [(i, (i + 1) % count) for i in range(count)]),
                cells,
                lax.ppermute(head, axis, [((i + 1) % count, i) for i in range(count)]),
            ],
            axis=dim,
        )
    return cells


def spline_table(fraction):
    previous = {0: jnp.ones_like(fraction)}
    fourth = previous
    for degree in range(2, 6):
        current = {}
        for offset in range(degree):
            abscissa = fraction + offset
            summed = abscissa * previous.get(offset, 0.0) + (degree - abscissa) * previous.get(
                offset - 1, 0.0
            )
            current[offset] = summed / (degree - 1)
        if degree == 4:
            fourth = current
        previous = current
    values = jnp.stack([previous[4 - stencil] for stencil in range(5)])
    slopes = jnp.stack(
        [fourth.get(4 - stencil, 0.0) - fourth.get(3 - stencil, 0.0) for stencil in range(5)]
    )
    return (values, slopes)


def spline_modulus(wave_index, length):
    spline_coef = (1.0 / 24.0, 11.0 / 24.0, 11.0 / 24.0, 1.0 / 24.0)
    cosine_sum = jnp.zeros(wave_index.shape, jnp.float32)
    sine_sum = jnp.zeros(wave_index.shape, jnp.float32)
    for offset in range(4):
        angles = 2.0 * math.pi / length * (wave_index * offset % length).astype(jnp.float32)
        cosine_sum = cosine_sum + spline_coef[offset] * jnp.cos(angles)
        sine_sum = sine_sum + spline_coef[offset] * jnp.sin(angles)
    return cosine_sum * cosine_sum + sine_sum * sine_sum


def folded_square(wave_index, length):
    nearest = jnp.minimum(wave_index, length - wave_index).astype(jnp.float32) / length
    return nearest * nearest


def influence(wave_x, wave_y, wave_z, length_x, length_y, length_z):
    wave_norm = (
        folded_square(wave_x, length_x)
        + folded_square(wave_y, length_y)
        + folded_square(wave_z, length_z)
    )
    modulus = (
        spline_modulus(wave_x, length_x)
        * spline_modulus(wave_y, length_y)
        * spline_modulus(wave_z, length_z)
    )
    excluded = (wave_x * 2 == length_x) | (wave_y * 2 == length_y) | (wave_z * 2 == length_z)
    excluded = excluded | (wave_x == 0) & (wave_y == 0) & (wave_z == 0)
    safe_norm = jnp.where(excluded, 1.0, wave_norm)
    safe_modulus = jnp.where(excluded, 1.0, modulus)
    result = jnp.exp(-(math.pi**2 / ewald_beta**2) * safe_norm) / (
        math.pi * safe_norm * safe_modulus
    )
    return jnp.where(excluded, 0.0, result)


def tile_field(own_static, near_static, near_dipole, box_spans):
    listed_count = near_static.shape[0]
    tile_width = own_static.shape[1]
    box_span = jnp.array(box_spans, dtype=jnp.float32)[None, :, None, None]
    separation = near_static[:, 0:3, None, :] - own_static[None, 0:3, :, None]
    separation = separation - box_span * jnp.floor(separation / box_span + 0.5)
    dist_sq = jnp.sum(separation * separation, axis=1)
    itself = (jnp.arange(listed_count)[:, None, None] == 0) & (
        jnp.arange(tile_width)[:, None] == jnp.arange(tile_width)[None, :]
    )[None]
    safe_sq = jnp.where(itself, 1.0, dist_sq)
    distance = jnp.sqrt(safe_sq)
    scaled = distance / (own_static[3][None, :, None] * near_static[:, 3][:, None, :])
    cubed = thole_a * scaled * scaled * scaled
    damping = jnp.exp(-cubed)
    screen = lax.erfc(ewald_beta * distance)
    gaussian = 2.0 * ewald_beta / math.sqrt(math.pi) * jnp.exp(-(ewald_beta * ewald_beta) * safe_sq)
    inverse_sq = 1.0 / safe_sq
    inverse_cube = inverse_sq / distance
    first_term = (screen - damping) * inverse_cube + gaussian * inverse_sq
    second = (
        3.0 * (screen - (1.0 + cubed) * damping) * inverse_cube * inverse_sq
        + gaussian * (2.0 * ewald_beta * ewald_beta + 3.0 * inverse_sq) * inverse_sq
    )
    first_term = jnp.where(itself, 0.0, first_term)
    second = jnp.where(itself, 0.0, second)
    projected = jnp.sum(near_dipole[:, :, :, None, :] * separation[:, None, :, :, :], axis=2)
    weighted = second[:, None] * projected
    outward = jnp.sum(weighted[:, :, None] * separation[:, None], axis=(0, 4))
    inward = jnp.sum(first_term[:, None, None] * near_dipole[:, :, :, None, :], axis=(0, 4))
    return outward - inward


def hartley(length):
    counter = jnp.arange(length, dtype=jnp.int32)
    angles = (
        2.0 * math.pi / length * (counter[:, None] * counter[None, :] % length).astype(jnp.float32)
    )
    return jnp.cos(angles) + jnp.sin(angles)


def placed_table(first_cell, weights, extent):
    slot_index = jnp.arange(extent, dtype=jnp.int32)[:, None]
    placed = jnp.zeros((extent, first_cell.shape[0]), jnp.float32)
    for stencil in range(5):
        placed = placed + jnp.where(
            slot_index == (first_cell[None, :] + stencil) % extent, weights[stencil][None, :], 0.0
        )
    return placed


def pad_axis(source, axis_pos, leading, trailing):
    widths = [(0, 0)] * source.ndim
    widths[axis_pos] = (leading, trailing)
    return jnp.pad(source, widths)


def fold_cycle(cycle_only, axis_pos, inner_len):
    middle = lax.slice_in_dim(cycle_only, 4, inner_len + 4, axis=axis_pos)
    lower_cycle = lax.slice_in_dim(cycle_only, 0, 2, axis=axis_pos)
    upper_cycle = lax.slice_in_dim(cycle_only, inner_len + 6, inner_len + 8, axis=axis_pos)
    return (
        middle
        + pad_axis(lower_cycle, axis_pos, 0, inner_len - 2)
        + pad_axis(upper_cycle, axis_pos, inner_len - 2, 0)
    )


def clear_inside(extended, extents):
    inside = None
    for axis_pos, inner_len in extents:
        slot_index = lax.broadcasted_iota(jnp.int32, extended.shape, axis_pos)
        within = (slot_index >= 2) & (slot_index < inner_len + 6)
        inside = within if inside is None else inside & within
    return jnp.where(inside, 0.0, extended)


def inner_sum(left_arr, right_arr):
    return lax.psum(jnp.sum(left_arr * right_arr, axis=(1, 2)), ("row", "col"))


def pencil_local(field_rhs, positions, polar, grid_base, tile_lists):
    rows_count = lax.axis_size("row")
    cols_count = lax.axis_size("col")
    grid_x = CX * rows_count
    grid_y = CY * cols_count
    atom_count = polar.shape[-1]
    tile_count = atom_count // TILE
    slab_depth = KZ // tile_count
    window_len = slab_depth + 4
    box_spans = (float(grid_x), float(grid_y), float(KZ))
    own_place = positions[0, 0]
    own_base = grid_base[0, 0]
    own_polar = polar[0, 0]
    lengths = jnp.array([grid_x, grid_y, KZ], dtype=jnp.int32)[:, None]
    cell_index = (own_base + 2) % lengths
    fraction = own_place - cell_index.astype(jnp.float32)
    values, slopes = spline_table(fraction)
    first_x = (own_base[0] - lax.axis_index("row") * CX + 2) % grid_x
    first_y = (own_base[1] - lax.axis_index("col") * CY + 2) % grid_y
    rows_x = placed_table(first_x, values[:, 0], CX + 4)
    slope_x = placed_table(first_x, slopes[:, 0], CX + 4)
    rows_y = placed_table(first_y, values[:, 1], CY + 4)
    slope_y = placed_table(first_y, slopes[:, 1], CY + 4)
    tile_start = jnp.arange(atom_count, dtype=jnp.int32) // TILE * slab_depth
    first_z = (own_base[2] + 2 - tile_start) % KZ
    rows_z = placed_table(first_z, values[:, 2], window_len)
    slope_z = placed_table(first_z, slopes[:, 2], window_len)
    plane_count = (CX + 4) * (CY + 4)
    plane_dx = (slope_x[:, None, :] * rows_y[None, :, :]).reshape(plane_count, atom_count)
    plane_dy = (rows_x[:, None, :] * slope_y[None, :, :]).reshape(plane_count, atom_count)
    plane_flat = (rows_x[:, None, :] * rows_y[None, :, :]).reshape(plane_count, atom_count)
    window_rows = jnp.moveaxis(rows_z.reshape(window_len, tile_count, TILE), 1, 0)
    window_slope = jnp.moveaxis(slope_z.reshape(window_len, tile_count, TILE), 1, 0)
    depth_table = jnp.concatenate([window_rows, window_slope], axis=2)
    grid_scale = 1.0 / (grid_x * grid_y * KZ)
    hartley_x = hartley(grid_x)
    hartley_y = hartley(grid_y)
    hartley_z = hartley(KZ)
    block_y = grid_y // rows_count
    block_z = KZ // cols_count
    wave_x = jnp.arange(grid_x, dtype=jnp.int32)[:, None, None]
    wave_y = (lax.axis_index("row") * block_y + jnp.arange(block_y, dtype=jnp.int32))[None, :, None]
    wave_z = (lax.axis_index("col") * block_z + jnp.arange(block_z, dtype=jnp.int32))[None, None, :]
    kernel = influence(wave_x, wave_y, wave_z, grid_x, grid_y, KZ) * grid_scale
    root_scale = jnp.power(own_polar, 1.0 / 6.0)
    own_static = jnp.concatenate([own_place, root_scale[None]], axis=0)
    near_static = with_halo(own_static[None, None], (("row", 0), ("col", 1)), 1)
    near_static = jnp.moveaxis(near_static.reshape(9, 4, tile_count, TILE), 2, 1).reshape(
        9 * tile_count, 4, TILE
    )
    own_tiles = jnp.moveaxis(own_static.reshape(4, tile_count, TILE), 1, 0)
    own_lists = tile_lists[0, 0]
    polar_wide = own_polar[None, None, :]
    solution = jnp.zeros_like(field_rhs[0, 0])
    residual = field_rhs[0, 0]
    scaled_res = polar_wide * residual
    direction = scaled_res
    progress = inner_sum(residual, scaled_res)
    for iteration in range(ITERS):
        near_dip = with_halo(direction[None, None], (("row", 0), ("col", 1)), 1)
        near_dip = jnp.moveaxis(near_dip.reshape(9, RHS, 3, tile_count, TILE), 3, 1).reshape(
            9 * tile_count, RHS, 3, TILE
        )

        def one_tile(tile_pos):
            picked = own_lists[tile_pos]
            return tile_field(own_tiles[tile_pos], near_static[picked], near_dip[picked], box_spans)

        fields = lax.map(one_tile, jnp.arange(tile_count, dtype=jnp.int32))
        direct = jnp.moveaxis(fields, 0, 2).reshape(RHS, 3, atom_count)
        slope_terms = (
            direction[:, 0, None, :] * plane_dx[None] + direction[:, 1, None, :] * plane_dy[None]
        )
        flat_terms = direction[:, 2, None, :] * plane_flat[None]
        spread_left = jnp.concatenate(
            [
                slope_terms.reshape(RHS, plane_count, tile_count, TILE),
                flat_terms.reshape(RHS, plane_count, tile_count, TILE),
            ],
            axis=3,
        )
        spread_windows = jnp.einsum("sptb,twb->sptw", spread_left, depth_table, precision=highest)
        main_part = spread_windows[..., :slab_depth].reshape(spread_windows.shape[:-2] + (KZ,))
        tail_part = pad_axis(
            spread_windows[..., slab_depth:], spread_windows.ndim - 1, 0, slab_depth - 4
        )
        tail_part = tail_part.reshape(spread_windows.shape[:-2] + (KZ,))[..., : KZ + 4 - slab_depth]
        last_axis = main_part.ndim - 1
        padded_line = pad_axis(main_part, last_axis, 0, 4) + pad_axis(
            tail_part, last_axis, slab_depth, 0
        )
        inner = padded_line[..., 2 : KZ + 2]
        spread_tile = (
            inner
            + pad_axis(padded_line[..., 0:2], last_axis, KZ - 2, 0)
            + pad_axis(padded_line[..., KZ + 2 : KZ + 4], last_axis, 0, KZ - 2)
        ).reshape(RHS, CX + 4, CY + 4, KZ)
        extended = with_halo(spread_tile, (("row", 1), ("col", 2)), 2)
        cycle_only = clear_inside(extended, ((1, CX), (2, CY)))
        folded = fold_cycle(fold_cycle(cycle_only, 1, CX), 2, CY)
        spectrum = jnp.einsum(
            "sxyz,zk->sxyk",
            spread_tile[:, 2 : CX + 2, 2 : CY + 2] + folded,
            hartley_z,
            precision=highest,
        )
        along_y = jnp.einsum(
            "sxyz,yk->sxkz",
            lax.all_to_all(spectrum, "col", split_axis=3, concat_axis=2, tiled=True),
            hartley_y,
            precision=highest,
        )
        along_x = (
            jnp.einsum(
                "sxyz,xk->skyz",
                lax.all_to_all(along_y, "row", split_axis=2, concat_axis=1, tiled=True),
                hartley_x,
                precision=highest,
            )
            * kernel[None]
        )
        mixed_part = jnp.einsum("sxyz,xk->skyz", along_x, hartley_x, precision=highest)
        returned = lax.all_to_all(mixed_part, "row", split_axis=1, concat_axis=2, tiled=True)
        swapped = jnp.einsum("sxyz,yk->sxkz", returned, hartley_y, precision=highest)
        restored = lax.all_to_all(swapped, "col", split_axis=2, concat_axis=3, tiled=True)
        padded = with_halo(
            jnp.einsum("sxyz,zk->sxyk", restored, hartley_z, precision=highest),
            (("row", 1), ("col", 2)),
            2,
        )
        line = padded.reshape(RHS, plane_count, KZ)
        extended_line = jnp.concatenate([line[..., KZ - 2 :], line, line[..., :2]], axis=-1)
        windows = jnp.stack(
            [
                extended_line[..., tile * slab_depth : tile * slab_depth + window_len]
                for tile in range(tile_count)
            ],
            axis=-2,
        )
        sampled = jnp.einsum("sptw,twb->sptb", windows, depth_table, precision=highest)
        with_flat = sampled[..., :TILE].reshape(RHS, plane_count, atom_count)
        with_slope = sampled[..., TILE:].reshape(RHS, plane_count, atom_count)
        recip_part = jnp.stack(
            [
                jnp.sum(with_flat * plane_dx[None], axis=1),
                jnp.sum(with_flat * plane_dy[None], axis=1),
                jnp.sum(with_slope * plane_flat[None], axis=1),
            ],
            axis=1,
        )
        image_field = direction / polar_wide - direct + recip_part - self_coef * direction
        step_size = (progress / inner_sum(direction, image_field))[:, None, None]
        solution = solution + step_size * direction
        residual = residual - step_size * image_field
        scaled_res = polar_wide * residual
        progress_next = inner_sum(residual, scaled_res)
        direction = scaled_res + (progress_next / progress)[:, None, None] * direction
        progress = progress_next
    return (solution[None, None], residual[None, None])


X_PAD = CX + 4
Y_PAD = CY + 4
SLOT_ROWS = 16
SPLIT = 2
VMEM_LIMIT = 60_000_000
SMALL_VMEM_LIMIT = 24_000_000
EARLY_TILES = 1
PAIR_ROWS = 32
GROUP = 8
SCREEN_SCALE = 0.4
SCREEN_COEF = (
    0.22567588090896606,
    0.2256690263748169,
    0.20785020291805267,
    0.16849851608276367,
    0.14156343042850494,
    -0.005832736846059561,
    0.16930203139781952,
    -0.1830107867717743,
    0.05028456076979637,
)


def halves(value):
    high = value.astype(jnp.bfloat16)
    return high, (value - high.astype(jnp.float32)).astype(jnp.bfloat16)


def halves_np(value):
    value = value.astype(np.float32)
    high = value.astype(ml_dtypes.bfloat16)
    return high, (value - high.astype(np.float32)).astype(ml_dtypes.bfloat16)


def product(left, right, left_dim=1, right_dim=0):
    def one(first, second):
        return lax.dot_general(
            first,
            second,
            (((left_dim,), (right_dim,)), ((), ())),
            preferred_element_type=jnp.float32,
        )

    return one(left[0], right[0]) + (one(left[1], right[0]) + one(left[0], right[1]))


def cas_np(wave, place, length):
    angles = 2.0 * np.pi / length * (wave[:, None] * place[None, :] % length)
    return np.cos(angles) + np.sin(angles)


def modulus_np(wave, length):
    coef = np.array([1.0, 11.0, 11.0, 1.0]) / 24.0
    angles = 2.0 * np.pi / length * (wave[:, None] * np.arange(4)[None, :])
    return (coef * np.cos(angles)).sum(1) ** 2 + (coef * np.sin(angles)).sum(1) ** 2


def influence_np(length_x, length_y, length_z):
    total = np.zeros((length_x, length_y, length_z))
    modulus = np.ones((length_x, length_y, length_z))
    excluded = np.zeros((length_x, length_y, length_z), bool)
    for axis, length in enumerate((length_x, length_y, length_z)):
        wave = np.arange(length)
        shape = [1, 1, 1]
        shape[axis] = length
        total = total + ((np.minimum(wave, length - wave) / length) ** 2).reshape(shape)
        modulus = modulus * modulus_np(wave, length).reshape(shape)
        excluded = excluded | (wave * 2 == length).reshape(shape)
    excluded[0, 0, 0] = True
    safe = np.where(excluded, 1.0, total)
    result = np.exp(-(np.pi**2) / ewald_beta**2 * safe) / (
        np.pi * safe * np.where(excluded, 1.0, modulus)
    )
    return np.where(excluded, 0.0, result) / (length_x * length_y * length_z)


def slab_tables(rows_count, cols_count):
    grid_x = CX * rows_count
    grid_y = CY * cols_count
    devices = rows_count * cols_count
    chunk = KZ // devices
    wave_z = (np.arange(devices)[None, :] * chunk + np.arange(chunk)[:, None]).reshape(-1)
    along_z = cas_np(wave_z, np.arange(KZ), KZ)
    place_x = np.arange(rows_count)[:, None] * CX + np.arange(X_PAD)[None, :] - 2
    along_x = cas_np(np.arange(grid_x), place_x.reshape(-1) % grid_x, grid_x)
    x_high, x_low = halves_np(along_x)
    forward_x = np.concatenate([x_high, x_low, x_high], axis=1)
    backward_x = np.concatenate([x_high.T, x_low.T, x_high.T], axis=1)
    place_y = (np.arange(cols_count)[:, None] * CY + np.arange(Y_PAD)[None, :] - 2) % grid_y
    along_y = cas_np(np.arange(grid_y), place_y.reshape(-1), grid_y)
    along_y = along_y.reshape(grid_y, cols_count, Y_PAD)
    units = chunk * RHS // SPLIT
    block = np.einsum("uv,kcy->cuyvk", np.eye(units), along_y)
    block = block.reshape(cols_count * units * Y_PAD, units * grid_y)
    kernel = influence_np(grid_x, grid_y, KZ).reshape(grid_x, grid_y, devices, chunk)
    kernel = np.transpose(kernel, (2, 0, 3, 1))[:, :, :, None, :]
    kernel = np.broadcast_to(kernel, (devices, grid_x, chunk, RHS, grid_y))
    kernel = kernel.reshape(devices, grid_x, SPLIT, units * grid_y)
    kernel = np.moveaxis(kernel, 2, 1).reshape(devices, SPLIT * grid_x, units * grid_y)
    kernel = kernel.astype(np.float32)
    return dict(
        along_z=halves_np(along_z),
        forward_x=forward_x,
        backward_x=backward_x,
        block=halves_np(block),
        kernel=kernel,
    )


def pack_body(rhs_ref, place_ref, polar_ref, start_ref, payload_ref):
    polar = polar_ref[...]
    start = read_rows(rhs_ref) * polar
    start_ref[...] = start
    place = [place_ref[dim] for dim in range(3)]
    everything = jnp.concatenate(place + [1.0 / jnp.sqrt(polar), start], axis=0)
    store_payload(payload_ref, everything)


def read_rows(rows_ref):
    return jnp.concatenate([rows_ref[dim] for dim in range(3)], axis=0)


def store_payload(payload_ref, everything):
    tile_count = everything.shape[1] // TILE
    for quantity in range(everything.shape[0]):
        for tile in range(tile_count):
            row = quantity * tile_count + tile
            payload_ref[row : row + 1, :] = everything[
                quantity : quantity + 1, tile * TILE : (tile + 1) * TILE
            ]


def placed_rows(slot, weights, extent):
    slot_index = lax.broadcasted_iota(jnp.int32, (extent, slot.shape[1]), 0)
    placed = jnp.zeros((extent, slot.shape[1]), jnp.float32)
    for stencil in range(5):
        target = slot + stencil
        if extent == KZ:
            target = jnp.where(target >= KZ, target - KZ, target)
        placed = placed + jnp.where(slot_index == target, weights[stencil], 0.0)
    return placed


def spread_into(message_ref, moment, rows_x, slope_x, rows_y, slope_y, depth, devices):
    blocks = []
    for step in range(X_PAD):
        flat_x = rows_x[step : step + 1]
        tilt_x = slope_x[step : step + 1]
        for rhs in range(RHS):
            part_x = tilt_x * moment[rhs : rhs + 1]
            part_y = flat_x * moment[RHS + rhs : RHS + rhs + 1]
            part_z = flat_x * moment[2 * RHS + rhs : 2 * RHS + rhs + 1]
            blocks.append(
                jnp.concatenate([part_x * rows_y + part_y * slope_y, part_z * rows_y], axis=1)
            )
    charges = jnp.concatenate(blocks, axis=0)
    spectrum = product(depth, halves(charges), 1, 1)
    slot_rows = message_ref.shape[0] // devices
    chunk = KZ // devices
    width = RHS * Y_PAD
    for step in range(X_PAD):
        message_ref[pl.ds(step, devices, stride=slot_rows), :] = jnp.concatenate(
            [
                spectrum[unit * devices : (unit + 1) * devices, step * width : (step + 1) * width]
                for unit in range(chunk)
            ],
            axis=1,
        )


def sample_from(message_ref, rows_x, slope_x, rows_y, slope_y, depth, devices):
    chunk = KZ // devices
    width = RHS * Y_PAD
    slot_rows = message_ref.shape[0] // devices
    pieces = [
        message_ref[pl.ds(step, devices, stride=slot_rows), :] for step in range(X_PAD)
    ]
    spare = jnp.zeros((devices, KZ - X_PAD * width), jnp.float32)
    spectrum = jnp.concatenate(
        [
            jnp.concatenate(
                [piece[:, unit * width : (unit + 1) * width] for piece in pieces] + [spare], axis=1
            )
            for unit in range(chunk)
        ],
        axis=0,
    )
    spectrum = jnp.transpose(spectrum)[: X_PAD * width]
    sampled = product(halves(spectrum), depth, 1, 0)
    atoms = rows_x.shape[1]
    fields = [None] * (3 * RHS)
    for rhs in range(RHS):
        sum_x = sum_y = sum_z = None
        for step in range(X_PAD):
            first = step * width + rhs * Y_PAD
            flat = sampled[first : first + Y_PAD, :atoms]
            tilt = sampled[first : first + Y_PAD, atoms:]
            part_x = slope_x[step : step + 1] * flat
            part_y = rows_x[step : step + 1] * flat
            part_z = rows_x[step : step + 1] * tilt
            sum_x = part_x if sum_x is None else sum_x + part_x
            sum_y = part_y if sum_y is None else sum_y + part_y
            sum_z = part_z if sum_z is None else sum_z + part_z
        fields[rhs] = jnp.sum(sum_x * rows_y, axis=0, keepdims=True)
        fields[RHS + rhs] = jnp.sum(sum_y * slope_y, axis=0, keepdims=True)
        fields[2 * RHS + rhs] = jnp.sum(sum_z * rows_y, axis=0, keepdims=True)
    return jnp.concatenate(fields, axis=0)


def read_tables(tables_ref):
    return (
        tables_ref[0:X_PAD],
        tables_ref[SLOT_ROWS : SLOT_ROWS + X_PAD],
        tables_ref[2 * SLOT_ROWS : 2 * SLOT_ROWS + Y_PAD],
        tables_ref[2 * SLOT_ROWS + Y_PAD : 2 * SLOT_ROWS + 2 * Y_PAD],
    )


def setup_body(
    lengths,
    devices,
    place_ref,
    base_ref,
    start_ref,
    z_high_ref,
    z_low_ref,
    message_ref,
    tables_ref,
    depth_high_ref,
    depth_low_ref,
):
    base = [base_ref[dim] for dim in range(3)]
    fractions = []
    cells = []
    for dim in range(3):
        cell = base[dim] + 2
        cell = jnp.where(cell >= lengths[dim], cell - lengths[dim], cell)
        cells.append(cell)
        fractions.append(place_ref[dim] - cell.astype(jnp.float32))
    values, slopes = spline_table(jnp.concatenate(fractions, axis=0))
    values = [[values[stencil][dim : dim + 1] for stencil in range(5)] for dim in range(3)]
    slopes = [[slopes[stencil][dim : dim + 1] for stencil in range(5)] for dim in range(3)]
    slot_x = lax.rem(cells[0], CX)
    slot_y = lax.rem(cells[1], CY)
    tables_ref[0:SLOT_ROWS] = placed_rows(slot_x, values[0], SLOT_ROWS)
    tables_ref[SLOT_ROWS : 2 * SLOT_ROWS] = placed_rows(slot_x, slopes[0], SLOT_ROWS)
    tables_ref[2 * SLOT_ROWS : 2 * SLOT_ROWS + Y_PAD] = placed_rows(slot_y, values[1], Y_PAD)
    tables_ref[2 * SLOT_ROWS + Y_PAD : 2 * SLOT_ROWS + 2 * Y_PAD] = placed_rows(
        slot_y, slopes[1], Y_PAD
    )
    window = jnp.concatenate(
        [
            placed_rows(base[2], values[2], KZ),
            placed_rows(base[2], slopes[2], KZ),
        ],
        axis=1,
    )
    depth = product((z_high_ref[...], z_low_ref[...]), halves(window), 1, 0)
    depth = halves(depth)
    depth_high_ref[...] = depth[0]
    depth_low_ref[...] = depth[1]
    spread_into(message_ref, start_ref[...], *read_tables(tables_ref), depth, devices)


def transform_in(message_ref, forward_ref, block_high_ref, block_low_ref, rows_count, cols_count):
    gathered = jnp.concatenate(
        [
            jnp.concatenate(
                [
                    message_ref[(r * cols_count + c) * X_PAD : (r * cols_count + c + 1) * X_PAD]
                    for r in range(rows_count)
                ],
                axis=0,
            )
            for c in range(cols_count)
        ],
        axis=1,
    )
    high, low = halves(gathered)
    along = jnp.dot(
        forward_ref[...],
        jnp.concatenate([high, high, low], axis=0),
        preferred_element_type=jnp.float32,
    )
    part = along.shape[1] // cols_count // SPLIT
    along = jnp.concatenate(
        [
            jnp.concatenate(
                [
                    along[:, (c * SPLIT + half) * part : (c * SPLIT + half + 1) * part]
                    for c in range(cols_count)
                ],
                axis=1,
            )
            for half in range(SPLIT)
        ],
        axis=0,
    )
    return product(halves(along), (block_high_ref[...], block_low_ref[...]))


def transform_out(result_ref, values, backward_ref, block_high_ref, block_low_ref, counts):
    rows_count, cols_count = counts
    spread = product(halves(values), (block_high_ref[...], block_low_ref[...]), 1, 1)
    grid_x = spread.shape[0] // SPLIT
    part = spread.shape[1] // cols_count
    spread = jnp.concatenate(
        [
            spread[half * grid_x : (half + 1) * grid_x, c * part : (c + 1) * part]
            for c in range(cols_count)
            for half in range(SPLIT)
        ],
        axis=1,
    )
    high, low = halves(spread)
    along = jnp.dot(
        backward_ref[...],
        jnp.concatenate([high, high, low], axis=0),
        preferred_element_type=jnp.float32,
    )
    width = along.shape[1] // cols_count
    slot_rows = result_ref.shape[0] // (rows_count * cols_count)
    for r in range(rows_count):
        for c in range(cols_count):
            first = (r * cols_count + c) * slot_rows
            result_ref[first : first + X_PAD, :] = along[
                r * X_PAD : (r + 1) * X_PAD, c * width : (c + 1) * width
            ]


def middle_first_body(
    counts,
    message_ref,
    kernel_ref,
    forward_ref,
    backward_ref,
    block_high_ref,
    block_low_ref,
    result_ref,
    wave_ref,
):
    wave = transform_in(message_ref, forward_ref, block_high_ref, block_low_ref, *counts)
    wave_ref[...] = wave
    transform_out(
        result_ref, wave * kernel_ref[...], backward_ref, block_high_ref, block_low_ref, counts
    )


def gather_rows(parts):
    tiles = [
        parts[GROUP * tile : GROUP * tile + GROUP, :] for tile in range(parts.shape[0] // GROUP)
    ]
    return jnp.concatenate(tiles, axis=1)[0 : 3 * RHS]


def row_total(value, rhs):
    row = lax.broadcasted_iota(jnp.int32, value.shape, 0)
    return total(jnp.where(lax.rem(row, RHS) == rhs, value, 0.0))


def total(value):
    return jnp.sum(jnp.sum(value, axis=0, keepdims=True), axis=1, keepdims=True)


def middle_second_body(
    counts,
    message_ref,
    kernel_ref,
    forward_ref,
    backward_ref,
    block_high_ref,
    block_low_ref,
    wave_ref,
    rhs_ref,
    start_ref,
    image_ref,
    second_ref,
    near_ref,
    polar_ref,
    result_ref,
):
    rhs_rows = read_rows(rhs_ref)
    near_rows = gather_rows(near_ref)
    wave = transform_in(message_ref, forward_ref, block_high_ref, block_low_ref, *counts)
    filtered = wave * kernel_ref[...]
    transform_out(result_ref, filtered, backward_ref, block_high_ref, block_low_ref, counts)
    before = wave_ref[...]
    grid_y = CY * counts[1]
    lane = lax.broadcasted_iota(jnp.int32, wave.shape, 1)
    own_rhs = lax.rem(lax.div(lane, grid_y), RHS)
    second = second_ref[...]
    start = start_ref[...]
    image = image_ref[...]
    local_part = second / polar_ref[...] - near_rows - self_coef * second
    slot = lax.broadcasted_iota(jnp.int32, (1, result_ref.shape[1]), 1)
    sums = jnp.zeros((1, result_ref.shape[1]), jnp.float32)
    for rhs in range(RHS):
        mine = own_rhs == rhs
        parts = (
            row_total(rhs_rows * start, rhs),
            row_total(start * image, rhs),
            row_total(second * image, rhs),
            row_total(start * local_part, rhs) + total(jnp.where(mine, before * filtered, 0.0)),
            row_total(second * local_part, rhs) + total(jnp.where(mine, wave * filtered, 0.0)),
        )
        for index, part in enumerate(parts):
            sums = jnp.where(slot == rhs * len(parts) + index, part, sums)
    devices = counts[0] * counts[1]
    result_ref[pl.ds(X_PAD, devices, stride=X_PAD + 1), :] = jnp.broadcast_to(
        sums, (devices, sums.shape[1])
    )


def sample_body(
    devices,
    message_ref,
    tables_ref,
    depth_high_ref,
    depth_low_ref,
    start_ref,
    near_ref,
    polar_ref,
    image_ref,
    second_ref,
    payload_ref,
):
    tables = read_tables(tables_ref)
    depth = (depth_high_ref[...], depth_low_ref[...])
    field = sample_from(message_ref, *tables, depth, devices)
    start = start_ref[...]
    polar = polar_ref[...]
    image = start / polar - gather_rows(near_ref) + field - self_coef * start
    second = polar * image
    image_ref[...] = image
    second_ref[...] = second
    store_payload(payload_ref, second)


def spread_body(
    devices,
    tables_ref,
    depth_high_ref,
    depth_low_ref,
    second_ref,
    result_ref,
):
    depth = (depth_high_ref[...], depth_low_ref[...])
    spread_into(result_ref, second_ref[...], *read_tables(tables_ref), depth, devices)


def final_body(
    devices,
    message_ref,
    tables_ref,
    depth_high_ref,
    depth_low_ref,
    rhs_ref,
    start_ref,
    image_ref,
    second_ref,
    near_ref,
    polar_ref,
    dipole_ref,
    residual_ref,
):
    tables = read_tables(tables_ref)
    depth = (depth_high_ref[...], depth_low_ref[...])
    field = sample_from(message_ref, *tables, depth, devices)
    second = second_ref[...]
    start = start_ref[...]
    image = image_ref[...]
    image_second = second / polar_ref[...] - gather_rows(near_ref) + field - self_coef * second
    sums = jnp.sum(
        message_ref[pl.ds(X_PAD, devices, stride=X_PAD + 1), :], axis=0, keepdims=True
    )
    steps = []
    for rhs in range(RHS):
        progress, start_image, second_image, start_next, second_next = [
            sums[:, rhs * 5 + index : rhs * 5 + index + 1] for index in range(5)
        ]
        step = progress / start_image
        progress_next = progress - 2.0 * step * start_image + step * step * second_image
        grown = 1.0 + progress_next / progress
        curvature = (
            grown * grown * start_image
            - step * grown * (start_next + second_image)
            + step * step * second_next
        )
        steps.append((step, grown, progress_next / curvature))
    row = lax.broadcasted_iota(jnp.int32, (RHS, 1), 0)
    step, grown, step_next = [
        sum(jnp.where(row == rhs, steps[rhs][index], 0.0) for rhs in range(RHS))
        for index in range(3)
    ]
    for dim in range(3):
        rows = slice(dim * RHS, (dim + 1) * RHS)
        direction = grown * start[rows] - step * second[rows]
        image_direction = grown * image[rows] - step * image_second[rows]
        dipole_ref[dim] = step * start[rows] + step_next * direction
        residual_ref[dim] = rhs_ref[dim] - step * image[rows] - step_next * image_direction


def near_base(entry, brick_rows):
    return lax.shift_right_logical(entry, 2) * brick_rows + lax.bitwise_and(entry, 3)


def nearest(places, origin, span):
    return places - span * jnp.floor((places - origin) * (1.0 / span) + 0.5)


def unwrap_near(near, tile_count, spans):
    rows = near.shape[0] // 9
    for dim in range(2):
        own = 4 * rows + dim * tile_count
        origin = near[own : own + 1, 0:1]
        for brick in range(9):
            first = brick * rows + dim * tile_count
            near[first : first + tile_count, :] = nearest(
                near[first : first + tile_count, :], origin, spans[dim]
            )


def pick_rows(picked, near, lists_ref, tile, place, tile_count, quantities, origin, span):
    rows = near.shape[0] // 9
    place = place * lists_ref.shape[1] * quantities * GROUP
    for entry in range(lists_ref.shape[1]):
        base = near_base(lists_ref[tile, entry], rows)
        for quantity in range(quantities):
            values = near[pl.ds(base + quantity * tile_count, 1), :]
            if quantity == 2 and span is not None:
                values = nearest(values, origin, span)
            first = place + (entry * quantities + quantity) * GROUP
            picked[first : first + GROUP, :] = jnp.broadcast_to(values, (GROUP, TILE))


def widen_own(near, quantities, tile_count, tile, place, wide):
    offset = near.shape[0] // 9 * 4
    rows = [
        near[offset + quantity * tile_count + tile : offset + quantity * tile_count + tile + 1, :]
        for quantity in range(quantities)
    ]
    spare = jnp.zeros((TILE - quantities, TILE), jnp.float32)
    columns = jnp.transpose(jnp.concatenate(rows + [spare], axis=0))
    for quantity in range(quantities):
        first = (place * quantities + quantity) * TILE
        wide[first : first + TILE, :] = jnp.broadcast_to(
            columns[:, quantity : quantity + 1], (TILE, TILE)
        )


def add_field(sums, first_term, second_term, apart, moments):
    for rhs in range(RHS):
        moment = [moments[RHS * dim + rhs] for dim in range(3)]
        projected = moment[0] * apart[0] + moment[1] * apart[1] + moment[2] * apart[2]
        weighted = second_term * projected
        for dim in range(3):
            index = RHS * dim + rhs
            sums[index] = sums[index] + (weighted * apart[dim] - first_term * moment[dim])


def finish_sums(field_ref, sums_ref, first_tile, place):
    place = place * 3 * RHS
    lane = lax.broadcasted_iota(jnp.int32, (TILE, TILE), 1)
    merged = jnp.zeros((TILE, TILE), jnp.float32)
    for index in range(3 * RHS):
        first = (place + index) * TILE
        column = jnp.sum(sums_ref[first : first + TILE, :], axis=1, keepdims=True)
        merged = jnp.where(lane == index, column, merged)
    first = (first_tile + place // (3 * RHS)) * GROUP
    field_ref[first : first + GROUP, :] = jnp.transpose(merged)[0:GROUP]


def pair_rows(start, group):
    return pl.ds(pl.multiple_of(start + group * GROUP, GROUP), GROUP)


def wide_rows(start, group, quantity):
    return pl.ds(pl.multiple_of(quantity * TILE + start + group * GROUP, GROUP), GROUP)


def pair_terms(square_dist, damp):
    inverse = lax.rsqrt(square_dist)
    distance = square_dist * inverse
    inverse_sq = inverse * inverse
    inverse_cube = inverse_sq * inverse
    cubed = damp * (distance * square_dist)
    damping = jnp.exp(cubed)
    bell = jnp.exp(-(ewald_beta * ewald_beta) * square_dist)
    stretched = 1.0 + (SCREEN_SCALE * ewald_beta) * distance
    turned = pl.reciprocal(stretched, approx=True)
    turned = turned * (2.0 - stretched * turned)
    series = SCREEN_COEF[-1] * turned + SCREEN_COEF[-2]
    for coef in SCREEN_COEF[-3::-1]:
        series = series * turned + coef
    screen = bell * turned * series
    gaussian = (2.0 * ewald_beta / math.sqrt(math.pi)) * bell
    bare = screen - damping
    first_term = bare * inverse_cube + gaussian * inverse_sq
    second_term = (
        3.0 * (first_term + (cubed * damping) * inverse_cube)
        + (2.0 * ewald_beta * ewald_beta) * gaussian
    ) * inverse_sq
    return first_term, second_term


def step_rows(step, size, offset):
    return pl.ds(pl.multiple_of(step * size + offset, GROUP), GROUP)


def tile_rows(step, rows):
    return pl.ds(pl.multiple_of(step * rows, GROUP), rows)


def start_all(copies):
    for copy in copies:
        copy.start()


def wait_all(copies):
    for copy in copies:
        copy.wait()


def near_copies(sources, near, semaphore):
    rows = sources[0].shape[0]
    return [
        pltpu.make_async_copy(
            source, near.at[index * rows : (index + 1) * rows, :], semaphore.at[index]
        )
        for index, source in enumerate(sources)
    ]


def term_copies(terms, buffers, semaphore, begin, step, size, inward):
    rows = pl.ds(pl.multiple_of((begin + step) * size, GROUP), size)
    place = pl.ds(pl.multiple_of(step * size, GROUP), size)
    copies = []
    for index in range(2):
        far, here = terms[index].at[rows, :], buffers[index].at[place, :]
        ends = (far, here) if inward else (here, far)
        copies.append(pltpu.make_async_copy(*ends, semaphore.at[index, step]))
    return copies


def pair_first_body(
    first_tile,
    last_tile,
    tile_count,
    spans,
    lists_ref,
    up_ref,
    stack_ref,
    down_ref,
    *others,
):
    first_ref, second_ref, field_ref, near_ref = others[-14:-10]
    near, picked, wide, sums_ref, kept, field, first_buffer, second_buffer, semaphore, busy = others[-10:]
    terms = (first_ref, second_ref)
    buffers = (first_buffer, second_buffer)
    copies = near_copies((up_ref, stack_ref, down_ref), near, semaphore.at[0])
    if first_tile > 0:
        copies.append(
            pltpu.make_async_copy(
                others[0], field.at[0 : first_tile * GROUP, :], semaphore.at[0, 3]
            )
        )
    start_all(copies)
    wait_all(copies)
    entries = lists_ref.shape[1]
    rows = near.shape[0] // 9
    quantities = rows // tile_count
    unwrap_near(near, tile_count, spans)
    for brick in range(9):
        kept[brick * 3 * tile_count : (brick + 1) * 3 * tile_count, :] = near[
            brick * rows : brick * rows + 3 * tile_count, :
        ]
    keep = pltpu.make_async_copy(kept, near_ref, semaphore.at[1, 3])
    keep.start()
    for place, tile in enumerate(range(first_tile, last_tile)):
        widen_own(near, 4, tile_count, tile, place, wide)
        own = rows * 4 + 2 * tile_count + tile
        origin = near[own : own + 1, 0:1]
        pick_rows(picked, near, lists_ref, tile, place, tile_count, quantities, origin, spans[2])
    parts = TILE // PAIR_ROWS
    steps = (last_tile - first_tile) * parts

    size = entries * PAIR_ROWS

    def sent(step):
        return term_copies(terms, buffers, busy, first_tile * parts, step, size, False)

    @pl.loop(0, steps)
    def _(step):
        tile = lax.div(step, parts)
        start = lax.rem(step, parts) * PAIR_ROWS
        step_picked = picked.at[tile_rows(tile, entries * quantities * GROUP), :]
        step_wide = wide.at[tile_rows(tile, 4 * TILE), :]
        step_sums = sums_ref.at[tile_rows(tile, 3 * RHS * TILE), :]
        for group in range(PAIR_ROWS // GROUP):
            own = [step_wide[wide_rows(start, group, dim), :] for dim in range(4)]
            own_damp = -thole_a * own[3]
            sums = [jnp.zeros((GROUP, TILE), jnp.float32) for _ in range(3 * RHS)]
            itself = (
                lax.broadcasted_iota(jnp.int32, (GROUP, TILE), 0) + (start + group * GROUP)
            ) == lax.broadcasted_iota(jnp.int32, (GROUP, TILE), 1)
            for entry in range(entries):
                first = entry * quantities * GROUP
                rows = [
                    step_picked[first + quantity * GROUP : first + (quantity + 1) * GROUP, :]
                    for quantity in range(quantities)
                ]
                apart = [rows[dim] - own[dim] for dim in range(3)]
                square_dist = apart[0] * apart[0] + apart[1] * apart[1] + apart[2] * apart[2]
                if entry == 0:
                    square_dist = jnp.where(itself, 1.0, square_dist)
                first_term, second_term = pair_terms(square_dist, own_damp * rows[3])
                if entry == 0:
                    first_term = jnp.where(itself, 0.0, first_term)
                    second_term = jnp.where(itself, 0.0, second_term)
                place = step_rows(step, size, entry * PAIR_ROWS + group * GROUP)
                first_buffer[place, :] = first_term
                second_buffer[place, :] = second_term
                add_field(sums, first_term, second_term, apart, rows[4:])
            for index, value in enumerate(sums):
                step_sums[wide_rows(start, group, index), :] = value
        start_all(sent(step))

    for place in range(last_tile - first_tile):
        finish_sums(field, sums_ref, first_tile, place)
    result = pltpu.make_async_copy(field, field_ref, semaphore.at[1, 2])
    result.start()

    @pl.loop(0, steps)
    def _(step):
        wait_all(sent(step))

    keep.wait()
    result.wait()


def pair_second_body(
    tile_count,
    spans,
    lists_ref,
    near_ref,
    up_ref,
    stack_ref,
    down_ref,
    first_ref,
    second_ref,
    field_ref,
    near,
    near_moment,
    picked,
    picked_moment,
    wide,
    sums_ref,
    field,
    first_buffer,
    second_buffer,
    semaphore,
    busy,
):
    terms = (first_ref, second_ref)
    buffers = (first_buffer, second_buffer)
    parts = TILE // PAIR_ROWS
    steps = tile_count * parts

    entries = lists_ref.shape[1]
    size = entries * PAIR_ROWS

    def fetched(step):
        return term_copies(terms, buffers, busy, 0, step, size, True)

    places = pltpu.make_async_copy(near_ref, near, semaphore.at[1, 3])
    places.start()
    copies = near_copies((up_ref, stack_ref, down_ref), near_moment, semaphore.at[2])
    start_all(copies)

    @pl.loop(0, steps)
    def _(step):
        start_all(fetched(step))

    places.wait()
    for tile in range(tile_count):
        widen_own(near, 3, tile_count, tile, tile, wide)
        own = near.shape[0] // 9 * 4 + 2 * tile_count + tile
        origin = near[own : own + 1, 0:1]
        pick_rows(picked, near, lists_ref, tile, tile, tile_count, 3, origin, spans[2])
    wait_all(copies)
    for tile in range(tile_count):
        pick_rows(
            picked_moment, near_moment, lists_ref, tile, tile, tile_count, 3 * RHS, None, None
        )

    @pl.loop(0, steps)
    def _(step):
        wait_all(fetched(step))
        tile = lax.div(step, parts)
        start = lax.rem(step, parts) * PAIR_ROWS
        step_picked = picked.at[tile_rows(tile, entries * 3 * GROUP), :]
        step_moment = picked_moment.at[tile_rows(tile, entries * 3 * RHS * GROUP), :]
        step_wide = wide.at[tile_rows(tile, 3 * TILE), :]
        step_sums = sums_ref.at[tile_rows(tile, 3 * RHS * TILE), :]
        for group in range(PAIR_ROWS // GROUP):
            own = [step_wide[wide_rows(start, group, dim), :] for dim in range(3)]
            sums = [jnp.zeros((GROUP, TILE), jnp.float32) for _ in range(3 * RHS)]
            for entry in range(entries):
                first = entry * 3 * GROUP
                apart = [
                    step_picked[first + dim * GROUP : first + (dim + 1) * GROUP, :] - own[dim]
                    for dim in range(3)
                ]
                first = first * RHS
                moments = [
                    step_moment[first + index * GROUP : first + (index + 1) * GROUP, :]
                    for index in range(3 * RHS)
                ]
                place = step_rows(step, size, entry * PAIR_ROWS + group * GROUP)
                add_field(sums, first_buffer[place, :], second_buffer[place, :], apart, moments)
            for index, value in enumerate(sums):
                step_sums[wide_rows(start, group, index), :] = value

    for place in range(tile_count):
        finish_sums(field, sums_ref, 0, place)
    result = pltpu.make_async_copy(field, field_ref, semaphore.at[1, 2])
    result.start()
    result.wait()


def shift(source, axis, step):
    count = lax.axis_size(axis)
    return lax.ppermute(source, axis, [(i, (i + step) % count) for i in range(count)])


def both_ways(source, axis):
    return shift(source, axis, 1), source, shift(source, axis, -1)


def whole(shape):
    return pl.BlockSpec(shape, lambda *_: (0,) * len(shape))


def anywhere():
    return pl.BlockSpec(memory_space=pl.ANY)


def join(message, payload):
    left, _, right = both_ways(payload, "col")
    message, left, right = lax.optimization_barrier((message, left, right))
    return message, both_ways(jnp.concatenate([left, payload, right], axis=0), "row")


class Fetched:
    def __init__(self, source, scratch, semaphore):
        self.copy = pltpu.make_async_copy(source, scratch, semaphore)
        self.copy.start()
        self.scratch = scratch
        self.shape = scratch.shape
        self.waiting = True

    def wait(self):
        if self.waiting:
            self.copy.wait()
            self.waiting = False

    def __getitem__(self, index):
        self.wait()
        return self.scratch[index]


def call(body, outs, *operands, after=(), own_block=None):
    fetched = [
        pltpu.VMEM(operand.shape[1:] if index == own_block else operand.shape, operand.dtype)
        for index, operand in enumerate(operands)
    ]
    count = len(operands)

    def run(*refs):
        refs = refs[len(after) :]
        sources, refs = refs[:count], refs[count:]
        results, refs = refs[: len(outs)], refs[len(outs) :]
        targets, written, semaphore = refs[:count], refs[count:-1], refs[-1]
        inputs = []
        for index, source in enumerate(sources):
            if index == own_block:
                place = lax.axis_index("row") * lax.axis_size("col") + lax.axis_index("col")
                source = source.at[place]
            inputs.append(Fetched(source, targets[index], semaphore.at[index]))
        body(*inputs, *written)
        for operand in inputs:
            operand.wait()
        copies = [
            pltpu.make_async_copy(value, result, semaphore.at[count + index])
            for index, (value, result) in enumerate(zip(written, results))
        ]
        for copy in copies:
            copy.start()
        for copy in copies:
            copy.wait()

    return pl.pallas_call(
        run,
        in_specs=[anywhere()] * (len(after) + count),
        out_specs=[anywhere()] * len(outs),
        out_shape=[jax.ShapeDtypeStruct(shape, dtype) for shape, dtype in outs],
        scratch_shapes=fetched
        + [pltpu.VMEM(shape, dtype) for shape, dtype in outs]
        + [pltpu.SemaphoreType.DMA((count + len(outs),))],
        compiler_params=pltpu.CompilerParams(vmem_limit_bytes=VMEM_LIMIT),
        cost_estimate=pl.CostEstimate(
            flops=200_000_000, bytes_accessed=4 << 20, transcendentals=0
        ),
    )(*after, *operands)


def final_call(body, outs, *operands):
    return pl.pallas_call(
        body,
        grid=(1,),
        in_specs=[whole(operand.shape) for operand in operands],
        out_specs=[whole(shape) for shape, _ in outs],
        out_shape=[jax.ShapeDtypeStruct(shape, dtype) for shape, dtype in outs],
        compiler_params=pltpu.CompilerParams(vmem_limit_bytes=SMALL_VMEM_LIMIT),
    )(*operands)


def pair_call(body, outs, scratch, lists, *operands, tiles, aliased=0):
    buffers = (tiles * lists.shape[1] * TILE, TILE)
    first = 1 + len(operands) - aliased
    return pl.pallas_call(
        body,
        in_specs=[pl.BlockSpec(memory_space=pltpu.SMEM)] + [anywhere()] * len(operands),
        out_specs=[anywhere()] * len(outs),
        out_shape=[jax.ShapeDtypeStruct(shape, jnp.float32) for shape in outs],
        scratch_shapes=[pltpu.VMEM(shape, jnp.float32) for shape in scratch + [buffers] * 2]
        + [
            pltpu.SemaphoreType.DMA((3, 4)),
            pltpu.SemaphoreType.DMA((2, tiles * TILE // PAIR_ROWS)),
        ],
        input_output_aliases={first + index: index for index in range(aliased)},
        compiler_params=pltpu.CompilerParams(vmem_limit_bytes=VMEM_LIMIT),
        cost_estimate=pl.CostEstimate(
            flops=80_000_000, bytes_accessed=8 << 20, transcendentals=1 << 21
        ),
    )(lists, *operands)


def exchange(message, devices):
    shape = message.shape
    sent = message.reshape(devices, 1, -1)
    return lax.all_to_all(sent, ("row", "col"), split_axis=0, concat_axis=0, tiled=True).reshape(
        shape
    )


def slab_local(field_rhs, positions, polar, grid_base, tile_lists):
    rows_count = lax.axis_size("row")
    cols_count = lax.axis_size("col")
    counts = (rows_count, cols_count)
    devices = rows_count * cols_count
    lengths = (CX * rows_count, CY * cols_count, KZ)
    spans = tuple(float(length) for length in lengths)
    atoms = polar.shape[-1]
    tile_count = atoms // TILE
    listed = tile_lists.shape[-1]
    tables = slab_tables(rows_count, cols_count)
    f32 = jnp.float32
    rhs = jnp.swapaxes(field_rhs[0, 0], 0, 1)
    place = jnp.swapaxes(positions[0], 0, 1)
    base = jnp.swapaxes(grid_base[0], 0, 1)
    polar = polar.reshape(1, atoms)
    lists = tile_lists[0, 0]
    quantities = 4 + 3 * RHS
    brick_rows = quantities * tile_count
    moment_rows = 3 * RHS * tile_count
    message_shape = (devices * X_PAD, KZ // devices * RHS * Y_PAD)
    last_shape = (devices * (X_PAD + 1), message_shape[1])
    row_shape = (3 * RHS, atoms)

    start, payload = call(pack_body, [(row_shape, f32), ((brick_rows, TILE), f32)], rhs, place, polar)

    def setup(*refs):
        setup_body(lengths, devices, *refs)

    message, splines, depth_high, depth_low = call(
        setup,
        [
            (message_shape, f32),
            ((2 * SLOT_ROWS + 2 * Y_PAD, atoms), f32),
            ((KZ, 2 * atoms), jnp.bfloat16),
            ((KZ, 2 * atoms), jnp.bfloat16),
        ],
        place,
        base,
        start,
        *[jnp.asarray(table) for table in tables["along_z"]],
    )
    constants = (
        jnp.asarray(tables["kernel"]),
        jnp.asarray(tables["forward_x"]),
        jnp.asarray(tables["backward_x"]),
        *[jnp.asarray(table) for table in tables["block"]],
    )
    message, near = join(message, payload)
    arrived = exchange(message, devices)

    def pair_first(first_tile, last_tile, fields, *after):
        def body(*refs):
            pair_first_body(first_tile, last_tile, tile_count, spans, *refs)

        tiles = last_tile - first_tile
        return pair_call(
            body,
            [(tile_count * listed * TILE, TILE)] * 2
            + [(last_tile * GROUP, TILE), (9 * 3 * tile_count, TILE)],
            [
                (9 * brick_rows, TILE),
                (tiles * listed * quantities * GROUP, TILE),
                (tiles * 4 * TILE, TILE),
                (tiles * 3 * RHS * TILE, TILE),
                (9 * 3 * tile_count, TILE),
                (last_tile * GROUP, TILE),
            ],
            lists,
            *near,
            *fields,
            *after,
            tiles=tiles,
            aliased=2 if first_tile > 0 else 0,
        )

    early = pair_first(0, EARLY_TILES, (), message)

    def middle_first(*refs):
        middle_first_body(counts, *refs)

    mixed, wave = call(
        middle_first,
        [(message_shape, f32), (tables["kernel"].shape[1:], f32)],
        arrived,
        *constants,
        after=(early[2],),
        own_block=1,
    )
    returned = exchange(mixed, devices)
    first_term, second_term, direct, near = pair_first(
        EARLY_TILES, tile_count, (early[2],), wave, *early[:2]
    )

    def sample(*refs):
        sample_body(devices, *refs)

    image, second, moments = call(
        sample,
        [(row_shape, f32), (row_shape, f32), ((moment_rows, TILE), f32)],
        returned,
        splines,
        depth_high,
        depth_low,
        start,
        direct,
        polar,
    )

    def spread(*refs):
        spread_body(devices, *refs)

    (message,) = call(spread, [(message_shape, f32)], splines, depth_high, depth_low, second)
    message, near_moments = join(message, moments)
    arrived = exchange(message, devices)

    def pair_second(*refs):
        pair_second_body(tile_count, spans, *refs)

    (direct,) = pair_call(
        pair_second,
        [(tile_count * GROUP, TILE)],
        [
            (9 * 3 * tile_count, TILE),
            (9 * moment_rows, TILE),
            (tile_count * listed * 3 * GROUP, TILE),
            (tile_count * listed * 3 * RHS * GROUP, TILE),
            (tile_count * 3 * TILE, TILE),
            (tile_count * 3 * RHS * TILE, TILE),
            (tile_count * GROUP, TILE),
        ],
        lists,
        near,
        *near_moments,
        first_term,
        second_term,
        tiles=tile_count,
    )

    def middle_second(*refs):
        middle_second_body(counts, *refs)

    (mixed,) = call(
        middle_second,
        [(last_shape, f32)],
        arrived,
        *constants,
        wave,
        rhs,
        start,
        image,
        second,
        direct,
        polar,
        own_block=1,
    )
    returned = exchange(mixed, devices)

    def final(*refs):
        final_body(devices, *refs)

    outs = final_call(
        final,
        [(rhs.shape, f32), (rhs.shape, f32)],
        returned,
        splines,
        depth_high,
        depth_low,
        rhs,
        start,
        image,
        second,
        direct,
        polar,
    )
    return tuple(jnp.swapaxes(out, 0, 1)[None, None] for out in outs)


def solution(mesh):
    placed = (
        P("row", "col", None, None, None),
        P("row", "col", None, None),
        P("row", "col", None),
        P("row", "col", None, None),
        P("row", "col", None, None),
    )
    devices = mesh.shape["row"] * mesh.shape["col"]
    return jax.shard_map(
        slab_local if KZ % devices == 0 else pencil_local,
        mesh=mesh,
        in_specs=placed,
        out_specs=(P("row", "col", None, None, None), P("row", "col", None, None, None)),
        check_vma=False,
    )
```

```python
import math

import jax
import jax.numpy as jnp
import ml_dtypes
import numpy as np
from jax import lax
from jax.experimental import pallas as pl
from jax.experimental.pallas import tpu as pltpu
from jax.sharding import PartitionSpec as P

CX = 8
CY = 4
KZ = 256
TILE = 128
RHS = 2
ITERS = 2


ewald_beta = 0.4
thole_a = 0.39
self_coef = 4.0 * ewald_beta**3 / (3.0 * math.sqrt(math.pi))
highest = lax.Precision.HIGHEST


def with_halo(cells, sides, width):
    for axis, dim in sides:
        count = lax.axis_size(axis)
        head = lax.slice_in_dim(cells, 0, width, axis=dim)
        tail = lax.slice_in_dim(cells, cells.shape[dim] - width, cells.shape[dim], axis=dim)
        cells = jnp.concatenate(
            [
                lax.ppermute(tail, axis, [(i, (i + 1) % count) for i in range(count)]),
                cells,
                lax.ppermute(head, axis, [((i + 1) % count, i) for i in range(count)]),
            ],
            axis=dim,
        )
    return cells


def spline_table(fraction):
    previous = {0: jnp.ones_like(fraction)}
    fourth = previous
    for degree in range(2, 6):
        current = {}
        for offset in range(degree):
            abscissa = fraction + offset
            summed = abscissa * previous.get(offset, 0.0) + (degree - abscissa) * previous.get(
                offset - 1, 0.0
            )
            current[offset] = summed / (degree - 1)
        if degree == 4:
            fourth = current
        previous = current
    values = jnp.stack([previous[4 - stencil] for stencil in range(5)])
    slopes = jnp.stack(
        [fourth.get(4 - stencil, 0.0) - fourth.get(3 - stencil, 0.0) for stencil in range(5)]
    )
    return (values, slopes)


def spline_modulus(wave_index, length):
    spline_coef = (1.0 / 24.0, 11.0 / 24.0, 11.0 / 24.0, 1.0 / 24.0)
    cosine_sum = jnp.zeros(wave_index.shape, jnp.float32)
    sine_sum = jnp.zeros(wave_index.shape, jnp.float32)
    for offset in range(4):
        angles = 2.0 * math.pi / length * (wave_index * offset % length).astype(jnp.float32)
        cosine_sum = cosine_sum + spline_coef[offset] * jnp.cos(angles)
        sine_sum = sine_sum + spline_coef[offset] * jnp.sin(angles)
    return cosine_sum * cosine_sum + sine_sum * sine_sum


def folded_square(wave_index, length):
    nearest = jnp.minimum(wave_index, length - wave_index).astype(jnp.float32) / length
    return nearest * nearest


def influence(wave_x, wave_y, wave_z, length_x, length_y, length_z):
    wave_norm = (
        folded_square(wave_x, length_x)
        + folded_square(wave_y, length_y)
        + folded_square(wave_z, length_z)
    )
    modulus = (
        spline_modulus(wave_x, length_x)
        * spline_modulus(wave_y, length_y)
        * spline_modulus(wave_z, length_z)
    )
    excluded = (wave_x * 2 == length_x) | (wave_y * 2 == length_y) | (wave_z * 2 == length_z)
    excluded = excluded | (wave_x == 0) & (wave_y == 0) & (wave_z == 0)
    safe_norm = jnp.where(excluded, 1.0, wave_norm)
    safe_modulus = jnp.where(excluded, 1.0, modulus)
    result = jnp.exp(-(math.pi**2 / ewald_beta**2) * safe_norm) / (
        math.pi * safe_norm * safe_modulus
    )
    return jnp.where(excluded, 0.0, result)


def tile_field(own_static, near_static, near_dipole, box_spans):
    listed_count = near_static.shape[0]
    tile_width = own_static.shape[1]
    box_span = jnp.array(box_spans, dtype=jnp.float32)[None, :, None, None]
    separation = near_static[:, 0:3, None, :] - own_static[None, 0:3, :, None]
    separation = separation - box_span * jnp.floor(separation / box_span + 0.5)
    dist_sq = jnp.sum(separation * separation, axis=1)
    itself = (jnp.arange(listed_count)[:, None, None] == 0) & (
        jnp.arange(tile_width)[:, None] == jnp.arange(tile_width)[None, :]
    )[None]
    safe_sq = jnp.where(itself, 1.0, dist_sq)
    distance = jnp.sqrt(safe_sq)
    scaled = distance / (own_static[3][None, :, None] * near_static[:, 3][:, None, :])
    cubed = thole_a * scaled * scaled * scaled
    damping = jnp.exp(-cubed)
    screen = lax.erfc(ewald_beta * distance)
    gaussian = 2.0 * ewald_beta / math.sqrt(math.pi) * jnp.exp(-(ewald_beta * ewald_beta) * safe_sq)
    inverse_sq = 1.0 / safe_sq
    inverse_cube = inverse_sq / distance
    first_term = (screen - damping) * inverse_cube + gaussian * inverse_sq
    second = (
        3.0 * (screen - (1.0 + cubed) * damping) * inverse_cube * inverse_sq
        + gaussian * (2.0 * ewald_beta * ewald_beta + 3.0 * inverse_sq) * inverse_sq
    )
    first_term = jnp.where(itself, 0.0, first_term)
    second = jnp.where(itself, 0.0, second)
    projected = jnp.sum(near_dipole[:, :, :, None, :] * separation[:, None, :, :, :], axis=2)
    weighted = second[:, None] * projected
    outward = jnp.sum(weighted[:, :, None] * separation[:, None], axis=(0, 4))
    inward = jnp.sum(first_term[:, None, None] * near_dipole[:, :, :, None, :], axis=(0, 4))
    return outward - inward


def hartley(length):
    counter = jnp.arange(length, dtype=jnp.int32)
    angles = (
        2.0 * math.pi / length * (counter[:, None] * counter[None, :] % length).astype(jnp.float32)
    )
    return jnp.cos(angles) + jnp.sin(angles)


def placed_table(first_cell, weights, extent):
    slot_index = jnp.arange(extent, dtype=jnp.int32)[:, None]
    placed = jnp.zeros((extent, first_cell.shape[0]), jnp.float32)
    for stencil in range(5):
        placed = placed + jnp.where(
            slot_index == (first_cell[None, :] + stencil) % extent, weights[stencil][None, :], 0.0
        )
    return placed


def pad_axis(source, axis_pos, leading, trailing):
    widths = [(0, 0)] * source.ndim
    widths[axis_pos] = (leading, trailing)
    return jnp.pad(source, widths)


def fold_cycle(cycle_only, axis_pos, inner_len):
    middle = lax.slice_in_dim(cycle_only, 4, inner_len + 4, axis=axis_pos)
    lower_cycle = lax.slice_in_dim(cycle_only, 0, 2, axis=axis_pos)
    upper_cycle = lax.slice_in_dim(cycle_only, inner_len + 6, inner_len + 8, axis=axis_pos)
    return (
        middle
        + pad_axis(lower_cycle, axis_pos, 0, inner_len - 2)
        + pad_axis(upper_cycle, axis_pos, inner_len - 2, 0)
    )


def clear_inside(extended, extents):
    inside = None
    for axis_pos, inner_len in extents:
        slot_index = lax.broadcasted_iota(jnp.int32, extended.shape, axis_pos)
        within = (slot_index >= 2) & (slot_index < inner_len + 6)
        inside = within if inside is None else inside & within
    return jnp.where(inside, 0.0, extended)


def inner_sum(left_arr, right_arr):
    return lax.psum(jnp.sum(left_arr * right_arr, axis=(1, 2)), ("row", "col"))


def pencil_local(field_rhs, positions, polar, grid_base, tile_lists):
    rows_count = lax.axis_size("row")
    cols_count = lax.axis_size("col")
    grid_x = CX * rows_count
    grid_y = CY * cols_count
    atom_count = polar.shape[-1]
    tile_count = atom_count // TILE
    slab_depth = KZ // tile_count
    window_len = slab_depth + 4
    box_spans = (float(grid_x), float(grid_y), float(KZ))
    own_place = positions[0, 0]
    own_base = grid_base[0, 0]
    own_polar = polar[0, 0]
    lengths = jnp.array([grid_x, grid_y, KZ], dtype=jnp.int32)[:, None]
    cell_index = (own_base + 2) % lengths
    fraction = own_place - cell_index.astype(jnp.float32)
    values, slopes = spline_table(fraction)
    first_x = (own_base[0] - lax.axis_index("row") * CX + 2) % grid_x
    first_y = (own_base[1] - lax.axis_index("col") * CY + 2) % grid_y
    rows_x = placed_table(first_x, values[:, 0], CX + 4)
    slope_x = placed_table(first_x, slopes[:, 0], CX + 4)
    rows_y = placed_table(first_y, values[:, 1], CY + 4)
    slope_y = placed_table(first_y, slopes[:, 1], CY + 4)
    tile_start = jnp.arange(atom_count, dtype=jnp.int32) // TILE * slab_depth
    first_z = (own_base[2] + 2 - tile_start) % KZ
    rows_z = placed_table(first_z, values[:, 2], window_len)
    slope_z = placed_table(first_z, slopes[:, 2], window_len)
    plane_count = (CX + 4) * (CY + 4)
    plane_dx = (slope_x[:, None, :] * rows_y[None, :, :]).reshape(plane_count, atom_count)
    plane_dy = (rows_x[:, None, :] * slope_y[None, :, :]).reshape(plane_count, atom_count)
    plane_flat = (rows_x[:, None, :] * rows_y[None, :, :]).reshape(plane_count, atom_count)
    window_rows = jnp.moveaxis(rows_z.reshape(window_len, tile_count, TILE), 1, 0)
    window_slope = jnp.moveaxis(slope_z.reshape(window_len, tile_count, TILE), 1, 0)
    depth_table = jnp.concatenate([window_rows, window_slope], axis=2)
    grid_scale = 1.0 / (grid_x * grid_y * KZ)
    hartley_x = hartley(grid_x)
    hartley_y = hartley(grid_y)
    hartley_z = hartley(KZ)
    block_y = grid_y // rows_count
    block_z = KZ // cols_count
    wave_x = jnp.arange(grid_x, dtype=jnp.int32)[:, None, None]
    wave_y = (lax.axis_index("row") * block_y + jnp.arange(block_y, dtype=jnp.int32))[None, :, None]
    wave_z = (lax.axis_index("col") * block_z + jnp.arange(block_z, dtype=jnp.int32))[None, None, :]
    kernel = influence(wave_x, wave_y, wave_z, grid_x, grid_y, KZ) * grid_scale
    root_scale = jnp.power(own_polar, 1.0 / 6.0)
    own_static = jnp.concatenate([own_place, root_scale[None]], axis=0)
    near_static = with_halo(own_static[None, None], (("row", 0), ("col", 1)), 1)
    near_static = jnp.moveaxis(near_static.reshape(9, 4, tile_count, TILE), 2, 1).reshape(
        9 * tile_count, 4, TILE
    )
    own_tiles = jnp.moveaxis(own_static.reshape(4, tile_count, TILE), 1, 0)
    own_lists = tile_lists[0, 0]
    polar_wide = own_polar[None, None, :]
    solution = jnp.zeros_like(field_rhs[0, 0])
    residual = field_rhs[0, 0]
    scaled_res = polar_wide * residual
    direction = scaled_res
    progress = inner_sum(residual, scaled_res)
    for iteration in range(ITERS):
        near_dip = with_halo(direction[None, None], (("row", 0), ("col", 1)), 1)
        near_dip = jnp.moveaxis(near_dip.reshape(9, RHS, 3, tile_count, TILE), 3, 1).reshape(
            9 * tile_count, RHS, 3, TILE
        )

        def one_tile(tile_pos):
            picked = own_lists[tile_pos]
            return tile_field(own_tiles[tile_pos], near_static[picked], near_dip[picked], box_spans)

        fields = lax.map(one_tile, jnp.arange(tile_count, dtype=jnp.int32))
        direct = jnp.moveaxis(fields, 0, 2).reshape(RHS, 3, atom_count)
        slope_terms = (
            direction[:, 0, None, :] * plane_dx[None] + direction[:, 1, None, :] * plane_dy[None]
        )
        flat_terms = direction[:, 2, None, :] * plane_flat[None]
        spread_left = jnp.concatenate(
            [
                slope_terms.reshape(RHS, plane_count, tile_count, TILE),
                flat_terms.reshape(RHS, plane_count, tile_count, TILE),
            ],
            axis=3,
        )
        spread_windows = jnp.einsum("sptb,twb->sptw", spread_left, depth_table, precision=highest)
        main_part = spread_windows[..., :slab_depth].reshape(spread_windows.shape[:-2] + (KZ,))
        tail_part = pad_axis(
            spread_windows[..., slab_depth:], spread_windows.ndim - 1, 0, slab_depth - 4
        )
        tail_part = tail_part.reshape(spread_windows.shape[:-2] + (KZ,))[..., : KZ + 4 - slab_depth]
        last_axis = main_part.ndim - 1
        padded_line = pad_axis(main_part, last_axis, 0, 4) + pad_axis(
            tail_part, last_axis, slab_depth, 0
        )
        inner = padded_line[..., 2 : KZ + 2]
        spread_tile = (
            inner
            + pad_axis(padded_line[..., 0:2], last_axis, KZ - 2, 0)
            + pad_axis(padded_line[..., KZ + 2 : KZ + 4], last_axis, 0, KZ - 2)
        ).reshape(RHS, CX + 4, CY + 4, KZ)
        extended = with_halo(spread_tile, (("row", 1), ("col", 2)), 2)
        cycle_only = clear_inside(extended, ((1, CX), (2, CY)))
        folded = fold_cycle(fold_cycle(cycle_only, 1, CX), 2, CY)
        spectrum = jnp.einsum(
            "sxyz,zk->sxyk",
            spread_tile[:, 2 : CX + 2, 2 : CY + 2] + folded,
            hartley_z,
            precision=highest,
        )
        along_y = jnp.einsum(
            "sxyz,yk->sxkz",
            lax.all_to_all(spectrum, "col", split_axis=3, concat_axis=2, tiled=True),
            hartley_y,
            precision=highest,
        )
        along_x = (
            jnp.einsum(
                "sxyz,xk->skyz",
                lax.all_to_all(along_y, "row", split_axis=2, concat_axis=1, tiled=True),
                hartley_x,
                precision=highest,
            )
            * kernel[None]
        )
        mixed_part = jnp.einsum("sxyz,xk->skyz", along_x, hartley_x, precision=highest)
        returned = lax.all_to_all(mixed_part, "row", split_axis=1, concat_axis=2, tiled=True)
        swapped = jnp.einsum("sxyz,yk->sxkz", returned, hartley_y, precision=highest)
        restored = lax.all_to_all(swapped, "col", split_axis=2, concat_axis=3, tiled=True)
        padded = with_halo(
            jnp.einsum("sxyz,zk->sxyk", restored, hartley_z, precision=highest),
            (("row", 1), ("col", 2)),
            2,
        )
        line = padded.reshape(RHS, plane_count, KZ)
        extended_line = jnp.concatenate([line[..., KZ - 2 :], line, line[..., :2]], axis=-1)
        windows = jnp.stack(
            [
                extended_line[..., tile * slab_depth : tile * slab_depth + window_len]
                for tile in range(tile_count)
            ],
            axis=-2,
        )
        sampled = jnp.einsum("sptw,twb->sptb", windows, depth_table, precision=highest)
        with_flat = sampled[..., :TILE].reshape(RHS, plane_count, atom_count)
        with_slope = sampled[..., TILE:].reshape(RHS, plane_count, atom_count)
        recip_part = jnp.stack(
            [
                jnp.sum(with_flat * plane_dx[None], axis=1),
                jnp.sum(with_flat * plane_dy[None], axis=1),
                jnp.sum(with_slope * plane_flat[None], axis=1),
            ],
            axis=1,
        )
        image_field = direction / polar_wide - direct + recip_part - self_coef * direction
        step_size = (progress / inner_sum(direction, image_field))[:, None, None]
        solution = solution + step_size * direction
        residual = residual - step_size * image_field
        scaled_res = polar_wide * residual
        progress_next = inner_sum(residual, scaled_res)
        direction = scaled_res + (progress_next / progress)[:, None, None] * direction
        progress = progress_next
    return (solution[None, None], residual[None, None])


X_PAD = CX + 4
Y_PAD = CY + 4
SLOT_ROWS = 16
SPLIT = 2
VMEM_LIMIT = 60_000_000
SMALL_VMEM_LIMIT = 24_000_000
EARLY_TILES = 1
PAIR_ROWS = 32
GROUP = 8
SHARED = 2
SCREEN_SCALE = 0.4
SCREEN_COEF = (
    0.22567588090896606,
    0.2256690263748169,
    0.20785020291805267,
    0.16849851608276367,
    0.14156343042850494,
    -0.005832736846059561,
    0.16930203139781952,
    -0.1830107867717743,
    0.05028456076979637,
)


def halves(value):
    high = value.astype(jnp.bfloat16)
    return high, (value - high.astype(jnp.float32)).astype(jnp.bfloat16)


def halves_np(value):
    value = value.astype(np.float32)
    high = value.astype(ml_dtypes.bfloat16)
    return high, (value - high.astype(np.float32)).astype(ml_dtypes.bfloat16)


def product(left, right, left_dim=1, right_dim=0):
    def one(first, second):
        return lax.dot_general(
            first,
            second,
            (((left_dim,), (right_dim,)), ((), ())),
            preferred_element_type=jnp.float32,
        )

    return one(left[0], right[0]) + (one(left[1], right[0]) + one(left[0], right[1]))


def cas_np(wave, place, length):
    angles = 2.0 * np.pi / length * (wave[:, None] * place[None, :] % length)
    return np.cos(angles) + np.sin(angles)


def modulus_np(wave, length):
    coef = np.array([1.0, 11.0, 11.0, 1.0]) / 24.0
    angles = 2.0 * np.pi / length * (wave[:, None] * np.arange(4)[None, :])
    return (coef * np.cos(angles)).sum(1) ** 2 + (coef * np.sin(angles)).sum(1) ** 2


def influence_np(length_x, length_y, length_z):
    total = np.zeros((length_x, length_y, length_z))
    modulus = np.ones((length_x, length_y, length_z))
    excluded = np.zeros((length_x, length_y, length_z), bool)
    for axis, length in enumerate((length_x, length_y, length_z)):
        wave = np.arange(length)
        shape = [1, 1, 1]
        shape[axis] = length
        total = total + ((np.minimum(wave, length - wave) / length) ** 2).reshape(shape)
        modulus = modulus * modulus_np(wave, length).reshape(shape)
        excluded = excluded | (wave * 2 == length).reshape(shape)
    excluded[0, 0, 0] = True
    safe = np.where(excluded, 1.0, total)
    result = np.exp(-(np.pi**2) / ewald_beta**2 * safe) / (
        np.pi * safe * np.where(excluded, 1.0, modulus)
    )
    return np.where(excluded, 0.0, result) / (length_x * length_y * length_z)


def slab_tables(rows_count, cols_count):
    grid_x = CX * rows_count
    grid_y = CY * cols_count
    devices = rows_count * cols_count
    chunk = KZ // devices
    wave_z = (np.arange(devices)[None, :] * chunk + np.arange(chunk)[:, None]).reshape(-1)
    along_z = cas_np(wave_z, np.arange(KZ), KZ)
    place_x = np.arange(rows_count)[:, None] * CX + np.arange(X_PAD)[None, :] - 2
    along_x = cas_np(np.arange(grid_x), place_x.reshape(-1) % grid_x, grid_x)
    x_high, x_low = halves_np(along_x)
    forward_x = np.concatenate([x_high, x_low, x_high], axis=1)
    backward_x = np.concatenate([x_high.T, x_low.T, x_high.T], axis=1)
    place_y = (np.arange(cols_count)[:, None] * CY + np.arange(Y_PAD)[None, :] - 2) % grid_y
    along_y = cas_np(np.arange(grid_y), place_y.reshape(-1), grid_y)
    along_y = along_y.reshape(grid_y, cols_count, Y_PAD)
    units = chunk * RHS // SPLIT
    block = np.einsum("uv,kcy->cuyvk", np.eye(units), along_y)
    block = block.reshape(cols_count * units * Y_PAD, units * grid_y)
    kernel = influence_np(grid_x, grid_y, KZ).reshape(grid_x, grid_y, devices, chunk)
    kernel = np.transpose(kernel, (2, 0, 3, 1))[:, :, :, None, :]
    kernel = np.broadcast_to(kernel, (devices, grid_x, chunk, RHS, grid_y))
    kernel = kernel.reshape(devices, grid_x, SPLIT, units * grid_y)
    kernel = np.moveaxis(kernel, 2, 1).reshape(devices, SPLIT * grid_x, units * grid_y)
    kernel = kernel.astype(np.float32)
    return dict(
        along_z=halves_np(along_z),
        forward_x=forward_x,
        backward_x=backward_x,
        block=halves_np(block),
        kernel=kernel,
    )


def pack_body(rhs_ref, place_ref, polar_ref, start_ref, payload_ref):
    polar = polar_ref[...]
    start = read_rows(rhs_ref) * polar
    start_ref[...] = start
    place = [place_ref[dim] for dim in range(3)]
    everything = jnp.concatenate(place + [1.0 / jnp.sqrt(polar), start], axis=0)
    store_payload(payload_ref, everything)


def read_rows(rows_ref):
    return jnp.concatenate([rows_ref[dim] for dim in range(3)], axis=0)


def store_payload(payload_ref, everything):
    tile_count = everything.shape[1] // TILE
    for quantity in range(everything.shape[0]):
        for tile in range(tile_count):
            row = quantity * tile_count + tile
            payload_ref[row : row + 1, :] = everything[
                quantity : quantity + 1, tile * TILE : (tile + 1) * TILE
            ]


def placed_rows(slot, weights, extent):
    slot_index = lax.broadcasted_iota(jnp.int32, (extent, slot.shape[1]), 0)
    placed = jnp.zeros((extent, slot.shape[1]), jnp.float32)
    for stencil in range(5):
        target = slot + stencil
        if extent == KZ:
            target = jnp.where(target >= KZ, target - KZ, target)
        placed = placed + jnp.where(slot_index == target, weights[stencil], 0.0)
    return placed


def spread_into(message_ref, moment, rows_x, slope_x, rows_y, slope_y, depth, devices):
    blocks = []
    for step in range(X_PAD):
        flat_x = rows_x[step : step + 1]
        tilt_x = slope_x[step : step + 1]
        for rhs in range(RHS):
            part_x = tilt_x * moment[rhs : rhs + 1]
            part_y = flat_x * moment[RHS + rhs : RHS + rhs + 1]
            part_z = flat_x * moment[2 * RHS + rhs : 2 * RHS + rhs + 1]
            blocks.append(
                jnp.concatenate([part_x * rows_y + part_y * slope_y, part_z * rows_y], axis=1)
            )
    charges = jnp.concatenate(blocks, axis=0)
    spectrum = product(depth, halves(charges), 1, 1)
    slot_rows = message_ref.shape[0] // devices
    chunk = KZ // devices
    width = RHS * Y_PAD
    for step in range(X_PAD):
        message_ref[pl.ds(step, devices, stride=slot_rows), :] = jnp.concatenate(
            [
                spectrum[unit * devices : (unit + 1) * devices, step * width : (step + 1) * width]
                for unit in range(chunk)
            ],
            axis=1,
        )


def sample_from(message_ref, rows_x, slope_x, rows_y, slope_y, depth, devices):
    chunk = KZ // devices
    width = RHS * Y_PAD
    slot_rows = message_ref.shape[0] // devices
    pieces = [
        message_ref[pl.ds(step, devices, stride=slot_rows), :] for step in range(X_PAD)
    ]
    spare = jnp.zeros((devices, KZ - X_PAD * width), jnp.float32)
    spectrum = jnp.concatenate(
        [
            jnp.concatenate(
                [piece[:, unit * width : (unit + 1) * width] for piece in pieces] + [spare], axis=1
            )
            for unit in range(chunk)
        ],
        axis=0,
    )
    spectrum = jnp.transpose(spectrum)[: X_PAD * width]
    sampled = product(halves(spectrum), depth, 1, 0)
    atoms = rows_x.shape[1]
    fields = [None] * (3 * RHS)
    for rhs in range(RHS):
        sum_x = sum_y = sum_z = None
        for step in range(X_PAD):
            first = step * width + rhs * Y_PAD
            flat = sampled[first : first + Y_PAD, :atoms]
            tilt = sampled[first : first + Y_PAD, atoms:]
            part_x = slope_x[step : step + 1] * flat
            part_y = rows_x[step : step + 1] * flat
            part_z = rows_x[step : step + 1] * tilt
            sum_x = part_x if sum_x is None else sum_x + part_x
            sum_y = part_y if sum_y is None else sum_y + part_y
            sum_z = part_z if sum_z is None else sum_z + part_z
        fields[rhs] = jnp.sum(sum_x * rows_y, axis=0, keepdims=True)
        fields[RHS + rhs] = jnp.sum(sum_y * slope_y, axis=0, keepdims=True)
        fields[2 * RHS + rhs] = jnp.sum(sum_z * rows_y, axis=0, keepdims=True)
    return jnp.concatenate(fields, axis=0)


def read_tables(tables_ref):
    return (
        tables_ref[0:X_PAD],
        tables_ref[SLOT_ROWS : SLOT_ROWS + X_PAD],
        tables_ref[2 * SLOT_ROWS : 2 * SLOT_ROWS + Y_PAD],
        tables_ref[2 * SLOT_ROWS + Y_PAD : 2 * SLOT_ROWS + 2 * Y_PAD],
    )


def setup_body(
    lengths,
    devices,
    place_ref,
    base_ref,
    start_ref,
    z_high_ref,
    z_low_ref,
    message_ref,
    tables_ref,
    depth_high_ref,
    depth_low_ref,
):
    base = [base_ref[dim] for dim in range(3)]
    fractions = []
    cells = []
    for dim in range(3):
        cell = base[dim] + 2
        cell = jnp.where(cell >= lengths[dim], cell - lengths[dim], cell)
        cells.append(cell)
        fractions.append(place_ref[dim] - cell.astype(jnp.float32))
    values, slopes = spline_table(jnp.concatenate(fractions, axis=0))
    values = [[values[stencil][dim : dim + 1] for stencil in range(5)] for dim in range(3)]
    slopes = [[slopes[stencil][dim : dim + 1] for stencil in range(5)] for dim in range(3)]
    slot_x = lax.rem(cells[0], CX)
    slot_y = lax.rem(cells[1], CY)
    tables_ref[0:SLOT_ROWS] = placed_rows(slot_x, values[0], SLOT_ROWS)
    tables_ref[SLOT_ROWS : 2 * SLOT_ROWS] = placed_rows(slot_x, slopes[0], SLOT_ROWS)
    tables_ref[2 * SLOT_ROWS : 2 * SLOT_ROWS + Y_PAD] = placed_rows(slot_y, values[1], Y_PAD)
    tables_ref[2 * SLOT_ROWS + Y_PAD : 2 * SLOT_ROWS + 2 * Y_PAD] = placed_rows(
        slot_y, slopes[1], Y_PAD
    )
    window = jnp.concatenate(
        [
            placed_rows(base[2], values[2], KZ),
            placed_rows(base[2], slopes[2], KZ),
        ],
        axis=1,
    )
    depth = product((z_high_ref[...], z_low_ref[...]), halves(window), 1, 0)
    depth = halves(depth)
    depth_high_ref[...] = depth[0]
    depth_low_ref[...] = depth[1]
    for made in (tables_ref, depth_high_ref, depth_low_ref):
        made.send()
    spread_into(message_ref, start_ref[...], *read_tables(tables_ref), depth, devices)


def transform_in(message_ref, forward_ref, block_high_ref, block_low_ref, rows_count, cols_count):
    gathered = jnp.concatenate(
        [
            jnp.concatenate(
                [
                    message_ref[(r * cols_count + c) * X_PAD : (r * cols_count + c + 1) * X_PAD]
                    for r in range(rows_count)
                ],
                axis=0,
            )
            for c in range(cols_count)
        ],
        axis=1,
    )
    high, low = halves(gathered)
    along = jnp.dot(
        forward_ref[...],
        jnp.concatenate([high, high, low], axis=0),
        preferred_element_type=jnp.float32,
    )
    part = along.shape[1] // cols_count // SPLIT
    along = jnp.concatenate(
        [
            jnp.concatenate(
                [
                    along[:, (c * SPLIT + half) * part : (c * SPLIT + half + 1) * part]
                    for c in range(cols_count)
                ],
                axis=1,
            )
            for half in range(SPLIT)
        ],
        axis=0,
    )
    return product(halves(along), (block_high_ref[...], block_low_ref[...]))


def transform_out(result_ref, values, backward_ref, block_high_ref, block_low_ref, counts):
    rows_count, cols_count = counts
    spread = product(halves(values), (block_high_ref[...], block_low_ref[...]), 1, 1)
    grid_x = spread.shape[0] // SPLIT
    part = spread.shape[1] // cols_count
    spread = jnp.concatenate(
        [
            spread[half * grid_x : (half + 1) * grid_x, c * part : (c + 1) * part]
            for c in range(cols_count)
            for half in range(SPLIT)
        ],
        axis=1,
    )
    high, low = halves(spread)
    along = jnp.dot(
        backward_ref[...],
        jnp.concatenate([high, high, low], axis=0),
        preferred_element_type=jnp.float32,
    )
    width = along.shape[1] // cols_count
    slot_rows = result_ref.shape[0] // (rows_count * cols_count)
    for r in range(rows_count):
        for c in range(cols_count):
            first = (r * cols_count + c) * slot_rows
            result_ref[first : first + X_PAD, :] = along[
                r * X_PAD : (r + 1) * X_PAD, c * width : (c + 1) * width
            ]


def middle_first_body(
    counts,
    message_ref,
    kernel_ref,
    forward_ref,
    backward_ref,
    block_high_ref,
    block_low_ref,
    result_ref,
    wave_ref,
):
    wave = transform_in(message_ref, forward_ref, block_high_ref, block_low_ref, *counts)
    wave_ref[...] = wave
    wave_ref.send()
    transform_out(
        result_ref, wave * kernel_ref[...], backward_ref, block_high_ref, block_low_ref, counts
    )


def gather_rows(parts):
    tiles = [
        parts[GROUP * tile : GROUP * tile + GROUP, :] for tile in range(parts.shape[0] // GROUP)
    ]
    return jnp.concatenate(tiles, axis=1)[0 : 3 * RHS]


def row_total(value, rhs):
    row = lax.broadcasted_iota(jnp.int32, value.shape, 0)
    return total(jnp.where(lax.rem(row, RHS) == rhs, value, 0.0))


def total(value):
    return jnp.sum(jnp.sum(value, axis=0, keepdims=True), axis=1, keepdims=True)


def middle_second_body(
    counts,
    message_ref,
    kernel_ref,
    forward_ref,
    backward_ref,
    block_high_ref,
    block_low_ref,
    wave_ref,
    rhs_ref,
    start_ref,
    image_ref,
    second_ref,
    near_ref,
    polar_ref,
    result_ref,
):
    rhs_rows = read_rows(rhs_ref)
    near_rows = gather_rows(near_ref)
    wave = transform_in(message_ref, forward_ref, block_high_ref, block_low_ref, *counts)
    filtered = wave * kernel_ref[...]
    transform_out(result_ref, filtered, backward_ref, block_high_ref, block_low_ref, counts)
    before = wave_ref[...]
    grid_y = CY * counts[1]
    lane = lax.broadcasted_iota(jnp.int32, wave.shape, 1)
    own_rhs = lax.rem(lax.div(lane, grid_y), RHS)
    second = second_ref[...]
    start = start_ref[...]
    image = image_ref[...]
    local_part = second / polar_ref[...] - near_rows - self_coef * second
    slot = lax.broadcasted_iota(jnp.int32, (1, result_ref.shape[1]), 1)
    sums = jnp.zeros((1, result_ref.shape[1]), jnp.float32)
    for rhs in range(RHS):
        mine = own_rhs == rhs
        parts = (
            row_total(rhs_rows * start, rhs),
            row_total(start * image, rhs),
            row_total(second * image, rhs),
            row_total(start * local_part, rhs) + total(jnp.where(mine, before * filtered, 0.0)),
            row_total(second * local_part, rhs) + total(jnp.where(mine, wave * filtered, 0.0)),
        )
        for index, part in enumerate(parts):
            sums = jnp.where(slot == rhs * len(parts) + index, part, sums)
    devices = counts[0] * counts[1]
    result_ref[pl.ds(X_PAD, devices, stride=X_PAD + 1), :] = jnp.broadcast_to(
        sums, (devices, sums.shape[1])
    )


def sample_body(
    devices,
    message_ref,
    tables_ref,
    depth_high_ref,
    depth_low_ref,
    start_ref,
    near_ref,
    polar_ref,
    image_ref,
    second_ref,
    payload_ref,
):
    tables = read_tables(tables_ref)
    depth = (depth_high_ref[...], depth_low_ref[...])
    field = sample_from(message_ref, *tables, depth, devices)
    start = start_ref[...]
    polar = polar_ref[...]
    image = start / polar - gather_rows(near_ref) + field - self_coef * start
    second = polar * image
    image_ref[...] = image
    second_ref[...] = second
    store_payload(payload_ref, second)


def spread_body(
    devices,
    tables_ref,
    depth_high_ref,
    depth_low_ref,
    second_ref,
    result_ref,
):
    depth = (depth_high_ref[...], depth_low_ref[...])
    spread_into(result_ref, second_ref[...], *read_tables(tables_ref), depth, devices)


def final_body(
    devices,
    message_ref,
    tables_ref,
    depth_high_ref,
    depth_low_ref,
    rhs_ref,
    start_ref,
    image_ref,
    second_ref,
    near_ref,
    polar_ref,
    dipole_ref,
    residual_ref,
):
    tables = read_tables(tables_ref)
    depth = (depth_high_ref[...], depth_low_ref[...])
    field = sample_from(message_ref, *tables, depth, devices)
    second = second_ref[...]
    start = start_ref[...]
    image = image_ref[...]
    image_second = second / polar_ref[...] - gather_rows(near_ref) + field - self_coef * second
    sums = jnp.sum(
        message_ref[pl.ds(X_PAD, devices, stride=X_PAD + 1), :], axis=0, keepdims=True
    )
    steps = []
    for rhs in range(RHS):
        progress, start_image, second_image, start_next, second_next = [
            sums[:, rhs * 5 + index : rhs * 5 + index + 1] for index in range(5)
        ]
        step = progress / start_image
        progress_next = progress - 2.0 * step * start_image + step * step * second_image
        grown = 1.0 + progress_next / progress
        curvature = (
            grown * grown * start_image
            - step * grown * (start_next + second_image)
            + step * step * second_next
        )
        steps.append((step, grown, progress_next / curvature))
    row = lax.broadcasted_iota(jnp.int32, (RHS, 1), 0)
    step, grown, step_next = [
        sum(jnp.where(row == rhs, steps[rhs][index], 0.0) for rhs in range(RHS))
        for index in range(3)
    ]
    for dim in range(3):
        rows = slice(dim * RHS, (dim + 1) * RHS)
        direction = grown * start[rows] - step * second[rows]
        image_direction = grown * image[rows] - step * image_second[rows]
        dipole_ref[dim] = step * start[rows] + step_next * direction
        residual_ref[dim] = rhs_ref[dim] - step * image[rows] - step_next * image_direction


def near_base(entry, brick_rows):
    return lax.shift_right_logical(entry, 2) * brick_rows + lax.bitwise_and(entry, 3)


def nearest(places, origin, span):
    return places - span * jnp.floor((places - origin) * (1.0 / span) + 0.5)


def unwrap_near(near, tile_count, spans):
    rows = near.shape[0] // 9
    for dim in range(2):
        own = 4 * rows + dim * tile_count
        origin = near[own : own + 1, 0:1]
        for brick in range(9):
            first = brick * rows + dim * tile_count
            near[first : first + tile_count, :] = nearest(
                near[first : first + tile_count, :], origin, spans[dim]
            )


def pick_rows(picked, near, lists_ref, tile, place, tile_count, quantities, origin, span):
    rows = near.shape[0] // 9
    place = place * lists_ref.shape[1] * quantities * GROUP
    for entry in range(lists_ref.shape[1]):
        base = near_base(lists_ref[tile, entry], rows)
        for quantity in range(quantities):
            values = near[pl.ds(base + quantity * tile_count, 1), :]
            if quantity == 2 and span is not None:
                values = nearest(values, origin, span)
            first = place + (entry * quantities + quantity) * GROUP
            picked[first : first + GROUP, :] = jnp.broadcast_to(values, (GROUP, TILE))


def widen_own(near, quantities, tile_count, tile, place, wide):
    offset = near.shape[0] // 9 * 4
    rows = [
        near[offset + quantity * tile_count + tile : offset + quantity * tile_count + tile + 1, :]
        for quantity in range(quantities)
    ]
    spare = jnp.zeros((TILE - quantities, TILE), jnp.float32)
    columns = jnp.transpose(jnp.concatenate(rows + [spare], axis=0))
    for quantity in range(quantities):
        first = (place * quantities + quantity) * TILE
        wide[first : first + TILE, :] = jnp.broadcast_to(
            columns[:, quantity : quantity + 1], (TILE, TILE)
        )


def add_field(sums, first_term, second_term, apart, moments):
    for rhs in range(RHS):
        moment = [moments[RHS * dim + rhs] for dim in range(3)]
        projected = moment[0] * apart[0] + moment[1] * apart[1] + moment[2] * apart[2]
        weighted = second_term * projected
        for dim in range(3):
            index = RHS * dim + rhs
            sums[index] = sums[index] + (weighted * apart[dim] - first_term * moment[dim])


def finish_sums(field_ref, sums_ref, first_tile, place):
    place = place * 3 * RHS
    lane = lax.broadcasted_iota(jnp.int32, (TILE, TILE), 1)
    merged = jnp.zeros((TILE, TILE), jnp.float32)
    for index in range(3 * RHS):
        first = (place + index) * TILE
        column = jnp.sum(sums_ref[first : first + TILE, :], axis=1, keepdims=True)
        merged = jnp.where(lane == index, column, merged)
    first = (first_tile + place // (3 * RHS)) * GROUP
    field_ref[first : first + GROUP, :] = jnp.transpose(merged)[0:GROUP]


def pair_rows(start, group):
    return pl.ds(pl.multiple_of(start + group * GROUP, GROUP), GROUP)


def wide_rows(start, group, quantity):
    return pl.ds(pl.multiple_of(quantity * TILE + start + group * GROUP, GROUP), GROUP)


def pair_terms(square_dist, damp):
    inverse = lax.rsqrt(square_dist)
    distance = square_dist * inverse
    inverse_sq = inverse * inverse
    inverse_cube = inverse_sq * inverse
    cubed = damp * (distance * square_dist)
    damping = jnp.exp(cubed)
    bell = jnp.exp(-(ewald_beta * ewald_beta) * square_dist)
    stretched = 1.0 + (SCREEN_SCALE * ewald_beta) * distance
    turned = pl.reciprocal(stretched, approx=True)
    turned = turned * (2.0 - stretched * turned)
    series = SCREEN_COEF[-1] * turned + SCREEN_COEF[-2]
    for coef in SCREEN_COEF[-3::-1]:
        series = series * turned + coef
    screen = bell * turned * series
    gaussian = (2.0 * ewald_beta / math.sqrt(math.pi)) * bell
    bare = screen - damping
    first_term = bare * inverse_cube + gaussian * inverse_sq
    second_term = (
        3.0 * (first_term + (cubed * damping) * inverse_cube)
        + (2.0 * ewald_beta * ewald_beta) * gaussian
    ) * inverse_sq
    return first_term, second_term


def step_rows(step, size, offset):
    return pl.ds(pl.multiple_of(step * size + offset, GROUP), GROUP)


def tile_rows(step, rows):
    return pl.ds(pl.multiple_of(step * rows, GROUP), rows)


def start_all(copies):
    for copy in copies:
        copy.start()


def wait_all(copies):
    for copy in copies:
        copy.wait()


def near_copies(sources, near, semaphore):
    rows = sources[0].shape[0]
    return [
        pltpu.make_async_copy(
            source, near.at[index * rows : (index + 1) * rows, :], semaphore.at[index]
        )
        for index, source in enumerate(sources)
    ]


def term_copies(terms, buffers, semaphore, begin, step, size, inward):
    rows = pl.ds(pl.multiple_of((begin + step) * size, GROUP), size)
    place = pl.ds(pl.multiple_of(step * size, GROUP), size)
    copies = []
    for index in range(2):
        far, here = terms[index].at[rows, :], buffers[index].at[place, :]
        ends = (far, here) if inward else (here, far)
        copies.append(pltpu.make_async_copy(*ends, semaphore.at[index, step]))
    return copies


def pair_first_body(
    first_tile,
    last_tile,
    tile_count,
    spans,
    lists_ref,
    up_ref,
    stack_ref,
    down_ref,
    *others,
):
    first_ref, second_ref, field_ref, near_ref = others[-14:-10]
    near, picked, wide, sums_ref, kept, field, first_buffer, second_buffer, semaphore, busy = others[-10:]
    terms = (first_ref, second_ref)
    buffers = (first_buffer, second_buffer)
    copies = near_copies((up_ref, stack_ref, down_ref), near, semaphore.at[0])
    if first_tile > 0:
        copies.append(
            pltpu.make_async_copy(
                others[0], field.at[0 : first_tile * GROUP, :], semaphore.at[0, 3]
            )
        )
    start_all(copies)
    wait_all(copies)
    entries = lists_ref.shape[1]
    rows = near.shape[0] // 9
    quantities = rows // tile_count
    unwrap_near(near, tile_count, spans)
    for brick in range(9):
        kept[brick * 3 * tile_count : (brick + 1) * 3 * tile_count, :] = near[
            brick * rows : brick * rows + 3 * tile_count, :
        ]
    keep = pltpu.make_async_copy(kept, near_ref, semaphore.at[1, 3])
    keep.start()
    for place, tile in enumerate(range(first_tile, last_tile)):
        widen_own(near, 4, tile_count, tile, place, wide)
        own = rows * 4 + 2 * tile_count + tile
        origin = near[own : own + 1, 0:1]
        pick_rows(picked, near, lists_ref, tile, place, tile_count, quantities, origin, spans[2])
    parts = TILE // PAIR_ROWS
    steps = (last_tile - first_tile) * parts

    size = entries * PAIR_ROWS

    def sent(step):
        return term_copies(terms, buffers, busy, first_tile * parts, step, size, False)

    @pl.loop(0, steps)
    def _(step):
        tile = lax.div(step, parts)
        start = lax.rem(step, parts) * PAIR_ROWS
        step_picked = picked.at[tile_rows(tile, entries * quantities * GROUP), :]
        step_wide = wide.at[tile_rows(tile, 4 * TILE), :]
        step_sums = sums_ref.at[tile_rows(tile, 3 * RHS * TILE), :]
        for pair in range(PAIR_ROWS // GROUP // SHARED):
            groups = range(pair * SHARED, (pair + 1) * SHARED)
            own = [
                [step_wide[wide_rows(start, group, dim), :] for dim in range(4)] for group in groups
            ]
            own_damp = [-thole_a * columns[3] for columns in own]
            sums = [
                [jnp.zeros((GROUP, TILE), jnp.float32) for _ in range(3 * RHS)] for _ in groups
            ]
            for entry in range(entries):
                first = entry * quantities * GROUP
                rows = [
                    step_picked[first + quantity * GROUP : first + (quantity + 1) * GROUP, :]
                    for quantity in range(quantities)
                ]
                for index, group in enumerate(groups):
                    apart = [rows[dim] - own[index][dim] for dim in range(3)]
                    square_dist = apart[0] * apart[0] + apart[1] * apart[1] + apart[2] * apart[2]
                    if entry == 0:
                        itself = (
                            lax.broadcasted_iota(jnp.int32, (GROUP, TILE), 0)
                            + (start + group * GROUP)
                        ) == lax.broadcasted_iota(jnp.int32, (GROUP, TILE), 1)
                        square_dist = jnp.where(itself, 1.0, square_dist)
                    first_term, second_term = pair_terms(square_dist, own_damp[index] * rows[3])
                    if entry == 0:
                        first_term = jnp.where(itself, 0.0, first_term)
                        second_term = jnp.where(itself, 0.0, second_term)
                    place = step_rows(step, size, entry * PAIR_ROWS + group * GROUP)
                    first_buffer[place, :] = first_term
                    second_buffer[place, :] = second_term
                    add_field(sums[index], first_term, second_term, apart, rows[4:])
            for index, group in enumerate(groups):
                for component, value in enumerate(sums[index]):
                    step_sums[wide_rows(start, group, component), :] = value
        start_all(sent(step))

    for place in range(last_tile - first_tile):
        finish_sums(field, sums_ref, first_tile, place)
    result = pltpu.make_async_copy(field, field_ref, semaphore.at[1, 2])
    result.start()

    @pl.loop(0, steps)
    def _(step):
        wait_all(sent(step))

    keep.wait()
    result.wait()


def pair_second_body(
    tile_count,
    spans,
    lists_ref,
    near_ref,
    up_ref,
    stack_ref,
    down_ref,
    first_ref,
    second_ref,
    field_ref,
    near,
    near_moment,
    picked,
    picked_moment,
    wide,
    sums_ref,
    field,
    first_buffer,
    second_buffer,
    semaphore,
    busy,
):
    terms = (first_ref, second_ref)
    buffers = (first_buffer, second_buffer)
    parts = TILE // PAIR_ROWS
    steps = tile_count * parts

    entries = lists_ref.shape[1]
    size = entries * PAIR_ROWS

    def fetched(step):
        return term_copies(terms, buffers, busy, 0, step, size, True)

    places = pltpu.make_async_copy(near_ref, near, semaphore.at[1, 3])
    places.start()
    copies = near_copies((up_ref, stack_ref, down_ref), near_moment, semaphore.at[2])
    start_all(copies)

    @pl.loop(0, steps)
    def _(step):
        start_all(fetched(step))

    places.wait()
    for tile in range(tile_count):
        widen_own(near, 3, tile_count, tile, tile, wide)
        own = near.shape[0] // 9 * 4 + 2 * tile_count + tile
        origin = near[own : own + 1, 0:1]
        pick_rows(picked, near, lists_ref, tile, tile, tile_count, 3, origin, spans[2])
    wait_all(copies)
    for tile in range(tile_count):
        pick_rows(
            picked_moment, near_moment, lists_ref, tile, tile, tile_count, 3 * RHS, None, None
        )

    @pl.loop(0, steps)
    def _(step):
        wait_all(fetched(step))
        tile = lax.div(step, parts)
        start = lax.rem(step, parts) * PAIR_ROWS
        step_picked = picked.at[tile_rows(tile, entries * 3 * GROUP), :]
        step_moment = picked_moment.at[tile_rows(tile, entries * 3 * RHS * GROUP), :]
        step_wide = wide.at[tile_rows(tile, 3 * TILE), :]
        step_sums = sums_ref.at[tile_rows(tile, 3 * RHS * TILE), :]
        for pair in range(PAIR_ROWS // GROUP // SHARED):
            groups = range(pair * SHARED, (pair + 1) * SHARED)
            own = [
                [step_wide[wide_rows(start, group, dim), :] for dim in range(3)] for group in groups
            ]
            sums = [
                [jnp.zeros((GROUP, TILE), jnp.float32) for _ in range(3 * RHS)] for _ in groups
            ]
            for entry in range(entries):
                first = entry * 3 * GROUP
                rows = [
                    step_picked[first + dim * GROUP : first + (dim + 1) * GROUP, :]
                    for dim in range(3)
                ]
                first = first * RHS
                moments = [
                    step_moment[first + index * GROUP : first + (index + 1) * GROUP, :]
                    for index in range(3 * RHS)
                ]
                for index, group in enumerate(groups):
                    apart = [rows[dim] - own[index][dim] for dim in range(3)]
                    place = step_rows(step, size, entry * PAIR_ROWS + group * GROUP)
                    add_field(
                        sums[index], first_buffer[place, :], second_buffer[place, :], apart, moments
                    )
            for index, group in enumerate(groups):
                for component, value in enumerate(sums[index]):
                    step_sums[wide_rows(start, group, component), :] = value

    for place in range(tile_count):
        finish_sums(field, sums_ref, 0, place)
    result = pltpu.make_async_copy(field, field_ref, semaphore.at[1, 2])
    result.start()
    result.wait()


def shift(source, axis, step):
    count = lax.axis_size(axis)
    return lax.ppermute(source, axis, [(i, (i + step) % count) for i in range(count)])


def both_ways(source, axis):
    return shift(source, axis, 1), source, shift(source, axis, -1)


def whole(shape):
    return pl.BlockSpec(shape, lambda *_: (0,) * len(shape))


def anywhere():
    return pl.BlockSpec(memory_space=pl.ANY)


def join(message, payload):
    left, _, right = both_ways(payload, "col")
    message, left, right = lax.optimization_barrier((message, left, right))
    return message, both_ways(jnp.concatenate([left, payload, right], axis=0), "row")


def piece_count(shape, dtype):
    size = math.prod(shape) * jnp.dtype(dtype).itemsize
    if len(shape) != 2:
        return 1
    count = max(1, min(8, size // 49152))
    while count > 1 and shape[0] % (count * 16 if dtype == jnp.bfloat16 else count * 8):
        count -= 1
    return count


class Moved:
    def __init__(self, here, far, semaphores, inward):
        rows = here.shape[0] // len(semaphores)
        self.copies = []
        for index, semaphore in enumerate(semaphores):
            ends = (far, here)
            if len(semaphores) > 1:
                place = pl.ds(index * rows, rows)
                ends = (far.at[place, :], here.at[place, :])
            ends = ends if inward else ends[::-1]
            self.copies.append(pltpu.make_async_copy(*ends, semaphore))
        self.here = here
        self.shape = here.shape
        self.inward = inward
        self.started = False
        self.waiting = False
        if inward:
            self.send()

    def send(self):
        if not self.started:
            start_all(self.copies)
            self.started = self.waiting = True

    def wait(self):
        if self.waiting:
            wait_all(self.copies)
            self.waiting = False

    def __getitem__(self, index):
        if self.inward:
            self.wait()
        return self.here[index]

    def __setitem__(self, index, value):
        self.here[index] = value


def call(body, outs, *operands, after=(), own_block=None):
    kinds = [
        (operand.shape[1:] if index == own_block else operand.shape, operand.dtype)
        for index, operand in enumerate(operands)
    ] + list(outs)
    counts = [piece_count(*kind) for kind in kinds]
    firsts = [sum(counts[:index]) for index in range(len(counts))]

    def run(*refs):
        refs = refs[len(after) :]
        far, here, semaphore = refs[: len(kinds)], refs[len(kinds) : -1], refs[-1]
        moved = []
        for index in range(len(kinds)):
            source = far[index]
            if index == own_block:
                place = lax.axis_index("row") * lax.axis_size("col") + lax.axis_index("col")
                source = source.at[place]
            semaphores = [semaphore.at[firsts[index] + piece] for piece in range(counts[index])]
            moved.append(Moved(here[index], source, semaphores, index < len(operands)))
        body(*moved)
        for value in moved[len(operands) :]:
            value.send()
        for value in moved:
            value.wait()

    return pl.pallas_call(
        run,
        in_specs=[anywhere()] * (len(after) + len(operands)),
        out_specs=[anywhere()] * len(outs),
        out_shape=[jax.ShapeDtypeStruct(shape, dtype) for shape, dtype in outs],
        scratch_shapes=[pltpu.VMEM(shape, dtype) for shape, dtype in kinds]
        + [pltpu.SemaphoreType.DMA((sum(counts),))],
        compiler_params=pltpu.CompilerParams(vmem_limit_bytes=VMEM_LIMIT),
        cost_estimate=pl.CostEstimate(
            flops=200_000_000, bytes_accessed=4 << 20, transcendentals=0
        ),
    )(*after, *operands)


def final_call(body, outs, *operands):
    return pl.pallas_call(
        body,
        grid=(1,),
        in_specs=[whole(operand.shape) for operand in operands],
        out_specs=[whole(shape) for shape, _ in outs],
        out_shape=[jax.ShapeDtypeStruct(shape, dtype) for shape, dtype in outs],
        compiler_params=pltpu.CompilerParams(vmem_limit_bytes=SMALL_VMEM_LIMIT),
    )(*operands)


def pair_call(body, outs, scratch, lists, *operands, tiles, aliased=0):
    buffers = (tiles * lists.shape[1] * TILE, TILE)
    first = 1 + len(operands) - aliased
    return pl.pallas_call(
        body,
        in_specs=[pl.BlockSpec(memory_space=pltpu.SMEM)] + [anywhere()] * len(operands),
        out_specs=[anywhere()] * len(outs),
        out_shape=[jax.ShapeDtypeStruct(shape, jnp.float32) for shape in outs],
        scratch_shapes=[pltpu.VMEM(shape, jnp.float32) for shape in scratch + [buffers] * 2]
        + [
            pltpu.SemaphoreType.DMA((3, 4)),
            pltpu.SemaphoreType.DMA((2, tiles * TILE // PAIR_ROWS)),
        ],
        input_output_aliases={first + index: index for index in range(aliased)},
        compiler_params=pltpu.CompilerParams(vmem_limit_bytes=VMEM_LIMIT),
        cost_estimate=pl.CostEstimate(
            flops=80_000_000, bytes_accessed=8 << 20, transcendentals=1 << 21
        ),
    )(lists, *operands)


def exchange(message, devices):
    shape = message.shape
    sent = message.reshape(devices, 1, -1)
    return lax.all_to_all(sent, ("row", "col"), split_axis=0, concat_axis=0, tiled=True).reshape(
        shape
    )


def slab_local(field_rhs, positions, polar, grid_base, tile_lists):
    rows_count = lax.axis_size("row")
    cols_count = lax.axis_size("col")
    counts = (rows_count, cols_count)
    devices = rows_count * cols_count
    lengths = (CX * rows_count, CY * cols_count, KZ)
    spans = tuple(float(length) for length in lengths)
    atoms = polar.shape[-1]
    tile_count = atoms // TILE
    listed = tile_lists.shape[-1]
    tables = slab_tables(rows_count, cols_count)
    f32 = jnp.float32
    rhs = jnp.swapaxes(field_rhs[0, 0], 0, 1)
    place = jnp.swapaxes(positions[0], 0, 1)
    base = jnp.swapaxes(grid_base[0], 0, 1)
    polar = polar.reshape(1, atoms)
    lists = tile_lists[0, 0]
    quantities = 4 + 3 * RHS
    brick_rows = quantities * tile_count
    moment_rows = 3 * RHS * tile_count
    message_shape = (devices * X_PAD, KZ // devices * RHS * Y_PAD)
    last_shape = (devices * (X_PAD + 1), message_shape[1])
    row_shape = (3 * RHS, atoms)

    start, payload = call(pack_body, [(row_shape, f32), ((brick_rows, TILE), f32)], rhs, place, polar)

    def setup(*refs):
        setup_body(lengths, devices, *refs)

    message, splines, depth_high, depth_low = call(
        setup,
        [
            (message_shape, f32),
            ((2 * SLOT_ROWS + 2 * Y_PAD, atoms), f32),
            ((KZ, 2 * atoms), jnp.bfloat16),
            ((KZ, 2 * atoms), jnp.bfloat16),
        ],
        place,
        base,
        start,
        *[jnp.asarray(table) for table in tables["along_z"]],
    )
    constants = (
        jnp.asarray(tables["kernel"]),
        jnp.asarray(tables["forward_x"]),
        jnp.asarray(tables["backward_x"]),
        *[jnp.asarray(table) for table in tables["block"]],
    )
    message, near = join(message, payload)
    arrived = exchange(message, devices)

    def pair_first(first_tile, last_tile, fields, *after):
        def body(*refs):
            pair_first_body(first_tile, last_tile, tile_count, spans, *refs)

        tiles = last_tile - first_tile
        return pair_call(
            body,
            [(tile_count * listed * TILE, TILE)] * 2
            + [(last_tile * GROUP, TILE), (9 * 3 * tile_count, TILE)],
            [
                (9 * brick_rows, TILE),
                (tiles * listed * quantities * GROUP, TILE),
                (tiles * 4 * TILE, TILE),
                (tiles * 3 * RHS * TILE, TILE),
                (9 * 3 * tile_count, TILE),
                (last_tile * GROUP, TILE),
            ],
            lists,
            *near,
            *fields,
            *after,
            tiles=tiles,
            aliased=2 if first_tile > 0 else 0,
        )

    early = pair_first(0, EARLY_TILES, (), message)

    def middle_first(*refs):
        middle_first_body(counts, *refs)

    mixed, wave = call(
        middle_first,
        [(message_shape, f32), (tables["kernel"].shape[1:], f32)],
        arrived,
        *constants,
        after=(early[2],),
        own_block=1,
    )
    returned = exchange(mixed, devices)
    first_term, second_term, direct, near = pair_first(
        EARLY_TILES, tile_count, (early[2],), wave, *early[:2]
    )

    def sample(*refs):
        sample_body(devices, *refs)

    image, second, moments = call(
        sample,
        [(row_shape, f32), (row_shape, f32), ((moment_rows, TILE), f32)],
        returned,
        splines,
        depth_high,
        depth_low,
        start,
        direct,
        polar,
    )

    def spread(*refs):
        spread_body(devices, *refs)

    (message,) = call(spread, [(message_shape, f32)], splines, depth_high, depth_low, second)
    message, near_moments = join(message, moments)
    arrived = exchange(message, devices)

    def pair_second(*refs):
        pair_second_body(tile_count, spans, *refs)

    (direct,) = pair_call(
        pair_second,
        [(tile_count * GROUP, TILE)],
        [
            (9 * 3 * tile_count, TILE),
            (9 * moment_rows, TILE),
            (tile_count * listed * 3 * GROUP, TILE),
            (tile_count * listed * 3 * RHS * GROUP, TILE),
            (tile_count * 3 * TILE, TILE),
            (tile_count * 3 * RHS * TILE, TILE),
            (tile_count * GROUP, TILE),
        ],
        lists,
        near,
        *near_moments,
        first_term,
        second_term,
        tiles=tile_count,
    )

    def middle_second(*refs):
        middle_second_body(counts, *refs)

    (mixed,) = call(
        middle_second,
        [(last_shape, f32)],
        arrived,
        *constants,
        wave,
        rhs,
        start,
        image,
        second,
        direct,
        polar,
        own_block=1,
    )
    returned = exchange(mixed, devices)

    def final(*refs):
        final_body(devices, *refs)

    outs = final_call(
        final,
        [(rhs.shape, f32), (rhs.shape, f32)],
        returned,
        splines,
        depth_high,
        depth_low,
        rhs,
        start,
        image,
        second,
        direct,
        polar,
    )
    return tuple(jnp.swapaxes(out, 0, 1)[None, None] for out in outs)


def solution(mesh):
    placed = (
        P("row", "col", None, None, None),
        P("row", "col", None, None),
        P("row", "col", None),
        P("row", "col", None, None),
        P("row", "col", None, None),
    )
    devices = mesh.shape["row"] * mesh.shape["col"]
    return jax.shard_map(
        slab_local if KZ % devices == 0 else pencil_local,
        mesh=mesh,
        in_specs=placed,
        out_specs=(P("row", "col", None, None, None), P("row", "col", None, None, None)),
        check_vma=False,
    )
```

```python
import math

import jax
import jax.numpy as jnp
import ml_dtypes
import numpy as np
from jax import lax
from jax.experimental import pallas as pl
from jax.experimental.pallas import tpu as pltpu
from jax.sharding import PartitionSpec as P

CX = 8
CY = 4
KZ = 256
TILE = 128
RHS = 2
ITERS = 2


ewald_beta = 0.4
thole_a = 0.39
self_coef = 4.0 * ewald_beta**3 / (3.0 * math.sqrt(math.pi))
highest = lax.Precision.HIGHEST


def with_halo(cells, sides, width):
    for axis, dim in sides:
        count = lax.axis_size(axis)
        head = lax.slice_in_dim(cells, 0, width, axis=dim)
        tail = lax.slice_in_dim(cells, cells.shape[dim] - width, cells.shape[dim], axis=dim)
        cells = jnp.concatenate(
            [
                lax.ppermute(tail, axis, [(i, (i + 1) % count) for i in range(count)]),
                cells,
                lax.ppermute(head, axis, [((i + 1) % count, i) for i in range(count)]),
            ],
            axis=dim,
        )
    return cells


def spline_table(fraction):
    previous = {0: jnp.ones_like(fraction)}
    fourth = previous
    for degree in range(2, 6):
        current = {}
        for offset in range(degree):
            abscissa = fraction + offset
            summed = abscissa * previous.get(offset, 0.0) + (degree - abscissa) * previous.get(
                offset - 1, 0.0
            )
            current[offset] = summed / (degree - 1)
        if degree == 4:
            fourth = current
        previous = current
    values = jnp.stack([previous[4 - stencil] for stencil in range(5)])
    slopes = jnp.stack(
        [fourth.get(4 - stencil, 0.0) - fourth.get(3 - stencil, 0.0) for stencil in range(5)]
    )
    return (values, slopes)


def spline_modulus(wave_index, length):
    spline_coef = (1.0 / 24.0, 11.0 / 24.0, 11.0 / 24.0, 1.0 / 24.0)
    cosine_sum = jnp.zeros(wave_index.shape, jnp.float32)
    sine_sum = jnp.zeros(wave_index.shape, jnp.float32)
    for offset in range(4):
        angles = 2.0 * math.pi / length * (wave_index * offset % length).astype(jnp.float32)
        cosine_sum = cosine_sum + spline_coef[offset] * jnp.cos(angles)
        sine_sum = sine_sum + spline_coef[offset] * jnp.sin(angles)
    return cosine_sum * cosine_sum + sine_sum * sine_sum


def folded_square(wave_index, length):
    nearest = jnp.minimum(wave_index, length - wave_index).astype(jnp.float32) / length
    return nearest * nearest


def influence(wave_x, wave_y, wave_z, length_x, length_y, length_z):
    wave_norm = (
        folded_square(wave_x, length_x)
        + folded_square(wave_y, length_y)
        + folded_square(wave_z, length_z)
    )
    modulus = (
        spline_modulus(wave_x, length_x)
        * spline_modulus(wave_y, length_y)
        * spline_modulus(wave_z, length_z)
    )
    excluded = (wave_x * 2 == length_x) | (wave_y * 2 == length_y) | (wave_z * 2 == length_z)
    excluded = excluded | (wave_x == 0) & (wave_y == 0) & (wave_z == 0)
    safe_norm = jnp.where(excluded, 1.0, wave_norm)
    safe_modulus = jnp.where(excluded, 1.0, modulus)
    result = jnp.exp(-(math.pi**2 / ewald_beta**2) * safe_norm) / (
        math.pi * safe_norm * safe_modulus
    )
    return jnp.where(excluded, 0.0, result)


def tile_field(own_static, near_static, near_dipole, box_spans):
    listed_count = near_static.shape[0]
    tile_width = own_static.shape[1]
    box_span = jnp.array(box_spans, dtype=jnp.float32)[None, :, None, None]
    separation = near_static[:, 0:3, None, :] - own_static[None, 0:3, :, None]
    separation = separation - box_span * jnp.floor(separation / box_span + 0.5)
    dist_sq = jnp.sum(separation * separation, axis=1)
    itself = (jnp.arange(listed_count)[:, None, None] == 0) & (
        jnp.arange(tile_width)[:, None] == jnp.arange(tile_width)[None, :]
    )[None]
    safe_sq = jnp.where(itself, 1.0, dist_sq)
    distance = jnp.sqrt(safe_sq)
    scaled = distance / (own_static[3][None, :, None] * near_static[:, 3][:, None, :])
    cubed = thole_a * scaled * scaled * scaled
    damping = jnp.exp(-cubed)
    screen = lax.erfc(ewald_beta * distance)
    gaussian = 2.0 * ewald_beta / math.sqrt(math.pi) * jnp.exp(-(ewald_beta * ewald_beta) * safe_sq)
    inverse_sq = 1.0 / safe_sq
    inverse_cube = inverse_sq / distance
    first_term = (screen - damping) * inverse_cube + gaussian * inverse_sq
    second = (
        3.0 * (screen - (1.0 + cubed) * damping) * inverse_cube * inverse_sq
        + gaussian * (2.0 * ewald_beta * ewald_beta + 3.0 * inverse_sq) * inverse_sq
    )
    first_term = jnp.where(itself, 0.0, first_term)
    second = jnp.where(itself, 0.0, second)
    projected = jnp.sum(near_dipole[:, :, :, None, :] * separation[:, None, :, :, :], axis=2)
    weighted = second[:, None] * projected
    outward = jnp.sum(weighted[:, :, None] * separation[:, None], axis=(0, 4))
    inward = jnp.sum(first_term[:, None, None] * near_dipole[:, :, :, None, :], axis=(0, 4))
    return outward - inward


def hartley(length):
    counter = jnp.arange(length, dtype=jnp.int32)
    angles = (
        2.0 * math.pi / length * (counter[:, None] * counter[None, :] % length).astype(jnp.float32)
    )
    return jnp.cos(angles) + jnp.sin(angles)


def placed_table(first_cell, weights, extent):
    slot_index = jnp.arange(extent, dtype=jnp.int32)[:, None]
    placed = jnp.zeros((extent, first_cell.shape[0]), jnp.float32)
    for stencil in range(5):
        placed = placed + jnp.where(
            slot_index == (first_cell[None, :] + stencil) % extent, weights[stencil][None, :], 0.0
        )
    return placed


def pad_axis(source, axis_pos, leading, trailing):
    widths = [(0, 0)] * source.ndim
    widths[axis_pos] = (leading, trailing)
    return jnp.pad(source, widths)


def fold_cycle(cycle_only, axis_pos, inner_len):
    middle = lax.slice_in_dim(cycle_only, 4, inner_len + 4, axis=axis_pos)
    lower_cycle = lax.slice_in_dim(cycle_only, 0, 2, axis=axis_pos)
    upper_cycle = lax.slice_in_dim(cycle_only, inner_len + 6, inner_len + 8, axis=axis_pos)
    return (
        middle
        + pad_axis(lower_cycle, axis_pos, 0, inner_len - 2)
        + pad_axis(upper_cycle, axis_pos, inner_len - 2, 0)
    )


def clear_inside(extended, extents):
    inside = None
    for axis_pos, inner_len in extents:
        slot_index = lax.broadcasted_iota(jnp.int32, extended.shape, axis_pos)
        within = (slot_index >= 2) & (slot_index < inner_len + 6)
        inside = within if inside is None else inside & within
    return jnp.where(inside, 0.0, extended)


def inner_sum(left_arr, right_arr):
    return lax.psum(jnp.sum(left_arr * right_arr, axis=(1, 2)), ("row", "col"))


def pencil_local(field_rhs, positions, polar, grid_base, tile_lists):
    rows_count = lax.axis_size("row")
    cols_count = lax.axis_size("col")
    grid_x = CX * rows_count
    grid_y = CY * cols_count
    atom_count = polar.shape[-1]
    tile_count = atom_count // TILE
    slab_depth = KZ // tile_count
    window_len = slab_depth + 4
    box_spans = (float(grid_x), float(grid_y), float(KZ))
    own_place = positions[0, 0]
    own_base = grid_base[0, 0]
    own_polar = polar[0, 0]
    lengths = jnp.array([grid_x, grid_y, KZ], dtype=jnp.int32)[:, None]
    cell_index = (own_base + 2) % lengths
    fraction = own_place - cell_index.astype(jnp.float32)
    values, slopes = spline_table(fraction)
    first_x = (own_base[0] - lax.axis_index("row") * CX + 2) % grid_x
    first_y = (own_base[1] - lax.axis_index("col") * CY + 2) % grid_y
    rows_x = placed_table(first_x, values[:, 0], CX + 4)
    slope_x = placed_table(first_x, slopes[:, 0], CX + 4)
    rows_y = placed_table(first_y, values[:, 1], CY + 4)
    slope_y = placed_table(first_y, slopes[:, 1], CY + 4)
    tile_start = jnp.arange(atom_count, dtype=jnp.int32) // TILE * slab_depth
    first_z = (own_base[2] + 2 - tile_start) % KZ
    rows_z = placed_table(first_z, values[:, 2], window_len)
    slope_z = placed_table(first_z, slopes[:, 2], window_len)
    plane_count = (CX + 4) * (CY + 4)
    plane_dx = (slope_x[:, None, :] * rows_y[None, :, :]).reshape(plane_count, atom_count)
    plane_dy = (rows_x[:, None, :] * slope_y[None, :, :]).reshape(plane_count, atom_count)
    plane_flat = (rows_x[:, None, :] * rows_y[None, :, :]).reshape(plane_count, atom_count)
    window_rows = jnp.moveaxis(rows_z.reshape(window_len, tile_count, TILE), 1, 0)
    window_slope = jnp.moveaxis(slope_z.reshape(window_len, tile_count, TILE), 1, 0)
    depth_table = jnp.concatenate([window_rows, window_slope], axis=2)
    grid_scale = 1.0 / (grid_x * grid_y * KZ)
    hartley_x = hartley(grid_x)
    hartley_y = hartley(grid_y)
    hartley_z = hartley(KZ)
    block_y = grid_y // rows_count
    block_z = KZ // cols_count
    wave_x = jnp.arange(grid_x, dtype=jnp.int32)[:, None, None]
    wave_y = (lax.axis_index("row") * block_y + jnp.arange(block_y, dtype=jnp.int32))[None, :, None]
    wave_z = (lax.axis_index("col") * block_z + jnp.arange(block_z, dtype=jnp.int32))[None, None, :]
    kernel = influence(wave_x, wave_y, wave_z, grid_x, grid_y, KZ) * grid_scale
    root_scale = jnp.power(own_polar, 1.0 / 6.0)
    own_static = jnp.concatenate([own_place, root_scale[None]], axis=0)
    near_static = with_halo(own_static[None, None], (("row", 0), ("col", 1)), 1)
    near_static = jnp.moveaxis(near_static.reshape(9, 4, tile_count, TILE), 2, 1).reshape(
        9 * tile_count, 4, TILE
    )
    own_tiles = jnp.moveaxis(own_static.reshape(4, tile_count, TILE), 1, 0)
    own_lists = tile_lists[0, 0]
    polar_wide = own_polar[None, None, :]
    solution = jnp.zeros_like(field_rhs[0, 0])
    residual = field_rhs[0, 0]
    scaled_res = polar_wide * residual
    direction = scaled_res
    progress = inner_sum(residual, scaled_res)
    for iteration in range(ITERS):
        near_dip = with_halo(direction[None, None], (("row", 0), ("col", 1)), 1)
        near_dip = jnp.moveaxis(near_dip.reshape(9, RHS, 3, tile_count, TILE), 3, 1).reshape(
            9 * tile_count, RHS, 3, TILE
        )

        def one_tile(tile_pos):
            picked = own_lists[tile_pos]
            return tile_field(own_tiles[tile_pos], near_static[picked], near_dip[picked], box_spans)

        fields = lax.map(one_tile, jnp.arange(tile_count, dtype=jnp.int32))
        direct = jnp.moveaxis(fields, 0, 2).reshape(RHS, 3, atom_count)
        slope_terms = (
            direction[:, 0, None, :] * plane_dx[None] + direction[:, 1, None, :] * plane_dy[None]
        )
        flat_terms = direction[:, 2, None, :] * plane_flat[None]
        spread_left = jnp.concatenate(
            [
                slope_terms.reshape(RHS, plane_count, tile_count, TILE),
                flat_terms.reshape(RHS, plane_count, tile_count, TILE),
            ],
            axis=3,
        )
        spread_windows = jnp.einsum("sptb,twb->sptw", spread_left, depth_table, precision=highest)
        main_part = spread_windows[..., :slab_depth].reshape(spread_windows.shape[:-2] + (KZ,))
        tail_part = pad_axis(
            spread_windows[..., slab_depth:], spread_windows.ndim - 1, 0, slab_depth - 4
        )
        tail_part = tail_part.reshape(spread_windows.shape[:-2] + (KZ,))[..., : KZ + 4 - slab_depth]
        last_axis = main_part.ndim - 1
        padded_line = pad_axis(main_part, last_axis, 0, 4) + pad_axis(
            tail_part, last_axis, slab_depth, 0
        )
        inner = padded_line[..., 2 : KZ + 2]
        spread_tile = (
            inner
            + pad_axis(padded_line[..., 0:2], last_axis, KZ - 2, 0)
            + pad_axis(padded_line[..., KZ + 2 : KZ + 4], last_axis, 0, KZ - 2)
        ).reshape(RHS, CX + 4, CY + 4, KZ)
        extended = with_halo(spread_tile, (("row", 1), ("col", 2)), 2)
        cycle_only = clear_inside(extended, ((1, CX), (2, CY)))
        folded = fold_cycle(fold_cycle(cycle_only, 1, CX), 2, CY)
        spectrum = jnp.einsum(
            "sxyz,zk->sxyk",
            spread_tile[:, 2 : CX + 2, 2 : CY + 2] + folded,
            hartley_z,
            precision=highest,
        )
        along_y = jnp.einsum(
            "sxyz,yk->sxkz",
            lax.all_to_all(spectrum, "col", split_axis=3, concat_axis=2, tiled=True),
            hartley_y,
            precision=highest,
        )
        along_x = (
            jnp.einsum(
                "sxyz,xk->skyz",
                lax.all_to_all(along_y, "row", split_axis=2, concat_axis=1, tiled=True),
                hartley_x,
                precision=highest,
            )
            * kernel[None]
        )
        mixed_part = jnp.einsum("sxyz,xk->skyz", along_x, hartley_x, precision=highest)
        returned = lax.all_to_all(mixed_part, "row", split_axis=1, concat_axis=2, tiled=True)
        swapped = jnp.einsum("sxyz,yk->sxkz", returned, hartley_y, precision=highest)
        restored = lax.all_to_all(swapped, "col", split_axis=2, concat_axis=3, tiled=True)
        padded = with_halo(
            jnp.einsum("sxyz,zk->sxyk", restored, hartley_z, precision=highest),
            (("row", 1), ("col", 2)),
            2,
        )
        line = padded.reshape(RHS, plane_count, KZ)
        extended_line = jnp.concatenate([line[..., KZ - 2 :], line, line[..., :2]], axis=-1)
        windows = jnp.stack(
            [
                extended_line[..., tile * slab_depth : tile * slab_depth + window_len]
                for tile in range(tile_count)
            ],
            axis=-2,
        )
        sampled = jnp.einsum("sptw,twb->sptb", windows, depth_table, precision=highest)
        with_flat = sampled[..., :TILE].reshape(RHS, plane_count, atom_count)
        with_slope = sampled[..., TILE:].reshape(RHS, plane_count, atom_count)
        recip_part = jnp.stack(
            [
                jnp.sum(with_flat * plane_dx[None], axis=1),
                jnp.sum(with_flat * plane_dy[None], axis=1),
                jnp.sum(with_slope * plane_flat[None], axis=1),
            ],
            axis=1,
        )
        image_field = direction / polar_wide - direct + recip_part - self_coef * direction
        step_size = (progress / inner_sum(direction, image_field))[:, None, None]
        solution = solution + step_size * direction
        residual = residual - step_size * image_field
        scaled_res = polar_wide * residual
        progress_next = inner_sum(residual, scaled_res)
        direction = scaled_res + (progress_next / progress)[:, None, None] * direction
        progress = progress_next
    return (solution[None, None], residual[None, None])


X_PAD = CX + 4
Y_PAD = CY + 4
SLOT_ROWS = 16
SPLIT = 2
VMEM_LIMIT = 60_000_000
SMALL_VMEM_LIMIT = 24_000_000
EARLY_TILES = 1
PAIR_ROWS = 32
GROUP = 8
SCREEN_SCALE = 0.4
SCREEN_COEF = (
    0.22567588090896606,
    0.2256690263748169,
    0.20785020291805267,
    0.16849851608276367,
    0.14156343042850494,
    -0.005832736846059561,
    0.16930203139781952,
    -0.1830107867717743,
    0.05028456076979637,
)


def halves(value):
    high = value.astype(jnp.bfloat16)
    return high, (value - high.astype(jnp.float32)).astype(jnp.bfloat16)


def halves_np(value):
    value = value.astype(np.float32)
    high = value.astype(ml_dtypes.bfloat16)
    return high, (value - high.astype(np.float32)).astype(ml_dtypes.bfloat16)


def product(left, right, left_dim=1, right_dim=0):
    def one(first, second):
        return lax.dot_general(
            first,
            second,
            (((left_dim,), (right_dim,)), ((), ())),
            preferred_element_type=jnp.float32,
        )

    return one(left[0], right[0]) + (one(left[1], right[0]) + one(left[0], right[1]))


def cas_np(wave, place, length):
    angles = 2.0 * np.pi / length * (wave[:, None] * place[None, :] % length)
    return np.cos(angles) + np.sin(angles)


def modulus_np(wave, length):
    coef = np.array([1.0, 11.0, 11.0, 1.0]) / 24.0
    angles = 2.0 * np.pi / length * (wave[:, None] * np.arange(4)[None, :])
    return (coef * np.cos(angles)).sum(1) ** 2 + (coef * np.sin(angles)).sum(1) ** 2


def influence_np(length_x, length_y, length_z):
    total = np.zeros((length_x, length_y, length_z))
    modulus = np.ones((length_x, length_y, length_z))
    excluded = np.zeros((length_x, length_y, length_z), bool)
    for axis, length in enumerate((length_x, length_y, length_z)):
        wave = np.arange(length)
        shape = [1, 1, 1]
        shape[axis] = length
        total = total + ((np.minimum(wave, length - wave) / length) ** 2).reshape(shape)
        modulus = modulus * modulus_np(wave, length).reshape(shape)
        excluded = excluded | (wave * 2 == length).reshape(shape)
    excluded[0, 0, 0] = True
    safe = np.where(excluded, 1.0, total)
    result = np.exp(-(np.pi**2) / ewald_beta**2 * safe) / (
        np.pi * safe * np.where(excluded, 1.0, modulus)
    )
    return np.where(excluded, 0.0, result) / (length_x * length_y * length_z)


def slab_tables(rows_count, cols_count):
    grid_x = CX * rows_count
    grid_y = CY * cols_count
    devices = rows_count * cols_count
    chunk = KZ // devices
    wave_z = (np.arange(devices)[None, :] * chunk + np.arange(chunk)[:, None]).reshape(-1)
    along_z = cas_np(wave_z, np.arange(KZ), KZ)
    place_x = np.arange(rows_count)[:, None] * CX + np.arange(X_PAD)[None, :] - 2
    along_x = cas_np(np.arange(grid_x), place_x.reshape(-1) % grid_x, grid_x)
    x_high, x_low = halves_np(along_x)
    forward_x = np.concatenate([x_high, x_low, x_high], axis=1)
    backward_x = np.concatenate([x_high.T, x_low.T, x_high.T], axis=1)
    place_y = (np.arange(cols_count)[:, None] * CY + np.arange(Y_PAD)[None, :] - 2) % grid_y
    along_y = cas_np(np.arange(grid_y), place_y.reshape(-1), grid_y)
    along_y = along_y.reshape(grid_y, cols_count, Y_PAD)
    units = chunk * RHS // SPLIT
    block = np.einsum("uv,kcy->cuyvk", np.eye(units), along_y)
    block = block.reshape(cols_count * units * Y_PAD, units * grid_y)
    kernel = influence_np(grid_x, grid_y, KZ).reshape(grid_x, grid_y, devices, chunk)
    kernel = np.transpose(kernel, (2, 0, 3, 1))[:, :, :, None, :]
    kernel = np.broadcast_to(kernel, (devices, grid_x, chunk, RHS, grid_y))
    kernel = kernel.reshape(devices, grid_x, SPLIT, units * grid_y)
    kernel = np.moveaxis(kernel, 2, 1).reshape(devices, SPLIT * grid_x, units * grid_y)
    kernel = kernel.astype(np.float32)
    return dict(
        along_z=halves_np(along_z),
        forward_x=forward_x,
        backward_x=backward_x,
        block=halves_np(block),
        kernel=kernel,
    )


def pack_body(rhs_far, place_far, polar_far, payload_ref, rhs_ref, place_ref, polar_ref, semaphore):
    copies = [
        pltpu.make_async_copy(far, here, semaphore.at[index])
        for index, (far, here) in enumerate(
            ((rhs_far, rhs_ref), (place_far, place_ref), (polar_far, polar_ref))
        )
    ]
    start_all(copies)
    wait_all(copies)
    polar = polar_ref[...]
    start = read_rows(rhs_ref) * polar
    place = [place_ref[dim] for dim in range(3)]
    everything = jnp.concatenate(place + [1.0 / jnp.sqrt(polar), start], axis=0)
    store_payload(payload_ref, everything)


def read_rows(rows_ref):
    return jnp.concatenate([rows_ref[dim] for dim in range(3)], axis=0)


def store_payload(payload_ref, everything):
    tile_count = everything.shape[1] // TILE
    for quantity in range(everything.shape[0]):
        for tile in range(tile_count):
            row = quantity * tile_count + tile
            payload_ref[row : row + 1, :] = everything[
                quantity : quantity + 1, tile * TILE : (tile + 1) * TILE
            ]


def placed_rows(slot, weights, extent):
    slot_index = lax.broadcasted_iota(jnp.int32, (extent, slot.shape[1]), 0)
    placed = jnp.zeros((extent, slot.shape[1]), jnp.float32)
    for stencil in range(5):
        target = slot + stencil
        if extent == KZ:
            target = jnp.where(target >= KZ, target - KZ, target)
        placed = placed + jnp.where(slot_index == target, weights[stencil], 0.0)
    return placed


def spread_into(message_ref, moment, rows_x, slope_x, rows_y, slope_y, depth, devices):
    blocks = []
    for step in range(X_PAD):
        flat_x = rows_x[step : step + 1]
        tilt_x = slope_x[step : step + 1]
        for rhs in range(RHS):
            part_x = tilt_x * moment[rhs : rhs + 1]
            part_y = flat_x * moment[RHS + rhs : RHS + rhs + 1]
            part_z = flat_x * moment[2 * RHS + rhs : 2 * RHS + rhs + 1]
            blocks.append(
                jnp.concatenate([part_x * rows_y + part_y * slope_y, part_z * rows_y], axis=1)
            )
    charges = jnp.concatenate(blocks, axis=0)
    spectrum = product(depth, halves(charges), 1, 1)
    slot_rows = message_ref.shape[0] // devices
    chunk = KZ // devices
    width = RHS * Y_PAD
    for step in range(X_PAD):
        message_ref[pl.ds(step, devices, stride=slot_rows), :] = jnp.concatenate(
            [
                spectrum[unit * devices : (unit + 1) * devices, step * width : (step + 1) * width]
                for unit in range(chunk)
            ],
            axis=1,
        )


def sample_from(message_ref, rows_x, slope_x, rows_y, slope_y, depth, devices):
    chunk = KZ // devices
    width = RHS * Y_PAD
    slot_rows = message_ref.shape[0] // devices
    pieces = [
        message_ref[pl.ds(step, devices, stride=slot_rows), :] for step in range(X_PAD)
    ]
    spare = jnp.zeros((devices, KZ - X_PAD * width), jnp.float32)
    spectrum = jnp.concatenate(
        [
            jnp.concatenate(
                [piece[:, unit * width : (unit + 1) * width] for piece in pieces] + [spare], axis=1
            )
            for unit in range(chunk)
        ],
        axis=0,
    )
    spectrum = jnp.transpose(spectrum)[: X_PAD * width]
    sampled = product(halves(spectrum), depth, 1, 0)
    atoms = rows_x.shape[1]
    fields = [None] * (3 * RHS)
    for rhs in range(RHS):
        sum_x = sum_y = sum_z = None
        for step in range(X_PAD):
            first = step * width + rhs * Y_PAD
            flat = sampled[first : first + Y_PAD, :atoms]
            tilt = sampled[first : first + Y_PAD, atoms:]
            part_x = slope_x[step : step + 1] * flat
            part_y = rows_x[step : step + 1] * flat
            part_z = rows_x[step : step + 1] * tilt
            sum_x = part_x if sum_x is None else sum_x + part_x
            sum_y = part_y if sum_y is None else sum_y + part_y
            sum_z = part_z if sum_z is None else sum_z + part_z
        fields[rhs] = jnp.sum(sum_x * rows_y, axis=0, keepdims=True)
        fields[RHS + rhs] = jnp.sum(sum_y * slope_y, axis=0, keepdims=True)
        fields[2 * RHS + rhs] = jnp.sum(sum_z * rows_y, axis=0, keepdims=True)
    return jnp.concatenate(fields, axis=0)


def read_tables(tables_ref):
    return (
        tables_ref[0:X_PAD],
        tables_ref[SLOT_ROWS : SLOT_ROWS + X_PAD],
        tables_ref[2 * SLOT_ROWS : 2 * SLOT_ROWS + Y_PAD],
        tables_ref[2 * SLOT_ROWS + Y_PAD : 2 * SLOT_ROWS + 2 * Y_PAD],
    )


def setup_body(
    lengths,
    devices,
    place_ref,
    base_ref,
    rhs_ref,
    polar_ref,
    z_high_ref,
    z_low_ref,
    message_ref,
    tables_ref,
    depth_high_ref,
    depth_low_ref,
    start_ref,
):
    start = read_rows(rhs_ref) * polar_ref[...]
    start_ref[...] = start
    base = [base_ref[dim] for dim in range(3)]
    fractions = []
    cells = []
    for dim in range(3):
        cell = base[dim] + 2
        cell = jnp.where(cell >= lengths[dim], cell - lengths[dim], cell)
        cells.append(cell)
        fractions.append(place_ref[dim] - cell.astype(jnp.float32))
    values, slopes = spline_table(jnp.concatenate(fractions, axis=0))
    values = [[values[stencil][dim : dim + 1] for stencil in range(5)] for dim in range(3)]
    slopes = [[slopes[stencil][dim : dim + 1] for stencil in range(5)] for dim in range(3)]
    slot_x = lax.rem(cells[0], CX)
    slot_y = lax.rem(cells[1], CY)
    tables_ref[0:SLOT_ROWS] = placed_rows(slot_x, values[0], SLOT_ROWS)
    tables_ref[SLOT_ROWS : 2 * SLOT_ROWS] = placed_rows(slot_x, slopes[0], SLOT_ROWS)
    tables_ref[2 * SLOT_ROWS : 2 * SLOT_ROWS + Y_PAD] = placed_rows(slot_y, values[1], Y_PAD)
    tables_ref[2 * SLOT_ROWS + Y_PAD : 2 * SLOT_ROWS + 2 * Y_PAD] = placed_rows(
        slot_y, slopes[1], Y_PAD
    )
    window = jnp.concatenate(
        [
            placed_rows(base[2], values[2], KZ),
            placed_rows(base[2], slopes[2], KZ),
        ],
        axis=1,
    )
    depth = product((z_high_ref[...], z_low_ref[...]), halves(window), 1, 0)
    depth = halves(depth)
    depth_high_ref[...] = depth[0]
    depth_low_ref[...] = depth[1]
    spread_into(message_ref, start, *read_tables(tables_ref), depth, devices)


def transform_in(message_ref, forward_ref, block_high_ref, block_low_ref, rows_count, cols_count):
    gathered = jnp.concatenate(
        [
            jnp.concatenate(
                [
                    message_ref[(r * cols_count + c) * X_PAD : (r * cols_count + c + 1) * X_PAD]
                    for r in range(rows_count)
                ],
                axis=0,
            )
            for c in range(cols_count)
        ],
        axis=1,
    )
    high, low = halves(gathered)
    along = jnp.dot(
        forward_ref[...],
        jnp.concatenate([high, high, low], axis=0),
        preferred_element_type=jnp.float32,
    )
    part = along.shape[1] // cols_count // SPLIT
    along = jnp.concatenate(
        [
            jnp.concatenate(
                [
                    along[:, (c * SPLIT + half) * part : (c * SPLIT + half + 1) * part]
                    for c in range(cols_count)
                ],
                axis=1,
            )
            for half in range(SPLIT)
        ],
        axis=0,
    )
    return product(halves(along), (block_high_ref[...], block_low_ref[...]))


def transform_out(result_ref, values, backward_ref, block_high_ref, block_low_ref, counts):
    rows_count, cols_count = counts
    spread = product(halves(values), (block_high_ref[...], block_low_ref[...]), 1, 1)
    grid_x = spread.shape[0] // SPLIT
    part = spread.shape[1] // cols_count
    spread = jnp.concatenate(
        [
            spread[half * grid_x : (half + 1) * grid_x, c * part : (c + 1) * part]
            for c in range(cols_count)
            for half in range(SPLIT)
        ],
        axis=1,
    )
    high, low = halves(spread)
    along = jnp.dot(
        backward_ref[...],
        jnp.concatenate([high, high, low], axis=0),
        preferred_element_type=jnp.float32,
    )
    width = along.shape[1] // cols_count
    slot_rows = result_ref.shape[0] // (rows_count * cols_count)
    for r in range(rows_count):
        for c in range(cols_count):
            first = (r * cols_count + c) * slot_rows
            result_ref[first : first + X_PAD, :] = along[
                r * X_PAD : (r + 1) * X_PAD, c * width : (c + 1) * width
            ]


def middle_first_body(
    counts,
    message_ref,
    kernel_ref,
    forward_ref,
    backward_ref,
    block_high_ref,
    block_low_ref,
    result_ref,
    wave_ref,
):
    wave = transform_in(message_ref, forward_ref, block_high_ref, block_low_ref, *counts)
    wave_ref[...] = wave
    transform_out(
        result_ref, wave * kernel_ref[...], backward_ref, block_high_ref, block_low_ref, counts
    )


def gather_rows(parts):
    tiles = [
        parts[GROUP * tile : GROUP * tile + GROUP, :] for tile in range(parts.shape[0] // GROUP)
    ]
    return jnp.concatenate(tiles, axis=1)[0 : 3 * RHS]


def row_total(value, rhs):
    row = lax.broadcasted_iota(jnp.int32, value.shape, 0)
    return total(jnp.where(lax.rem(row, RHS) == rhs, value, 0.0))


def total(value):
    return jnp.sum(jnp.sum(value, axis=0, keepdims=True), axis=1, keepdims=True)


def middle_second_body(
    counts,
    message_ref,
    kernel_ref,
    forward_ref,
    backward_ref,
    block_high_ref,
    block_low_ref,
    wave_ref,
    rhs_ref,
    start_ref,
    image_ref,
    second_ref,
    near_ref,
    polar_ref,
    result_ref,
):
    rhs_rows = read_rows(rhs_ref)
    near_rows = gather_rows(near_ref)
    wave = transform_in(message_ref, forward_ref, block_high_ref, block_low_ref, *counts)
    filtered = wave * kernel_ref[...]
    transform_out(result_ref, filtered, backward_ref, block_high_ref, block_low_ref, counts)
    before = wave_ref[...]
    grid_y = CY * counts[1]
    lane = lax.broadcasted_iota(jnp.int32, wave.shape, 1)
    own_rhs = lax.rem(lax.div(lane, grid_y), RHS)
    second = second_ref[...]
    start = start_ref[...]
    image = image_ref[...]
    local_part = second / polar_ref[...] - near_rows - self_coef * second
    slot = lax.broadcasted_iota(jnp.int32, (1, result_ref.shape[1]), 1)
    sums = jnp.zeros((1, result_ref.shape[1]), jnp.float32)
    for rhs in range(RHS):
        mine = own_rhs == rhs
        parts = (
            row_total(rhs_rows * start, rhs),
            row_total(start * image, rhs),
            row_total(second * image, rhs),
            row_total(start * local_part, rhs) + total(jnp.where(mine, before * filtered, 0.0)),
            row_total(second * local_part, rhs) + total(jnp.where(mine, wave * filtered, 0.0)),
        )
        for index, part in enumerate(parts):
            sums = jnp.where(slot == rhs * len(parts) + index, part, sums)
    devices = counts[0] * counts[1]
    result_ref[pl.ds(X_PAD, devices, stride=X_PAD + 1), :] = jnp.broadcast_to(
        sums, (devices, sums.shape[1])
    )


def sample_body(
    devices,
    message_ref,
    tables_ref,
    depth_high_ref,
    depth_low_ref,
    start_ref,
    near_ref,
    polar_ref,
    image_ref,
    second_ref,
    payload_ref,
):
    tables = read_tables(tables_ref)
    depth = (depth_high_ref[...], depth_low_ref[...])
    field = sample_from(message_ref, *tables, depth, devices)
    start = start_ref[...]
    polar = polar_ref[...]
    image = start / polar - gather_rows(near_ref) + field - self_coef * start
    second = polar * image
    image_ref[...] = image
    second_ref[...] = second
    store_payload(payload_ref, second)


def spread_body(
    devices,
    tables_ref,
    depth_high_ref,
    depth_low_ref,
    second_ref,
    result_ref,
):
    depth = (depth_high_ref[...], depth_low_ref[...])
    spread_into(result_ref, second_ref[...], *read_tables(tables_ref), depth, devices)


def final_body(
    devices,
    message_ref,
    tables_ref,
    depth_high_ref,
    depth_low_ref,
    rhs_ref,
    start_ref,
    image_ref,
    second_ref,
    near_ref,
    polar_ref,
    dipole_ref,
    residual_ref,
):
    tables = read_tables(tables_ref)
    depth = (depth_high_ref[...], depth_low_ref[...])
    field = sample_from(message_ref, *tables, depth, devices)
    second = second_ref[...]
    start = start_ref[...]
    image = image_ref[...]
    image_second = second / polar_ref[...] - gather_rows(near_ref) + field - self_coef * second
    sums = jnp.sum(
        message_ref[pl.ds(X_PAD, devices, stride=X_PAD + 1), :], axis=0, keepdims=True
    )
    steps = []
    for rhs in range(RHS):
        progress, start_image, second_image, start_next, second_next = [
            sums[:, rhs * 5 + index : rhs * 5 + index + 1] for index in range(5)
        ]
        step = progress / start_image
        progress_next = progress - 2.0 * step * start_image + step * step * second_image
        grown = 1.0 + progress_next / progress
        curvature = (
            grown * grown * start_image
            - step * grown * (start_next + second_image)
            + step * step * second_next
        )
        steps.append((step, grown, progress_next / curvature))
    row = lax.broadcasted_iota(jnp.int32, (RHS, 1), 0)
    step, grown, step_next = [
        sum(jnp.where(row == rhs, steps[rhs][index], 0.0) for rhs in range(RHS))
        for index in range(3)
    ]
    for dim in range(3):
        rows = slice(dim * RHS, (dim + 1) * RHS)
        direction = grown * start[rows] - step * second[rows]
        image_direction = grown * image[rows] - step * image_second[rows]
        dipole_ref[dim] = step * start[rows] + step_next * direction
        residual_ref[dim] = rhs_ref[dim] - step * image[rows] - step_next * image_direction


def near_base(entry, brick_rows):
    return lax.shift_right_logical(entry, 2) * brick_rows + lax.bitwise_and(entry, 3)


def nearest(places, origin, span):
    return places - span * jnp.floor((places - origin) * (1.0 / span) + 0.5)


def unwrap_near(near, tile_count, spans):
    rows = near.shape[0] // 9
    for dim in range(2):
        own = 4 * rows + dim * tile_count
        origin = near[own : own + 1, 0:1]
        for brick in range(9):
            first = brick * rows + dim * tile_count
            near[first : first + tile_count, :] = nearest(
                near[first : first + tile_count, :], origin, spans[dim]
            )


def pick_rows(picked, near, lists_ref, tile, place, tile_count, quantities, origin, span):
    rows = near.shape[0] // 9
    place = place * lists_ref.shape[1] * quantities * GROUP
    for entry in range(lists_ref.shape[1]):
        base = near_base(lists_ref[tile, entry], rows)
        for quantity in range(quantities):
            values = near[pl.ds(base + quantity * tile_count, 1), :]
            if quantity == 2 and span is not None:
                values = nearest(values, origin, span)
            first = place + (entry * quantities + quantity) * GROUP
            picked[first : first + GROUP, :] = jnp.broadcast_to(values, (GROUP, TILE))


def widen_own(near, quantities, tile_count, tile, place, wide):
    offset = near.shape[0] // 9 * 4
    rows = [
        near[offset + quantity * tile_count + tile : offset + quantity * tile_count + tile + 1, :]
        for quantity in range(quantities)
    ]
    spare = jnp.zeros((TILE - quantities, TILE), jnp.float32)
    columns = jnp.transpose(jnp.concatenate(rows + [spare], axis=0))
    for quantity in range(quantities):
        first = (place * quantities + quantity) * TILE
        wide[first : first + TILE, :] = jnp.broadcast_to(
            columns[:, quantity : quantity + 1], (TILE, TILE)
        )


def add_field(sums, first_term, second_term, apart, moments):
    for rhs in range(RHS):
        moment = [moments[RHS * dim + rhs] for dim in range(3)]
        projected = moment[0] * apart[0] + moment[1] * apart[1] + moment[2] * apart[2]
        weighted = second_term * projected
        for dim in range(3):
            index = RHS * dim + rhs
            sums[index] = sums[index] + (weighted * apart[dim] - first_term * moment[dim])


def finish_sums(field_ref, sums_ref, first_tile, place):
    place = place * 3 * RHS
    lane = lax.broadcasted_iota(jnp.int32, (TILE, TILE), 1)
    merged = jnp.zeros((TILE, TILE), jnp.float32)
    for index in range(3 * RHS):
        first = (place + index) * TILE
        column = jnp.sum(sums_ref[first : first + TILE, :], axis=1, keepdims=True)
        merged = jnp.where(lane == index, column, merged)
    first = (first_tile + place // (3 * RHS)) * GROUP
    field_ref[first : first + GROUP, :] = jnp.transpose(merged)[0:GROUP]


def pair_rows(start, group):
    return pl.ds(pl.multiple_of(start + group * GROUP, GROUP), GROUP)


def wide_rows(start, group, quantity):
    return pl.ds(pl.multiple_of(quantity * TILE + start + group * GROUP, GROUP), GROUP)


def pair_terms(square_dist, damp):
    inverse = lax.rsqrt(square_dist)
    distance = square_dist * inverse
    inverse_sq = inverse * inverse
    inverse_cube = inverse_sq * inverse
    cubed = damp * (distance * square_dist)
    damping = jnp.exp(cubed)
    bell = jnp.exp(-(ewald_beta * ewald_beta) * square_dist)
    stretched = 1.0 + (SCREEN_SCALE * ewald_beta) * distance
    turned = pl.reciprocal(stretched, approx=True)
    turned = turned * (2.0 - stretched * turned)
    series = SCREEN_COEF[-1] * turned + SCREEN_COEF[-2]
    for coef in SCREEN_COEF[-3::-1]:
        series = series * turned + coef
    screen = bell * turned * series
    gaussian = (2.0 * ewald_beta / math.sqrt(math.pi)) * bell
    bare = screen - damping
    first_term = bare * inverse_cube + gaussian * inverse_sq
    second_term = (
        3.0 * (first_term + (cubed * damping) * inverse_cube)
        + (2.0 * ewald_beta * ewald_beta) * gaussian
    ) * inverse_sq
    return first_term, second_term


def step_rows(step, size, offset):
    return pl.ds(pl.multiple_of(step * size + offset, GROUP), GROUP)


def tile_rows(step, rows):
    return pl.ds(pl.multiple_of(step * rows, GROUP), rows)


def start_all(copies):
    for copy in copies:
        copy.start()


def wait_all(copies):
    for copy in copies:
        copy.wait()


def near_copies(sources, near, semaphore):
    rows = sources[0].shape[0]
    return [
        pltpu.make_async_copy(
            source, near.at[index * rows : (index + 1) * rows, :], semaphore.at[index]
        )
        for index, source in enumerate(sources)
    ]


def term_copies(terms, buffers, semaphore, begin, step, size, inward):
    rows = pl.ds(pl.multiple_of((begin + step) * size, GROUP), size)
    place = pl.ds(pl.multiple_of(step * size, GROUP), size)
    copies = []
    for index in range(2):
        far, here = terms[index].at[rows, :], buffers[index].at[place, :]
        ends = (far, here) if inward else (here, far)
        copies.append(pltpu.make_async_copy(*ends, semaphore.at[index, step]))
    return copies


def pair_first_body(
    first_tile,
    last_tile,
    tile_count,
    spans,
    lists_ref,
    up_ref,
    stack_ref,
    down_ref,
    *others,
):
    first_ref, second_ref, field_ref, near_ref = others[-14:-10]
    near, picked, wide, sums_ref, kept, field, first_buffer, second_buffer, semaphore, busy = others[-10:]
    terms = (first_ref, second_ref)
    buffers = (first_buffer, second_buffer)
    copies = near_copies((up_ref, stack_ref, down_ref), near, semaphore.at[0])
    if first_tile > 0:
        copies.append(
            pltpu.make_async_copy(
                others[0], field.at[0 : first_tile * GROUP, :], semaphore.at[0, 3]
            )
        )
    start_all(copies)
    wait_all(copies)
    entries = lists_ref.shape[1]
    rows = near.shape[0] // 9
    quantities = rows // tile_count
    unwrap_near(near, tile_count, spans)
    for brick in range(9):
        kept[brick * 3 * tile_count : (brick + 1) * 3 * tile_count, :] = near[
            brick * rows : brick * rows + 3 * tile_count, :
        ]
    keep = pltpu.make_async_copy(kept, near_ref, semaphore.at[1, 3])
    keep.start()
    for place, tile in enumerate(range(first_tile, last_tile)):
        widen_own(near, 4, tile_count, tile, place, wide)
        own = rows * 4 + 2 * tile_count + tile
        origin = near[own : own + 1, 0:1]
        pick_rows(picked, near, lists_ref, tile, place, tile_count, quantities, origin, spans[2])
    parts = TILE // PAIR_ROWS
    steps = (last_tile - first_tile) * parts

    size = entries * PAIR_ROWS

    def sent(step):
        return term_copies(terms, buffers, busy, first_tile * parts, step, size, False)

    @pl.loop(0, steps)
    def _(step):
        tile = lax.div(step, parts)
        start = lax.rem(step, parts) * PAIR_ROWS
        step_picked = picked.at[tile_rows(tile, entries * quantities * GROUP), :]
        step_wide = wide.at[tile_rows(tile, 4 * TILE), :]
        step_sums = sums_ref.at[tile_rows(tile, 3 * RHS * TILE), :]
        for group in range(PAIR_ROWS // GROUP):
            own = [step_wide[wide_rows(start, group, dim), :] for dim in range(4)]
            own_damp = -thole_a * own[3]
            sums = [jnp.zeros((GROUP, TILE), jnp.float32) for _ in range(3 * RHS)]
            itself = (
                lax.broadcasted_iota(jnp.int32, (GROUP, TILE), 0) + (start + group * GROUP)
            ) == lax.broadcasted_iota(jnp.int32, (GROUP, TILE), 1)
            for entry in range(entries):
                first = entry * quantities * GROUP
                rows = [
                    step_picked[first + quantity * GROUP : first + (quantity + 1) * GROUP, :]
                    for quantity in range(quantities)
                ]
                apart = [rows[dim] - own[dim] for dim in range(3)]
                square_dist = apart[0] * apart[0] + apart[1] * apart[1] + apart[2] * apart[2]
                if entry == 0:
                    square_dist = jnp.where(itself, 1.0, square_dist)
                first_term, second_term = pair_terms(square_dist, own_damp * rows[3])
                if entry == 0:
                    first_term = jnp.where(itself, 0.0, first_term)
                    second_term = jnp.where(itself, 0.0, second_term)
                place = step_rows(step, size, entry * PAIR_ROWS + group * GROUP)
                first_buffer[place, :] = first_term
                second_buffer[place, :] = second_term
                add_field(sums, first_term, second_term, apart, rows[4:])
            for index, value in enumerate(sums):
                step_sums[wide_rows(start, group, index), :] = value
        start_all(sent(step))

    for place in range(last_tile - first_tile):
        finish_sums(field, sums_ref, first_tile, place)
    result = pltpu.make_async_copy(field, field_ref, semaphore.at[1, 2])
    result.start()

    @pl.loop(0, steps)
    def _(step):
        wait_all(sent(step))

    keep.wait()
    result.wait()


def pair_second_body(
    tile_count,
    spans,
    lists_ref,
    near_ref,
    up_ref,
    stack_ref,
    down_ref,
    first_ref,
    second_ref,
    field_ref,
    near,
    near_moment,
    picked,
    picked_moment,
    wide,
    sums_ref,
    field,
    first_buffer,
    second_buffer,
    semaphore,
    busy,
):
    terms = (first_ref, second_ref)
    buffers = (first_buffer, second_buffer)
    parts = TILE // PAIR_ROWS
    steps = tile_count * parts

    entries = lists_ref.shape[1]
    size = entries * PAIR_ROWS

    def fetched(step):
        return term_copies(terms, buffers, busy, 0, step, size, True)

    places = pltpu.make_async_copy(near_ref, near, semaphore.at[1, 3])
    places.start()
    copies = near_copies((up_ref, stack_ref, down_ref), near_moment, semaphore.at[2])
    start_all(copies)

    @pl.loop(0, steps)
    def _(step):
        start_all(fetched(step))

    places.wait()
    for tile in range(tile_count):
        widen_own(near, 3, tile_count, tile, tile, wide)
        own = near.shape[0] // 9 * 4 + 2 * tile_count + tile
        origin = near[own : own + 1, 0:1]
        pick_rows(picked, near, lists_ref, tile, tile, tile_count, 3, origin, spans[2])
    wait_all(copies)
    for tile in range(tile_count):
        pick_rows(
            picked_moment, near_moment, lists_ref, tile, tile, tile_count, 3 * RHS, None, None
        )

    @pl.loop(0, steps)
    def _(step):
        wait_all(fetched(step))
        tile = lax.div(step, parts)
        start = lax.rem(step, parts) * PAIR_ROWS
        step_picked = picked.at[tile_rows(tile, entries * 3 * GROUP), :]
        step_moment = picked_moment.at[tile_rows(tile, entries * 3 * RHS * GROUP), :]
        step_wide = wide.at[tile_rows(tile, 3 * TILE), :]
        step_sums = sums_ref.at[tile_rows(tile, 3 * RHS * TILE), :]
        for group in range(PAIR_ROWS // GROUP):
            own = [step_wide[wide_rows(start, group, dim), :] for dim in range(3)]
            sums = [jnp.zeros((GROUP, TILE), jnp.float32) for _ in range(3 * RHS)]
            for entry in range(entries):
                first = entry * 3 * GROUP
                apart = [
                    step_picked[first + dim * GROUP : first + (dim + 1) * GROUP, :] - own[dim]
                    for dim in range(3)
                ]
                first = first * RHS
                moments = [
                    step_moment[first + index * GROUP : first + (index + 1) * GROUP, :]
                    for index in range(3 * RHS)
                ]
                place = step_rows(step, size, entry * PAIR_ROWS + group * GROUP)
                add_field(sums, first_buffer[place, :], second_buffer[place, :], apart, moments)
            for index, value in enumerate(sums):
                step_sums[wide_rows(start, group, index), :] = value

    for place in range(tile_count):
        finish_sums(field, sums_ref, 0, place)
    result = pltpu.make_async_copy(field, field_ref, semaphore.at[1, 2])
    result.start()
    result.wait()


def shift(source, axis, step):
    count = lax.axis_size(axis)
    return lax.ppermute(source, axis, [(i, (i + step) % count) for i in range(count)])


def both_ways(source, axis):
    return shift(source, axis, 1), source, shift(source, axis, -1)


def whole(shape):
    return pl.BlockSpec(shape, lambda *_: (0,) * len(shape))


def anywhere():
    return pl.BlockSpec(memory_space=pl.ANY)


def join(message, payload):
    left, _, right = both_ways(payload, "col")
    message, left, right = lax.optimization_barrier((message, left, right))
    return message, both_ways(jnp.concatenate([left, payload, right], axis=0), "row")


class Fetched:
    def __init__(self, source, scratch, semaphore):
        self.copy = pltpu.make_async_copy(source, scratch, semaphore)
        self.copy.start()
        self.scratch = scratch
        self.shape = scratch.shape
        self.waiting = True

    def wait(self):
        if self.waiting:
            self.copy.wait()
            self.waiting = False

    def __getitem__(self, index):
        self.wait()
        return self.scratch[index]


def call(body, outs, *operands, after=(), own_block=None):
    fetched = [
        pltpu.VMEM(operand.shape[1:] if index == own_block else operand.shape, operand.dtype)
        for index, operand in enumerate(operands)
    ]
    count = len(operands)

    def run(*refs):
        refs = refs[len(after) :]
        sources, refs = refs[:count], refs[count:]
        results, refs = refs[: len(outs)], refs[len(outs) :]
        targets, written, semaphore = refs[:count], refs[count:-1], refs[-1]
        inputs = []
        for index, source in enumerate(sources):
            if index == own_block:
                place = lax.axis_index("row") * lax.axis_size("col") + lax.axis_index("col")
                source = source.at[place]
            inputs.append(Fetched(source, targets[index], semaphore.at[index]))
        body(*inputs, *written)
        for operand in inputs:
            operand.wait()
        copies = [
            pltpu.make_async_copy(value, result, semaphore.at[count + index])
            for index, (value, result) in enumerate(zip(written, results))
        ]
        for copy in copies:
            copy.start()
        for copy in copies:
            copy.wait()

    return pl.pallas_call(
        run,
        in_specs=[anywhere()] * (len(after) + count),
        out_specs=[anywhere()] * len(outs),
        out_shape=[jax.ShapeDtypeStruct(shape, dtype) for shape, dtype in outs],
        scratch_shapes=fetched
        + [pltpu.VMEM(shape, dtype) for shape, dtype in outs]
        + [pltpu.SemaphoreType.DMA((count + len(outs),))],
        compiler_params=pltpu.CompilerParams(vmem_limit_bytes=VMEM_LIMIT),
        cost_estimate=pl.CostEstimate(
            flops=200_000_000, bytes_accessed=10 << 20, transcendentals=0
        ),
    )(*after, *operands)


def final_call(body, outs, *operands):
    return pl.pallas_call(
        body,
        grid=(1,),
        in_specs=[whole(operand.shape) for operand in operands],
        out_specs=[whole(shape) for shape, _ in outs],
        out_shape=[jax.ShapeDtypeStruct(shape, dtype) for shape, dtype in outs],
        compiler_params=pltpu.CompilerParams(vmem_limit_bytes=SMALL_VMEM_LIMIT),
    )(*operands)


def pair_call(body, outs, scratch, lists, *operands, tiles, cost, aliased=0):
    buffers = (tiles * lists.shape[1] * TILE, TILE)
    first = 1 + len(operands) - aliased
    return pl.pallas_call(
        body,
        in_specs=[pl.BlockSpec(memory_space=pltpu.SMEM)] + [anywhere()] * len(operands),
        out_specs=[anywhere()] * len(outs),
        out_shape=[jax.ShapeDtypeStruct(shape, jnp.float32) for shape in outs],
        scratch_shapes=[pltpu.VMEM(shape, jnp.float32) for shape in scratch + [buffers] * 2]
        + [
            pltpu.SemaphoreType.DMA((3, 4)),
            pltpu.SemaphoreType.DMA((2, tiles * TILE // PAIR_ROWS)),
        ],
        input_output_aliases={first + index: index for index in range(aliased)},
        compiler_params=pltpu.CompilerParams(vmem_limit_bytes=VMEM_LIMIT),
        cost_estimate=pl.CostEstimate(
            flops=80_000_000, bytes_accessed=cost, transcendentals=1 << 21
        ),
    )(lists, *operands)


def exchange(message, devices):
    shape = message.shape
    sent = message.reshape(devices, 1, -1)
    return lax.all_to_all(sent, ("row", "col"), split_axis=0, concat_axis=0, tiled=True).reshape(
        shape
    )


def slab_local(field_rhs, positions, polar, grid_base, tile_lists):
    rows_count = lax.axis_size("row")
    cols_count = lax.axis_size("col")
    counts = (rows_count, cols_count)
    devices = rows_count * cols_count
    lengths = (CX * rows_count, CY * cols_count, KZ)
    spans = tuple(float(length) for length in lengths)
    atoms = polar.shape[-1]
    tile_count = atoms // TILE
    listed = tile_lists.shape[-1]
    tables = slab_tables(rows_count, cols_count)
    f32 = jnp.float32
    rhs = jnp.swapaxes(field_rhs[0, 0], 0, 1)
    place = jnp.swapaxes(positions[0], 0, 1)
    base = jnp.swapaxes(grid_base[0], 0, 1)
    polar = polar.reshape(1, atoms)
    lists = tile_lists[0, 0]
    quantities = 4 + 3 * RHS
    brick_rows = quantities * tile_count
    moment_rows = 3 * RHS * tile_count
    message_shape = (devices * X_PAD, KZ // devices * RHS * Y_PAD)
    last_shape = (devices * (X_PAD + 1), message_shape[1])
    row_shape = (3 * RHS, atoms)

    payload = pl.pallas_call(
        pack_body,
        in_specs=[anywhere()] * 3,
        out_specs=pl.BlockSpec(memory_space=pltpu.VMEM),
        out_shape=jax.ShapeDtypeStruct((brick_rows, TILE), f32),
        scratch_shapes=[pltpu.VMEM(array.shape, f32) for array in (rhs, place, polar)]
        + [pltpu.SemaphoreType.DMA((3,))],
        compiler_params=pltpu.CompilerParams(vmem_limit_bytes=SMALL_VMEM_LIMIT),
    )(rhs, place, polar)

    def setup(*refs):
        setup_body(lengths, devices, *refs)

    message, splines, depth_high, depth_low, start = call(
        setup,
        [
            (message_shape, f32),
            ((2 * SLOT_ROWS + 2 * Y_PAD, atoms), f32),
            ((KZ, 2 * atoms), jnp.bfloat16),
            ((KZ, 2 * atoms), jnp.bfloat16),
            (row_shape, f32),
        ],
        place,
        base,
        rhs,
        polar,
        *[jnp.asarray(table) for table in tables["along_z"]],
        after=(payload,),
    )
    constants = (
        jnp.asarray(tables["kernel"]),
        jnp.asarray(tables["forward_x"]),
        jnp.asarray(tables["backward_x"]),
        *[jnp.asarray(table) for table in tables["block"]],
    )
    message, near = join(message, payload)
    arrived = exchange(message, devices)

    def pair_first(first_tile, last_tile, fields, *after):
        def body(*refs):
            pair_first_body(first_tile, last_tile, tile_count, spans, *refs)

        tiles = last_tile - first_tile
        return pair_call(
            body,
            [(tile_count * listed * TILE, TILE)] * 2
            + [(last_tile * GROUP, TILE), (9 * 3 * tile_count, TILE)],
            [
                (9 * brick_rows, TILE),
                (tiles * listed * quantities * GROUP, TILE),
                (tiles * 4 * TILE, TILE),
                (tiles * 3 * RHS * TILE, TILE),
                (9 * 3 * tile_count, TILE),
                (last_tile * GROUP, TILE),
            ],
            lists,
            *near,
            *fields,
            *after,
            tiles=tiles,
            cost=(8 + 10 * tiles) << 20,
            aliased=2 if first_tile > 0 else 0,
        )

    early = pair_first(0, EARLY_TILES, (), message)

    def middle_first(*refs):
        middle_first_body(counts, *refs)

    mixed, wave = call(
        middle_first,
        [(message_shape, f32), (tables["kernel"].shape[1:], f32)],
        arrived,
        *constants,
        after=(early[2],),
        own_block=1,
    )
    returned = exchange(mixed, devices)
    first_term, second_term, direct, near = pair_first(
        EARLY_TILES, tile_count, (early[2],), wave, *early[:2]
    )

    def sample(*refs):
        sample_body(devices, *refs)

    image, second, moments = call(
        sample,
        [(row_shape, f32), (row_shape, f32), ((moment_rows, TILE), f32)],
        returned,
        splines,
        depth_high,
        depth_low,
        start,
        direct,
        polar,
    )

    def spread(*refs):
        spread_body(devices, *refs)

    (message,) = call(spread, [(message_shape, f32)], splines, depth_high, depth_low, second)
    message, near_moments = join(message, moments)
    arrived = exchange(message, devices)

    def pair_second(*refs):
        pair_second_body(tile_count, spans, *refs)

    (direct,) = pair_call(
        pair_second,
        [(tile_count * GROUP, TILE)],
        [
            (9 * 3 * tile_count, TILE),
            (9 * moment_rows, TILE),
            (tile_count * listed * 3 * GROUP, TILE),
            (tile_count * listed * 3 * RHS * GROUP, TILE),
            (tile_count * 3 * TILE, TILE),
            (tile_count * 3 * RHS * TILE, TILE),
            (tile_count * GROUP, TILE),
        ],
        lists,
        near,
        *near_moments,
        first_term,
        second_term,
        tiles=tile_count,
        cost=32 << 20,
    )

    def middle_second(*refs):
        middle_second_body(counts, *refs)

    (mixed,) = call(
        middle_second,
        [(last_shape, f32)],
        arrived,
        *constants,
        wave,
        rhs,
        start,
        image,
        second,
        direct,
        polar,
        own_block=1,
    )
    returned = exchange(mixed, devices)

    def final(*refs):
        final_body(devices, *refs)

    outs = final_call(
        final,
        [(rhs.shape, f32), (rhs.shape, f32)],
        returned,
        splines,
        depth_high,
        depth_low,
        rhs,
        start,
        image,
        second,
        direct,
        polar,
    )
    return tuple(jnp.swapaxes(out, 0, 1)[None, None] for out in outs)


def solution(mesh):
    placed = (
        P("row", "col", None, None, None),
        P("row", "col", None, None),
        P("row", "col", None),
        P("row", "col", None, None),
        P("row", "col", None, None),
    )
    devices = mesh.shape["row"] * mesh.shape["col"]
    return jax.shard_map(
        slab_local if KZ % devices == 0 else pencil_local,
        mesh=mesh,
        in_specs=placed,
        out_specs=(P("row", "col", None, None, None), P("row", "col", None, None, None)),
        check_vma=False,
    )
```

```python
import math

import jax
import jax.numpy as jnp
import ml_dtypes
import numpy as np
from jax import lax
from jax.experimental import pallas as pl
from jax.experimental.pallas import tpu as pltpu
from jax.sharding import PartitionSpec as P

CX = 8
CY = 4
KZ = 256
TILE = 128
RHS = 2
ITERS = 2


ewald_beta = 0.4
thole_a = 0.39
self_coef = 4.0 * ewald_beta**3 / (3.0 * math.sqrt(math.pi))
highest = lax.Precision.HIGHEST


def with_halo(cells, sides, width):
    for axis, dim in sides:
        count = lax.axis_size(axis)
        head = lax.slice_in_dim(cells, 0, width, axis=dim)
        tail = lax.slice_in_dim(cells, cells.shape[dim] - width, cells.shape[dim], axis=dim)
        cells = jnp.concatenate(
            [
                lax.ppermute(tail, axis, [(i, (i + 1) % count) for i in range(count)]),
                cells,
                lax.ppermute(head, axis, [((i + 1) % count, i) for i in range(count)]),
            ],
            axis=dim,
        )
    return cells


def spline_table(fraction):
    previous = {0: jnp.ones_like(fraction)}
    fourth = previous
    for degree in range(2, 6):
        current = {}
        for offset in range(degree):
            abscissa = fraction + offset
            summed = abscissa * previous.get(offset, 0.0) + (degree - abscissa) * previous.get(
                offset - 1, 0.0
            )
            current[offset] = summed / (degree - 1)
        if degree == 4:
            fourth = current
        previous = current
    values = jnp.stack([previous[4 - stencil] for stencil in range(5)])
    slopes = jnp.stack(
        [fourth.get(4 - stencil, 0.0) - fourth.get(3 - stencil, 0.0) for stencil in range(5)]
    )
    return (values, slopes)


def spline_modulus(wave_index, length):
    spline_coef = (1.0 / 24.0, 11.0 / 24.0, 11.0 / 24.0, 1.0 / 24.0)
    cosine_sum = jnp.zeros(wave_index.shape, jnp.float32)
    sine_sum = jnp.zeros(wave_index.shape, jnp.float32)
    for offset in range(4):
        angles = 2.0 * math.pi / length * (wave_index * offset % length).astype(jnp.float32)
        cosine_sum = cosine_sum + spline_coef[offset] * jnp.cos(angles)
        sine_sum = sine_sum + spline_coef[offset] * jnp.sin(angles)
    return cosine_sum * cosine_sum + sine_sum * sine_sum


def folded_square(wave_index, length):
    nearest = jnp.minimum(wave_index, length - wave_index).astype(jnp.float32) / length
    return nearest * nearest


def influence(wave_x, wave_y, wave_z, length_x, length_y, length_z):
    wave_norm = (
        folded_square(wave_x, length_x)
        + folded_square(wave_y, length_y)
        + folded_square(wave_z, length_z)
    )
    modulus = (
        spline_modulus(wave_x, length_x)
        * spline_modulus(wave_y, length_y)
        * spline_modulus(wave_z, length_z)
    )
    excluded = (wave_x * 2 == length_x) | (wave_y * 2 == length_y) | (wave_z * 2 == length_z)
    excluded = excluded | (wave_x == 0) & (wave_y == 0) & (wave_z == 0)
    safe_norm = jnp.where(excluded, 1.0, wave_norm)
    safe_modulus = jnp.where(excluded, 1.0, modulus)
    result = jnp.exp(-(math.pi**2 / ewald_beta**2) * safe_norm) / (
        math.pi * safe_norm * safe_modulus
    )
    return jnp.where(excluded, 0.0, result)


def tile_field(own_static, near_static, near_dipole, box_spans):
    listed_count = near_static.shape[0]
    tile_width = own_static.shape[1]
    box_span = jnp.array(box_spans, dtype=jnp.float32)[None, :, None, None]
    separation = near_static[:, 0:3, None, :] - own_static[None, 0:3, :, None]
    separation = separation - box_span * jnp.floor(separation / box_span + 0.5)
    dist_sq = jnp.sum(separation * separation, axis=1)
    itself = (jnp.arange(listed_count)[:, None, None] == 0) & (
        jnp.arange(tile_width)[:, None] == jnp.arange(tile_width)[None, :]
    )[None]
    safe_sq = jnp.where(itself, 1.0, dist_sq)
    distance = jnp.sqrt(safe_sq)
    scaled = distance / (own_static[3][None, :, None] * near_static[:, 3][:, None, :])
    cubed = thole_a * scaled * scaled * scaled
    damping = jnp.exp(-cubed)
    screen = lax.erfc(ewald_beta * distance)
    gaussian = 2.0 * ewald_beta / math.sqrt(math.pi) * jnp.exp(-(ewald_beta * ewald_beta) * safe_sq)
    inverse_sq = 1.0 / safe_sq
    inverse_cube = inverse_sq / distance
    first_term = (screen - damping) * inverse_cube + gaussian * inverse_sq
    second = (
        3.0 * (screen - (1.0 + cubed) * damping) * inverse_cube * inverse_sq
        + gaussian * (2.0 * ewald_beta * ewald_beta + 3.0 * inverse_sq) * inverse_sq
    )
    first_term = jnp.where(itself, 0.0, first_term)
    second = jnp.where(itself, 0.0, second)
    projected = jnp.sum(near_dipole[:, :, :, None, :] * separation[:, None, :, :, :], axis=2)
    weighted = second[:, None] * projected
    outward = jnp.sum(weighted[:, :, None] * separation[:, None], axis=(0, 4))
    inward = jnp.sum(first_term[:, None, None] * near_dipole[:, :, :, None, :], axis=(0, 4))
    return outward - inward


def hartley(length):
    counter = jnp.arange(length, dtype=jnp.int32)
    angles = (
        2.0 * math.pi / length * (counter[:, None] * counter[None, :] % length).astype(jnp.float32)
    )
    return jnp.cos(angles) + jnp.sin(angles)


def placed_table(first_cell, weights, extent):
    slot_index = jnp.arange(extent, dtype=jnp.int32)[:, None]
    placed = jnp.zeros((extent, first_cell.shape[0]), jnp.float32)
    for stencil in range(5):
        placed = placed + jnp.where(
            slot_index == (first_cell[None, :] + stencil) % extent, weights[stencil][None, :], 0.0
        )
    return placed


def pad_axis(source, axis_pos, leading, trailing):
    widths = [(0, 0)] * source.ndim
    widths[axis_pos] = (leading, trailing)
    return jnp.pad(source, widths)


def fold_cycle(cycle_only, axis_pos, inner_len):
    middle = lax.slice_in_dim(cycle_only, 4, inner_len + 4, axis=axis_pos)
    lower_cycle = lax.slice_in_dim(cycle_only, 0, 2, axis=axis_pos)
    upper_cycle = lax.slice_in_dim(cycle_only, inner_len + 6, inner_len + 8, axis=axis_pos)
    return (
        middle
        + pad_axis(lower_cycle, axis_pos, 0, inner_len - 2)
        + pad_axis(upper_cycle, axis_pos, inner_len - 2, 0)
    )


def clear_inside(extended, extents):
    inside = None
    for axis_pos, inner_len in extents:
        slot_index = lax.broadcasted_iota(jnp.int32, extended.shape, axis_pos)
        within = (slot_index >= 2) & (slot_index < inner_len + 6)
        inside = within if inside is None else inside & within
    return jnp.where(inside, 0.0, extended)


def inner_sum(left_arr, right_arr):
    return lax.psum(jnp.sum(left_arr * right_arr, axis=(1, 2)), ("row", "col"))


def pencil_local(field_rhs, positions, polar, grid_base, tile_lists):
    rows_count = lax.axis_size("row")
    cols_count = lax.axis_size("col")
    grid_x = CX * rows_count
    grid_y = CY * cols_count
    atom_count = polar.shape[-1]
    tile_count = atom_count // TILE
    slab_depth = KZ // tile_count
    window_len = slab_depth + 4
    box_spans = (float(grid_x), float(grid_y), float(KZ))
    own_place = positions[0, 0]
    own_base = grid_base[0, 0]
    own_polar = polar[0, 0]
    lengths = jnp.array([grid_x, grid_y, KZ], dtype=jnp.int32)[:, None]
    cell_index = (own_base + 2) % lengths
    fraction = own_place - cell_index.astype(jnp.float32)
    values, slopes = spline_table(fraction)
    first_x = (own_base[0] - lax.axis_index("row") * CX + 2) % grid_x
    first_y = (own_base[1] - lax.axis_index("col") * CY + 2) % grid_y
    rows_x = placed_table(first_x, values[:, 0], CX + 4)
    slope_x = placed_table(first_x, slopes[:, 0], CX + 4)
    rows_y = placed_table(first_y, values[:, 1], CY + 4)
    slope_y = placed_table(first_y, slopes[:, 1], CY + 4)
    tile_start = jnp.arange(atom_count, dtype=jnp.int32) // TILE * slab_depth
    first_z = (own_base[2] + 2 - tile_start) % KZ
    rows_z = placed_table(first_z, values[:, 2], window_len)
    slope_z = placed_table(first_z, slopes[:, 2], window_len)
    plane_count = (CX + 4) * (CY + 4)
    plane_dx = (slope_x[:, None, :] * rows_y[None, :, :]).reshape(plane_count, atom_count)
    plane_dy = (rows_x[:, None, :] * slope_y[None, :, :]).reshape(plane_count, atom_count)
    plane_flat = (rows_x[:, None, :] * rows_y[None, :, :]).reshape(plane_count, atom_count)
    window_rows = jnp.moveaxis(rows_z.reshape(window_len, tile_count, TILE), 1, 0)
    window_slope = jnp.moveaxis(slope_z.reshape(window_len, tile_count, TILE), 1, 0)
    depth_table = jnp.concatenate([window_rows, window_slope], axis=2)
    grid_scale = 1.0 / (grid_x * grid_y * KZ)
    hartley_x = hartley(grid_x)
    hartley_y = hartley(grid_y)
    hartley_z = hartley(KZ)
    block_y = grid_y // rows_count
    block_z = KZ // cols_count
    wave_x = jnp.arange(grid_x, dtype=jnp.int32)[:, None, None]
    wave_y = (lax.axis_index("row") * block_y + jnp.arange(block_y, dtype=jnp.int32))[None, :, None]
    wave_z = (lax.axis_index("col") * block_z + jnp.arange(block_z, dtype=jnp.int32))[None, None, :]
    kernel = influence(wave_x, wave_y, wave_z, grid_x, grid_y, KZ) * grid_scale
    root_scale = jnp.power(own_polar, 1.0 / 6.0)
    own_static = jnp.concatenate([own_place, root_scale[None]], axis=0)
    near_static = with_halo(own_static[None, None], (("row", 0), ("col", 1)), 1)
    near_static = jnp.moveaxis(near_static.reshape(9, 4, tile_count, TILE), 2, 1).reshape(
        9 * tile_count, 4, TILE
    )
    own_tiles = jnp.moveaxis(own_static.reshape(4, tile_count, TILE), 1, 0)
    own_lists = tile_lists[0, 0]
    polar_wide = own_polar[None, None, :]
    solution = jnp.zeros_like(field_rhs[0, 0])
    residual = field_rhs[0, 0]
    scaled_res = polar_wide * residual
    direction = scaled_res
    progress = inner_sum(residual, scaled_res)
    for iteration in range(ITERS):
        near_dip = with_halo(direction[None, None], (("row", 0), ("col", 1)), 1)
        near_dip = jnp.moveaxis(near_dip.reshape(9, RHS, 3, tile_count, TILE), 3, 1).reshape(
            9 * tile_count, RHS, 3, TILE
        )

        def one_tile(tile_pos):
            picked = own_lists[tile_pos]
            return tile_field(own_tiles[tile_pos], near_static[picked], near_dip[picked], box_spans)

        fields = lax.map(one_tile, jnp.arange(tile_count, dtype=jnp.int32))
        direct = jnp.moveaxis(fields, 0, 2).reshape(RHS, 3, atom_count)
        slope_terms = (
            direction[:, 0, None, :] * plane_dx[None] + direction[:, 1, None, :] * plane_dy[None]
        )
        flat_terms = direction[:, 2, None, :] * plane_flat[None]
        spread_left = jnp.concatenate(
            [
                slope_terms.reshape(RHS, plane_count, tile_count, TILE),
                flat_terms.reshape(RHS, plane_count, tile_count, TILE),
            ],
            axis=3,
        )
        spread_windows = jnp.einsum("sptb,twb->sptw", spread_left, depth_table, precision=highest)
        main_part = spread_windows[..., :slab_depth].reshape(spread_windows.shape[:-2] + (KZ,))
        tail_part = pad_axis(
            spread_windows[..., slab_depth:], spread_windows.ndim - 1, 0, slab_depth - 4
        )
        tail_part = tail_part.reshape(spread_windows.shape[:-2] + (KZ,))[..., : KZ + 4 - slab_depth]
        last_axis = main_part.ndim - 1
        padded_line = pad_axis(main_part, last_axis, 0, 4) + pad_axis(
            tail_part, last_axis, slab_depth, 0
        )
        inner = padded_line[..., 2 : KZ + 2]
        spread_tile = (
            inner
            + pad_axis(padded_line[..., 0:2], last_axis, KZ - 2, 0)
            + pad_axis(padded_line[..., KZ + 2 : KZ + 4], last_axis, 0, KZ - 2)
        ).reshape(RHS, CX + 4, CY + 4, KZ)
        extended = with_halo(spread_tile, (("row", 1), ("col", 2)), 2)
        cycle_only = clear_inside(extended, ((1, CX), (2, CY)))
        folded = fold_cycle(fold_cycle(cycle_only, 1, CX), 2, CY)
        spectrum = jnp.einsum(
            "sxyz,zk->sxyk",
            spread_tile[:, 2 : CX + 2, 2 : CY + 2] + folded,
            hartley_z,
            precision=highest,
        )
        along_y = jnp.einsum(
            "sxyz,yk->sxkz",
            lax.all_to_all(spectrum, "col", split_axis=3, concat_axis=2, tiled=True),
            hartley_y,
            precision=highest,
        )
        along_x = (
            jnp.einsum(
                "sxyz,xk->skyz",
                lax.all_to_all(along_y, "row", split_axis=2, concat_axis=1, tiled=True),
                hartley_x,
                precision=highest,
            )
            * kernel[None]
        )
        mixed_part = jnp.einsum("sxyz,xk->skyz", along_x, hartley_x, precision=highest)
        returned = lax.all_to_all(mixed_part, "row", split_axis=1, concat_axis=2, tiled=True)
        swapped = jnp.einsum("sxyz,yk->sxkz", returned, hartley_y, precision=highest)
        restored = lax.all_to_all(swapped, "col", split_axis=2, concat_axis=3, tiled=True)
        padded = with_halo(
            jnp.einsum("sxyz,zk->sxyk", restored, hartley_z, precision=highest),
            (("row", 1), ("col", 2)),
            2,
        )
        line = padded.reshape(RHS, plane_count, KZ)
        extended_line = jnp.concatenate([line[..., KZ - 2 :], line, line[..., :2]], axis=-1)
        windows = jnp.stack(
            [
                extended_line[..., tile * slab_depth : tile * slab_depth + window_len]
                for tile in range(tile_count)
            ],
            axis=-2,
        )
        sampled = jnp.einsum("sptw,twb->sptb", windows, depth_table, precision=highest)
        with_flat = sampled[..., :TILE].reshape(RHS, plane_count, atom_count)
        with_slope = sampled[..., TILE:].reshape(RHS, plane_count, atom_count)
        recip_part = jnp.stack(
            [
                jnp.sum(with_flat * plane_dx[None], axis=1),
                jnp.sum(with_flat * plane_dy[None], axis=1),
                jnp.sum(with_slope * plane_flat[None], axis=1),
            ],
            axis=1,
        )
        image_field = direction / polar_wide - direct + recip_part - self_coef * direction
        step_size = (progress / inner_sum(direction, image_field))[:, None, None]
        solution = solution + step_size * direction
        residual = residual - step_size * image_field
        scaled_res = polar_wide * residual
        progress_next = inner_sum(residual, scaled_res)
        direction = scaled_res + (progress_next / progress)[:, None, None] * direction
        progress = progress_next
    return (solution[None, None], residual[None, None])


X_PAD = CX + 4
Y_PAD = CY + 4
SLOT_ROWS = 16
SPLIT = 2
VMEM_LIMIT = 60_000_000
SMALL_VMEM_LIMIT = 24_000_000
EARLY_TILES = 1
PAIR_ROWS = 32
GROUP = 8
SCREEN_SCALE = 0.4
SCREEN_COEF = (
    0.22567588090896606,
    0.2256690263748169,
    0.20785020291805267,
    0.16849851608276367,
    0.14156343042850494,
    -0.005832736846059561,
    0.16930203139781952,
    -0.1830107867717743,
    0.05028456076979637,
)


def halves(value):
    high = value.astype(jnp.bfloat16)
    return high, (value - high.astype(jnp.float32)).astype(jnp.bfloat16)


def halves_np(value):
    value = value.astype(np.float32)
    high = value.astype(ml_dtypes.bfloat16)
    return high, (value - high.astype(np.float32)).astype(ml_dtypes.bfloat16)


def product(left, right, left_dim=1, right_dim=0):
    def one(first, second):
        return lax.dot_general(
            first,
            second,
            (((left_dim,), (right_dim,)), ((), ())),
            preferred_element_type=jnp.float32,
        )

    return one(left[0], right[0]) + (one(left[1], right[0]) + one(left[0], right[1]))


def cas_np(wave, place, length):
    angles = 2.0 * np.pi / length * (wave[:, None] * place[None, :] % length)
    return np.cos(angles) + np.sin(angles)


def modulus_np(wave, length):
    coef = np.array([1.0, 11.0, 11.0, 1.0]) / 24.0
    angles = 2.0 * np.pi / length * (wave[:, None] * np.arange(4)[None, :])
    return (coef * np.cos(angles)).sum(1) ** 2 + (coef * np.sin(angles)).sum(1) ** 2


def influence_np(length_x, length_y, length_z):
    total = np.zeros((length_x, length_y, length_z))
    modulus = np.ones((length_x, length_y, length_z))
    excluded = np.zeros((length_x, length_y, length_z), bool)
    for axis, length in enumerate((length_x, length_y, length_z)):
        wave = np.arange(length)
        shape = [1, 1, 1]
        shape[axis] = length
        total = total + ((np.minimum(wave, length - wave) / length) ** 2).reshape(shape)
        modulus = modulus * modulus_np(wave, length).reshape(shape)
        excluded = excluded | (wave * 2 == length).reshape(shape)
    excluded[0, 0, 0] = True
    safe = np.where(excluded, 1.0, total)
    result = np.exp(-(np.pi**2) / ewald_beta**2 * safe) / (
        np.pi * safe * np.where(excluded, 1.0, modulus)
    )
    return np.where(excluded, 0.0, result) / (length_x * length_y * length_z)


def slab_tables(rows_count, cols_count):
    grid_x = CX * rows_count
    grid_y = CY * cols_count
    devices = rows_count * cols_count
    chunk = KZ // devices
    wave_z = (np.arange(devices)[None, :] * chunk + np.arange(chunk)[:, None]).reshape(-1)
    along_z = cas_np(wave_z, np.arange(KZ), KZ)
    place_x = np.arange(rows_count)[:, None] * CX + np.arange(X_PAD)[None, :] - 2
    along_x = cas_np(np.arange(grid_x), place_x.reshape(-1) % grid_x, grid_x)
    x_high, x_low = halves_np(along_x)
    forward_x = np.concatenate([x_high, x_low, x_high], axis=1)
    backward_x = np.concatenate([x_high.T, x_low.T, x_high.T], axis=1)
    place_y = (np.arange(cols_count)[:, None] * CY + np.arange(Y_PAD)[None, :] - 2) % grid_y
    along_y = cas_np(np.arange(grid_y), place_y.reshape(-1), grid_y)
    along_y = along_y.reshape(grid_y, cols_count, Y_PAD)
    units = chunk * RHS // SPLIT
    block = np.einsum("uv,kcy->cuyvk", np.eye(units), along_y)
    block = block.reshape(cols_count * units * Y_PAD, units * grid_y)
    kernel = influence_np(grid_x, grid_y, KZ).reshape(grid_x, grid_y, devices, chunk)
    kernel = np.transpose(kernel, (2, 0, 3, 1))[:, :, :, None, :]
    kernel = np.broadcast_to(kernel, (devices, grid_x, chunk, RHS, grid_y))
    kernel = kernel.reshape(devices, grid_x, SPLIT, units * grid_y)
    kernel = np.moveaxis(kernel, 2, 1).reshape(devices, SPLIT * grid_x, units * grid_y)
    kernel = kernel.astype(np.float32)
    return dict(
        along_z=halves_np(along_z),
        forward_x=forward_x,
        backward_x=backward_x,
        block=halves_np(block),
        kernel=kernel,
    )


def pack_body(rhs_ref, place_ref, polar_ref, start_ref, payload_ref):
    polar = polar_ref[...]
    start = read_rows(rhs_ref) * polar
    start_ref[...] = start
    place = [place_ref[dim] for dim in range(3)]
    everything = jnp.concatenate(place + [1.0 / jnp.sqrt(polar), start], axis=0)
    store_payload(payload_ref, everything)


def read_rows(rows_ref):
    return jnp.concatenate([rows_ref[dim] for dim in range(3)], axis=0)


def store_payload(payload_ref, everything):
    tile_count = everything.shape[1] // TILE
    for quantity in range(everything.shape[0]):
        for tile in range(tile_count):
            row = quantity * tile_count + tile
            payload_ref[row : row + 1, :] = everything[
                quantity : quantity + 1, tile * TILE : (tile + 1) * TILE
            ]


def placed_rows(slot, weights, extent):
    slot_index = lax.broadcasted_iota(jnp.int32, (extent, slot.shape[1]), 0)
    placed = jnp.zeros((extent, slot.shape[1]), jnp.float32)
    for stencil in range(5):
        target = slot + stencil
        if extent == KZ:
            target = jnp.where(target >= KZ, target - KZ, target)
        placed = placed + jnp.where(slot_index == target, weights[stencil], 0.0)
    return placed


def spread_into(message_ref, moment, rows_x, slope_x, rows_y, slope_y, depth, devices):
    blocks = []
    for step in range(X_PAD):
        flat_x = rows_x[step : step + 1]
        tilt_x = slope_x[step : step + 1]
        for rhs in range(RHS):
            part_x = tilt_x * moment[rhs : rhs + 1]
            part_y = flat_x * moment[RHS + rhs : RHS + rhs + 1]
            part_z = flat_x * moment[2 * RHS + rhs : 2 * RHS + rhs + 1]
            blocks.append(
                jnp.concatenate([part_x * rows_y + part_y * slope_y, part_z * rows_y], axis=1)
            )
    charges = jnp.concatenate(blocks, axis=0)
    spectrum = product(depth, halves(charges), 1, 1)
    slot_rows = message_ref.shape[0] // devices
    chunk = KZ // devices
    width = RHS * Y_PAD
    for step in range(X_PAD):
        message_ref[pl.ds(step, devices, stride=slot_rows), :] = jnp.concatenate(
            [
                spectrum[unit * devices : (unit + 1) * devices, step * width : (step + 1) * width]
                for unit in range(chunk)
            ],
            axis=1,
        )


def sample_from(message_ref, rows_x, slope_x, rows_y, slope_y, depth, devices):
    chunk = KZ // devices
    width = RHS * Y_PAD
    slot_rows = message_ref.shape[0] // devices
    pieces = [
        message_ref[pl.ds(step, devices, stride=slot_rows), :] for step in range(X_PAD)
    ]
    spare = jnp.zeros((devices, KZ - X_PAD * width), jnp.float32)
    spectrum = jnp.concatenate(
        [
            jnp.concatenate(
                [piece[:, unit * width : (unit + 1) * width] for piece in pieces] + [spare], axis=1
            )
            for unit in range(chunk)
        ],
        axis=0,
    )
    spectrum = jnp.transpose(spectrum)[: X_PAD * width]
    sampled = product(halves(spectrum), depth, 1, 0)
    atoms = rows_x.shape[1]
    fields = [None] * (3 * RHS)
    for rhs in range(RHS):
        sum_x = sum_y = sum_z = None
        for step in range(X_PAD):
            first = step * width + rhs * Y_PAD
            flat = sampled[first : first + Y_PAD, :atoms]
            tilt = sampled[first : first + Y_PAD, atoms:]
            part_x = slope_x[step : step + 1] * flat
            part_y = rows_x[step : step + 1] * flat
            part_z = rows_x[step : step + 1] * tilt
            sum_x = part_x if sum_x is None else sum_x + part_x
            sum_y = part_y if sum_y is None else sum_y + part_y
            sum_z = part_z if sum_z is None else sum_z + part_z
        fields[rhs] = jnp.sum(sum_x * rows_y, axis=0, keepdims=True)
        fields[RHS + rhs] = jnp.sum(sum_y * slope_y, axis=0, keepdims=True)
        fields[2 * RHS + rhs] = jnp.sum(sum_z * rows_y, axis=0, keepdims=True)
    return jnp.concatenate(fields, axis=0)


def read_tables(tables_ref):
    return (
        tables_ref[0:X_PAD],
        tables_ref[SLOT_ROWS : SLOT_ROWS + X_PAD],
        tables_ref[2 * SLOT_ROWS : 2 * SLOT_ROWS + Y_PAD],
        tables_ref[2 * SLOT_ROWS + Y_PAD : 2 * SLOT_ROWS + 2 * Y_PAD],
    )


def setup_body(
    lengths,
    devices,
    place_ref,
    base_ref,
    start_ref,
    z_high_ref,
    z_low_ref,
    message_ref,
    tables_ref,
    depth_high_ref,
    depth_low_ref,
):
    base = [base_ref[dim] for dim in range(3)]
    fractions = []
    cells = []
    for dim in range(3):
        cell = base[dim] + 2
        cell = jnp.where(cell >= lengths[dim], cell - lengths[dim], cell)
        cells.append(cell)
        fractions.append(place_ref[dim] - cell.astype(jnp.float32))
    values, slopes = spline_table(jnp.concatenate(fractions, axis=0))
    values = [[values[stencil][dim : dim + 1] for stencil in range(5)] for dim in range(3)]
    slopes = [[slopes[stencil][dim : dim + 1] for stencil in range(5)] for dim in range(3)]
    slot_x = lax.rem(cells[0], CX)
    slot_y = lax.rem(cells[1], CY)
    tables_ref[0:SLOT_ROWS] = placed_rows(slot_x, values[0], SLOT_ROWS)
    tables_ref[SLOT_ROWS : 2 * SLOT_ROWS] = placed_rows(slot_x, slopes[0], SLOT_ROWS)
    tables_ref[2 * SLOT_ROWS : 2 * SLOT_ROWS + Y_PAD] = placed_rows(slot_y, values[1], Y_PAD)
    tables_ref[2 * SLOT_ROWS + Y_PAD : 2 * SLOT_ROWS + 2 * Y_PAD] = placed_rows(
        slot_y, slopes[1], Y_PAD
    )
    window = jnp.concatenate(
        [
            placed_rows(base[2], values[2], KZ),
            placed_rows(base[2], slopes[2], KZ),
        ],
        axis=1,
    )
    depth = product((z_high_ref[...], z_low_ref[...]), halves(window), 1, 0)
    depth = halves(depth)
    depth_high_ref[...] = depth[0]
    depth_low_ref[...] = depth[1]
    spread_into(message_ref, start_ref[...], *read_tables(tables_ref), depth, devices)


def transform_in(message_ref, forward_ref, block_high_ref, block_low_ref, rows_count, cols_count):
    gathered = jnp.concatenate(
        [
            jnp.concatenate(
                [
                    message_ref[(r * cols_count + c) * X_PAD : (r * cols_count + c + 1) * X_PAD]
                    for r in range(rows_count)
                ],
                axis=0,
            )
            for c in range(cols_count)
        ],
        axis=1,
    )
    high, low = halves(gathered)
    along = jnp.dot(
        forward_ref[...],
        jnp.concatenate([high, high, low], axis=0),
        preferred_element_type=jnp.float32,
    )
    part = along.shape[1] // cols_count // SPLIT
    along = jnp.concatenate(
        [
            jnp.concatenate(
                [
                    along[:, (c * SPLIT + half) * part : (c * SPLIT + half + 1) * part]
                    for c in range(cols_count)
                ],
                axis=1,
            )
            for half in range(SPLIT)
        ],
        axis=0,
    )
    return product(halves(along), (block_high_ref[...], block_low_ref[...]))


def transform_out(result_ref, values, backward_ref, block_high_ref, block_low_ref, counts):
    rows_count, cols_count = counts
    spread = product(halves(values), (block_high_ref[...], block_low_ref[...]), 1, 1)
    grid_x = spread.shape[0] // SPLIT
    part = spread.shape[1] // cols_count
    spread = jnp.concatenate(
        [
            spread[half * grid_x : (half + 1) * grid_x, c * part : (c + 1) * part]
            for c in range(cols_count)
            for half in range(SPLIT)
        ],
        axis=1,
    )
    high, low = halves(spread)
    along = jnp.dot(
        backward_ref[...],
        jnp.concatenate([high, high, low], axis=0),
        preferred_element_type=jnp.float32,
    )
    width = along.shape[1] // cols_count
    slot_rows = result_ref.shape[0] // (rows_count * cols_count)
    for r in range(rows_count):
        for c in range(cols_count):
            first = (r * cols_count + c) * slot_rows
            result_ref[first : first + X_PAD, :] = along[
                r * X_PAD : (r + 1) * X_PAD, c * width : (c + 1) * width
            ]


def middle_first_body(
    counts,
    message_ref,
    kernel_ref,
    forward_ref,
    backward_ref,
    block_high_ref,
    block_low_ref,
    result_ref,
    wave_ref,
):
    wave = transform_in(message_ref, forward_ref, block_high_ref, block_low_ref, *counts)
    wave_ref[...] = wave
    transform_out(
        result_ref, wave * kernel_ref[...], backward_ref, block_high_ref, block_low_ref, counts
    )


def gather_rows(parts):
    tiles = [
        parts[GROUP * tile : GROUP * tile + GROUP, :] for tile in range(parts.shape[0] // GROUP)
    ]
    return jnp.concatenate(tiles, axis=1)[0 : 3 * RHS]


def row_total(value, rhs):
    row = lax.broadcasted_iota(jnp.int32, value.shape, 0)
    return total(jnp.where(lax.rem(row, RHS) == rhs, value, 0.0))


def total(value):
    return jnp.sum(jnp.sum(value, axis=0, keepdims=True), axis=1, keepdims=True)


def middle_second_body(
    counts,
    message_ref,
    kernel_ref,
    forward_ref,
    backward_ref,
    block_high_ref,
    block_low_ref,
    wave_ref,
    rhs_ref,
    start_ref,
    image_ref,
    second_ref,
    near_ref,
    polar_ref,
    result_ref,
):
    rhs_rows = read_rows(rhs_ref)
    near_rows = gather_rows(near_ref)
    wave = transform_in(message_ref, forward_ref, block_high_ref, block_low_ref, *counts)
    filtered = wave * kernel_ref[...]
    transform_out(result_ref, filtered, backward_ref, block_high_ref, block_low_ref, counts)
    before = wave_ref[...]
    grid_y = CY * counts[1]
    lane = lax.broadcasted_iota(jnp.int32, wave.shape, 1)
    own_rhs = lax.rem(lax.div(lane, grid_y), RHS)
    second = second_ref[...]
    start = start_ref[...]
    image = image_ref[...]
    local_part = second / polar_ref[...] - near_rows - self_coef * second
    slot = lax.broadcasted_iota(jnp.int32, (1, result_ref.shape[1]), 1)
    sums = jnp.zeros((1, result_ref.shape[1]), jnp.float32)
    for rhs in range(RHS):
        mine = own_rhs == rhs
        parts = (
            row_total(rhs_rows * start, rhs),
            row_total(start * image, rhs),
            row_total(second * image, rhs),
            row_total(start * local_part, rhs) + total(jnp.where(mine, before * filtered, 0.0)),
            row_total(second * local_part, rhs) + total(jnp.where(mine, wave * filtered, 0.0)),
        )
        for index, part in enumerate(parts):
            sums = jnp.where(slot == rhs * len(parts) + index, part, sums)
    devices = counts[0] * counts[1]
    result_ref[pl.ds(X_PAD, devices, stride=X_PAD + 1), :] = jnp.broadcast_to(
        sums, (devices, sums.shape[1])
    )


def sample_body(
    devices,
    message_ref,
    tables_ref,
    depth_high_ref,
    depth_low_ref,
    start_ref,
    near_ref,
    polar_ref,
    image_ref,
    second_ref,
    payload_ref,
):
    tables = read_tables(tables_ref)
    depth = (depth_high_ref[...], depth_low_ref[...])
    field = sample_from(message_ref, *tables, depth, devices)
    start = start_ref[...]
    polar = polar_ref[...]
    image = start / polar - gather_rows(near_ref) + field - self_coef * start
    second = polar * image
    image_ref[...] = image
    second_ref[...] = second
    store_payload(payload_ref, second)


def spread_body(
    devices,
    tables_ref,
    depth_high_ref,
    depth_low_ref,
    second_ref,
    result_ref,
):
    depth = (depth_high_ref[...], depth_low_ref[...])
    spread_into(result_ref, second_ref[...], *read_tables(tables_ref), depth, devices)


def final_body(
    devices,
    message_ref,
    tables_ref,
    depth_high_ref,
    depth_low_ref,
    rhs_ref,
    start_ref,
    image_ref,
    second_ref,
    near_ref,
    polar_ref,
    dipole_ref,
    residual_ref,
):
    tables = read_tables(tables_ref)
    depth = (depth_high_ref[...], depth_low_ref[...])
    field = sample_from(message_ref, *tables, depth, devices)
    second = second_ref[...]
    start = start_ref[...]
    image = image_ref[...]
    image_second = second / polar_ref[...] - gather_rows(near_ref) + field - self_coef * second
    sums = jnp.sum(
        message_ref[pl.ds(X_PAD, devices, stride=X_PAD + 1), :], axis=0, keepdims=True
    )
    steps = []
    for rhs in range(RHS):
        progress, start_image, second_image, start_next, second_next = [
            sums[:, rhs * 5 + index : rhs * 5 + index + 1] for index in range(5)
        ]
        step = progress / start_image
        progress_next = progress - 2.0 * step * start_image + step * step * second_image
        grown = 1.0 + progress_next / progress
        curvature = (
            grown * grown * start_image
            - step * grown * (start_next + second_image)
            + step * step * second_next
        )
        steps.append((step, grown, progress_next / curvature))
    row = lax.broadcasted_iota(jnp.int32, (RHS, 1), 0)
    step, grown, step_next = [
        sum(jnp.where(row == rhs, steps[rhs][index], 0.0) for rhs in range(RHS))
        for index in range(3)
    ]
    for dim in range(3):
        rows = slice(dim * RHS, (dim + 1) * RHS)
        direction = grown * start[rows] - step * second[rows]
        image_direction = grown * image[rows] - step * image_second[rows]
        dipole_ref[dim] = step * start[rows] + step_next * direction
        residual_ref[dim] = rhs_ref[dim] - step * image[rows] - step_next * image_direction


def near_base(entry, brick_rows):
    return lax.shift_right_logical(entry, 2) * brick_rows + lax.bitwise_and(entry, 3)


def nearest(places, origin, span):
    return places - span * jnp.floor((places - origin) * (1.0 / span) + 0.5)


def unwrap_near(near, tile_count, spans):
    rows = near.shape[0] // 9
    for dim in range(2):
        own = 4 * rows + dim * tile_count
        origin = near[own : own + 1, 0:1]
        for brick in range(9):
            first = brick * rows + dim * tile_count
            near[first : first + tile_count, :] = nearest(
                near[first : first + tile_count, :], origin, spans[dim]
            )


def pick_rows(picked, near, lists_ref, tile, place, tile_count, quantities, origin, span):
    rows = near.shape[0] // 9
    place = place * lists_ref.shape[1] * quantities * GROUP
    for entry in range(lists_ref.shape[1]):
        base = near_base(lists_ref[tile, entry], rows)
        for quantity in range(quantities):
            values = near[pl.ds(base + quantity * tile_count, 1), :]
            if quantity == 2 and span is not None:
                values = nearest(values, origin, span)
            first = place + (entry * quantities + quantity) * GROUP
            picked[first : first + GROUP, :] = jnp.broadcast_to(values, (GROUP, TILE))


def widen_own(near, quantities, tile_count, tile, place, wide):
    offset = near.shape[0] // 9 * 4
    rows = [
        near[offset + quantity * tile_count + tile : offset + quantity * tile_count + tile + 1, :]
        for quantity in range(quantities)
    ]
    spare = jnp.zeros((TILE - quantities, TILE), jnp.float32)
    columns = jnp.transpose(jnp.concatenate(rows + [spare], axis=0))
    for quantity in range(quantities):
        first = (place * quantities + quantity) * TILE
        wide[first : first + TILE, :] = jnp.broadcast_to(
            columns[:, quantity : quantity + 1], (TILE, TILE)
        )


def add_field(sums, first_term, second_term, apart, moments):
    for rhs in range(RHS):
        moment = [moments[RHS * dim + rhs] for dim in range(3)]
        projected = moment[0] * apart[0] + moment[1] * apart[1] + moment[2] * apart[2]
        weighted = second_term * projected
        for dim in range(3):
            index = RHS * dim + rhs
            sums[index] = sums[index] + (weighted * apart[dim] - first_term * moment[dim])


def finish_sums(field_ref, sums_ref, first_tile, place):
    place = place * 3 * RHS
    lane = lax.broadcasted_iota(jnp.int32, (TILE, TILE), 1)
    merged = jnp.zeros((TILE, TILE), jnp.float32)
    for index in range(3 * RHS):
        first = (place + index) * TILE
        column = jnp.sum(sums_ref[first : first + TILE, :], axis=1, keepdims=True)
        merged = jnp.where(lane == index, column, merged)
    first = (first_tile + place // (3 * RHS)) * GROUP
    field_ref[first : first + GROUP, :] = jnp.transpose(merged)[0:GROUP]


def pair_rows(start, group):
    return pl.ds(pl.multiple_of(start + group * GROUP, GROUP), GROUP)


def wide_rows(start, group, quantity):
    return pl.ds(pl.multiple_of(quantity * TILE + start + group * GROUP, GROUP), GROUP)


def pair_terms(square_dist, damp):
    inverse = lax.rsqrt(square_dist)
    distance = square_dist * inverse
    inverse_sq = inverse * inverse
    inverse_cube = inverse_sq * inverse
    cubed = damp * (distance * square_dist)
    damping = jnp.exp(cubed)
    bell = jnp.exp(-(ewald_beta * ewald_beta) * square_dist)
    stretched = 1.0 + (SCREEN_SCALE * ewald_beta) * distance
    turned = pl.reciprocal(stretched, approx=True)
    turned = turned * (2.0 - stretched * turned)
    series = SCREEN_COEF[-1] * turned + SCREEN_COEF[-2]
    for coef in SCREEN_COEF[-3::-1]:
        series = series * turned + coef
    screen = bell * turned * series
    gaussian = (2.0 * ewald_beta / math.sqrt(math.pi)) * bell
    bare = screen - damping
    first_term = bare * inverse_cube + gaussian * inverse_sq
    second_term = (
        3.0 * (first_term + (cubed * damping) * inverse_cube)
        + (2.0 * ewald_beta * ewald_beta) * gaussian
    ) * inverse_sq
    return first_term, second_term


def step_rows(step, size, offset):
    return pl.ds(pl.multiple_of(step * size + offset, GROUP), GROUP)


def tile_rows(step, rows):
    return pl.ds(pl.multiple_of(step * rows, GROUP), rows)


def start_all(copies):
    for copy in copies:
        copy.start()


def wait_all(copies):
    for copy in copies:
        copy.wait()


def near_copies(sources, near, semaphore):
    rows = sources[0].shape[0]
    return [
        pltpu.make_async_copy(
            source, near.at[index * rows : (index + 1) * rows, :], semaphore.at[index]
        )
        for index, source in enumerate(sources)
    ]


def term_copies(terms, buffers, semaphore, begin, step, size, inward):
    rows = pl.ds(pl.multiple_of((begin + step) * size, GROUP), size)
    place = pl.ds(pl.multiple_of(step * size, GROUP), size)
    copies = []
    for index in range(2):
        far, here = terms[index].at[rows, :], buffers[index].at[place, :]
        ends = (far, here) if inward else (here, far)
        copies.append(pltpu.make_async_copy(*ends, semaphore.at[index, step]))
    return copies


def pair_first_body(
    first_tile,
    last_tile,
    tile_count,
    spans,
    lists_ref,
    up_ref,
    stack_ref,
    down_ref,
    *others,
):
    first_ref, second_ref, field_ref, near_ref = others[-14:-10]
    near, picked, wide, sums_ref, kept, field, first_buffer, second_buffer, semaphore, busy = others[-10:]
    terms = (first_ref, second_ref)
    buffers = (first_buffer, second_buffer)
    copies = near_copies((up_ref, stack_ref, down_ref), near, semaphore.at[0])
    if first_tile > 0:
        copies.append(
            pltpu.make_async_copy(
                others[0], field.at[0 : first_tile * GROUP, :], semaphore.at[0, 3]
            )
        )
    start_all(copies)
    wait_all(copies)
    entries = lists_ref.shape[1]
    rows = near.shape[0] // 9
    quantities = rows // tile_count
    unwrap_near(near, tile_count, spans)
    for brick in range(9):
        kept[brick * 3 * tile_count : (brick + 1) * 3 * tile_count, :] = near[
            brick * rows : brick * rows + 3 * tile_count, :
        ]
    keep = pltpu.make_async_copy(kept, near_ref, semaphore.at[1, 3])
    keep.start()
    for place, tile in enumerate(range(first_tile, last_tile)):
        widen_own(near, 4, tile_count, tile, place, wide)
        own = rows * 4 + 2 * tile_count + tile
        origin = near[own : own + 1, 0:1]
        pick_rows(picked, near, lists_ref, tile, place, tile_count, quantities, origin, spans[2])
    parts = TILE // PAIR_ROWS
    steps = (last_tile - first_tile) * parts

    size = entries * PAIR_ROWS

    def sent(step):
        return term_copies(terms, buffers, busy, first_tile * parts, step, size, False)

    @pl.loop(0, steps)
    def _(step):
        tile = lax.div(step, parts)
        start = lax.rem(step, parts) * PAIR_ROWS
        step_picked = picked.at[tile_rows(tile, entries * quantities * GROUP), :]
        step_wide = wide.at[tile_rows(tile, 4 * TILE), :]
        step_sums = sums_ref.at[tile_rows(tile, 3 * RHS * TILE), :]
        for group in range(PAIR_ROWS // GROUP):
            own = [step_wide[wide_rows(start, group, dim), :] for dim in range(4)]
            own_damp = -thole_a * own[3]
            sums = [jnp.zeros((GROUP, TILE), jnp.float32) for _ in range(3 * RHS)]
            itself = (
                lax.broadcasted_iota(jnp.int32, (GROUP, TILE), 0) + (start + group * GROUP)
            ) == lax.broadcasted_iota(jnp.int32, (GROUP, TILE), 1)
            for entry in range(entries):
                first = entry * quantities * GROUP
                rows = [
                    step_picked[first + quantity * GROUP : first + (quantity + 1) * GROUP, :]
                    for quantity in range(quantities)
                ]
                apart = [rows[dim] - own[dim] for dim in range(3)]
                square_dist = apart[0] * apart[0] + apart[1] * apart[1] + apart[2] * apart[2]
                if entry == 0:
                    square_dist = jnp.where(itself, 1.0, square_dist)
                first_term, second_term = pair_terms(square_dist, own_damp * rows[3])
                if entry == 0:
                    first_term = jnp.where(itself, 0.0, first_term)
                    second_term = jnp.where(itself, 0.0, second_term)
                place = step_rows(step, size, entry * PAIR_ROWS + group * GROUP)
                first_buffer[place, :] = first_term
                second_buffer[place, :] = second_term
                add_field(sums, first_term, second_term, apart, rows[4:])
            for index, value in enumerate(sums):
                step_sums[wide_rows(start, group, index), :] = value
        start_all(sent(step))

    for place in range(last_tile - first_tile):
        finish_sums(field, sums_ref, first_tile, place)
    result = pltpu.make_async_copy(field, field_ref, semaphore.at[1, 2])
    result.start()

    @pl.loop(0, steps)
    def _(step):
        wait_all(sent(step))

    keep.wait()
    result.wait()


def pair_second_body(
    tile_count,
    spans,
    lists_ref,
    near_ref,
    up_ref,
    stack_ref,
    down_ref,
    first_ref,
    second_ref,
    field_ref,
    near,
    near_moment,
    picked,
    picked_moment,
    wide,
    sums_ref,
    field,
    first_buffer,
    second_buffer,
    semaphore,
    busy,
):
    terms = (first_ref, second_ref)
    buffers = (first_buffer, second_buffer)
    parts = TILE // PAIR_ROWS
    steps = tile_count * parts

    entries = lists_ref.shape[1]
    size = entries * PAIR_ROWS

    def fetched(step):
        return term_copies(terms, buffers, busy, 0, step, size, True)

    places = pltpu.make_async_copy(near_ref, near, semaphore.at[1, 3])
    places.start()
    copies = near_copies((up_ref, stack_ref, down_ref), near_moment, semaphore.at[2])
    start_all(copies)

    @pl.loop(0, steps)
    def _(step):
        start_all(fetched(step))

    places.wait()
    for tile in range(tile_count):
        widen_own(near, 3, tile_count, tile, tile, wide)
        own = near.shape[0] // 9 * 4 + 2 * tile_count + tile
        origin = near[own : own + 1, 0:1]
        pick_rows(picked, near, lists_ref, tile, tile, tile_count, 3, origin, spans[2])
    wait_all(copies)
    for tile in range(tile_count):
        pick_rows(
            picked_moment, near_moment, lists_ref, tile, tile, tile_count, 3 * RHS, None, None
        )

    @pl.loop(0, steps)
    def _(step):
        wait_all(fetched(step))
        tile = lax.div(step, parts)
        start = lax.rem(step, parts) * PAIR_ROWS
        step_picked = picked.at[tile_rows(tile, entries * 3 * GROUP), :]
        step_moment = picked_moment.at[tile_rows(tile, entries * 3 * RHS * GROUP), :]
        step_wide = wide.at[tile_rows(tile, 3 * TILE), :]
        step_sums = sums_ref.at[tile_rows(tile, 3 * RHS * TILE), :]
        for group in range(PAIR_ROWS // GROUP):
            own = [step_wide[wide_rows(start, group, dim), :] for dim in range(3)]
            sums = [jnp.zeros((GROUP, TILE), jnp.float32) for _ in range(3 * RHS)]
            for entry in range(entries):
                first = entry * 3 * GROUP
                apart = [
                    step_picked[first + dim * GROUP : first + (dim + 1) * GROUP, :] - own[dim]
                    for dim in range(3)
                ]
                first = first * RHS
                moments = [
                    step_moment[first + index * GROUP : first + (index + 1) * GROUP, :]
                    for index in range(3 * RHS)
                ]
                place = step_rows(step, size, entry * PAIR_ROWS + group * GROUP)
                add_field(sums, first_buffer[place, :], second_buffer[place, :], apart, moments)
            for index, value in enumerate(sums):
                step_sums[wide_rows(start, group, index), :] = value

    for place in range(tile_count):
        finish_sums(field, sums_ref, 0, place)
    result = pltpu.make_async_copy(field, field_ref, semaphore.at[1, 2])
    result.start()
    result.wait()


def shift(source, axis, step):
    count = lax.axis_size(axis)
    return lax.ppermute(source, axis, [(i, (i + step) % count) for i in range(count)])


def both_ways(source, axis):
    return shift(source, axis, 1), source, shift(source, axis, -1)


def whole(shape):
    return pl.BlockSpec(shape, lambda *_: (0,) * len(shape))


def anywhere():
    return pl.BlockSpec(memory_space=pl.ANY)


def join(message, payload):
    left, _, right = both_ways(payload, "col")
    message, left, right = lax.optimization_barrier((message, left, right))
    return message, both_ways(jnp.concatenate([left, payload, right], axis=0), "row")


class Fetched:
    def __init__(self, source, scratch, semaphore):
        self.copy = pltpu.make_async_copy(source, scratch, semaphore)
        self.copy.start()
        self.scratch = scratch
        self.shape = scratch.shape
        self.waiting = True

    def wait(self):
        if self.waiting:
            self.copy.wait()
            self.waiting = False

    def __getitem__(self, index):
        self.wait()
        return self.scratch[index]


def call(body, outs, *operands, after=(), own_block=None):
    fetched = [
        pltpu.VMEM(operand.shape[1:] if index == own_block else operand.shape, operand.dtype)
        for index, operand in enumerate(operands)
    ]
    count = len(operands)

    def run(*refs):
        refs = refs[len(after) :]
        sources, refs = refs[:count], refs[count:]
        results, refs = refs[: len(outs)], refs[len(outs) :]
        targets, written, semaphore = refs[:count], refs[count:-1], refs[-1]
        inputs = []
        for index, source in enumerate(sources):
            if index == own_block:
                place = lax.axis_index("row") * lax.axis_size("col") + lax.axis_index("col")
                source = source.at[place]
            inputs.append(Fetched(source, targets[index], semaphore.at[index]))
        body(*inputs, *written)
        for operand in inputs:
            operand.wait()
        copies = [
            pltpu.make_async_copy(value, result, semaphore.at[count + index])
            for index, (value, result) in enumerate(zip(written, results))
        ]
        for copy in copies:
            copy.start()
        for copy in copies:
            copy.wait()

    return pl.pallas_call(
        run,
        in_specs=[anywhere()] * (len(after) + count),
        out_specs=[anywhere()] * len(outs),
        out_shape=[jax.ShapeDtypeStruct(shape, dtype) for shape, dtype in outs],
        scratch_shapes=fetched
        + [pltpu.VMEM(shape, dtype) for shape, dtype in outs]
        + [pltpu.SemaphoreType.DMA((count + len(outs),))],
        compiler_params=pltpu.CompilerParams(vmem_limit_bytes=VMEM_LIMIT),
        cost_estimate=pl.CostEstimate(
            flops=200_000_000, bytes_accessed=4 << 20, transcendentals=0
        ),
    )(*after, *operands)


def final_call(body, outs, *operands):
    return pl.pallas_call(
        body,
        grid=(1,),
        in_specs=[whole(operand.shape) for operand in operands],
        out_specs=[whole(shape) for shape, _ in outs],
        out_shape=[jax.ShapeDtypeStruct(shape, dtype) for shape, dtype in outs],
        compiler_params=pltpu.CompilerParams(vmem_limit_bytes=SMALL_VMEM_LIMIT),
    )(*operands)


def pair_call(body, outs, scratch, lists, *operands, tiles, cost=8 << 20, aliased=0):
    buffers = (tiles * lists.shape[1] * TILE, TILE)
    first = 1 + len(operands) - aliased
    return pl.pallas_call(
        body,
        in_specs=[pl.BlockSpec(memory_space=pltpu.SMEM)] + [anywhere()] * len(operands),
        out_specs=[anywhere()] * len(outs),
        out_shape=[jax.ShapeDtypeStruct(shape, jnp.float32) for shape in outs],
        scratch_shapes=[pltpu.VMEM(shape, jnp.float32) for shape in scratch + [buffers] * 2]
        + [
            pltpu.SemaphoreType.DMA((3, 4)),
            pltpu.SemaphoreType.DMA((2, tiles * TILE // PAIR_ROWS)),
        ],
        input_output_aliases={first + index: index for index in range(aliased)},
        compiler_params=pltpu.CompilerParams(vmem_limit_bytes=VMEM_LIMIT),
        cost_estimate=pl.CostEstimate(
            flops=80_000_000, bytes_accessed=cost, transcendentals=1 << 21
        ),
    )(lists, *operands)


def exchange(message, devices):
    shape = message.shape
    sent = message.reshape(devices, 1, -1)
    return lax.all_to_all(sent, ("row", "col"), split_axis=0, concat_axis=0, tiled=True).reshape(
        shape
    )


def slab_local(field_rhs, positions, polar, grid_base, tile_lists):
    rows_count = lax.axis_size("row")
    cols_count = lax.axis_size("col")
    counts = (rows_count, cols_count)
    devices = rows_count * cols_count
    lengths = (CX * rows_count, CY * cols_count, KZ)
    spans = tuple(float(length) for length in lengths)
    atoms = polar.shape[-1]
    tile_count = atoms // TILE
    listed = tile_lists.shape[-1]
    tables = slab_tables(rows_count, cols_count)
    f32 = jnp.float32
    rhs = jnp.swapaxes(field_rhs[0, 0], 0, 1)
    place = jnp.swapaxes(positions[0], 0, 1)
    base = jnp.swapaxes(grid_base[0], 0, 1)
    polar = polar.reshape(1, atoms)
    lists = tile_lists[0, 0]
    quantities = 4 + 3 * RHS
    brick_rows = quantities * tile_count
    moment_rows = 3 * RHS * tile_count
    message_shape = (devices * X_PAD, KZ // devices * RHS * Y_PAD)
    last_shape = (devices * (X_PAD + 1), message_shape[1])
    row_shape = (3 * RHS, atoms)

    start, payload = call(pack_body, [(row_shape, f32), ((brick_rows, TILE), f32)], rhs, place, polar)

    def setup(*refs):
        setup_body(lengths, devices, *refs)

    message, splines, depth_high, depth_low = call(
        setup,
        [
            (message_shape, f32),
            ((2 * SLOT_ROWS + 2 * Y_PAD, atoms), f32),
            ((KZ, 2 * atoms), jnp.bfloat16),
            ((KZ, 2 * atoms), jnp.bfloat16),
        ],
        place,
        base,
        start,
        *[jnp.asarray(table) for table in tables["along_z"]],
    )
    constants = (
        jnp.asarray(tables["kernel"]),
        jnp.asarray(tables["forward_x"]),
        jnp.asarray(tables["backward_x"]),
        *[jnp.asarray(table) for table in tables["block"]],
    )
    message, near = join(message, payload)
    arrived = exchange(message, devices)

    def pair_first(first_tile, last_tile, fields, *after):
        def body(*refs):
            pair_first_body(first_tile, last_tile, tile_count, spans, *refs)

        tiles = last_tile - first_tile
        return pair_call(
            body,
            [(tile_count * listed * TILE, TILE)] * 2
            + [(last_tile * GROUP, TILE), (9 * 3 * tile_count, TILE)],
            [
                (9 * brick_rows, TILE),
                (tiles * listed * quantities * GROUP, TILE),
                (tiles * 4 * TILE, TILE),
                (tiles * 3 * RHS * TILE, TILE),
                (9 * 3 * tile_count, TILE),
                (last_tile * GROUP, TILE),
            ],
            lists,
            *near,
            *fields,
            *after,
            tiles=tiles,
            aliased=2 if first_tile > 0 else 0,
        )

    early = pair_first(0, EARLY_TILES, (), message)

    def middle_first(*refs):
        middle_first_body(counts, *refs)

    mixed, wave = call(
        middle_first,
        [(message_shape, f32), (tables["kernel"].shape[1:], f32)],
        arrived,
        *constants,
        after=(early[2],),
        own_block=1,
    )
    returned = exchange(mixed, devices)
    first_term, second_term, direct, near = pair_first(
        EARLY_TILES, tile_count, (early[2],), wave, *early[:2]
    )

    def sample(*refs):
        sample_body(devices, *refs)

    image, second, moments = call(
        sample,
        [(row_shape, f32), (row_shape, f32), ((moment_rows, TILE), f32)],
        returned,
        splines,
        depth_high,
        depth_low,
        start,
        direct,
        polar,
    )

    def spread(*refs):
        spread_body(devices, *refs)

    (message,) = call(spread, [(message_shape, f32)], splines, depth_high, depth_low, second)
    message, near_moments = join(message, moments)
    arrived = exchange(message, devices)

    def pair_second(*refs):
        pair_second_body(tile_count, spans, *refs)

    (direct,) = pair_call(
        pair_second,
        [(tile_count * GROUP, TILE)],
        [
            (9 * 3 * tile_count, TILE),
            (9 * moment_rows, TILE),
            (tile_count * listed * 3 * GROUP, TILE),
            (tile_count * listed * 3 * RHS * GROUP, TILE),
            (tile_count * 3 * TILE, TILE),
            (tile_count * 3 * RHS * TILE, TILE),
            (tile_count * GROUP, TILE),
        ],
        lists,
        near,
        *near_moments,
        first_term,
        second_term,
        tiles=tile_count,
        cost=400 << 20,
    )

    def middle_second(*refs):
        middle_second_body(counts, *refs)

    (mixed,) = call(
        middle_second,
        [(last_shape, f32)],
        arrived,
        *constants,
        wave,
        rhs,
        start,
        image,
        second,
        direct,
        polar,
        own_block=1,
    )
    returned = exchange(mixed, devices)

    def final(*refs):
        final_body(devices, *refs)

    outs = final_call(
        final,
        [(rhs.shape, f32), (rhs.shape, f32)],
        returned,
        splines,
        depth_high,
        depth_low,
        rhs,
        start,
        image,
        second,
        direct,
        polar,
    )
    return tuple(jnp.swapaxes(out, 0, 1)[None, None] for out in outs)


def solution(mesh):
    placed = (
        P("row", "col", None, None, None),
        P("row", "col", None, None),
        P("row", "col", None),
        P("row", "col", None, None),
        P("row", "col", None, None),
    )
    devices = mesh.shape["row"] * mesh.shape["col"]
    return jax.shard_map(
        slab_local if KZ % devices == 0 else pencil_local,
        mesh=mesh,
        in_specs=placed,
        out_specs=(P("row", "col", None, None, None), P("row", "col", None, None, None)),
        check_vma=False,
    )
```

```python
import math

import jax
import jax.numpy as jnp
import ml_dtypes
import numpy as np
from jax import lax
from jax.experimental import pallas as pl
from jax.experimental.pallas import tpu as pltpu
from jax.sharding import PartitionSpec as P

CX = 8
CY = 4
KZ = 256
TILE = 128
RHS = 2
ITERS = 2


ewald_beta = 0.4
thole_a = 0.39
self_coef = 4.0 * ewald_beta**3 / (3.0 * math.sqrt(math.pi))
highest = lax.Precision.HIGHEST


def with_halo(cells, sides, width):
    for axis, dim in sides:
        count = lax.axis_size(axis)
        head = lax.slice_in_dim(cells, 0, width, axis=dim)
        tail = lax.slice_in_dim(cells, cells.shape[dim] - width, cells.shape[dim], axis=dim)
        cells = jnp.concatenate(
            [
                lax.ppermute(tail, axis, [(i, (i + 1) % count) for i in range(count)]),
                cells,
                lax.ppermute(head, axis, [((i + 1) % count, i) for i in range(count)]),
            ],
            axis=dim,
        )
    return cells


def spline_table(fraction):
    previous = {0: jnp.ones_like(fraction)}
    fourth = previous
    for degree in range(2, 6):
        current = {}
        for offset in range(degree):
            abscissa = fraction + offset
            summed = abscissa * previous.get(offset, 0.0) + (degree - abscissa) * previous.get(
                offset - 1, 0.0
            )
            current[offset] = summed / (degree - 1)
        if degree == 4:
            fourth = current
        previous = current
    values = jnp.stack([previous[4 - stencil] for stencil in range(5)])
    slopes = jnp.stack(
        [fourth.get(4 - stencil, 0.0) - fourth.get(3 - stencil, 0.0) for stencil in range(5)]
    )
    return (values, slopes)


def spline_modulus(wave_index, length):
    spline_coef = (1.0 / 24.0, 11.0 / 24.0, 11.0 / 24.0, 1.0 / 24.0)
    cosine_sum = jnp.zeros(wave_index.shape, jnp.float32)
    sine_sum = jnp.zeros(wave_index.shape, jnp.float32)
    for offset in range(4):
        angles = 2.0 * math.pi / length * (wave_index * offset % length).astype(jnp.float32)
        cosine_sum = cosine_sum + spline_coef[offset] * jnp.cos(angles)
        sine_sum = sine_sum + spline_coef[offset] * jnp.sin(angles)
    return cosine_sum * cosine_sum + sine_sum * sine_sum


def folded_square(wave_index, length):
    nearest = jnp.minimum(wave_index, length - wave_index).astype(jnp.float32) / length
    return nearest * nearest


def influence(wave_x, wave_y, wave_z, length_x, length_y, length_z):
    wave_norm = (
        folded_square(wave_x, length_x)
        + folded_square(wave_y, length_y)
        + folded_square(wave_z, length_z)
    )
    modulus = (
        spline_modulus(wave_x, length_x)
        * spline_modulus(wave_y, length_y)
        * spline_modulus(wave_z, length_z)
    )
    excluded = (wave_x * 2 == length_x) | (wave_y * 2 == length_y) | (wave_z * 2 == length_z)
    excluded = excluded | (wave_x == 0) & (wave_y == 0) & (wave_z == 0)
    safe_norm = jnp.where(excluded, 1.0, wave_norm)
    safe_modulus = jnp.where(excluded, 1.0, modulus)
    result = jnp.exp(-(math.pi**2 / ewald_beta**2) * safe_norm) / (
        math.pi * safe_norm * safe_modulus
    )
    return jnp.where(excluded, 0.0, result)


def tile_field(own_static, near_static, near_dipole, box_spans):
    listed_count = near_static.shape[0]
    tile_width = own_static.shape[1]
    box_span = jnp.array(box_spans, dtype=jnp.float32)[None, :, None, None]
    separation = near_static[:, 0:3, None, :] - own_static[None, 0:3, :, None]
    separation = separation - box_span * jnp.floor(separation / box_span + 0.5)
    dist_sq = jnp.sum(separation * separation, axis=1)
    itself = (jnp.arange(listed_count)[:, None, None] == 0) & (
        jnp.arange(tile_width)[:, None] == jnp.arange(tile_width)[None, :]
    )[None]
    safe_sq = jnp.where(itself, 1.0, dist_sq)
    distance = jnp.sqrt(safe_sq)
    scaled = distance / (own_static[3][None, :, None] * near_static[:, 3][:, None, :])
    cubed = thole_a * scaled * scaled * scaled
    damping = jnp.exp(-cubed)
    screen = lax.erfc(ewald_beta * distance)
    gaussian = 2.0 * ewald_beta / math.sqrt(math.pi) * jnp.exp(-(ewald_beta * ewald_beta) * safe_sq)
    inverse_sq = 1.0 / safe_sq
    inverse_cube = inverse_sq / distance
    first_term = (screen - damping) * inverse_cube + gaussian * inverse_sq
    second = (
        3.0 * (screen - (1.0 + cubed) * damping) * inverse_cube * inverse_sq
        + gaussian * (2.0 * ewald_beta * ewald_beta + 3.0 * inverse_sq) * inverse_sq
    )
    first_term = jnp.where(itself, 0.0, first_term)
    second = jnp.where(itself, 0.0, second)
    projected = jnp.sum(near_dipole[:, :, :, None, :] * separation[:, None, :, :, :], axis=2)
    weighted = second[:, None] * projected
    outward = jnp.sum(weighted[:, :, None] * separation[:, None], axis=(0, 4))
    inward = jnp.sum(first_term[:, None, None] * near_dipole[:, :, :, None, :], axis=(0, 4))
    return outward - inward


def hartley(length):
    counter = jnp.arange(length, dtype=jnp.int32)
    angles = (
        2.0 * math.pi / length * (counter[:, None] * counter[None, :] % length).astype(jnp.float32)
    )
    return jnp.cos(angles) + jnp.sin(angles)


def placed_table(first_cell, weights, extent):
    slot_index = jnp.arange(extent, dtype=jnp.int32)[:, None]
    placed = jnp.zeros((extent, first_cell.shape[0]), jnp.float32)
    for stencil in range(5):
        placed = placed + jnp.where(
            slot_index == (first_cell[None, :] + stencil) % extent, weights[stencil][None, :], 0.0
        )
    return placed


def pad_axis(source, axis_pos, leading, trailing):
    widths = [(0, 0)] * source.ndim
    widths[axis_pos] = (leading, trailing)
    return jnp.pad(source, widths)


def fold_cycle(cycle_only, axis_pos, inner_len):
    middle = lax.slice_in_dim(cycle_only, 4, inner_len + 4, axis=axis_pos)
    lower_cycle = lax.slice_in_dim(cycle_only, 0, 2, axis=axis_pos)
    upper_cycle = lax.slice_in_dim(cycle_only, inner_len + 6, inner_len + 8, axis=axis_pos)
    return (
        middle
        + pad_axis(lower_cycle, axis_pos, 0, inner_len - 2)
        + pad_axis(upper_cycle, axis_pos, inner_len - 2, 0)
    )


def clear_inside(extended, extents):
    inside = None
    for axis_pos, inner_len in extents:
        slot_index = lax.broadcasted_iota(jnp.int32, extended.shape, axis_pos)
        within = (slot_index >= 2) & (slot_index < inner_len + 6)
        inside = within if inside is None else inside & within
    return jnp.where(inside, 0.0, extended)


def inner_sum(left_arr, right_arr):
    return lax.psum(jnp.sum(left_arr * right_arr, axis=(1, 2)), ("row", "col"))


def pencil_local(field_rhs, positions, polar, grid_base, tile_lists):
    rows_count = lax.axis_size("row")
    cols_count = lax.axis_size("col")
    grid_x = CX * rows_count
    grid_y = CY * cols_count
    atom_count = polar.shape[-1]
    tile_count = atom_count // TILE
    slab_depth = KZ // tile_count
    window_len = slab_depth + 4
    box_spans = (float(grid_x), float(grid_y), float(KZ))
    own_place = positions[0, 0]
    own_base = grid_base[0, 0]
    own_polar = polar[0, 0]
    lengths = jnp.array([grid_x, grid_y, KZ], dtype=jnp.int32)[:, None]
    cell_index = (own_base + 2) % lengths
    fraction = own_place - cell_index.astype(jnp.float32)
    values, slopes = spline_table(fraction)
    first_x = (own_base[0] - lax.axis_index("row") * CX + 2) % grid_x
    first_y = (own_base[1] - lax.axis_index("col") * CY + 2) % grid_y
    rows_x = placed_table(first_x, values[:, 0], CX + 4)
    slope_x = placed_table(first_x, slopes[:, 0], CX + 4)
    rows_y = placed_table(first_y, values[:, 1], CY + 4)
    slope_y = placed_table(first_y, slopes[:, 1], CY + 4)
    tile_start = jnp.arange(atom_count, dtype=jnp.int32) // TILE * slab_depth
    first_z = (own_base[2] + 2 - tile_start) % KZ
    rows_z = placed_table(first_z, values[:, 2], window_len)
    slope_z = placed_table(first_z, slopes[:, 2], window_len)
    plane_count = (CX + 4) * (CY + 4)
    plane_dx = (slope_x[:, None, :] * rows_y[None, :, :]).reshape(plane_count, atom_count)
    plane_dy = (rows_x[:, None, :] * slope_y[None, :, :]).reshape(plane_count, atom_count)
    plane_flat = (rows_x[:, None, :] * rows_y[None, :, :]).reshape(plane_count, atom_count)
    window_rows = jnp.moveaxis(rows_z.reshape(window_len, tile_count, TILE), 1, 0)
    window_slope = jnp.moveaxis(slope_z.reshape(window_len, tile_count, TILE), 1, 0)
    depth_table = jnp.concatenate([window_rows, window_slope], axis=2)
    grid_scale = 1.0 / (grid_x * grid_y * KZ)
    hartley_x = hartley(grid_x)
    hartley_y = hartley(grid_y)
    hartley_z = hartley(KZ)
    block_y = grid_y // rows_count
    block_z = KZ // cols_count
    wave_x = jnp.arange(grid_x, dtype=jnp.int32)[:, None, None]
    wave_y = (lax.axis_index("row") * block_y + jnp.arange(block_y, dtype=jnp.int32))[None, :, None]
    wave_z = (lax.axis_index("col") * block_z + jnp.arange(block_z, dtype=jnp.int32))[None, None, :]
    kernel = influence(wave_x, wave_y, wave_z, grid_x, grid_y, KZ) * grid_scale
    root_scale = jnp.power(own_polar, 1.0 / 6.0)
    own_static = jnp.concatenate([own_place, root_scale[None]], axis=0)
    near_static = with_halo(own_static[None, None], (("row", 0), ("col", 1)), 1)
    near_static = jnp.moveaxis(near_static.reshape(9, 4, tile_count, TILE), 2, 1).reshape(
        9 * tile_count, 4, TILE
    )
    own_tiles = jnp.moveaxis(own_static.reshape(4, tile_count, TILE), 1, 0)
    own_lists = tile_lists[0, 0]
    polar_wide = own_polar[None, None, :]
    solution = jnp.zeros_like(field_rhs[0, 0])
    residual = field_rhs[0, 0]
    scaled_res = polar_wide * residual
    direction = scaled_res
    progress = inner_sum(residual, scaled_res)
    for iteration in range(ITERS):
        near_dip = with_halo(direction[None, None], (("row", 0), ("col", 1)), 1)
        near_dip = jnp.moveaxis(near_dip.reshape(9, RHS, 3, tile_count, TILE), 3, 1).reshape(
            9 * tile_count, RHS, 3, TILE
        )

        def one_tile(tile_pos):
            picked = own_lists[tile_pos]
            return tile_field(own_tiles[tile_pos], near_static[picked], near_dip[picked], box_spans)

        fields = lax.map(one_tile, jnp.arange(tile_count, dtype=jnp.int32))
        direct = jnp.moveaxis(fields, 0, 2).reshape(RHS, 3, atom_count)
        slope_terms = (
            direction[:, 0, None, :] * plane_dx[None] + direction[:, 1, None, :] * plane_dy[None]
        )
        flat_terms = direction[:, 2, None, :] * plane_flat[None]
        spread_left = jnp.concatenate(
            [
                slope_terms.reshape(RHS, plane_count, tile_count, TILE),
                flat_terms.reshape(RHS, plane_count, tile_count, TILE),
            ],
            axis=3,
        )
        spread_windows = jnp.einsum("sptb,twb->sptw", spread_left, depth_table, precision=highest)
        main_part = spread_windows[..., :slab_depth].reshape(spread_windows.shape[:-2] + (KZ,))
        tail_part = pad_axis(
            spread_windows[..., slab_depth:], spread_windows.ndim - 1, 0, slab_depth - 4
        )
        tail_part = tail_part.reshape(spread_windows.shape[:-2] + (KZ,))[..., : KZ + 4 - slab_depth]
        last_axis = main_part.ndim - 1
        padded_line = pad_axis(main_part, last_axis, 0, 4) + pad_axis(
            tail_part, last_axis, slab_depth, 0
        )
        inner = padded_line[..., 2 : KZ + 2]
        spread_tile = (
            inner
            + pad_axis(padded_line[..., 0:2], last_axis, KZ - 2, 0)
            + pad_axis(padded_line[..., KZ + 2 : KZ + 4], last_axis, 0, KZ - 2)
        ).reshape(RHS, CX + 4, CY + 4, KZ)
        extended = with_halo(spread_tile, (("row", 1), ("col", 2)), 2)
        cycle_only = clear_inside(extended, ((1, CX), (2, CY)))
        folded = fold_cycle(fold_cycle(cycle_only, 1, CX), 2, CY)
        spectrum = jnp.einsum(
            "sxyz,zk->sxyk",
            spread_tile[:, 2 : CX + 2, 2 : CY + 2] + folded,
            hartley_z,
            precision=highest,
        )
        along_y = jnp.einsum(
            "sxyz,yk->sxkz",
            lax.all_to_all(spectrum, "col", split_axis=3, concat_axis=2, tiled=True),
            hartley_y,
            precision=highest,
        )
        along_x = (
            jnp.einsum(
                "sxyz,xk->skyz",
                lax.all_to_all(along_y, "row", split_axis=2, concat_axis=1, tiled=True),
                hartley_x,
                precision=highest,
            )
            * kernel[None]
        )
        mixed_part = jnp.einsum("sxyz,xk->skyz", along_x, hartley_x, precision=highest)
        returned = lax.all_to_all(mixed_part, "row", split_axis=1, concat_axis=2, tiled=True)
        swapped = jnp.einsum("sxyz,yk->sxkz", returned, hartley_y, precision=highest)
        restored = lax.all_to_all(swapped, "col", split_axis=2, concat_axis=3, tiled=True)
        padded = with_halo(
            jnp.einsum("sxyz,zk->sxyk", restored, hartley_z, precision=highest),
            (("row", 1), ("col", 2)),
            2,
        )
        line = padded.reshape(RHS, plane_count, KZ)
        extended_line = jnp.concatenate([line[..., KZ - 2 :], line, line[..., :2]], axis=-1)
        windows = jnp.stack(
            [
                extended_line[..., tile * slab_depth : tile * slab_depth + window_len]
                for tile in range(tile_count)
            ],
            axis=-2,
        )
        sampled = jnp.einsum("sptw,twb->sptb", windows, depth_table, precision=highest)
        with_flat = sampled[..., :TILE].reshape(RHS, plane_count, atom_count)
        with_slope = sampled[..., TILE:].reshape(RHS, plane_count, atom_count)
        recip_part = jnp.stack(
            [
                jnp.sum(with_flat * plane_dx[None], axis=1),
                jnp.sum(with_flat * plane_dy[None], axis=1),
                jnp.sum(with_slope * plane_flat[None], axis=1),
            ],
            axis=1,
        )
        image_field = direction / polar_wide - direct + recip_part - self_coef * direction
        step_size = (progress / inner_sum(direction, image_field))[:, None, None]
        solution = solution + step_size * direction
        residual = residual - step_size * image_field
        scaled_res = polar_wide * residual
        progress_next = inner_sum(residual, scaled_res)
        direction = scaled_res + (progress_next / progress)[:, None, None] * direction
        progress = progress_next
    return (solution[None, None], residual[None, None])


X_PAD = CX + 4
Y_PAD = CY + 4
SLOT_ROWS = 16
SPLIT = 2
VMEM_LIMIT = 60_000_000
SMALL_VMEM_LIMIT = 24_000_000
MIDDLE_VMEM_LIMIT = 56_000_000
ROOMY_BYTES = 12 << 20
EARLY_TILES = 1
PAIR_ROWS = 32
GROUP = 8
SCREEN_SCALE = 0.4
SCREEN_COEF = (
    0.22567588090896606,
    0.2256690263748169,
    0.20785020291805267,
    0.16849851608276367,
    0.14156343042850494,
    -0.005832736846059561,
    0.16930203139781952,
    -0.1830107867717743,
    0.05028456076979637,
)


def halves(value):
    high = value.astype(jnp.bfloat16)
    return high, (value - high.astype(jnp.float32)).astype(jnp.bfloat16)


def halves_np(value):
    value = value.astype(np.float32)
    high = value.astype(ml_dtypes.bfloat16)
    return high, (value - high.astype(np.float32)).astype(ml_dtypes.bfloat16)


def product(left, right, left_dim=1, right_dim=0):
    def one(first, second):
        return lax.dot_general(
            first,
            second,
            (((left_dim,), (right_dim,)), ((), ())),
            preferred_element_type=jnp.float32,
        )

    return one(left[0], right[0]) + (one(left[1], right[0]) + one(left[0], right[1]))


def cas_np(wave, place, length):
    angles = 2.0 * np.pi / length * (wave[:, None] * place[None, :] % length)
    return np.cos(angles) + np.sin(angles)


def modulus_np(wave, length):
    coef = np.array([1.0, 11.0, 11.0, 1.0]) / 24.0
    angles = 2.0 * np.pi / length * (wave[:, None] * np.arange(4)[None, :])
    return (coef * np.cos(angles)).sum(1) ** 2 + (coef * np.sin(angles)).sum(1) ** 2


def influence_np(length_x, length_y, length_z):
    total = np.zeros((length_x, length_y, length_z))
    modulus = np.ones((length_x, length_y, length_z))
    excluded = np.zeros((length_x, length_y, length_z), bool)
    for axis, length in enumerate((length_x, length_y, length_z)):
        wave = np.arange(length)
        shape = [1, 1, 1]
        shape[axis] = length
        total = total + ((np.minimum(wave, length - wave) / length) ** 2).reshape(shape)
        modulus = modulus * modulus_np(wave, length).reshape(shape)
        excluded = excluded | (wave * 2 == length).reshape(shape)
    excluded[0, 0, 0] = True
    safe = np.where(excluded, 1.0, total)
    result = np.exp(-(np.pi**2) / ewald_beta**2 * safe) / (
        np.pi * safe * np.where(excluded, 1.0, modulus)
    )
    return np.where(excluded, 0.0, result) / (length_x * length_y * length_z)


def slab_tables(rows_count, cols_count):
    grid_x = CX * rows_count
    grid_y = CY * cols_count
    devices = rows_count * cols_count
    chunk = KZ // devices
    wave_z = (np.arange(devices)[None, :] * chunk + np.arange(chunk)[:, None]).reshape(-1)
    along_z = cas_np(wave_z, np.arange(KZ), KZ)
    place_x = np.arange(rows_count)[:, None] * CX + np.arange(X_PAD)[None, :] - 2
    along_x = cas_np(np.arange(grid_x), place_x.reshape(-1) % grid_x, grid_x)
    x_high, x_low = halves_np(along_x)
    forward_x = np.concatenate([x_high, x_low, x_high], axis=1)
    backward_x = np.concatenate([x_high.T, x_low.T, x_high.T], axis=1)
    place_y = (np.arange(cols_count)[:, None] * CY + np.arange(Y_PAD)[None, :] - 2) % grid_y
    along_y = cas_np(np.arange(grid_y), place_y.reshape(-1), grid_y)
    along_y = along_y.reshape(grid_y, cols_count, Y_PAD)
    units = chunk * RHS // SPLIT
    block = np.einsum("uv,kcy->cuyvk", np.eye(units), along_y)
    block = block.reshape(cols_count * units * Y_PAD, units * grid_y)
    kernel = influence_np(grid_x, grid_y, KZ).reshape(grid_x, grid_y, devices, chunk)
    kernel = np.transpose(kernel, (2, 0, 3, 1))[:, :, :, None, :]
    kernel = np.broadcast_to(kernel, (devices, grid_x, chunk, RHS, grid_y))
    kernel = kernel.reshape(devices, grid_x, SPLIT, units * grid_y)
    kernel = np.moveaxis(kernel, 2, 1).reshape(devices, SPLIT * grid_x, units * grid_y)
    kernel = kernel.astype(np.float32)
    return dict(
        along_z=halves_np(along_z),
        forward_x=forward_x,
        backward_x=backward_x,
        block=halves_np(block),
        kernel=kernel,
    )


def pack_body(rhs_ref, place_ref, polar_ref, start_ref, payload_ref):
    polar = polar_ref[...]
    start = read_rows(rhs_ref) * polar
    start_ref[...] = start
    place = [place_ref[dim] for dim in range(3)]
    everything = jnp.concatenate(place + [1.0 / jnp.sqrt(polar), start], axis=0)
    store_payload(payload_ref, everything)


def read_rows(rows_ref):
    return jnp.concatenate([rows_ref[dim] for dim in range(3)], axis=0)


def store_payload(payload_ref, everything):
    tile_count = everything.shape[1] // TILE
    for quantity in range(everything.shape[0]):
        for tile in range(tile_count):
            row = quantity * tile_count + tile
            payload_ref[row : row + 1, :] = everything[
                quantity : quantity + 1, tile * TILE : (tile + 1) * TILE
            ]


def placed_rows(slot, weights, extent):
    slot_index = lax.broadcasted_iota(jnp.int32, (extent, slot.shape[1]), 0)
    placed = jnp.zeros((extent, slot.shape[1]), jnp.float32)
    for stencil in range(5):
        target = slot + stencil
        if extent == KZ:
            target = jnp.where(target >= KZ, target - KZ, target)
        placed = placed + jnp.where(slot_index == target, weights[stencil], 0.0)
    return placed


def spread_into(message_ref, moment, rows_x, slope_x, rows_y, slope_y, depth, devices):
    blocks = []
    for step in range(X_PAD):
        flat_x = rows_x[step : step + 1]
        tilt_x = slope_x[step : step + 1]
        for rhs in range(RHS):
            part_x = tilt_x * moment[rhs : rhs + 1]
            part_y = flat_x * moment[RHS + rhs : RHS + rhs + 1]
            part_z = flat_x * moment[2 * RHS + rhs : 2 * RHS + rhs + 1]
            blocks.append(
                jnp.concatenate([part_x * rows_y + part_y * slope_y, part_z * rows_y], axis=1)
            )
    charges = jnp.concatenate(blocks, axis=0)
    spectrum = product(depth, halves(charges), 1, 1)
    slot_rows = message_ref.shape[0] // devices
    chunk = KZ // devices
    width = RHS * Y_PAD
    for step in range(X_PAD):
        message_ref[pl.ds(step, devices, stride=slot_rows), :] = jnp.concatenate(
            [
                spectrum[unit * devices : (unit + 1) * devices, step * width : (step + 1) * width]
                for unit in range(chunk)
            ],
            axis=1,
        )


def sample_from(message_ref, rows_x, slope_x, rows_y, slope_y, depth, devices):
    chunk = KZ // devices
    width = RHS * Y_PAD
    slot_rows = message_ref.shape[0] // devices
    pieces = [
        message_ref[pl.ds(step, devices, stride=slot_rows), :] for step in range(X_PAD)
    ]
    spare = jnp.zeros((devices, KZ - X_PAD * width), jnp.float32)
    spectrum = jnp.concatenate(
        [
            jnp.concatenate(
                [piece[:, unit * width : (unit + 1) * width] for piece in pieces] + [spare], axis=1
            )
            for unit in range(chunk)
        ],
        axis=0,
    )
    spectrum = jnp.transpose(spectrum)[: X_PAD * width]
    sampled = product(halves(spectrum), depth, 1, 0)
    atoms = rows_x.shape[1]
    fields = [None] * (3 * RHS)
    for rhs in range(RHS):
        sum_x = sum_y = sum_z = None
        for step in range(X_PAD):
            first = step * width + rhs * Y_PAD
            flat = sampled[first : first + Y_PAD, :atoms]
            tilt = sampled[first : first + Y_PAD, atoms:]
            part_x = slope_x[step : step + 1] * flat
            part_y = rows_x[step : step + 1] * flat
            part_z = rows_x[step : step + 1] * tilt
            sum_x = part_x if sum_x is None else sum_x + part_x
            sum_y = part_y if sum_y is None else sum_y + part_y
            sum_z = part_z if sum_z is None else sum_z + part_z
        fields[rhs] = jnp.sum(sum_x * rows_y, axis=0, keepdims=True)
        fields[RHS + rhs] = jnp.sum(sum_y * slope_y, axis=0, keepdims=True)
        fields[2 * RHS + rhs] = jnp.sum(sum_z * rows_y, axis=0, keepdims=True)
    return jnp.concatenate(fields, axis=0)


def read_tables(tables_ref):
    return (
        tables_ref[0:X_PAD],
        tables_ref[SLOT_ROWS : SLOT_ROWS + X_PAD],
        tables_ref[2 * SLOT_ROWS : 2 * SLOT_ROWS + Y_PAD],
        tables_ref[2 * SLOT_ROWS + Y_PAD : 2 * SLOT_ROWS + 2 * Y_PAD],
    )


def setup_body(
    lengths,
    devices,
    place_ref,
    base_ref,
    start_ref,
    z_high_ref,
    z_low_ref,
    message_ref,
    tables_ref,
    depth_high_ref,
    depth_low_ref,
):
    base = [base_ref[dim] for dim in range(3)]
    fractions = []
    cells = []
    for dim in range(3):
        cell = base[dim] + 2
        cell = jnp.where(cell >= lengths[dim], cell - lengths[dim], cell)
        cells.append(cell)
        fractions.append(place_ref[dim] - cell.astype(jnp.float32))
    values, slopes = spline_table(jnp.concatenate(fractions, axis=0))
    values = [[values[stencil][dim : dim + 1] for stencil in range(5)] for dim in range(3)]
    slopes = [[slopes[stencil][dim : dim + 1] for stencil in range(5)] for dim in range(3)]
    slot_x = lax.rem(cells[0], CX)
    slot_y = lax.rem(cells[1], CY)
    tables_ref[0:SLOT_ROWS] = placed_rows(slot_x, values[0], SLOT_ROWS)
    tables_ref[SLOT_ROWS : 2 * SLOT_ROWS] = placed_rows(slot_x, slopes[0], SLOT_ROWS)
    tables_ref[2 * SLOT_ROWS : 2 * SLOT_ROWS + Y_PAD] = placed_rows(slot_y, values[1], Y_PAD)
    tables_ref[2 * SLOT_ROWS + Y_PAD : 2 * SLOT_ROWS + 2 * Y_PAD] = placed_rows(
        slot_y, slopes[1], Y_PAD
    )
    window = jnp.concatenate(
        [
            placed_rows(base[2], values[2], KZ),
            placed_rows(base[2], slopes[2], KZ),
        ],
        axis=1,
    )
    depth = product((z_high_ref[...], z_low_ref[...]), halves(window), 1, 0)
    depth = halves(depth)
    depth_high_ref[...] = depth[0]
    depth_low_ref[...] = depth[1]
    spread_into(message_ref, start_ref[...], *read_tables(tables_ref), depth, devices)


def transform_in(message_ref, forward_ref, block_high_ref, block_low_ref, rows_count, cols_count):
    gathered = jnp.concatenate(
        [
            jnp.concatenate(
                [
                    message_ref[(r * cols_count + c) * X_PAD : (r * cols_count + c + 1) * X_PAD]
                    for r in range(rows_count)
                ],
                axis=0,
            )
            for c in range(cols_count)
        ],
        axis=1,
    )
    high, low = halves(gathered)
    along = jnp.dot(
        forward_ref[...],
        jnp.concatenate([high, high, low], axis=0),
        preferred_element_type=jnp.float32,
    )
    part = along.shape[1] // cols_count // SPLIT
    along = jnp.concatenate(
        [
            jnp.concatenate(
                [
                    along[:, (c * SPLIT + half) * part : (c * SPLIT + half + 1) * part]
                    for c in range(cols_count)
                ],
                axis=1,
            )
            for half in range(SPLIT)
        ],
        axis=0,
    )
    return product(halves(along), (block_high_ref[...], block_low_ref[...]))


def transform_out(result_ref, values, backward_ref, block_high_ref, block_low_ref, counts):
    rows_count, cols_count = counts
    spread = product(halves(values), (block_high_ref[...], block_low_ref[...]), 1, 1)
    grid_x = spread.shape[0] // SPLIT
    part = spread.shape[1] // cols_count
    spread = jnp.concatenate(
        [
            spread[half * grid_x : (half + 1) * grid_x, c * part : (c + 1) * part]
            for c in range(cols_count)
            for half in range(SPLIT)
        ],
        axis=1,
    )
    high, low = halves(spread)
    along = jnp.dot(
        backward_ref[...],
        jnp.concatenate([high, high, low], axis=0),
        preferred_element_type=jnp.float32,
    )
    width = along.shape[1] // cols_count
    slot_rows = result_ref.shape[0] // (rows_count * cols_count)
    for r in range(rows_count):
        for c in range(cols_count):
            first = (r * cols_count + c) * slot_rows
            result_ref[first : first + X_PAD, :] = along[
                r * X_PAD : (r + 1) * X_PAD, c * width : (c + 1) * width
            ]


def middle_first_body(
    counts,
    message_ref,
    kernel_ref,
    forward_ref,
    backward_ref,
    block_high_ref,
    block_low_ref,
    result_ref,
    wave_ref,
):
    wave = transform_in(message_ref, forward_ref, block_high_ref, block_low_ref, *counts)
    wave_ref[...] = wave
    transform_out(
        result_ref, wave * kernel_ref[...], backward_ref, block_high_ref, block_low_ref, counts
    )


def gather_rows(parts):
    tiles = [
        parts[GROUP * tile : GROUP * tile + GROUP, :] for tile in range(parts.shape[0] // GROUP)
    ]
    return jnp.concatenate(tiles, axis=1)[0 : 3 * RHS]


def row_total(value, rhs):
    row = lax.broadcasted_iota(jnp.int32, value.shape, 0)
    return total(jnp.where(lax.rem(row, RHS) == rhs, value, 0.0))


def total(value):
    return jnp.sum(jnp.sum(value, axis=0, keepdims=True), axis=1, keepdims=True)


def middle_second_body(
    counts,
    message_ref,
    kernel_ref,
    forward_ref,
    backward_ref,
    block_high_ref,
    block_low_ref,
    wave_ref,
    start_ref,
    carried_ref,
    near_ref,
    polar_ref,
    result_ref,
    local_ref,
):
    near_rows = gather_rows(near_ref)
    wave = transform_in(message_ref, forward_ref, block_high_ref, block_low_ref, *counts)
    filtered = wave * kernel_ref[...]
    transform_out(result_ref, filtered, backward_ref, block_high_ref, block_low_ref, counts)
    before = wave_ref[...]
    grid_y = CY * counts[1]
    lane = lax.broadcasted_iota(jnp.int32, wave.shape, 1)
    own_rhs = lax.rem(lax.div(lane, grid_y), RHS)
    image = carried_ref[0 : 3 * RHS]
    second = carried_ref[8 : 8 + 3 * RHS]
    start = start_ref[...]
    local_part = second / polar_ref[...] - near_rows - self_coef * second
    local_ref[0 : 3 * RHS] = image
    local_ref[8 : 8 + 3 * RHS] = second
    local_ref[16 : 16 + 3 * RHS] = local_part
    local_ref[24 : 24 + 3 * RHS] = start
    slot = lax.broadcasted_iota(jnp.int32, (1, result_ref.shape[1]), 1)
    sums = jnp.zeros((1, result_ref.shape[1]), jnp.float32)
    for rhs in range(RHS):
        mine = own_rhs == rhs
        parts = (
            row_total(start * start / polar_ref[...], rhs),
            row_total(start * image, rhs),
            row_total(second * image, rhs),
            row_total(start * local_part, rhs) + total(jnp.where(mine, before * filtered, 0.0)),
            row_total(second * local_part, rhs) + total(jnp.where(mine, wave * filtered, 0.0)),
        )
        for index, part in enumerate(parts):
            sums = jnp.where(slot == rhs * len(parts) + index, part, sums)
    devices = counts[0] * counts[1]
    result_ref[pl.ds(X_PAD, devices, stride=X_PAD + 1), :] = jnp.broadcast_to(
        sums, (devices, sums.shape[1])
    )


def sample_body(
    devices,
    message_ref,
    tables_ref,
    depth_high_ref,
    depth_low_ref,
    start_ref,
    near_ref,
    polar_ref,
    carried_ref,
    payload_ref,
):
    tables = read_tables(tables_ref)
    depth = (depth_high_ref[...], depth_low_ref[...])
    field = sample_from(message_ref, *tables, depth, devices)
    start = start_ref[...]
    polar = polar_ref[...]
    image = start / polar - gather_rows(near_ref) + field - self_coef * start
    second = polar * image
    carried_ref[0 : 3 * RHS] = image
    carried_ref[8 : 8 + 3 * RHS] = second
    store_payload(payload_ref, second)


def spread_body(
    devices,
    tables_ref,
    depth_high_ref,
    depth_low_ref,
    carried_ref,
    result_ref,
):
    depth = (depth_high_ref[...], depth_low_ref[...])
    second = carried_ref[8 : 8 + 3 * RHS]
    spread_into(result_ref, second, *read_tables(tables_ref), depth, devices)


def final_body(
    devices,
    message_ref,
    tables_ref,
    depth_high_ref,
    depth_low_ref,
    rhs_ref,
    local_ref,
    dipole_ref,
    residual_ref,
):
    tables = read_tables(tables_ref)
    depth = (depth_high_ref[...], depth_low_ref[...])
    field = sample_from(message_ref, *tables, depth, devices)
    image = local_ref[0 : 3 * RHS]
    second = local_ref[8 : 8 + 3 * RHS]
    image_second = local_ref[16 : 16 + 3 * RHS] + field
    start = local_ref[24 : 24 + 3 * RHS]
    sums = jnp.sum(
        message_ref[pl.ds(X_PAD, devices, stride=X_PAD + 1), :], axis=0, keepdims=True
    )
    steps = []
    for rhs in range(RHS):
        progress, start_image, second_image, start_next, second_next = [
            sums[:, rhs * 5 + index : rhs * 5 + index + 1] for index in range(5)
        ]
        step = progress / start_image
        progress_next = progress - 2.0 * step * start_image + step * step * second_image
        grown = 1.0 + progress_next / progress
        curvature = (
            grown * grown * start_image
            - step * grown * (start_next + second_image)
            + step * step * second_next
        )
        steps.append((step, grown, progress_next / curvature))
    row = lax.broadcasted_iota(jnp.int32, (RHS, 1), 0)
    step, grown, step_next = [
        sum(jnp.where(row == rhs, steps[rhs][index], 0.0) for rhs in range(RHS))
        for index in range(3)
    ]
    for dim in range(3):
        rows = slice(dim * RHS, (dim + 1) * RHS)
        direction = grown * start[rows] - step * second[rows]
        image_direction = grown * image[rows] - step * image_second[rows]
        dipole_ref[dim] = step * start[rows] + step_next * direction
        residual_ref[dim] = rhs_ref[dim] - step * image[rows] - step_next * image_direction


def near_base(entry, brick_rows):
    return lax.shift_right_logical(entry, 2) * brick_rows + lax.bitwise_and(entry, 3)


def nearest(places, origin, span):
    return places - span * jnp.floor((places - origin) * (1.0 / span) + 0.5)


def unwrap_near(near, tile_count, spans):
    rows = near.shape[0] // 9
    for dim in range(2):
        own = 4 * rows + dim * tile_count
        origin = near[own : own + 1, 0:1]
        for brick in range(9):
            first = brick * rows + dim * tile_count
            near[first : first + tile_count, :] = nearest(
                near[first : first + tile_count, :], origin, spans[dim]
            )


def pick_rows(picked, near, lists_ref, tile, place, tile_count, quantities, origin, span):
    rows = near.shape[0] // 9
    place = place * lists_ref.shape[1] * quantities * GROUP
    for entry in range(lists_ref.shape[1]):
        base = near_base(lists_ref[tile, entry], rows)
        for quantity in range(quantities):
            values = near[pl.ds(base + quantity * tile_count, 1), :]
            if quantity == 2 and span is not None:
                values = nearest(values, origin, span)
            first = place + (entry * quantities + quantity) * GROUP
            picked[first : first + GROUP, :] = jnp.broadcast_to(values, (GROUP, TILE))


def widen_own(near, quantities, tile_count, tile, place, wide):
    offset = near.shape[0] // 9 * 4
    rows = [
        near[offset + quantity * tile_count + tile : offset + quantity * tile_count + tile + 1, :]
        for quantity in range(quantities)
    ]
    spare = jnp.zeros((TILE - quantities, TILE), jnp.float32)
    columns = jnp.transpose(jnp.concatenate(rows + [spare], axis=0))
    for quantity in range(quantities):
        first = (place * quantities + quantity) * TILE
        wide[first : first + TILE, :] = jnp.broadcast_to(
            columns[:, quantity : quantity + 1], (TILE, TILE)
        )


def add_field(sums, first_term, second_term, apart, moments):
    for rhs in range(RHS):
        moment = [moments[RHS * dim + rhs] for dim in range(3)]
        projected = moment[0] * apart[0] + moment[1] * apart[1] + moment[2] * apart[2]
        weighted = second_term * projected
        for dim in range(3):
            index = RHS * dim + rhs
            sums[index] = sums[index] + (weighted * apart[dim] - first_term * moment[dim])


def finish_sums(field_ref, sums_ref, first_tile, place):
    place = place * 3 * RHS
    lane = lax.broadcasted_iota(jnp.int32, (TILE, TILE), 1)
    merged = jnp.zeros((TILE, TILE), jnp.float32)
    for index in range(3 * RHS):
        first = (place + index) * TILE
        column = jnp.sum(sums_ref[first : first + TILE, :], axis=1, keepdims=True)
        merged = jnp.where(lane == index, column, merged)
    first = (first_tile + place // (3 * RHS)) * GROUP
    field_ref[first : first + GROUP, :] = jnp.transpose(merged)[0:GROUP]


def pair_rows(start, group):
    return pl.ds(pl.multiple_of(start + group * GROUP, GROUP), GROUP)


def wide_rows(start, group, quantity):
    return pl.ds(pl.multiple_of(quantity * TILE + start + group * GROUP, GROUP), GROUP)


def pair_terms(square_dist, damp):
    inverse = lax.rsqrt(square_dist)
    distance = square_dist * inverse
    inverse_sq = inverse * inverse
    inverse_cube = inverse_sq * inverse
    cubed = damp * (distance * square_dist)
    damping = jnp.exp(cubed)
    bell = jnp.exp(-(ewald_beta * ewald_beta) * square_dist)
    stretched = 1.0 + (SCREEN_SCALE * ewald_beta) * distance
    turned = pl.reciprocal(stretched, approx=True)
    turned = turned * (2.0 - stretched * turned)
    series = SCREEN_COEF[-1] * turned + SCREEN_COEF[-2]
    for coef in SCREEN_COEF[-3::-1]:
        series = series * turned + coef
    screen = bell * turned * series
    gaussian = (2.0 * ewald_beta / math.sqrt(math.pi)) * bell
    bare = screen - damping
    first_term = bare * inverse_cube + gaussian * inverse_sq
    second_term = (
        3.0 * (first_term + (cubed * damping) * inverse_cube)
        + (2.0 * ewald_beta * ewald_beta) * gaussian
    ) * inverse_sq
    return first_term, second_term


def step_rows(step, size, offset):
    return pl.ds(pl.multiple_of(step * size + offset, GROUP), GROUP)


def tile_rows(step, rows):
    return pl.ds(pl.multiple_of(step * rows, GROUP), rows)


def start_all(copies):
    for copy in copies:
        copy.start()


def wait_all(copies):
    for copy in copies:
        copy.wait()


def near_copies(sources, near, semaphore):
    rows = sources[0].shape[0]
    return [
        pltpu.make_async_copy(
            source, near.at[index * rows : (index + 1) * rows, :], semaphore.at[index]
        )
        for index, source in enumerate(sources)
    ]


def term_copies(terms, buffers, semaphore, begin, step, size, inward):
    rows = pl.ds(pl.multiple_of((begin + step) * size, GROUP), size)
    place = pl.ds(pl.multiple_of(step * size, GROUP), size)
    copies = []
    for index in range(2):
        far, here = terms[index].at[rows, :], buffers[index].at[place, :]
        ends = (far, here) if inward else (here, far)
        copies.append(pltpu.make_async_copy(*ends, semaphore.at[index, step]))
    return copies


def pair_first_body(
    first_tile,
    last_tile,
    tile_count,
    spans,
    lists_ref,
    up_ref,
    stack_ref,
    down_ref,
    *others,
):
    first_ref, second_ref, field_ref, near_ref = others[-14:-10]
    near, picked, wide, sums_ref, kept, field, first_buffer, second_buffer, semaphore, busy = others[-10:]
    terms = (first_ref, second_ref)
    buffers = (first_buffer, second_buffer)
    copies = near_copies((up_ref, stack_ref, down_ref), near, semaphore.at[0])
    if first_tile > 0:
        copies.append(
            pltpu.make_async_copy(
                others[0], field.at[0 : first_tile * GROUP, :], semaphore.at[0, 3]
            )
        )
    start_all(copies)
    wait_all(copies)
    entries = lists_ref.shape[1]
    rows = near.shape[0] // 9
    quantities = rows // tile_count
    unwrap_near(near, tile_count, spans)
    for brick in range(9):
        kept[brick * 3 * tile_count : (brick + 1) * 3 * tile_count, :] = near[
            brick * rows : brick * rows + 3 * tile_count, :
        ]
    keep = pltpu.make_async_copy(kept, near_ref, semaphore.at[1, 3])
    keep.start()
    for place, tile in enumerate(range(first_tile, last_tile)):
        widen_own(near, 4, tile_count, tile, place, wide)
        own = rows * 4 + 2 * tile_count + tile
        origin = near[own : own + 1, 0:1]
        pick_rows(picked, near, lists_ref, tile, place, tile_count, quantities, origin, spans[2])
    parts = TILE // PAIR_ROWS
    steps = (last_tile - first_tile) * parts

    size = entries * PAIR_ROWS

    def sent(step):
        return term_copies(terms, buffers, busy, first_tile * parts, step, size, False)

    @pl.loop(0, steps)
    def _(step):
        tile = lax.div(step, parts)
        start = lax.rem(step, parts) * PAIR_ROWS
        step_picked = picked.at[tile_rows(tile, entries * quantities * GROUP), :]
        step_wide = wide.at[tile_rows(tile, 4 * TILE), :]
        step_sums = sums_ref.at[tile_rows(tile, 3 * RHS * TILE), :]
        for group in range(PAIR_ROWS // GROUP):
            own = [step_wide[wide_rows(start, group, dim), :] for dim in range(4)]
            own_damp = -thole_a * own[3]
            sums = [jnp.zeros((GROUP, TILE), jnp.float32) for _ in range(3 * RHS)]
            itself = (
                lax.broadcasted_iota(jnp.int32, (GROUP, TILE), 0) + (start + group * GROUP)
            ) == lax.broadcasted_iota(jnp.int32, (GROUP, TILE), 1)
            for entry in range(entries):
                first = entry * quantities * GROUP
                rows = [
                    step_picked[first + quantity * GROUP : first + (quantity + 1) * GROUP, :]
                    for quantity in range(quantities)
                ]
                apart = [rows[dim] - own[dim] for dim in range(3)]
                square_dist = apart[0] * apart[0] + apart[1] * apart[1] + apart[2] * apart[2]
                if entry == 0:
                    square_dist = jnp.where(itself, 1.0, square_dist)
                first_term, second_term = pair_terms(square_dist, own_damp * rows[3])
                if entry == 0:
                    first_term = jnp.where(itself, 0.0, first_term)
                    second_term = jnp.where(itself, 0.0, second_term)
                place = step_rows(step, size, entry * PAIR_ROWS + group * GROUP)
                first_buffer[place, :] = first_term
                second_buffer[place, :] = second_term
                add_field(sums, first_term, second_term, apart, rows[4:])
            for index, value in enumerate(sums):
                step_sums[wide_rows(start, group, index), :] = value
        start_all(sent(step))

    for place in range(last_tile - first_tile):
        finish_sums(field, sums_ref, first_tile, place)
    result = pltpu.make_async_copy(field, head_of(field_ref, field), semaphore.at[1, 2])
    result.start()

    @pl.loop(0, steps)
    def _(step):
        wait_all(sent(step))

    keep.wait()
    result.wait()


def pair_second_body(
    tile_count,
    spans,
    lists_ref,
    near_ref,
    up_ref,
    stack_ref,
    down_ref,
    first_ref,
    second_ref,
    field_ref,
    near,
    near_moment,
    picked,
    picked_moment,
    wide,
    sums_ref,
    field,
    first_buffer,
    second_buffer,
    semaphore,
    busy,
):
    terms = (first_ref, second_ref)
    buffers = (first_buffer, second_buffer)
    parts = TILE // PAIR_ROWS
    steps = tile_count * parts

    entries = lists_ref.shape[1]
    size = entries * PAIR_ROWS

    def fetched(step):
        return term_copies(terms, buffers, busy, 0, step, size, True)

    places = pltpu.make_async_copy(near_ref, near, semaphore.at[1, 3])
    places.start()
    copies = near_copies((up_ref, stack_ref, down_ref), near_moment, semaphore.at[2])
    start_all(copies)

    @pl.loop(0, steps)
    def _(step):
        start_all(fetched(step))

    places.wait()
    for tile in range(tile_count):
        widen_own(near, 3, tile_count, tile, tile, wide)
        own = near.shape[0] // 9 * 4 + 2 * tile_count + tile
        origin = near[own : own + 1, 0:1]
        pick_rows(picked, near, lists_ref, tile, tile, tile_count, 3, origin, spans[2])
    wait_all(copies)
    for tile in range(tile_count):
        pick_rows(
            picked_moment, near_moment, lists_ref, tile, tile, tile_count, 3 * RHS, None, None
        )

    @pl.loop(0, steps)
    def _(step):
        wait_all(fetched(step))
        tile = lax.div(step, parts)
        start = lax.rem(step, parts) * PAIR_ROWS
        step_picked = picked.at[tile_rows(tile, entries * 3 * GROUP), :]
        step_moment = picked_moment.at[tile_rows(tile, entries * 3 * RHS * GROUP), :]
        step_wide = wide.at[tile_rows(tile, 3 * TILE), :]
        step_sums = sums_ref.at[tile_rows(tile, 3 * RHS * TILE), :]
        for group in range(PAIR_ROWS // GROUP):
            own = [step_wide[wide_rows(start, group, dim), :] for dim in range(3)]
            sums = [jnp.zeros((GROUP, TILE), jnp.float32) for _ in range(3 * RHS)]
            for entry in range(entries):
                first = entry * 3 * GROUP
                apart = [
                    step_picked[first + dim * GROUP : first + (dim + 1) * GROUP, :] - own[dim]
                    for dim in range(3)
                ]
                first = first * RHS
                moments = [
                    step_moment[first + index * GROUP : first + (index + 1) * GROUP, :]
                    for index in range(3 * RHS)
                ]
                place = step_rows(step, size, entry * PAIR_ROWS + group * GROUP)
                add_field(sums, first_buffer[place, :], second_buffer[place, :], apart, moments)
            for index, value in enumerate(sums):
                step_sums[wide_rows(start, group, index), :] = value

    for place in range(tile_count):
        finish_sums(field, sums_ref, 0, place)
    result = pltpu.make_async_copy(field, head_of(field_ref, field), semaphore.at[1, 2])
    result.start()
    result.wait()


def shift(source, axis, step):
    count = lax.axis_size(axis)
    return lax.ppermute(source, axis, [(i, (i + step) % count) for i in range(count)])


def both_ways(source, axis):
    return shift(source, axis, 1), source, shift(source, axis, -1)


def whole(shape):
    return pl.BlockSpec(shape, lambda *_: (0,) * len(shape))


def anywhere():
    return pl.BlockSpec(memory_space=pl.ANY)


def join(message, payload):
    left, _, right = both_ways(payload, "col")
    message, left, right = lax.optimization_barrier((message, left, right))
    return message, both_ways(jnp.concatenate([left, payload, right], axis=0), "row")


class Fetched:
    def __init__(self, source, scratch, semaphore):
        self.copy = pltpu.make_async_copy(source, scratch, semaphore)
        self.copy.start()
        self.scratch = scratch
        self.shape = scratch.shape
        self.waiting = True

    def wait(self):
        if self.waiting:
            self.copy.wait()
            self.waiting = False

    def __getitem__(self, index):
        self.wait()
        return self.scratch[index]


class Head:
    def __init__(self, array, shape):
        self.array = array
        self.shape = shape
        self.dtype = array.dtype


def roomy(shape):
    return (ROOMY_BYTES // 4 // shape[1], shape[1])


def head_of(far, here):
    if far.shape == here.shape:
        return far
    return far.at[0 : here.shape[0], :]


def call(body, outs, *operands, after=(), own_block=None, near=0, large=(), vmem=VMEM_LIMIT):
    count = len(operands)
    fetched = [
        pltpu.VMEM(operand.shape[1:] if index == own_block else operand.shape, operand.dtype)
        for index, operand in enumerate(operands)
        if index >= near
    ]
    arrays = [operand.array if isinstance(operand, Head) else operand for operand in operands]

    def run(*refs):
        refs = refs[len(after) :]
        sources, refs = refs[:count], refs[count:]
        results, refs = refs[: len(outs)], refs[len(outs) :]
        targets, written, semaphore = refs[: count - near], refs[count - near : -1], refs[-1]
        inputs = list(sources[:near])
        for index in range(near, count):
            source = sources[index]
            if index == own_block:
                place = lax.axis_index("row") * lax.axis_size("col") + lax.axis_index("col")
                source = source.at[place]
            else:
                source = head_of(source, targets[index - near])
            inputs.append(Fetched(source, targets[index - near], semaphore.at[index]))
        body(*inputs, *written)
        for operand in inputs[near:]:
            operand.wait()
        copies = [
            pltpu.make_async_copy(value, head_of(result, value), semaphore.at[count + index])
            for index, (value, result) in enumerate(zip(written, results))
        ]
        for copy in copies:
            copy.start()
        for copy in copies:
            copy.wait()

    return pl.pallas_call(
        run,
        in_specs=[anywhere()] * len(after)
        + [pl.BlockSpec(memory_space=pltpu.VMEM)] * near
        + [anywhere()] * (count - near),
        out_specs=[anywhere()] * len(outs),
        out_shape=[
            jax.ShapeDtypeStruct(roomy(shape) if index in large else shape, dtype)
            for index, (shape, dtype) in enumerate(outs)
        ],
        scratch_shapes=fetched
        + [pltpu.VMEM(shape, dtype) for shape, dtype in outs]
        + [pltpu.SemaphoreType.DMA((count + len(outs),))],
        compiler_params=pltpu.CompilerParams(vmem_limit_bytes=vmem),
        cost_estimate=pl.CostEstimate(
            flops=200_000_000, bytes_accessed=4 << 20, transcendentals=0
        ),
    )(*after, *arrays)


def final_call(body, outs, *operands):
    return pl.pallas_call(
        body,
        grid=(1,),
        in_specs=[whole(operand.shape) for operand in operands],
        out_specs=[whole(shape) for shape, _ in outs],
        out_shape=[jax.ShapeDtypeStruct(shape, dtype) for shape, dtype in outs],
        compiler_params=pltpu.CompilerParams(vmem_limit_bytes=SMALL_VMEM_LIMIT),
    )(*operands)


def pair_call(body, outs, scratch, lists, *operands, tiles, large, aliased=0):
    buffers = (tiles * lists.shape[1] * TILE, TILE)
    first = 1 + len(operands) - aliased
    return pl.pallas_call(
        body,
        in_specs=[pl.BlockSpec(memory_space=pltpu.SMEM)] + [anywhere()] * len(operands),
        out_specs=[anywhere()] * len(outs),
        out_shape=[
            jax.ShapeDtypeStruct(roomy(shape) if index == large else shape, jnp.float32)
            for index, shape in enumerate(outs)
        ],
        scratch_shapes=[pltpu.VMEM(shape, jnp.float32) for shape in scratch + [buffers] * 2]
        + [
            pltpu.SemaphoreType.DMA((3, 4)),
            pltpu.SemaphoreType.DMA((2, tiles * TILE // PAIR_ROWS)),
        ],
        input_output_aliases={first + index: index for index in range(aliased)},
        compiler_params=pltpu.CompilerParams(vmem_limit_bytes=VMEM_LIMIT),
        cost_estimate=pl.CostEstimate(
            flops=80_000_000, bytes_accessed=8 << 20, transcendentals=1 << 21
        ),
    )(lists, *operands)


def exchange(message, devices):
    shape = message.shape
    sent = message.reshape(devices, 1, -1)
    return lax.all_to_all(sent, ("row", "col"), split_axis=0, concat_axis=0, tiled=True).reshape(
        shape
    )


def slab_local(field_rhs, positions, polar, grid_base, tile_lists):
    rows_count = lax.axis_size("row")
    cols_count = lax.axis_size("col")
    counts = (rows_count, cols_count)
    devices = rows_count * cols_count
    lengths = (CX * rows_count, CY * cols_count, KZ)
    spans = tuple(float(length) for length in lengths)
    atoms = polar.shape[-1]
    tile_count = atoms // TILE
    listed = tile_lists.shape[-1]
    tables = slab_tables(rows_count, cols_count)
    f32 = jnp.float32
    rhs = jnp.swapaxes(field_rhs[0, 0], 0, 1)
    place = jnp.swapaxes(positions[0], 0, 1)
    base = jnp.swapaxes(grid_base[0], 0, 1)
    polar = polar.reshape(1, atoms)
    lists = tile_lists[0, 0]
    quantities = 4 + 3 * RHS
    brick_rows = quantities * tile_count
    moment_rows = 3 * RHS * tile_count
    message_shape = (devices * X_PAD, KZ // devices * RHS * Y_PAD)
    last_shape = (devices * (X_PAD + 1), message_shape[1])
    row_shape = (3 * RHS, atoms)

    start, payload = call(pack_body, [(row_shape, f32), ((brick_rows, TILE), f32)], rhs, place, polar)

    def setup(*refs):
        setup_body(lengths, devices, *refs)

    message, splines, depth_high, depth_low = call(
        setup,
        [
            (message_shape, f32),
            ((2 * SLOT_ROWS + 2 * Y_PAD, atoms), f32),
            ((KZ, 2 * atoms), jnp.bfloat16),
            ((KZ, 2 * atoms), jnp.bfloat16),
        ],
        place,
        base,
        start,
        *[jnp.asarray(table) for table in tables["along_z"]],
    )
    constants = (
        jnp.asarray(tables["kernel"]),
        jnp.asarray(tables["forward_x"]),
        jnp.asarray(tables["backward_x"]),
        *[jnp.asarray(table) for table in tables["block"]],
    )
    message, near = join(message, payload)
    arrived = exchange(message, devices)

    def pair_first(first_tile, last_tile, fields, *after):
        def body(*refs):
            pair_first_body(first_tile, last_tile, tile_count, spans, *refs)

        tiles = last_tile - first_tile
        return pair_call(
            body,
            [(tile_count * listed * TILE, TILE)] * 2
            + [(last_tile * GROUP, TILE), (9 * 3 * tile_count, TILE)],
            [
                (9 * brick_rows, TILE),
                (tiles * listed * quantities * GROUP, TILE),
                (tiles * 4 * TILE, TILE),
                (tiles * 3 * RHS * TILE, TILE),
                (9 * 3 * tile_count, TILE),
                (last_tile * GROUP, TILE),
            ],
            lists,
            *near,
            *fields,
            *after,
            tiles=tiles,
            large=2 if first_tile > 0 else None,
            aliased=2 if first_tile > 0 else 0,
        )

    early = pair_first(0, EARLY_TILES, (), message)

    def middle_first(*refs):
        middle_first_body(counts, *refs)

    arrived, early = lax.optimization_barrier((arrived, tuple(early)))
    wave_shape = tables["kernel"].shape[1:]
    mixed, wave = call(
        middle_first,
        [(message_shape, f32), (wave_shape, f32)],
        arrived,
        *constants,
        own_block=1,
        near=1,
        large=(1,),
        vmem=MIDDLE_VMEM_LIMIT,
    )
    returned = exchange(mixed, devices)
    first_term, second_term, direct, near = pair_first(
        EARLY_TILES, tile_count, (early[2],), wave, *early[:2]
    )

    def sample(*refs):
        sample_body(devices, *refs)

    carried_shape = (16, atoms)
    field_shape = (tile_count * GROUP, TILE)
    carried, moments = call(
        sample,
        [(carried_shape, f32), ((moment_rows, TILE), f32)],
        returned,
        splines,
        depth_high,
        depth_low,
        start,
        Head(direct, field_shape),
        polar,
        near=1,
        large=(0,),
        vmem=MIDDLE_VMEM_LIMIT,
    )

    def spread(*refs):
        spread_body(devices, *refs)

    (message,) = call(
        spread,
        [(message_shape, f32)],
        splines,
        depth_high,
        depth_low,
        Head(carried, carried_shape),
    )
    message, near_moments = join(message, moments)
    arrived = exchange(message, devices)

    def pair_second(*refs):
        pair_second_body(tile_count, spans, *refs)

    (direct,) = pair_call(
        pair_second,
        [(tile_count * GROUP, TILE)],
        [
            (9 * 3 * tile_count, TILE),
            (9 * moment_rows, TILE),
            (tile_count * listed * 3 * GROUP, TILE),
            (tile_count * listed * 3 * RHS * GROUP, TILE),
            (tile_count * 3 * TILE, TILE),
            (tile_count * 3 * RHS * TILE, TILE),
            (tile_count * GROUP, TILE),
        ],
        lists,
        near,
        *near_moments,
        first_term,
        second_term,
        tiles=tile_count,
        large=0,
    )

    def middle_second(*refs):
        middle_second_body(counts, *refs)

    mixed, local = call(
        middle_second,
        [(last_shape, f32), ((32, atoms), f32)],
        arrived,
        *constants,
        Head(wave, wave_shape),
        start,
        Head(carried, carried_shape),
        Head(direct, field_shape),
        polar,
        own_block=1,
        near=1,
        vmem=MIDDLE_VMEM_LIMIT,
    )
    returned = exchange(mixed, devices)

    def final(*refs):
        final_body(devices, *refs)

    outs = final_call(
        final,
        [(rhs.shape, f32), (rhs.shape, f32)],
        returned,
        splines,
        depth_high,
        depth_low,
        rhs,
        local,
    )
    return tuple(jnp.swapaxes(out, 0, 1)[None, None] for out in outs)


def solution(mesh):
    placed = (
        P("row", "col", None, None, None),
        P("row", "col", None, None),
        P("row", "col", None),
        P("row", "col", None, None),
        P("row", "col", None, None),
    )
    devices = mesh.shape["row"] * mesh.shape["col"]
    return jax.shard_map(
        slab_local if KZ % devices == 0 else pencil_local,
        mesh=mesh,
        in_specs=placed,
        out_specs=(P("row", "col", None, None, None), P("row", "col", None, None, None)),
        check_vma=False,
    )
```

```python
import math

import jax
import jax.numpy as jnp
import ml_dtypes
import numpy as np
from jax import lax
from jax.experimental import pallas as pl
from jax.experimental.pallas import tpu as pltpu
from jax.sharding import PartitionSpec as P

CX = 8
CY = 4
KZ = 256
TILE = 128
RHS = 2
ITERS = 2


ewald_beta = 0.4
thole_a = 0.39
self_coef = 4.0 * ewald_beta**3 / (3.0 * math.sqrt(math.pi))
highest = lax.Precision.HIGHEST


def with_halo(cells, sides, width):
    for axis, dim in sides:
        count = lax.axis_size(axis)
        head = lax.slice_in_dim(cells, 0, width, axis=dim)
        tail = lax.slice_in_dim(cells, cells.shape[dim] - width, cells.shape[dim], axis=dim)
        cells = jnp.concatenate(
            [
                lax.ppermute(tail, axis, [(i, (i + 1) % count) for i in range(count)]),
                cells,
                lax.ppermute(head, axis, [((i + 1) % count, i) for i in range(count)]),
            ],
            axis=dim,
        )
    return cells


def spline_table(fraction):
    previous = {0: jnp.ones_like(fraction)}
    fourth = previous
    for degree in range(2, 6):
        current = {}
        for offset in range(degree):
            abscissa = fraction + offset
            summed = abscissa * previous.get(offset, 0.0) + (degree - abscissa) * previous.get(
                offset - 1, 0.0
            )
            current[offset] = summed / (degree - 1)
        if degree == 4:
            fourth = current
        previous = current
    values = jnp.stack([previous[4 - stencil] for stencil in range(5)])
    slopes = jnp.stack(
        [fourth.get(4 - stencil, 0.0) - fourth.get(3 - stencil, 0.0) for stencil in range(5)]
    )
    return (values, slopes)


def spline_modulus(wave_index, length):
    spline_coef = (1.0 / 24.0, 11.0 / 24.0, 11.0 / 24.0, 1.0 / 24.0)
    cosine_sum = jnp.zeros(wave_index.shape, jnp.float32)
    sine_sum = jnp.zeros(wave_index.shape, jnp.float32)
    for offset in range(4):
        angles = 2.0 * math.pi / length * (wave_index * offset % length).astype(jnp.float32)
        cosine_sum = cosine_sum + spline_coef[offset] * jnp.cos(angles)
        sine_sum = sine_sum + spline_coef[offset] * jnp.sin(angles)
    return cosine_sum * cosine_sum + sine_sum * sine_sum


def folded_square(wave_index, length):
    nearest = jnp.minimum(wave_index, length - wave_index).astype(jnp.float32) / length
    return nearest * nearest


def influence(wave_x, wave_y, wave_z, length_x, length_y, length_z):
    wave_norm = (
        folded_square(wave_x, length_x)
        + folded_square(wave_y, length_y)
        + folded_square(wave_z, length_z)
    )
    modulus = (
        spline_modulus(wave_x, length_x)
        * spline_modulus(wave_y, length_y)
        * spline_modulus(wave_z, length_z)
    )
    excluded = (wave_x * 2 == length_x) | (wave_y * 2 == length_y) | (wave_z * 2 == length_z)
    excluded = excluded | (wave_x == 0) & (wave_y == 0) & (wave_z == 0)
    safe_norm = jnp.where(excluded, 1.0, wave_norm)
    safe_modulus = jnp.where(excluded, 1.0, modulus)
    result = jnp.exp(-(math.pi**2 / ewald_beta**2) * safe_norm) / (
        math.pi * safe_norm * safe_modulus
    )
    return jnp.where(excluded, 0.0, result)


def tile_field(own_static, near_static, near_dipole, box_spans):
    listed_count = near_static.shape[0]
    tile_width = own_static.shape[1]
    box_span = jnp.array(box_spans, dtype=jnp.float32)[None, :, None, None]
    separation = near_static[:, 0:3, None, :] - own_static[None, 0:3, :, None]
    separation = separation - box_span * jnp.floor(separation / box_span + 0.5)
    dist_sq = jnp.sum(separation * separation, axis=1)
    itself = (jnp.arange(listed_count)[:, None, None] == 0) & (
        jnp.arange(tile_width)[:, None] == jnp.arange(tile_width)[None, :]
    )[None]
    safe_sq = jnp.where(itself, 1.0, dist_sq)
    distance = jnp.sqrt(safe_sq)
    scaled = distance / (own_static[3][None, :, None] * near_static[:, 3][:, None, :])
    cubed = thole_a * scaled * scaled * scaled
    damping = jnp.exp(-cubed)
    screen = lax.erfc(ewald_beta * distance)
    gaussian = 2.0 * ewald_beta / math.sqrt(math.pi) * jnp.exp(-(ewald_beta * ewald_beta) * safe_sq)
    inverse_sq = 1.0 / safe_sq
    inverse_cube = inverse_sq / distance
    first_term = (screen - damping) * inverse_cube + gaussian * inverse_sq
    second = (
        3.0 * (screen - (1.0 + cubed) * damping) * inverse_cube * inverse_sq
        + gaussian * (2.0 * ewald_beta * ewald_beta + 3.0 * inverse_sq) * inverse_sq
    )
    first_term = jnp.where(itself, 0.0, first_term)
    second = jnp.where(itself, 0.0, second)
    projected = jnp.sum(near_dipole[:, :, :, None, :] * separation[:, None, :, :, :], axis=2)
    weighted = second[:, None] * projected
    outward = jnp.sum(weighted[:, :, None] * separation[:, None], axis=(0, 4))
    inward = jnp.sum(first_term[:, None, None] * near_dipole[:, :, :, None, :], axis=(0, 4))
    return outward - inward


def hartley(length):
    counter = jnp.arange(length, dtype=jnp.int32)
    angles = (
        2.0 * math.pi / length * (counter[:, None] * counter[None, :] % length).astype(jnp.float32)
    )
    return jnp.cos(angles) + jnp.sin(angles)


def placed_table(first_cell, weights, extent):
    slot_index = jnp.arange(extent, dtype=jnp.int32)[:, None]
    placed = jnp.zeros((extent, first_cell.shape[0]), jnp.float32)
    for stencil in range(5):
        placed = placed + jnp.where(
            slot_index == (first_cell[None, :] + stencil) % extent, weights[stencil][None, :], 0.0
        )
    return placed


def pad_axis(source, axis_pos, leading, trailing):
    widths = [(0, 0)] * source.ndim
    widths[axis_pos] = (leading, trailing)
    return jnp.pad(source, widths)


def fold_cycle(cycle_only, axis_pos, inner_len):
    middle = lax.slice_in_dim(cycle_only, 4, inner_len + 4, axis=axis_pos)
    lower_cycle = lax.slice_in_dim(cycle_only, 0, 2, axis=axis_pos)
    upper_cycle = lax.slice_in_dim(cycle_only, inner_len + 6, inner_len + 8, axis=axis_pos)
    return (
        middle
        + pad_axis(lower_cycle, axis_pos, 0, inner_len - 2)
        + pad_axis(upper_cycle, axis_pos, inner_len - 2, 0)
    )


def clear_inside(extended, extents):
    inside = None
    for axis_pos, inner_len in extents:
        slot_index = lax.broadcasted_iota(jnp.int32, extended.shape, axis_pos)
        within = (slot_index >= 2) & (slot_index < inner_len + 6)
        inside = within if inside is None else inside & within
    return jnp.where(inside, 0.0, extended)


def inner_sum(left_arr, right_arr):
    return lax.psum(jnp.sum(left_arr * right_arr, axis=(1, 2)), ("row", "col"))


def pencil_local(field_rhs, positions, polar, grid_base, tile_lists):
    rows_count = lax.axis_size("row")
    cols_count = lax.axis_size("col")
    grid_x = CX * rows_count
    grid_y = CY * cols_count
    atom_count = polar.shape[-1]
    tile_count = atom_count // TILE
    slab_depth = KZ // tile_count
    window_len = slab_depth + 4
    box_spans = (float(grid_x), float(grid_y), float(KZ))
    own_place = positions[0, 0]
    own_base = grid_base[0, 0]
    own_polar = polar[0, 0]
    lengths = jnp.array([grid_x, grid_y, KZ], dtype=jnp.int32)[:, None]
    cell_index = (own_base + 2) % lengths
    fraction = own_place - cell_index.astype(jnp.float32)
    values, slopes = spline_table(fraction)
    first_x = (own_base[0] - lax.axis_index("row") * CX + 2) % grid_x
    first_y = (own_base[1] - lax.axis_index("col") * CY + 2) % grid_y
    rows_x = placed_table(first_x, values[:, 0], CX + 4)
    slope_x = placed_table(first_x, slopes[:, 0], CX + 4)
    rows_y = placed_table(first_y, values[:, 1], CY + 4)
    slope_y = placed_table(first_y, slopes[:, 1], CY + 4)
    tile_start = jnp.arange(atom_count, dtype=jnp.int32) // TILE * slab_depth
    first_z = (own_base[2] + 2 - tile_start) % KZ
    rows_z = placed_table(first_z, values[:, 2], window_len)
    slope_z = placed_table(first_z, slopes[:, 2], window_len)
    plane_count = (CX + 4) * (CY + 4)
    plane_dx = (slope_x[:, None, :] * rows_y[None, :, :]).reshape(plane_count, atom_count)
    plane_dy = (rows_x[:, None, :] * slope_y[None, :, :]).reshape(plane_count, atom_count)
    plane_flat = (rows_x[:, None, :] * rows_y[None, :, :]).reshape(plane_count, atom_count)
    window_rows = jnp.moveaxis(rows_z.reshape(window_len, tile_count, TILE), 1, 0)
    window_slope = jnp.moveaxis(slope_z.reshape(window_len, tile_count, TILE), 1, 0)
    depth_table = jnp.concatenate([window_rows, window_slope], axis=2)
    grid_scale = 1.0 / (grid_x * grid_y * KZ)
    hartley_x = hartley(grid_x)
    hartley_y = hartley(grid_y)
    hartley_z = hartley(KZ)
    block_y = grid_y // rows_count
    block_z = KZ // cols_count
    wave_x = jnp.arange(grid_x, dtype=jnp.int32)[:, None, None]
    wave_y = (lax.axis_index("row") * block_y + jnp.arange(block_y, dtype=jnp.int32))[None, :, None]
    wave_z = (lax.axis_index("col") * block_z + jnp.arange(block_z, dtype=jnp.int32))[None, None, :]
    kernel = influence(wave_x, wave_y, wave_z, grid_x, grid_y, KZ) * grid_scale
    root_scale = jnp.power(own_polar, 1.0 / 6.0)
    own_static = jnp.concatenate([own_place, root_scale[None]], axis=0)
    near_static = with_halo(own_static[None, None], (("row", 0), ("col", 1)), 1)
    near_static = jnp.moveaxis(near_static.reshape(9, 4, tile_count, TILE), 2, 1).reshape(
        9 * tile_count, 4, TILE
    )
    own_tiles = jnp.moveaxis(own_static.reshape(4, tile_count, TILE), 1, 0)
    own_lists = tile_lists[0, 0]
    polar_wide = own_polar[None, None, :]
    solution = jnp.zeros_like(field_rhs[0, 0])
    residual = field_rhs[0, 0]
    scaled_res = polar_wide * residual
    direction = scaled_res
    progress = inner_sum(residual, scaled_res)
    for iteration in range(ITERS):
        near_dip = with_halo(direction[None, None], (("row", 0), ("col", 1)), 1)
        near_dip = jnp.moveaxis(near_dip.reshape(9, RHS, 3, tile_count, TILE), 3, 1).reshape(
            9 * tile_count, RHS, 3, TILE
        )

        def one_tile(tile_pos):
            picked = own_lists[tile_pos]
            return tile_field(own_tiles[tile_pos], near_static[picked], near_dip[picked], box_spans)

        fields = lax.map(one_tile, jnp.arange(tile_count, dtype=jnp.int32))
        direct = jnp.moveaxis(fields, 0, 2).reshape(RHS, 3, atom_count)
        slope_terms = (
            direction[:, 0, None, :] * plane_dx[None] + direction[:, 1, None, :] * plane_dy[None]
        )
        flat_terms = direction[:, 2, None, :] * plane_flat[None]
        spread_left = jnp.concatenate(
            [
                slope_terms.reshape(RHS, plane_count, tile_count, TILE),
                flat_terms.reshape(RHS, plane_count, tile_count, TILE),
            ],
            axis=3,
        )
        spread_windows = jnp.einsum("sptb,twb->sptw", spread_left, depth_table, precision=highest)
        main_part = spread_windows[..., :slab_depth].reshape(spread_windows.shape[:-2] + (KZ,))
        tail_part = pad_axis(
            spread_windows[..., slab_depth:], spread_windows.ndim - 1, 0, slab_depth - 4
        )
        tail_part = tail_part.reshape(spread_windows.shape[:-2] + (KZ,))[..., : KZ + 4 - slab_depth]
        last_axis = main_part.ndim - 1
        padded_line = pad_axis(main_part, last_axis, 0, 4) + pad_axis(
            tail_part, last_axis, slab_depth, 0
        )
        inner = padded_line[..., 2 : KZ + 2]
        spread_tile = (
            inner
            + pad_axis(padded_line[..., 0:2], last_axis, KZ - 2, 0)
            + pad_axis(padded_line[..., KZ + 2 : KZ + 4], last_axis, 0, KZ - 2)
        ).reshape(RHS, CX + 4, CY + 4, KZ)
        extended = with_halo(spread_tile, (("row", 1), ("col", 2)), 2)
        cycle_only = clear_inside(extended, ((1, CX), (2, CY)))
        folded = fold_cycle(fold_cycle(cycle_only, 1, CX), 2, CY)
        spectrum = jnp.einsum(
            "sxyz,zk->sxyk",
            spread_tile[:, 2 : CX + 2, 2 : CY + 2] + folded,
            hartley_z,
            precision=highest,
        )
        along_y = jnp.einsum(
            "sxyz,yk->sxkz",
            lax.all_to_all(spectrum, "col", split_axis=3, concat_axis=2, tiled=True),
            hartley_y,
            precision=highest,
        )
        along_x = (
            jnp.einsum(
                "sxyz,xk->skyz",
                lax.all_to_all(along_y, "row", split_axis=2, concat_axis=1, tiled=True),
                hartley_x,
                precision=highest,
            )
            * kernel[None]
        )
        mixed_part = jnp.einsum("sxyz,xk->skyz", along_x, hartley_x, precision=highest)
        returned = lax.all_to_all(mixed_part, "row", split_axis=1, concat_axis=2, tiled=True)
        swapped = jnp.einsum("sxyz,yk->sxkz", returned, hartley_y, precision=highest)
        restored = lax.all_to_all(swapped, "col", split_axis=2, concat_axis=3, tiled=True)
        padded = with_halo(
            jnp.einsum("sxyz,zk->sxyk", restored, hartley_z, precision=highest),
            (("row", 1), ("col", 2)),
            2,
        )
        line = padded.reshape(RHS, plane_count, KZ)
        extended_line = jnp.concatenate([line[..., KZ - 2 :], line, line[..., :2]], axis=-1)
        windows = jnp.stack(
            [
                extended_line[..., tile * slab_depth : tile * slab_depth + window_len]
                for tile in range(tile_count)
            ],
            axis=-2,
        )
        sampled = jnp.einsum("sptw,twb->sptb", windows, depth_table, precision=highest)
        with_flat = sampled[..., :TILE].reshape(RHS, plane_count, atom_count)
        with_slope = sampled[..., TILE:].reshape(RHS, plane_count, atom_count)
        recip_part = jnp.stack(
            [
                jnp.sum(with_flat * plane_dx[None], axis=1),
                jnp.sum(with_flat * plane_dy[None], axis=1),
                jnp.sum(with_slope * plane_flat[None], axis=1),
            ],
            axis=1,
        )
        image_field = direction / polar_wide - direct + recip_part - self_coef * direction
        step_size = (progress / inner_sum(direction, image_field))[:, None, None]
        solution = solution + step_size * direction
        residual = residual - step_size * image_field
        scaled_res = polar_wide * residual
        progress_next = inner_sum(residual, scaled_res)
        direction = scaled_res + (progress_next / progress)[:, None, None] * direction
        progress = progress_next
    return (solution[None, None], residual[None, None])


X_PAD = CX + 4
Y_PAD = CY + 4
SLOT_ROWS = 16
SPLIT = 2
VMEM_LIMIT = 60_000_000
SMALL_VMEM_LIMIT = 24_000_000
MIDDLE_VMEM_LIMIT = 56_000_000
ROOMY_BYTES = 12 << 20
EARLY_TILES = 1
PAIR_ROWS = 32
GROUP = 8
SCREEN_SCALE = 0.4
SCREEN_COEF = (
    0.22567588090896606,
    0.2256690263748169,
    0.20785020291805267,
    0.16849851608276367,
    0.14156343042850494,
    -0.005832736846059561,
    0.16930203139781952,
    -0.1830107867717743,
    0.05028456076979637,
)


def halves(value):
    high = value.astype(jnp.bfloat16)
    return high, (value - high.astype(jnp.float32)).astype(jnp.bfloat16)


def halves_np(value):
    value = value.astype(np.float32)
    high = value.astype(ml_dtypes.bfloat16)
    return high, (value - high.astype(np.float32)).astype(ml_dtypes.bfloat16)


def product(left, right, left_dim=1, right_dim=0):
    def one(first, second):
        return lax.dot_general(
            first,
            second,
            (((left_dim,), (right_dim,)), ((), ())),
            preferred_element_type=jnp.float32,
        )

    return one(left[0], right[0]) + (one(left[1], right[0]) + one(left[0], right[1]))


def cas_np(wave, place, length):
    angles = 2.0 * np.pi / length * (wave[:, None] * place[None, :] % length)
    return np.cos(angles) + np.sin(angles)


def modulus_np(wave, length):
    coef = np.array([1.0, 11.0, 11.0, 1.0]) / 24.0
    angles = 2.0 * np.pi / length * (wave[:, None] * np.arange(4)[None, :])
    return (coef * np.cos(angles)).sum(1) ** 2 + (coef * np.sin(angles)).sum(1) ** 2


def influence_np(length_x, length_y, length_z):
    total = np.zeros((length_x, length_y, length_z))
    modulus = np.ones((length_x, length_y, length_z))
    excluded = np.zeros((length_x, length_y, length_z), bool)
    for axis, length in enumerate((length_x, length_y, length_z)):
        wave = np.arange(length)
        shape = [1, 1, 1]
        shape[axis] = length
        total = total + ((np.minimum(wave, length - wave) / length) ** 2).reshape(shape)
        modulus = modulus * modulus_np(wave, length).reshape(shape)
        excluded = excluded | (wave * 2 == length).reshape(shape)
    excluded[0, 0, 0] = True
    safe = np.where(excluded, 1.0, total)
    result = np.exp(-(np.pi**2) / ewald_beta**2 * safe) / (
        np.pi * safe * np.where(excluded, 1.0, modulus)
    )
    return np.where(excluded, 0.0, result) / (length_x * length_y * length_z)


def slab_tables(rows_count, cols_count):
    grid_x = CX * rows_count
    grid_y = CY * cols_count
    devices = rows_count * cols_count
    chunk = KZ // devices
    wave_z = (np.arange(devices)[None, :] * chunk + np.arange(chunk)[:, None]).reshape(-1)
    along_z = cas_np(wave_z, np.arange(KZ), KZ)
    place_x = np.arange(rows_count)[:, None] * CX + np.arange(X_PAD)[None, :] - 2
    along_x = cas_np(np.arange(grid_x), place_x.reshape(-1) % grid_x, grid_x)
    x_high, x_low = halves_np(along_x)
    forward_x = np.concatenate([x_high, x_low, x_high], axis=1)
    backward_x = np.concatenate([x_high.T, x_low.T, x_high.T], axis=1)
    place_y = (np.arange(cols_count)[:, None] * CY + np.arange(Y_PAD)[None, :] - 2) % grid_y
    along_y = cas_np(np.arange(grid_y), place_y.reshape(-1), grid_y)
    along_y = along_y.reshape(grid_y, cols_count, Y_PAD)
    units = chunk * RHS // SPLIT
    block = np.einsum("uv,kcy->cuyvk", np.eye(units), along_y)
    block = block.reshape(cols_count * units * Y_PAD, units * grid_y)
    kernel = influence_np(grid_x, grid_y, KZ).reshape(grid_x, grid_y, devices, chunk)
    kernel = np.transpose(kernel, (2, 0, 3, 1))[:, :, :, None, :]
    kernel = np.broadcast_to(kernel, (devices, grid_x, chunk, RHS, grid_y))
    kernel = kernel.reshape(devices, grid_x, SPLIT, units * grid_y)
    kernel = np.moveaxis(kernel, 2, 1).reshape(devices, SPLIT * grid_x, units * grid_y)
    kernel = kernel.astype(np.float32)
    return dict(
        along_z=halves_np(along_z),
        forward_x=forward_x,
        backward_x=backward_x,
        block=halves_np(block),
        kernel=kernel,
    )


def pack_body(rhs_ref, place_ref, polar_ref, start_ref, payload_ref):
    polar = polar_ref[...]
    start = read_rows(rhs_ref) * polar
    start_ref[...] = start
    place = [place_ref[dim] for dim in range(3)]
    everything = jnp.concatenate(place + [1.0 / jnp.sqrt(polar), start], axis=0)
    store_payload(payload_ref, everything)


def read_rows(rows_ref):
    return jnp.concatenate([rows_ref[dim] for dim in range(3)], axis=0)


def store_payload(payload_ref, everything):
    tile_count = everything.shape[1] // TILE
    for quantity in range(everything.shape[0]):
        for tile in range(tile_count):
            row = quantity * tile_count + tile
            payload_ref[row : row + 1, :] = everything[
                quantity : quantity + 1, tile * TILE : (tile + 1) * TILE
            ]


def placed_rows(slot, weights, extent):
    slot_index = lax.broadcasted_iota(jnp.int32, (extent, slot.shape[1]), 0)
    placed = jnp.zeros((extent, slot.shape[1]), jnp.float32)
    for stencil in range(5):
        target = slot + stencil
        if extent == KZ:
            target = jnp.where(target >= KZ, target - KZ, target)
        placed = placed + jnp.where(slot_index == target, weights[stencil], 0.0)
    return placed


def spread_into(message_ref, moment, rows_x, slope_x, rows_y, slope_y, depth, devices):
    blocks = []
    for step in range(X_PAD):
        flat_x = rows_x[step : step + 1]
        tilt_x = slope_x[step : step + 1]
        for rhs in range(RHS):
            part_x = tilt_x * moment[rhs : rhs + 1]
            part_y = flat_x * moment[RHS + rhs : RHS + rhs + 1]
            part_z = flat_x * moment[2 * RHS + rhs : 2 * RHS + rhs + 1]
            blocks.append(
                jnp.concatenate([part_x * rows_y + part_y * slope_y, part_z * rows_y], axis=1)
            )
    charges = jnp.concatenate(blocks, axis=0)
    spectrum = product(depth, halves(charges), 1, 1)
    slot_rows = message_ref.shape[0] // devices
    chunk = KZ // devices
    width = RHS * Y_PAD
    for step in range(X_PAD):
        message_ref[pl.ds(step, devices, stride=slot_rows), :] = jnp.concatenate(
            [
                spectrum[unit * devices : (unit + 1) * devices, step * width : (step + 1) * width]
                for unit in range(chunk)
            ],
            axis=1,
        )


def sample_from(message_ref, rows_x, slope_x, rows_y, slope_y, depth, devices):
    chunk = KZ // devices
    width = RHS * Y_PAD
    slot_rows = message_ref.shape[0] // devices
    pieces = [
        message_ref[pl.ds(step, devices, stride=slot_rows), :] for step in range(X_PAD)
    ]
    spare = jnp.zeros((devices, KZ - X_PAD * width), jnp.float32)
    spectrum = jnp.concatenate(
        [
            jnp.concatenate(
                [piece[:, unit * width : (unit + 1) * width] for piece in pieces] + [spare], axis=1
            )
            for unit in range(chunk)
        ],
        axis=0,
    )
    spectrum = jnp.transpose(spectrum)[: X_PAD * width]
    sampled = product(halves(spectrum), depth, 1, 0)
    atoms = rows_x.shape[1]
    fields = [None] * (3 * RHS)
    for rhs in range(RHS):
        sum_x = sum_y = sum_z = None
        for step in range(X_PAD):
            first = step * width + rhs * Y_PAD
            flat = sampled[first : first + Y_PAD, :atoms]
            tilt = sampled[first : first + Y_PAD, atoms:]
            part_x = slope_x[step : step + 1] * flat
            part_y = rows_x[step : step + 1] * flat
            part_z = rows_x[step : step + 1] * tilt
            sum_x = part_x if sum_x is None else sum_x + part_x
            sum_y = part_y if sum_y is None else sum_y + part_y
            sum_z = part_z if sum_z is None else sum_z + part_z
        fields[rhs] = jnp.sum(sum_x * rows_y, axis=0, keepdims=True)
        fields[RHS + rhs] = jnp.sum(sum_y * slope_y, axis=0, keepdims=True)
        fields[2 * RHS + rhs] = jnp.sum(sum_z * rows_y, axis=0, keepdims=True)
    return jnp.concatenate(fields, axis=0)


def read_tables(tables_ref):
    return (
        tables_ref[0:X_PAD],
        tables_ref[SLOT_ROWS : SLOT_ROWS + X_PAD],
        tables_ref[2 * SLOT_ROWS : 2 * SLOT_ROWS + Y_PAD],
        tables_ref[2 * SLOT_ROWS + Y_PAD : 2 * SLOT_ROWS + 2 * Y_PAD],
    )


def setup_body(
    lengths,
    devices,
    place_ref,
    base_ref,
    start_ref,
    z_high_ref,
    z_low_ref,
    message_ref,
    tables_ref,
    depth_high_ref,
    depth_low_ref,
):
    base = [base_ref[dim] for dim in range(3)]
    fractions = []
    cells = []
    for dim in range(3):
        cell = base[dim] + 2
        cell = jnp.where(cell >= lengths[dim], cell - lengths[dim], cell)
        cells.append(cell)
        fractions.append(place_ref[dim] - cell.astype(jnp.float32))
    values, slopes = spline_table(jnp.concatenate(fractions, axis=0))
    values = [[values[stencil][dim : dim + 1] for stencil in range(5)] for dim in range(3)]
    slopes = [[slopes[stencil][dim : dim + 1] for stencil in range(5)] for dim in range(3)]
    slot_x = lax.rem(cells[0], CX)
    slot_y = lax.rem(cells[1], CY)
    tables_ref[0:SLOT_ROWS] = placed_rows(slot_x, values[0], SLOT_ROWS)
    tables_ref[SLOT_ROWS : 2 * SLOT_ROWS] = placed_rows(slot_x, slopes[0], SLOT_ROWS)
    tables_ref[2 * SLOT_ROWS : 2 * SLOT_ROWS + Y_PAD] = placed_rows(slot_y, values[1], Y_PAD)
    tables_ref[2 * SLOT_ROWS + Y_PAD : 2 * SLOT_ROWS + 2 * Y_PAD] = placed_rows(
        slot_y, slopes[1], Y_PAD
    )
    window = jnp.concatenate(
        [
            placed_rows(base[2], values[2], KZ),
            placed_rows(base[2], slopes[2], KZ),
        ],
        axis=1,
    )
    depth = product((z_high_ref[...], z_low_ref[...]), halves(window), 1, 0)
    depth = halves(depth)
    depth_high_ref[...] = depth[0]
    depth_low_ref[...] = depth[1]
    spread_into(message_ref, start_ref[...], *read_tables(tables_ref), depth, devices)


def transform_in(message_ref, forward_ref, block_high_ref, block_low_ref, rows_count, cols_count):
    gathered = jnp.concatenate(
        [
            jnp.concatenate(
                [
                    message_ref[(r * cols_count + c) * X_PAD : (r * cols_count + c + 1) * X_PAD]
                    for r in range(rows_count)
                ],
                axis=0,
            )
            for c in range(cols_count)
        ],
        axis=1,
    )
    high, low = halves(gathered)
    along = jnp.dot(
        forward_ref[...],
        jnp.concatenate([high, high, low], axis=0),
        preferred_element_type=jnp.float32,
    )
    part = along.shape[1] // cols_count // SPLIT
    along = jnp.concatenate(
        [
            jnp.concatenate(
                [
                    along[:, (c * SPLIT + half) * part : (c * SPLIT + half + 1) * part]
                    for c in range(cols_count)
                ],
                axis=1,
            )
            for half in range(SPLIT)
        ],
        axis=0,
    )
    return product(halves(along), (block_high_ref[...], block_low_ref[...]))


def transform_out(result_ref, values, backward_ref, block_high_ref, block_low_ref, counts):
    rows_count, cols_count = counts
    spread = product(halves(values), (block_high_ref[...], block_low_ref[...]), 1, 1)
    grid_x = spread.shape[0] // SPLIT
    part = spread.shape[1] // cols_count
    spread = jnp.concatenate(
        [
            spread[half * grid_x : (half + 1) * grid_x, c * part : (c + 1) * part]
            for c in range(cols_count)
            for half in range(SPLIT)
        ],
        axis=1,
    )
    high, low = halves(spread)
    along = jnp.dot(
        backward_ref[...],
        jnp.concatenate([high, high, low], axis=0),
        preferred_element_type=jnp.float32,
    )
    width = along.shape[1] // cols_count
    slot_rows = result_ref.shape[0] // (rows_count * cols_count)
    for r in range(rows_count):
        for c in range(cols_count):
            first = (r * cols_count + c) * slot_rows
            result_ref[first : first + X_PAD, :] = along[
                r * X_PAD : (r + 1) * X_PAD, c * width : (c + 1) * width
            ]


def middle_first_body(
    counts,
    message_ref,
    kernel_ref,
    forward_ref,
    backward_ref,
    block_high_ref,
    block_low_ref,
    result_ref,
    wave_ref,
):
    wave = transform_in(message_ref, forward_ref, block_high_ref, block_low_ref, *counts)
    wave_ref[...] = wave
    transform_out(
        result_ref, wave * kernel_ref[...], backward_ref, block_high_ref, block_low_ref, counts
    )


def gather_rows(parts):
    tiles = [
        parts[GROUP * tile : GROUP * tile + GROUP, :] for tile in range(parts.shape[0] // GROUP)
    ]
    return jnp.concatenate(tiles, axis=1)[0 : 3 * RHS]


def row_total(value, rhs):
    row = lax.broadcasted_iota(jnp.int32, value.shape, 0)
    return total(jnp.where(lax.rem(row, RHS) == rhs, value, 0.0))


def total(value):
    return jnp.sum(jnp.sum(value, axis=0, keepdims=True), axis=1, keepdims=True)


def middle_second_body(
    counts,
    message_ref,
    kernel_ref,
    forward_ref,
    backward_ref,
    block_high_ref,
    block_low_ref,
    wave_ref,
    start_ref,
    carried_ref,
    near_ref,
    polar_ref,
    result_ref,
    local_ref,
):
    near_rows = gather_rows(near_ref)
    wave = transform_in(message_ref, forward_ref, block_high_ref, block_low_ref, *counts)
    filtered = wave * kernel_ref[...]
    transform_out(result_ref, filtered, backward_ref, block_high_ref, block_low_ref, counts)
    before = wave_ref[...]
    grid_y = CY * counts[1]
    lane = lax.broadcasted_iota(jnp.int32, wave.shape, 1)
    own_rhs = lax.rem(lax.div(lane, grid_y), RHS)
    image = carried_ref[0 : 3 * RHS]
    second = carried_ref[8 : 8 + 3 * RHS]
    start = start_ref[...]
    local_part = second / polar_ref[...] - near_rows - self_coef * second
    local_ref[0 : 3 * RHS] = image
    local_ref[8 : 8 + 3 * RHS] = second
    local_ref[16 : 16 + 3 * RHS] = local_part
    local_ref[24 : 24 + 3 * RHS] = start
    slot = lax.broadcasted_iota(jnp.int32, (1, result_ref.shape[1]), 1)
    sums = jnp.zeros((1, result_ref.shape[1]), jnp.float32)
    for rhs in range(RHS):
        mine = own_rhs == rhs
        parts = (
            row_total(start * start / polar_ref[...], rhs),
            row_total(start * image, rhs),
            row_total(second * image, rhs),
            row_total(start * local_part, rhs) + total(jnp.where(mine, before * filtered, 0.0)),
            row_total(second * local_part, rhs) + total(jnp.where(mine, wave * filtered, 0.0)),
        )
        for index, part in enumerate(parts):
            sums = jnp.where(slot == rhs * len(parts) + index, part, sums)
    devices = counts[0] * counts[1]
    result_ref[pl.ds(X_PAD, devices, stride=X_PAD + 1), :] = jnp.broadcast_to(
        sums, (devices, sums.shape[1])
    )


def sample_body(
    devices,
    message_ref,
    tables_ref,
    depth_high_ref,
    depth_low_ref,
    start_ref,
    near_ref,
    polar_ref,
    carried_ref,
    payload_ref,
):
    tables = read_tables(tables_ref)
    depth = (depth_high_ref[...], depth_low_ref[...])
    field = sample_from(message_ref, *tables, depth, devices)
    start = start_ref[...]
    polar = polar_ref[...]
    image = start / polar - gather_rows(near_ref) + field - self_coef * start
    second = polar * image
    carried_ref[0 : 3 * RHS] = image
    carried_ref[8 : 8 + 3 * RHS] = second
    store_payload(payload_ref, second)


def spread_body(
    devices,
    tables_ref,
    depth_high_ref,
    depth_low_ref,
    carried_ref,
    result_ref,
):
    depth = (depth_high_ref[...], depth_low_ref[...])
    second = carried_ref[8 : 8 + 3 * RHS]
    spread_into(result_ref, second, *read_tables(tables_ref), depth, devices)


def final_body(
    devices,
    message_ref,
    tables_ref,
    depth_high_ref,
    depth_low_ref,
    rhs_ref,
    local_ref,
    dipole_ref,
    residual_ref,
):
    tables = read_tables(tables_ref)
    depth = (depth_high_ref[...], depth_low_ref[...])
    field = sample_from(message_ref, *tables, depth, devices)
    image = local_ref[0 : 3 * RHS]
    second = local_ref[8 : 8 + 3 * RHS]
    image_second = local_ref[16 : 16 + 3 * RHS] + field
    start = local_ref[24 : 24 + 3 * RHS]
    sums = jnp.sum(
        message_ref[pl.ds(X_PAD, devices, stride=X_PAD + 1), :], axis=0, keepdims=True
    )
    steps = []
    for rhs in range(RHS):
        progress, start_image, second_image, start_next, second_next = [
            sums[:, rhs * 5 + index : rhs * 5 + index + 1] for index in range(5)
        ]
        step = progress / start_image
        progress_next = progress - 2.0 * step * start_image + step * step * second_image
        grown = 1.0 + progress_next / progress
        curvature = (
            grown * grown * start_image
            - step * grown * (start_next + second_image)
            + step * step * second_next
        )
        steps.append((step, grown, progress_next / curvature))
    row = lax.broadcasted_iota(jnp.int32, (RHS, 1), 0)
    step, grown, step_next = [
        sum(jnp.where(row == rhs, steps[rhs][index], 0.0) for rhs in range(RHS))
        for index in range(3)
    ]
    for dim in range(3):
        rows = slice(dim * RHS, (dim + 1) * RHS)
        direction = grown * start[rows] - step * second[rows]
        image_direction = grown * image[rows] - step * image_second[rows]
        dipole_ref[dim] = step * start[rows] + step_next * direction
        residual_ref[dim] = rhs_ref[dim] - step * image[rows] - step_next * image_direction


def near_base(entry, brick_rows):
    return lax.shift_right_logical(entry, 2) * brick_rows + lax.bitwise_and(entry, 3)


def nearest(places, origin, span):
    return places - span * jnp.floor((places - origin) * (1.0 / span) + 0.5)


def unwrap_near(near, tile_count, spans):
    rows = near.shape[0] // 9
    for dim in range(2):
        own = 4 * rows + dim * tile_count
        origin = near[own : own + 1, 0:1]
        for brick in range(9):
            first = brick * rows + dim * tile_count
            near[first : first + tile_count, :] = nearest(
                near[first : first + tile_count, :], origin, spans[dim]
            )


def pick_rows(picked, near, lists_ref, tile, place, tile_count, quantities, origin, span):
    rows = near.shape[0] // 9
    place = place * lists_ref.shape[1] * quantities * GROUP
    for entry in range(lists_ref.shape[1]):
        base = near_base(lists_ref[tile, entry], rows)
        for quantity in range(quantities):
            values = near[pl.ds(base + quantity * tile_count, 1), :]
            if quantity == 2 and span is not None:
                values = nearest(values, origin, span)
            first = place + (entry * quantities + quantity) * GROUP
            picked[first : first + GROUP, :] = jnp.broadcast_to(values, (GROUP, TILE))


def widen_own(near, quantities, tile_count, tile, place, wide):
    offset = near.shape[0] // 9 * 4
    rows = [
        near[offset + quantity * tile_count + tile : offset + quantity * tile_count + tile + 1, :]
        for quantity in range(quantities)
    ]
    spare = jnp.zeros((TILE - quantities, TILE), jnp.float32)
    columns = jnp.transpose(jnp.concatenate(rows + [spare], axis=0))
    for quantity in range(quantities):
        first = (place * quantities + quantity) * TILE
        wide[first : first + TILE, :] = jnp.broadcast_to(
            columns[:, quantity : quantity + 1], (TILE, TILE)
        )


def add_field(sums, first_term, second_term, apart, moments):
    for rhs in range(RHS):
        moment = [moments[RHS * dim + rhs] for dim in range(3)]
        projected = moment[0] * apart[0] + moment[1] * apart[1] + moment[2] * apart[2]
        weighted = second_term * projected
        for dim in range(3):
            index = RHS * dim + rhs
            sums[index] = sums[index] + (weighted * apart[dim] - first_term * moment[dim])


def finish_sums(field_ref, sums_ref, first_tile, place):
    place = place * 3 * RHS
    lane = lax.broadcasted_iota(jnp.int32, (TILE, TILE), 1)
    merged = jnp.zeros((TILE, TILE), jnp.float32)
    for index in range(3 * RHS):
        first = (place + index) * TILE
        column = jnp.sum(sums_ref[first : first + TILE, :], axis=1, keepdims=True)
        merged = jnp.where(lane == index, column, merged)
    first = (first_tile + place // (3 * RHS)) * GROUP
    field_ref[first : first + GROUP, :] = jnp.transpose(merged)[0:GROUP]


def pair_rows(start, group):
    return pl.ds(pl.multiple_of(start + group * GROUP, GROUP), GROUP)


def wide_rows(start, group, quantity):
    return pl.ds(pl.multiple_of(quantity * TILE + start + group * GROUP, GROUP), GROUP)


def pair_terms(square_dist, damp):
    inverse = lax.rsqrt(square_dist)
    distance = square_dist * inverse
    inverse_sq = inverse * inverse
    inverse_cube = inverse_sq * inverse
    cubed = damp * (distance * square_dist)
    damping = jnp.exp(cubed)
    bell = jnp.exp(-(ewald_beta * ewald_beta) * square_dist)
    stretched = 1.0 + (SCREEN_SCALE * ewald_beta) * distance
    turned = pl.reciprocal(stretched, approx=True)
    turned = turned * (2.0 - stretched * turned)
    series = SCREEN_COEF[-1] * turned + SCREEN_COEF[-2]
    for coef in SCREEN_COEF[-3::-1]:
        series = series * turned + coef
    screen = bell * turned * series
    gaussian = (2.0 * ewald_beta / math.sqrt(math.pi)) * bell
    bare = screen - damping
    first_term = bare * inverse_cube + gaussian * inverse_sq
    second_term = (
        3.0 * (first_term + (cubed * damping) * inverse_cube)
        + (2.0 * ewald_beta * ewald_beta) * gaussian
    ) * inverse_sq
    return first_term, second_term


def step_rows(step, size, offset):
    return pl.ds(pl.multiple_of(step * size + offset, GROUP), GROUP)


def tile_rows(step, rows):
    return pl.ds(pl.multiple_of(step * rows, GROUP), rows)


def start_all(copies):
    for copy in copies:
        copy.start()


def wait_all(copies):
    for copy in copies:
        copy.wait()


def near_copies(sources, near, semaphore):
    rows = sources[0].shape[0]
    return [
        pltpu.make_async_copy(
            source, near.at[index * rows : (index + 1) * rows, :], semaphore.at[index]
        )
        for index, source in enumerate(sources)
    ]


def term_copies(terms, buffers, semaphore, begin, step, size, inward):
    rows = pl.ds(pl.multiple_of((begin + step) * size, GROUP), size)
    place = pl.ds(pl.multiple_of(step * size, GROUP), size)
    copies = []
    for index in range(2):
        far, here = terms[index].at[rows, :], buffers[index].at[place, :]
        ends = (far, here) if inward else (here, far)
        copies.append(pltpu.make_async_copy(*ends, semaphore.at[index, step]))
    return copies


def pair_first_body(
    first_tile,
    last_tile,
    tile_count,
    spans,
    lists_ref,
    up_ref,
    stack_ref,
    down_ref,
    *others,
):
    first_ref, second_ref, field_ref, near_ref = others[-14:-10]
    near, picked, wide, sums_ref, kept, field, first_buffer, second_buffer, semaphore, busy = others[-10:]
    terms = (first_ref, second_ref)
    buffers = (first_buffer, second_buffer)
    copies = near_copies((up_ref, stack_ref, down_ref), near, semaphore.at[0])
    if first_tile > 0:
        copies.append(
            pltpu.make_async_copy(
                others[0], field.at[0 : first_tile * GROUP, :], semaphore.at[0, 3]
            )
        )
    start_all(copies)
    wait_all(copies)
    entries = lists_ref.shape[1]
    rows = near.shape[0] // 9
    quantities = rows // tile_count
    unwrap_near(near, tile_count, spans)
    for brick in range(9):
        kept[brick * 3 * tile_count : (brick + 1) * 3 * tile_count, :] = near[
            brick * rows : brick * rows + 3 * tile_count, :
        ]
    keep = pltpu.make_async_copy(kept, near_ref, semaphore.at[1, 3])
    keep.start()
    for place, tile in enumerate(range(first_tile, last_tile)):
        widen_own(near, 4, tile_count, tile, place, wide)
        own = rows * 4 + 2 * tile_count + tile
        origin = near[own : own + 1, 0:1]
        pick_rows(picked, near, lists_ref, tile, place, tile_count, quantities, origin, spans[2])
    parts = TILE // PAIR_ROWS
    steps = (last_tile - first_tile) * parts

    size = entries * PAIR_ROWS

    def sent(step):
        return term_copies(terms, buffers, busy, first_tile * parts, step, size, False)

    @pl.loop(0, steps)
    def _(step):
        tile = lax.div(step, parts)
        start = lax.rem(step, parts) * PAIR_ROWS
        step_picked = picked.at[tile_rows(tile, entries * quantities * GROUP), :]
        step_wide = wide.at[tile_rows(tile, 4 * TILE), :]
        step_sums = sums_ref.at[tile_rows(tile, 3 * RHS * TILE), :]
        for group in range(PAIR_ROWS // GROUP):
            own = [step_wide[wide_rows(start, group, dim), :] for dim in range(4)]
            own_damp = -thole_a * own[3]
            sums = [jnp.zeros((GROUP, TILE), jnp.float32) for _ in range(3 * RHS)]
            itself = (
                lax.broadcasted_iota(jnp.int32, (GROUP, TILE), 0) + (start + group * GROUP)
            ) == lax.broadcasted_iota(jnp.int32, (GROUP, TILE), 1)
            for entry in range(entries):
                first = entry * quantities * GROUP
                rows = [
                    step_picked[first + quantity * GROUP : first + (quantity + 1) * GROUP, :]
                    for quantity in range(quantities)
                ]
                apart = [rows[dim] - own[dim] for dim in range(3)]
                square_dist = apart[0] * apart[0] + apart[1] * apart[1] + apart[2] * apart[2]
                if entry == 0:
                    square_dist = jnp.where(itself, 1.0, square_dist)
                first_term, second_term = pair_terms(square_dist, own_damp * rows[3])
                if entry == 0:
                    first_term = jnp.where(itself, 0.0, first_term)
                    second_term = jnp.where(itself, 0.0, second_term)
                place = step_rows(step, size, entry * PAIR_ROWS + group * GROUP)
                first_buffer[place, :] = first_term
                second_buffer[place, :] = second_term
                add_field(sums, first_term, second_term, apart, rows[4:])
            for index, value in enumerate(sums):
                step_sums[wide_rows(start, group, index), :] = value
        start_all(sent(step))

    for place in range(last_tile - first_tile):
        finish_sums(field, sums_ref, first_tile, place)
    result = pltpu.make_async_copy(field, head_of(field_ref, field), semaphore.at[1, 2])
    result.start()

    @pl.loop(0, steps)
    def _(step):
        wait_all(sent(step))

    keep.wait()
    result.wait()


def pair_second_body(
    tile_count,
    spans,
    lists_ref,
    near_ref,
    up_ref,
    stack_ref,
    down_ref,
    first_ref,
    second_ref,
    field_ref,
    near,
    near_moment,
    picked,
    picked_moment,
    wide,
    sums_ref,
    field,
    first_buffer,
    second_buffer,
    semaphore,
    busy,
):
    terms = (first_ref, second_ref)
    buffers = (first_buffer, second_buffer)
    parts = TILE // PAIR_ROWS
    steps = tile_count * parts

    entries = lists_ref.shape[1]
    size = entries * PAIR_ROWS

    def fetched(step):
        return term_copies(terms, buffers, busy, 0, step, size, True)

    places = pltpu.make_async_copy(near_ref, near, semaphore.at[1, 3])
    places.start()
    copies = near_copies((up_ref, stack_ref, down_ref), near_moment, semaphore.at[2])
    start_all(copies)

    @pl.loop(0, steps)
    def _(step):
        start_all(fetched(step))

    places.wait()
    for tile in range(tile_count):
        widen_own(near, 3, tile_count, tile, tile, wide)
        own = near.shape[0] // 9 * 4 + 2 * tile_count + tile
        origin = near[own : own + 1, 0:1]
        pick_rows(picked, near, lists_ref, tile, tile, tile_count, 3, origin, spans[2])
    wait_all(copies)
    for tile in range(tile_count):
        pick_rows(
            picked_moment, near_moment, lists_ref, tile, tile, tile_count, 3 * RHS, None, None
        )

    @pl.loop(0, steps)
    def _(step):
        wait_all(fetched(step))
        tile = lax.div(step, parts)
        start = lax.rem(step, parts) * PAIR_ROWS
        step_picked = picked.at[tile_rows(tile, entries * 3 * GROUP), :]
        step_moment = picked_moment.at[tile_rows(tile, entries * 3 * RHS * GROUP), :]
        step_wide = wide.at[tile_rows(tile, 3 * TILE), :]
        step_sums = sums_ref.at[tile_rows(tile, 3 * RHS * TILE), :]
        for group in range(PAIR_ROWS // GROUP):
            own = [step_wide[wide_rows(start, group, dim), :] for dim in range(3)]
            sums = [jnp.zeros((GROUP, TILE), jnp.float32) for _ in range(3 * RHS)]
            for entry in range(entries):
                first = entry * 3 * GROUP
                apart = [
                    step_picked[first + dim * GROUP : first + (dim + 1) * GROUP, :] - own[dim]
                    for dim in range(3)
                ]
                first = first * RHS
                moments = [
                    step_moment[first + index * GROUP : first + (index + 1) * GROUP, :]
                    for index in range(3 * RHS)
                ]
                place = step_rows(step, size, entry * PAIR_ROWS + group * GROUP)
                add_field(sums, first_buffer[place, :], second_buffer[place, :], apart, moments)
            for index, value in enumerate(sums):
                step_sums[wide_rows(start, group, index), :] = value

    for place in range(tile_count):
        finish_sums(field, sums_ref, 0, place)
    result = pltpu.make_async_copy(field, head_of(field_ref, field), semaphore.at[1, 2])
    result.start()
    result.wait()


def shift(source, axis, step):
    count = lax.axis_size(axis)
    return lax.ppermute(source, axis, [(i, (i + step) % count) for i in range(count)])


def both_ways(source, axis):
    return shift(source, axis, 1), source, shift(source, axis, -1)


def whole(shape):
    return pl.BlockSpec(shape, lambda *_: (0,) * len(shape))


def anywhere():
    return pl.BlockSpec(memory_space=pl.ANY)


def join(message, payload):
    right = shift(payload, "col", -1)
    left = shift(payload, "col", 1)
    message, right, left = lax.optimization_barrier((message, right, left))
    return message, both_ways(jnp.concatenate([left, payload, right], axis=0), "row")


class Fetched:
    def __init__(self, source, scratch, semaphore):
        self.copy = pltpu.make_async_copy(source, scratch, semaphore)
        self.copy.start()
        self.scratch = scratch
        self.shape = scratch.shape
        self.waiting = True

    def wait(self):
        if self.waiting:
            self.copy.wait()
            self.waiting = False

    def __getitem__(self, index):
        self.wait()
        return self.scratch[index]


class Head:
    def __init__(self, array, shape):
        self.array = array
        self.shape = shape
        self.dtype = array.dtype


def roomy(shape):
    return (ROOMY_BYTES // 4 // shape[1], shape[1])


def head_of(far, here):
    if far.shape == here.shape:
        return far
    return far.at[0 : here.shape[0], :]


def call(body, outs, *operands, after=(), own_block=None, near=0, large=(), vmem=VMEM_LIMIT):
    count = len(operands)
    fetched = [
        pltpu.VMEM(operand.shape[1:] if index == own_block else operand.shape, operand.dtype)
        for index, operand in enumerate(operands)
        if index >= near
    ]
    arrays = [operand.array if isinstance(operand, Head) else operand for operand in operands]

    def run(*refs):
        refs = refs[len(after) :]
        sources, refs = refs[:count], refs[count:]
        results, refs = refs[: len(outs)], refs[len(outs) :]
        targets, written, semaphore = refs[: count - near], refs[count - near : -1], refs[-1]
        inputs = list(sources[:near])
        for index in range(near, count):
            source = sources[index]
            if index == own_block:
                place = lax.axis_index("row") * lax.axis_size("col") + lax.axis_index("col")
                source = source.at[place]
            else:
                source = head_of(source, targets[index - near])
            inputs.append(Fetched(source, targets[index - near], semaphore.at[index]))
        body(*inputs, *written)
        for operand in inputs[near:]:
            operand.wait()
        copies = [
            pltpu.make_async_copy(value, head_of(result, value), semaphore.at[count + index])
            for index, (value, result) in enumerate(zip(written, results))
        ]
        for copy in copies:
            copy.start()
        for copy in copies:
            copy.wait()

    return pl.pallas_call(
        run,
        in_specs=[anywhere()] * len(after)
        + [pl.BlockSpec(memory_space=pltpu.VMEM)] * near
        + [anywhere()] * (count - near),
        out_specs=[anywhere()] * len(outs),
        out_shape=[
            jax.ShapeDtypeStruct(roomy(shape) if index in large else shape, dtype)
            for index, (shape, dtype) in enumerate(outs)
        ],
        scratch_shapes=fetched
        + [pltpu.VMEM(shape, dtype) for shape, dtype in outs]
        + [pltpu.SemaphoreType.DMA((count + len(outs),))],
        compiler_params=pltpu.CompilerParams(vmem_limit_bytes=vmem),
        cost_estimate=pl.CostEstimate(
            flops=200_000_000, bytes_accessed=4 << 20, transcendentals=0
        ),
    )(*after, *arrays)


def final_call(body, outs, *operands):
    return pl.pallas_call(
        body,
        grid=(1,),
        in_specs=[whole(operand.shape) for operand in operands],
        out_specs=[whole(shape) for shape, _ in outs],
        out_shape=[jax.ShapeDtypeStruct(shape, dtype) for shape, dtype in outs],
        compiler_params=pltpu.CompilerParams(vmem_limit_bytes=SMALL_VMEM_LIMIT),
    )(*operands)


def pair_call(body, outs, scratch, lists, *operands, tiles, large, aliased=0):
    buffers = (tiles * lists.shape[1] * TILE, TILE)
    first = 1 + len(operands) - aliased
    return pl.pallas_call(
        body,
        in_specs=[pl.BlockSpec(memory_space=pltpu.SMEM)] + [anywhere()] * len(operands),
        out_specs=[anywhere()] * len(outs),
        out_shape=[
            jax.ShapeDtypeStruct(roomy(shape) if index == large else shape, jnp.float32)
            for index, shape in enumerate(outs)
        ],
        scratch_shapes=[pltpu.VMEM(shape, jnp.float32) for shape in scratch + [buffers] * 2]
        + [
            pltpu.SemaphoreType.DMA((3, 4)),
            pltpu.SemaphoreType.DMA((2, tiles * TILE // PAIR_ROWS)),
        ],
        input_output_aliases={first + index: index for index in range(aliased)},
        compiler_params=pltpu.CompilerParams(vmem_limit_bytes=VMEM_LIMIT),
        cost_estimate=pl.CostEstimate(
            flops=80_000_000, bytes_accessed=8 << 20, transcendentals=1 << 21
        ),
    )(lists, *operands)


def exchange(message, devices):
    shape = message.shape
    sent = message.reshape(devices, 1, -1)
    return lax.all_to_all(sent, ("row", "col"), split_axis=0, concat_axis=0, tiled=True).reshape(
        shape
    )


def slab_local(field_rhs, positions, polar, grid_base, tile_lists):
    rows_count = lax.axis_size("row")
    cols_count = lax.axis_size("col")
    counts = (rows_count, cols_count)
    devices = rows_count * cols_count
    lengths = (CX * rows_count, CY * cols_count, KZ)
    spans = tuple(float(length) for length in lengths)
    atoms = polar.shape[-1]
    tile_count = atoms // TILE
    listed = tile_lists.shape[-1]
    tables = slab_tables(rows_count, cols_count)
    f32 = jnp.float32
    rhs = jnp.swapaxes(field_rhs[0, 0], 0, 1)
    place = jnp.swapaxes(positions[0], 0, 1)
    base = jnp.swapaxes(grid_base[0], 0, 1)
    polar = polar.reshape(1, atoms)
    lists = tile_lists[0, 0]
    quantities = 4 + 3 * RHS
    brick_rows = quantities * tile_count
    moment_rows = 3 * RHS * tile_count
    message_shape = (devices * X_PAD, KZ // devices * RHS * Y_PAD)
    last_shape = (devices * (X_PAD + 1), message_shape[1])
    row_shape = (3 * RHS, atoms)

    start, payload = call(pack_body, [(row_shape, f32), ((brick_rows, TILE), f32)], rhs, place, polar)

    def setup(*refs):
        setup_body(lengths, devices, *refs)

    message, splines, depth_high, depth_low = call(
        setup,
        [
            (message_shape, f32),
            ((2 * SLOT_ROWS + 2 * Y_PAD, atoms), f32),
            ((KZ, 2 * atoms), jnp.bfloat16),
            ((KZ, 2 * atoms), jnp.bfloat16),
        ],
        place,
        base,
        start,
        *[jnp.asarray(table) for table in tables["along_z"]],
    )
    constants = (
        jnp.asarray(tables["kernel"]),
        jnp.asarray(tables["forward_x"]),
        jnp.asarray(tables["backward_x"]),
        *[jnp.asarray(table) for table in tables["block"]],
    )
    message, near = join(message, payload)
    arrived = exchange(message, devices)

    def pair_first(first_tile, last_tile, fields, *after):
        def body(*refs):
            pair_first_body(first_tile, last_tile, tile_count, spans, *refs)

        tiles = last_tile - first_tile
        return pair_call(
            body,
            [(tile_count * listed * TILE, TILE)] * 2
            + [(last_tile * GROUP, TILE), (9 * 3 * tile_count, TILE)],
            [
                (9 * brick_rows, TILE),
                (tiles * listed * quantities * GROUP, TILE),
                (tiles * 4 * TILE, TILE),
                (tiles * 3 * RHS * TILE, TILE),
                (9 * 3 * tile_count, TILE),
                (last_tile * GROUP, TILE),
            ],
            lists,
            *near,
            *fields,
            *after,
            tiles=tiles,
            large=2 if first_tile > 0 else None,
            aliased=2 if first_tile > 0 else 0,
        )

    early = pair_first(0, EARLY_TILES, (), message)

    def middle_first(*refs):
        middle_first_body(counts, *refs)

    arrived, early = lax.optimization_barrier((arrived, tuple(early)))
    wave_shape = tables["kernel"].shape[1:]
    mixed, wave = call(
        middle_first,
        [(message_shape, f32), (wave_shape, f32)],
        arrived,
        *constants,
        own_block=1,
        near=1,
        large=(1,),
        vmem=MIDDLE_VMEM_LIMIT,
    )
    returned = exchange(mixed, devices)
    first_term, second_term, direct, near = pair_first(
        EARLY_TILES, tile_count, (early[2],), wave, *early[:2]
    )

    def sample(*refs):
        sample_body(devices, *refs)

    carried_shape = (16, atoms)
    field_shape = (tile_count * GROUP, TILE)
    carried, moments = call(
        sample,
        [(carried_shape, f32), ((moment_rows, TILE), f32)],
        returned,
        splines,
        depth_high,
        depth_low,
        start,
        Head(direct, field_shape),
        polar,
        near=1,
        large=(0,),
        vmem=MIDDLE_VMEM_LIMIT,
    )

    def spread(*refs):
        spread_body(devices, *refs)

    (message,) = call(
        spread,
        [(message_shape, f32)],
        splines,
        depth_high,
        depth_low,
        Head(carried, carried_shape),
    )
    message, near_moments = join(message, moments)
    arrived = exchange(message, devices)

    def pair_second(*refs):
        pair_second_body(tile_count, spans, *refs)

    (direct,) = pair_call(
        pair_second,
        [(tile_count * GROUP, TILE)],
        [
            (9 * 3 * tile_count, TILE),
            (9 * moment_rows, TILE),
            (tile_count * listed * 3 * GROUP, TILE),
            (tile_count * listed * 3 * RHS * GROUP, TILE),
            (tile_count * 3 * TILE, TILE),
            (tile_count * 3 * RHS * TILE, TILE),
            (tile_count * GROUP, TILE),
        ],
        lists,
        near,
        *near_moments,
        first_term,
        second_term,
        tiles=tile_count,
        large=0,
    )

    def middle_second(*refs):
        middle_second_body(counts, *refs)

    mixed, local = call(
        middle_second,
        [(last_shape, f32), ((32, atoms), f32)],
        arrived,
        *constants,
        Head(wave, wave_shape),
        start,
        Head(carried, carried_shape),
        Head(direct, field_shape),
        polar,
        own_block=1,
        near=1,
        vmem=MIDDLE_VMEM_LIMIT,
    )
    returned = exchange(mixed, devices)

    def final(*refs):
        final_body(devices, *refs)

    outs = final_call(
        final,
        [(rhs.shape, f32), (rhs.shape, f32)],
        returned,
        splines,
        depth_high,
        depth_low,
        rhs,
        local,
    )
    return tuple(jnp.swapaxes(out, 0, 1)[None, None] for out in outs)


def solution(mesh):
    placed = (
        P("row", "col", None, None, None),
        P("row", "col", None, None),
        P("row", "col", None),
        P("row", "col", None, None),
        P("row", "col", None, None),
    )
    devices = mesh.shape["row"] * mesh.shape["col"]
    return jax.shard_map(
        slab_local if KZ % devices == 0 else pencil_local,
        mesh=mesh,
        in_specs=placed,
        out_specs=(P("row", "col", None, None, None), P("row", "col", None, None, None)),
        check_vma=False,
    )
```

```python
import math

import jax
import jax.numpy as jnp
import ml_dtypes
import numpy as np
from jax import lax
from jax.experimental import pallas as pl
from jax.experimental.pallas import tpu as pltpu
from jax.sharding import PartitionSpec as P

CX = 8
CY = 4
KZ = 256
TILE = 128
RHS = 2
ITERS = 2


ewald_beta = 0.4
thole_a = 0.39
self_coef = 4.0 * ewald_beta**3 / (3.0 * math.sqrt(math.pi))
highest = lax.Precision.HIGHEST


def with_halo(cells, sides, width):
    for axis, dim in sides:
        count = lax.axis_size(axis)
        head = lax.slice_in_dim(cells, 0, width, axis=dim)
        tail = lax.slice_in_dim(cells, cells.shape[dim] - width, cells.shape[dim], axis=dim)
        cells = jnp.concatenate(
            [
                lax.ppermute(tail, axis, [(i, (i + 1) % count) for i in range(count)]),
                cells,
                lax.ppermute(head, axis, [((i + 1) % count, i) for i in range(count)]),
            ],
            axis=dim,
        )
    return cells


def spline_table(fraction):
    previous = {0: jnp.ones_like(fraction)}
    fourth = previous
    for degree in range(2, 6):
        current = {}
        for offset in range(degree):
            abscissa = fraction + offset
            summed = abscissa * previous.get(offset, 0.0) + (degree - abscissa) * previous.get(
                offset - 1, 0.0
            )
            current[offset] = summed / (degree - 1)
        if degree == 4:
            fourth = current
        previous = current
    values = jnp.stack([previous[4 - stencil] for stencil in range(5)])
    slopes = jnp.stack(
        [fourth.get(4 - stencil, 0.0) - fourth.get(3 - stencil, 0.0) for stencil in range(5)]
    )
    return (values, slopes)


def spline_modulus(wave_index, length):
    spline_coef = (1.0 / 24.0, 11.0 / 24.0, 11.0 / 24.0, 1.0 / 24.0)
    cosine_sum = jnp.zeros(wave_index.shape, jnp.float32)
    sine_sum = jnp.zeros(wave_index.shape, jnp.float32)
    for offset in range(4):
        angles = 2.0 * math.pi / length * (wave_index * offset % length).astype(jnp.float32)
        cosine_sum = cosine_sum + spline_coef[offset] * jnp.cos(angles)
        sine_sum = sine_sum + spline_coef[offset] * jnp.sin(angles)
    return cosine_sum * cosine_sum + sine_sum * sine_sum


def folded_square(wave_index, length):
    nearest = jnp.minimum(wave_index, length - wave_index).astype(jnp.float32) / length
    return nearest * nearest


def influence(wave_x, wave_y, wave_z, length_x, length_y, length_z):
    wave_norm = (
        folded_square(wave_x, length_x)
        + folded_square(wave_y, length_y)
        + folded_square(wave_z, length_z)
    )
    modulus = (
        spline_modulus(wave_x, length_x)
        * spline_modulus(wave_y, length_y)
        * spline_modulus(wave_z, length_z)
    )
    excluded = (wave_x * 2 == length_x) | (wave_y * 2 == length_y) | (wave_z * 2 == length_z)
    excluded = excluded | (wave_x == 0) & (wave_y == 0) & (wave_z == 0)
    safe_norm = jnp.where(excluded, 1.0, wave_norm)
    safe_modulus = jnp.where(excluded, 1.0, modulus)
    result = jnp.exp(-(math.pi**2 / ewald_beta**2) * safe_norm) / (
        math.pi * safe_norm * safe_modulus
    )
    return jnp.where(excluded, 0.0, result)


def tile_field(own_static, near_static, near_dipole, box_spans):
    listed_count = near_static.shape[0]
    tile_width = own_static.shape[1]
    box_span = jnp.array(box_spans, dtype=jnp.float32)[None, :, None, None]
    separation = near_static[:, 0:3, None, :] - own_static[None, 0:3, :, None]
    separation = separation - box_span * jnp.floor(separation / box_span + 0.5)
    dist_sq = jnp.sum(separation * separation, axis=1)
    itself = (jnp.arange(listed_count)[:, None, None] == 0) & (
        jnp.arange(tile_width)[:, None] == jnp.arange(tile_width)[None, :]
    )[None]
    safe_sq = jnp.where(itself, 1.0, dist_sq)
    distance = jnp.sqrt(safe_sq)
    scaled = distance / (own_static[3][None, :, None] * near_static[:, 3][:, None, :])
    cubed = thole_a * scaled * scaled * scaled
    damping = jnp.exp(-cubed)
    screen = lax.erfc(ewald_beta * distance)
    gaussian = 2.0 * ewald_beta / math.sqrt(math.pi) * jnp.exp(-(ewald_beta * ewald_beta) * safe_sq)
    inverse_sq = 1.0 / safe_sq
    inverse_cube = inverse_sq / distance
    first_term = (screen - damping) * inverse_cube + gaussian * inverse_sq
    second = (
        3.0 * (screen - (1.0 + cubed) * damping) * inverse_cube * inverse_sq
        + gaussian * (2.0 * ewald_beta * ewald_beta + 3.0 * inverse_sq) * inverse_sq
    )
    first_term = jnp.where(itself, 0.0, first_term)
    second = jnp.where(itself, 0.0, second)
    projected = jnp.sum(near_dipole[:, :, :, None, :] * separation[:, None, :, :, :], axis=2)
    weighted = second[:, None] * projected
    outward = jnp.sum(weighted[:, :, None] * separation[:, None], axis=(0, 4))
    inward = jnp.sum(first_term[:, None, None] * near_dipole[:, :, :, None, :], axis=(0, 4))
    return outward - inward


def hartley(length):
    counter = jnp.arange(length, dtype=jnp.int32)
    angles = (
        2.0 * math.pi / length * (counter[:, None] * counter[None, :] % length).astype(jnp.float32)
    )
    return jnp.cos(angles) + jnp.sin(angles)


def placed_table(first_cell, weights, extent):
    slot_index = jnp.arange(extent, dtype=jnp.int32)[:, None]
    placed = jnp.zeros((extent, first_cell.shape[0]), jnp.float32)
    for stencil in range(5):
        placed = placed + jnp.where(
            slot_index == (first_cell[None, :] + stencil) % extent, weights[stencil][None, :], 0.0
        )
    return placed


def pad_axis(source, axis_pos, leading, trailing):
    widths = [(0, 0)] * source.ndim
    widths[axis_pos] = (leading, trailing)
    return jnp.pad(source, widths)


def fold_cycle(cycle_only, axis_pos, inner_len):
    middle = lax.slice_in_dim(cycle_only, 4, inner_len + 4, axis=axis_pos)
    lower_cycle = lax.slice_in_dim(cycle_only, 0, 2, axis=axis_pos)
    upper_cycle = lax.slice_in_dim(cycle_only, inner_len + 6, inner_len + 8, axis=axis_pos)
    return (
        middle
        + pad_axis(lower_cycle, axis_pos, 0, inner_len - 2)
        + pad_axis(upper_cycle, axis_pos, inner_len - 2, 0)
    )


def clear_inside(extended, extents):
    inside = None
    for axis_pos, inner_len in extents:
        slot_index = lax.broadcasted_iota(jnp.int32, extended.shape, axis_pos)
        within = (slot_index >= 2) & (slot_index < inner_len + 6)
        inside = within if inside is None else inside & within
    return jnp.where(inside, 0.0, extended)


def inner_sum(left_arr, right_arr):
    return lax.psum(jnp.sum(left_arr * right_arr, axis=(1, 2)), ("row", "col"))


def pencil_local(field_rhs, positions, polar, grid_base, tile_lists):
    rows_count = lax.axis_size("row")
    cols_count = lax.axis_size("col")
    grid_x = CX * rows_count
    grid_y = CY * cols_count
    atom_count = polar.shape[-1]
    tile_count = atom_count // TILE
    slab_depth = KZ // tile_count
    window_len = slab_depth + 4
    box_spans = (float(grid_x), float(grid_y), float(KZ))
    own_place = positions[0, 0]
    own_base = grid_base[0, 0]
    own_polar = polar[0, 0]
    lengths = jnp.array([grid_x, grid_y, KZ], dtype=jnp.int32)[:, None]
    cell_index = (own_base + 2) % lengths
    fraction = own_place - cell_index.astype(jnp.float32)
    values, slopes = spline_table(fraction)
    first_x = (own_base[0] - lax.axis_index("row") * CX + 2) % grid_x
    first_y = (own_base[1] - lax.axis_index("col") * CY + 2) % grid_y
    rows_x = placed_table(first_x, values[:, 0], CX + 4)
    slope_x = placed_table(first_x, slopes[:, 0], CX + 4)
    rows_y = placed_table(first_y, values[:, 1], CY + 4)
    slope_y = placed_table(first_y, slopes[:, 1], CY + 4)
    tile_start = jnp.arange(atom_count, dtype=jnp.int32) // TILE * slab_depth
    first_z = (own_base[2] + 2 - tile_start) % KZ
    rows_z = placed_table(first_z, values[:, 2], window_len)
    slope_z = placed_table(first_z, slopes[:, 2], window_len)
    plane_count = (CX + 4) * (CY + 4)
    plane_dx = (slope_x[:, None, :] * rows_y[None, :, :]).reshape(plane_count, atom_count)
    plane_dy = (rows_x[:, None, :] * slope_y[None, :, :]).reshape(plane_count, atom_count)
    plane_flat = (rows_x[:, None, :] * rows_y[None, :, :]).reshape(plane_count, atom_count)
    window_rows = jnp.moveaxis(rows_z.reshape(window_len, tile_count, TILE), 1, 0)
    window_slope = jnp.moveaxis(slope_z.reshape(window_len, tile_count, TILE), 1, 0)
    depth_table = jnp.concatenate([window_rows, window_slope], axis=2)
    grid_scale = 1.0 / (grid_x * grid_y * KZ)
    hartley_x = hartley(grid_x)
    hartley_y = hartley(grid_y)
    hartley_z = hartley(KZ)
    block_y = grid_y // rows_count
    block_z = KZ // cols_count
    wave_x = jnp.arange(grid_x, dtype=jnp.int32)[:, None, None]
    wave_y = (lax.axis_index("row") * block_y + jnp.arange(block_y, dtype=jnp.int32))[None, :, None]
    wave_z = (lax.axis_index("col") * block_z + jnp.arange(block_z, dtype=jnp.int32))[None, None, :]
    kernel = influence(wave_x, wave_y, wave_z, grid_x, grid_y, KZ) * grid_scale
    root_scale = jnp.power(own_polar, 1.0 / 6.0)
    own_static = jnp.concatenate([own_place, root_scale[None]], axis=0)
    near_static = with_halo(own_static[None, None], (("row", 0), ("col", 1)), 1)
    near_static = jnp.moveaxis(near_static.reshape(9, 4, tile_count, TILE), 2, 1).reshape(
        9 * tile_count, 4, TILE
    )
    own_tiles = jnp.moveaxis(own_static.reshape(4, tile_count, TILE), 1, 0)
    own_lists = tile_lists[0, 0]
    polar_wide = own_polar[None, None, :]
    solution = jnp.zeros_like(field_rhs[0, 0])
    residual = field_rhs[0, 0]
    scaled_res = polar_wide * residual
    direction = scaled_res
    progress = inner_sum(residual, scaled_res)
    for iteration in range(ITERS):
        near_dip = with_halo(direction[None, None], (("row", 0), ("col", 1)), 1)
        near_dip = jnp.moveaxis(near_dip.reshape(9, RHS, 3, tile_count, TILE), 3, 1).reshape(
            9 * tile_count, RHS, 3, TILE
        )

        def one_tile(tile_pos):
            picked = own_lists[tile_pos]
            return tile_field(own_tiles[tile_pos], near_static[picked], near_dip[picked], box_spans)

        fields = lax.map(one_tile, jnp.arange(tile_count, dtype=jnp.int32))
        direct = jnp.moveaxis(fields, 0, 2).reshape(RHS, 3, atom_count)
        slope_terms = (
            direction[:, 0, None, :] * plane_dx[None] + direction[:, 1, None, :] * plane_dy[None]
        )
        flat_terms = direction[:, 2, None, :] * plane_flat[None]
        spread_left = jnp.concatenate(
            [
                slope_terms.reshape(RHS, plane_count, tile_count, TILE),
                flat_terms.reshape(RHS, plane_count, tile_count, TILE),
            ],
            axis=3,
        )
        spread_windows = jnp.einsum("sptb,twb->sptw", spread_left, depth_table, precision=highest)
        main_part = spread_windows[..., :slab_depth].reshape(spread_windows.shape[:-2] + (KZ,))
        tail_part = pad_axis(
            spread_windows[..., slab_depth:], spread_windows.ndim - 1, 0, slab_depth - 4
        )
        tail_part = tail_part.reshape(spread_windows.shape[:-2] + (KZ,))[..., : KZ + 4 - slab_depth]
        last_axis = main_part.ndim - 1
        padded_line = pad_axis(main_part, last_axis, 0, 4) + pad_axis(
            tail_part, last_axis, slab_depth, 0
        )
        inner = padded_line[..., 2 : KZ + 2]
        spread_tile = (
            inner
            + pad_axis(padded_line[..., 0:2], last_axis, KZ - 2, 0)
            + pad_axis(padded_line[..., KZ + 2 : KZ + 4], last_axis, 0, KZ - 2)
        ).reshape(RHS, CX + 4, CY + 4, KZ)
        extended = with_halo(spread_tile, (("row", 1), ("col", 2)), 2)
        cycle_only = clear_inside(extended, ((1, CX), (2, CY)))
        folded = fold_cycle(fold_cycle(cycle_only, 1, CX), 2, CY)
        spectrum = jnp.einsum(
            "sxyz,zk->sxyk",
            spread_tile[:, 2 : CX + 2, 2 : CY + 2] + folded,
            hartley_z,
            precision=highest,
        )
        along_y = jnp.einsum(
            "sxyz,yk->sxkz",
            lax.all_to_all(spectrum, "col", split_axis=3, concat_axis=2, tiled=True),
            hartley_y,
            precision=highest,
        )
        along_x = (
            jnp.einsum(
                "sxyz,xk->skyz",
                lax.all_to_all(along_y, "row", split_axis=2, concat_axis=1, tiled=True),
                hartley_x,
                precision=highest,
            )
            * kernel[None]
        )
        mixed_part = jnp.einsum("sxyz,xk->skyz", along_x, hartley_x, precision=highest)
        returned = lax.all_to_all(mixed_part, "row", split_axis=1, concat_axis=2, tiled=True)
        swapped = jnp.einsum("sxyz,yk->sxkz", returned, hartley_y, precision=highest)
        restored = lax.all_to_all(swapped, "col", split_axis=2, concat_axis=3, tiled=True)
        padded = with_halo(
            jnp.einsum("sxyz,zk->sxyk", restored, hartley_z, precision=highest),
            (("row", 1), ("col", 2)),
            2,
        )
        line = padded.reshape(RHS, plane_count, KZ)
        extended_line = jnp.concatenate([line[..., KZ - 2 :], line, line[..., :2]], axis=-1)
        windows = jnp.stack(
            [
                extended_line[..., tile * slab_depth : tile * slab_depth + window_len]
                for tile in range(tile_count)
            ],
            axis=-2,
        )
        sampled = jnp.einsum("sptw,twb->sptb", windows, depth_table, precision=highest)
        with_flat = sampled[..., :TILE].reshape(RHS, plane_count, atom_count)
        with_slope = sampled[..., TILE:].reshape(RHS, plane_count, atom_count)
        recip_part = jnp.stack(
            [
                jnp.sum(with_flat * plane_dx[None], axis=1),
                jnp.sum(with_flat * plane_dy[None], axis=1),
                jnp.sum(with_slope * plane_flat[None], axis=1),
            ],
            axis=1,
        )
        image_field = direction / polar_wide - direct + recip_part - self_coef * direction
        step_size = (progress / inner_sum(direction, image_field))[:, None, None]
        solution = solution + step_size * direction
        residual = residual - step_size * image_field
        scaled_res = polar_wide * residual
        progress_next = inner_sum(residual, scaled_res)
        direction = scaled_res + (progress_next / progress)[:, None, None] * direction
        progress = progress_next
    return (solution[None, None], residual[None, None])


X_PAD = CX + 4
Y_PAD = CY + 4
SLOT_ROWS = 16
SPLIT = 2
VMEM_LIMIT = 60_000_000
SMALL_VMEM_LIMIT = 24_000_000
MIDDLE_VMEM_LIMIT = 56_000_000
ROOMY_BYTES = 12 << 20
EARLY_TILES = 1
PAIR_ROWS = 32
GROUP = 8
SCREEN_SCALE = 0.4
SCREEN_COEF = (
    0.22567588090896606,
    0.2256690263748169,
    0.20785020291805267,
    0.16849851608276367,
    0.14156343042850494,
    -0.005832736846059561,
    0.16930203139781952,
    -0.1830107867717743,
    0.05028456076979637,
)


def halves(value):
    high = value.astype(jnp.bfloat16)
    return high, (value - high.astype(jnp.float32)).astype(jnp.bfloat16)


def halves_np(value):
    value = value.astype(np.float32)
    high = value.astype(ml_dtypes.bfloat16)
    return high, (value - high.astype(np.float32)).astype(ml_dtypes.bfloat16)


def product(left, right, left_dim=1, right_dim=0):
    def one(first, second):
        return lax.dot_general(
            first,
            second,
            (((left_dim,), (right_dim,)), ((), ())),
            preferred_element_type=jnp.float32,
        )

    return one(left[0], right[0]) + (one(left[1], right[0]) + one(left[0], right[1]))


def cas_np(wave, place, length):
    angles = 2.0 * np.pi / length * (wave[:, None] * place[None, :] % length)
    return np.cos(angles) + np.sin(angles)


def modulus_np(wave, length):
    coef = np.array([1.0, 11.0, 11.0, 1.0]) / 24.0
    angles = 2.0 * np.pi / length * (wave[:, None] * np.arange(4)[None, :])
    return (coef * np.cos(angles)).sum(1) ** 2 + (coef * np.sin(angles)).sum(1) ** 2


def influence_np(length_x, length_y, length_z):
    total = np.zeros((length_x, length_y, length_z))
    modulus = np.ones((length_x, length_y, length_z))
    excluded = np.zeros((length_x, length_y, length_z), bool)
    for axis, length in enumerate((length_x, length_y, length_z)):
        wave = np.arange(length)
        shape = [1, 1, 1]
        shape[axis] = length
        total = total + ((np.minimum(wave, length - wave) / length) ** 2).reshape(shape)
        modulus = modulus * modulus_np(wave, length).reshape(shape)
        excluded = excluded | (wave * 2 == length).reshape(shape)
    excluded[0, 0, 0] = True
    safe = np.where(excluded, 1.0, total)
    result = np.exp(-(np.pi**2) / ewald_beta**2 * safe) / (
        np.pi * safe * np.where(excluded, 1.0, modulus)
    )
    return np.where(excluded, 0.0, result) / (length_x * length_y * length_z)


def slab_tables(rows_count, cols_count):
    grid_x = CX * rows_count
    grid_y = CY * cols_count
    devices = rows_count * cols_count
    chunk = KZ // devices
    wave_z = (np.arange(devices)[None, :] * chunk + np.arange(chunk)[:, None]).reshape(-1)
    along_z = cas_np(wave_z, np.arange(KZ), KZ)
    place_x = np.arange(rows_count)[:, None] * CX + np.arange(X_PAD)[None, :] - 2
    along_x = cas_np(np.arange(grid_x), place_x.reshape(-1) % grid_x, grid_x)
    x_high, x_low = halves_np(along_x)
    forward_x = np.concatenate([x_high, x_low, x_high], axis=1)
    backward_x = np.concatenate([x_high.T, x_low.T, x_high.T], axis=1)
    place_y = (np.arange(cols_count)[:, None] * CY + np.arange(Y_PAD)[None, :] - 2) % grid_y
    along_y = cas_np(np.arange(grid_y), place_y.reshape(-1), grid_y)
    along_y = along_y.reshape(grid_y, cols_count, Y_PAD)
    units = chunk * RHS // SPLIT
    block = np.einsum("uv,kcy->cuyvk", np.eye(units), along_y)
    block = block.reshape(cols_count * units * Y_PAD, units * grid_y)
    kernel = influence_np(grid_x, grid_y, KZ).reshape(grid_x, grid_y, devices, chunk)
    kernel = np.transpose(kernel, (2, 0, 3, 1))[:, :, :, None, :]
    kernel = np.broadcast_to(kernel, (devices, grid_x, chunk, RHS, grid_y))
    kernel = kernel.reshape(devices, grid_x, SPLIT, units * grid_y)
    kernel = np.moveaxis(kernel, 2, 1).reshape(devices, SPLIT * grid_x, units * grid_y)
    kernel = kernel.astype(np.float32)
    return dict(
        along_z=halves_np(along_z),
        forward_x=forward_x,
        backward_x=backward_x,
        block=halves_np(block),
        kernel=kernel,
    )


def pack_body(rhs_ref, place_ref, polar_ref, start_ref, payload_ref):
    polar = polar_ref[...]
    start = read_rows(rhs_ref) * polar
    start_ref[...] = start
    place = [place_ref[dim] for dim in range(3)]
    everything = jnp.concatenate(place + [1.0 / jnp.sqrt(polar), start], axis=0)
    store_payload(payload_ref, everything)


def read_rows(rows_ref):
    return jnp.concatenate([rows_ref[dim] for dim in range(3)], axis=0)


def store_payload(payload_ref, everything):
    tile_count = everything.shape[1] // TILE
    for quantity in range(everything.shape[0]):
        for tile in range(tile_count):
            row = quantity * tile_count + tile
            payload_ref[row : row + 1, :] = everything[
                quantity : quantity + 1, tile * TILE : (tile + 1) * TILE
            ]


def placed_rows(slot, weights, extent):
    slot_index = lax.broadcasted_iota(jnp.int32, (extent, slot.shape[1]), 0)
    placed = jnp.zeros((extent, slot.shape[1]), jnp.float32)
    for stencil in range(5):
        target = slot + stencil
        if extent == KZ:
            target = jnp.where(target >= KZ, target - KZ, target)
        placed = placed + jnp.where(slot_index == target, weights[stencil], 0.0)
    return placed


def spread_into(message_ref, moment, rows_x, slope_x, rows_y, slope_y, depth, devices):
    blocks = []
    for step in range(X_PAD):
        flat_x = rows_x[step : step + 1]
        tilt_x = slope_x[step : step + 1]
        for rhs in range(RHS):
            part_x = tilt_x * moment[rhs : rhs + 1]
            part_y = flat_x * moment[RHS + rhs : RHS + rhs + 1]
            part_z = flat_x * moment[2 * RHS + rhs : 2 * RHS + rhs + 1]
            blocks.append(
                jnp.concatenate([part_x * rows_y + part_y * slope_y, part_z * rows_y], axis=1)
            )
    charges = jnp.concatenate(blocks, axis=0)
    spectrum = product(depth, halves(charges), 1, 1)
    slot_rows = message_ref.shape[0] // devices
    chunk = KZ // devices
    width = RHS * Y_PAD
    for step in range(X_PAD):
        message_ref[pl.ds(step, devices, stride=slot_rows), :] = jnp.concatenate(
            [
                spectrum[unit * devices : (unit + 1) * devices, step * width : (step + 1) * width]
                for unit in range(chunk)
            ],
            axis=1,
        )


def sample_from(message_ref, rows_x, slope_x, rows_y, slope_y, depth, devices):
    chunk = KZ // devices
    width = RHS * Y_PAD
    slot_rows = message_ref.shape[0] // devices
    pieces = [
        message_ref[pl.ds(step, devices, stride=slot_rows), :] for step in range(X_PAD)
    ]
    spare = jnp.zeros((devices, KZ - X_PAD * width), jnp.float32)
    spectrum = jnp.concatenate(
        [
            jnp.concatenate(
                [piece[:, unit * width : (unit + 1) * width] for piece in pieces] + [spare], axis=1
            )
            for unit in range(chunk)
        ],
        axis=0,
    )
    spectrum = jnp.transpose(spectrum)[: X_PAD * width]
    sampled = product(halves(spectrum), depth, 1, 0)
    atoms = rows_x.shape[1]
    fields = [None] * (3 * RHS)
    for rhs in range(RHS):
        sum_x = sum_y = sum_z = None
        for step in range(X_PAD):
            first = step * width + rhs * Y_PAD
            flat = sampled[first : first + Y_PAD, :atoms]
            tilt = sampled[first : first + Y_PAD, atoms:]
            part_x = slope_x[step : step + 1] * flat
            part_y = rows_x[step : step + 1] * flat
            part_z = rows_x[step : step + 1] * tilt
            sum_x = part_x if sum_x is None else sum_x + part_x
            sum_y = part_y if sum_y is None else sum_y + part_y
            sum_z = part_z if sum_z is None else sum_z + part_z
        fields[rhs] = jnp.sum(sum_x * rows_y, axis=0, keepdims=True)
        fields[RHS + rhs] = jnp.sum(sum_y * slope_y, axis=0, keepdims=True)
        fields[2 * RHS + rhs] = jnp.sum(sum_z * rows_y, axis=0, keepdims=True)
    return jnp.concatenate(fields, axis=0)


def read_tables(tables_ref):
    return (
        tables_ref[0:X_PAD],
        tables_ref[SLOT_ROWS : SLOT_ROWS + X_PAD],
        tables_ref[2 * SLOT_ROWS : 2 * SLOT_ROWS + Y_PAD],
        tables_ref[2 * SLOT_ROWS + Y_PAD : 2 * SLOT_ROWS + 2 * Y_PAD],
    )


def setup_body(
    lengths,
    devices,
    place_ref,
    base_ref,
    start_ref,
    z_high_ref,
    z_low_ref,
    message_ref,
    tables_ref,
    depth_high_ref,
    depth_low_ref,
):
    base = [base_ref[dim] for dim in range(3)]
    fractions = []
    cells = []
    for dim in range(3):
        cell = base[dim] + 2
        cell = jnp.where(cell >= lengths[dim], cell - lengths[dim], cell)
        cells.append(cell)
        fractions.append(place_ref[dim] - cell.astype(jnp.float32))
    values, slopes = spline_table(jnp.concatenate(fractions, axis=0))
    values = [[values[stencil][dim : dim + 1] for stencil in range(5)] for dim in range(3)]
    slopes = [[slopes[stencil][dim : dim + 1] for stencil in range(5)] for dim in range(3)]
    slot_x = lax.rem(cells[0], CX)
    slot_y = lax.rem(cells[1], CY)
    tables_ref[0:SLOT_ROWS] = placed_rows(slot_x, values[0], SLOT_ROWS)
    tables_ref[SLOT_ROWS : 2 * SLOT_ROWS] = placed_rows(slot_x, slopes[0], SLOT_ROWS)
    tables_ref[2 * SLOT_ROWS : 2 * SLOT_ROWS + Y_PAD] = placed_rows(slot_y, values[1], Y_PAD)
    tables_ref[2 * SLOT_ROWS + Y_PAD : 2 * SLOT_ROWS + 2 * Y_PAD] = placed_rows(
        slot_y, slopes[1], Y_PAD
    )
    window = jnp.concatenate(
        [
            placed_rows(base[2], values[2], KZ),
            placed_rows(base[2], slopes[2], KZ),
        ],
        axis=1,
    )
    depth = product((z_high_ref[...], z_low_ref[...]), halves(window), 1, 0)
    depth = halves(depth)
    depth_high_ref[...] = depth[0]
    depth_low_ref[...] = depth[1]
    spread_into(message_ref, start_ref[...], *read_tables(tables_ref), depth, devices)


def transform_in(message_ref, forward_ref, block_high_ref, block_low_ref, rows_count, cols_count):
    gathered = jnp.concatenate(
        [
            jnp.concatenate(
                [
                    message_ref[(r * cols_count + c) * X_PAD : (r * cols_count + c + 1) * X_PAD]
                    for r in range(rows_count)
                ],
                axis=0,
            )
            for c in range(cols_count)
        ],
        axis=1,
    )
    high, low = halves(gathered)
    along = jnp.dot(
        forward_ref[...],
        jnp.concatenate([high, high, low], axis=0),
        preferred_element_type=jnp.float32,
    )
    part = along.shape[1] // cols_count // SPLIT
    along = jnp.concatenate(
        [
            jnp.concatenate(
                [
                    along[:, (c * SPLIT + half) * part : (c * SPLIT + half + 1) * part]
                    for c in range(cols_count)
                ],
                axis=1,
            )
            for half in range(SPLIT)
        ],
        axis=0,
    )
    return product(halves(along), (block_high_ref[...], block_low_ref[...]))


def transform_out(result_ref, values, backward_ref, block_high_ref, block_low_ref, counts):
    rows_count, cols_count = counts
    spread = product(halves(values), (block_high_ref[...], block_low_ref[...]), 1, 1)
    grid_x = spread.shape[0] // SPLIT
    part = spread.shape[1] // cols_count
    spread = jnp.concatenate(
        [
            spread[half * grid_x : (half + 1) * grid_x, c * part : (c + 1) * part]
            for c in range(cols_count)
            for half in range(SPLIT)
        ],
        axis=1,
    )
    high, low = halves(spread)
    along = jnp.dot(
        backward_ref[...],
        jnp.concatenate([high, high, low], axis=0),
        preferred_element_type=jnp.float32,
    )
    width = along.shape[1] // cols_count
    slot_rows = result_ref.shape[0] // (rows_count * cols_count)
    for r in range(rows_count):
        for c in range(cols_count):
            first = (r * cols_count + c) * slot_rows
            result_ref[first : first + X_PAD, :] = along[
                r * X_PAD : (r + 1) * X_PAD, c * width : (c + 1) * width
            ]


def middle_first_body(
    counts,
    message_ref,
    kernel_ref,
    forward_ref,
    backward_ref,
    block_high_ref,
    block_low_ref,
    result_ref,
    wave_ref,
):
    wave = transform_in(message_ref, forward_ref, block_high_ref, block_low_ref, *counts)
    wave_ref[...] = wave
    transform_out(
        result_ref, wave * kernel_ref[...], backward_ref, block_high_ref, block_low_ref, counts
    )


def gather_rows(parts):
    tiles = [
        parts[GROUP * tile : GROUP * tile + GROUP, :] for tile in range(parts.shape[0] // GROUP)
    ]
    return jnp.concatenate(tiles, axis=1)[0 : 3 * RHS]


def row_total(value, rhs):
    row = lax.broadcasted_iota(jnp.int32, value.shape, 0)
    return total(jnp.where(lax.rem(row, RHS) == rhs, value, 0.0))


def total(value):
    return jnp.sum(jnp.sum(value, axis=0, keepdims=True), axis=1, keepdims=True)


def middle_second_body(
    counts,
    message_ref,
    kernel_ref,
    forward_ref,
    backward_ref,
    block_high_ref,
    block_low_ref,
    wave_ref,
    start_ref,
    carried_ref,
    near_ref,
    polar_ref,
    result_ref,
    local_ref,
):
    near_rows = gather_rows(near_ref)
    wave = transform_in(message_ref, forward_ref, block_high_ref, block_low_ref, *counts)
    filtered = wave * kernel_ref[...]
    transform_out(result_ref, filtered, backward_ref, block_high_ref, block_low_ref, counts)
    before = wave_ref[...]
    grid_y = CY * counts[1]
    lane = lax.broadcasted_iota(jnp.int32, wave.shape, 1)
    own_rhs = lax.rem(lax.div(lane, grid_y), RHS)
    image = carried_ref[0 : 3 * RHS]
    second = carried_ref[8 : 8 + 3 * RHS]
    start = start_ref[...]
    local_part = second / polar_ref[...] - near_rows - self_coef * second
    local_ref[0 : 3 * RHS] = image
    local_ref[8 : 8 + 3 * RHS] = second
    local_ref[16 : 16 + 3 * RHS] = local_part
    local_ref[24 : 24 + 3 * RHS] = start
    slot = lax.broadcasted_iota(jnp.int32, (1, result_ref.shape[1]), 1)
    sums = jnp.zeros((1, result_ref.shape[1]), jnp.float32)
    for rhs in range(RHS):
        mine = own_rhs == rhs
        parts = (
            row_total(start * start / polar_ref[...], rhs),
            row_total(start * image, rhs),
            row_total(second * image, rhs),
            row_total(start * local_part, rhs) + total(jnp.where(mine, before * filtered, 0.0)),
            row_total(second * local_part, rhs) + total(jnp.where(mine, wave * filtered, 0.0)),
        )
        for index, part in enumerate(parts):
            sums = jnp.where(slot == rhs * len(parts) + index, part, sums)
    devices = counts[0] * counts[1]
    result_ref[pl.ds(X_PAD, devices, stride=X_PAD + 1), :] = jnp.broadcast_to(
        sums, (devices, sums.shape[1])
    )


def sample_body(
    devices,
    message_ref,
    tables_ref,
    depth_high_ref,
    depth_low_ref,
    start_ref,
    near_ref,
    polar_ref,
    carried_ref,
    payload_ref,
):
    tables = read_tables(tables_ref)
    depth = (depth_high_ref[...], depth_low_ref[...])
    field = sample_from(message_ref, *tables, depth, devices)
    start = start_ref[...]
    polar = polar_ref[...]
    image = start / polar - gather_rows(near_ref) + field - self_coef * start
    second = polar * image
    carried_ref[0 : 3 * RHS] = image
    carried_ref[8 : 8 + 3 * RHS] = second
    store_payload(payload_ref, second)


def spread_body(
    devices,
    tables_ref,
    depth_high_ref,
    depth_low_ref,
    carried_ref,
    result_ref,
):
    depth = (depth_high_ref[...], depth_low_ref[...])
    second = carried_ref[8 : 8 + 3 * RHS]
    spread_into(result_ref, second, *read_tables(tables_ref), depth, devices)


def final_body(
    devices,
    message_ref,
    tables_ref,
    depth_high_ref,
    depth_low_ref,
    rhs_ref,
    local_ref,
    dipole_ref,
    residual_ref,
):
    tables = read_tables(tables_ref)
    depth = (depth_high_ref[...], depth_low_ref[...])
    field = sample_from(message_ref, *tables, depth, devices)
    image = local_ref[0 : 3 * RHS]
    second = local_ref[8 : 8 + 3 * RHS]
    image_second = local_ref[16 : 16 + 3 * RHS] + field
    start = local_ref[24 : 24 + 3 * RHS]
    sums = jnp.sum(
        message_ref[pl.ds(X_PAD, devices, stride=X_PAD + 1), :], axis=0, keepdims=True
    )
    steps = []
    for rhs in range(RHS):
        progress, start_image, second_image, start_next, second_next = [
            sums[:, rhs * 5 + index : rhs * 5 + index + 1] for index in range(5)
        ]
        step = progress / start_image
        progress_next = progress - 2.0 * step * start_image + step * step * second_image
        grown = 1.0 + progress_next / progress
        curvature = (
            grown * grown * start_image
            - step * grown * (start_next + second_image)
            + step * step * second_next
        )
        steps.append((step, grown, progress_next / curvature))
    row = lax.broadcasted_iota(jnp.int32, (RHS, 1), 0)
    step, grown, step_next = [
        sum(jnp.where(row == rhs, steps[rhs][index], 0.0) for rhs in range(RHS))
        for index in range(3)
    ]
    for dim in range(3):
        rows = slice(dim * RHS, (dim + 1) * RHS)
        direction = grown * start[rows] - step * second[rows]
        image_direction = grown * image[rows] - step * image_second[rows]
        dipole_ref[dim] = step * start[rows] + step_next * direction
        residual_ref[dim] = rhs_ref[dim] - step * image[rows] - step_next * image_direction


def near_base(entry, brick_rows):
    return lax.shift_right_logical(entry, 2) * brick_rows + lax.bitwise_and(entry, 3)


def nearest(places, origin, span):
    return places - span * jnp.floor((places - origin) * (1.0 / span) + 0.5)


def unwrap_near(near, tile_count, spans):
    rows = near.shape[0] // 9
    for dim in range(2):
        own = 4 * rows + dim * tile_count
        origin = near[own : own + 1, 0:1]
        for brick in range(9):
            first = brick * rows + dim * tile_count
            near[first : first + tile_count, :] = nearest(
                near[first : first + tile_count, :], origin, spans[dim]
            )


def pick_rows(picked, near, lists_ref, tile, place, tile_count, quantities, origin, span):
    rows = near.shape[0] // 9
    place = place * lists_ref.shape[1] * quantities * GROUP
    for entry in range(lists_ref.shape[1]):
        base = near_base(lists_ref[tile, entry], rows)
        for quantity in range(quantities):
            values = near[pl.ds(base + quantity * tile_count, 1), :]
            if quantity == 2 and span is not None:
                values = nearest(values, origin, span)
            first = place + (entry * quantities + quantity) * GROUP
            picked[first : first + GROUP, :] = jnp.broadcast_to(values, (GROUP, TILE))


def widen_own(near, quantities, tile_count, tile, place, wide):
    offset = near.shape[0] // 9 * 4
    rows = [
        near[offset + quantity * tile_count + tile : offset + quantity * tile_count + tile + 1, :]
        for quantity in range(quantities)
    ]
    spare = jnp.zeros((TILE - quantities, TILE), jnp.float32)
    columns = jnp.transpose(jnp.concatenate(rows + [spare], axis=0))
    for quantity in range(quantities):
        first = (place * quantities + quantity) * TILE
        wide[first : first + TILE, :] = jnp.broadcast_to(
            columns[:, quantity : quantity + 1], (TILE, TILE)
        )


def add_field(sums, first_term, second_term, apart, moments):
    for rhs in range(RHS):
        moment = [moments[RHS * dim + rhs] for dim in range(3)]
        projected = moment[0] * apart[0] + moment[1] * apart[1] + moment[2] * apart[2]
        weighted = second_term * projected
        for dim in range(3):
            index = RHS * dim + rhs
            sums[index] = sums[index] + (weighted * apart[dim] - first_term * moment[dim])


def finish_sums(field_ref, sums_ref, first_tile, place):
    place = place * 3 * RHS
    lane = lax.broadcasted_iota(jnp.int32, (TILE, TILE), 1)
    merged = jnp.zeros((TILE, TILE), jnp.float32)
    for index in range(3 * RHS):
        first = (place + index) * TILE
        column = jnp.sum(sums_ref[first : first + TILE, :], axis=1, keepdims=True)
        merged = jnp.where(lane == index, column, merged)
    first = (first_tile + place // (3 * RHS)) * GROUP
    field_ref[first : first + GROUP, :] = jnp.transpose(merged)[0:GROUP]


def pair_rows(start, group):
    return pl.ds(pl.multiple_of(start + group * GROUP, GROUP), GROUP)


def wide_rows(start, group, quantity):
    return pl.ds(pl.multiple_of(quantity * TILE + start + group * GROUP, GROUP), GROUP)


def pair_terms(square_dist, damp):
    inverse = lax.rsqrt(square_dist)
    distance = square_dist * inverse
    inverse_sq = inverse * inverse
    inverse_cube = inverse_sq * inverse
    cubed = damp * (distance * square_dist)
    damping = jnp.exp(cubed)
    bell = jnp.exp(-(ewald_beta * ewald_beta) * square_dist)
    stretched = 1.0 + (SCREEN_SCALE * ewald_beta) * distance
    turned = pl.reciprocal(stretched, approx=True)
    turned = turned * (2.0 - stretched * turned)
    series = SCREEN_COEF[-1] * turned + SCREEN_COEF[-2]
    for coef in SCREEN_COEF[-3::-1]:
        series = series * turned + coef
    screen = bell * turned * series
    gaussian = (2.0 * ewald_beta / math.sqrt(math.pi)) * bell
    bare = screen - damping
    first_term = bare * inverse_cube + gaussian * inverse_sq
    second_term = (
        3.0 * (first_term + (cubed * damping) * inverse_cube)
        + (2.0 * ewald_beta * ewald_beta) * gaussian
    ) * inverse_sq
    return first_term, second_term


def step_rows(step, size, offset):
    return pl.ds(pl.multiple_of(step * size + offset, GROUP), GROUP)


def tile_rows(step, rows):
    return pl.ds(pl.multiple_of(step * rows, GROUP), rows)


def start_all(copies):
    for copy in copies:
        copy.start()


def wait_all(copies):
    for copy in copies:
        copy.wait()


def near_copies(sources, near, semaphore):
    rows = sources[0].shape[0]
    return [
        pltpu.make_async_copy(
            source, near.at[index * rows : (index + 1) * rows, :], semaphore.at[index]
        )
        for index, source in enumerate(sources)
    ]


def term_copies(terms, buffers, semaphore, begin, step, size, inward):
    rows = pl.ds(pl.multiple_of((begin + step) * size, GROUP), size)
    place = pl.ds(pl.multiple_of(step * size, GROUP), size)
    copies = []
    for index in range(2):
        far, here = terms[index].at[rows, :], buffers[index].at[place, :]
        ends = (far, here) if inward else (here, far)
        copies.append(pltpu.make_async_copy(*ends, semaphore.at[index, step]))
    return copies


def pair_first_body(
    first_tile,
    last_tile,
    tile_count,
    spans,
    lists_ref,
    up_ref,
    stack_ref,
    down_ref,
    *others,
):
    first_ref, second_ref, field_ref, near_ref = others[-14:-10]
    near, picked, wide, sums_ref, kept, field, first_buffer, second_buffer, semaphore, busy = others[-10:]
    terms = (first_ref, second_ref)
    buffers = (first_buffer, second_buffer)
    copies = near_copies((up_ref, stack_ref, down_ref), near, semaphore.at[0])
    if first_tile > 0:
        copies.append(
            pltpu.make_async_copy(
                others[0], field.at[0 : first_tile * GROUP, :], semaphore.at[0, 3]
            )
        )
    start_all(copies)
    wait_all(copies)
    entries = lists_ref.shape[1]
    rows = near.shape[0] // 9
    quantities = rows // tile_count
    unwrap_near(near, tile_count, spans)
    for brick in range(9):
        kept[brick * 3 * tile_count : (brick + 1) * 3 * tile_count, :] = near[
            brick * rows : brick * rows + 3 * tile_count, :
        ]
    keep = pltpu.make_async_copy(kept, near_ref, semaphore.at[1, 3])
    keep.start()
    for place, tile in enumerate(range(first_tile, last_tile)):
        widen_own(near, 4, tile_count, tile, place, wide)
        own = rows * 4 + 2 * tile_count + tile
        origin = near[own : own + 1, 0:1]
        pick_rows(picked, near, lists_ref, tile, place, tile_count, quantities, origin, spans[2])
    parts = TILE // PAIR_ROWS
    steps = (last_tile - first_tile) * parts

    size = entries * PAIR_ROWS

    def sent(step):
        return term_copies(terms, buffers, busy, first_tile * parts, step, size, False)

    @pl.loop(0, steps)
    def _(step):
        tile = lax.div(step, parts)
        start = lax.rem(step, parts) * PAIR_ROWS
        step_picked = picked.at[tile_rows(tile, entries * quantities * GROUP), :]
        step_wide = wide.at[tile_rows(tile, 4 * TILE), :]
        step_sums = sums_ref.at[tile_rows(tile, 3 * RHS * TILE), :]
        for group in range(PAIR_ROWS // GROUP):
            own = [step_wide[wide_rows(start, group, dim), :] for dim in range(4)]
            own_damp = -thole_a * own[3]
            sums = [jnp.zeros((GROUP, TILE), jnp.float32) for _ in range(3 * RHS)]
            itself = (
                lax.broadcasted_iota(jnp.int32, (GROUP, TILE), 0) + (start + group * GROUP)
            ) == lax.broadcasted_iota(jnp.int32, (GROUP, TILE), 1)
            for entry in range(entries):
                first = entry * quantities * GROUP
                rows = [
                    step_picked[first + quantity * GROUP : first + (quantity + 1) * GROUP, :]
                    for quantity in range(quantities)
                ]
                apart = [rows[dim] - own[dim] for dim in range(3)]
                square_dist = apart[0] * apart[0] + apart[1] * apart[1] + apart[2] * apart[2]
                if entry == 0:
                    square_dist = jnp.where(itself, 1.0, square_dist)
                first_term, second_term = pair_terms(square_dist, own_damp * rows[3])
                if entry == 0:
                    first_term = jnp.where(itself, 0.0, first_term)
                    second_term = jnp.where(itself, 0.0, second_term)
                place = step_rows(step, size, entry * PAIR_ROWS + group * GROUP)
                first_buffer[place, :] = first_term
                second_buffer[place, :] = second_term
                add_field(sums, first_term, second_term, apart, rows[4:])
            for index, value in enumerate(sums):
                step_sums[wide_rows(start, group, index), :] = value
        start_all(sent(step))

    for place in range(last_tile - first_tile):
        finish_sums(field, sums_ref, first_tile, place)
    result = pltpu.make_async_copy(field, head_of(field_ref, field), semaphore.at[1, 2])
    result.start()

    @pl.loop(0, steps)
    def _(step):
        wait_all(sent(step))

    keep.wait()
    result.wait()


def pair_second_body(
    tile_count,
    spans,
    lists_ref,
    near_ref,
    up_ref,
    stack_ref,
    down_ref,
    first_ref,
    second_ref,
    field_ref,
    near,
    near_moment,
    picked,
    picked_moment,
    wide,
    sums_ref,
    field,
    first_buffer,
    second_buffer,
    semaphore,
    busy,
):
    terms = (first_ref, second_ref)
    buffers = (first_buffer, second_buffer)
    parts = TILE // PAIR_ROWS
    steps = tile_count * parts

    entries = lists_ref.shape[1]
    size = entries * PAIR_ROWS

    def fetched(tile):
        return term_copies(terms, buffers, busy, 0, tile, size * parts, True)

    places = pltpu.make_async_copy(near_ref, near, semaphore.at[1, 3])
    places.start()
    copies = near_copies((up_ref, stack_ref, down_ref), near_moment, semaphore.at[2])
    start_all(copies)

    for tile in range(tile_count):
        start_all(fetched(tile))
    places.wait()
    for tile in range(tile_count):
        widen_own(near, 3, tile_count, tile, tile, wide)
        own = near.shape[0] // 9 * 4 + 2 * tile_count + tile
        origin = near[own : own + 1, 0:1]
        pick_rows(picked, near, lists_ref, tile, tile, tile_count, 3, origin, spans[2])
    wait_all(copies)
    for tile in range(tile_count):
        pick_rows(
            picked_moment, near_moment, lists_ref, tile, tile, tile_count, 3 * RHS, None, None
        )

    @pl.loop(0, steps)
    def _(step):
        tile = lax.div(step, parts)

        @pl.when(lax.rem(step, parts) == 0)
        def _():
            wait_all(fetched(tile))

        start = lax.rem(step, parts) * PAIR_ROWS
        step_picked = picked.at[tile_rows(tile, entries * 3 * GROUP), :]
        step_moment = picked_moment.at[tile_rows(tile, entries * 3 * RHS * GROUP), :]
        step_wide = wide.at[tile_rows(tile, 3 * TILE), :]
        step_sums = sums_ref.at[tile_rows(tile, 3 * RHS * TILE), :]
        for group in range(PAIR_ROWS // GROUP):
            own = [step_wide[wide_rows(start, group, dim), :] for dim in range(3)]
            sums = [jnp.zeros((GROUP, TILE), jnp.float32) for _ in range(3 * RHS)]
            for entry in range(entries):
                first = entry * 3 * GROUP
                apart = [
                    step_picked[first + dim * GROUP : first + (dim + 1) * GROUP, :] - own[dim]
                    for dim in range(3)
                ]
                first = first * RHS
                moments = [
                    step_moment[first + index * GROUP : first + (index + 1) * GROUP, :]
                    for index in range(3 * RHS)
                ]
                place = step_rows(step, size, entry * PAIR_ROWS + group * GROUP)
                add_field(sums, first_buffer[place, :], second_buffer[place, :], apart, moments)
            for index, value in enumerate(sums):
                step_sums[wide_rows(start, group, index), :] = value

    for place in range(tile_count):
        finish_sums(field, sums_ref, 0, place)
    result = pltpu.make_async_copy(field, head_of(field_ref, field), semaphore.at[1, 2])
    result.start()
    result.wait()


def shift(source, axis, step):
    count = lax.axis_size(axis)
    return lax.ppermute(source, axis, [(i, (i + step) % count) for i in range(count)])


def both_ways(source, axis):
    return shift(source, axis, 1), source, shift(source, axis, -1)


def whole(shape):
    return pl.BlockSpec(shape, lambda *_: (0,) * len(shape))


def anywhere():
    return pl.BlockSpec(memory_space=pl.ANY)


def join(message, payload):
    right = shift(payload, "col", -1)
    left = shift(payload, "col", 1)
    message, right, left = lax.optimization_barrier((message, right, left))
    return message, both_ways(jnp.concatenate([left, payload, right], axis=0), "row")


class Fetched:
    def __init__(self, source, scratch, semaphore):
        self.copy = pltpu.make_async_copy(source, scratch, semaphore)
        self.copy.start()
        self.scratch = scratch
        self.shape = scratch.shape
        self.waiting = True

    def wait(self):
        if self.waiting:
            self.copy.wait()
            self.waiting = False

    def __getitem__(self, index):
        self.wait()
        return self.scratch[index]


class Head:
    def __init__(self, array, shape):
        self.array = array
        self.shape = shape
        self.dtype = array.dtype


def roomy(shape):
    return (ROOMY_BYTES // 4 // shape[1], shape[1])


def head_of(far, here):
    if far.shape == here.shape:
        return far
    return far.at[0 : here.shape[0], :]


def call(body, outs, *operands, after=(), own_block=None, near=0, large=(), vmem=VMEM_LIMIT):
    count = len(operands)
    fetched = [
        pltpu.VMEM(operand.shape[1:] if index == own_block else operand.shape, operand.dtype)
        for index, operand in enumerate(operands)
        if index >= near
    ]
    arrays = [operand.array if isinstance(operand, Head) else operand for operand in operands]

    def run(*refs):
        refs = refs[len(after) :]
        sources, refs = refs[:count], refs[count:]
        results, refs = refs[: len(outs)], refs[len(outs) :]
        targets, written, semaphore = refs[: count - near], refs[count - near : -1], refs[-1]
        inputs = list(sources[:near])
        for index in range(near, count):
            source = sources[index]
            if index == own_block:
                place = lax.axis_index("row") * lax.axis_size("col") + lax.axis_index("col")
                source = source.at[place]
            else:
                source = head_of(source, targets[index - near])
            inputs.append(Fetched(source, targets[index - near], semaphore.at[index]))
        body(*inputs, *written)
        for operand in inputs[near:]:
            operand.wait()
        copies = [
            pltpu.make_async_copy(value, head_of(result, value), semaphore.at[count + index])
            for index, (value, result) in enumerate(zip(written, results))
        ]
        for copy in copies:
            copy.start()
        for copy in copies:
            copy.wait()

    return pl.pallas_call(
        run,
        in_specs=[anywhere()] * len(after)
        + [pl.BlockSpec(memory_space=pltpu.VMEM)] * near
        + [anywhere()] * (count - near),
        out_specs=[anywhere()] * len(outs),
        out_shape=[
            jax.ShapeDtypeStruct(roomy(shape) if index in large else shape, dtype)
            for index, (shape, dtype) in enumerate(outs)
        ],
        scratch_shapes=fetched
        + [pltpu.VMEM(shape, dtype) for shape, dtype in outs]
        + [pltpu.SemaphoreType.DMA((count + len(outs),))],
        compiler_params=pltpu.CompilerParams(vmem_limit_bytes=vmem),
        cost_estimate=pl.CostEstimate(
            flops=200_000_000, bytes_accessed=4 << 20, transcendentals=0
        ),
    )(*after, *arrays)


def final_call(body, outs, *operands):
    return pl.pallas_call(
        body,
        grid=(1,),
        in_specs=[whole(operand.shape) for operand in operands],
        out_specs=[whole(shape) for shape, _ in outs],
        out_shape=[jax.ShapeDtypeStruct(shape, dtype) for shape, dtype in outs],
        compiler_params=pltpu.CompilerParams(vmem_limit_bytes=SMALL_VMEM_LIMIT),
    )(*operands)


def pair_call(body, outs, scratch, lists, *operands, tiles, large, aliased=0):
    buffers = (tiles * lists.shape[1] * TILE, TILE)
    first = 1 + len(operands) - aliased
    return pl.pallas_call(
        body,
        in_specs=[pl.BlockSpec(memory_space=pltpu.SMEM)] + [anywhere()] * len(operands),
        out_specs=[anywhere()] * len(outs),
        out_shape=[
            jax.ShapeDtypeStruct(roomy(shape) if index == large else shape, jnp.float32)
            for index, shape in enumerate(outs)
        ],
        scratch_shapes=[pltpu.VMEM(shape, jnp.float32) for shape in scratch + [buffers] * 2]
        + [
            pltpu.SemaphoreType.DMA((3, 4)),
            pltpu.SemaphoreType.DMA((2, tiles * TILE // PAIR_ROWS)),
        ],
        input_output_aliases={first + index: index for index in range(aliased)},
        compiler_params=pltpu.CompilerParams(vmem_limit_bytes=VMEM_LIMIT),
        cost_estimate=pl.CostEstimate(
            flops=80_000_000, bytes_accessed=8 << 20, transcendentals=1 << 21
        ),
    )(lists, *operands)


def exchange(message, devices):
    shape = message.shape
    sent = message.reshape(devices, 1, -1)
    return lax.all_to_all(sent, ("row", "col"), split_axis=0, concat_axis=0, tiled=True).reshape(
        shape
    )


def slab_local(field_rhs, positions, polar, grid_base, tile_lists):
    rows_count = lax.axis_size("row")
    cols_count = lax.axis_size("col")
    counts = (rows_count, cols_count)
    devices = rows_count * cols_count
    lengths = (CX * rows_count, CY * cols_count, KZ)
    spans = tuple(float(length) for length in lengths)
    atoms = polar.shape[-1]
    tile_count = atoms // TILE
    listed = tile_lists.shape[-1]
    tables = slab_tables(rows_count, cols_count)
    f32 = jnp.float32
    rhs = jnp.swapaxes(field_rhs[0, 0], 0, 1)
    place = jnp.swapaxes(positions[0], 0, 1)
    base = jnp.swapaxes(grid_base[0], 0, 1)
    polar = polar.reshape(1, atoms)
    lists = tile_lists[0, 0]
    quantities = 4 + 3 * RHS
    brick_rows = quantities * tile_count
    moment_rows = 3 * RHS * tile_count
    message_shape = (devices * X_PAD, KZ // devices * RHS * Y_PAD)
    last_shape = (devices * (X_PAD + 1), message_shape[1])
    row_shape = (3 * RHS, atoms)

    start, payload = call(pack_body, [(row_shape, f32), ((brick_rows, TILE), f32)], rhs, place, polar)

    def setup(*refs):
        setup_body(lengths, devices, *refs)

    message, splines, depth_high, depth_low = call(
        setup,
        [
            (message_shape, f32),
            ((2 * SLOT_ROWS + 2 * Y_PAD, atoms), f32),
            ((KZ, 2 * atoms), jnp.bfloat16),
            ((KZ, 2 * atoms), jnp.bfloat16),
        ],
        place,
        base,
        start,
        *[jnp.asarray(table) for table in tables["along_z"]],
    )
    constants = (
        jnp.asarray(tables["kernel"]),
        jnp.asarray(tables["forward_x"]),
        jnp.asarray(tables["backward_x"]),
        *[jnp.asarray(table) for table in tables["block"]],
    )
    message, near = join(message, payload)
    arrived = exchange(message, devices)

    def pair_first(first_tile, last_tile, fields, *after):
        def body(*refs):
            pair_first_body(first_tile, last_tile, tile_count, spans, *refs)

        tiles = last_tile - first_tile
        return pair_call(
            body,
            [(tile_count * listed * TILE, TILE)] * 2
            + [(last_tile * GROUP, TILE), (9 * 3 * tile_count, TILE)],
            [
                (9 * brick_rows, TILE),
                (tiles * listed * quantities * GROUP, TILE),
                (tiles * 4 * TILE, TILE),
                (tiles * 3 * RHS * TILE, TILE),
                (9 * 3 * tile_count, TILE),
                (last_tile * GROUP, TILE),
            ],
            lists,
            *near,
            *fields,
            *after,
            tiles=tiles,
            large=2 if first_tile > 0 else None,
            aliased=2 if first_tile > 0 else 0,
        )

    early = pair_first(0, EARLY_TILES, (), message)

    def middle_first(*refs):
        middle_first_body(counts, *refs)

    arrived, early = lax.optimization_barrier((arrived, tuple(early)))
    wave_shape = tables["kernel"].shape[1:]
    mixed, wave = call(
        middle_first,
        [(message_shape, f32), (wave_shape, f32)],
        arrived,
        *constants,
        own_block=1,
        near=1,
        large=(1,),
        vmem=MIDDLE_VMEM_LIMIT,
    )
    returned = exchange(mixed, devices)
    first_term, second_term, direct, near = pair_first(
        EARLY_TILES, tile_count, (early[2],), wave, *early[:2]
    )

    def sample(*refs):
        sample_body(devices, *refs)

    carried_shape = (16, atoms)
    field_shape = (tile_count * GROUP, TILE)
    carried, moments = call(
        sample,
        [(carried_shape, f32), ((moment_rows, TILE), f32)],
        returned,
        splines,
        depth_high,
        depth_low,
        start,
        Head(direct, field_shape),
        polar,
        near=1,
        large=(0,),
        vmem=MIDDLE_VMEM_LIMIT,
    )

    def spread(*refs):
        spread_body(devices, *refs)

    (message,) = call(
        spread,
        [(message_shape, f32)],
        splines,
        depth_high,
        depth_low,
        Head(carried, carried_shape),
    )
    message, near_moments = join(message, moments)
    arrived = exchange(message, devices)

    def pair_second(*refs):
        pair_second_body(tile_count, spans, *refs)

    (direct,) = pair_call(
        pair_second,
        [(tile_count * GROUP, TILE)],
        [
            (9 * 3 * tile_count, TILE),
            (9 * moment_rows, TILE),
            (tile_count * listed * 3 * GROUP, TILE),
            (tile_count * listed * 3 * RHS * GROUP, TILE),
            (tile_count * 3 * TILE, TILE),
            (tile_count * 3 * RHS * TILE, TILE),
            (tile_count * GROUP, TILE),
        ],
        lists,
        near,
        *near_moments,
        first_term,
        second_term,
        tiles=tile_count,
        large=0,
    )

    def middle_second(*refs):
        middle_second_body(counts, *refs)

    mixed, local = call(
        middle_second,
        [(last_shape, f32), ((32, atoms), f32)],
        arrived,
        *constants,
        Head(wave, wave_shape),
        start,
        Head(carried, carried_shape),
        Head(direct, field_shape),
        polar,
        own_block=1,
        near=1,
        vmem=MIDDLE_VMEM_LIMIT,
    )
    returned = exchange(mixed, devices)

    def final(*refs):
        final_body(devices, *refs)

    outs = final_call(
        final,
        [(rhs.shape, f32), (rhs.shape, f32)],
        returned,
        splines,
        depth_high,
        depth_low,
        rhs,
        local,
    )
    return tuple(jnp.swapaxes(out, 0, 1)[None, None] for out in outs)


def solution(mesh):
    placed = (
        P("row", "col", None, None, None),
        P("row", "col", None, None),
        P("row", "col", None),
        P("row", "col", None, None),
        P("row", "col", None, None),
    )
    devices = mesh.shape["row"] * mesh.shape["col"]
    return jax.shard_map(
        slab_local if KZ % devices == 0 else pencil_local,
        mesh=mesh,
        in_specs=placed,
        out_specs=(P("row", "col", None, None, None), P("row", "col", None, None, None)),
        check_vma=False,
    )
```

```python
import math

import jax
import jax.numpy as jnp
import ml_dtypes
import numpy as np
from jax import lax
from jax.experimental import pallas as pl
from jax.experimental.pallas import tpu as pltpu
from jax.sharding import PartitionSpec as P

CX = 8
CY = 4
KZ = 256
TILE = 128
RHS = 2
ITERS = 2


ewald_beta = 0.4
thole_a = 0.39
self_coef = 4.0 * ewald_beta**3 / (3.0 * math.sqrt(math.pi))
highest = lax.Precision.HIGHEST


def with_halo(cells, sides, width):
    for axis, dim in sides:
        count = lax.axis_size(axis)
        head = lax.slice_in_dim(cells, 0, width, axis=dim)
        tail = lax.slice_in_dim(cells, cells.shape[dim] - width, cells.shape[dim], axis=dim)
        cells = jnp.concatenate(
            [
                lax.ppermute(tail, axis, [(i, (i + 1) % count) for i in range(count)]),
                cells,
                lax.ppermute(head, axis, [((i + 1) % count, i) for i in range(count)]),
            ],
            axis=dim,
        )
    return cells


def spline_table(fraction):
    previous = {0: jnp.ones_like(fraction)}
    fourth = previous
    for degree in range(2, 6):
        current = {}
        for offset in range(degree):
            abscissa = fraction + offset
            summed = abscissa * previous.get(offset, 0.0) + (degree - abscissa) * previous.get(
                offset - 1, 0.0
            )
            current[offset] = summed / (degree - 1)
        if degree == 4:
            fourth = current
        previous = current
    values = jnp.stack([previous[4 - stencil] for stencil in range(5)])
    slopes = jnp.stack(
        [fourth.get(4 - stencil, 0.0) - fourth.get(3 - stencil, 0.0) for stencil in range(5)]
    )
    return (values, slopes)


def spline_modulus(wave_index, length):
    spline_coef = (1.0 / 24.0, 11.0 / 24.0, 11.0 / 24.0, 1.0 / 24.0)
    cosine_sum = jnp.zeros(wave_index.shape, jnp.float32)
    sine_sum = jnp.zeros(wave_index.shape, jnp.float32)
    for offset in range(4):
        angles = 2.0 * math.pi / length * (wave_index * offset % length).astype(jnp.float32)
        cosine_sum = cosine_sum + spline_coef[offset] * jnp.cos(angles)
        sine_sum = sine_sum + spline_coef[offset] * jnp.sin(angles)
    return cosine_sum * cosine_sum + sine_sum * sine_sum


def folded_square(wave_index, length):
    nearest = jnp.minimum(wave_index, length - wave_index).astype(jnp.float32) / length
    return nearest * nearest


def influence(wave_x, wave_y, wave_z, length_x, length_y, length_z):
    wave_norm = (
        folded_square(wave_x, length_x)
        + folded_square(wave_y, length_y)
        + folded_square(wave_z, length_z)
    )
    modulus = (
        spline_modulus(wave_x, length_x)
        * spline_modulus(wave_y, length_y)
        * spline_modulus(wave_z, length_z)
    )
    excluded = (wave_x * 2 == length_x) | (wave_y * 2 == length_y) | (wave_z * 2 == length_z)
    excluded = excluded | (wave_x == 0) & (wave_y == 0) & (wave_z == 0)
    safe_norm = jnp.where(excluded, 1.0, wave_norm)
    safe_modulus = jnp.where(excluded, 1.0, modulus)
    result = jnp.exp(-(math.pi**2 / ewald_beta**2) * safe_norm) / (
        math.pi * safe_norm * safe_modulus
    )
    return jnp.where(excluded, 0.0, result)


def tile_field(own_static, near_static, near_dipole, box_spans):
    listed_count = near_static.shape[0]
    tile_width = own_static.shape[1]
    box_span = jnp.array(box_spans, dtype=jnp.float32)[None, :, None, None]
    separation = near_static[:, 0:3, None, :] - own_static[None, 0:3, :, None]
    separation = separation - box_span * jnp.floor(separation / box_span + 0.5)
    dist_sq = jnp.sum(separation * separation, axis=1)
    itself = (jnp.arange(listed_count)[:, None, None] == 0) & (
        jnp.arange(tile_width)[:, None] == jnp.arange(tile_width)[None, :]
    )[None]
    safe_sq = jnp.where(itself, 1.0, dist_sq)
    distance = jnp.sqrt(safe_sq)
    scaled = distance / (own_static[3][None, :, None] * near_static[:, 3][:, None, :])
    cubed = thole_a * scaled * scaled * scaled
    damping = jnp.exp(-cubed)
    screen = lax.erfc(ewald_beta * distance)
    gaussian = 2.0 * ewald_beta / math.sqrt(math.pi) * jnp.exp(-(ewald_beta * ewald_beta) * safe_sq)
    inverse_sq = 1.0 / safe_sq
    inverse_cube = inverse_sq / distance
    first_term = (screen - damping) * inverse_cube + gaussian * inverse_sq
    second = (
        3.0 * (screen - (1.0 + cubed) * damping) * inverse_cube * inverse_sq
        + gaussian * (2.0 * ewald_beta * ewald_beta + 3.0 * inverse_sq) * inverse_sq
    )
    first_term = jnp.where(itself, 0.0, first_term)
    second = jnp.where(itself, 0.0, second)
    projected = jnp.sum(near_dipole[:, :, :, None, :] * separation[:, None, :, :, :], axis=2)
    weighted = second[:, None] * projected
    outward = jnp.sum(weighted[:, :, None] * separation[:, None], axis=(0, 4))
    inward = jnp.sum(first_term[:, None, None] * near_dipole[:, :, :, None, :], axis=(0, 4))
    return outward - inward


def hartley(length):
    counter = jnp.arange(length, dtype=jnp.int32)
    angles = (
        2.0 * math.pi / length * (counter[:, None] * counter[None, :] % length).astype(jnp.float32)
    )
    return jnp.cos(angles) + jnp.sin(angles)


def placed_table(first_cell, weights, extent):
    slot_index = jnp.arange(extent, dtype=jnp.int32)[:, None]
    placed = jnp.zeros((extent, first_cell.shape[0]), jnp.float32)
    for stencil in range(5):
        placed = placed + jnp.where(
            slot_index == (first_cell[None, :] + stencil) % extent, weights[stencil][None, :], 0.0
        )
    return placed


def pad_axis(source, axis_pos, leading, trailing):
    widths = [(0, 0)] * source.ndim
    widths[axis_pos] = (leading, trailing)
    return jnp.pad(source, widths)


def fold_cycle(cycle_only, axis_pos, inner_len):
    middle = lax.slice_in_dim(cycle_only, 4, inner_len + 4, axis=axis_pos)
    lower_cycle = lax.slice_in_dim(cycle_only, 0, 2, axis=axis_pos)
    upper_cycle = lax.slice_in_dim(cycle_only, inner_len + 6, inner_len + 8, axis=axis_pos)
    return (
        middle
        + pad_axis(lower_cycle, axis_pos, 0, inner_len - 2)
        + pad_axis(upper_cycle, axis_pos, inner_len - 2, 0)
    )


def clear_inside(extended, extents):
    inside = None
    for axis_pos, inner_len in extents:
        slot_index = lax.broadcasted_iota(jnp.int32, extended.shape, axis_pos)
        within = (slot_index >= 2) & (slot_index < inner_len + 6)
        inside = within if inside is None else inside & within
    return jnp.where(inside, 0.0, extended)


def inner_sum(left_arr, right_arr):
    return lax.psum(jnp.sum(left_arr * right_arr, axis=(1, 2)), ("row", "col"))


def pencil_local(field_rhs, positions, polar, grid_base, tile_lists):
    rows_count = lax.axis_size("row")
    cols_count = lax.axis_size("col")
    grid_x = CX * rows_count
    grid_y = CY * cols_count
    atom_count = polar.shape[-1]
    tile_count = atom_count // TILE
    slab_depth = KZ // tile_count
    window_len = slab_depth + 4
    box_spans = (float(grid_x), float(grid_y), float(KZ))
    own_place = positions[0, 0]
    own_base = grid_base[0, 0]
    own_polar = polar[0, 0]
    lengths = jnp.array([grid_x, grid_y, KZ], dtype=jnp.int32)[:, None]
    cell_index = (own_base + 2) % lengths
    fraction = own_place - cell_index.astype(jnp.float32)
    values, slopes = spline_table(fraction)
    first_x = (own_base[0] - lax.axis_index("row") * CX + 2) % grid_x
    first_y = (own_base[1] - lax.axis_index("col") * CY + 2) % grid_y
    rows_x = placed_table(first_x, values[:, 0], CX + 4)
    slope_x = placed_table(first_x, slopes[:, 0], CX + 4)
    rows_y = placed_table(first_y, values[:, 1], CY + 4)
    slope_y = placed_table(first_y, slopes[:, 1], CY + 4)
    tile_start = jnp.arange(atom_count, dtype=jnp.int32) // TILE * slab_depth
    first_z = (own_base[2] + 2 - tile_start) % KZ
    rows_z = placed_table(first_z, values[:, 2], window_len)
    slope_z = placed_table(first_z, slopes[:, 2], window_len)
    plane_count = (CX + 4) * (CY + 4)
    plane_dx = (slope_x[:, None, :] * rows_y[None, :, :]).reshape(plane_count, atom_count)
    plane_dy = (rows_x[:, None, :] * slope_y[None, :, :]).reshape(plane_count, atom_count)
    plane_flat = (rows_x[:, None, :] * rows_y[None, :, :]).reshape(plane_count, atom_count)
    window_rows = jnp.moveaxis(rows_z.reshape(window_len, tile_count, TILE), 1, 0)
    window_slope = jnp.moveaxis(slope_z.reshape(window_len, tile_count, TILE), 1, 0)
    depth_table = jnp.concatenate([window_rows, window_slope], axis=2)
    grid_scale = 1.0 / (grid_x * grid_y * KZ)
    hartley_x = hartley(grid_x)
    hartley_y = hartley(grid_y)
    hartley_z = hartley(KZ)
    block_y = grid_y // rows_count
    block_z = KZ // cols_count
    wave_x = jnp.arange(grid_x, dtype=jnp.int32)[:, None, None]
    wave_y = (lax.axis_index("row") * block_y + jnp.arange(block_y, dtype=jnp.int32))[None, :, None]
    wave_z = (lax.axis_index("col") * block_z + jnp.arange(block_z, dtype=jnp.int32))[None, None, :]
    kernel = influence(wave_x, wave_y, wave_z, grid_x, grid_y, KZ) * grid_scale
    root_scale = jnp.power(own_polar, 1.0 / 6.0)
    own_static = jnp.concatenate([own_place, root_scale[None]], axis=0)
    near_static = with_halo(own_static[None, None], (("row", 0), ("col", 1)), 1)
    near_static = jnp.moveaxis(near_static.reshape(9, 4, tile_count, TILE), 2, 1).reshape(
        9 * tile_count, 4, TILE
    )
    own_tiles = jnp.moveaxis(own_static.reshape(4, tile_count, TILE), 1, 0)
    own_lists = tile_lists[0, 0]
    polar_wide = own_polar[None, None, :]
    solution = jnp.zeros_like(field_rhs[0, 0])
    residual = field_rhs[0, 0]
    scaled_res = polar_wide * residual
    direction = scaled_res
    progress = inner_sum(residual, scaled_res)
    for iteration in range(ITERS):
        near_dip = with_halo(direction[None, None], (("row", 0), ("col", 1)), 1)
        near_dip = jnp.moveaxis(near_dip.reshape(9, RHS, 3, tile_count, TILE), 3, 1).reshape(
            9 * tile_count, RHS, 3, TILE
        )

        def one_tile(tile_pos):
            picked = own_lists[tile_pos]
            return tile_field(own_tiles[tile_pos], near_static[picked], near_dip[picked], box_spans)

        fields = lax.map(one_tile, jnp.arange(tile_count, dtype=jnp.int32))
        direct = jnp.moveaxis(fields, 0, 2).reshape(RHS, 3, atom_count)
        slope_terms = (
            direction[:, 0, None, :] * plane_dx[None] + direction[:, 1, None, :] * plane_dy[None]
        )
        flat_terms = direction[:, 2, None, :] * plane_flat[None]
        spread_left = jnp.concatenate(
            [
                slope_terms.reshape(RHS, plane_count, tile_count, TILE),
                flat_terms.reshape(RHS, plane_count, tile_count, TILE),
            ],
            axis=3,
        )
        spread_windows = jnp.einsum("sptb,twb->sptw", spread_left, depth_table, precision=highest)
        main_part = spread_windows[..., :slab_depth].reshape(spread_windows.shape[:-2] + (KZ,))
        tail_part = pad_axis(
            spread_windows[..., slab_depth:], spread_windows.ndim - 1, 0, slab_depth - 4
        )
        tail_part = tail_part.reshape(spread_windows.shape[:-2] + (KZ,))[..., : KZ + 4 - slab_depth]
        last_axis = main_part.ndim - 1
        padded_line = pad_axis(main_part, last_axis, 0, 4) + pad_axis(
            tail_part, last_axis, slab_depth, 0
        )
        inner = padded_line[..., 2 : KZ + 2]
        spread_tile = (
            inner
            + pad_axis(padded_line[..., 0:2], last_axis, KZ - 2, 0)
            + pad_axis(padded_line[..., KZ + 2 : KZ + 4], last_axis, 0, KZ - 2)
        ).reshape(RHS, CX + 4, CY + 4, KZ)
        extended = with_halo(spread_tile, (("row", 1), ("col", 2)), 2)
        cycle_only = clear_inside(extended, ((1, CX), (2, CY)))
        folded = fold_cycle(fold_cycle(cycle_only, 1, CX), 2, CY)
        spectrum = jnp.einsum(
            "sxyz,zk->sxyk",
            spread_tile[:, 2 : CX + 2, 2 : CY + 2] + folded,
            hartley_z,
            precision=highest,
        )
        along_y = jnp.einsum(
            "sxyz,yk->sxkz",
            lax.all_to_all(spectrum, "col", split_axis=3, concat_axis=2, tiled=True),
            hartley_y,
            precision=highest,
        )
        along_x = (
            jnp.einsum(
                "sxyz,xk->skyz",
                lax.all_to_all(along_y, "row", split_axis=2, concat_axis=1, tiled=True),
                hartley_x,
                precision=highest,
            )
            * kernel[None]
        )
        mixed_part = jnp.einsum("sxyz,xk->skyz", along_x, hartley_x, precision=highest)
        returned = lax.all_to_all(mixed_part, "row", split_axis=1, concat_axis=2, tiled=True)
        swapped = jnp.einsum("sxyz,yk->sxkz", returned, hartley_y, precision=highest)
        restored = lax.all_to_all(swapped, "col", split_axis=2, concat_axis=3, tiled=True)
        padded = with_halo(
            jnp.einsum("sxyz,zk->sxyk", restored, hartley_z, precision=highest),
            (("row", 1), ("col", 2)),
            2,
        )
        line = padded.reshape(RHS, plane_count, KZ)
        extended_line = jnp.concatenate([line[..., KZ - 2 :], line, line[..., :2]], axis=-1)
        windows = jnp.stack(
            [
                extended_line[..., tile * slab_depth : tile * slab_depth + window_len]
                for tile in range(tile_count)
            ],
            axis=-2,
        )
        sampled = jnp.einsum("sptw,twb->sptb", windows, depth_table, precision=highest)
        with_flat = sampled[..., :TILE].reshape(RHS, plane_count, atom_count)
        with_slope = sampled[..., TILE:].reshape(RHS, plane_count, atom_count)
        recip_part = jnp.stack(
            [
                jnp.sum(with_flat * plane_dx[None], axis=1),
                jnp.sum(with_flat * plane_dy[None], axis=1),
                jnp.sum(with_slope * plane_flat[None], axis=1),
            ],
            axis=1,
        )
        image_field = direction / polar_wide - direct + recip_part - self_coef * direction
        step_size = (progress / inner_sum(direction, image_field))[:, None, None]
        solution = solution + step_size * direction
        residual = residual - step_size * image_field
        scaled_res = polar_wide * residual
        progress_next = inner_sum(residual, scaled_res)
        direction = scaled_res + (progress_next / progress)[:, None, None] * direction
        progress = progress_next
    return (solution[None, None], residual[None, None])


X_PAD = CX + 4
Y_PAD = CY + 4
SLOT_ROWS = 16
SPLIT = 2
VMEM_LIMIT = 60_000_000
SMALL_VMEM_LIMIT = 24_000_000
MIDDLE_VMEM_LIMIT = 56_000_000
ROOMY_BYTES = 12 << 20
EARLY_TILES = 1
PAIR_ROWS = 32
GROUP = 8
SCREEN_SCALE = 0.4
SCREEN_COEF = (
    0.22567588090896606,
    0.2256690263748169,
    0.20785020291805267,
    0.16849851608276367,
    0.14156343042850494,
    -0.005832736846059561,
    0.16930203139781952,
    -0.1830107867717743,
    0.05028456076979637,
)


def halves(value):
    high = value.astype(jnp.bfloat16)
    return high, (value - high.astype(jnp.float32)).astype(jnp.bfloat16)


def halves_np(value):
    value = value.astype(np.float32)
    high = value.astype(ml_dtypes.bfloat16)
    return high, (value - high.astype(np.float32)).astype(ml_dtypes.bfloat16)


def product(left, right, left_dim=1, right_dim=0):
    def one(first, second):
        return lax.dot_general(
            first,
            second,
            (((left_dim,), (right_dim,)), ((), ())),
            preferred_element_type=jnp.float32,
        )

    return one(left[0], right[0]) + (one(left[1], right[0]) + one(left[0], right[1]))


def cas_np(wave, place, length):
    angles = 2.0 * np.pi / length * (wave[:, None] * place[None, :] % length)
    return np.cos(angles) + np.sin(angles)


def modulus_np(wave, length):
    coef = np.array([1.0, 11.0, 11.0, 1.0]) / 24.0
    angles = 2.0 * np.pi / length * (wave[:, None] * np.arange(4)[None, :])
    return (coef * np.cos(angles)).sum(1) ** 2 + (coef * np.sin(angles)).sum(1) ** 2


def influence_np(length_x, length_y, length_z):
    total = np.zeros((length_x, length_y, length_z))
    modulus = np.ones((length_x, length_y, length_z))
    excluded = np.zeros((length_x, length_y, length_z), bool)
    for axis, length in enumerate((length_x, length_y, length_z)):
        wave = np.arange(length)
        shape = [1, 1, 1]
        shape[axis] = length
        total = total + ((np.minimum(wave, length - wave) / length) ** 2).reshape(shape)
        modulus = modulus * modulus_np(wave, length).reshape(shape)
        excluded = excluded | (wave * 2 == length).reshape(shape)
    excluded[0, 0, 0] = True
    safe = np.where(excluded, 1.0, total)
    result = np.exp(-(np.pi**2) / ewald_beta**2 * safe) / (
        np.pi * safe * np.where(excluded, 1.0, modulus)
    )
    return np.where(excluded, 0.0, result) / (length_x * length_y * length_z)


def slab_tables(rows_count, cols_count):
    grid_x = CX * rows_count
    grid_y = CY * cols_count
    devices = rows_count * cols_count
    chunk = KZ // devices
    wave_z = (np.arange(devices)[None, :] * chunk + np.arange(chunk)[:, None]).reshape(-1)
    along_z = cas_np(wave_z, np.arange(KZ), KZ)
    place_x = np.arange(rows_count)[:, None] * CX + np.arange(X_PAD)[None, :] - 2
    along_x = cas_np(np.arange(grid_x), place_x.reshape(-1) % grid_x, grid_x)
    x_high, x_low = halves_np(along_x)
    forward_x = np.concatenate([x_high, x_low, x_high], axis=1)
    backward_x = np.concatenate([x_high.T, x_low.T, x_high.T], axis=1)
    place_y = (np.arange(cols_count)[:, None] * CY + np.arange(Y_PAD)[None, :] - 2) % grid_y
    along_y = cas_np(np.arange(grid_y), place_y.reshape(-1), grid_y)
    along_y = along_y.reshape(grid_y, cols_count, Y_PAD)
    units = chunk * RHS // SPLIT
    block = np.einsum("uv,kcy->cuyvk", np.eye(units), along_y)
    block = block.reshape(cols_count * units * Y_PAD, units * grid_y)
    kernel = influence_np(grid_x, grid_y, KZ).reshape(grid_x, grid_y, devices, chunk)
    kernel = np.transpose(kernel, (2, 0, 3, 1))[:, :, :, None, :]
    kernel = np.broadcast_to(kernel, (devices, grid_x, chunk, RHS, grid_y))
    kernel = kernel.reshape(devices, grid_x, SPLIT, units * grid_y)
    kernel = np.moveaxis(kernel, 2, 1).reshape(devices, SPLIT * grid_x, units * grid_y)
    kernel = kernel.astype(np.float32)
    return dict(
        along_z=halves_np(along_z),
        forward_x=forward_x,
        backward_x=backward_x,
        block=halves_np(block),
        kernel=kernel,
    )


def pack_body(rhs_ref, place_ref, polar_ref, start_ref, payload_ref):
    polar = polar_ref[...]
    start = read_rows(rhs_ref) * polar
    start_ref[...] = start
    place = [place_ref[dim] for dim in range(3)]
    everything = jnp.concatenate(place + [1.0 / jnp.sqrt(polar), start], axis=0)
    store_payload(payload_ref, everything)


def read_rows(rows_ref):
    return jnp.concatenate([rows_ref[dim] for dim in range(3)], axis=0)


def store_payload(payload_ref, everything):
    tile_count = everything.shape[1] // TILE
    for quantity in range(everything.shape[0]):
        for tile in range(tile_count):
            row = quantity * tile_count + tile
            payload_ref[row : row + 1, :] = everything[
                quantity : quantity + 1, tile * TILE : (tile + 1) * TILE
            ]


def placed_rows(slot, weights, extent):
    slot_index = lax.broadcasted_iota(jnp.int32, (extent, slot.shape[1]), 0)
    placed = jnp.zeros((extent, slot.shape[1]), jnp.float32)
    for stencil in range(5):
        target = slot + stencil
        if extent == KZ:
            target = jnp.where(target >= KZ, target - KZ, target)
        placed = placed + jnp.where(slot_index == target, weights[stencil], 0.0)
    return placed


def spread_into(message_ref, moment, rows_x, slope_x, rows_y, slope_y, depth, devices):
    blocks = []
    for step in range(X_PAD):
        flat_x = rows_x[step : step + 1]
        tilt_x = slope_x[step : step + 1]
        for rhs in range(RHS):
            part_x = tilt_x * moment[rhs : rhs + 1]
            part_y = flat_x * moment[RHS + rhs : RHS + rhs + 1]
            part_z = flat_x * moment[2 * RHS + rhs : 2 * RHS + rhs + 1]
            blocks.append(
                jnp.concatenate([part_x * rows_y + part_y * slope_y, part_z * rows_y], axis=1)
            )
    charges = jnp.concatenate(blocks, axis=0)
    spectrum = product(depth, halves(charges), 1, 1)
    slot_rows = message_ref.shape[0] // devices
    chunk = KZ // devices
    width = RHS * Y_PAD
    for step in range(X_PAD):
        message_ref[pl.ds(step, devices, stride=slot_rows), :] = jnp.concatenate(
            [
                spectrum[unit * devices : (unit + 1) * devices, step * width : (step + 1) * width]
                for unit in range(chunk)
            ],
            axis=1,
        )


def sample_from(message_ref, rows_x, slope_x, rows_y, slope_y, depth, devices):
    chunk = KZ // devices
    width = RHS * Y_PAD
    slot_rows = message_ref.shape[0] // devices
    pieces = [
        message_ref[pl.ds(step, devices, stride=slot_rows), :] for step in range(X_PAD)
    ]
    spare = jnp.zeros((devices, KZ - X_PAD * width), jnp.float32)
    spectrum = jnp.concatenate(
        [
            jnp.concatenate(
                [piece[:, unit * width : (unit + 1) * width] for piece in pieces] + [spare], axis=1
            )
            for unit in range(chunk)
        ],
        axis=0,
    )
    spectrum = jnp.transpose(spectrum)[: X_PAD * width]
    sampled = product(halves(spectrum), depth, 1, 0)
    atoms = rows_x.shape[1]
    fields = [None] * (3 * RHS)
    for rhs in range(RHS):
        sum_x = sum_y = sum_z = None
        for step in range(X_PAD):
            first = step * width + rhs * Y_PAD
            flat = sampled[first : first + Y_PAD, :atoms]
            tilt = sampled[first : first + Y_PAD, atoms:]
            part_x = slope_x[step : step + 1] * flat
            part_y = rows_x[step : step + 1] * flat
            part_z = rows_x[step : step + 1] * tilt
            sum_x = part_x if sum_x is None else sum_x + part_x
            sum_y = part_y if sum_y is None else sum_y + part_y
            sum_z = part_z if sum_z is None else sum_z + part_z
        fields[rhs] = jnp.sum(sum_x * rows_y, axis=0, keepdims=True)
        fields[RHS + rhs] = jnp.sum(sum_y * slope_y, axis=0, keepdims=True)
        fields[2 * RHS + rhs] = jnp.sum(sum_z * rows_y, axis=0, keepdims=True)
    return jnp.concatenate(fields, axis=0)


def read_tables(tables_ref):
    return (
        tables_ref[0:X_PAD],
        tables_ref[SLOT_ROWS : SLOT_ROWS + X_PAD],
        tables_ref[2 * SLOT_ROWS : 2 * SLOT_ROWS + Y_PAD],
        tables_ref[2 * SLOT_ROWS + Y_PAD : 2 * SLOT_ROWS + 2 * Y_PAD],
    )


def setup_body(
    lengths,
    devices,
    place_ref,
    base_ref,
    start_ref,
    z_high_ref,
    z_low_ref,
    message_ref,
    tables_ref,
    depth_high_ref,
    depth_low_ref,
):
    base = [base_ref[dim] for dim in range(3)]
    fractions = []
    cells = []
    for dim in range(3):
        cell = base[dim] + 2
        cell = jnp.where(cell >= lengths[dim], cell - lengths[dim], cell)
        cells.append(cell)
        fractions.append(place_ref[dim] - cell.astype(jnp.float32))
    values, slopes = spline_table(jnp.concatenate(fractions, axis=0))
    values = [[values[stencil][dim : dim + 1] for stencil in range(5)] for dim in range(3)]
    slopes = [[slopes[stencil][dim : dim + 1] for stencil in range(5)] for dim in range(3)]
    slot_x = lax.rem(cells[0], CX)
    slot_y = lax.rem(cells[1], CY)
    tables_ref[0:SLOT_ROWS] = placed_rows(slot_x, values[0], SLOT_ROWS)
    tables_ref[SLOT_ROWS : 2 * SLOT_ROWS] = placed_rows(slot_x, slopes[0], SLOT_ROWS)
    tables_ref[2 * SLOT_ROWS : 2 * SLOT_ROWS + Y_PAD] = placed_rows(slot_y, values[1], Y_PAD)
    tables_ref[2 * SLOT_ROWS + Y_PAD : 2 * SLOT_ROWS + 2 * Y_PAD] = placed_rows(
        slot_y, slopes[1], Y_PAD
    )
    window = jnp.concatenate(
        [
            placed_rows(base[2], values[2], KZ),
            placed_rows(base[2], slopes[2], KZ),
        ],
        axis=1,
    )
    depth = product((z_high_ref[...], z_low_ref[...]), halves(window), 1, 0)
    depth = halves(depth)
    depth_high_ref[...] = depth[0]
    depth_low_ref[...] = depth[1]
    spread_into(message_ref, start_ref[...], *read_tables(tables_ref), depth, devices)


def transform_in(message_ref, forward_ref, block_high_ref, block_low_ref, rows_count, cols_count):
    gathered = jnp.concatenate(
        [
            jnp.concatenate(
                [
                    message_ref[(r * cols_count + c) * X_PAD : (r * cols_count + c + 1) * X_PAD]
                    for r in range(rows_count)
                ],
                axis=0,
            )
            for c in range(cols_count)
        ],
        axis=1,
    )
    high, low = halves(gathered)
    along = jnp.dot(
        forward_ref[...],
        jnp.concatenate([high, high, low], axis=0),
        preferred_element_type=jnp.float32,
    )
    part = along.shape[1] // cols_count // SPLIT
    along = jnp.concatenate(
        [
            jnp.concatenate(
                [
                    along[:, (c * SPLIT + half) * part : (c * SPLIT + half + 1) * part]
                    for c in range(cols_count)
                ],
                axis=1,
            )
            for half in range(SPLIT)
        ],
        axis=0,
    )
    return product(halves(along), (block_high_ref[...], block_low_ref[...]))


def transform_out(result_ref, values, backward_ref, block_high_ref, block_low_ref, counts):
    rows_count, cols_count = counts
    spread = product(halves(values), (block_high_ref[...], block_low_ref[...]), 1, 1)
    grid_x = spread.shape[0] // SPLIT
    part = spread.shape[1] // cols_count
    spread = jnp.concatenate(
        [
            spread[half * grid_x : (half + 1) * grid_x, c * part : (c + 1) * part]
            for c in range(cols_count)
            for half in range(SPLIT)
        ],
        axis=1,
    )
    high, low = halves(spread)
    along = jnp.dot(
        backward_ref[...],
        jnp.concatenate([high, high, low], axis=0),
        preferred_element_type=jnp.float32,
    )
    width = along.shape[1] // cols_count
    slot_rows = result_ref.shape[0] // (rows_count * cols_count)
    for r in range(rows_count):
        for c in range(cols_count):
            first = (r * cols_count + c) * slot_rows
            result_ref[first : first + X_PAD, :] = along[
                r * X_PAD : (r + 1) * X_PAD, c * width : (c + 1) * width
            ]


def middle_first_body(
    counts,
    message_ref,
    kernel_ref,
    forward_ref,
    backward_ref,
    block_high_ref,
    block_low_ref,
    result_ref,
    wave_ref,
):
    wave = transform_in(message_ref, forward_ref, block_high_ref, block_low_ref, *counts)
    wave_ref[...] = wave
    transform_out(
        result_ref, wave * kernel_ref[...], backward_ref, block_high_ref, block_low_ref, counts
    )


def gather_rows(parts):
    tiles = [
        parts[GROUP * tile : GROUP * tile + GROUP, :] for tile in range(parts.shape[0] // GROUP)
    ]
    return jnp.concatenate(tiles, axis=1)[0 : 3 * RHS]


def row_total(value, rhs):
    row = lax.broadcasted_iota(jnp.int32, value.shape, 0)
    return total(jnp.where(lax.rem(row, RHS) == rhs, value, 0.0))


def total(value):
    return jnp.sum(jnp.sum(value, axis=0, keepdims=True), axis=1, keepdims=True)


def middle_second_body(
    counts,
    message_ref,
    kernel_ref,
    forward_ref,
    backward_ref,
    block_high_ref,
    block_low_ref,
    wave_ref,
    start_ref,
    carried_ref,
    near_ref,
    polar_ref,
    result_ref,
    local_ref,
):
    near_rows = gather_rows(near_ref)
    wave = transform_in(message_ref, forward_ref, block_high_ref, block_low_ref, *counts)
    filtered = wave * kernel_ref[...]
    transform_out(result_ref, filtered, backward_ref, block_high_ref, block_low_ref, counts)
    before = wave_ref[...]
    grid_y = CY * counts[1]
    lane = lax.broadcasted_iota(jnp.int32, wave.shape, 1)
    own_rhs = lax.rem(lax.div(lane, grid_y), RHS)
    image = carried_ref[0 : 3 * RHS]
    second = carried_ref[8 : 8 + 3 * RHS]
    start = start_ref[...]
    local_part = second / polar_ref[...] - near_rows - self_coef * second
    local_ref[0 : 3 * RHS] = image
    local_ref[8 : 8 + 3 * RHS] = second
    local_ref[16 : 16 + 3 * RHS] = local_part
    local_ref[24 : 24 + 3 * RHS] = start
    slot = lax.broadcasted_iota(jnp.int32, (1, result_ref.shape[1]), 1)
    sums = jnp.zeros((1, result_ref.shape[1]), jnp.float32)
    for rhs in range(RHS):
        mine = own_rhs == rhs
        parts = (
            row_total(start * start / polar_ref[...], rhs),
            row_total(start * image, rhs),
            row_total(second * image, rhs),
            row_total(start * local_part, rhs) + total(jnp.where(mine, before * filtered, 0.0)),
            row_total(second * local_part, rhs) + total(jnp.where(mine, wave * filtered, 0.0)),
        )
        for index, part in enumerate(parts):
            sums = jnp.where(slot == rhs * len(parts) + index, part, sums)
    devices = counts[0] * counts[1]
    result_ref[pl.ds(X_PAD, devices, stride=X_PAD + 1), :] = jnp.broadcast_to(
        sums, (devices, sums.shape[1])
    )


def sample_body(
    devices,
    message_ref,
    tables_ref,
    depth_high_ref,
    depth_low_ref,
    start_ref,
    near_ref,
    polar_ref,
    carried_ref,
    payload_ref,
):
    tables = read_tables(tables_ref)
    depth = (depth_high_ref[...], depth_low_ref[...])
    field = sample_from(message_ref, *tables, depth, devices)
    start = start_ref[...]
    polar = polar_ref[...]
    image = start / polar - gather_rows(near_ref) + field - self_coef * start
    second = polar * image
    carried_ref[0 : 3 * RHS] = image
    carried_ref[8 : 8 + 3 * RHS] = second
    store_payload(payload_ref, second)


def spread_body(
    devices,
    tables_ref,
    depth_high_ref,
    depth_low_ref,
    carried_ref,
    result_ref,
):
    depth = (depth_high_ref[...], depth_low_ref[...])
    second = carried_ref[8 : 8 + 3 * RHS]
    spread_into(result_ref, second, *read_tables(tables_ref), depth, devices)


def final_body(
    devices,
    message_ref,
    tables_ref,
    depth_high_ref,
    depth_low_ref,
    rhs_ref,
    local_ref,
    dipole_ref,
    residual_ref,
):
    tables = read_tables(tables_ref)
    depth = (depth_high_ref[...], depth_low_ref[...])
    field = sample_from(message_ref, *tables, depth, devices)
    image = local_ref[0 : 3 * RHS]
    second = local_ref[8 : 8 + 3 * RHS]
    image_second = local_ref[16 : 16 + 3 * RHS] + field
    start = local_ref[24 : 24 + 3 * RHS]
    sums = jnp.sum(
        message_ref[pl.ds(X_PAD, devices, stride=X_PAD + 1), :], axis=0, keepdims=True
    )
    steps = []
    for rhs in range(RHS):
        progress, start_image, second_image, start_next, second_next = [
            sums[:, rhs * 5 + index : rhs * 5 + index + 1] for index in range(5)
        ]
        step = progress / start_image
        progress_next = progress - 2.0 * step * start_image + step * step * second_image
        grown = 1.0 + progress_next / progress
        curvature = (
            grown * grown * start_image
            - step * grown * (start_next + second_image)
            + step * step * second_next
        )
        steps.append((step, grown, progress_next / curvature))
    row = lax.broadcasted_iota(jnp.int32, (RHS, 1), 0)
    step, grown, step_next = [
        sum(jnp.where(row == rhs, steps[rhs][index], 0.0) for rhs in range(RHS))
        for index in range(3)
    ]
    for dim in range(3):
        rows = slice(dim * RHS, (dim + 1) * RHS)
        direction = grown * start[rows] - step * second[rows]
        image_direction = grown * image[rows] - step * image_second[rows]
        dipole_ref[dim] = step * start[rows] + step_next * direction
        residual_ref[dim] = rhs_ref[dim] - step * image[rows] - step_next * image_direction


def near_base(entry, brick_rows):
    return lax.shift_right_logical(entry, 2) * brick_rows + lax.bitwise_and(entry, 3)


def nearest(places, origin, span):
    return places - span * jnp.floor((places - origin) * (1.0 / span) + 0.5)


def unwrap_near(near, tile_count, spans):
    rows = near.shape[0] // 9
    for dim in range(2):
        own = 4 * rows + dim * tile_count
        origin = near[own : own + 1, 0:1]
        for brick in range(9):
            first = brick * rows + dim * tile_count
            near[first : first + tile_count, :] = nearest(
                near[first : first + tile_count, :], origin, spans[dim]
            )


def pick_rows(picked, near, lists_ref, tile, place, tile_count, quantities, origin, span):
    rows = near.shape[0] // 9
    place = place * lists_ref.shape[1] * quantities * GROUP
    for entry in range(lists_ref.shape[1]):
        base = near_base(lists_ref[tile, entry], rows)
        for quantity in range(quantities):
            values = near[pl.ds(base + quantity * tile_count, 1), :]
            if quantity == 2 and span is not None:
                values = nearest(values, origin, span)
            first = place + (entry * quantities + quantity) * GROUP
            picked[first : first + GROUP, :] = jnp.broadcast_to(values, (GROUP, TILE))


def widen_own(near, quantities, tile_count, tile, place, wide):
    offset = near.shape[0] // 9 * 4
    rows = [
        near[offset + quantity * tile_count + tile : offset + quantity * tile_count + tile + 1, :]
        for quantity in range(quantities)
    ]
    spare = jnp.zeros((TILE - quantities, TILE), jnp.float32)
    columns = jnp.transpose(jnp.concatenate(rows + [spare], axis=0))
    for quantity in range(quantities):
        first = (place * quantities + quantity) * TILE
        wide[first : first + TILE, :] = jnp.broadcast_to(
            columns[:, quantity : quantity + 1], (TILE, TILE)
        )


def add_field(sums, first_term, second_term, apart, moments):
    for rhs in range(RHS):
        moment = [moments[RHS * dim + rhs] for dim in range(3)]
        projected = moment[0] * apart[0] + moment[1] * apart[1] + moment[2] * apart[2]
        weighted = second_term * projected
        for dim in range(3):
            index = RHS * dim + rhs
            sums[index] = sums[index] + (weighted * apart[dim] - first_term * moment[dim])


def finish_sums(field_ref, sums_ref, first_tile, place):
    place = place * 3 * RHS
    lane = lax.broadcasted_iota(jnp.int32, (TILE, TILE), 1)
    merged = jnp.zeros((TILE, TILE), jnp.float32)
    for index in range(3 * RHS):
        first = (place + index) * TILE
        column = jnp.sum(sums_ref[first : first + TILE, :], axis=1, keepdims=True)
        merged = jnp.where(lane == index, column, merged)
    first = (first_tile + place // (3 * RHS)) * GROUP
    field_ref[first : first + GROUP, :] = jnp.transpose(merged)[0:GROUP]


def pair_rows(start, group):
    return pl.ds(pl.multiple_of(start + group * GROUP, GROUP), GROUP)


def wide_rows(start, group, quantity):
    return pl.ds(pl.multiple_of(quantity * TILE + start + group * GROUP, GROUP), GROUP)


def pair_terms(square_dist, damp):
    inverse = lax.rsqrt(square_dist)
    distance = square_dist * inverse
    inverse_sq = inverse * inverse
    inverse_cube = inverse_sq * inverse
    cubed = damp * (distance * square_dist)
    damping = jnp.exp(cubed)
    bell = jnp.exp(-(ewald_beta * ewald_beta) * square_dist)
    stretched = 1.0 + (SCREEN_SCALE * ewald_beta) * distance
    turned = pl.reciprocal(stretched, approx=True)
    turned = turned * (2.0 - stretched * turned)
    series = SCREEN_COEF[-1] * turned + SCREEN_COEF[-2]
    for coef in SCREEN_COEF[-3::-1]:
        series = series * turned + coef
    screen = bell * turned * series
    gaussian = (2.0 * ewald_beta / math.sqrt(math.pi)) * bell
    bare = screen - damping
    first_term = bare * inverse_cube + gaussian * inverse_sq
    second_term = (
        3.0 * (first_term + (cubed * damping) * inverse_cube)
        + (2.0 * ewald_beta * ewald_beta) * gaussian
    ) * inverse_sq
    return first_term, second_term


def step_rows(step, size, offset):
    return pl.ds(pl.multiple_of(step * size + offset, GROUP), GROUP)


def tile_rows(step, rows):
    return pl.ds(pl.multiple_of(step * rows, GROUP), rows)


def start_all(copies):
    for copy in copies:
        copy.start()


def wait_all(copies):
    for copy in copies:
        copy.wait()


def near_copies(sources, near, semaphore):
    rows = sources[0].shape[0]
    return [
        pltpu.make_async_copy(
            source, near.at[index * rows : (index + 1) * rows, :], semaphore.at[index]
        )
        for index, source in enumerate(sources)
    ]


def term_copies(terms, buffers, semaphore, begin, step, size, inward):
    rows = pl.ds(pl.multiple_of((begin + step) * size, GROUP), size)
    place = pl.ds(pl.multiple_of(step * size, GROUP), size)
    copies = []
    for index in range(2):
        far, here = terms[index].at[rows, :], buffers[index].at[place, :]
        ends = (far, here) if inward else (here, far)
        copies.append(pltpu.make_async_copy(*ends, semaphore.at[index, step]))
    return copies


def pair_first_body(
    first_tile,
    last_tile,
    tile_count,
    spans,
    lists_ref,
    up_ref,
    stack_ref,
    down_ref,
    *others,
):
    first_ref, second_ref, field_ref, near_ref = others[-14:-10]
    near, picked, wide, sums_ref, kept, field, first_buffer, second_buffer, semaphore, busy = others[-10:]
    terms = (first_ref, second_ref)
    buffers = (first_buffer, second_buffer)
    copies = near_copies((up_ref, stack_ref, down_ref), near, semaphore.at[0])
    if first_tile > 0:
        copies.append(
            pltpu.make_async_copy(
                others[0], field.at[0 : first_tile * GROUP, :], semaphore.at[0, 3]
            )
        )
    start_all(copies)
    wait_all(copies)
    entries = lists_ref.shape[1]
    rows = near.shape[0] // 9
    quantities = rows // tile_count
    unwrap_near(near, tile_count, spans)
    for brick in range(9):
        kept[brick * 3 * tile_count : (brick + 1) * 3 * tile_count, :] = near[
            brick * rows : brick * rows + 3 * tile_count, :
        ]
    keep = pltpu.make_async_copy(kept, near_ref, semaphore.at[1, 3])
    keep.start()
    for place, tile in enumerate(range(first_tile, last_tile)):
        widen_own(near, 4, tile_count, tile, place, wide)
        own = rows * 4 + 2 * tile_count + tile
        origin = near[own : own + 1, 0:1]
        pick_rows(picked, near, lists_ref, tile, place, tile_count, quantities, origin, spans[2])
    parts = TILE // PAIR_ROWS
    steps = (last_tile - first_tile) * parts

    size = entries * PAIR_ROWS

    def sent(step):
        return term_copies(terms, buffers, busy, first_tile * parts, step, size, False)

    @pl.loop(0, steps)
    def _(step):
        tile = lax.div(step, parts)
        start = lax.rem(step, parts) * PAIR_ROWS
        step_picked = picked.at[tile_rows(tile, entries * quantities * GROUP), :]
        step_wide = wide.at[tile_rows(tile, 4 * TILE), :]
        step_sums = sums_ref.at[tile_rows(tile, 3 * RHS * TILE), :]
        for group in range(PAIR_ROWS // GROUP):
            own = [step_wide[wide_rows(start, group, dim), :] for dim in range(4)]
            own_damp = -thole_a * own[3]
            sums = [jnp.zeros((GROUP, TILE), jnp.float32) for _ in range(3 * RHS)]
            itself = (
                lax.broadcasted_iota(jnp.int32, (GROUP, TILE), 0) + (start + group * GROUP)
            ) == lax.broadcasted_iota(jnp.int32, (GROUP, TILE), 1)
            for entry in range(entries):
                first = entry * quantities * GROUP
                rows = [
                    step_picked[first + quantity * GROUP : first + (quantity + 1) * GROUP, :]
                    for quantity in range(quantities)
                ]
                apart = [rows[dim] - own[dim] for dim in range(3)]
                square_dist = apart[0] * apart[0] + apart[1] * apart[1] + apart[2] * apart[2]
                if entry == 0:
                    square_dist = jnp.where(itself, 1.0, square_dist)
                first_term, second_term = pair_terms(square_dist, own_damp * rows[3])
                if entry == 0:
                    first_term = jnp.where(itself, 0.0, first_term)
                    second_term = jnp.where(itself, 0.0, second_term)
                place = step_rows(step, size, entry * PAIR_ROWS + group * GROUP)
                first_buffer[place, :] = first_term
                second_buffer[place, :] = second_term
                add_field(sums, first_term, second_term, apart, rows[4:])
            for index, value in enumerate(sums):
                step_sums[wide_rows(start, group, index), :] = value
        start_all(sent(step))

    for place in range(last_tile - first_tile):
        finish_sums(field, sums_ref, first_tile, place)
    result = pltpu.make_async_copy(field, head_of(field_ref, field), semaphore.at[1, 2])
    result.start()

    @pl.loop(0, steps)
    def _(step):
        wait_all(sent(step))

    keep.wait()
    result.wait()


def pair_second_body(
    tile_count,
    spans,
    lists_ref,
    near_ref,
    up_ref,
    stack_ref,
    down_ref,
    first_ref,
    second_ref,
    field_ref,
    near,
    near_moment,
    picked,
    picked_moment,
    wide,
    sums_ref,
    field,
    first_buffer,
    second_buffer,
    semaphore,
    busy,
):
    terms = (first_ref, second_ref)
    buffers = (first_buffer, second_buffer)
    parts = TILE // PAIR_ROWS
    steps = tile_count * parts

    entries = lists_ref.shape[1]
    size = entries * PAIR_ROWS

    def fetched(step):
        return term_copies(terms, buffers, busy, 0, step, size, True)

    places = pltpu.make_async_copy(
        near_ref, near.at[0 : near_ref.shape[0], :], semaphore.at[1, 3]
    )
    places.start()
    copies = near_copies((up_ref, stack_ref, down_ref), near_moment, semaphore.at[2])
    start_all(copies)

    @pl.loop(0, steps)
    def _(step):
        start_all(fetched(step))

    places.wait()
    for tile in range(tile_count):
        widen_own(near, 3, tile_count, tile, tile, wide)
        own = near.shape[0] // 9 * 4 + 2 * tile_count + tile
        origin = near[own : own + 1, 0:1]
        pick_rows(picked, near, lists_ref, tile, tile, tile_count, 3, origin, spans[2])
    wait_all(copies)
    for tile in range(tile_count):
        pick_rows(
            picked_moment, near_moment, lists_ref, tile, tile, tile_count, 3 * RHS, None, None
        )

    @pl.loop(0, steps)
    def _(step):
        wait_all(fetched(step))
        tile = lax.div(step, parts)
        start = lax.rem(step, parts) * PAIR_ROWS
        step_picked = picked.at[tile_rows(tile, entries * 3 * GROUP), :]
        step_moment = picked_moment.at[tile_rows(tile, entries * 3 * RHS * GROUP), :]
        step_wide = wide.at[tile_rows(tile, 3 * TILE), :]
        step_sums = sums_ref.at[tile_rows(tile, 3 * RHS * TILE), :]
        for group in range(PAIR_ROWS // GROUP):
            own = [step_wide[wide_rows(start, group, dim), :] for dim in range(3)]
            sums = [jnp.zeros((GROUP, TILE), jnp.float32) for _ in range(3 * RHS)]
            for entry in range(entries):
                first = entry * 3 * GROUP
                apart = [
                    step_picked[first + dim * GROUP : first + (dim + 1) * GROUP, :] - own[dim]
                    for dim in range(3)
                ]
                first = first * RHS
                moments = [
                    step_moment[first + index * GROUP : first + (index + 1) * GROUP, :]
                    for index in range(3 * RHS)
                ]
                place = step_rows(step, size, entry * PAIR_ROWS + group * GROUP)
                add_field(sums, first_buffer[place, :], second_buffer[place, :], apart, moments)
            for index, value in enumerate(sums):
                step_sums[wide_rows(start, group, index), :] = value

    for place in range(tile_count):
        finish_sums(field, sums_ref, 0, place)
    result = pltpu.make_async_copy(field, head_of(field_ref, field), semaphore.at[1, 2])
    result.start()
    result.wait()


def shift(source, axis, step):
    count = lax.axis_size(axis)
    return lax.ppermute(source, axis, [(i, (i + step) % count) for i in range(count)])


def both_ways(source, axis):
    return shift(source, axis, 1), source, shift(source, axis, -1)


def whole(shape):
    return pl.BlockSpec(shape, lambda *_: (0,) * len(shape))


def anywhere():
    return pl.BlockSpec(memory_space=pl.ANY)


def join(message, payload):
    right = shift(payload, "col", -1)
    left = shift(payload, "col", 1)
    message, right, left = lax.optimization_barrier((message, right, left))
    return message, both_ways(jnp.concatenate([left, payload, right], axis=0), "row")


class Fetched:
    def __init__(self, source, scratch, semaphore):
        self.copy = pltpu.make_async_copy(source, scratch, semaphore)
        self.copy.start()
        self.scratch = scratch
        self.shape = scratch.shape
        self.waiting = True

    def wait(self):
        if self.waiting:
            self.copy.wait()
            self.waiting = False

    def __getitem__(self, index):
        self.wait()
        return self.scratch[index]


class Head:
    def __init__(self, array, shape):
        self.array = array
        self.shape = shape
        self.dtype = array.dtype


def roomy(shape):
    return (ROOMY_BYTES // 4 // shape[1], shape[1])


def head_of(far, here):
    if far.shape == here.shape:
        return far
    return far.at[0 : here.shape[0], :]


def call(body, outs, *operands, after=(), own_block=None, near=0, large=(), vmem=VMEM_LIMIT):
    count = len(operands)
    fetched = [
        pltpu.VMEM(operand.shape[1:] if index == own_block else operand.shape, operand.dtype)
        for index, operand in enumerate(operands)
        if index >= near
    ]
    arrays = [operand.array if isinstance(operand, Head) else operand for operand in operands]

    def run(*refs):
        refs = refs[len(after) :]
        sources, refs = refs[:count], refs[count:]
        results, refs = refs[: len(outs)], refs[len(outs) :]
        targets, written, semaphore = refs[: count - near], refs[count - near : -1], refs[-1]
        inputs = list(sources[:near])
        for index in range(near, count):
            source = sources[index]
            if index == own_block:
                place = lax.axis_index("row") * lax.axis_size("col") + lax.axis_index("col")
                source = source.at[place]
            else:
                source = head_of(source, targets[index - near])
            inputs.append(Fetched(source, targets[index - near], semaphore.at[index]))
        body(*inputs, *written)
        for operand in inputs[near:]:
            operand.wait()
        copies = [
            pltpu.make_async_copy(value, head_of(result, value), semaphore.at[count + index])
            for index, (value, result) in enumerate(zip(written, results))
        ]
        for copy in copies:
            copy.start()
        for copy in copies:
            copy.wait()

    return pl.pallas_call(
        run,
        in_specs=[anywhere()] * len(after)
        + [pl.BlockSpec(memory_space=pltpu.VMEM)] * near
        + [anywhere()] * (count - near),
        out_specs=[anywhere()] * len(outs),
        out_shape=[
            jax.ShapeDtypeStruct(roomy(shape) if index in large else shape, dtype)
            for index, (shape, dtype) in enumerate(outs)
        ],
        scratch_shapes=fetched
        + [pltpu.VMEM(shape, dtype) for shape, dtype in outs]
        + [pltpu.SemaphoreType.DMA((count + len(outs),))],
        compiler_params=pltpu.CompilerParams(vmem_limit_bytes=vmem),
        cost_estimate=pl.CostEstimate(
            flops=200_000_000, bytes_accessed=4 << 20, transcendentals=0
        ),
    )(*after, *arrays)


def final_call(body, outs, *operands):
    return pl.pallas_call(
        body,
        grid=(1,),
        in_specs=[whole(operand.shape) for operand in operands],
        out_specs=[whole(shape) for shape, _ in outs],
        out_shape=[jax.ShapeDtypeStruct(shape, dtype) for shape, dtype in outs],
        compiler_params=pltpu.CompilerParams(vmem_limit_bytes=SMALL_VMEM_LIMIT),
    )(*operands)


def pair_call(body, outs, scratch, lists, *operands, tiles, large, aliased=0):
    buffers = (tiles * lists.shape[1] * TILE, TILE)
    first = 1 + len(operands) - aliased
    return pl.pallas_call(
        body,
        in_specs=[pl.BlockSpec(memory_space=pltpu.SMEM)] + [anywhere()] * len(operands),
        out_specs=[anywhere()] * len(outs),
        out_shape=[
            jax.ShapeDtypeStruct(roomy(shape) if index == large else shape, jnp.float32)
            for index, shape in enumerate(outs)
        ],
        scratch_shapes=[pltpu.VMEM(shape, jnp.float32) for shape in scratch + [buffers] * 2]
        + [
            pltpu.SemaphoreType.DMA((3, 4)),
            pltpu.SemaphoreType.DMA((2, tiles * TILE // PAIR_ROWS)),
        ],
        input_output_aliases={first + index: index for index in range(aliased)},
        compiler_params=pltpu.CompilerParams(vmem_limit_bytes=VMEM_LIMIT),
        cost_estimate=pl.CostEstimate(
            flops=80_000_000, bytes_accessed=8 << 20, transcendentals=1 << 21
        ),
    )(lists, *operands)


def exchange(message, devices):
    shape = message.shape
    sent = message.reshape(devices, 1, -1)
    return lax.all_to_all(sent, ("row", "col"), split_axis=0, concat_axis=0, tiled=True).reshape(
        shape
    )


def slab_local(field_rhs, positions, polar, grid_base, tile_lists):
    rows_count = lax.axis_size("row")
    cols_count = lax.axis_size("col")
    counts = (rows_count, cols_count)
    devices = rows_count * cols_count
    lengths = (CX * rows_count, CY * cols_count, KZ)
    spans = tuple(float(length) for length in lengths)
    atoms = polar.shape[-1]
    tile_count = atoms // TILE
    listed = tile_lists.shape[-1]
    tables = slab_tables(rows_count, cols_count)
    f32 = jnp.float32
    rhs = jnp.swapaxes(field_rhs[0, 0], 0, 1)
    place = jnp.swapaxes(positions[0], 0, 1)
    base = jnp.swapaxes(grid_base[0], 0, 1)
    polar = polar.reshape(1, atoms)
    lists = tile_lists[0, 0]
    quantities = 4 + 3 * RHS
    brick_rows = quantities * tile_count
    moment_rows = 3 * RHS * tile_count
    message_shape = (devices * X_PAD, KZ // devices * RHS * Y_PAD)
    last_shape = (devices * (X_PAD + 1), message_shape[1])
    row_shape = (3 * RHS, atoms)

    start, payload = call(pack_body, [(row_shape, f32), ((brick_rows, TILE), f32)], rhs, place, polar)

    def setup(*refs):
        setup_body(lengths, devices, *refs)

    message, splines, depth_high, depth_low = call(
        setup,
        [
            (message_shape, f32),
            ((2 * SLOT_ROWS + 2 * Y_PAD, atoms), f32),
            ((KZ, 2 * atoms), jnp.bfloat16),
            ((KZ, 2 * atoms), jnp.bfloat16),
        ],
        place,
        base,
        start,
        *[jnp.asarray(table) for table in tables["along_z"]],
    )
    constants = (
        jnp.asarray(tables["kernel"]),
        jnp.asarray(tables["forward_x"]),
        jnp.asarray(tables["backward_x"]),
        *[jnp.asarray(table) for table in tables["block"]],
    )
    message, near = join(message, payload)
    arrived = exchange(message, devices)

    def pair_first(first_tile, last_tile, fields, *after):
        def body(*refs):
            pair_first_body(first_tile, last_tile, tile_count, spans, *refs)

        tiles = last_tile - first_tile
        return pair_call(
            body,
            [(tile_count * listed * TILE, TILE)] * 2
            + [(last_tile * GROUP, TILE), (9 * 3 * tile_count, TILE)],
            [
                (9 * brick_rows + GROUP, TILE),
                (tiles * listed * quantities * GROUP, TILE),
                (tiles * 4 * TILE, TILE),
                (tiles * 3 * RHS * TILE, TILE),
                (9 * 3 * tile_count, TILE),
                (last_tile * GROUP, TILE),
            ],
            lists,
            *near,
            *fields,
            *after,
            tiles=tiles,
            large=2 if first_tile > 0 else None,
            aliased=2 if first_tile > 0 else 0,
        )

    early = pair_first(0, EARLY_TILES, (), message)

    def middle_first(*refs):
        middle_first_body(counts, *refs)

    arrived, early = lax.optimization_barrier((arrived, tuple(early)))
    wave_shape = tables["kernel"].shape[1:]
    mixed, wave = call(
        middle_first,
        [(message_shape, f32), (wave_shape, f32)],
        arrived,
        *constants,
        own_block=1,
        near=1,
        large=(1,),
        vmem=MIDDLE_VMEM_LIMIT,
    )
    returned = exchange(mixed, devices)
    first_term, second_term, direct, near = pair_first(
        EARLY_TILES, tile_count, (early[2],), wave, *early[:2]
    )

    def sample(*refs):
        sample_body(devices, *refs)

    carried_shape = (16, atoms)
    field_shape = (tile_count * GROUP, TILE)
    carried, moments = call(
        sample,
        [(carried_shape, f32), ((moment_rows, TILE), f32)],
        returned,
        splines,
        depth_high,
        depth_low,
        start,
        Head(direct, field_shape),
        polar,
        near=1,
        large=(0,),
        vmem=MIDDLE_VMEM_LIMIT,
    )

    def spread(*refs):
        spread_body(devices, *refs)

    (message,) = call(
        spread,
        [(message_shape, f32)],
        splines,
        depth_high,
        depth_low,
        Head(carried, carried_shape),
    )
    message, near_moments = join(message, moments)
    arrived = exchange(message, devices)

    def pair_second(*refs):
        pair_second_body(tile_count, spans, *refs)

    (direct,) = pair_call(
        pair_second,
        [(tile_count * GROUP, TILE)],
        [
            (9 * 3 * tile_count + GROUP, TILE),
            (9 * moment_rows + GROUP, TILE),
            (tile_count * listed * 3 * GROUP, TILE),
            (tile_count * listed * 3 * RHS * GROUP, TILE),
            (tile_count * 3 * TILE, TILE),
            (tile_count * 3 * RHS * TILE, TILE),
            (tile_count * GROUP, TILE),
        ],
        lists,
        near,
        *near_moments,
        first_term,
        second_term,
        tiles=tile_count,
        large=0,
    )

    def middle_second(*refs):
        middle_second_body(counts, *refs)

    mixed, local = call(
        middle_second,
        [(last_shape, f32), ((32, atoms), f32)],
        arrived,
        *constants,
        Head(wave, wave_shape),
        start,
        Head(carried, carried_shape),
        Head(direct, field_shape),
        polar,
        own_block=1,
        near=1,
        vmem=MIDDLE_VMEM_LIMIT,
    )
    returned = exchange(mixed, devices)

    def final(*refs):
        final_body(devices, *refs)

    outs = final_call(
        final,
        [(rhs.shape, f32), (rhs.shape, f32)],
        returned,
        splines,
        depth_high,
        depth_low,
        rhs,
        local,
    )
    return tuple(jnp.swapaxes(out, 0, 1)[None, None] for out in outs)


def solution(mesh):
    placed = (
        P("row", "col", None, None, None),
        P("row", "col", None, None),
        P("row", "col", None),
        P("row", "col", None, None),
        P("row", "col", None, None),
    )
    devices = mesh.shape["row"] * mesh.shape["col"]
    return jax.shard_map(
        slab_local if KZ % devices == 0 else pencil_local,
        mesh=mesh,
        in_specs=placed,
        out_specs=(P("row", "col", None, None, None), P("row", "col", None, None, None)),
        check_vma=False,
    )
```

```python
import math

import jax
import jax.numpy as jnp
import ml_dtypes
import numpy as np
from jax import lax
from jax.experimental import pallas as pl
from jax.experimental.pallas import tpu as pltpu
from jax.sharding import PartitionSpec as P

CX = 8
CY = 4
KZ = 256
TILE = 128
RHS = 2
ITERS = 2


ewald_beta = 0.4
thole_a = 0.39
self_coef = 4.0 * ewald_beta**3 / (3.0 * math.sqrt(math.pi))
highest = lax.Precision.HIGHEST


def with_halo(cells, sides, width):
    for axis, dim in sides:
        count = lax.axis_size(axis)
        head = lax.slice_in_dim(cells, 0, width, axis=dim)
        tail = lax.slice_in_dim(cells, cells.shape[dim] - width, cells.shape[dim], axis=dim)
        cells = jnp.concatenate(
            [
                lax.ppermute(tail, axis, [(i, (i + 1) % count) for i in range(count)]),
                cells,
                lax.ppermute(head, axis, [((i + 1) % count, i) for i in range(count)]),
            ],
            axis=dim,
        )
    return cells


def spline_table(fraction):
    previous = {0: jnp.ones_like(fraction)}
    fourth = previous
    for degree in range(2, 6):
        current = {}
        for offset in range(degree):
            abscissa = fraction + offset
            summed = abscissa * previous.get(offset, 0.0) + (degree - abscissa) * previous.get(
                offset - 1, 0.0
            )
            current[offset] = summed / (degree - 1)
        if degree == 4:
            fourth = current
        previous = current
    values = jnp.stack([previous[4 - stencil] for stencil in range(5)])
    slopes = jnp.stack(
        [fourth.get(4 - stencil, 0.0) - fourth.get(3 - stencil, 0.0) for stencil in range(5)]
    )
    return (values, slopes)


def spline_modulus(wave_index, length):
    spline_coef = (1.0 / 24.0, 11.0 / 24.0, 11.0 / 24.0, 1.0 / 24.0)
    cosine_sum = jnp.zeros(wave_index.shape, jnp.float32)
    sine_sum = jnp.zeros(wave_index.shape, jnp.float32)
    for offset in range(4):
        angles = 2.0 * math.pi / length * (wave_index * offset % length).astype(jnp.float32)
        cosine_sum = cosine_sum + spline_coef[offset] * jnp.cos(angles)
        sine_sum = sine_sum + spline_coef[offset] * jnp.sin(angles)
    return cosine_sum * cosine_sum + sine_sum * sine_sum


def folded_square(wave_index, length):
    nearest = jnp.minimum(wave_index, length - wave_index).astype(jnp.float32) / length
    return nearest * nearest


def influence(wave_x, wave_y, wave_z, length_x, length_y, length_z):
    wave_norm = (
        folded_square(wave_x, length_x)
        + folded_square(wave_y, length_y)
        + folded_square(wave_z, length_z)
    )
    modulus = (
        spline_modulus(wave_x, length_x)
        * spline_modulus(wave_y, length_y)
        * spline_modulus(wave_z, length_z)
    )
    excluded = (wave_x * 2 == length_x) | (wave_y * 2 == length_y) | (wave_z * 2 == length_z)
    excluded = excluded | (wave_x == 0) & (wave_y == 0) & (wave_z == 0)
    safe_norm = jnp.where(excluded, 1.0, wave_norm)
    safe_modulus = jnp.where(excluded, 1.0, modulus)
    result = jnp.exp(-(math.pi**2 / ewald_beta**2) * safe_norm) / (
        math.pi * safe_norm * safe_modulus
    )
    return jnp.where(excluded, 0.0, result)


def tile_field(own_static, near_static, near_dipole, box_spans):
    listed_count = near_static.shape[0]
    tile_width = own_static.shape[1]
    box_span = jnp.array(box_spans, dtype=jnp.float32)[None, :, None, None]
    separation = near_static[:, 0:3, None, :] - own_static[None, 0:3, :, None]
    separation = separation - box_span * jnp.floor(separation / box_span + 0.5)
    dist_sq = jnp.sum(separation * separation, axis=1)
    itself = (jnp.arange(listed_count)[:, None, None] == 0) & (
        jnp.arange(tile_width)[:, None] == jnp.arange(tile_width)[None, :]
    )[None]
    safe_sq = jnp.where(itself, 1.0, dist_sq)
    distance = jnp.sqrt(safe_sq)
    scaled = distance / (own_static[3][None, :, None] * near_static[:, 3][:, None, :])
    cubed = thole_a * scaled * scaled * scaled
    damping = jnp.exp(-cubed)
    screen = lax.erfc(ewald_beta * distance)
    gaussian = 2.0 * ewald_beta / math.sqrt(math.pi) * jnp.exp(-(ewald_beta * ewald_beta) * safe_sq)
    inverse_sq = 1.0 / safe_sq
    inverse_cube = inverse_sq / distance
    first_term = (screen - damping) * inverse_cube + gaussian * inverse_sq
    second = (
        3.0 * (screen - (1.0 + cubed) * damping) * inverse_cube * inverse_sq
        + gaussian * (2.0 * ewald_beta * ewald_beta + 3.0 * inverse_sq) * inverse_sq
    )
    first_term = jnp.where(itself, 0.0, first_term)
    second = jnp.where(itself, 0.0, second)
    projected = jnp.sum(near_dipole[:, :, :, None, :] * separation[:, None, :, :, :], axis=2)
    weighted = second[:, None] * projected
    outward = jnp.sum(weighted[:, :, None] * separation[:, None], axis=(0, 4))
    inward = jnp.sum(first_term[:, None, None] * near_dipole[:, :, :, None, :], axis=(0, 4))
    return outward - inward


def hartley(length):
    counter = jnp.arange(length, dtype=jnp.int32)
    angles = (
        2.0 * math.pi / length * (counter[:, None] * counter[None, :] % length).astype(jnp.float32)
    )
    return jnp.cos(angles) + jnp.sin(angles)


def placed_table(first_cell, weights, extent):
    slot_index = jnp.arange(extent, dtype=jnp.int32)[:, None]
    placed = jnp.zeros((extent, first_cell.shape[0]), jnp.float32)
    for stencil in range(5):
        placed = placed + jnp.where(
            slot_index == (first_cell[None, :] + stencil) % extent, weights[stencil][None, :], 0.0
        )
    return placed


def pad_axis(source, axis_pos, leading, trailing):
    widths = [(0, 0)] * source.ndim
    widths[axis_pos] = (leading, trailing)
    return jnp.pad(source, widths)


def fold_cycle(cycle_only, axis_pos, inner_len):
    middle = lax.slice_in_dim(cycle_only, 4, inner_len + 4, axis=axis_pos)
    lower_cycle = lax.slice_in_dim(cycle_only, 0, 2, axis=axis_pos)
    upper_cycle = lax.slice_in_dim(cycle_only, inner_len + 6, inner_len + 8, axis=axis_pos)
    return (
        middle
        + pad_axis(lower_cycle, axis_pos, 0, inner_len - 2)
        + pad_axis(upper_cycle, axis_pos, inner_len - 2, 0)
    )


def clear_inside(extended, extents):
    inside = None
    for axis_pos, inner_len in extents:
        slot_index = lax.broadcasted_iota(jnp.int32, extended.shape, axis_pos)
        within = (slot_index >= 2) & (slot_index < inner_len + 6)
        inside = within if inside is None else inside & within
    return jnp.where(inside, 0.0, extended)


def inner_sum(left_arr, right_arr):
    return lax.psum(jnp.sum(left_arr * right_arr, axis=(1, 2)), ("row", "col"))


def pencil_local(field_rhs, positions, polar, grid_base, tile_lists):
    rows_count = lax.axis_size("row")
    cols_count = lax.axis_size("col")
    grid_x = CX * rows_count
    grid_y = CY * cols_count
    atom_count = polar.shape[-1]
    tile_count = atom_count // TILE
    slab_depth = KZ // tile_count
    window_len = slab_depth + 4
    box_spans = (float(grid_x), float(grid_y), float(KZ))
    own_place = positions[0, 0]
    own_base = grid_base[0, 0]
    own_polar = polar[0, 0]
    lengths = jnp.array([grid_x, grid_y, KZ], dtype=jnp.int32)[:, None]
    cell_index = (own_base + 2) % lengths
    fraction = own_place - cell_index.astype(jnp.float32)
    values, slopes = spline_table(fraction)
    first_x = (own_base[0] - lax.axis_index("row") * CX + 2) % grid_x
    first_y = (own_base[1] - lax.axis_index("col") * CY + 2) % grid_y
    rows_x = placed_table(first_x, values[:, 0], CX + 4)
    slope_x = placed_table(first_x, slopes[:, 0], CX + 4)
    rows_y = placed_table(first_y, values[:, 1], CY + 4)
    slope_y = placed_table(first_y, slopes[:, 1], CY + 4)
    tile_start = jnp.arange(atom_count, dtype=jnp.int32) // TILE * slab_depth
    first_z = (own_base[2] + 2 - tile_start) % KZ
    rows_z = placed_table(first_z, values[:, 2], window_len)
    slope_z = placed_table(first_z, slopes[:, 2], window_len)
    plane_count = (CX + 4) * (CY + 4)
    plane_dx = (slope_x[:, None, :] * rows_y[None, :, :]).reshape(plane_count, atom_count)
    plane_dy = (rows_x[:, None, :] * slope_y[None, :, :]).reshape(plane_count, atom_count)
    plane_flat = (rows_x[:, None, :] * rows_y[None, :, :]).reshape(plane_count, atom_count)
    window_rows = jnp.moveaxis(rows_z.reshape(window_len, tile_count, TILE), 1, 0)
    window_slope = jnp.moveaxis(slope_z.reshape(window_len, tile_count, TILE), 1, 0)
    depth_table = jnp.concatenate([window_rows, window_slope], axis=2)
    grid_scale = 1.0 / (grid_x * grid_y * KZ)
    hartley_x = hartley(grid_x)
    hartley_y = hartley(grid_y)
    hartley_z = hartley(KZ)
    block_y = grid_y // rows_count
    block_z = KZ // cols_count
    wave_x = jnp.arange(grid_x, dtype=jnp.int32)[:, None, None]
    wave_y = (lax.axis_index("row") * block_y + jnp.arange(block_y, dtype=jnp.int32))[None, :, None]
    wave_z = (lax.axis_index("col") * block_z + jnp.arange(block_z, dtype=jnp.int32))[None, None, :]
    kernel = influence(wave_x, wave_y, wave_z, grid_x, grid_y, KZ) * grid_scale
    root_scale = jnp.power(own_polar, 1.0 / 6.0)
    own_static = jnp.concatenate([own_place, root_scale[None]], axis=0)
    near_static = with_halo(own_static[None, None], (("row", 0), ("col", 1)), 1)
    near_static = jnp.moveaxis(near_static.reshape(9, 4, tile_count, TILE), 2, 1).reshape(
        9 * tile_count, 4, TILE
    )
    own_tiles = jnp.moveaxis(own_static.reshape(4, tile_count, TILE), 1, 0)
    own_lists = tile_lists[0, 0]
    polar_wide = own_polar[None, None, :]
    solution = jnp.zeros_like(field_rhs[0, 0])
    residual = field_rhs[0, 0]
    scaled_res = polar_wide * residual
    direction = scaled_res
    progress = inner_sum(residual, scaled_res)
    for iteration in range(ITERS):
        near_dip = with_halo(direction[None, None], (("row", 0), ("col", 1)), 1)
        near_dip = jnp.moveaxis(near_dip.reshape(9, RHS, 3, tile_count, TILE), 3, 1).reshape(
            9 * tile_count, RHS, 3, TILE
        )

        def one_tile(tile_pos):
            picked = own_lists[tile_pos]
            return tile_field(own_tiles[tile_pos], near_static[picked], near_dip[picked], box_spans)

        fields = lax.map(one_tile, jnp.arange(tile_count, dtype=jnp.int32))
        direct = jnp.moveaxis(fields, 0, 2).reshape(RHS, 3, atom_count)
        slope_terms = (
            direction[:, 0, None, :] * plane_dx[None] + direction[:, 1, None, :] * plane_dy[None]
        )
        flat_terms = direction[:, 2, None, :] * plane_flat[None]
        spread_left = jnp.concatenate(
            [
                slope_terms.reshape(RHS, plane_count, tile_count, TILE),
                flat_terms.reshape(RHS, plane_count, tile_count, TILE),
            ],
            axis=3,
        )
        spread_windows = jnp.einsum("sptb,twb->sptw", spread_left, depth_table, precision=highest)
        main_part = spread_windows[..., :slab_depth].reshape(spread_windows.shape[:-2] + (KZ,))
        tail_part = pad_axis(
            spread_windows[..., slab_depth:], spread_windows.ndim - 1, 0, slab_depth - 4
        )
        tail_part = tail_part.reshape(spread_windows.shape[:-2] + (KZ,))[..., : KZ + 4 - slab_depth]
        last_axis = main_part.ndim - 1
        padded_line = pad_axis(main_part, last_axis, 0, 4) + pad_axis(
            tail_part, last_axis, slab_depth, 0
        )
        inner = padded_line[..., 2 : KZ + 2]
        spread_tile = (
            inner
            + pad_axis(padded_line[..., 0:2], last_axis, KZ - 2, 0)
            + pad_axis(padded_line[..., KZ + 2 : KZ + 4], last_axis, 0, KZ - 2)
        ).reshape(RHS, CX + 4, CY + 4, KZ)
        extended = with_halo(spread_tile, (("row", 1), ("col", 2)), 2)
        cycle_only = clear_inside(extended, ((1, CX), (2, CY)))
        folded = fold_cycle(fold_cycle(cycle_only, 1, CX), 2, CY)
        spectrum = jnp.einsum(
            "sxyz,zk->sxyk",
            spread_tile[:, 2 : CX + 2, 2 : CY + 2] + folded,
            hartley_z,
            precision=highest,
        )
        along_y = jnp.einsum(
            "sxyz,yk->sxkz",
            lax.all_to_all(spectrum, "col", split_axis=3, concat_axis=2, tiled=True),
            hartley_y,
            precision=highest,
        )
        along_x = (
            jnp.einsum(
                "sxyz,xk->skyz",
                lax.all_to_all(along_y, "row", split_axis=2, concat_axis=1, tiled=True),
                hartley_x,
                precision=highest,
            )
            * kernel[None]
        )
        mixed_part = jnp.einsum("sxyz,xk->skyz", along_x, hartley_x, precision=highest)
        returned = lax.all_to_all(mixed_part, "row", split_axis=1, concat_axis=2, tiled=True)
        swapped = jnp.einsum("sxyz,yk->sxkz", returned, hartley_y, precision=highest)
        restored = lax.all_to_all(swapped, "col", split_axis=2, concat_axis=3, tiled=True)
        padded = with_halo(
            jnp.einsum("sxyz,zk->sxyk", restored, hartley_z, precision=highest),
            (("row", 1), ("col", 2)),
            2,
        )
        line = padded.reshape(RHS, plane_count, KZ)
        extended_line = jnp.concatenate([line[..., KZ - 2 :], line, line[..., :2]], axis=-1)
        windows = jnp.stack(
            [
                extended_line[..., tile * slab_depth : tile * slab_depth + window_len]
                for tile in range(tile_count)
            ],
            axis=-2,
        )
        sampled = jnp.einsum("sptw,twb->sptb", windows, depth_table, precision=highest)
        with_flat = sampled[..., :TILE].reshape(RHS, plane_count, atom_count)
        with_slope = sampled[..., TILE:].reshape(RHS, plane_count, atom_count)
        recip_part = jnp.stack(
            [
                jnp.sum(with_flat * plane_dx[None], axis=1),
                jnp.sum(with_flat * plane_dy[None], axis=1),
                jnp.sum(with_slope * plane_flat[None], axis=1),
            ],
            axis=1,
        )
        image_field = direction / polar_wide - direct + recip_part - self_coef * direction
        step_size = (progress / inner_sum(direction, image_field))[:, None, None]
        solution = solution + step_size * direction
        residual = residual - step_size * image_field
        scaled_res = polar_wide * residual
        progress_next = inner_sum(residual, scaled_res)
        direction = scaled_res + (progress_next / progress)[:, None, None] * direction
        progress = progress_next
    return (solution[None, None], residual[None, None])


X_PAD = CX + 4
Y_PAD = CY + 4
SLOT_ROWS = 16
SPLIT = 2
VMEM_LIMIT = 60_000_000
SMALL_VMEM_LIMIT = 24_000_000
MIDDLE_VMEM_LIMIT = 56_000_000
ROOMY_BYTES = 12 << 20
EARLY_TILES = 1
PAIR_ROWS = 64
GROUP = 8
SCREEN_SCALE = 0.4
SCREEN_COEF = (
    0.22567588090896606,
    0.2256690263748169,
    0.20785020291805267,
    0.16849851608276367,
    0.14156343042850494,
    -0.005832736846059561,
    0.16930203139781952,
    -0.1830107867717743,
    0.05028456076979637,
)


def halves(value):
    high = value.astype(jnp.bfloat16)
    return high, (value - high.astype(jnp.float32)).astype(jnp.bfloat16)


def halves_np(value):
    value = value.astype(np.float32)
    high = value.astype(ml_dtypes.bfloat16)
    return high, (value - high.astype(np.float32)).astype(ml_dtypes.bfloat16)


def product(left, right, left_dim=1, right_dim=0):
    def one(first, second):
        return lax.dot_general(
            first,
            second,
            (((left_dim,), (right_dim,)), ((), ())),
            preferred_element_type=jnp.float32,
        )

    return one(left[0], right[0]) + (one(left[1], right[0]) + one(left[0], right[1]))


def cas_np(wave, place, length):
    angles = 2.0 * np.pi / length * (wave[:, None] * place[None, :] % length)
    return np.cos(angles) + np.sin(angles)


def modulus_np(wave, length):
    coef = np.array([1.0, 11.0, 11.0, 1.0]) / 24.0
    angles = 2.0 * np.pi / length * (wave[:, None] * np.arange(4)[None, :])
    return (coef * np.cos(angles)).sum(1) ** 2 + (coef * np.sin(angles)).sum(1) ** 2


def influence_np(length_x, length_y, length_z):
    total = np.zeros((length_x, length_y, length_z))
    modulus = np.ones((length_x, length_y, length_z))
    excluded = np.zeros((length_x, length_y, length_z), bool)
    for axis, length in enumerate((length_x, length_y, length_z)):
        wave = np.arange(length)
        shape = [1, 1, 1]
        shape[axis] = length
        total = total + ((np.minimum(wave, length - wave) / length) ** 2).reshape(shape)
        modulus = modulus * modulus_np(wave, length).reshape(shape)
        excluded = excluded | (wave * 2 == length).reshape(shape)
    excluded[0, 0, 0] = True
    safe = np.where(excluded, 1.0, total)
    result = np.exp(-(np.pi**2) / ewald_beta**2 * safe) / (
        np.pi * safe * np.where(excluded, 1.0, modulus)
    )
    return np.where(excluded, 0.0, result) / (length_x * length_y * length_z)


def slab_tables(rows_count, cols_count):
    grid_x = CX * rows_count
    grid_y = CY * cols_count
    devices = rows_count * cols_count
    chunk = KZ // devices
    wave_z = (np.arange(devices)[None, :] * chunk + np.arange(chunk)[:, None]).reshape(-1)
    along_z = cas_np(wave_z, np.arange(KZ), KZ)
    place_x = np.arange(rows_count)[:, None] * CX + np.arange(X_PAD)[None, :] - 2
    along_x = cas_np(np.arange(grid_x), place_x.reshape(-1) % grid_x, grid_x)
    x_high, x_low = halves_np(along_x)
    forward_x = np.concatenate([x_high, x_low, x_high], axis=1)
    backward_x = np.concatenate([x_high.T, x_low.T, x_high.T], axis=1)
    place_y = (np.arange(cols_count)[:, None] * CY + np.arange(Y_PAD)[None, :] - 2) % grid_y
    along_y = cas_np(np.arange(grid_y), place_y.reshape(-1), grid_y)
    along_y = along_y.reshape(grid_y, cols_count, Y_PAD)
    units = chunk * RHS // SPLIT
    block = np.einsum("uv,kcy->cuyvk", np.eye(units), along_y)
    block = block.reshape(cols_count * units * Y_PAD, units * grid_y)
    kernel = influence_np(grid_x, grid_y, KZ).reshape(grid_x, grid_y, devices, chunk)
    kernel = np.transpose(kernel, (2, 0, 3, 1))[:, :, :, None, :]
    kernel = np.broadcast_to(kernel, (devices, grid_x, chunk, RHS, grid_y))
    kernel = kernel.reshape(devices, grid_x, SPLIT, units * grid_y)
    kernel = np.moveaxis(kernel, 2, 1).reshape(devices, SPLIT * grid_x, units * grid_y)
    kernel = kernel.astype(np.float32)
    return dict(
        along_z=halves_np(along_z),
        forward_x=forward_x,
        backward_x=backward_x,
        block=halves_np(block),
        kernel=kernel,
    )


def pack_body(rhs_ref, place_ref, polar_ref, start_ref, payload_ref):
    polar = polar_ref[...]
    start = read_rows(rhs_ref) * polar
    start_ref[...] = start
    place = [place_ref[dim] for dim in range(3)]
    everything = jnp.concatenate(place + [1.0 / jnp.sqrt(polar), start], axis=0)
    store_payload(payload_ref, everything)


def read_rows(rows_ref):
    return jnp.concatenate([rows_ref[dim] for dim in range(3)], axis=0)


def store_payload(payload_ref, everything):
    tile_count = everything.shape[1] // TILE
    for quantity in range(everything.shape[0]):
        for tile in range(tile_count):
            row = quantity * tile_count + tile
            payload_ref[row : row + 1, :] = everything[
                quantity : quantity + 1, tile * TILE : (tile + 1) * TILE
            ]


def placed_rows(slot, weights, extent):
    slot_index = lax.broadcasted_iota(jnp.int32, (extent, slot.shape[1]), 0)
    placed = jnp.zeros((extent, slot.shape[1]), jnp.float32)
    for stencil in range(5):
        target = slot + stencil
        if extent == KZ:
            target = jnp.where(target >= KZ, target - KZ, target)
        placed = placed + jnp.where(slot_index == target, weights[stencil], 0.0)
    return placed


def spread_into(message_ref, moment, rows_x, slope_x, rows_y, slope_y, depth, devices):
    blocks = []
    for step in range(X_PAD):
        flat_x = rows_x[step : step + 1]
        tilt_x = slope_x[step : step + 1]
        for rhs in range(RHS):
            part_x = tilt_x * moment[rhs : rhs + 1]
            part_y = flat_x * moment[RHS + rhs : RHS + rhs + 1]
            part_z = flat_x * moment[2 * RHS + rhs : 2 * RHS + rhs + 1]
            blocks.append(
                jnp.concatenate([part_x * rows_y + part_y * slope_y, part_z * rows_y], axis=1)
            )
    charges = jnp.concatenate(blocks, axis=0)
    spectrum = product(depth, halves(charges), 1, 1)
    slot_rows = message_ref.shape[0] // devices
    chunk = KZ // devices
    width = RHS * Y_PAD
    for step in range(X_PAD):
        message_ref[pl.ds(step, devices, stride=slot_rows), :] = jnp.concatenate(
            [
                spectrum[unit * devices : (unit + 1) * devices, step * width : (step + 1) * width]
                for unit in range(chunk)
            ],
            axis=1,
        )


def sample_from(message_ref, rows_x, slope_x, rows_y, slope_y, depth, devices):
    chunk = KZ // devices
    width = RHS * Y_PAD
    slot_rows = message_ref.shape[0] // devices
    pieces = [
        message_ref[pl.ds(step, devices, stride=slot_rows), :] for step in range(X_PAD)
    ]
    spare = jnp.zeros((devices, KZ - X_PAD * width), jnp.float32)
    spectrum = jnp.concatenate(
        [
            jnp.concatenate(
                [piece[:, unit * width : (unit + 1) * width] for piece in pieces] + [spare], axis=1
            )
            for unit in range(chunk)
        ],
        axis=0,
    )
    spectrum = jnp.transpose(spectrum)[: X_PAD * width]
    sampled = product(halves(spectrum), depth, 1, 0)
    atoms = rows_x.shape[1]
    fields = [None] * (3 * RHS)
    for rhs in range(RHS):
        sum_x = sum_y = sum_z = None
        for step in range(X_PAD):
            first = step * width + rhs * Y_PAD
            flat = sampled[first : first + Y_PAD, :atoms]
            tilt = sampled[first : first + Y_PAD, atoms:]
            part_x = slope_x[step : step + 1] * flat
            part_y = rows_x[step : step + 1] * flat
            part_z = rows_x[step : step + 1] * tilt
            sum_x = part_x if sum_x is None else sum_x + part_x
            sum_y = part_y if sum_y is None else sum_y + part_y
            sum_z = part_z if sum_z is None else sum_z + part_z
        fields[rhs] = jnp.sum(sum_x * rows_y, axis=0, keepdims=True)
        fields[RHS + rhs] = jnp.sum(sum_y * slope_y, axis=0, keepdims=True)
        fields[2 * RHS + rhs] = jnp.sum(sum_z * rows_y, axis=0, keepdims=True)
    return jnp.concatenate(fields, axis=0)


def read_tables(tables_ref):
    return (
        tables_ref[0:X_PAD],
        tables_ref[SLOT_ROWS : SLOT_ROWS + X_PAD],
        tables_ref[2 * SLOT_ROWS : 2 * SLOT_ROWS + Y_PAD],
        tables_ref[2 * SLOT_ROWS + Y_PAD : 2 * SLOT_ROWS + 2 * Y_PAD],
    )


def setup_body(
    lengths,
    devices,
    place_ref,
    base_ref,
    start_ref,
    z_high_ref,
    z_low_ref,
    message_ref,
    tables_ref,
    depth_high_ref,
    depth_low_ref,
):
    base = [base_ref[dim] for dim in range(3)]
    fractions = []
    cells = []
    for dim in range(3):
        cell = base[dim] + 2
        cell = jnp.where(cell >= lengths[dim], cell - lengths[dim], cell)
        cells.append(cell)
        fractions.append(place_ref[dim] - cell.astype(jnp.float32))
    values, slopes = spline_table(jnp.concatenate(fractions, axis=0))
    values = [[values[stencil][dim : dim + 1] for stencil in range(5)] for dim in range(3)]
    slopes = [[slopes[stencil][dim : dim + 1] for stencil in range(5)] for dim in range(3)]
    slot_x = lax.rem(cells[0], CX)
    slot_y = lax.rem(cells[1], CY)
    tables_ref[0:SLOT_ROWS] = placed_rows(slot_x, values[0], SLOT_ROWS)
    tables_ref[SLOT_ROWS : 2 * SLOT_ROWS] = placed_rows(slot_x, slopes[0], SLOT_ROWS)
    tables_ref[2 * SLOT_ROWS : 2 * SLOT_ROWS + Y_PAD] = placed_rows(slot_y, values[1], Y_PAD)
    tables_ref[2 * SLOT_ROWS + Y_PAD : 2 * SLOT_ROWS + 2 * Y_PAD] = placed_rows(
        slot_y, slopes[1], Y_PAD
    )
    window = jnp.concatenate(
        [
            placed_rows(base[2], values[2], KZ),
            placed_rows(base[2], slopes[2], KZ),
        ],
        axis=1,
    )
    depth = product((z_high_ref[...], z_low_ref[...]), halves(window), 1, 0)
    depth = halves(depth)
    depth_high_ref[...] = depth[0]
    depth_low_ref[...] = depth[1]
    spread_into(message_ref, start_ref[...], *read_tables(tables_ref), depth, devices)


def transform_in(message_ref, forward_ref, block_high_ref, block_low_ref, rows_count, cols_count):
    gathered = jnp.concatenate(
        [
            jnp.concatenate(
                [
                    message_ref[(r * cols_count + c) * X_PAD : (r * cols_count + c + 1) * X_PAD]
                    for r in range(rows_count)
                ],
                axis=0,
            )
            for c in range(cols_count)
        ],
        axis=1,
    )
    high, low = halves(gathered)
    along = jnp.dot(
        forward_ref[...],
        jnp.concatenate([high, high, low], axis=0),
        preferred_element_type=jnp.float32,
    )
    part = along.shape[1] // cols_count // SPLIT
    along = jnp.concatenate(
        [
            jnp.concatenate(
                [
                    along[:, (c * SPLIT + half) * part : (c * SPLIT + half + 1) * part]
                    for c in range(cols_count)
                ],
                axis=1,
            )
            for half in range(SPLIT)
        ],
        axis=0,
    )
    return product(halves(along), (block_high_ref[...], block_low_ref[...]))


def transform_out(result_ref, values, backward_ref, block_high_ref, block_low_ref, counts):
    rows_count, cols_count = counts
    spread = product(halves(values), (block_high_ref[...], block_low_ref[...]), 1, 1)
    grid_x = spread.shape[0] // SPLIT
    part = spread.shape[1] // cols_count
    spread = jnp.concatenate(
        [
            spread[half * grid_x : (half + 1) * grid_x, c * part : (c + 1) * part]
            for c in range(cols_count)
            for half in range(SPLIT)
        ],
        axis=1,
    )
    high, low = halves(spread)
    along = jnp.dot(
        backward_ref[...],
        jnp.concatenate([high, high, low], axis=0),
        preferred_element_type=jnp.float32,
    )
    width = along.shape[1] // cols_count
    slot_rows = result_ref.shape[0] // (rows_count * cols_count)
    for r in range(rows_count):
        for c in range(cols_count):
            first = (r * cols_count + c) * slot_rows
            result_ref[first : first + X_PAD, :] = along[
                r * X_PAD : (r + 1) * X_PAD, c * width : (c + 1) * width
            ]


def middle_first_body(
    counts,
    message_ref,
    kernel_ref,
    forward_ref,
    backward_ref,
    block_high_ref,
    block_low_ref,
    result_ref,
    wave_ref,
):
    wave = transform_in(message_ref, forward_ref, block_high_ref, block_low_ref, *counts)
    wave_ref[...] = wave
    transform_out(
        result_ref, wave * kernel_ref[...], backward_ref, block_high_ref, block_low_ref, counts
    )


def gather_rows(parts):
    tiles = [
        parts[GROUP * tile : GROUP * tile + GROUP, :] for tile in range(parts.shape[0] // GROUP)
    ]
    return jnp.concatenate(tiles, axis=1)[0 : 3 * RHS]


def row_total(value, rhs):
    row = lax.broadcasted_iota(jnp.int32, value.shape, 0)
    return total(jnp.where(lax.rem(row, RHS) == rhs, value, 0.0))


def total(value):
    return jnp.sum(jnp.sum(value, axis=0, keepdims=True), axis=1, keepdims=True)


def middle_second_body(
    counts,
    message_ref,
    kernel_ref,
    forward_ref,
    backward_ref,
    block_high_ref,
    block_low_ref,
    wave_ref,
    start_ref,
    carried_ref,
    near_ref,
    polar_ref,
    result_ref,
    local_ref,
):
    near_rows = gather_rows(near_ref)
    wave = transform_in(message_ref, forward_ref, block_high_ref, block_low_ref, *counts)
    filtered = wave * kernel_ref[...]
    transform_out(result_ref, filtered, backward_ref, block_high_ref, block_low_ref, counts)
    before = wave_ref[...]
    grid_y = CY * counts[1]
    lane = lax.broadcasted_iota(jnp.int32, wave.shape, 1)
    own_rhs = lax.rem(lax.div(lane, grid_y), RHS)
    image = carried_ref[0 : 3 * RHS]
    second = carried_ref[8 : 8 + 3 * RHS]
    start = start_ref[...]
    local_part = second / polar_ref[...] - near_rows - self_coef * second
    local_ref[0 : 3 * RHS] = image
    local_ref[8 : 8 + 3 * RHS] = second
    local_ref[16 : 16 + 3 * RHS] = local_part
    local_ref[24 : 24 + 3 * RHS] = start
    slot = lax.broadcasted_iota(jnp.int32, (1, result_ref.shape[1]), 1)
    sums = jnp.zeros((1, result_ref.shape[1]), jnp.float32)
    for rhs in range(RHS):
        mine = own_rhs == rhs
        parts = (
            row_total(start * start / polar_ref[...], rhs),
            row_total(start * image, rhs),
            row_total(second * image, rhs),
            row_total(start * local_part, rhs) + total(jnp.where(mine, before * filtered, 0.0)),
            row_total(second * local_part, rhs) + total(jnp.where(mine, wave * filtered, 0.0)),
        )
        for index, part in enumerate(parts):
            sums = jnp.where(slot == rhs * len(parts) + index, part, sums)
    devices = counts[0] * counts[1]
    result_ref[pl.ds(X_PAD, devices, stride=X_PAD + 1), :] = jnp.broadcast_to(
        sums, (devices, sums.shape[1])
    )


def sample_body(
    devices,
    message_ref,
    tables_ref,
    depth_high_ref,
    depth_low_ref,
    start_ref,
    near_ref,
    polar_ref,
    carried_ref,
    payload_ref,
):
    tables = read_tables(tables_ref)
    depth = (depth_high_ref[...], depth_low_ref[...])
    field = sample_from(message_ref, *tables, depth, devices)
    start = start_ref[...]
    polar = polar_ref[...]
    image = start / polar - gather_rows(near_ref) + field - self_coef * start
    second = polar * image
    carried_ref[0 : 3 * RHS] = image
    carried_ref[8 : 8 + 3 * RHS] = second
    store_payload(payload_ref, second)


def spread_body(
    devices,
    tables_ref,
    depth_high_ref,
    depth_low_ref,
    carried_ref,
    result_ref,
):
    depth = (depth_high_ref[...], depth_low_ref[...])
    second = carried_ref[8 : 8 + 3 * RHS]
    spread_into(result_ref, second, *read_tables(tables_ref), depth, devices)


def final_body(
    devices,
    message_ref,
    tables_ref,
    depth_high_ref,
    depth_low_ref,
    rhs_ref,
    local_ref,
    dipole_ref,
    residual_ref,
):
    tables = read_tables(tables_ref)
    depth = (depth_high_ref[...], depth_low_ref[...])
    field = sample_from(message_ref, *tables, depth, devices)
    image = local_ref[0 : 3 * RHS]
    second = local_ref[8 : 8 + 3 * RHS]
    image_second = local_ref[16 : 16 + 3 * RHS] + field
    start = local_ref[24 : 24 + 3 * RHS]
    sums = jnp.sum(
        message_ref[pl.ds(X_PAD, devices, stride=X_PAD + 1), :], axis=0, keepdims=True
    )
    steps = []
    for rhs in range(RHS):
        progress, start_image, second_image, start_next, second_next = [
            sums[:, rhs * 5 + index : rhs * 5 + index + 1] for index in range(5)
        ]
        step = progress / start_image
        progress_next = progress - 2.0 * step * start_image + step * step * second_image
        grown = 1.0 + progress_next / progress
        curvature = (
            grown * grown * start_image
            - step * grown * (start_next + second_image)
            + step * step * second_next
        )
        steps.append((step, grown, progress_next / curvature))
    row = lax.broadcasted_iota(jnp.int32, (RHS, 1), 0)
    step, grown, step_next = [
        sum(jnp.where(row == rhs, steps[rhs][index], 0.0) for rhs in range(RHS))
        for index in range(3)
    ]
    for dim in range(3):
        rows = slice(dim * RHS, (dim + 1) * RHS)
        direction = grown * start[rows] - step * second[rows]
        image_direction = grown * image[rows] - step * image_second[rows]
        dipole_ref[dim] = step * start[rows] + step_next * direction
        residual_ref[dim] = rhs_ref[dim] - step * image[rows] - step_next * image_direction


def near_base(entry, brick_rows):
    return lax.shift_right_logical(entry, 2) * brick_rows + lax.bitwise_and(entry, 3)


def nearest(places, origin, span):
    return places - span * jnp.floor((places - origin) * (1.0 / span) + 0.5)


def unwrap_near(near, tile_count, spans):
    rows = near.shape[0] // 9
    for dim in range(2):
        own = 4 * rows + dim * tile_count
        origin = near[own : own + 1, 0:1]
        for brick in range(9):
            first = brick * rows + dim * tile_count
            near[first : first + tile_count, :] = nearest(
                near[first : first + tile_count, :], origin, spans[dim]
            )


def pick_rows(picked, near, lists_ref, tile, place, tile_count, quantities, origin, span):
    rows = near.shape[0] // 9
    place = place * lists_ref.shape[1] * quantities * GROUP
    for entry in range(lists_ref.shape[1]):
        base = near_base(lists_ref[tile, entry], rows)
        for quantity in range(quantities):
            values = near[pl.ds(base + quantity * tile_count, 1), :]
            if quantity == 2 and span is not None:
                values = nearest(values, origin, span)
            first = place + (entry * quantities + quantity) * GROUP
            picked[first : first + GROUP, :] = jnp.broadcast_to(values, (GROUP, TILE))


def widen_own(near, quantities, tile_count, tile, place, wide):
    offset = near.shape[0] // 9 * 4
    rows = [
        near[offset + quantity * tile_count + tile : offset + quantity * tile_count + tile + 1, :]
        for quantity in range(quantities)
    ]
    spare = jnp.zeros((TILE - quantities, TILE), jnp.float32)
    columns = jnp.transpose(jnp.concatenate(rows + [spare], axis=0))
    for quantity in range(quantities):
        first = (place * quantities + quantity) * TILE
        wide[first : first + TILE, :] = jnp.broadcast_to(
            columns[:, quantity : quantity + 1], (TILE, TILE)
        )


def add_field(sums, first_term, second_term, apart, moments):
    for rhs in range(RHS):
        moment = [moments[RHS * dim + rhs] for dim in range(3)]
        projected = moment[0] * apart[0] + moment[1] * apart[1] + moment[2] * apart[2]
        weighted = second_term * projected
        for dim in range(3):
            index = RHS * dim + rhs
            sums[index] = sums[index] + (weighted * apart[dim] - first_term * moment[dim])


def finish_sums(field_ref, sums_ref, first_tile, place):
    place = place * 3 * RHS
    lane = lax.broadcasted_iota(jnp.int32, (TILE, TILE), 1)
    merged = jnp.zeros((TILE, TILE), jnp.float32)
    for index in range(3 * RHS):
        first = (place + index) * TILE
        column = jnp.sum(sums_ref[first : first + TILE, :], axis=1, keepdims=True)
        merged = jnp.where(lane == index, column, merged)
    first = (first_tile + place // (3 * RHS)) * GROUP
    field_ref[first : first + GROUP, :] = jnp.transpose(merged)[0:GROUP]


def pair_rows(start, group):
    return pl.ds(pl.multiple_of(start + group * GROUP, GROUP), GROUP)


def wide_rows(start, group, quantity):
    return pl.ds(pl.multiple_of(quantity * TILE + start + group * GROUP, GROUP), GROUP)


def pair_terms(square_dist, damp):
    inverse = lax.rsqrt(square_dist)
    distance = square_dist * inverse
    inverse_sq = inverse * inverse
    inverse_cube = inverse_sq * inverse
    cubed = damp * (distance * square_dist)
    damping = jnp.exp(cubed)
    bell = jnp.exp(-(ewald_beta * ewald_beta) * square_dist)
    stretched = 1.0 + (SCREEN_SCALE * ewald_beta) * distance
    turned = pl.reciprocal(stretched, approx=True)
    turned = turned * (2.0 - stretched * turned)
    series = SCREEN_COEF[-1] * turned + SCREEN_COEF[-2]
    for coef in SCREEN_COEF[-3::-1]:
        series = series * turned + coef
    screen = bell * turned * series
    gaussian = (2.0 * ewald_beta / math.sqrt(math.pi)) * bell
    bare = screen - damping
    first_term = bare * inverse_cube + gaussian * inverse_sq
    second_term = (
        3.0 * (first_term + (cubed * damping) * inverse_cube)
        + (2.0 * ewald_beta * ewald_beta) * gaussian
    ) * inverse_sq
    return first_term, second_term


def step_rows(step, size, offset):
    return pl.ds(pl.multiple_of(step * size + offset, GROUP), GROUP)


def tile_rows(step, rows):
    return pl.ds(pl.multiple_of(step * rows, GROUP), rows)


def start_all(copies):
    for copy in copies:
        copy.start()


def wait_all(copies):
    for copy in copies:
        copy.wait()


def near_copies(sources, near, semaphore):
    rows = sources[0].shape[0]
    return [
        pltpu.make_async_copy(
            source, near.at[index * rows : (index + 1) * rows, :], semaphore.at[index]
        )
        for index, source in enumerate(sources)
    ]


def term_copies(terms, buffers, semaphore, begin, step, size, inward):
    rows = pl.ds(pl.multiple_of((begin + step) * size, GROUP), size)
    place = pl.ds(pl.multiple_of(step * size, GROUP), size)
    copies = []
    for index in range(2):
        far, here = terms[index].at[rows, :], buffers[index].at[place, :]
        ends = (far, here) if inward else (here, far)
        copies.append(pltpu.make_async_copy(*ends, semaphore.at[index, step]))
    return copies


def pair_first_body(
    first_tile,
    last_tile,
    tile_count,
    spans,
    lists_ref,
    up_ref,
    stack_ref,
    down_ref,
    *others,
):
    first_ref, second_ref, field_ref, near_ref = others[-14:-10]
    near, picked, wide, sums_ref, kept, field, first_buffer, second_buffer, semaphore, busy = others[-10:]
    terms = (first_ref, second_ref)
    buffers = (first_buffer, second_buffer)
    copies = near_copies((up_ref, stack_ref, down_ref), near, semaphore.at[0])
    if first_tile > 0:
        copies.append(
            pltpu.make_async_copy(
                others[0], field.at[0 : first_tile * GROUP, :], semaphore.at[0, 3]
            )
        )
    start_all(copies)
    wait_all(copies)
    entries = lists_ref.shape[1]
    rows = near.shape[0] // 9
    quantities = rows // tile_count
    unwrap_near(near, tile_count, spans)
    for brick in range(9):
        kept[brick * 3 * tile_count : (brick + 1) * 3 * tile_count, :] = near[
            brick * rows : brick * rows + 3 * tile_count, :
        ]
    keep = pltpu.make_async_copy(kept, near_ref, semaphore.at[1, 3])
    keep.start()
    for place, tile in enumerate(range(first_tile, last_tile)):
        widen_own(near, 4, tile_count, tile, place, wide)
        own = rows * 4 + 2 * tile_count + tile
        origin = near[own : own + 1, 0:1]
        pick_rows(picked, near, lists_ref, tile, place, tile_count, quantities, origin, spans[2])
    parts = TILE // PAIR_ROWS
    steps = (last_tile - first_tile) * parts

    size = entries * PAIR_ROWS

    def sent(step):
        return term_copies(terms, buffers, busy, first_tile * parts, step, size, False)

    @pl.loop(0, steps)
    def _(step):
        tile = lax.div(step, parts)
        start = lax.rem(step, parts) * PAIR_ROWS
        step_picked = picked.at[tile_rows(tile, entries * quantities * GROUP), :]
        step_wide = wide.at[tile_rows(tile, 4 * TILE), :]
        step_sums = sums_ref.at[tile_rows(tile, 3 * RHS * TILE), :]
        for group in range(PAIR_ROWS // GROUP):
            own = [step_wide[wide_rows(start, group, dim), :] for dim in range(4)]
            own_damp = -thole_a * own[3]
            sums = [jnp.zeros((GROUP, TILE), jnp.float32) for _ in range(3 * RHS)]
            itself = (
                lax.broadcasted_iota(jnp.int32, (GROUP, TILE), 0) + (start + group * GROUP)
            ) == lax.broadcasted_iota(jnp.int32, (GROUP, TILE), 1)
            for entry in range(entries):
                first = entry * quantities * GROUP
                rows = [
                    step_picked[first + quantity * GROUP : first + (quantity + 1) * GROUP, :]
                    for quantity in range(quantities)
                ]
                apart = [rows[dim] - own[dim] for dim in range(3)]
                square_dist = apart[0] * apart[0] + apart[1] * apart[1] + apart[2] * apart[2]
                if entry == 0:
                    square_dist = jnp.where(itself, 1.0, square_dist)
                first_term, second_term = pair_terms(square_dist, own_damp * rows[3])
                if entry == 0:
                    first_term = jnp.where(itself, 0.0, first_term)
                    second_term = jnp.where(itself, 0.0, second_term)
                place = step_rows(step, size, entry * PAIR_ROWS + group * GROUP)
                first_buffer[place, :] = first_term
                second_buffer[place, :] = second_term
                add_field(sums, first_term, second_term, apart, rows[4:])
            for index, value in enumerate(sums):
                step_sums[wide_rows(start, group, index), :] = value
        start_all(sent(step))

    for place in range(last_tile - first_tile):
        finish_sums(field, sums_ref, first_tile, place)
    result = pltpu.make_async_copy(field, head_of(field_ref, field), semaphore.at[1, 2])
    result.start()

    @pl.loop(0, steps)
    def _(step):
        wait_all(sent(step))

    keep.wait()
    result.wait()


def pair_second_body(
    tile_count,
    spans,
    lists_ref,
    near_ref,
    up_ref,
    stack_ref,
    down_ref,
    first_ref,
    second_ref,
    field_ref,
    near,
    near_moment,
    picked,
    picked_moment,
    wide,
    sums_ref,
    field,
    first_buffer,
    second_buffer,
    semaphore,
    busy,
):
    terms = (first_ref, second_ref)
    buffers = (first_buffer, second_buffer)
    parts = TILE // PAIR_ROWS
    steps = tile_count * parts

    entries = lists_ref.shape[1]
    size = entries * PAIR_ROWS

    def fetched(step):
        return term_copies(terms, buffers, busy, 0, step, size, True)

    places = pltpu.make_async_copy(
        near_ref, near.at[0 : near_ref.shape[0], :], semaphore.at[1, 3]
    )
    places.start()
    copies = near_copies((up_ref, stack_ref, down_ref), near_moment, semaphore.at[2])
    start_all(copies)

    @pl.loop(0, steps)
    def _(step):
        start_all(fetched(step))

    places.wait()
    for tile in range(tile_count):
        widen_own(near, 3, tile_count, tile, tile, wide)
        own = near.shape[0] // 9 * 4 + 2 * tile_count + tile
        origin = near[own : own + 1, 0:1]
        pick_rows(picked, near, lists_ref, tile, tile, tile_count, 3, origin, spans[2])
    wait_all(copies)
    for tile in range(tile_count):
        pick_rows(
            picked_moment, near_moment, lists_ref, tile, tile, tile_count, 3 * RHS, None, None
        )

    @pl.loop(0, steps)
    def _(step):
        wait_all(fetched(step))
        tile = lax.div(step, parts)
        start = lax.rem(step, parts) * PAIR_ROWS
        step_picked = picked.at[tile_rows(tile, entries * 3 * GROUP), :]
        step_moment = picked_moment.at[tile_rows(tile, entries * 3 * RHS * GROUP), :]
        step_wide = wide.at[tile_rows(tile, 3 * TILE), :]
        step_sums = sums_ref.at[tile_rows(tile, 3 * RHS * TILE), :]
        for group in range(PAIR_ROWS // GROUP):
            own = [step_wide[wide_rows(start, group, dim), :] for dim in range(3)]
            sums = [jnp.zeros((GROUP, TILE), jnp.float32) for _ in range(3 * RHS)]
            for entry in range(entries):
                first = entry * 3 * GROUP
                apart = [
                    step_picked[first + dim * GROUP : first + (dim + 1) * GROUP, :] - own[dim]
                    for dim in range(3)
                ]
                first = first * RHS
                moments = [
                    step_moment[first + index * GROUP : first + (index + 1) * GROUP, :]
                    for index in range(3 * RHS)
                ]
                place = step_rows(step, size, entry * PAIR_ROWS + group * GROUP)
                add_field(sums, first_buffer[place, :], second_buffer[place, :], apart, moments)
            for index, value in enumerate(sums):
                step_sums[wide_rows(start, group, index), :] = value

    for place in range(tile_count):
        finish_sums(field, sums_ref, 0, place)
    result = pltpu.make_async_copy(field, head_of(field_ref, field), semaphore.at[1, 2])
    result.start()
    result.wait()


def shift(source, axis, step):
    count = lax.axis_size(axis)
    return lax.ppermute(source, axis, [(i, (i + step) % count) for i in range(count)])


def both_ways(source, axis):
    return shift(source, axis, 1), source, shift(source, axis, -1)


def whole(shape):
    return pl.BlockSpec(shape, lambda *_: (0,) * len(shape))


def anywhere():
    return pl.BlockSpec(memory_space=pl.ANY)


def join(message, payload):
    right = shift(payload, "col", -1)
    left = shift(payload, "col", 1)
    message, right, left = lax.optimization_barrier((message, right, left))
    return message, both_ways(jnp.concatenate([left, payload, right], axis=0), "row")


class Fetched:
    def __init__(self, source, scratch, semaphore):
        self.copy = pltpu.make_async_copy(source, scratch, semaphore)
        self.copy.start()
        self.scratch = scratch
        self.shape = scratch.shape
        self.waiting = True

    def wait(self):
        if self.waiting:
            self.copy.wait()
            self.waiting = False

    def __getitem__(self, index):
        self.wait()
        return self.scratch[index]


class Head:
    def __init__(self, array, shape):
        self.array = array
        self.shape = shape
        self.dtype = array.dtype


def roomy(shape):
    return (ROOMY_BYTES // 4 // shape[1], shape[1])


def head_of(far, here):
    if far.shape == here.shape:
        return far
    return far.at[0 : here.shape[0], :]


def call(body, outs, *operands, after=(), own_block=None, near=0, large=(), vmem=VMEM_LIMIT):
    count = len(operands)
    fetched = [
        pltpu.VMEM(operand.shape[1:] if index == own_block else operand.shape, operand.dtype)
        for index, operand in enumerate(operands)
        if index >= near
    ]
    arrays = [operand.array if isinstance(operand, Head) else operand for operand in operands]

    def run(*refs):
        refs = refs[len(after) :]
        sources, refs = refs[:count], refs[count:]
        results, refs = refs[: len(outs)], refs[len(outs) :]
        targets, written, semaphore = refs[: count - near], refs[count - near : -1], refs[-1]
        inputs = list(sources[:near])
        for index in range(near, count):
            source = sources[index]
            if index == own_block:
                place = lax.axis_index("row") * lax.axis_size("col") + lax.axis_index("col")
                source = source.at[place]
            else:
                source = head_of(source, targets[index - near])
            inputs.append(Fetched(source, targets[index - near], semaphore.at[index]))
        body(*inputs, *written)
        for operand in inputs[near:]:
            operand.wait()
        copies = [
            pltpu.make_async_copy(value, head_of(result, value), semaphore.at[count + index])
            for index, (value, result) in enumerate(zip(written, results))
        ]
        for copy in copies:
            copy.start()
        for copy in copies:
            copy.wait()

    return pl.pallas_call(
        run,
        in_specs=[anywhere()] * len(after)
        + [pl.BlockSpec(memory_space=pltpu.VMEM)] * near
        + [anywhere()] * (count - near),
        out_specs=[anywhere()] * len(outs),
        out_shape=[
            jax.ShapeDtypeStruct(roomy(shape) if index in large else shape, dtype)
            for index, (shape, dtype) in enumerate(outs)
        ],
        scratch_shapes=fetched
        + [pltpu.VMEM(shape, dtype) for shape, dtype in outs]
        + [pltpu.SemaphoreType.DMA((count + len(outs),))],
        compiler_params=pltpu.CompilerParams(vmem_limit_bytes=vmem),
        cost_estimate=pl.CostEstimate(
            flops=200_000_000, bytes_accessed=4 << 20, transcendentals=0
        ),
    )(*after, *arrays)


def final_call(body, outs, *operands):
    return pl.pallas_call(
        body,
        grid=(1,),
        in_specs=[whole(operand.shape) for operand in operands],
        out_specs=[whole(shape) for shape, _ in outs],
        out_shape=[jax.ShapeDtypeStruct(shape, dtype) for shape, dtype in outs],
        compiler_params=pltpu.CompilerParams(vmem_limit_bytes=SMALL_VMEM_LIMIT),
    )(*operands)


def pair_call(body, outs, scratch, lists, *operands, tiles, large, aliased=0):
    buffers = (tiles * lists.shape[1] * TILE, TILE)
    first = 1 + len(operands) - aliased
    return pl.pallas_call(
        body,
        in_specs=[pl.BlockSpec(memory_space=pltpu.SMEM)] + [anywhere()] * len(operands),
        out_specs=[anywhere()] * len(outs),
        out_shape=[
            jax.ShapeDtypeStruct(roomy(shape) if index == large else shape, jnp.float32)
            for index, shape in enumerate(outs)
        ],
        scratch_shapes=[pltpu.VMEM(shape, jnp.float32) for shape in scratch + [buffers] * 2]
        + [
            pltpu.SemaphoreType.DMA((3, 4)),
            pltpu.SemaphoreType.DMA((2, tiles * TILE // PAIR_ROWS)),
        ],
        input_output_aliases={first + index: index for index in range(aliased)},
        compiler_params=pltpu.CompilerParams(vmem_limit_bytes=VMEM_LIMIT),
        cost_estimate=pl.CostEstimate(
            flops=80_000_000, bytes_accessed=8 << 20, transcendentals=1 << 21
        ),
    )(lists, *operands)


def exchange(message, devices):
    shape = message.shape
    sent = message.reshape(devices, 1, -1)
    return lax.all_to_all(sent, ("row", "col"), split_axis=0, concat_axis=0, tiled=True).reshape(
        shape
    )


def slab_local(field_rhs, positions, polar, grid_base, tile_lists):
    rows_count = lax.axis_size("row")
    cols_count = lax.axis_size("col")
    counts = (rows_count, cols_count)
    devices = rows_count * cols_count
    lengths = (CX * rows_count, CY * cols_count, KZ)
    spans = tuple(float(length) for length in lengths)
    atoms = polar.shape[-1]
    tile_count = atoms // TILE
    listed = tile_lists.shape[-1]
    tables = slab_tables(rows_count, cols_count)
    f32 = jnp.float32
    rhs = jnp.swapaxes(field_rhs[0, 0], 0, 1)
    place = jnp.swapaxes(positions[0], 0, 1)
    base = jnp.swapaxes(grid_base[0], 0, 1)
    polar = polar.reshape(1, atoms)
    lists = tile_lists[0, 0]
    quantities = 4 + 3 * RHS
    brick_rows = quantities * tile_count
    moment_rows = 3 * RHS * tile_count
    message_shape = (devices * X_PAD, KZ // devices * RHS * Y_PAD)
    last_shape = (devices * (X_PAD + 1), message_shape[1])
    row_shape = (3 * RHS, atoms)

    start, payload = call(pack_body, [(row_shape, f32), ((brick_rows, TILE), f32)], rhs, place, polar)

    def setup(*refs):
        setup_body(lengths, devices, *refs)

    message, splines, depth_high, depth_low = call(
        setup,
        [
            (message_shape, f32),
            ((2 * SLOT_ROWS + 2 * Y_PAD, atoms), f32),
            ((KZ, 2 * atoms), jnp.bfloat16),
            ((KZ, 2 * atoms), jnp.bfloat16),
        ],
        place,
        base,
        start,
        *[jnp.asarray(table) for table in tables["along_z"]],
    )
    constants = (
        jnp.asarray(tables["kernel"]),
        jnp.asarray(tables["forward_x"]),
        jnp.asarray(tables["backward_x"]),
        *[jnp.asarray(table) for table in tables["block"]],
    )
    message, near = join(message, payload)
    arrived = exchange(message, devices)

    def pair_first(first_tile, last_tile, fields, *after):
        def body(*refs):
            pair_first_body(first_tile, last_tile, tile_count, spans, *refs)

        tiles = last_tile - first_tile
        return pair_call(
            body,
            [(tile_count * listed * TILE, TILE)] * 2
            + [(last_tile * GROUP, TILE), (9 * 3 * tile_count, TILE)],
            [
                (9 * brick_rows + GROUP, TILE),
                (tiles * listed * quantities * GROUP, TILE),
                (tiles * 4 * TILE, TILE),
                (tiles * 3 * RHS * TILE, TILE),
                (9 * 3 * tile_count, TILE),
                (last_tile * GROUP, TILE),
            ],
            lists,
            *near,
            *fields,
            *after,
            tiles=tiles,
            large=2 if first_tile > 0 else None,
            aliased=2 if first_tile > 0 else 0,
        )

    early = pair_first(0, EARLY_TILES, (), message)

    def middle_first(*refs):
        middle_first_body(counts, *refs)

    arrived, early = lax.optimization_barrier((arrived, tuple(early)))
    wave_shape = tables["kernel"].shape[1:]
    mixed, wave = call(
        middle_first,
        [(message_shape, f32), (wave_shape, f32)],
        arrived,
        *constants,
        own_block=1,
        near=1,
        large=(1,),
        vmem=MIDDLE_VMEM_LIMIT,
    )
    returned = exchange(mixed, devices)
    first_term, second_term, direct, near = pair_first(
        EARLY_TILES, tile_count, (early[2],), wave, *early[:2]
    )

    def sample(*refs):
        sample_body(devices, *refs)

    carried_shape = (16, atoms)
    field_shape = (tile_count * GROUP, TILE)
    carried, moments = call(
        sample,
        [(carried_shape, f32), ((moment_rows, TILE), f32)],
        returned,
        splines,
        depth_high,
        depth_low,
        start,
        Head(direct, field_shape),
        polar,
        near=1,
        large=(0,),
        vmem=MIDDLE_VMEM_LIMIT,
    )

    def spread(*refs):
        spread_body(devices, *refs)

    (message,) = call(
        spread,
        [(message_shape, f32)],
        splines,
        depth_high,
        depth_low,
        Head(carried, carried_shape),
    )
    message, near_moments = join(message, moments)
    arrived = exchange(message, devices)

    def pair_second(*refs):
        pair_second_body(tile_count, spans, *refs)

    (direct,) = pair_call(
        pair_second,
        [(tile_count * GROUP, TILE)],
        [
            (9 * 3 * tile_count + GROUP, TILE),
            (9 * moment_rows + GROUP, TILE),
            (tile_count * listed * 3 * GROUP, TILE),
            (tile_count * listed * 3 * RHS * GROUP, TILE),
            (tile_count * 3 * TILE, TILE),
            (tile_count * 3 * RHS * TILE, TILE),
            (tile_count * GROUP, TILE),
        ],
        lists,
        near,
        *near_moments,
        first_term,
        second_term,
        tiles=tile_count,
        large=0,
    )

    def middle_second(*refs):
        middle_second_body(counts, *refs)

    mixed, local = call(
        middle_second,
        [(last_shape, f32), ((32, atoms), f32)],
        arrived,
        *constants,
        Head(wave, wave_shape),
        start,
        Head(carried, carried_shape),
        Head(direct, field_shape),
        polar,
        own_block=1,
        near=1,
        vmem=MIDDLE_VMEM_LIMIT,
    )
    returned = exchange(mixed, devices)

    def final(*refs):
        final_body(devices, *refs)

    outs = final_call(
        final,
        [(rhs.shape, f32), (rhs.shape, f32)],
        returned,
        splines,
        depth_high,
        depth_low,
        rhs,
        local,
    )
    return tuple(jnp.swapaxes(out, 0, 1)[None, None] for out in outs)


def solution(mesh):
    placed = (
        P("row", "col", None, None, None),
        P("row", "col", None, None),
        P("row", "col", None),
        P("row", "col", None, None),
        P("row", "col", None, None),
    )
    devices = mesh.shape["row"] * mesh.shape["col"]
    return jax.shard_map(
        slab_local if KZ % devices == 0 else pencil_local,
        mesh=mesh,
        in_specs=placed,
        out_specs=(P("row", "col", None, None, None), P("row", "col", None, None, None)),
        check_vma=False,
    )
```

```python
import math

import jax
import jax.numpy as jnp
import ml_dtypes
import numpy as np
from jax import lax
from jax.experimental import pallas as pl
from jax.experimental.pallas import tpu as pltpu
from jax.sharding import PartitionSpec as P

CX = 8
CY = 4
KZ = 256
TILE = 128
RHS = 2
ITERS = 2


ewald_beta = 0.4
thole_a = 0.39
self_coef = 4.0 * ewald_beta**3 / (3.0 * math.sqrt(math.pi))
highest = lax.Precision.HIGHEST


def with_halo(cells, sides, width):
    for axis, dim in sides:
        count = lax.axis_size(axis)
        head = lax.slice_in_dim(cells, 0, width, axis=dim)
        tail = lax.slice_in_dim(cells, cells.shape[dim] - width, cells.shape[dim], axis=dim)
        cells = jnp.concatenate(
            [
                lax.ppermute(tail, axis, [(i, (i + 1) % count) for i in range(count)]),
                cells,
                lax.ppermute(head, axis, [((i + 1) % count, i) for i in range(count)]),
            ],
            axis=dim,
        )
    return cells


def spline_table(fraction):
    previous = {0: jnp.ones_like(fraction)}
    fourth = previous
    for degree in range(2, 6):
        current = {}
        for offset in range(degree):
            abscissa = fraction + offset
            summed = abscissa * previous.get(offset, 0.0) + (degree - abscissa) * previous.get(
                offset - 1, 0.0
            )
            current[offset] = summed / (degree - 1)
        if degree == 4:
            fourth = current
        previous = current
    values = jnp.stack([previous[4 - stencil] for stencil in range(5)])
    slopes = jnp.stack(
        [fourth.get(4 - stencil, 0.0) - fourth.get(3 - stencil, 0.0) for stencil in range(5)]
    )
    return (values, slopes)


def spline_modulus(wave_index, length):
    spline_coef = (1.0 / 24.0, 11.0 / 24.0, 11.0 / 24.0, 1.0 / 24.0)
    cosine_sum = jnp.zeros(wave_index.shape, jnp.float32)
    sine_sum = jnp.zeros(wave_index.shape, jnp.float32)
    for offset in range(4):
        angles = 2.0 * math.pi / length * (wave_index * offset % length).astype(jnp.float32)
        cosine_sum = cosine_sum + spline_coef[offset] * jnp.cos(angles)
        sine_sum = sine_sum + spline_coef[offset] * jnp.sin(angles)
    return cosine_sum * cosine_sum + sine_sum * sine_sum


def folded_square(wave_index, length):
    nearest = jnp.minimum(wave_index, length - wave_index).astype(jnp.float32) / length
    return nearest * nearest


def influence(wave_x, wave_y, wave_z, length_x, length_y, length_z):
    wave_norm = (
        folded_square(wave_x, length_x)
        + folded_square(wave_y, length_y)
        + folded_square(wave_z, length_z)
    )
    modulus = (
        spline_modulus(wave_x, length_x)
        * spline_modulus(wave_y, length_y)
        * spline_modulus(wave_z, length_z)
    )
    excluded = (wave_x * 2 == length_x) | (wave_y * 2 == length_y) | (wave_z * 2 == length_z)
    excluded = excluded | (wave_x == 0) & (wave_y == 0) & (wave_z == 0)
    safe_norm = jnp.where(excluded, 1.0, wave_norm)
    safe_modulus = jnp.where(excluded, 1.0, modulus)
    result = jnp.exp(-(math.pi**2 / ewald_beta**2) * safe_norm) / (
        math.pi * safe_norm * safe_modulus
    )
    return jnp.where(excluded, 0.0, result)


def tile_field(own_static, near_static, near_dipole, box_spans):
    listed_count = near_static.shape[0]
    tile_width = own_static.shape[1]
    box_span = jnp.array(box_spans, dtype=jnp.float32)[None, :, None, None]
    separation = near_static[:, 0:3, None, :] - own_static[None, 0:3, :, None]
    separation = separation - box_span * jnp.floor(separation / box_span + 0.5)
    dist_sq = jnp.sum(separation * separation, axis=1)
    itself = (jnp.arange(listed_count)[:, None, None] == 0) & (
        jnp.arange(tile_width)[:, None] == jnp.arange(tile_width)[None, :]
    )[None]
    safe_sq = jnp.where(itself, 1.0, dist_sq)
    distance = jnp.sqrt(safe_sq)
    scaled = distance / (own_static[3][None, :, None] * near_static[:, 3][:, None, :])
    cubed = thole_a * scaled * scaled * scaled
    damping = jnp.exp(-cubed)
    screen = lax.erfc(ewald_beta * distance)
    gaussian = 2.0 * ewald_beta / math.sqrt(math.pi) * jnp.exp(-(ewald_beta * ewald_beta) * safe_sq)
    inverse_sq = 1.0 / safe_sq
    inverse_cube = inverse_sq / distance
    first_term = (screen - damping) * inverse_cube + gaussian * inverse_sq
    second = (
        3.0 * (screen - (1.0 + cubed) * damping) * inverse_cube * inverse_sq
        + gaussian * (2.0 * ewald_beta * ewald_beta + 3.0 * inverse_sq) * inverse_sq
    )
    first_term = jnp.where(itself, 0.0, first_term)
    second = jnp.where(itself, 0.0, second)
    projected = jnp.sum(near_dipole[:, :, :, None, :] * separation[:, None, :, :, :], axis=2)
    weighted = second[:, None] * projected
    outward = jnp.sum(weighted[:, :, None] * separation[:, None], axis=(0, 4))
    inward = jnp.sum(first_term[:, None, None] * near_dipole[:, :, :, None, :], axis=(0, 4))
    return outward - inward


def hartley(length):
    counter = jnp.arange(length, dtype=jnp.int32)
    angles = (
        2.0 * math.pi / length * (counter[:, None] * counter[None, :] % length).astype(jnp.float32)
    )
    return jnp.cos(angles) + jnp.sin(angles)


def placed_table(first_cell, weights, extent):
    slot_index = jnp.arange(extent, dtype=jnp.int32)[:, None]
    placed = jnp.zeros((extent, first_cell.shape[0]), jnp.float32)
    for stencil in range(5):
        placed = placed + jnp.where(
            slot_index == (first_cell[None, :] + stencil) % extent, weights[stencil][None, :], 0.0
        )
    return placed


def pad_axis(source, axis_pos, leading, trailing):
    widths = [(0, 0)] * source.ndim
    widths[axis_pos] = (leading, trailing)
    return jnp.pad(source, widths)


def fold_cycle(cycle_only, axis_pos, inner_len):
    middle = lax.slice_in_dim(cycle_only, 4, inner_len + 4, axis=axis_pos)
    lower_cycle = lax.slice_in_dim(cycle_only, 0, 2, axis=axis_pos)
    upper_cycle = lax.slice_in_dim(cycle_only, inner_len + 6, inner_len + 8, axis=axis_pos)
    return (
        middle
        + pad_axis(lower_cycle, axis_pos, 0, inner_len - 2)
        + pad_axis(upper_cycle, axis_pos, inner_len - 2, 0)
    )


def clear_inside(extended, extents):
    inside = None
    for axis_pos, inner_len in extents:
        slot_index = lax.broadcasted_iota(jnp.int32, extended.shape, axis_pos)
        within = (slot_index >= 2) & (slot_index < inner_len + 6)
        inside = within if inside is None else inside & within
    return jnp.where(inside, 0.0, extended)


def inner_sum(left_arr, right_arr):
    return lax.psum(jnp.sum(left_arr * right_arr, axis=(1, 2)), ("row", "col"))


def pencil_local(field_rhs, positions, polar, grid_base, tile_lists):
    rows_count = lax.axis_size("row")
    cols_count = lax.axis_size("col")
    grid_x = CX * rows_count
    grid_y = CY * cols_count
    atom_count = polar.shape[-1]
    tile_count = atom_count // TILE
    slab_depth = KZ // tile_count
    window_len = slab_depth + 4
    box_spans = (float(grid_x), float(grid_y), float(KZ))
    own_place = positions[0, 0]
    own_base = grid_base[0, 0]
    own_polar = polar[0, 0]
    lengths = jnp.array([grid_x, grid_y, KZ], dtype=jnp.int32)[:, None]
    cell_index = (own_base + 2) % lengths
    fraction = own_place - cell_index.astype(jnp.float32)
    values, slopes = spline_table(fraction)
    first_x = (own_base[0] - lax.axis_index("row") * CX + 2) % grid_x
    first_y = (own_base[1] - lax.axis_index("col") * CY + 2) % grid_y
    rows_x = placed_table(first_x, values[:, 0], CX + 4)
    slope_x = placed_table(first_x, slopes[:, 0], CX + 4)
    rows_y = placed_table(first_y, values[:, 1], CY + 4)
    slope_y = placed_table(first_y, slopes[:, 1], CY + 4)
    tile_start = jnp.arange(atom_count, dtype=jnp.int32) // TILE * slab_depth
    first_z = (own_base[2] + 2 - tile_start) % KZ
    rows_z = placed_table(first_z, values[:, 2], window_len)
    slope_z = placed_table(first_z, slopes[:, 2], window_len)
    plane_count = (CX + 4) * (CY + 4)
    plane_dx = (slope_x[:, None, :] * rows_y[None, :, :]).reshape(plane_count, atom_count)
    plane_dy = (rows_x[:, None, :] * slope_y[None, :, :]).reshape(plane_count, atom_count)
    plane_flat = (rows_x[:, None, :] * rows_y[None, :, :]).reshape(plane_count, atom_count)
    window_rows = jnp.moveaxis(rows_z.reshape(window_len, tile_count, TILE), 1, 0)
    window_slope = jnp.moveaxis(slope_z.reshape(window_len, tile_count, TILE), 1, 0)
    depth_table = jnp.concatenate([window_rows, window_slope], axis=2)
    grid_scale = 1.0 / (grid_x * grid_y * KZ)
    hartley_x = hartley(grid_x)
    hartley_y = hartley(grid_y)
    hartley_z = hartley(KZ)
    block_y = grid_y // rows_count
    block_z = KZ // cols_count
    wave_x = jnp.arange(grid_x, dtype=jnp.int32)[:, None, None]
    wave_y = (lax.axis_index("row") * block_y + jnp.arange(block_y, dtype=jnp.int32))[None, :, None]
    wave_z = (lax.axis_index("col") * block_z + jnp.arange(block_z, dtype=jnp.int32))[None, None, :]
    kernel = influence(wave_x, wave_y, wave_z, grid_x, grid_y, KZ) * grid_scale
    root_scale = jnp.power(own_polar, 1.0 / 6.0)
    own_static = jnp.concatenate([own_place, root_scale[None]], axis=0)
    near_static = with_halo(own_static[None, None], (("row", 0), ("col", 1)), 1)
    near_static = jnp.moveaxis(near_static.reshape(9, 4, tile_count, TILE), 2, 1).reshape(
        9 * tile_count, 4, TILE
    )
    own_tiles = jnp.moveaxis(own_static.reshape(4, tile_count, TILE), 1, 0)
    own_lists = tile_lists[0, 0]
    polar_wide = own_polar[None, None, :]
    solution = jnp.zeros_like(field_rhs[0, 0])
    residual = field_rhs[0, 0]
    scaled_res = polar_wide * residual
    direction = scaled_res
    progress = inner_sum(residual, scaled_res)
    for iteration in range(ITERS):
        near_dip = with_halo(direction[None, None], (("row", 0), ("col", 1)), 1)
        near_dip = jnp.moveaxis(near_dip.reshape(9, RHS, 3, tile_count, TILE), 3, 1).reshape(
            9 * tile_count, RHS, 3, TILE
        )

        def one_tile(tile_pos):
            picked = own_lists[tile_pos]
            return tile_field(own_tiles[tile_pos], near_static[picked], near_dip[picked], box_spans)

        fields = lax.map(one_tile, jnp.arange(tile_count, dtype=jnp.int32))
        direct = jnp.moveaxis(fields, 0, 2).reshape(RHS, 3, atom_count)
        slope_terms = (
            direction[:, 0, None, :] * plane_dx[None] + direction[:, 1, None, :] * plane_dy[None]
        )
        flat_terms = direction[:, 2, None, :] * plane_flat[None]
        spread_left = jnp.concatenate(
            [
                slope_terms.reshape(RHS, plane_count, tile_count, TILE),
                flat_terms.reshape(RHS, plane_count, tile_count, TILE),
            ],
            axis=3,
        )
        spread_windows = jnp.einsum("sptb,twb->sptw", spread_left, depth_table, precision=highest)
        main_part = spread_windows[..., :slab_depth].reshape(spread_windows.shape[:-2] + (KZ,))
        tail_part = pad_axis(
            spread_windows[..., slab_depth:], spread_windows.ndim - 1, 0, slab_depth - 4
        )
        tail_part = tail_part.reshape(spread_windows.shape[:-2] + (KZ,))[..., : KZ + 4 - slab_depth]
        last_axis = main_part.ndim - 1
        padded_line = pad_axis(main_part, last_axis, 0, 4) + pad_axis(
            tail_part, last_axis, slab_depth, 0
        )
        inner = padded_line[..., 2 : KZ + 2]
        spread_tile = (
            inner
            + pad_axis(padded_line[..., 0:2], last_axis, KZ - 2, 0)
            + pad_axis(padded_line[..., KZ + 2 : KZ + 4], last_axis, 0, KZ - 2)
        ).reshape(RHS, CX + 4, CY + 4, KZ)
        extended = with_halo(spread_tile, (("row", 1), ("col", 2)), 2)
        cycle_only = clear_inside(extended, ((1, CX), (2, CY)))
        folded = fold_cycle(fold_cycle(cycle_only, 1, CX), 2, CY)
        spectrum = jnp.einsum(
            "sxyz,zk->sxyk",
            spread_tile[:, 2 : CX + 2, 2 : CY + 2] + folded,
            hartley_z,
            precision=highest,
        )
        along_y = jnp.einsum(
            "sxyz,yk->sxkz",
            lax.all_to_all(spectrum, "col", split_axis=3, concat_axis=2, tiled=True),
            hartley_y,
            precision=highest,
        )
        along_x = (
            jnp.einsum(
                "sxyz,xk->skyz",
                lax.all_to_all(along_y, "row", split_axis=2, concat_axis=1, tiled=True),
                hartley_x,
                precision=highest,
            )
            * kernel[None]
        )
        mixed_part = jnp.einsum("sxyz,xk->skyz", along_x, hartley_x, precision=highest)
        returned = lax.all_to_all(mixed_part, "row", split_axis=1, concat_axis=2, tiled=True)
        swapped = jnp.einsum("sxyz,yk->sxkz", returned, hartley_y, precision=highest)
        restored = lax.all_to_all(swapped, "col", split_axis=2, concat_axis=3, tiled=True)
        padded = with_halo(
            jnp.einsum("sxyz,zk->sxyk", restored, hartley_z, precision=highest),
            (("row", 1), ("col", 2)),
            2,
        )
        line = padded.reshape(RHS, plane_count, KZ)
        extended_line = jnp.concatenate([line[..., KZ - 2 :], line, line[..., :2]], axis=-1)
        windows = jnp.stack(
            [
                extended_line[..., tile * slab_depth : tile * slab_depth + window_len]
                for tile in range(tile_count)
            ],
            axis=-2,
        )
        sampled = jnp.einsum("sptw,twb->sptb", windows, depth_table, precision=highest)
        with_flat = sampled[..., :TILE].reshape(RHS, plane_count, atom_count)
        with_slope = sampled[..., TILE:].reshape(RHS, plane_count, atom_count)
        recip_part = jnp.stack(
            [
                jnp.sum(with_flat * plane_dx[None], axis=1),
                jnp.sum(with_flat * plane_dy[None], axis=1),
                jnp.sum(with_slope * plane_flat[None], axis=1),
            ],
            axis=1,
        )
        image_field = direction / polar_wide - direct + recip_part - self_coef * direction
        step_size = (progress / inner_sum(direction, image_field))[:, None, None]
        solution = solution + step_size * direction
        residual = residual - step_size * image_field
        scaled_res = polar_wide * residual
        progress_next = inner_sum(residual, scaled_res)
        direction = scaled_res + (progress_next / progress)[:, None, None] * direction
        progress = progress_next
    return (solution[None, None], residual[None, None])


X_PAD = CX + 4
Y_PAD = CY + 4
SLOT_ROWS = 16
SPLIT = 2
VMEM_LIMIT = 60_000_000
SMALL_VMEM_LIMIT = 24_000_000
MIDDLE_VMEM_LIMIT = 56_000_000
ROOMY_BYTES = 12 << 20
EARLY_TILES = 1
PAIR_ROWS = 32
GROUP = 8
SCREEN_SCALE = 0.4
SCREEN_COEF = (
    0.22567588090896606,
    0.2256690263748169,
    0.20785020291805267,
    0.16849851608276367,
    0.14156343042850494,
    -0.005832736846059561,
    0.16930203139781952,
    -0.1830107867717743,
    0.05028456076979637,
)


def halves(value):
    high = value.astype(jnp.bfloat16)
    return high, (value - high.astype(jnp.float32)).astype(jnp.bfloat16)


def halves_np(value):
    value = value.astype(np.float32)
    high = value.astype(ml_dtypes.bfloat16)
    return high, (value - high.astype(np.float32)).astype(ml_dtypes.bfloat16)


def product(left, right, left_dim=1, right_dim=0):
    def one(first, second):
        return lax.dot_general(
            first,
            second,
            (((left_dim,), (right_dim,)), ((), ())),
            preferred_element_type=jnp.float32,
        )

    return one(left[0], right[0]) + (one(left[1], right[0]) + one(left[0], right[1]))


def cas_np(wave, place, length):
    angles = 2.0 * np.pi / length * (wave[:, None] * place[None, :] % length)
    return np.cos(angles) + np.sin(angles)


def modulus_np(wave, length):
    coef = np.array([1.0, 11.0, 11.0, 1.0]) / 24.0
    angles = 2.0 * np.pi / length * (wave[:, None] * np.arange(4)[None, :])
    return (coef * np.cos(angles)).sum(1) ** 2 + (coef * np.sin(angles)).sum(1) ** 2


def influence_np(length_x, length_y, length_z):
    total = np.zeros((length_x, length_y, length_z))
    modulus = np.ones((length_x, length_y, length_z))
    excluded = np.zeros((length_x, length_y, length_z), bool)
    for axis, length in enumerate((length_x, length_y, length_z)):
        wave = np.arange(length)
        shape = [1, 1, 1]
        shape[axis] = length
        total = total + ((np.minimum(wave, length - wave) / length) ** 2).reshape(shape)
        modulus = modulus * modulus_np(wave, length).reshape(shape)
        excluded = excluded | (wave * 2 == length).reshape(shape)
    excluded[0, 0, 0] = True
    safe = np.where(excluded, 1.0, total)
    result = np.exp(-(np.pi**2) / ewald_beta**2 * safe) / (
        np.pi * safe * np.where(excluded, 1.0, modulus)
    )
    return np.where(excluded, 0.0, result) / (length_x * length_y * length_z)


def slab_tables(rows_count, cols_count):
    grid_x = CX * rows_count
    grid_y = CY * cols_count
    devices = rows_count * cols_count
    chunk = KZ // devices
    wave_z = (np.arange(devices)[None, :] * chunk + np.arange(chunk)[:, None]).reshape(-1)
    along_z = cas_np(wave_z, np.arange(KZ), KZ)
    place_x = np.arange(rows_count)[:, None] * CX + np.arange(X_PAD)[None, :] - 2
    along_x = cas_np(np.arange(grid_x), place_x.reshape(-1) % grid_x, grid_x)
    x_high, x_low = halves_np(along_x)
    forward_x = np.concatenate([x_high, x_low, x_high], axis=1)
    backward_x = np.concatenate([x_high.T, x_low.T, x_high.T], axis=1)
    place_y = (np.arange(cols_count)[:, None] * CY + np.arange(Y_PAD)[None, :] - 2) % grid_y
    along_y = cas_np(np.arange(grid_y), place_y.reshape(-1), grid_y)
    along_y = along_y.reshape(grid_y, cols_count, Y_PAD)
    units = chunk * RHS // SPLIT
    block = np.einsum("uv,kcy->cuyvk", np.eye(units), along_y)
    block = block.reshape(cols_count * units * Y_PAD, units * grid_y)
    kernel = influence_np(grid_x, grid_y, KZ).reshape(grid_x, grid_y, devices, chunk)
    kernel = np.transpose(kernel, (2, 0, 3, 1))[:, :, :, None, :]
    kernel = np.broadcast_to(kernel, (devices, grid_x, chunk, RHS, grid_y))
    kernel = kernel.reshape(devices, grid_x, SPLIT, units * grid_y)
    kernel = np.moveaxis(kernel, 2, 1).reshape(devices, SPLIT * grid_x, units * grid_y)
    kernel = kernel.astype(np.float32)
    return dict(
        along_z=halves_np(along_z),
        forward_x=forward_x,
        backward_x=backward_x,
        block=halves_np(block),
        kernel=kernel,
    )


def pack_body(rhs_ref, place_ref, polar_ref, start_ref, payload_ref):
    polar = polar_ref[...]
    start = read_rows(rhs_ref) * polar
    start_ref[...] = start
    place = [place_ref[dim] for dim in range(3)]
    everything = jnp.concatenate(place + [1.0 / jnp.sqrt(polar), start], axis=0)
    store_payload(payload_ref, everything)


def read_rows(rows_ref):
    return jnp.concatenate([rows_ref[dim] for dim in range(3)], axis=0)


def store_payload(payload_ref, everything):
    tile_count = everything.shape[1] // TILE
    for quantity in range(everything.shape[0]):
        for tile in range(tile_count):
            row = quantity * tile_count + tile
            payload_ref[row : row + 1, :] = everything[
                quantity : quantity + 1, tile * TILE : (tile + 1) * TILE
            ]


def placed_rows(slot, weights, extent):
    slot_index = lax.broadcasted_iota(jnp.int32, (extent, slot.shape[1]), 0)
    placed = jnp.zeros((extent, slot.shape[1]), jnp.float32)
    for stencil in range(5):
        target = slot + stencil
        if extent == KZ:
            target = jnp.where(target >= KZ, target - KZ, target)
        placed = placed + jnp.where(slot_index == target, weights[stencil], 0.0)
    return placed


def spread_into(message_ref, moment, rows_x, slope_x, rows_y, slope_y, depth, devices):
    blocks = []
    for step in range(X_PAD):
        flat_x = rows_x[step : step + 1]
        tilt_x = slope_x[step : step + 1]
        for rhs in range(RHS):
            part_x = tilt_x * moment[rhs : rhs + 1]
            part_y = flat_x * moment[RHS + rhs : RHS + rhs + 1]
            part_z = flat_x * moment[2 * RHS + rhs : 2 * RHS + rhs + 1]
            blocks.append(
                jnp.concatenate([part_x * rows_y + part_y * slope_y, part_z * rows_y], axis=1)
            )
    charges = jnp.concatenate(blocks, axis=0)
    spectrum = product(depth, halves(charges), 1, 1)
    slot_rows = message_ref.shape[0] // devices
    chunk = KZ // devices
    width = RHS * Y_PAD
    for step in range(X_PAD):
        message_ref[pl.ds(step, devices, stride=slot_rows), :] = jnp.concatenate(
            [
                spectrum[unit * devices : (unit + 1) * devices, step * width : (step + 1) * width]
                for unit in range(chunk)
            ],
            axis=1,
        )


def sample_from(message_ref, rows_x, slope_x, rows_y, slope_y, depth, devices):
    chunk = KZ // devices
    width = RHS * Y_PAD
    slot_rows = message_ref.shape[0] // devices
    pieces = [
        message_ref[pl.ds(step, devices, stride=slot_rows), :] for step in range(X_PAD)
    ]
    spare = jnp.zeros((devices, KZ - X_PAD * width), jnp.float32)
    spectrum = jnp.concatenate(
        [
            jnp.concatenate(
                [piece[:, unit * width : (unit + 1) * width] for piece in pieces] + [spare], axis=1
            )
            for unit in range(chunk)
        ],
        axis=0,
    )
    spectrum = jnp.transpose(spectrum)[: X_PAD * width]
    sampled = product(halves(spectrum), depth, 1, 0)
    atoms = rows_x.shape[1]
    fields = [None] * (3 * RHS)
    for rhs in range(RHS):
        sum_x = sum_y = sum_z = None
        for step in range(X_PAD):
            first = step * width + rhs * Y_PAD
            flat = sampled[first : first + Y_PAD, :atoms]
            tilt = sampled[first : first + Y_PAD, atoms:]
            part_x = slope_x[step : step + 1] * flat
            part_y = rows_x[step : step + 1] * flat
            part_z = rows_x[step : step + 1] * tilt
            sum_x = part_x if sum_x is None else sum_x + part_x
            sum_y = part_y if sum_y is None else sum_y + part_y
            sum_z = part_z if sum_z is None else sum_z + part_z
        fields[rhs] = jnp.sum(sum_x * rows_y, axis=0, keepdims=True)
        fields[RHS + rhs] = jnp.sum(sum_y * slope_y, axis=0, keepdims=True)
        fields[2 * RHS + rhs] = jnp.sum(sum_z * rows_y, axis=0, keepdims=True)
    return jnp.concatenate(fields, axis=0)


def read_tables(tables_ref):
    return (
        tables_ref[0:X_PAD],
        tables_ref[SLOT_ROWS : SLOT_ROWS + X_PAD],
        tables_ref[2 * SLOT_ROWS : 2 * SLOT_ROWS + Y_PAD],
        tables_ref[2 * SLOT_ROWS + Y_PAD : 2 * SLOT_ROWS + 2 * Y_PAD],
    )


def setup_body(
    lengths,
    devices,
    place_ref,
    base_ref,
    start_ref,
    z_high_ref,
    z_low_ref,
    message_ref,
    tables_ref,
    depth_high_ref,
    depth_low_ref,
    send_tables,
):
    base = [base_ref[dim] for dim in range(3)]
    fractions = []
    cells = []
    for dim in range(3):
        cell = base[dim] + 2
        cell = jnp.where(cell >= lengths[dim], cell - lengths[dim], cell)
        cells.append(cell)
        fractions.append(place_ref[dim] - cell.astype(jnp.float32))
    values, slopes = spline_table(jnp.concatenate(fractions, axis=0))
    values = [[values[stencil][dim : dim + 1] for stencil in range(5)] for dim in range(3)]
    slopes = [[slopes[stencil][dim : dim + 1] for stencil in range(5)] for dim in range(3)]
    slot_x = lax.rem(cells[0], CX)
    slot_y = lax.rem(cells[1], CY)
    tables_ref[0:SLOT_ROWS] = placed_rows(slot_x, values[0], SLOT_ROWS)
    tables_ref[SLOT_ROWS : 2 * SLOT_ROWS] = placed_rows(slot_x, slopes[0], SLOT_ROWS)
    tables_ref[2 * SLOT_ROWS : 2 * SLOT_ROWS + Y_PAD] = placed_rows(slot_y, values[1], Y_PAD)
    tables_ref[2 * SLOT_ROWS + Y_PAD : 2 * SLOT_ROWS + 2 * Y_PAD] = placed_rows(
        slot_y, slopes[1], Y_PAD
    )
    window = jnp.concatenate(
        [
            placed_rows(base[2], values[2], KZ),
            placed_rows(base[2], slopes[2], KZ),
        ],
        axis=1,
    )
    depth = product((z_high_ref[...], z_low_ref[...]), halves(window), 1, 0)
    depth = halves(depth)
    depth_high_ref[...] = depth[0]
    depth_low_ref[...] = depth[1]
    send_tables()
    spread_into(message_ref, start_ref[...], *read_tables(tables_ref), depth, devices)


def transform_in(message_ref, forward_ref, block_high_ref, block_low_ref, rows_count, cols_count):
    gathered = jnp.concatenate(
        [
            jnp.concatenate(
                [
                    message_ref[(r * cols_count + c) * X_PAD : (r * cols_count + c + 1) * X_PAD]
                    for r in range(rows_count)
                ],
                axis=0,
            )
            for c in range(cols_count)
        ],
        axis=1,
    )
    high, low = halves(gathered)
    along = jnp.dot(
        forward_ref[...],
        jnp.concatenate([high, high, low], axis=0),
        preferred_element_type=jnp.float32,
    )
    part = along.shape[1] // cols_count // SPLIT
    along = jnp.concatenate(
        [
            jnp.concatenate(
                [
                    along[:, (c * SPLIT + half) * part : (c * SPLIT + half + 1) * part]
                    for c in range(cols_count)
                ],
                axis=1,
            )
            for half in range(SPLIT)
        ],
        axis=0,
    )
    return product(halves(along), (block_high_ref[...], block_low_ref[...]))


def transform_out(result_ref, values, backward_ref, block_high_ref, block_low_ref, counts):
    rows_count, cols_count = counts
    spread = product(halves(values), (block_high_ref[...], block_low_ref[...]), 1, 1)
    grid_x = spread.shape[0] // SPLIT
    part = spread.shape[1] // cols_count
    spread = jnp.concatenate(
        [
            spread[half * grid_x : (half + 1) * grid_x, c * part : (c + 1) * part]
            for c in range(cols_count)
            for half in range(SPLIT)
        ],
        axis=1,
    )
    high, low = halves(spread)
    along = jnp.dot(
        backward_ref[...],
        jnp.concatenate([high, high, low], axis=0),
        preferred_element_type=jnp.float32,
    )
    width = along.shape[1] // cols_count
    slot_rows = result_ref.shape[0] // (rows_count * cols_count)
    for r in range(rows_count):
        for c in range(cols_count):
            first = (r * cols_count + c) * slot_rows
            result_ref[first : first + X_PAD, :] = along[
                r * X_PAD : (r + 1) * X_PAD, c * width : (c + 1) * width
            ]


def middle_first_body(
    counts,
    message_ref,
    kernel_ref,
    forward_ref,
    backward_ref,
    block_high_ref,
    block_low_ref,
    result_ref,
    wave_ref,
):
    wave = transform_in(message_ref, forward_ref, block_high_ref, block_low_ref, *counts)
    wave_ref[...] = wave
    transform_out(
        result_ref, wave * kernel_ref[...], backward_ref, block_high_ref, block_low_ref, counts
    )


def gather_rows(parts):
    tiles = [
        parts[GROUP * tile : GROUP * tile + GROUP, :] for tile in range(parts.shape[0] // GROUP)
    ]
    return jnp.concatenate(tiles, axis=1)[0 : 3 * RHS]


def row_total(value, rhs):
    row = lax.broadcasted_iota(jnp.int32, value.shape, 0)
    return total(jnp.where(lax.rem(row, RHS) == rhs, value, 0.0))


def total(value):
    return jnp.sum(jnp.sum(value, axis=0, keepdims=True), axis=1, keepdims=True)


def middle_second_body(
    counts,
    message_ref,
    kernel_ref,
    forward_ref,
    backward_ref,
    block_high_ref,
    block_low_ref,
    wave_ref,
    start_ref,
    carried_ref,
    near_ref,
    polar_ref,
    result_ref,
    local_ref,
):
    near_rows = gather_rows(near_ref)
    wave = transform_in(message_ref, forward_ref, block_high_ref, block_low_ref, *counts)
    filtered = wave * kernel_ref[...]
    transform_out(result_ref, filtered, backward_ref, block_high_ref, block_low_ref, counts)
    before = wave_ref[...]
    grid_y = CY * counts[1]
    lane = lax.broadcasted_iota(jnp.int32, wave.shape, 1)
    own_rhs = lax.rem(lax.div(lane, grid_y), RHS)
    image = carried_ref[0 : 3 * RHS]
    second = carried_ref[8 : 8 + 3 * RHS]
    start = start_ref[...]
    local_part = second / polar_ref[...] - near_rows - self_coef * second
    local_ref[0 : 3 * RHS] = image
    local_ref[8 : 8 + 3 * RHS] = second
    local_ref[16 : 16 + 3 * RHS] = local_part
    local_ref[24 : 24 + 3 * RHS] = start
    slot = lax.broadcasted_iota(jnp.int32, (1, result_ref.shape[1]), 1)
    sums = jnp.zeros((1, result_ref.shape[1]), jnp.float32)
    for rhs in range(RHS):
        mine = own_rhs == rhs
        parts = (
            row_total(start * start / polar_ref[...], rhs),
            row_total(start * image, rhs),
            row_total(second * image, rhs),
            row_total(start * local_part, rhs) + total(jnp.where(mine, before * filtered, 0.0)),
            row_total(second * local_part, rhs) + total(jnp.where(mine, wave * filtered, 0.0)),
        )
        for index, part in enumerate(parts):
            sums = jnp.where(slot == rhs * len(parts) + index, part, sums)
    devices = counts[0] * counts[1]
    result_ref[pl.ds(X_PAD, devices, stride=X_PAD + 1), :] = jnp.broadcast_to(
        sums, (devices, sums.shape[1])
    )


def sample_body(
    devices,
    message_ref,
    tables_ref,
    depth_high_ref,
    depth_low_ref,
    start_ref,
    near_ref,
    polar_ref,
    carried_ref,
    payload_ref,
):
    tables = read_tables(tables_ref)
    depth = (depth_high_ref[...], depth_low_ref[...])
    field = sample_from(message_ref, *tables, depth, devices)
    start = start_ref[...]
    polar = polar_ref[...]
    image = start / polar - gather_rows(near_ref) + field - self_coef * start
    second = polar * image
    carried_ref[0 : 3 * RHS] = image
    carried_ref[8 : 8 + 3 * RHS] = second
    store_payload(payload_ref, second)


def spread_body(
    devices,
    tables_ref,
    depth_high_ref,
    depth_low_ref,
    carried_ref,
    result_ref,
):
    depth = (depth_high_ref[...], depth_low_ref[...])
    second = carried_ref[8 : 8 + 3 * RHS]
    spread_into(result_ref, second, *read_tables(tables_ref), depth, devices)


def final_body(
    devices,
    message_ref,
    tables_ref,
    depth_high_ref,
    depth_low_ref,
    rhs_ref,
    local_ref,
    dipole_ref,
    residual_ref,
):
    tables = read_tables(tables_ref)
    depth = (depth_high_ref[...], depth_low_ref[...])
    field = sample_from(message_ref, *tables, depth, devices)
    image = local_ref[0 : 3 * RHS]
    second = local_ref[8 : 8 + 3 * RHS]
    image_second = local_ref[16 : 16 + 3 * RHS] + field
    start = local_ref[24 : 24 + 3 * RHS]
    sums = jnp.sum(
        message_ref[pl.ds(X_PAD, devices, stride=X_PAD + 1), :], axis=0, keepdims=True
    )
    steps = []
    for rhs in range(RHS):
        progress, start_image, second_image, start_next, second_next = [
            sums[:, rhs * 5 + index : rhs * 5 + index + 1] for index in range(5)
        ]
        step = progress / start_image
        progress_next = progress - 2.0 * step * start_image + step * step * second_image
        grown = 1.0 + progress_next / progress
        curvature = (
            grown * grown * start_image
            - step * grown * (start_next + second_image)
            + step * step * second_next
        )
        steps.append((step, grown, progress_next / curvature))
    row = lax.broadcasted_iota(jnp.int32, (RHS, 1), 0)
    step, grown, step_next = [
        sum(jnp.where(row == rhs, steps[rhs][index], 0.0) for rhs in range(RHS))
        for index in range(3)
    ]
    for dim in range(3):
        rows = slice(dim * RHS, (dim + 1) * RHS)
        direction = grown * start[rows] - step * second[rows]
        image_direction = grown * image[rows] - step * image_second[rows]
        dipole_ref[dim] = step * start[rows] + step_next * direction
        residual_ref[dim] = rhs_ref[dim] - step * image[rows] - step_next * image_direction


def near_base(entry, brick_rows):
    return lax.shift_right_logical(entry, 2) * brick_rows + lax.bitwise_and(entry, 3)


def nearest(places, origin, span):
    return places - span * jnp.floor((places - origin) * (1.0 / span) + 0.5)


def unwrap_near(near, tile_count, spans):
    rows = near.shape[0] // 9
    for dim in range(2):
        own = 4 * rows + dim * tile_count
        origin = near[own : own + 1, 0:1]
        for brick in range(9):
            first = brick * rows + dim * tile_count
            near[first : first + tile_count, :] = nearest(
                near[first : first + tile_count, :], origin, spans[dim]
            )


def pick_rows(picked, near, lists_ref, tile, place, tile_count, quantities, origin, span):
    rows = near.shape[0] // 9
    place = place * lists_ref.shape[1] * quantities * GROUP
    for entry in range(lists_ref.shape[1]):
        base = near_base(lists_ref[tile, entry], rows)
        for quantity in range(quantities):
            values = near[pl.ds(base + quantity * tile_count, 1), :]
            if quantity == 2 and span is not None:
                values = nearest(values, origin, span)
            first = place + (entry * quantities + quantity) * GROUP
            picked[first : first + GROUP, :] = jnp.broadcast_to(values, (GROUP, TILE))


def widen_own(near, quantities, tile_count, tile, place, wide):
    offset = near.shape[0] // 9 * 4
    rows = [
        near[offset + quantity * tile_count + tile : offset + quantity * tile_count + tile + 1, :]
        for quantity in range(quantities)
    ]
    spare = jnp.zeros((TILE - quantities, TILE), jnp.float32)
    columns = jnp.transpose(jnp.concatenate(rows + [spare], axis=0))
    for quantity in range(quantities):
        first = (place * quantities + quantity) * TILE
        wide[first : first + TILE, :] = jnp.broadcast_to(
            columns[:, quantity : quantity + 1], (TILE, TILE)
        )


def add_field(sums, first_term, second_term, apart, moments):
    for rhs in range(RHS):
        moment = [moments[RHS * dim + rhs] for dim in range(3)]
        projected = moment[0] * apart[0] + moment[1] * apart[1] + moment[2] * apart[2]
        weighted = second_term * projected
        for dim in range(3):
            index = RHS * dim + rhs
            sums[index] = sums[index] + (weighted * apart[dim] - first_term * moment[dim])


def finish_sums(field_ref, sums_ref, first_tile, place):
    place = place * 3 * RHS
    lane = lax.broadcasted_iota(jnp.int32, (TILE, TILE), 1)
    merged = jnp.zeros((TILE, TILE), jnp.float32)
    for index in range(3 * RHS):
        first = (place + index) * TILE
        column = jnp.sum(sums_ref[first : first + TILE, :], axis=1, keepdims=True)
        merged = jnp.where(lane == index, column, merged)
    first = (first_tile + place // (3 * RHS)) * GROUP
    field_ref[first : first + GROUP, :] = jnp.transpose(merged)[0:GROUP]


def pair_rows(start, group):
    return pl.ds(pl.multiple_of(start + group * GROUP, GROUP), GROUP)


def wide_rows(start, group, quantity):
    return pl.ds(pl.multiple_of(quantity * TILE + start + group * GROUP, GROUP), GROUP)


def pair_terms(square_dist, damp):
    inverse = lax.rsqrt(square_dist)
    distance = square_dist * inverse
    inverse_sq = inverse * inverse
    inverse_cube = inverse_sq * inverse
    cubed = damp * (distance * square_dist)
    damping = jnp.exp(cubed)
    bell = jnp.exp(-(ewald_beta * ewald_beta) * square_dist)
    stretched = 1.0 + (SCREEN_SCALE * ewald_beta) * distance
    turned = pl.reciprocal(stretched, approx=True)
    turned = turned * (2.0 - stretched * turned)
    series = SCREEN_COEF[-1] * turned + SCREEN_COEF[-2]
    for coef in SCREEN_COEF[-3::-1]:
        series = series * turned + coef
    screen = bell * turned * series
    gaussian = (2.0 * ewald_beta / math.sqrt(math.pi)) * bell
    bare = screen - damping
    first_term = bare * inverse_cube + gaussian * inverse_sq
    second_term = (
        3.0 * (first_term + (cubed * damping) * inverse_cube)
        + (2.0 * ewald_beta * ewald_beta) * gaussian
    ) * inverse_sq
    return first_term, second_term


def step_rows(step, size, offset):
    return pl.ds(pl.multiple_of(step * size + offset, GROUP), GROUP)


def tile_rows(step, rows):
    return pl.ds(pl.multiple_of(step * rows, GROUP), rows)


def start_all(copies):
    for copy in copies:
        copy.start()


def wait_all(copies):
    for copy in copies:
        copy.wait()


def near_copies(sources, near, semaphore):
    rows = sources[0].shape[0]
    return [
        pltpu.make_async_copy(
            source, near.at[index * rows : (index + 1) * rows, :], semaphore.at[index]
        )
        for index, source in enumerate(sources)
    ]


def term_copies(terms, buffers, semaphore, begin, step, size, inward):
    rows = pl.ds(pl.multiple_of((begin + step) * size, GROUP), size)
    place = pl.ds(pl.multiple_of(step * size, GROUP), size)
    copies = []
    for index in range(2):
        far, here = terms[index].at[rows, :], buffers[index].at[place, :]
        ends = (far, here) if inward else (here, far)
        copies.append(pltpu.make_async_copy(*ends, semaphore.at[index, step]))
    return copies


def pair_first_body(
    first_tile,
    last_tile,
    tile_count,
    spans,
    lists_ref,
    up_ref,
    stack_ref,
    down_ref,
    *others,
):
    first_ref, second_ref, field_ref, near_ref = others[-14:-10]
    near, picked, wide, sums_ref, kept, field, first_buffer, second_buffer, semaphore, busy = others[-10:]
    terms = (first_ref, second_ref)
    buffers = (first_buffer, second_buffer)
    copies = near_copies((up_ref, stack_ref, down_ref), near, semaphore.at[0])
    if first_tile > 0:
        copies.append(
            pltpu.make_async_copy(
                others[0], field.at[0 : first_tile * GROUP, :], semaphore.at[0, 3]
            )
        )
    start_all(copies)
    wait_all(copies)
    entries = lists_ref.shape[1]
    rows = near.shape[0] // 9
    quantities = rows // tile_count
    unwrap_near(near, tile_count, spans)
    for brick in range(9):
        kept[brick * 3 * tile_count : (brick + 1) * 3 * tile_count, :] = near[
            brick * rows : brick * rows + 3 * tile_count, :
        ]
    keep = pltpu.make_async_copy(kept, near_ref, semaphore.at[1, 3])
    keep.start()
    for place, tile in enumerate(range(first_tile, last_tile)):
        widen_own(near, 4, tile_count, tile, place, wide)
        own = rows * 4 + 2 * tile_count + tile
        origin = near[own : own + 1, 0:1]
        pick_rows(picked, near, lists_ref, tile, place, tile_count, quantities, origin, spans[2])
    parts = TILE // PAIR_ROWS
    steps = (last_tile - first_tile) * parts

    size = entries * PAIR_ROWS

    def sent(step):
        return term_copies(terms, buffers, busy, first_tile * parts, step, size, False)

    @pl.loop(0, steps)
    def _(step):
        tile = lax.div(step, parts)
        start = lax.rem(step, parts) * PAIR_ROWS
        step_picked = picked.at[tile_rows(tile, entries * quantities * GROUP), :]
        step_wide = wide.at[tile_rows(tile, 4 * TILE), :]
        step_sums = sums_ref.at[tile_rows(tile, 3 * RHS * TILE), :]
        for group in range(PAIR_ROWS // GROUP):
            own = [step_wide[wide_rows(start, group, dim), :] for dim in range(4)]
            own_damp = -thole_a * own[3]
            sums = [jnp.zeros((GROUP, TILE), jnp.float32) for _ in range(3 * RHS)]
            itself = (
                lax.broadcasted_iota(jnp.int32, (GROUP, TILE), 0) + (start + group * GROUP)
            ) == lax.broadcasted_iota(jnp.int32, (GROUP, TILE), 1)
            for entry in range(entries):
                first = entry * quantities * GROUP
                rows = [
                    step_picked[first + quantity * GROUP : first + (quantity + 1) * GROUP, :]
                    for quantity in range(quantities)
                ]
                apart = [rows[dim] - own[dim] for dim in range(3)]
                square_dist = apart[0] * apart[0] + apart[1] * apart[1] + apart[2] * apart[2]
                if entry == 0:
                    square_dist = jnp.where(itself, 1.0, square_dist)
                first_term, second_term = pair_terms(square_dist, own_damp * rows[3])
                if entry == 0:
                    first_term = jnp.where(itself, 0.0, first_term)
                    second_term = jnp.where(itself, 0.0, second_term)
                place = step_rows(step, size, entry * PAIR_ROWS + group * GROUP)
                first_buffer[place, :] = first_term
                second_buffer[place, :] = second_term
                add_field(sums, first_term, second_term, apart, rows[4:])
            for index, value in enumerate(sums):
                step_sums[wide_rows(start, group, index), :] = value
        start_all(sent(step))

    for place in range(last_tile - first_tile):
        finish_sums(field, sums_ref, first_tile, place)
    result = pltpu.make_async_copy(field, head_of(field_ref, field), semaphore.at[1, 2])
    result.start()

    @pl.loop(0, steps)
    def _(step):
        wait_all(sent(step))

    keep.wait()
    result.wait()


def pair_second_body(
    tile_count,
    spans,
    lists_ref,
    near_ref,
    up_ref,
    stack_ref,
    down_ref,
    first_ref,
    second_ref,
    field_ref,
    near,
    near_moment,
    picked,
    picked_moment,
    wide,
    sums_ref,
    field,
    first_buffer,
    second_buffer,
    semaphore,
    busy,
):
    terms = (first_ref, second_ref)
    buffers = (first_buffer, second_buffer)
    parts = TILE // PAIR_ROWS
    steps = tile_count * parts

    entries = lists_ref.shape[1]
    size = entries * PAIR_ROWS

    def fetched(step):
        return term_copies(terms, buffers, busy, 0, step, size, True)

    places = pltpu.make_async_copy(near_ref, near, semaphore.at[1, 3])
    places.start()
    copies = near_copies((up_ref, stack_ref, down_ref), near_moment, semaphore.at[2])
    start_all(copies)

    @pl.loop(0, steps)
    def _(step):
        start_all(fetched(step))

    places.wait()
    for tile in range(tile_count):
        widen_own(near, 3, tile_count, tile, tile, wide)
        own = near.shape[0] // 9 * 4 + 2 * tile_count + tile
        origin = near[own : own + 1, 0:1]
        pick_rows(picked, near, lists_ref, tile, tile, tile_count, 3, origin, spans[2])
    wait_all(copies)
    for tile in range(tile_count):
        pick_rows(
            picked_moment, near_moment, lists_ref, tile, tile, tile_count, 3 * RHS, None, None
        )

    @pl.loop(0, steps)
    def _(step):
        wait_all(fetched(step))
        tile = lax.div(step, parts)
        start = lax.rem(step, parts) * PAIR_ROWS
        step_picked = picked.at[tile_rows(tile, entries * 3 * GROUP), :]
        step_moment = picked_moment.at[tile_rows(tile, entries * 3 * RHS * GROUP), :]
        step_wide = wide.at[tile_rows(tile, 3 * TILE), :]
        step_sums = sums_ref.at[tile_rows(tile, 3 * RHS * TILE), :]
        for group in range(PAIR_ROWS // GROUP):
            own = [step_wide[wide_rows(start, group, dim), :] for dim in range(3)]
            sums = [jnp.zeros((GROUP, TILE), jnp.float32) for _ in range(3 * RHS)]
            for entry in range(entries):
                first = entry * 3 * GROUP
                apart = [
                    step_picked[first + dim * GROUP : first + (dim + 1) * GROUP, :] - own[dim]
                    for dim in range(3)
                ]
                first = first * RHS
                moments = [
                    step_moment[first + index * GROUP : first + (index + 1) * GROUP, :]
                    for index in range(3 * RHS)
                ]
                place = step_rows(step, size, entry * PAIR_ROWS + group * GROUP)
                add_field(sums, first_buffer[place, :], second_buffer[place, :], apart, moments)
            for index, value in enumerate(sums):
                step_sums[wide_rows(start, group, index), :] = value

    for place in range(tile_count):
        finish_sums(field, sums_ref, 0, place)
    result = pltpu.make_async_copy(field, head_of(field_ref, field), semaphore.at[1, 2])
    result.start()
    result.wait()


def shift(source, axis, step):
    count = lax.axis_size(axis)
    return lax.ppermute(source, axis, [(i, (i + step) % count) for i in range(count)])


def both_ways(source, axis):
    return shift(source, axis, 1), source, shift(source, axis, -1)


def whole(shape):
    return pl.BlockSpec(shape, lambda *_: (0,) * len(shape))


def anywhere():
    return pl.BlockSpec(memory_space=pl.ANY)


def join(message, payload):
    right = shift(payload, "col", -1)
    left = shift(payload, "col", 1)
    message, right, left = lax.optimization_barrier((message, right, left))
    return message, both_ways(jnp.concatenate([left, payload, right], axis=0), "row")


class Fetched:
    def __init__(self, source, scratch, semaphore):
        self.copy = pltpu.make_async_copy(source, scratch, semaphore)
        self.copy.start()
        self.scratch = scratch
        self.shape = scratch.shape
        self.waiting = True

    def wait(self):
        if self.waiting:
            self.copy.wait()
            self.waiting = False

    def __getitem__(self, index):
        self.wait()
        return self.scratch[index]


class Head:
    def __init__(self, array, shape):
        self.array = array
        self.shape = shape
        self.dtype = array.dtype


def roomy(shape):
    return (ROOMY_BYTES // 4 // shape[1], shape[1])


def head_of(far, here):
    if far.shape == here.shape:
        return far
    return far.at[0 : here.shape[0], :]


def call(body, outs, *operands, after=(), own_block=None, near=0, large=(), early=(), vmem=VMEM_LIMIT):
    count = len(operands)
    fetched = [
        pltpu.VMEM(operand.shape[1:] if index == own_block else operand.shape, operand.dtype)
        for index, operand in enumerate(operands)
        if index >= near
    ]
    arrays = [operand.array if isinstance(operand, Head) else operand for operand in operands]

    def run(*refs):
        refs = refs[len(after) :]
        sources, refs = refs[:count], refs[count:]
        results, refs = refs[: len(outs)], refs[len(outs) :]
        targets, written, semaphore = refs[: count - near], refs[count - near : -1], refs[-1]
        inputs = list(sources[:near])
        for index in range(near, count):
            source = sources[index]
            if index == own_block:
                place = lax.axis_index("row") * lax.axis_size("col") + lax.axis_index("col")
                source = source.at[place]
            else:
                source = head_of(source, targets[index - near])
            inputs.append(Fetched(source, targets[index - near], semaphore.at[index]))
        copies = [
            pltpu.make_async_copy(value, head_of(result, value), semaphore.at[count + index])
            for index, (value, result) in enumerate(zip(written, results))
        ]
        if early:
            body(*inputs, *written, lambda: start_all(copies[index] for index in early))
        else:
            body(*inputs, *written)
        for operand in inputs[near:]:
            operand.wait()
        start_all(copy for index, copy in enumerate(copies) if index not in early)
        for copy in copies:
            copy.wait()

    return pl.pallas_call(
        run,
        in_specs=[anywhere()] * len(after)
        + [pl.BlockSpec(memory_space=pltpu.VMEM)] * near
        + [anywhere()] * (count - near),
        out_specs=[anywhere()] * len(outs),
        out_shape=[
            jax.ShapeDtypeStruct(roomy(shape) if index in large else shape, dtype)
            for index, (shape, dtype) in enumerate(outs)
        ],
        scratch_shapes=fetched
        + [pltpu.VMEM(shape, dtype) for shape, dtype in outs]
        + [pltpu.SemaphoreType.DMA((count + len(outs),))],
        compiler_params=pltpu.CompilerParams(vmem_limit_bytes=vmem),
        cost_estimate=pl.CostEstimate(
            flops=200_000_000, bytes_accessed=4 << 20, transcendentals=0
        ),
    )(*after, *arrays)


def final_call(body, outs, *operands):
    return pl.pallas_call(
        body,
        grid=(1,),
        in_specs=[whole(operand.shape) for operand in operands],
        out_specs=[whole(shape) for shape, _ in outs],
        out_shape=[jax.ShapeDtypeStruct(shape, dtype) for shape, dtype in outs],
        compiler_params=pltpu.CompilerParams(vmem_limit_bytes=SMALL_VMEM_LIMIT),
    )(*operands)


def pair_call(body, outs, scratch, lists, *operands, tiles, large, aliased=0):
    buffers = (tiles * lists.shape[1] * TILE, TILE)
    first = 1 + len(operands) - aliased
    return pl.pallas_call(
        body,
        in_specs=[pl.BlockSpec(memory_space=pltpu.SMEM)] + [anywhere()] * len(operands),
        out_specs=[anywhere()] * len(outs),
        out_shape=[
            jax.ShapeDtypeStruct(roomy(shape) if index == large else shape, jnp.float32)
            for index, shape in enumerate(outs)
        ],
        scratch_shapes=[pltpu.VMEM(shape, jnp.float32) for shape in scratch + [buffers] * 2]
        + [
            pltpu.SemaphoreType.DMA((3, 4)),
            pltpu.SemaphoreType.DMA((2, tiles * TILE // PAIR_ROWS)),
        ],
        input_output_aliases={first + index: index for index in range(aliased)},
        compiler_params=pltpu.CompilerParams(vmem_limit_bytes=VMEM_LIMIT),
        cost_estimate=pl.CostEstimate(
            flops=80_000_000, bytes_accessed=8 << 20, transcendentals=1 << 21
        ),
    )(lists, *operands)


def exchange(message, devices):
    shape = message.shape
    sent = message.reshape(devices, 1, -1)
    return lax.all_to_all(sent, ("row", "col"), split_axis=0, concat_axis=0, tiled=True).reshape(
        shape
    )


def slab_local(field_rhs, positions, polar, grid_base, tile_lists):
    rows_count = lax.axis_size("row")
    cols_count = lax.axis_size("col")
    counts = (rows_count, cols_count)
    devices = rows_count * cols_count
    lengths = (CX * rows_count, CY * cols_count, KZ)
    spans = tuple(float(length) for length in lengths)
    atoms = polar.shape[-1]
    tile_count = atoms // TILE
    listed = tile_lists.shape[-1]
    tables = slab_tables(rows_count, cols_count)
    f32 = jnp.float32
    rhs = jnp.swapaxes(field_rhs[0, 0], 0, 1)
    place = jnp.swapaxes(positions[0], 0, 1)
    base = jnp.swapaxes(grid_base[0], 0, 1)
    polar = polar.reshape(1, atoms)
    lists = tile_lists[0, 0]
    quantities = 4 + 3 * RHS
    brick_rows = quantities * tile_count
    moment_rows = 3 * RHS * tile_count
    message_shape = (devices * X_PAD, KZ // devices * RHS * Y_PAD)
    last_shape = (devices * (X_PAD + 1), message_shape[1])
    row_shape = (3 * RHS, atoms)

    start, payload = call(pack_body, [(row_shape, f32), ((brick_rows, TILE), f32)], rhs, place, polar)

    def setup(*refs):
        setup_body(lengths, devices, *refs)

    message, splines, depth_high, depth_low = call(
        setup,
        [
            (message_shape, f32),
            ((2 * SLOT_ROWS + 2 * Y_PAD, atoms), f32),
            ((KZ, 2 * atoms), jnp.bfloat16),
            ((KZ, 2 * atoms), jnp.bfloat16),
        ],
        place,
        base,
        start,
        *[jnp.asarray(table) for table in tables["along_z"]],
        early=(1, 2, 3),
    )
    constants = (
        jnp.asarray(tables["kernel"]),
        jnp.asarray(tables["forward_x"]),
        jnp.asarray(tables["backward_x"]),
        *[jnp.asarray(table) for table in tables["block"]],
    )
    message, near = join(message, payload)
    arrived = exchange(message, devices)

    def pair_first(first_tile, last_tile, fields, *after):
        def body(*refs):
            pair_first_body(first_tile, last_tile, tile_count, spans, *refs)

        tiles = last_tile - first_tile
        return pair_call(
            body,
            [(tile_count * listed * TILE, TILE)] * 2
            + [(last_tile * GROUP, TILE), (9 * 3 * tile_count, TILE)],
            [
                (9 * brick_rows, TILE),
                (tiles * listed * quantities * GROUP, TILE),
                (tiles * 4 * TILE, TILE),
                (tiles * 3 * RHS * TILE, TILE),
                (9 * 3 * tile_count, TILE),
                (last_tile * GROUP, TILE),
            ],
            lists,
            *near,
            *fields,
            *after,
            tiles=tiles,
            large=2 if first_tile > 0 else None,
            aliased=2 if first_tile > 0 else 0,
        )

    early = pair_first(0, EARLY_TILES, (), message)

    def middle_first(*refs):
        middle_first_body(counts, *refs)

    arrived, early = lax.optimization_barrier((arrived, tuple(early)))
    wave_shape = tables["kernel"].shape[1:]
    mixed, wave = call(
        middle_first,
        [(message_shape, f32), (wave_shape, f32)],
        arrived,
        *constants,
        own_block=1,
        near=1,
        large=(1,),
        vmem=MIDDLE_VMEM_LIMIT,
    )
    returned = exchange(mixed, devices)
    first_term, second_term, direct, near = pair_first(
        EARLY_TILES, tile_count, (early[2],), wave, *early[:2]
    )

    def sample(*refs):
        sample_body(devices, *refs)

    carried_shape = (16, atoms)
    field_shape = (tile_count * GROUP, TILE)
    carried, moments = call(
        sample,
        [(carried_shape, f32), ((moment_rows, TILE), f32)],
        returned,
        splines,
        depth_high,
        depth_low,
        start,
        Head(direct, field_shape),
        polar,
        near=1,
        large=(0,),
        vmem=MIDDLE_VMEM_LIMIT,
    )

    def spread(*refs):
        spread_body(devices, *refs)

    (message,) = call(
        spread,
        [(message_shape, f32)],
        splines,
        depth_high,
        depth_low,
        Head(carried, carried_shape),
    )
    message, near_moments = join(message, moments)
    arrived = exchange(message, devices)

    def pair_second(*refs):
        pair_second_body(tile_count, spans, *refs)

    (direct,) = pair_call(
        pair_second,
        [(tile_count * GROUP, TILE)],
        [
            (9 * 3 * tile_count, TILE),
            (9 * moment_rows, TILE),
            (tile_count * listed * 3 * GROUP, TILE),
            (tile_count * listed * 3 * RHS * GROUP, TILE),
            (tile_count * 3 * TILE, TILE),
            (tile_count * 3 * RHS * TILE, TILE),
            (tile_count * GROUP, TILE),
        ],
        lists,
        near,
        *near_moments,
        first_term,
        second_term,
        tiles=tile_count,
        large=0,
    )

    def middle_second(*refs):
        middle_second_body(counts, *refs)

    mixed, local = call(
        middle_second,
        [(last_shape, f32), ((32, atoms), f32)],
        arrived,
        *constants,
        Head(wave, wave_shape),
        start,
        Head(carried, carried_shape),
        Head(direct, field_shape),
        polar,
        own_block=1,
        near=1,
        vmem=MIDDLE_VMEM_LIMIT,
    )
    returned = exchange(mixed, devices)

    def final(*refs):
        final_body(devices, *refs)

    outs = final_call(
        final,
        [(rhs.shape, f32), (rhs.shape, f32)],
        returned,
        splines,
        depth_high,
        depth_low,
        rhs,
        local,
    )
    return tuple(jnp.swapaxes(out, 0, 1)[None, None] for out in outs)


def solution(mesh):
    placed = (
        P("row", "col", None, None, None),
        P("row", "col", None, None),
        P("row", "col", None),
        P("row", "col", None, None),
        P("row", "col", None, None),
    )
    devices = mesh.shape["row"] * mesh.shape["col"]
    return jax.shard_map(
        slab_local if KZ % devices == 0 else pencil_local,
        mesh=mesh,
        in_specs=placed,
        out_specs=(P("row", "col", None, None, None), P("row", "col", None, None, None)),
        check_vma=False,
    )
```
